32 devices in a mesh: dp: 8 (over z, y), feat: 4 (over x, core).
Axes of the slice: x: 2, y: 2, z: 4, core: 2. Of those that a mesh axis runs over, the one named last changes fastest.
Arguments:
- hidden_in: bfloat16 [24, 1024, 768], P('dp', 'feat'), may hold values from -6 to 6
- norm1_gain: float32 [768], replicated, may hold values from 0.5 to 1.5
- norm1_bias: float32 [768], replicated, may hold values from -1.5 to 1.5
- qkv_weight: bfloat16 [768, 2304], replicated, may hold values from -0.21875 to 0.21875
- qkv_bias: float32 [2304], replicated, may hold values from -1.5 to 1.5
- feature_draws: bfloat16 [12, 64, 256], P(None, None, 'feat'), may hold values from -2 to 2
- out_weight: bfloat16 [768, 768], replicated, may hold values from -3.5 to 3.5
- out_bias: float32 [768], replicated, may hold values from -1.5 to 1.5
- norm2_gain: float32 [768], replicated, may hold values from 0.5 to 1.5
- norm2_bias: float32 [768], replicated, may hold values from -1.5 to 1.5
- up_weight: bfloat16 [768, 3072], replicated, may hold values from -0.21875 to 0.21875
- up_bias: float32 [3072], replicated, may hold values from -1.5 to 1.5
- down_weight: bfloat16 [3072, 768], replicated, may hold values from -0.15625 to 0.15625
- down_bias: float32 [768], replicated, may hold values from -1.5 to 1.5
- block_bucket: int32 [24, 16, 1], P('dp'), may hold values from 0 to 3; in each aligned block of 16 rows (0 to 15, 16 to 31, ..., all dimensions but the last counted through in order) at most 8 rows name the same one
- out_grad: bfloat16 [24, 1024, 768], P('dp', 'feat'), may hold values from -6 to 6
Outputs:
- layer_out: bfloat16 [24, 1024, 768], P('dp', 'feat')
- input_grad: float32 [24, 1024, 768], P('dp', 'feat')
- norm1_gain_grad: float32 [768], P(('dp', 'feat'))
- norm1_bias_grad: float32 [768], P(('dp', 'feat'))
- qkv_weight_grad: float32 [768, 2304], P(('dp', 'feat'))
- qkv_bias_grad: float32 [2304], P(('dp', 'feat'))
- out_weight_grad: float32 [768, 768], P(('dp', 'feat'))
- out_bias_grad: float32 [768], P(('dp', 'feat'))
- norm2_gain_grad: float32 [768], P(('dp', 'feat'))
- norm2_bias_grad: float32 [768], P(('dp', 'feat'))
- up_weight_grad: float32 [768, 3072], P(('dp', 'feat'))
- up_bias_grad: float32 [3072], P(('dp', 'feat'))
- down_weight_grad: float32 [3072, 768], P(('dp', 'feat'))
- down_bias_grad: float32 [768], P(('dp', 'feat'))
The draws below stay inside these ranges and needn't reach their ends.
Inputs may be any that keep to these rules, and one draw needn't show every extreme that they name: `block_bucket`: within each sequence no bucket holds more than 8 of its 16 blocks; in some sequence one bucket holds exactly 8.
All inputs are finite; a program needn't handle non-finite values.
Results may differ from the reference program's by a relative error of at most 0.024.
Values may be sent and summed in bfloat16 or wider, within the bound.
A program may use at most 384 MiB of HBM per device.

```python
import math
import jax
import jax.numpy as jnp
import numpy as np
from jax import lax

D = 768
HEADS = 12
HD = 64
FF = 3072
FEAT = 256
BLOCK = 64
LEN = 1024
NBUCK = 4
CAP = 8
SEQS = 24
NB = 16


def steps_of(own_key, shape, split, least, largest):
    gain = 1.0
    for position, parts in split:
        steps = jax.random.uniform(jax.random.fold_in(jax.random.fold_in(own_key, 6), position), (parts,), jnp.float32, least / len(split), largest / len(split))
        gain = gain * jnp.repeat(jnp.exp(steps), shape[position] // parts).reshape((-1,) + (1,) * (len(shape) - 1 - position))
    return gain


def assign_block(key, own, number, rows, number_of, top, limit, slope):
    order = jax.random.permutation(key, number_of)
    packed, ordinary = load_shares(number_of, rows * top, limit, slope, True), load_shares(number_of, rows * top, limit, slope, False)
    places = jnp.arange(number_of)

    def named(lengths, turn):
        used = int((lengths > 0).sum())
        fixed = max(1, used // 4)
        moved = fixed + (places - fixed + turn * (used - fixed)) % max(1, number_of - fixed)
        return jnp.zeros((number_of,), jnp.int32).at[order[jnp.where(places < fixed, places, moved)]].set(jnp.asarray(lengths, jnp.int32))

    lengths = jnp.where(number % 4 == 0, named(packed, number // 4), named(ordinary, number - number // 4 - 1))
    mixed = jax.random.permutation(jax.random.fold_in(own, 3), number_of)
    giver, sink = mixed[0:number_of // 2 * 2:2], mixed[1:number_of // 2 * 2:2]
    room = jnp.minimum(lengths[giver] - 1, limit - lengths[sink]) // 2
    room = jnp.where((giver == order[0]) | (sink == order[0]) | (lengths[sink] == 0), 0, jnp.maximum(room, 0))
    moved = jax.random.randint(jax.random.fold_in(own, 4), (number_of // 2,), 0, 1 << 20) % (room + 1)
    lengths = lengths.at[giver].add(-moved).at[sink].add(moved)
    members = jnp.searchsorted(jnp.cumsum(lengths), jnp.arange(rows * top), side="right").astype(jnp.int32)
    grid = members.reshape(top, rows).T
    grid = grid[jax.random.permutation(jax.random.fold_in(own, 1), rows)]
    turn = jax.random.randint(jax.random.fold_in(own, 2), (rows, 1), 0, top)
    return jnp.take_along_axis(grid, (jnp.arange(top)[None, :] + turn) % top, axis=1)


def load_shares(number_of, total, most, slope, full):
    loads = [(1 << 20) // math.isqrt(grade ** slope) + 1 for grade in range(1, number_of + 1)]
    largest = most if full else min(most, max(-(-total // number_of), total * loads[0] // sum(loads)))
    least = 1 if total - largest >= number_of - 1 else 0
    given, surplus = [largest] + [least] * (number_of - 1), total - largest - least * (number_of - 1)
    while surplus > 0:
        candidates = [i for i in range(1, number_of) if given[i] < largest] or [i for i in range(1, number_of) if given[i] < most]
        pool, left = sum([loads[i] for i in candidates]), surplus
        for i in candidates:
            more = min(most - given[i], max(1, left * loads[i] // pool), surplus)
            given[i] = given[i] + more
            surplus = surplus - more
    return np.array(given)


def gaussian(rng, extent, width, most, split=(), kind=jnp.bfloat16):
    factor_of = steps_of(rng, extent, split, -0.22, 0.18) if split else 1.0
    values = jax.random.normal(rng, extent, jnp.float32) * width * factor_of
    return jnp.minimum(jnp.maximum(values, -most), most).astype(kind)


def setup_inputs(seed: int = 0) -> dict:
    key_list = jax.random.split(jax.random.key(seed), 17)
    hidden_in = gaussian(key_list[0], (SEQS, LEN, D), 1.0, 6.0, ((0, 8), (1, 4)))
    norm1_gain = jnp.clip(1.0 + 0.1 * jax.random.normal(key_list[1], (D,), jnp.float32), 0.5, 1.5)
    norm1_bias = gaussian(key_list[2], (D,), 0.3, 1.5, (), jnp.float32)
    qkv_weight = gaussian(key_list[3], (D, 3 * D), D ** -0.5, 0.21875)
    qkv_bias = gaussian(key_list[4], (3 * D,), 0.3, 1.5, (), jnp.float32)
    feature_draws = gaussian(key_list[5], (HEADS, HD, FEAT), (HD // 8) ** -0.5, 2.0, ((2, 4),))
    out_weight = gaussian(key_list[6], (D, D), (max(1, 4 * D // LEN)) ** -0.5, 3.5)
    out_bias = gaussian(key_list[7], (D,), 0.3, 1.5, (), jnp.float32)
    norm2_gain = jnp.clip(1.0 + 0.1 * jax.random.normal(key_list[8], (D,), jnp.float32), 0.5, 1.5)
    norm2_bias = gaussian(key_list[9], (D,), 0.3, 1.5, (), jnp.float32)
    up_weight = gaussian(key_list[10], (D, FF), D ** -0.5, 0.21875)
    up_bias = gaussian(key_list[11], (FF,), 0.3, 1.5, (), jnp.float32)
    down_weight = gaussian(key_list[12], (FF, D), (FF // 2) ** -0.5, 0.15625)
    down_bias = gaussian(key_list[13], (D,), 0.3, 1.5, (), jnp.float32)
    block_bucket_keys = jax.random.split(jax.random.fold_in(key_list[14], 1), SEQS * NB // (LEN // BLOCK))
    block_bucket_turns = jax.random.permutation(jax.random.fold_in(key_list[14], 3), SEQS * NB // (LEN // BLOCK))
    block_bucket = jax.vmap(lambda own, number: assign_block(jax.random.fold_in(key_list[14], 2), own, number, LEN // BLOCK, NBUCK, 1, CAP, 2))(block_bucket_keys, block_bucket_turns).reshape((SEQS, NB, 1))
    out_grad = gaussian(key_list[15], (SEQS, LEN, D), 1.0, 6.0, ((0, 8), (1, 4)))
    return dict(hidden_in=hidden_in, norm1_gain=norm1_gain, norm1_bias=norm1_bias, qkv_weight=qkv_weight, qkv_bias=qkv_bias, feature_draws=feature_draws, out_weight=out_weight, out_bias=out_bias, norm2_gain=norm2_gain, norm2_bias=norm2_bias, up_weight=up_weight, up_bias=up_bias, down_weight=down_weight, down_bias=down_bias, block_bucket=block_bucket, out_grad=out_grad)


HIGH = lax.Precision.HIGHEST

@jax.custom_vjp
def low(v):
    return lax.optimization_barrier(v.astype(jnp.bfloat16)).astype(jnp.float32)

@jax.custom_vjp
def low_back(v):
    return v

def low_keep(v):
    return (low(v), None)

def low_pass(kept, grad):
    return (grad,)

def back_keep(v):
    return (v, None)

def back_low(kept, grad):
    return (low(grad),)
low.defvjp(low_keep, low_pass)
low_back.defvjp(back_keep, back_low)

def normalize(values):
    row_mean = lax.optimization_barrier(jnp.mean(values, axis=-1, keepdims=True))
    centered = values - row_mean
    return centered * lax.rsqrt(lax.optimization_barrier(jnp.mean(centered * centered, axis=-1, keepdims=True)) + 1e-05)

def feature_map(vectors, draws):
    projection = low_back(jnp.einsum('lhd,hdm->lhm', vectors, draws, precision=HIGH))
    square = lax.optimization_barrier(jnp.sum(vectors * vectors, axis=-1, keepdims=True)) / (2.0 * math.sqrt(HD))
    return low(jnp.exp(projection - square) / math.sqrt(FEAT))

def exact_head(same_bucket, operands):
    queries, keys_head, values_head = operands
    scores = low_back(jnp.dot(queries, keys_head.T, precision=HIGH) / math.sqrt(HD))
    weights = low(jnp.exp(scores)) * same_bucket
    return (jnp.dot(weights, values_head, precision=HIGH), lax.optimization_barrier(jnp.sum(weights, axis=-1)))

def block_layer(hidden, buckets, draws, params):
    norm1_gain, norm1_bias, qkv_weight, qkv_bias, out_weight, out_bias, norm2_gain, norm2_bias, up_weight, up_bias, down_weight, down_bias = params
    count = hidden.shape[0]
    attn_in = low(normalize(hidden) * norm1_gain + norm1_bias)
    projected = low(low_back(jnp.dot(attn_in, qkv_weight, precision=HIGH)) + qkv_bias)
    queries = projected[:, :D].reshape(count, HEADS, HD)
    keys_all = projected[:, D:2 * D].reshape(count, HEADS, HD)
    values_all = projected[:, 2 * D:].reshape(count, HEADS, HD)
    phi_q = feature_map(queries, draws)
    phi_k = feature_map(keys_all, draws)
    token_bucket = jnp.repeat(buckets, BLOCK)
    one_hot = (token_bucket[:, None] == jnp.arange(NBUCK, dtype=jnp.int32)[None, :]).astype(hidden.dtype)
    away = 1.0 - one_hot
    masked_values = values_all[:, None] * away[:, :, None, None]
    state_num = low_back(low(jnp.einsum('jhm,juhd->uhmd', phi_k, masked_values, precision=HIGH)))
    state_den = low_back(low(jnp.einsum('jhm,ju->uhm', phi_k, away, precision=HIGH)))
    spread_q = phi_q[:, None] * one_hot[:, :, None, None]
    low_num = jnp.einsum('iuhm,uhmd->ihd', spread_q, state_num, precision=HIGH)
    low_den = jnp.einsum('iuhm,uhm->ih', spread_q, state_den, precision=HIGH)
    same_bucket = (token_bucket[:, None] == token_bucket[None, :]).astype(hidden.dtype)
    checked = jax.checkpoint(exact_head)
    exact_num, exact_den = lax.map(lambda operands: checked(same_bucket, operands), (queries.transpose(1, 0, 2), keys_all.transpose(1, 0, 2), values_all.transpose(1, 0, 2)))
    total_num = low_back(low_num + exact_num.transpose(1, 0, 2))
    total_den = low_back(low_den + exact_den.T)
    mixed = low((total_num / total_den[:, :, None]).reshape(count, D))
    resid = hidden + low_back(jnp.dot(mixed, out_weight, precision=HIGH)) + out_bias
    mlp_in = low(normalize(resid) * norm2_gain + norm2_bias)
    act = low(jax.nn.gelu(low_back(jnp.dot(mlp_in, up_weight, precision=HIGH)) + up_bias, approximate=True))
    return resid + low_back(jnp.dot(act, down_weight, precision=HIGH)) + down_bias

def reference(hidden_in, norm1_gain, norm1_bias, qkv_weight, qkv_bias, feature_draws, out_weight, out_bias, norm2_gain, norm2_bias, up_weight, up_bias, down_weight, down_bias, block_bucket, out_grad):
    params = (norm1_gain.astype(jnp.float32), norm1_bias.astype(jnp.float32), qkv_weight.astype(jnp.float32), qkv_bias.astype(jnp.float32), out_weight.astype(jnp.float32), out_bias.astype(jnp.float32), norm2_gain.astype(jnp.float32), norm2_bias.astype(jnp.float32), up_weight.astype(jnp.float32), up_bias.astype(jnp.float32), down_weight.astype(jnp.float32), down_bias.astype(jnp.float32))
    draws = feature_draws.astype(jnp.float32)

    def one_sequence(totals, sequence):
        hidden, buckets, cotangent = sequence

        def forward(hidden_rows, weights):
            return block_layer(hidden_rows, buckets, draws, weights)
        result, pull = jax.vjp(forward, hidden, params)
        grad_hidden, grad_params = pull(cotangent)
        return (jax.tree.map(jnp.add, totals, grad_params), (result.astype(jnp.bfloat16), grad_hidden))
    grad_init = jax.tree.map(jnp.zeros_like, params)
    totals, outputs = lax.scan(one_sequence, grad_init, (hidden_in.astype(jnp.float32), block_bucket[..., 0], out_grad.astype(jnp.float32)))
    layer_out, input_grad = outputs
    return (layer_out, input_grad, totals[0], totals[1], totals[2], totals[3], totals[4], totals[5], totals[6], totals[7], totals[8], totals[9], totals[10], totals[11])
```

```python
import math

import jax
import jax.numpy as jnp
from jax import lax
from jax.experimental import pallas as pl
from jax.experimental.pallas import tpu as pltpu
from jax.sharding import PartitionSpec as P

HD = 64
FEAT = 256
BLOCK = 64
NBUCK = 4
GROUP = 4
CHUNK = 256
FAR = 16384.0
VMEM = 56 * 1024 * 1024

F32 = jnp.float32
BF16 = jnp.bfloat16


def mat(left, right):
    return jnp.dot(left, right, preferred_element_type=F32)


def mat_nt(left, right):
    return lax.dot_general(left, right, (((1,), (1,)), ((), ())), preferred_element_type=F32)


def mat_tn(left, right):
    return lax.dot_general(left, right, (((0,), (0,)), ((), ())), preferred_element_type=F32)


def row_stats(values):
    row_mean = jnp.mean(values, axis=-1, keepdims=True)
    centered = values - row_mean
    scale = lax.rsqrt(jnp.mean(centered * centered, axis=-1, keepdims=True) + 1e-05)
    return (centered * scale, scale)


def norm_back(cotangent, normed, scale):
    mean_one = jnp.mean(cotangent, axis=-1, keepdims=True)
    mean_two = jnp.mean(cotangent * normed, axis=-1, keepdims=True)
    return scale * (cotangent - mean_one - normed * mean_two)


def features(vectors, draws):
    wide = vectors.astype(F32)
    square = jnp.sum(wide * wide, axis=0, keepdims=True) * (0.5 / math.sqrt(HD))
    return jnp.exp(mat(draws, vectors) - square) * (1.0 / math.sqrt(FEAT))


def spread(rows, marks):
    return [rows * marks[u : u + 1] for u in range(NBUCK)]


def pick(stacked, marks):
    total = stacked[0:HD] * marks[0:1]
    for u in range(1, NBUCK):
        total = total + stacked[u * HD : (u + 1) * HD] * marks[u : u + 1]
    return total


def attend_kernel(
    x0, x1, x2, x3, weight, bias, draws, hot_ref, mix_out, proj_out, state_out, mixed_out, den_out,
    query_scr, key_scr, value_scr, low_scr, gather_scr,
):
    head = pl.program_id(0)
    rows = x0.shape[0]
    total = GROUP * rows
    for r, part in enumerate((x0, x1, x2, x3)):
        piece = mat_nt(weight[...], part[...]) + bias[...]
        proj_out[:, r * rows : (r + 1) * rows] = piece.astype(BF16)
    query = proj_out[0:HD]
    key = proj_out[HD : 2 * HD]
    value = proj_out[2 * HD : 3 * HD]
    hot = hot_ref[...]
    hot_wide = hot.astype(F32)
    live = (lax.broadcasted_iota(jnp.int32, hot.shape, 0) < NBUCK).astype(F32)
    away_wide = live - hot_wide
    away = away_wide.astype(BF16)
    phi_q = features(query, draws[...]).astype(BF16)
    phi_k = features(key, draws[...]).astype(BF16)
    spread_value = jnp.concatenate(spread(value, away) + [away], axis=0)
    state = mat_nt(spread_value, phi_k).astype(BF16)
    state_out[...] = state
    low = mat(state, phi_q)
    low_scr[0:HD] = pick(low, hot_wide)
    low_den = jnp.sum(low[NBUCK * HD :] * hot_wide, axis=0, keepdims=True)
    low_scr[HD : HD + 8] = jnp.broadcast_to(low_den, (8, total))
    query_scr[...] = jnp.concatenate([query * (1.0 / math.sqrt(HD)), hot], axis=0).astype(BF16)
    key_scr[...] = jnp.concatenate([key, away * -FAR], axis=0).astype(F32).T.astype(BF16)
    value_scr[0:HD] = value
    value_scr[HD:] = jnp.ones((16, total), BF16)

    def step(c, carry):
        cols = pl.ds(pl.multiple_of(c * CHUNK, CHUNK), CHUNK)
        weights = jnp.exp(mat(key_scr[...], query_scr[:, cols])).astype(BF16)
        exact = mat(value_scr[...], weights)
        den = low_scr[HD : HD + 8, cols] + exact[HD : HD + 8]
        mixed = (low_scr[0:HD, cols] + exact[0:HD]) / den[0:1]
        mixed_out[:, cols] = mixed
        den_out[:, cols] = den
        gather_scr[pl.ds(pl.multiple_of(head * HD, HD), HD), cols] = mixed
        return carry

    lax.fori_loop(0, total // CHUNK, step, 0)

    @pl.when(head == pl.num_programs(0) - 1)
    def _():
        mix_out[...] = gather_scr[...].T.astype(BF16)


def attend(parts, weight, bias, draws, hot):
    heads, width, model = weight.shape
    rows = parts[0].shape[0]
    total = GROUP * rows
    whole = lambda *shape: pl.BlockSpec(shape, lambda h: (0,) * len(shape))
    by_head = lambda *shape: pl.BlockSpec((None,) + shape, lambda h: (h,) + (0,) * len(shape))
    states = NBUCK * HD + 16
    return pl.pallas_call(
        attend_kernel,
        grid=(heads,),
        out_shape=(
            jax.ShapeDtypeStruct((total, heads * HD), BF16),
            jax.ShapeDtypeStruct((heads, width, total), BF16),
            jax.ShapeDtypeStruct((heads, states, FEAT), BF16),
            jax.ShapeDtypeStruct((heads, HD, total), F32),
            jax.ShapeDtypeStruct((heads, 8, total), F32),
        ),
        in_specs=[whole(rows, model)] * 4
        + [by_head(width, model), by_head(width, 1), by_head(FEAT, HD), whole(16, total)],
        out_specs=(
            whole(total, heads * HD),
            by_head(width, total),
            by_head(states, FEAT),
            by_head(HD, total),
            by_head(8, total),
        ),
        scratch_shapes=[
            pltpu.VMEM((HD + 16, total), BF16),
            pltpu.VMEM((total, HD + 16), BF16),
            pltpu.VMEM((HD + 16, total), BF16),
            pltpu.VMEM((HD + 8, total), F32),
            pltpu.VMEM((heads * HD, total), F32),
        ],
        compiler_params=pltpu.CompilerParams(vmem_limit_bytes=VMEM),
        cost_estimate=pl.CostEstimate(flops=8_000_000_000, bytes_accessed=8_000_000, transcendentals=0),
        name="attend",
    )(*parts, weight, bias, draws, hot)


def attend_back_kernel(
    x0, x1, x2, x3, g0, g1, g2, g3, weight, draws, draws_ext, hot_ref, proj, state_ref, mixed_ref, den_ref,
    p0, p1, p2, p3, weight_out, bias_out,
    grad_scr, query_scr, key_scr, num_scr, value_scr, soft_scr, score_scr, exact_scr, proj_scr,
):
    head = pl.program_id(0)
    rows = x0.shape[0]
    total = GROUP * rows
    root = 1.0 / math.sqrt(HD)

    @pl.when(head == 0)
    def _():
        for r, part in enumerate((g0, g1, g2, g3)):
            grad_scr[:, r * rows : (r + 1) * rows] = part[...].astype(F32).T

    query = proj[0:HD]
    key = proj[HD : 2 * HD]
    value = proj[2 * HD : 3 * HD]
    hot = hot_ref[...]
    hot_wide = hot.astype(F32)
    live = (lax.broadcasted_iota(jnp.int32, hot.shape, 0) < NBUCK).astype(F32)
    away_wide = live - hot_wide
    away = away_wide.astype(BF16)
    inverse = 1.0 / den_ref[0:1]
    mixed_grad = grad_scr[pl.ds(pl.multiple_of(head * HD, HD), HD)]
    grad_num = (mixed_grad * inverse).astype(BF16)
    grad_den = -jnp.sum(mixed_grad * mixed_ref[...], axis=0, keepdims=True) * inverse
    den_rows = jnp.broadcast_to(grad_den, (16, total)).astype(BF16)
    spread_grad = jnp.concatenate(spread(grad_num, hot) + [den_rows * hot], axis=0)
    spread_value = jnp.concatenate(spread(value, away) + [away], axis=0)

    wide_q = features(query, draws[...])
    state_grad = mat_nt(spread_grad, wide_q.astype(BF16)).astype(BF16)
    scaled_q = mat_tn(state_ref[...], spread_grad) * wide_q
    back_q = mat(draws_ext[...], scaled_q.astype(BF16))
    query_grad = back_q[0:HD] - query.astype(F32) * (back_q[HD : HD + 1] * root)

    wide_k = features(key, draws[...])
    scaled_k = mat_tn(state_grad, spread_value) * wide_k
    back_k = mat(draws_ext[...], scaled_k.astype(BF16))
    key_grad = back_k[0:HD] - key.astype(F32) * (back_k[HD : HD + 1] * root)
    value_grad = pick(mat(state_grad[0 : NBUCK * HD], wide_k.astype(BF16)), away_wide)

    query_scr[...] = jnp.concatenate([query * root, hot], axis=0).astype(BF16)
    key_scr[...] = jnp.concatenate([key, away * -FAR], axis=0).astype(F32).T.astype(BF16)
    first = (lax.broadcasted_iota(jnp.int32, hot.shape, 0) < 1).astype(BF16)
    num_scr[...] = jnp.concatenate([grad_num, den_rows], axis=0)
    value_scr[...] = jnp.concatenate([value, first], axis=0).astype(F32).T.astype(BF16)

    def step(c, carry):
        cols = pl.ds(pl.multiple_of(c * CHUNK, CHUNK), CHUNK)
        soft = jnp.exp(mat(key_scr[...], query_scr[:, cols]))
        soft_scr[:, cols] = soft.astype(BF16)
        score = (mat(value_scr[...], num_scr[:, cols]) * soft).astype(BF16)
        score_scr[:, cols] = score
        exact_scr[:, cols] = mat(proj[HD : 2 * HD], score)
        return carry

    lax.fori_loop(0, total // CHUNK, step, 0)
    query_grad = query_grad + exact_scr[...] * root
    key_grad = key_grad + mat_nt(query, score_scr[...]) * root
    value_grad = value_grad + mat_nt(grad_num, soft_scr[...])
    proj_grad = jnp.concatenate([query_grad, key_grad, value_grad], axis=0)
    bias_out[...] = jnp.sum(proj_grad, axis=1, keepdims=True)
    proj_low = proj_grad.astype(BF16)
    proj_scr[pl.ds(pl.multiple_of(head * 3 * HD, 3 * HD), 3 * HD)] = proj_low
    weight_grad = mat(proj_low[:, 0:rows], x0[...])
    for r, part in ((1, x1), (2, x2), (3, x3)):
        weight_grad = weight_grad + mat(proj_low[:, r * rows : (r + 1) * rows], part[...])
    weight_out[...] = weight_grad

    @pl.when(head == pl.num_programs(0) - 1)
    def _():
        for r, out in enumerate((p0, p1, p2, p3)):
            out[...] = mat_tn(proj_scr[:, r * rows : (r + 1) * rows], weight[...]).astype(BF16)


def attend_back(parts, grads, weight, draws, draws_ext, hot, kept):
    proj, state, mixed, den = kept
    heads, width, model = weight.shape
    rows = parts[0].shape[0]
    total = GROUP * rows
    whole = lambda *shape: pl.BlockSpec(shape, lambda h: (0,) * len(shape))
    by_head = lambda *shape: pl.BlockSpec((None,) + shape, lambda h: (h,) + (0,) * len(shape))
    states = NBUCK * HD + 16
    return pl.pallas_call(
        attend_back_kernel,
        grid=(heads,),
        out_shape=tuple([jax.ShapeDtypeStruct((rows, model), BF16)] * 4)
        + (
            jax.ShapeDtypeStruct((heads, width, model), F32),
            jax.ShapeDtypeStruct((heads, width, 1), F32),
        ),
        in_specs=[whole(rows, model)] * 4
        + [whole(rows, heads * HD)] * 4
        + [
            whole(heads * width, model),
            by_head(FEAT, HD),
            by_head(HD + 16, FEAT),
            whole(16, total),
            by_head(width, total),
            by_head(states, FEAT),
            by_head(HD, total),
            by_head(8, total),
        ],
        out_specs=tuple([whole(rows, model)] * 4) + (by_head(width, model), by_head(width, 1)),
        scratch_shapes=[
            pltpu.VMEM((heads * HD, total), F32),
            pltpu.VMEM((HD + 16, total), BF16),
            pltpu.VMEM((total, HD + 16), BF16),
            pltpu.VMEM((HD + 16, total), BF16),
            pltpu.VMEM((total, HD + 16), BF16),
            pltpu.VMEM((total, total), BF16),
            pltpu.VMEM((total, total), BF16),
            pltpu.VMEM((HD, total), F32),
            pltpu.VMEM((heads * width, total), BF16),
        ],
        compiler_params=pltpu.CompilerParams(vmem_limit_bytes=VMEM),
        cost_estimate=pl.CostEstimate(flops=16_000_000_000, bytes_accessed=10_000_000, transcendentals=0),
        name="attend_back",
    )(*parts, *grads, weight.reshape(heads * width, model), draws, draws_ext, hot, proj, state, mixed, den)


def per_device(
    hidden_in, norm1_gain, norm1_bias, qkv_weight, qkv_bias, feature_draws, out_weight, out_bias,
    norm2_gain, norm2_bias, up_weight, up_bias, down_weight, down_bias, block_bucket, out_grad,
):
    seq_count, rows, model = hidden_in.shape
    ff = up_weight.shape[1]
    dp_size = lax.axis_size("dp")
    devices = dp_size * GROUP
    own = lax.axis_index("feat")
    own_x, own_core = own // 2, own % 2
    all_heads = feature_draws.shape[0]
    heads = all_heads // GROUP
    width = 3 * HD

    def swap(values, r):
        return lax.ppermute(values, "feat", [(f, f ^ r) for f in range(GROUP)])

    def at(values, index, axis=0):
        return lax.dynamic_index_in_dim(values, index, axis, keepdims=False)

    def relative(values, axis=0):
        return [at(values, own ^ r, axis) for r in range(GROUP)]

    def scatter_sum(values, rest):
        pairs = values.astype(BF16).reshape((dp_size, 2, 2) + rest)
        chip = at(pairs, own_core, 2).astype(F32) + swap(at(pairs, 1 - own_core, 2), 1).astype(F32)
        chip = chip.astype(BF16).reshape((dp_size * 2 * rest[0],) + rest[1:])
        lines = lax.psum_scatter(chip, "dp", scatter_dimension=0, tiled=True).reshape((2,) + rest)
        return at(lines, own_x).astype(F32) + swap(at(lines, 1 - own_x), 2).astype(F32)

    head_draws = feature_draws.reshape(GROUP, heads, HD, feature_draws.shape[2])
    pieces = [at(head_draws, own)] + [swap(at(head_draws, own ^ r), r) for r in (1, 2, 3)]
    own_draws = jnp.concatenate(pieces, axis=2)
    draws_t = own_draws.transpose(0, 2, 1)
    draws_ext = jnp.concatenate(
        [own_draws, jnp.ones((heads, 1, FEAT), BF16), jnp.zeros((heads, 15, FEAT), BF16)], axis=1
    )
    own_weight = at(qkv_weight.reshape(model, 3, GROUP, heads, HD), own, 2)
    own_weight = own_weight.transpose(2, 1, 3, 0).reshape(heads, width, model)
    own_bias = at(qkv_bias.reshape(3, GROUP, heads, HD), own, 1)
    own_bias = own_bias.transpose(1, 0, 2).reshape(heads, width, 1)
    out_rel = jnp.concatenate(relative(out_weight.reshape(GROUP, heads * HD, model)), axis=0)
    block_ids = block_bucket[..., 0].reshape(seq_count, GROUP, rows // BLOCK)
    block_ids = jnp.concatenate(relative(block_ids, 1), axis=1)
    token_ids = jnp.repeat(block_ids, BLOCK, axis=1)
    hot = (token_ids[:, None, :] == jnp.arange(16, dtype=jnp.int32)[:, None]).astype(BF16)

    parts, mixes, kept = [], [], []
    for s in range(seq_count):
        normed, _ = row_stats(hidden_in[s].astype(F32))
        mine = (normed * norm1_gain + norm1_bias).astype(BF16)
        across = swap(mine, 2)
        parts.append([mine, swap(mine, 1), across, swap(across, 1)])
    for s in range(seq_count):
        mixed_rows, *saved = attend(parts[s], own_weight, own_bias, draws_t, hot[s])
        kept.append(saved)
        blocks = mixed_rows.reshape(GROUP, rows, heads * HD)
        mixes.append(
            jnp.concatenate([blocks[0]] + [swap(blocks[r], r) for r in (1, 2, 3)], axis=1)
        )
    mixed = jnp.concatenate(mixes, axis=0)
    flat_in = hidden_in.astype(F32).reshape(seq_count * rows, model)

    resid = flat_in + mat(mixed, out_rel) + out_bias
    normed2, scale2 = row_stats(resid)
    mlp_in = (normed2 * norm2_gain + norm2_bias).astype(BF16)
    pre_act = mat(mlp_in, up_weight) + up_bias
    gelu = lambda t: jax.nn.gelu(t, approximate=True)
    act = gelu(pre_act).astype(BF16)
    result = resid + mat(act, down_weight) + down_bias
    layer_out = result.reshape(hidden_in.shape).astype(BF16)
    out_low = out_grad.reshape(seq_count * rows, model)
    out_rows = out_low.astype(F32)
    act_grad = mat_nt(out_low, down_weight)
    pre_grad = jax.vjp(gelu, pre_act)[1](act_grad)[0]
    pre_low = pre_grad.astype(BF16)
    mlp_grad = mat_nt(pre_low, up_weight)
    resid_grad = out_rows + norm_back(mlp_grad * norm2_gain, normed2, scale2)
    resid_low = resid_grad.astype(BF16)
    mixed_grad = mat_nt(resid_low, out_rel).astype(BF16).reshape(seq_count, rows, GROUP, heads * HD)

    terms, weight_terms, bias_terms = [], [], []
    sent = []
    for s in range(seq_count):
        blocks = [mixed_grad[s, :, r] for r in range(GROUP)]
        sent.append([blocks[0]] + [swap(blocks[r], r) for r in (1, 2, 3)])
    for s in range(seq_count):
        p0, p1, p2, p3, weight_term, bias_term = attend_back(
            parts[s], sent[s], own_weight, draws_t, draws_ext, hot[s], kept[s]
        )
        weight_terms.append(weight_term)
        bias_terms.append(bias_term)
        chip_own = p0.astype(F32) + swap(p1, 1).astype(F32)
        chip_far = (p2.astype(F32) + swap(p3, 1).astype(F32)).astype(BF16)
        terms.append(chip_own + swap(chip_far, 2).astype(F32))

    down_sum = scatter_sum(mat_tn(act, out_low), (ff // devices, model))
    up_sum = scatter_sum(mat_tn(mlp_in, pre_low), (model // devices, ff))
    out_term = mat_tn(mixed, resid_low).reshape(2, 2, heads * HD, model)
    out_term = jnp.where(own_x == 1, out_term[::-1], out_term)
    out_term = jnp.where(own_core == 1, out_term[:, ::-1], out_term)
    vectors = [
        jnp.sum(out_rows, axis=0),
        jnp.sum(resid_grad, axis=0),
        jnp.sum(mlp_grad * normed2, axis=0),
        jnp.sum(mlp_grad, axis=0),
        jnp.sum(pre_grad, axis=0),
    ]
    row = jnp.concatenate([v.reshape(devices, -1) for v in vectors], axis=1)
    row = jnp.pad(row, ((0, 0), (0, model - row.shape[1])))
    small = model // devices
    out_term = jnp.concatenate([out_term.reshape(devices, small, model), row[:, None]], axis=1)
    out_term = jnp.pad(out_term, ((0, 0), (0, -(small + 1) % 16), (0, 0)))
    out_sum = scatter_sum(out_term, out_term.shape[1:])
    out_weight_sum, row_sum = out_sum[:small], out_sum[small]
    down_bias_sum, out_bias_sum, norm2_gain_sum, norm2_bias_sum = [
        row_sum[i * small : (i + 1) * small] for i in range(4)
    ]
    up_bias_sum = row_sum[4 * small : 4 * small + ff // devices]

    attn_grad = jnp.stack(terms)
    normed1, scale1 = row_stats(hidden_in.astype(F32))
    input_grad = resid_grad.reshape(hidden_in.shape) + norm_back(
        attn_grad * norm1_gain, normed1, scale1
    )
    weight_term = (weight_terms[0] + weight_terms[1] + weight_terms[2]).reshape(
        heads, 3, HD, dp_size, -1
    )
    weight_term = weight_term.transpose(3, 4, 1, 0, 2).reshape(dp_size, -1, 3 * heads * HD)
    bias_term = (bias_terms[0] + bias_terms[1] + bias_terms[2]).reshape(heads, 3, HD)
    bias_term = bias_term.transpose(1, 0, 2).reshape(1, 1, 3 * heads * HD)
    bias_term = jnp.broadcast_to(bias_term, (dp_size, 1, 3 * heads * HD))
    proj_term = jnp.concatenate([weight_term, bias_term], axis=1).astype(BF16)
    proj_term = jnp.pad(proj_term, ((0, 0), (0, -proj_term.shape[1] % 16), (0, 0)))
    proj_rows = proj_term.shape[1]
    proj_line = lax.psum_scatter(
        proj_term.reshape(dp_size * proj_rows, -1), "dp", scatter_dimension=0, tiled=True
    )
    weight_line = proj_line[: GROUP * small].reshape(GROUP, small, -1)
    bias_line = proj_line[GROUP * small : GROUP * small + 1]
    piece = lambda r: jnp.concatenate([at(weight_line, own ^ r), bias_line], axis=0)
    pieces = [piece(0)] + [swap(piece(r), r) for r in (1, 2, 3)]
    grid = jnp.stack(pieces).reshape(2, 2, small + 1, 3, heads * HD)
    grid = jnp.where(own_x == 1, grid[::-1], grid)
    grid = jnp.where(own_core == 1, grid[:, ::-1], grid)
    grid = grid.reshape(GROUP, small + 1, 3, heads * HD).transpose(1, 2, 0, 3)
    grid = grid.reshape(small + 1, 3 * model).astype(F32)
    qkv_weight_sum, bias_sum = grid[:-1], grid[-1]
    index = lax.axis_index("dp") * GROUP + own
    weight_rows = lax.dynamic_slice_in_dim(qkv_weight, index * small, small, 0).astype(F32)
    own_gain = lax.dynamic_slice_in_dim(norm1_gain, index * small, small, 0)
    own_shift = lax.dynamic_slice_in_dim(norm1_bias, index * small, small, 0)
    norm1_bias_sum = jnp.sum(weight_rows * bias_sum, axis=1)
    norm1_gain_sum = jnp.sum(weight_rows * qkv_weight_sum, axis=1)
    norm1_gain_sum = (norm1_gain_sum - own_shift * norm1_bias_sum) / own_gain
    share = 3 * model // devices
    qkv_bias_sum = lax.dynamic_slice_in_dim(bias_sum, index * share, share, 0)
    return (
        layer_out, input_grad, norm1_gain_sum, norm1_bias_sum, qkv_weight_sum, qkv_bias_sum,
        out_weight_sum, out_bias_sum, norm2_gain_sum, norm2_bias_sum, up_sum, up_bias_sum,
        down_sum, down_bias_sum,
    )


def solution(mesh):
    both = ("dp", "feat")
    rows = P("dp", "feat", None)
    in_specs = (
        rows, P(), P(), P(), P(), P(None, None, "feat"), P(), P(), P(), P(), P(), P(), P(), P(),
        P("dp", None, None), rows,
    )
    out_specs = (
        rows, rows, P(both), P(both), P(both, None), P(both), P(both, None), P(both), P(both),
        P(both), P(both, None), P(both), P(both, None), P(both),
    )
    return jax.shard_map(
        per_device, mesh=mesh, in_specs=in_specs, out_specs=out_specs, check_vma=False
    )
```

```python
import math

import jax
import jax.numpy as jnp
from jax import lax
from jax.experimental import pallas as pl
from jax.experimental.pallas import tpu as pltpu
from jax.sharding import PartitionSpec as P

HD = 64
FEAT = 256
BLOCK = 64
NBUCK = 4
GROUP = 4
CHUNK = 256
FAR = 16384.0
VMEM = 56 * 1024 * 1024

F32 = jnp.float32
BF16 = jnp.bfloat16


def mat(left, right):
    return jnp.dot(left, right, preferred_element_type=F32)


def mat_nt(left, right):
    return lax.dot_general(left, right, (((1,), (1,)), ((), ())), preferred_element_type=F32)


def mat_tn(left, right):
    return lax.dot_general(left, right, (((0,), (0,)), ((), ())), preferred_element_type=F32)


def row_stats(values):
    row_mean = jnp.mean(values, axis=-1, keepdims=True)
    centered = values - row_mean
    scale = lax.rsqrt(jnp.mean(centered * centered, axis=-1, keepdims=True) + 1e-05)
    return (centered * scale, scale)


def norm_back(cotangent, normed, scale):
    mean_one = jnp.mean(cotangent, axis=-1, keepdims=True)
    mean_two = jnp.mean(cotangent * normed, axis=-1, keepdims=True)
    return scale * (cotangent - mean_one - normed * mean_two)


def features(vectors, draws):
    wide = vectors.astype(F32)
    square = jnp.sum(wide * wide, axis=0, keepdims=True) * (0.5 / math.sqrt(HD))
    return jnp.exp(mat(draws, vectors) - square) * (1.0 / math.sqrt(FEAT))


def spread(rows, marks):
    return [rows * marks[u : u + 1] for u in range(NBUCK)]


def pick(stacked, marks):
    total = stacked[0:HD] * marks[0:1]
    for u in range(1, NBUCK):
        total = total + stacked[u * HD : (u + 1) * HD] * marks[u : u + 1]
    return total


def attend_kernel(
    x0, x1, x2, x3, weight, bias, draws, hot_ref, mix_out, proj_out, state_out, mixed_out, den_out,
    query_scr, key_scr, value_scr, low_scr, gather_scr,
):
    head = pl.program_id(0)
    rows = x0.shape[0]
    total = GROUP * rows
    for r, part in enumerate((x0, x1, x2, x3)):
        piece = mat_nt(weight[...], part[...]) + bias[...]
        proj_out[:, r * rows : (r + 1) * rows] = piece.astype(BF16)
    query = proj_out[0:HD]
    key = proj_out[HD : 2 * HD]
    value = proj_out[2 * HD : 3 * HD]
    hot = hot_ref[...]
    hot_wide = hot.astype(F32)
    live = (lax.broadcasted_iota(jnp.int32, hot.shape, 0) < NBUCK).astype(F32)
    away_wide = live - hot_wide
    away = away_wide.astype(BF16)
    phi_q = features(query, draws[...]).astype(BF16)
    phi_k = features(key, draws[...]).astype(BF16)
    spread_value = jnp.concatenate(spread(value, away) + [away], axis=0)
    state = mat_nt(spread_value, phi_k).astype(BF16)
    state_out[...] = state
    low = mat(state, phi_q)
    low_scr[0:HD] = pick(low, hot_wide)
    low_den = jnp.sum(low[NBUCK * HD :] * hot_wide, axis=0, keepdims=True)
    low_scr[HD : HD + 8] = jnp.broadcast_to(low_den, (8, total))
    query_scr[...] = jnp.concatenate([query * (1.0 / math.sqrt(HD)), hot], axis=0).astype(BF16)
    key_scr[...] = jnp.concatenate([key, away * -FAR], axis=0).astype(F32).T.astype(BF16)
    value_scr[0:HD] = value
    value_scr[HD:] = jnp.ones((16, total), BF16)

    def step(c, carry):
        cols = pl.ds(pl.multiple_of(c * CHUNK, CHUNK), CHUNK)
        weights = jnp.exp(mat(key_scr[...], query_scr[:, cols])).astype(BF16)
        exact = mat(value_scr[...], weights)
        den = low_scr[HD : HD + 8, cols] + exact[HD : HD + 8]
        mixed = (low_scr[0:HD, cols] + exact[0:HD]) / den[0:1]
        mixed_out[:, cols] = mixed
        den_out[:, cols] = den
        gather_scr[pl.ds(pl.multiple_of(head * HD, HD), HD), cols] = mixed
        return carry

    lax.fori_loop(0, total // CHUNK, step, 0)

    @pl.when(head == pl.num_programs(0) - 1)
    def _():
        mix_out[...] = gather_scr[...].T.astype(BF16)


def attend(parts, weight, bias, draws, hot):
    heads, width, model = weight.shape
    rows = parts[0].shape[0]
    total = GROUP * rows
    whole = lambda *shape: pl.BlockSpec(shape, lambda h: (0,) * len(shape))
    by_head = lambda *shape: pl.BlockSpec((None,) + shape, lambda h: (h,) + (0,) * len(shape))
    states = NBUCK * HD + 16
    return pl.pallas_call(
        attend_kernel,
        grid=(heads,),
        out_shape=(
            jax.ShapeDtypeStruct((total, heads * HD), BF16),
            jax.ShapeDtypeStruct((heads, width, total), BF16),
            jax.ShapeDtypeStruct((heads, states, FEAT), BF16),
            jax.ShapeDtypeStruct((heads, HD, total), F32),
            jax.ShapeDtypeStruct((heads, 8, total), F32),
        ),
        in_specs=[whole(rows, model)] * 4
        + [by_head(width, model), by_head(width, 1), by_head(FEAT, HD), whole(16, total)],
        out_specs=(
            whole(total, heads * HD),
            by_head(width, total),
            by_head(states, FEAT),
            by_head(HD, total),
            by_head(8, total),
        ),
        scratch_shapes=[
            pltpu.VMEM((HD + 16, total), BF16),
            pltpu.VMEM((total, HD + 16), BF16),
            pltpu.VMEM((HD + 16, total), BF16),
            pltpu.VMEM((HD + 8, total), F32),
            pltpu.VMEM((heads * HD, total), F32),
        ],
        compiler_params=pltpu.CompilerParams(vmem_limit_bytes=VMEM),
        cost_estimate=pl.CostEstimate(flops=8_000_000_000, bytes_accessed=8_000_000, transcendentals=0),
        name="attend",
    )(*parts, weight, bias, draws, hot)


def attend_back_kernel(
    x0, x1, x2, x3, g0, g1, g2, g3, weight, draws, draws_ext, hot_ref, proj, state_ref, mixed_ref, den_ref,
    after, p0, p1, p2, p3, weight_out, bias_out,
    grad_scr, query_scr, key_scr, num_scr, value_scr, soft_scr, score_scr, exact_scr, proj_scr,
):
    head = pl.program_id(0)
    rows = x0.shape[0]
    total = GROUP * rows
    root = 1.0 / math.sqrt(HD)

    @pl.when(head == 0)
    def _():
        for r, part in enumerate((g0, g1, g2, g3)):
            grad_scr[:, r * rows : (r + 1) * rows] = part[...].astype(F32).T

    query = proj[0:HD]
    key = proj[HD : 2 * HD]
    value = proj[2 * HD : 3 * HD]
    hot = hot_ref[...]
    hot_wide = hot.astype(F32)
    live = (lax.broadcasted_iota(jnp.int32, hot.shape, 0) < NBUCK).astype(F32)
    away_wide = live - hot_wide
    away = away_wide.astype(BF16)
    inverse = 1.0 / den_ref[0:1]
    mixed_grad = grad_scr[pl.ds(pl.multiple_of(head * HD, HD), HD)]
    grad_num = (mixed_grad * inverse).astype(BF16)
    grad_den = -jnp.sum(mixed_grad * mixed_ref[...], axis=0, keepdims=True) * inverse
    den_rows = jnp.broadcast_to(grad_den, (16, total)).astype(BF16)
    spread_grad = jnp.concatenate(spread(grad_num, hot) + [den_rows * hot], axis=0)
    spread_value = jnp.concatenate(spread(value, away) + [away], axis=0)

    wide_q = features(query, draws[...])
    state_grad = mat_nt(spread_grad, wide_q.astype(BF16)).astype(BF16)
    scaled_q = mat_tn(state_ref[...], spread_grad) * wide_q
    back_q = mat(draws_ext[...], scaled_q.astype(BF16))
    query_grad = back_q[0:HD] - query.astype(F32) * (back_q[HD : HD + 1] * root)

    wide_k = features(key, draws[...])
    scaled_k = mat_tn(state_grad, spread_value) * wide_k
    back_k = mat(draws_ext[...], scaled_k.astype(BF16))
    key_grad = back_k[0:HD] - key.astype(F32) * (back_k[HD : HD + 1] * root)
    value_grad = pick(mat(state_grad[0 : NBUCK * HD], wide_k.astype(BF16)), away_wide)

    query_scr[...] = jnp.concatenate([query * root, hot], axis=0).astype(BF16)
    key_scr[...] = jnp.concatenate([key, away * -FAR], axis=0).astype(F32).T.astype(BF16)
    first = (lax.broadcasted_iota(jnp.int32, hot.shape, 0) < 1).astype(BF16)
    num_scr[...] = jnp.concatenate([grad_num, den_rows], axis=0)
    value_scr[...] = jnp.concatenate([value, first], axis=0).astype(F32).T.astype(BF16)

    def step(c, carry):
        cols = pl.ds(pl.multiple_of(c * CHUNK, CHUNK), CHUNK)
        soft = jnp.exp(mat(key_scr[...], query_scr[:, cols]))
        soft_scr[:, cols] = soft.astype(BF16)
        score = (mat(value_scr[...], num_scr[:, cols]) * soft).astype(BF16)
        score_scr[:, cols] = score
        exact_scr[:, cols] = mat(proj[HD : 2 * HD], score)
        return carry

    lax.fori_loop(0, total // CHUNK, step, 0)
    query_grad = query_grad + exact_scr[...] * root
    key_grad = key_grad + mat_nt(query, score_scr[...]) * root
    value_grad = value_grad + mat_nt(grad_num, soft_scr[...])
    proj_grad = jnp.concatenate([query_grad, key_grad, value_grad], axis=0)
    bias_out[...] = jnp.sum(proj_grad, axis=1, keepdims=True)
    proj_low = proj_grad.astype(BF16)
    proj_scr[pl.ds(pl.multiple_of(head * 3 * HD, 3 * HD), 3 * HD)] = proj_low
    weight_grad = mat(proj_low[:, 0:rows], x0[...])
    for r, part in ((1, x1), (2, x2), (3, x3)):
        weight_grad = weight_grad + mat(proj_low[:, r * rows : (r + 1) * rows], part[...])
    weight_out[...] = weight_grad

    @pl.when(head == pl.num_programs(0) - 1)
    def _():
        for r, out in enumerate((p0, p1, p2, p3)):
            out[...] = mat_tn(proj_scr[:, r * rows : (r + 1) * rows], weight[...]).astype(BF16)


def attend_back(parts, grads, weight, draws, draws_ext, hot, kept, after):
    proj, state, mixed, den = kept
    heads, width, model = weight.shape
    rows = parts[0].shape[0]
    total = GROUP * rows
    whole = lambda *shape: pl.BlockSpec(shape, lambda h: (0,) * len(shape))
    by_head = lambda *shape: pl.BlockSpec((None,) + shape, lambda h: (h,) + (0,) * len(shape))
    states = NBUCK * HD + 16
    return pl.pallas_call(
        attend_back_kernel,
        grid=(heads,),
        out_shape=tuple([jax.ShapeDtypeStruct((rows, model), BF16)] * 4)
        + (
            jax.ShapeDtypeStruct((heads, width, model), F32),
            jax.ShapeDtypeStruct((heads, width, 1), F32),
        ),
        in_specs=[whole(rows, model)] * 4
        + [whole(rows, heads * HD)] * 4
        + [
            whole(heads * width, model),
            by_head(FEAT, HD),
            by_head(HD + 16, FEAT),
            whole(16, total),
            by_head(width, total),
            by_head(states, FEAT),
            by_head(HD, total),
            by_head(8, total),
            pl.BlockSpec(memory_space=pl.ANY),
        ],
        out_specs=tuple([whole(rows, model)] * 4) + (by_head(width, model), by_head(width, 1)),
        scratch_shapes=[
            pltpu.VMEM((heads * HD, total), F32),
            pltpu.VMEM((HD + 16, total), BF16),
            pltpu.VMEM((total, HD + 16), BF16),
            pltpu.VMEM((HD + 16, total), BF16),
            pltpu.VMEM((total, HD + 16), BF16),
            pltpu.VMEM((total, total), BF16),
            pltpu.VMEM((total, total), BF16),
            pltpu.VMEM((HD, total), F32),
            pltpu.VMEM((heads * width, total), BF16),
        ],
        compiler_params=pltpu.CompilerParams(vmem_limit_bytes=VMEM),
        cost_estimate=pl.CostEstimate(flops=16_000_000_000, bytes_accessed=10_000_000, transcendentals=0),
        name="attend_back",
    )(*parts, *grads, weight.reshape(heads * width, model), draws, draws_ext, hot, proj, state, mixed, den, after)


def block_kernel(
    mixed, hidden, grad, out_w, rows_ref, up_b, up, down,
    layer_out, resid_out, d0, d1, d2, d3, down_out, up_out, outw_out, vec_out, upb_out,
    resid_scr, in_scr, in_t, acc_out, acc_in, act_scr, pre_scr,
):
    step = pl.program_id(0)
    count = hidden.shape[0] // CHUNK
    spans = [slice(c * CHUNK, (c + 1) * CHUNK) for c in range(count)]

    @pl.when(step == 0)
    def _():
        for span in spans:
            resid = hidden[span].astype(F32) + mat(mixed[span], out_w[...]) + rows_ref[0:1]
            resid_scr[span] = resid
            normed, _ = row_stats(resid)
            inner = normed * rows_ref[1:2] + rows_ref[2:3]
            in_scr[span] = inner.astype(BF16)
            in_t[:, span] = inner.T.astype(BF16)
        acc_out[...] = jnp.zeros_like(acc_out)
        acc_in[...] = jnp.zeros_like(acc_in)

    total = jnp.zeros((1, up.shape[1]), F32)
    for span in spans:
        pre = mat(in_scr[span], up[...]) + up_b[...]
        square = pre * pre
        slope = math.sqrt(2.0 / math.pi)
        tanh = jnp.tanh(pre * (slope + (slope * 0.044715) * square))
        half = 0.5 * (1.0 + tanh)
        act = (pre * half).astype(BF16)
        bend = half + (0.5 * pre) * (1.0 - tanh * tanh) * (slope + (3.0 * slope * 0.044715) * square)
        pre_grad = mat_nt(grad[span], down[...]) * bend
        total = total + jnp.sum(pre_grad, axis=0, keepdims=True)
        pre_low = pre_grad.astype(BF16)
        act_scr[span] = act
        pre_scr[span] = pre_low
        acc_out[span] += mat(act, down[...])
        acc_in[span] += mat_nt(pre_low, up[...])
    upb_out[...] = total
    down_out[...] = mat_tn(act_scr[...], grad[...]).astype(BF16)
    up_out[...] = mat(in_t[...], pre_scr[...]).astype(BF16)

    @pl.when(step == pl.num_programs(0) - 1)
    def _():
        sums = [jnp.zeros((1, hidden.shape[1]), F32) for _ in range(4)]
        for span in spans:
            resid = resid_scr[span]
            layer_out[span] = (resid + acc_out[span] + rows_ref[3:4]).astype(BF16)
            normed, scale = row_stats(resid)
            inner_grad = acc_in[span]
            wide = grad[span].astype(F32)
            resid_grad = wide + norm_back(inner_grad * rows_ref[1:2], normed, scale)
            resid_out[span] = resid_grad
            low = resid_grad.astype(BF16)
            in_scr[span] = low
            for i, term in enumerate((wide, resid_grad, inner_grad * normed, inner_grad)):
                sums[i] = sums[i] + jnp.sum(term, axis=0, keepdims=True)
            back = mat_nt(low, out_w[...]).astype(BF16)
            part = back.shape[1] // GROUP
            for r, out in enumerate((d0, d1, d2, d3)):
                out[span] = back[:, r * part : (r + 1) * part]
        outw_out[...] = mat_tn(mixed[...], in_scr[...]).astype(BF16)
        vec_out[...] = jnp.concatenate(sums + [jnp.zeros((4, hidden.shape[1]), F32)], axis=0)


def block_layer(mixed, hidden, grad, out_w, rows_in, up_b, up, down):
    tokens, model = hidden.shape
    ff = up.shape[1]
    tile = 512
    whole = lambda *shape: pl.BlockSpec(shape, lambda t: (0,) * len(shape))
    part = model // GROUP
    return pl.pallas_call(
        block_kernel,
        grid=(ff // tile,),
        out_shape=(
            jax.ShapeDtypeStruct((tokens, model), BF16),
            jax.ShapeDtypeStruct((tokens, model), F32),
        )
        + tuple([jax.ShapeDtypeStruct((tokens, part), BF16)] * 4)
        + (
            jax.ShapeDtypeStruct((ff, model), BF16),
            jax.ShapeDtypeStruct((model, ff), BF16),
            jax.ShapeDtypeStruct((model, model), BF16),
            jax.ShapeDtypeStruct((8, model), F32),
            jax.ShapeDtypeStruct((1, ff), F32),
        ),
        in_specs=[
            whole(tokens, model), whole(tokens, model), whole(tokens, model), whole(model, model),
            whole(8, model),
            pl.BlockSpec((1, tile), lambda t: (0, t)),
            pl.BlockSpec((model, tile), lambda t: (0, t)),
            pl.BlockSpec((tile, model), lambda t: (t, 0)),
        ],
        out_specs=(whole(tokens, model), whole(tokens, model))
        + tuple([whole(tokens, part)] * 4)
        + (
            pl.BlockSpec((tile, model), lambda t: (t, 0)),
            pl.BlockSpec((model, tile), lambda t: (0, t)),
            whole(model, model),
            whole(8, model),
            pl.BlockSpec((1, tile), lambda t: (0, t)),
        ),
        scratch_shapes=[
            pltpu.VMEM((tokens, model), F32),
            pltpu.VMEM((tokens, model), BF16),
            pltpu.VMEM((model, tokens), BF16),
            pltpu.VMEM((tokens, model), F32),
            pltpu.VMEM((tokens, model), F32),
            pltpu.VMEM((tokens, tile), BF16),
            pltpu.VMEM((tokens, tile), BF16),
        ],
        compiler_params=pltpu.CompilerParams(vmem_limit_bytes=VMEM),
        cost_estimate=pl.CostEstimate(flops=26_000_000_000, bytes_accessed=30_000_000, transcendentals=0),
        name="block_layer",
    )(mixed, hidden, grad, out_w, rows_in, up_b, up, down)


def owner_sum_kernel(dp_size, term, out, landed, send_sem, recv_sem):
    devices = dp_size * GROUP
    me = lax.axis_index("dp") * GROUP + lax.axis_index("feat")
    barrier = pltpu.get_barrier_semaphore()

    def place(k):
        other = lax.rem(me + k, devices)
        return other, (other // GROUP, lax.rem(other, GROUP))

    def greet(k, carry):
        _, spot = place(k)
        pl.semaphore_signal(barrier, inc=1, device_id=spot, device_id_type=pl.DeviceIdType.MESH)
        return carry

    lax.fori_loop(1, devices, greet, 0)
    pl.semaphore_wait(barrier, devices - 1)

    def copy(k):
        other, spot = place(k)
        return pltpu.make_async_remote_copy(
            src_ref=term.at[other],
            dst_ref=landed.at[k],
            send_sem=send_sem.at[k],
            recv_sem=recv_sem.at[k],
            device_id=spot,
            device_id_type=pl.DeviceIdType.MESH,
        )

    def begin(k, carry):
        copy(k).start()
        return carry

    lax.fori_loop(1, devices, begin, 0)
    landed[0] = term[me]

    def finish(k, carry):
        copy(k).wait()
        return carry

    lax.fori_loop(1, devices, finish, 0)
    for f in range(GROUP):
        first = lax.rem(me - f + devices, GROUP)
        total = landed[first].astype(F32)
        for i in range(1, dp_size):
            total = total + landed[first + i * GROUP].astype(F32)
        out[f] = total


def owner_sum(term):
    devices, rows, width = term.shape
    dp_size = devices // GROUP
    return pl.pallas_call(
        lambda *refs: owner_sum_kernel(dp_size, *refs),
        out_shape=jax.ShapeDtypeStruct((GROUP, rows, width), F32),
        in_specs=[pl.BlockSpec(memory_space=pltpu.VMEM)],
        out_specs=pl.BlockSpec(memory_space=pltpu.VMEM),
        scratch_shapes=[
            pltpu.VMEM((devices, rows, width), BF16),
            pltpu.SemaphoreType.DMA((devices,)),
            pltpu.SemaphoreType.DMA((devices,)),
        ],
        compiler_params=pltpu.CompilerParams(
            vmem_limit_bytes=VMEM, collective_id=0, has_side_effects=True
        ),
        name="owner_sum",
    )(term)


def per_device(
    hidden_in, norm1_gain, norm1_bias, qkv_weight, qkv_bias, feature_draws, out_weight, out_bias,
    norm2_gain, norm2_bias, up_weight, up_bias, down_weight, down_bias, block_bucket, out_grad,
):
    seq_count, rows, model = hidden_in.shape
    ff = up_weight.shape[1]
    dp_size = lax.axis_size("dp")
    devices = dp_size * GROUP
    own = lax.axis_index("feat")
    own_x, own_core = own // 2, own % 2
    all_heads = feature_draws.shape[0]
    heads = all_heads // GROUP
    width = 3 * HD

    def swap(values, r):
        return lax.ppermute(values, "feat", [(f, f ^ r) for f in range(GROUP)])

    def at(values, index, axis=0):
        return lax.dynamic_index_in_dim(values, index, axis, keepdims=False)

    def relative(values, axis=0):
        return [at(values, own ^ r, axis) for r in range(GROUP)]

    head_draws = feature_draws.reshape(GROUP, heads, HD, feature_draws.shape[2])
    pieces = [at(head_draws, own)] + [swap(at(head_draws, own ^ r), r) for r in (1, 2, 3)]
    own_draws = jnp.concatenate(pieces, axis=2)
    draws_t = own_draws.transpose(0, 2, 1)
    draws_ext = jnp.concatenate(
        [own_draws, jnp.ones((heads, 1, FEAT), BF16), jnp.zeros((heads, 15, FEAT), BF16)], axis=1
    )
    own_weight = at(qkv_weight.reshape(model, 3, GROUP, heads, HD), own, 2)
    own_weight = own_weight.transpose(2, 1, 3, 0).reshape(heads, width, model)
    own_bias = at(qkv_bias.reshape(3, GROUP, heads, HD), own, 1)
    own_bias = own_bias.transpose(1, 0, 2).reshape(heads, width, 1)
    out_rel = jnp.concatenate(relative(out_weight.reshape(GROUP, heads * HD, model)), axis=0)
    block_ids = block_bucket[..., 0].reshape(seq_count, GROUP, rows // BLOCK)
    block_ids = jnp.concatenate(relative(block_ids, 1), axis=1)
    token_ids = jnp.repeat(block_ids, BLOCK, axis=1)
    hot = (token_ids[:, None, :] == jnp.arange(16, dtype=jnp.int32)[:, None]).astype(BF16)

    parts, mixes, kept = [], [], []
    for s in range(seq_count):
        normed, _ = row_stats(hidden_in[s].astype(F32))
        mine = (normed * norm1_gain + norm1_bias).astype(BF16)
        across = swap(mine, 2)
        parts.append([mine, swap(mine, 1), across, swap(across, 1)])
    for s in range(seq_count):
        mixed_rows, *saved = attend(parts[s], own_weight, own_bias, draws_t, hot[s])
        kept.append(saved)
        blocks = mixed_rows.reshape(GROUP, rows, heads * HD)
        mixes.append(
            jnp.concatenate([blocks[0]] + [swap(blocks[r], r) for r in (1, 2, 3)], axis=1)
        )
    mixed = jnp.concatenate(mixes, axis=0)

    zero = jnp.zeros_like(out_bias)
    rows_in = jnp.stack([out_bias, norm2_gain, norm2_bias, down_bias, zero, zero, zero, zero])
    flat = (seq_count * rows, model)
    layer_out, resid_grad, *mixed_grads, down_term, up_term, out_term, vec_term, up_bias_term = (
        block_layer(
            mixed, hidden_in.reshape(flat), out_grad.reshape(flat), out_rel, rows_in,
            up_bias.reshape(1, ff), up_weight, down_weight,
        )
    )
    layer_out = layer_out.reshape(hidden_in.shape)
    mixed_grads = [term.reshape(seq_count, rows, heads * HD) for term in mixed_grads]
    sent = []
    for s in range(seq_count):
        sent.append([mixed_grads[0][s]] + [swap(mixed_grads[r][s], r) for r in (1, 2, 3)])

    small = model // devices
    out_term = out_term.reshape(2, 2, heads * HD, model)
    out_term = jnp.where(own_x == 1, out_term[::-1], out_term)
    out_term = jnp.where(own_core == 1, out_term[:, ::-1], out_term)
    vectors = [vec_term[0], vec_term[1], vec_term[2], vec_term[3], up_bias_term[0]]
    row = jnp.concatenate([v.reshape(devices, -1) for v in vectors], axis=1)
    row = jnp.pad(row, ((0, 0), (0, -row.shape[1] % model)))
    tail = jnp.concatenate(
        [out_term.reshape(devices, small, model), row.reshape(devices, -1, model).astype(BF16)], axis=1
    )
    ff_rows = ff // devices
    tail = jnp.pad(tail, ((0, 0), (0, -(tail.shape[1] + 2 * ff_rows) % 16), (0, 0)))
    pieces = (down_term.reshape(devices, ff_rows, model), up_term.reshape(devices, ff_rows, model), tail)
    keep, send = [], []
    for piece in pieces:
        pairs = piece.reshape(dp_size, 2, 2, -1, model)
        keep.append(at(pairs, own_core, 2))
        send.append(at(pairs, 1 - own_core, 2))
    met = swap(jnp.concatenate(send, axis=2), 1)
    chip = (jnp.concatenate(keep, axis=2).astype(F32) + met.astype(F32)).astype(BF16)
    lines = lax.psum_scatter(
        chip.reshape(-1, model), "dp", scatter_dimension=0, tiled=True
    ).reshape(2, -1, model)

    terms, weight_terms, bias_terms = [], [], []
    after = chip
    for s in range(seq_count):
        p0, p1, p2, p3, weight_term, bias_term = attend_back(
            parts[s], sent[s], own_weight, draws_t, draws_ext, hot[s], kept[s], after
        )
        weight_terms.append(weight_term)
        bias_terms.append(bias_term)
        chip_own = p0.astype(F32) + swap(p1, 1).astype(F32)
        chip_far = (p2.astype(F32) + swap(p3, 1).astype(F32)).astype(BF16)
        after = chip_far
        terms.append(chip_own + swap(chip_far, 2).astype(F32))

    weight_term = (weight_terms[0] + weight_terms[1] + weight_terms[2]).reshape(
        heads, 3, HD, devices, small
    )
    weight_term = weight_term.transpose(3, 4, 1, 0, 2).reshape(devices, small, 3 * heads * HD)
    bias_term = (bias_terms[0] + bias_terms[1] + bias_terms[2]).reshape(heads, 3, HD)
    bias_term = bias_term.transpose(1, 0, 2).reshape(1, 1, 3 * heads * HD)
    bias_term = jnp.broadcast_to(bias_term, (devices, 1, 3 * heads * HD))
    proj_term = jnp.concatenate([weight_term, bias_term], axis=1).astype(BF16)
    proj_term = jnp.pad(proj_term, ((0, 0), (0, -(small + 1) % 16), (0, 0)))
    grid = owner_sum(proj_term)[:, : small + 1]
    grid = grid.reshape(GROUP, small + 1, 3, heads * HD).transpose(1, 2, 0, 3)
    grid = grid.reshape(small + 1, 3 * model)
    qkv_weight_sum, bias_sum = grid[:-1], grid[-1]

    attn_grad = jnp.stack(terms)
    normed1, scale1 = row_stats(hidden_in.astype(F32))
    input_grad = resid_grad.reshape(hidden_in.shape) + norm_back(
        attn_grad * norm1_gain, normed1, scale1
    )
    index = lax.axis_index("dp") * GROUP + own
    weight_rows = lax.dynamic_slice_in_dim(qkv_weight, index * small, small, 0).astype(F32)
    own_gain = lax.dynamic_slice_in_dim(norm1_gain, index * small, small, 0)
    own_shift = lax.dynamic_slice_in_dim(norm1_bias, index * small, small, 0)
    norm1_bias_sum = jnp.sum(weight_rows * bias_sum, axis=1)
    norm1_gain_sum = jnp.sum(weight_rows * qkv_weight_sum, axis=1)
    norm1_gain_sum = (norm1_gain_sum - own_shift * norm1_bias_sum) / own_gain
    share = 3 * model // devices
    qkv_bias_sum = lax.dynamic_slice_in_dim(bias_sum, index * share, share, 0)

    summed = at(lines, own_x).astype(F32) + swap(at(lines, 1 - own_x), 2).astype(F32)
    down_sum = summed[:ff_rows]
    up_sum = summed[ff_rows : 2 * ff_rows].reshape(small, ff)
    out_weight_sum = summed[2 * ff_rows : 2 * ff_rows + small]
    row_sum = summed[2 * ff_rows + small :].reshape(-1)
    down_bias_sum, out_bias_sum, norm2_gain_sum, norm2_bias_sum = [
        row_sum[i * small : (i + 1) * small] for i in range(4)
    ]
    up_bias_sum = row_sum[4 * small : 4 * small + ff_rows]
    return (
        layer_out, input_grad, norm1_gain_sum, norm1_bias_sum, qkv_weight_sum, qkv_bias_sum,
        out_weight_sum, out_bias_sum, norm2_gain_sum, norm2_bias_sum, up_sum, up_bias_sum,
        down_sum, down_bias_sum,
    )


def solution(mesh):
    both = ("dp", "feat")
    rows = P("dp", "feat", None)
    in_specs = (
        rows, P(), P(), P(), P(), P(None, None, "feat"), P(), P(), P(), P(), P(), P(), P(), P(),
        P("dp", None, None), rows,
    )
    out_specs = (
        rows, rows, P(both), P(both), P(both, None), P(both), P(both, None), P(both), P(both),
        P(both), P(both, None), P(both), P(both, None), P(both),
    )
    return jax.shard_map(
        per_device, mesh=mesh, in_specs=in_specs, out_specs=out_specs, check_vma=False
    )
```

```python
import math

import jax
import jax.numpy as jnp
from jax import lax
from jax.experimental import pallas as pl
from jax.experimental.pallas import tpu as pltpu
from jax.sharding import PartitionSpec as P

HD = 64
FEAT = 256
BLOCK = 64
NBUCK = 4
GROUP = 4
CHUNK = 256
STATES = NBUCK * HD + 16
FAR = 16384.0
VMEM = 60 * 1024 * 1024

F32 = jnp.float32
BF16 = jnp.bfloat16
MESH = pl.DeviceIdType.MESH


def mat(left, right):
    return jnp.dot(left, right, preferred_element_type=F32)


def mat_nt(left, right):
    return lax.dot_general(left, right, (((1,), (1,)), ((), ())), preferred_element_type=F32)


def mat_tn(left, right):
    return lax.dot_general(left, right, (((0,), (0,)), ((), ())), preferred_element_type=F32)


def row_stats(values):
    row_mean = jnp.mean(values, axis=-1, keepdims=True)
    centered = values - row_mean
    scale = lax.rsqrt(jnp.mean(centered * centered, axis=-1, keepdims=True) + 1e-05)
    return (centered * scale, scale)


def norm_back(cotangent, normed, scale):
    mean_one = jnp.mean(cotangent, axis=-1, keepdims=True)
    mean_two = jnp.mean(cotangent * normed, axis=-1, keepdims=True)
    return scale * (cotangent - mean_one - normed * mean_two)


def features(vectors, draws):
    wide = vectors.astype(F32)
    square = jnp.sum(wide * wide, axis=0, keepdims=True) * (0.5 / math.sqrt(HD))
    return jnp.exp(mat_tn(draws, vectors) - square) * (1.0 / math.sqrt(FEAT))


def spread(rows, marks):
    return [rows * marks[u : u + 1] for u in range(NBUCK)]


def pick(stacked, marks):
    total = stacked[0:HD] * marks[0:1]
    for u in range(1, NBUCK):
        total = total + stacked[u * HD : (u + 1) * HD] * marks[u : u + 1]
    return total


def away_marks(hot):
    live = (lax.broadcasted_iota(jnp.int32, hot.shape, 0) < NBUCK).astype(F32)
    return live - hot.astype(F32)


def partner(own, r):
    x, core = own // 2, own % 2
    if r & 2:
        x = 1 - x
    if r & 1:
        core = 1 - core
    return 2 * x + core


def aligned(count):
    return -(-count // 16) * 16


def remote(src, dst, send, recv, place):
    return pltpu.make_async_remote_copy(
        src_ref=src, dst_ref=dst, send_sem=send, recv_sem=recv, device_id=place, device_id_type=MESH
    )


def head_rows(h, kind, heads):
    return pl.ds(pl.multiple_of((kind * heads + h) * HD, HD), HD)


def attend_kernel(
    bucket, hidden, gain, shift, weight_any, bias_ref, draws_in,
    parts_any, mix_any, proj_out, state_out, mixed_out, den_out, hot_out, weight_out, draws_out,
    parts, mix_land, mix_send, raw, bias_scr, draws_land,
    query_scr, key_scr, value_scr, low_scr, gather_scr,
    raw_sem, part_send, part_recv, draw_send, draw_recv, mix_send_sem, mix_recv_sem, out_sem,
):
    s, h = pl.program_id(0), pl.program_id(1)
    seqs, rows, model = hidden.shape
    heads = draws_out.shape[0]
    total = GROUP * rows
    width = heads * HD
    own = lax.axis_index("feat")
    near, across = {"feat": partner(own, 1)}, {"feat": partner(own, 2)}

    def part_copy(q, kind):
        src, dst, place = ((0, 1, near), (0, 2, across), (2, 3, near))[kind]
        return remote(
            parts.at[q, src], parts.at[q, dst], part_send.at[q, kind], part_recv.at[q, kind], place
        )

    def draw_copy(r):
        other = partner(own, r)
        return remote(
            draws_in.at[pl.ds(other * heads, heads)], draws_land.at[r - 1],
            draw_send.at[r - 1], draw_recv.at[r - 1], {"feat": other},
        )

    def mix_copy(q, r):
        return remote(
            mix_send.at[q, r], mix_land.at[q, r], mix_send_sem.at[q, r - 1],
            mix_recv_sem.at[q, r - 1], {"feat": partner(own, r)},
        )

    def raw_copy(j):
        cols = pl.ds(pl.multiple_of(j * model + (own // 2) * 2 * width, 2 * width), 2 * width)
        return pltpu.make_async_copy(weight_any.at[:, cols], raw.at[j], raw_sem.at[j])

    def out_copy(q):
        return pltpu.make_async_copy(parts.at[q], parts_any.at[q], out_sem.at[q])

    @pl.when((s == 0) & (h == 0))
    def _():
        for j in range(3):
            raw_copy(j).start()
        barrier = pltpu.get_barrier_semaphore()
        for r in (1, 2, 3):
            pl.semaphore_signal(
                barrier, inc=1, device_id={"feat": partner(own, r)}, device_id_type=MESH
            )
        first = row_stats(hidden[0].astype(F32))[0] * gain[...] + shift[...]
        parts[0, 0] = first.astype(BF16)
        pl.semaphore_wait(barrier, 3)
        part_copy(0, 1).start()
        part_copy(0, 0).start()
        for r in (1, 2, 3):
            draw_copy(r).start()
        for q in range(1, seqs):
            normed = row_stats(hidden[q].astype(F32))[0] * gain[...] + shift[...]
            parts[q, 0] = normed.astype(BF16)
            part_copy(q, 1).start()
            part_copy(q, 0).start()
        core = own % 2
        for j in range(3):
            raw_copy(j).wait()
            piece = raw[j].astype(F32)
            piece = jnp.where(core == 0, piece[:, 0:width], piece[:, width:])
            weight_out[j * width : (j + 1) * width] = piece.T.astype(BF16)
            cols = pl.ds(pl.multiple_of(j * model + (own // 2) * 2 * width, 2 * width), 2 * width)
            pair = jnp.broadcast_to(bias_ref[:, cols], (128, 2 * width))
            pair = jnp.where(core == 0, pair[:, 0:width], pair[:, width:])
            bias_scr[j * width : (j + 1) * width] = pair.T
        part_copy(0, 1).wait_recv()
        part_copy(0, 2).start()
        for r in (1, 2, 3):
            draw_copy(r).wait_recv()
        mine = draws_in[pl.ds(own * heads, heads)]
        draws_out[...] = jnp.concatenate(
            [mine] + [draws_land[r - 1] for r in (1, 2, 3)], axis=2
        )

    @pl.when(h == 0)
    def _():
        per = rows // BLOCK
        lanes = lax.broadcasted_iota(jnp.int32, (16, total), 1) // BLOCK
        level = lax.broadcasted_iota(jnp.int32, (16, total), 0)
        ids = jnp.full((16, total), -1, jnp.int32)
        for r in range(GROUP):
            for i in range(per):
                ids = jnp.where(
                    lanes == r * per + i, bucket[s, partner(own, r) * per + i], ids
                )
        hot_out[...] = (ids == level).astype(F32).astype(BF16)

        def project(r):
            cols = slice(r * rows, (r + 1) * rows)
            piece = mat_nt(weight_out[...], parts[s, r]) + bias_scr[:, 0:1]
            proj_out[:, cols] = piece.astype(BF16)

        project(0)
        part_copy(s, 0).wait_recv()
        project(1)
        project(2)
        part_copy(s, 2).wait_recv()
        project(3)
        out_copy(s).start()

    query = proj_out[head_rows(h, 0, heads)]
    key = proj_out[head_rows(h, 1, heads)]
    value = proj_out[head_rows(h, 2, heads)]
    draws = draws_out[h]
    hot = hot_out[...]
    hot_wide = hot.astype(F32)
    away = away_marks(hot).astype(BF16)
    phi_q = features(query, draws).astype(BF16)
    phi_k = features(key, draws).astype(BF16)
    spread_value = jnp.concatenate(spread(value, away) + [away], axis=0)
    state = mat_nt(spread_value, phi_k).astype(BF16)
    state_out[...] = state
    low = mat(state, phi_q)
    low_scr[0:HD] = pick(low, hot_wide)
    low_den = jnp.sum(low[NBUCK * HD :] * hot_wide, axis=0, keepdims=True)
    low_scr[HD : HD + 8] = jnp.broadcast_to(low_den, (8, total))
    query_scr[...] = jnp.concatenate([query * (1.0 / math.sqrt(HD)), hot], axis=0).astype(BF16)
    key_scr[...] = jnp.concatenate([key, away * -FAR], axis=0).astype(F32).T.astype(BF16)
    value_scr[0:HD] = value
    value_scr[HD:] = jnp.ones((16, total), BF16)

    def step(c, carry):
        cols = pl.ds(pl.multiple_of(c * CHUNK, CHUNK), CHUNK)
        weights = jnp.exp(mat(key_scr[...], query_scr[:, cols])).astype(BF16)
        exact = mat(value_scr[...], weights)
        den = low_scr[HD : HD + 8, cols] + exact[HD : HD + 8]
        mixed = (low_scr[0:HD, cols] + exact[0:HD]) / den[0:1]
        mixed_out[:, cols] = mixed
        den_out[:, cols] = den
        gather_scr[pl.ds(pl.multiple_of(h * HD, HD), HD), cols] = mixed
        return carry

    lax.fori_loop(0, total // CHUNK, step, 0)

    @pl.when(h == heads - 1)
    def _():
        for r in range(GROUP):
            piece = gather_scr[:, r * rows : (r + 1) * rows].T.astype(BF16)
            if r == 0:
                mix_land[s, 0] = piece
            else:
                mix_send[s, r] = piece
                mix_copy(s, r).start()

        @pl.when(s < seqs - 1)
        def _():
            part_copy(s + 1, 1).wait_recv()
            part_copy(s + 1, 2).start()

    @pl.when((s == seqs - 1) & (h == heads - 1))
    def _():
        for q in range(seqs):
            for r in (1, 2, 3):
                mix_copy(q, r).wait_recv()
        done = pltpu.make_async_copy(mix_land, mix_any, out_sem.at[seqs])
        done.start()
        for q in range(seqs):
            for kind in range(3):
                part_copy(q, kind).wait_send()
            for r in (1, 2, 3):
                mix_copy(q, r).wait_send()
            out_copy(q).wait()
        for r in (1, 2, 3):
            draw_copy(r).wait_send()
        done.wait()


def attend(bucket, hidden, gain, shift, weight, bias, draws):
    seqs, rows, model = hidden.shape
    heads = draws.shape[0] // GROUP
    width = heads * HD
    total = GROUP * rows
    whole = lambda *shape: pl.BlockSpec(shape, lambda s, h: (0,) * len(shape))
    by_seq = lambda *shape: pl.BlockSpec((None,) + shape, lambda s, h: (s,) + (0,) * len(shape))
    by_head = lambda *shape: pl.BlockSpec(
        (None, None) + shape, lambda s, h: (s, h) + (0,) * len(shape)
    )
    anywhere = pl.BlockSpec(memory_space=pl.ANY)
    return pl.pallas_call(
        attend_kernel,
        grid=(seqs, heads),
        out_shape=(
            jax.ShapeDtypeStruct((seqs, GROUP, rows, model), BF16),
            jax.ShapeDtypeStruct((seqs, GROUP, rows, width), BF16),
            jax.ShapeDtypeStruct((seqs, 3 * width, total), BF16),
            jax.ShapeDtypeStruct((seqs, heads, STATES, FEAT), BF16),
            jax.ShapeDtypeStruct((seqs, heads, HD, total), F32),
            jax.ShapeDtypeStruct((seqs, heads, 8, total), F32),
            jax.ShapeDtypeStruct((seqs, 16, total), BF16),
            jax.ShapeDtypeStruct((3 * width, model), BF16),
            jax.ShapeDtypeStruct((heads, HD, FEAT), BF16),
        ),
        in_specs=[
            pl.BlockSpec(memory_space=pltpu.SMEM),
            whole(seqs, rows, model), whole(1, model), whole(1, model), anywhere,
            whole(1, 3 * model), whole(*draws.shape),
        ],
        out_specs=(
            anywhere, anywhere, by_seq(3 * width, total), by_head(STATES, FEAT), by_head(HD, total),
            by_head(8, total), by_seq(16, total), whole(3 * width, model), whole(heads, HD, FEAT),
        ),
        scratch_shapes=[
            pltpu.VMEM((seqs, GROUP, rows, model), BF16),
            pltpu.VMEM((seqs, GROUP, rows, width), BF16),
            pltpu.VMEM((seqs, GROUP, rows, width), BF16),
            pltpu.VMEM((3, model, 2 * width), BF16),
            pltpu.VMEM((3 * width, 128), F32),
            pltpu.VMEM((3, heads, HD, draws.shape[2]), BF16),
            pltpu.VMEM((HD + 16, total), BF16),
            pltpu.VMEM((total, HD + 16), BF16),
            pltpu.VMEM((HD + 16, total), BF16),
            pltpu.VMEM((HD + 8, total), F32),
            pltpu.VMEM((width, total), F32),
            pltpu.SemaphoreType.DMA((3,)),
            pltpu.SemaphoreType.DMA((seqs, 3)),
            pltpu.SemaphoreType.DMA((seqs, 3)),
            pltpu.SemaphoreType.DMA((3,)),
            pltpu.SemaphoreType.DMA((3,)),
            pltpu.SemaphoreType.DMA((seqs, 3)),
            pltpu.SemaphoreType.DMA((seqs, 3)),
            pltpu.SemaphoreType.DMA((seqs + 1,)),
        ],
        compiler_params=pltpu.CompilerParams(
            vmem_limit_bytes=VMEM, collective_id=1, has_side_effects=True
        ),
        cost_estimate=pl.CostEstimate(
            flops=24_000_000_000, bytes_accessed=20_000_000, transcendentals=0
        ),
        name="attend",
    )(bucket, hidden, gain, shift, weight, bias, draws)


def block_kernel(
    direct, parts_ref, hidden, grad, out_w, rows_ref, up_b, up, down,
    layer_out, resid_out, mixed_grad, down_out, up_out, tail_out,
    mixed, resid_scr, in_scr, in_t, acc_out, acc_in, act_scr, pre_scr, vec_scr,
):
    step = pl.program_id(0)
    model = hidden.shape[1]
    count = hidden.shape[0] // CHUNK
    spans = [slice(c * CHUNK, (c + 1) * CHUNK) for c in range(count)]
    subs = [slice(u * model, (u + 1) * model) for u in range(up.shape[1] // model)]
    owners = tail_out.shape[0]
    small = model // owners

    @pl.when(step == 0)
    def _():
        own = lax.axis_index("feat")
        for c, span in enumerate(spans):
            pieces = [parts_ref[c, r] for r in range(GROUP)]
            pieces = [jnp.where(own % 2 == 1, pieces[r ^ 1], pieces[r]) for r in range(GROUP)]
            pieces = [jnp.where(own // 2 == 1, pieces[r ^ 2], pieces[r]) for r in range(GROUP)]
            mixed[span] = jnp.concatenate(pieces, axis=1)
            resid = hidden[span].astype(F32) + mat(mixed[span], out_w[...]) + rows_ref[0:1]
            resid_scr[span] = resid
            normed, _ = row_stats(resid)
            inner = normed * rows_ref[1:2] + rows_ref[2:3]
            in_scr[span] = inner.astype(BF16)
            in_t[:, span] = inner.T.astype(BF16)
        acc_out[...] = jnp.zeros_like(acc_out)
        acc_in[...] = jnp.zeros_like(acc_in)

    slope = math.sqrt(2.0 / math.pi)
    up_terms = []
    for u, sub in enumerate(subs):
        total = jnp.zeros((1, model), F32)
        for span in spans:
            pre = mat(in_scr[span], up[:, sub]) + up_b[:, sub]
            square = pre * pre
            tanh = jnp.tanh(pre * (slope + (slope * 0.044715) * square))
            half = 0.5 * (1.0 + tanh)
            act = (pre * half).astype(BF16)
            bend = half + (0.5 * pre) * (1.0 - tanh * tanh) * (
                slope + (3.0 * slope * 0.044715) * square
            )
            pre_grad = mat_nt(grad[span], down[sub]) * bend
            total = total + jnp.sum(pre_grad, axis=0, keepdims=True)
            pre_low = pre_grad.astype(BF16)
            act_scr[span] = act
            pre_scr[span] = pre_low
            acc_out[span] += mat(act, down[sub])
            acc_in[span] += mat_nt(pre_low, up[:, sub])
        vec_scr[pl.ds(4 + step * len(subs) + u, 1)] = total
        down_term = mat_tn(act_scr[...], grad[...])
        up_term = mat(in_t[...], pre_scr[...])
        if direct:
            share = down_out.shape[1]
            for i in range(model // share):
                down_out[u * (model // share) + i] = down_term[
                    i * share : (i + 1) * share
                ].astype(BF16)
            up_terms.append(up_term)
        else:
            down_out[sub] = down_term.astype(BF16)
            up_out[:, sub] = up_term.astype(BF16)
    if direct:
        for i in range(owners):
            own_rows = slice(i * small, (i + 1) * small)
            up_out[i] = jnp.concatenate([term[own_rows] for term in up_terms], axis=0).astype(BF16)

    @pl.when(step == pl.num_programs(0) - 1)
    def _():
        sums = [jnp.zeros((1, model), F32) for _ in range(4)]
        for span in spans:
            resid = resid_scr[span]
            layer_out[span] = (resid + acc_out[span] + rows_ref[3:4]).astype(BF16)
            normed, scale = row_stats(resid)
            inner_grad = acc_in[span]
            wide = grad[span].astype(F32)
            resid_grad = wide + norm_back(inner_grad * rows_ref[1:2], normed, scale)
            resid_out[span] = resid_grad
            low = resid_grad.astype(BF16)
            in_scr[span] = low
            for i, term in enumerate((wide, resid_grad, inner_grad * normed, inner_grad)):
                sums[i] = sums[i] + jnp.sum(term, axis=0, keepdims=True)
            back = mat_nt(low, out_w[...]).astype(BF16)
            part = model // GROUP
            for a in range(GROUP):
                mixed_grad[a, span] = back[:, a * part : (a + 1) * part]
        for i in range(4):
            vec_scr[i : i + 1] = sums[i]
        out_term = mat_tn(mixed[...], in_scr[...])
        fill = tail_out.shape[1] - small - 8
        extra = [jnp.zeros((fill, model), F32)] if fill else []
        for i in range(owners):
            tail_out[i] = jnp.concatenate(
                [out_term[i * small : (i + 1) * small], vec_scr[...]] + extra, axis=0
            ).astype(BF16)


def block_layer(parts, hidden, grad, out_w, rows_in, up_b, up, down, devices):
    tokens, model = hidden.shape
    ff = up.shape[1]
    steps = 2
    tile = ff // steps
    small, share = model // devices, ff // devices
    direct = small % 8 == 0 and share % 16 == 0
    tail_rows = aligned(small + 8)
    single = pl.Buffered(1)
    whole = lambda *shape: pl.BlockSpec(
        shape, lambda t: (0,) * len(shape), pipeline_mode=single
    )
    part = model // GROUP
    if direct:
        grad_shapes = (
            jax.ShapeDtypeStruct((devices, share, model), BF16),
            jax.ShapeDtypeStruct((devices, ff // model * small, model), BF16),
        )
        grad_specs = (
            pl.BlockSpec((devices // steps, share, model), lambda t: (t, 0, 0)),
            pl.BlockSpec((devices, tile // model * small, model), lambda t: (0, t, 0)),
        )
    else:
        grad_shapes = (
            jax.ShapeDtypeStruct((ff, model), BF16),
            jax.ShapeDtypeStruct((model, ff), BF16),
        )
        grad_specs = (
            pl.BlockSpec((tile, model), lambda t: (t, 0)),
            pl.BlockSpec((model, tile), lambda t: (0, t)),
        )
    layer_out, resid_grad, mixed_grad, down_grad, up_grad, tail = pl.pallas_call(
        lambda *refs: block_kernel(direct, *refs),
        grid=(steps,),
        out_shape=(
            jax.ShapeDtypeStruct((tokens, model), BF16),
            jax.ShapeDtypeStruct((tokens, model), F32),
            jax.ShapeDtypeStruct((GROUP, tokens, part), BF16),
        )
        + grad_shapes
        + (jax.ShapeDtypeStruct((devices, tail_rows, model), BF16),),
        in_specs=[
            whole(*parts.shape), whole(tokens, model), whole(tokens, model), whole(model, model),
            whole(8, model),
            pl.BlockSpec((1, tile), lambda t: (0, t)),
            pl.BlockSpec((model, tile), lambda t: (0, t)),
            pl.BlockSpec((tile, model), lambda t: (t, 0)),
        ],
        out_specs=(whole(tokens, model), whole(tokens, model), whole(GROUP, tokens, part))
        + grad_specs
        + (whole(devices, tail_rows, model),),
        scratch_shapes=[
            pltpu.VMEM((tokens, model), BF16),
            pltpu.VMEM((tokens, model), F32),
            pltpu.VMEM((tokens, model), BF16),
            pltpu.VMEM((model, tokens), BF16),
            pltpu.VMEM((tokens, model), F32),
            pltpu.VMEM((tokens, model), F32),
            pltpu.VMEM((tokens, model), BF16),
            pltpu.VMEM((tokens, model), BF16),
            pltpu.VMEM((8, model), F32),
        ],
        compiler_params=pltpu.CompilerParams(vmem_limit_bytes=VMEM),
        cost_estimate=pl.CostEstimate(
            flops=26_000_000_000, bytes_accessed=30_000_000, transcendentals=0
        ),
        name="block_layer",
    )(parts, hidden, grad, out_w, rows_in, up_b, up, down)
    if not direct:
        fit = lambda a: jnp.pad(a, ((0, 0), (0, aligned(a.shape[1]) - a.shape[1]), (0, 0)))
        down_grad = fit(down_grad.reshape(devices, share, model))
        up_grad = up_grad.reshape(devices, small, ff // model, model).transpose(0, 2, 1, 3)
        up_grad = fit(up_grad.reshape(devices, ff // model * small, model))
    return layer_out, resid_grad, mixed_grad, down_grad, up_grad, tail


def attend_back_kernel(
    dp_size, x_ref, mixed_grad, weight, draws_ref, hot_ref, proj, state_ref, mixed_ref, den_ref,
    hidden, resid_grad, gain, down_any, up_any, tail_any,
    input_out, ring_out, proj_out,
    grad_scr, query_scr, key_scr, num_scr, value_scr, soft_scr, score_scr, exact_scr, proj_scr,
    grad_land, near_send, near_land, far_keep, far_send, far_land,
    mine, met, ring_land, cross_land,
    weight_acc, first_send, last_send, first_land, last_land, part_send, part_land,
    grad_sems, near_sems, far_sems, mine_sem, met_sems, ring_sems, cross_sems, own_sems, part_sems,
):
    s, h = pl.program_id(0), pl.program_id(1)
    seqs, heads = pl.num_programs(0), pl.num_programs(1)
    rows, model = x_ref.shape[1], x_ref.shape[2]
    head_count = proj_scr.shape[0] // (3 * HD)
    width = head_count * HD
    total = GROUP * rows
    root = 1.0 / math.sqrt(HD)
    own, me = lax.axis_index("feat"), lax.axis_index("dp")
    own_x, own_core = own // 2, own % 2
    near, across = {"feat": partner(own, 1)}, {"feat": partner(own, 2)}
    last = (s == seqs - 1) & (h == heads - 1)

    def grad_copy(q, r):
        other = partner(own, r)
        return remote(
            mixed_grad.at[other, pl.ds(q * rows, rows)], grad_land.at[q, r - 1],
            grad_sems.at[0, q, r - 1], grad_sems.at[1, q, r - 1], {"feat": other},
        )

    def near_copy(q, i):
        return remote(
            near_send.at[i], near_land.at[q, i], near_sems.at[0, q, i], near_sems.at[1, q, i], near
        )

    def far_copy(q):
        return remote(far_send, far_land.at[q], far_sems.at[0, q], far_sems.at[1, q], across)

    odd = me % 2
    half = dp_size // 2
    spot = (1 - odd) * (me // 2) + odd * (dp_size - 1 - me // 2)

    def at_spot(p):
        p = lax.rem(p + dp_size, dp_size)
        upper = p // half
        return (1 - upper) * (2 * p) + upper * (2 * (dp_size - 1 - p) + 1)

    def chunk(k, way):
        return at_spot(spot - 1 - k) if way == 0 else at_spot(lax.rem(spot + 1 + k, dp_size))

    sources = (down_any, up_any, tail_any)
    lengths = [ref.shape[1] for ref in sources]
    starts = [sum(lengths[:i]) for i in range(3)]

    def owner(k, way, core):
        return chunk(k, way) * GROUP + 2 * way + core

    def mine_copy(k, way, i):
        return pltpu.make_async_copy(
            sources[i].at[owner(k, way, own_core)],
            mine.at[k, way, pl.ds(starts[i], lengths[i])],
            mine_sem.at[k, way, i],
        )

    def met_copy(k, way, i):
        return remote(
            sources[i].at[owner(k, way, 1 - own_core)],
            met.at[k, way, pl.ds(starts[i], lengths[i])],
            met_sems.at[0, k, way, i], met_sems.at[1, k, way, i], near,
        )

    def ring_copy(k, way):
        place = at_spot(spot + 1) if way == 0 else at_spot(spot - 1)
        return remote(
            mine.at[k, way], ring_land.at[k, way], ring_sems.at[0, k, way], ring_sems.at[1, k, way],
            {"dp": place},
        )

    def cross_copy():
        return remote(
            mine.at[dp_size - 1, 1 - own_x], cross_land, cross_sems.at[0], cross_sems.at[1], across
        )

    def ring_step(k, carry):
        @pl.when(k < dp_size)
        def _():
            for way in range(2):
                for i in range(3):
                    mine_copy(k, way, i).wait()
                    met_copy(k, way, i).wait_recv()
                base = mine[k, way].astype(F32) + met[k, way].astype(F32)

                @pl.when(k == 0)
                def _():
                    mine[k, way] = base.astype(BF16)

                @pl.when(k > 0)
                def _():
                    ring_copy(k - 1, way).wait_recv()
                    mine[k, way] = (base + ring_land[k - 1, way].astype(F32)).astype(BF16)

                @pl.when(k < dp_size - 1)
                def _():
                    ring_copy(k, way).start()

            @pl.when(k == dp_size - 1)
            def _():
                cross_copy().start()

        @pl.when(k == dp_size)
        def _():
            cross_copy().wait_recv()
            ring_out[...] = mine[dp_size - 1, own_x].astype(F32) + cross_land[...].astype(F32)

        return carry

    def own_copy(k, which):
        to = lax.rem(me + k, dp_size)
        src, dst = ((first_send, first_land), (last_send, last_land))[which]
        return remote(
            src.at[to], dst.at[k], own_sems.at[0, which, k], own_sems.at[1, which, k], {"dp": to}
        )

    def part_copy(r):
        other = partner(own, r)
        return remote(
            part_send.at[other], part_land.at[r - 1], part_sems.at[0, r - 1],
            part_sems.at[1, r - 1], {"feat": other},
        )

    def stage(send, lanes):
        base = model // dp_size
        turned = weight_acc[lanes].T
        fill = turned[model : model + send.shape[1] - base]
        for c in range(dp_size):
            send[c] = jnp.concatenate([turned[c * base : (c + 1) * base], fill], axis=0).astype(BF16)

    def begin_own(which):
        def start(k, carry):
            own_copy(k, which).start()
            return carry

        lax.fori_loop(1, dp_size, start, 0)

    def add_near(q):
        near_copy(q, 1).wait_recv()

        @pl.when(q > 0)
        def _():
            far_copy(q - 1).wait_send()

        far_send[...] = (far_keep[1] + near_land[q, 1].astype(F32)).astype(BF16)
        far_copy(q).start()
        near_copy(q, 0).wait_recv()
        far_keep[0] = far_keep[0] + near_land[q, 0].astype(F32)

    def finish(q):
        far_copy(q).wait_recv()
        attn_grad = far_keep[0] + far_land[q].astype(F32)
        normed, scale = row_stats(hidden[q].astype(F32))
        span = pl.ds(pl.multiple_of(q * rows, rows), rows)
        input_out[span] = resid_grad[span] + norm_back(attn_grad * gain[...], normed, scale)

    @pl.when((s == 0) & (h == 0))
    def _():
        barrier = pltpu.get_barrier_semaphore()
        for r in (1, 2, 3):
            pl.semaphore_signal(
                barrier, inc=1, device_id={"feat": partner(own, r)}, device_id_type=MESH
            )

        def greet(k, carry):
            pl.semaphore_signal(
                barrier, inc=1, device_id={"dp": lax.rem(me + k, dp_size)}, device_id_type=MESH
            )
            return carry

        lax.fori_loop(1, dp_size, greet, 0)
        pl.semaphore_wait(barrier, 3 + dp_size - 1)
        for q in range(grad_land.shape[0]):
            for r in (2, 3, 1):
                grad_copy(q, r).start()

        def begin(k, carry):
            for way in range(2):
                for i in range(3):
                    mine_copy(k, way, i).start()
                    met_copy(k, way, i).start()
            return carry

        lax.fori_loop(0, dp_size, begin, 0)
        weight_acc[...] = jnp.zeros_like(weight_acc)

    @pl.when((s > 0) & (h == 0))
    def _():
        add_near(s - 1)

    @pl.when(h == 0)
    def _():
        span = pl.ds(pl.multiple_of(s * rows, rows), rows)
        grad_scr[:, 0:rows] = mixed_grad[own, span].astype(F32).T
        for r in (1, 2, 3):
            grad_copy(s, r).wait_recv()
            grad_scr[:, r * rows : (r + 1) * rows] = grad_land[s, r - 1].astype(F32).T

    query = proj[head_rows(h, 0, head_count)]
    key = proj[head_rows(h, 1, head_count)]
    value = proj[head_rows(h, 2, head_count)]
    draws = draws_ref[...]
    draws_ext = jnp.concatenate([draws, jnp.ones((16, FEAT), BF16)], axis=0)
    hot = hot_ref[...]
    away_wide = away_marks(hot)
    away = away_wide.astype(BF16)
    inverse = 1.0 / den_ref[0:1]
    head_grad = grad_scr[pl.ds(pl.multiple_of(h * HD, HD), HD)]
    grad_num = (head_grad * inverse).astype(BF16)
    grad_den = -jnp.sum(head_grad * mixed_ref[...], axis=0, keepdims=True) * inverse
    den_rows = jnp.broadcast_to(grad_den, (16, total)).astype(BF16)
    spread_grad = jnp.concatenate(spread(grad_num, hot) + [den_rows * hot], axis=0)
    spread_value = jnp.concatenate(spread(value, away) + [away], axis=0)

    wide_q = features(query, draws)
    state_grad = mat_nt(spread_grad, wide_q.astype(BF16)).astype(BF16)
    scaled_q = mat_tn(state_ref[...], spread_grad) * wide_q
    back_q = mat(draws_ext, scaled_q.astype(BF16))
    query_grad = back_q[0:HD] - query.astype(F32) * (back_q[HD : HD + 1] * root)

    wide_k = features(key, draws)
    scaled_k = mat_tn(state_grad, spread_value) * wide_k
    back_k = mat(draws_ext, scaled_k.astype(BF16))
    key_grad = back_k[0:HD] - key.astype(F32) * (back_k[HD : HD + 1] * root)
    value_grad = pick(mat(state_grad[0 : NBUCK * HD], wide_k.astype(BF16)), away_wide)

    query_scr[...] = jnp.concatenate([query * root, hot], axis=0).astype(BF16)
    key_scr[...] = jnp.concatenate([key, away * -FAR], axis=0).astype(F32).T.astype(BF16)
    one = (lax.broadcasted_iota(jnp.int32, hot.shape, 0) < 1).astype(F32).astype(BF16)
    num_scr[...] = jnp.concatenate([grad_num, den_rows], axis=0)
    value_scr[...] = jnp.concatenate([value, one], axis=0).astype(F32).T.astype(BF16)

    def step(c, carry):
        cols = pl.ds(pl.multiple_of(c * CHUNK, CHUNK), CHUNK)
        soft = jnp.exp(mat(key_scr[...], query_scr[:, cols]))
        soft_scr[:, cols] = soft.astype(BF16)
        score = (mat(value_scr[...], num_scr[:, cols]) * soft).astype(BF16)
        score_scr[:, cols] = score
        exact_scr[:, cols] = mat(proj[head_rows(h, 1, head_count)], score)
        return carry

    lax.fori_loop(0, total // CHUNK, step, 0)
    query_grad = query_grad + exact_scr[...] * root
    key_grad = key_grad + mat_nt(query, score_scr[...]) * root
    value_grad = value_grad + mat_nt(grad_num, soft_scr[...])
    for kind, term in enumerate((query_grad, key_grad, value_grad)):
        low = term.astype(BF16)
        proj_scr[head_rows(h, kind, head_count)] = low
        weight_grad = mat(low[:, 0:rows], x_ref[0])
        for r in (1, 2, 3):
            weight_grad = weight_grad + mat(low[:, r * rows : (r + 1) * rows], x_ref[r])
        span = pl.ds(pl.multiple_of((h * 3 + kind) * HD, HD), HD)
        weight_acc[span, 0:model] += weight_grad
        weight_acc[span, model:] += jnp.broadcast_to(
            jnp.sum(term, axis=1, keepdims=True), (HD, 128)
        )

    @pl.when(h == heads - 1)
    def _():
        @pl.when(s > 0)
        def _():
            finish(s - 1)
            for i in range(2):
                near_copy(s - 1, i).wait_send()

        for r in (3, 1, 2, 0):
            term = mat_tn(proj_scr[:, r * rows : (r + 1) * rows], weight[...])
            if r % 2:
                near_send[r // 2] = term.astype(BF16)
                near_copy(s, r // 2).start()
            else:
                far_keep[r // 2] = term

    @pl.when((s == seqs - 1) & (h == heads - 2))
    def _():
        stage(first_send, slice(0, first_send.shape[2]))
        begin_own(0)

    @pl.when(last)
    def _():
        stage(last_send, slice(first_send.shape[2], 3 * width))
        begin_own(1)

    turn = s * heads + h
    count = seqs * heads
    steps = dp_size + 1
    lax.fori_loop(turn * steps // count, (turn + 1) * steps // count, ring_step, 0)

    @pl.when(last)
    def _():
        add_near(s)

        def arrive(k, carry):
            for which in range(2):
                own_copy(k, which).wait_recv()
            return carry

        lax.fori_loop(1, dp_size, arrive, 0)
        sums = []
        for send, land in ((first_send, first_land), (last_send, last_land)):
            sums.append(
                lax.fori_loop(
                    1, dp_size, lambda k, t: t + land[k].astype(F32), send[me].astype(F32)
                )
            )
        joined = jnp.concatenate(sums, axis=1)
        base = model // dp_size
        small = base // GROUP
        fill = jnp.broadcast_to(
            joined[base : base + 1], (part_send.shape[1] - small, joined.shape[1])
        )
        for a in range(GROUP):
            part_send[a] = jnp.concatenate(
                [joined[a * small : (a + 1) * small], fill], axis=0
            ).astype(BF16)
        for r in (2, 3, 1):
            part_copy(r).start()
        finish(s)
        proj_out[own] = part_send[own].astype(F32)
        for r in (1, 2, 3):
            part_copy(r).wait_recv()
            proj_out[partner(own, r)] = part_land[r - 1].astype(F32)

        for q in range(grad_land.shape[0]):
            for r in (1, 2, 3):
                grad_copy(q, r).wait_send()
        for i in range(2):
            near_copy(s, i).wait_send()
        far_copy(s).wait_send()
        for r in (1, 2, 3):
            part_copy(r).wait_send()
        cross_copy().wait_send()

        def leave(k, carry):
            for way in range(2):
                for i in range(3):
                    met_copy(k, way, i).wait_send()
            return carry

        lax.fori_loop(0, dp_size, leave, 0)

        def leave_ring(k, carry):
            for way in range(2):
                ring_copy(k, way).wait_send()
            for which in range(2):
                own_copy(k + 1, which).wait_send()
            return carry

        lax.fori_loop(0, dp_size - 1, leave_ring, 0)


def attend_back(
    dp_size, parts, mixed_grad, weight, draws, hot, proj, state, mixed, den, hidden, resid_grad,
    gain, down_grad, up_grad, tail,
):
    seqs, _, rows, model = parts.shape
    heads = draws.shape[0]
    width = heads * HD
    total = GROUP * rows
    n = dp_size
    ring_rows = down_grad.shape[1] + up_grad.shape[1] + tail.shape[1]
    own_rows = aligned(model // n + 1)
    part_rows = aligned(model // (n * GROUP) + 1)
    early = (heads - 1) * 3 * HD
    single = pl.Buffered(1)
    whole = lambda *shape: pl.BlockSpec(
        shape, lambda s, h: (0,) * len(shape), pipeline_mode=single
    )
    mode = single if n > 16 else None
    by_seq = lambda *shape: pl.BlockSpec(
        (None,) + shape, lambda s, h: (s,) + (0,) * len(shape), pipeline_mode=mode
    )
    by_head = lambda *shape: pl.BlockSpec(
        (None, None) + shape, lambda s, h: (s, h) + (0,) * len(shape)
    )
    anywhere = pl.BlockSpec(memory_space=pl.ANY)
    dma = pltpu.SemaphoreType.DMA
    return pl.pallas_call(
        lambda *refs: attend_back_kernel(dp_size, *refs),
        grid=(seqs, heads),
        out_shape=(
            jax.ShapeDtypeStruct((seqs * rows, model), F32),
            jax.ShapeDtypeStruct((ring_rows, model), F32),
            jax.ShapeDtypeStruct((GROUP, part_rows, 3 * width), F32),
        ),
        in_specs=[
            by_seq(GROUP, rows, model), whole(*mixed_grad.shape), whole(3 * width, model),
            pl.BlockSpec((None, HD, FEAT), lambda s, h: (h, 0, 0)),
            by_seq(16, total), by_seq(3 * width, total), by_head(STATES, FEAT), by_head(HD, total),
            by_head(8, total), whole(seqs, rows, model), whole(seqs * rows, model), whole(1, model),
            anywhere, anywhere, anywhere,
        ],
        out_specs=(
            whole(seqs * rows, model), whole(ring_rows, model), whole(GROUP, part_rows, 3 * width),
        ),
        scratch_shapes=[
            pltpu.VMEM((width, total), F32),
            pltpu.VMEM((HD + 16, total), BF16),
            pltpu.VMEM((total, HD + 16), BF16),
            pltpu.VMEM((HD + 16, total), BF16),
            pltpu.VMEM((total, HD + 16), BF16),
            pltpu.VMEM((total, total), BF16),
            pltpu.VMEM((total, total), BF16),
            pltpu.VMEM((HD, total), F32),
            pltpu.VMEM((3 * width, total), BF16),
            pltpu.VMEM((seqs, 3, rows, width), BF16),
            pltpu.VMEM((2, rows, model), BF16),
            pltpu.VMEM((seqs, 2, rows, model), BF16),
            pltpu.VMEM((2, rows, model), F32),
            pltpu.VMEM((rows, model), BF16),
            pltpu.VMEM((seqs, rows, model), BF16),
            pltpu.VMEM((n, 2, ring_rows, model), BF16),
            pltpu.VMEM((n, 2, ring_rows, model), BF16),
            pltpu.VMEM((n - 1, 2, ring_rows, model), BF16),
            pltpu.VMEM((ring_rows, model), BF16),
            pltpu.VMEM((3 * width, model + 128), F32),
            pltpu.VMEM((n, own_rows, early), BF16),
            pltpu.VMEM((n, own_rows, 3 * width - early), BF16),
            pltpu.VMEM((n, own_rows, early), BF16),
            pltpu.VMEM((n, own_rows, 3 * width - early), BF16),
            pltpu.VMEM((GROUP, part_rows, 3 * width), BF16),
            pltpu.VMEM((3, part_rows, 3 * width), BF16),
            dma((2, seqs, 3)),
            dma((2, seqs, 2)),
            dma((2, seqs)),
            dma((n, 2, 3)),
            dma((2, n, 2, 3)),
            dma((2, n - 1, 2)),
            dma((2,)),
            dma((2, 2, n)),
            dma((2, 3)),
        ],
        compiler_params=pltpu.CompilerParams(
            vmem_limit_bytes=VMEM + (3 * 1024 * 1024 if n > 16 else 0), collective_id=2, has_side_effects=True
        ),
        cost_estimate=pl.CostEstimate(
            flops=48_000_000_000, bytes_accessed=40_000_000, transcendentals=0
        ),
        name="attend_back",
    )(
        parts, mixed_grad, weight, draws, hot, proj, state, mixed, den, hidden, resid_grad, gain,
        down_grad, up_grad, tail,
    )


def per_device(
    hidden_in, norm1_gain, norm1_bias, qkv_weight, qkv_bias, feature_draws, out_weight, out_bias,
    norm2_gain, norm2_bias, up_weight, up_bias, down_weight, down_bias, block_bucket, out_grad,
):
    seqs, rows, model = hidden_in.shape
    ff = up_weight.shape[1]
    dp_size = lax.axis_size("dp")
    devices = dp_size * GROUP
    small, share = model // devices, ff // devices
    heads = feature_draws.shape[0] // GROUP
    flat = (seqs * rows, model)

    parts, mixed_parts, proj, state, mixed, den, hot, own_weight, own_draws = attend(
        block_bucket.reshape(seqs, -1), hidden_in, norm1_gain.reshape(1, model),
        norm1_bias.reshape(1, model), qkv_weight, qkv_bias.reshape(1, 3 * model), feature_draws,
    )
    zero = jnp.zeros_like(out_bias)
    rows_in = jnp.stack([out_bias, norm2_gain, norm2_bias, down_bias, zero, zero, zero, zero])
    layer_out, resid_grad, mixed_grad, down_grad, up_grad, tail = block_layer(
        mixed_parts, hidden_in.reshape(flat), out_grad.reshape(flat), out_weight, rows_in,
        up_bias.reshape(1, ff), up_weight, down_weight, devices,
    )
    input_grad, sums, proj_sums = attend_back(
        dp_size, parts, mixed_grad, own_weight, own_draws, hot, proj, state, mixed, den, hidden_in,
        resid_grad, norm1_gain.reshape(1, model), down_grad, up_grad, tail,
    )

    index = lax.axis_index("dp") * GROUP + lax.axis_index("feat")
    own_slice = lambda values, size: lax.dynamic_slice_in_dim(values, index * size, size, 0)
    down_sum = sums[:share]
    up_sum = sums[down_grad.shape[1] :][: share].reshape(ff // model, small, model)
    up_sum = up_sum.transpose(1, 0, 2).reshape(small, ff)
    rest = sums[down_grad.shape[1] + up_grad.shape[1] :]
    out_weight_sum, vectors = rest[:small], rest[small : small + 8]
    down_bias_sum, out_bias_sum, norm2_gain_sum, norm2_bias_sum = [
        own_slice(vectors[i], small) for i in range(4)
    ]
    up_bias_sum = own_slice(vectors[4:].reshape(ff), share)
    grid = proj_sums[:, : small + 1].reshape(GROUP, small + 1, heads, 3, HD)
    grid = grid.transpose(1, 3, 0, 2, 4).reshape(small + 1, 3 * model)
    qkv_weight_sum, bias_sum = grid[:-1], grid[-1]
    weight_rows = own_slice(qkv_weight, small).astype(F32)
    norm1_bias_sum = jnp.sum(weight_rows * bias_sum, axis=1)
    norm1_gain_sum = jnp.sum(weight_rows * qkv_weight_sum, axis=1)
    norm1_gain_sum = (norm1_gain_sum - own_slice(norm1_bias, small) * norm1_bias_sum) / own_slice(
        norm1_gain, small
    )
    qkv_bias_sum = own_slice(bias_sum, 3 * model // devices)
    return (
        layer_out.reshape(hidden_in.shape), input_grad.reshape(hidden_in.shape), norm1_gain_sum,
        norm1_bias_sum, qkv_weight_sum, qkv_bias_sum, out_weight_sum, out_bias_sum, norm2_gain_sum,
        norm2_bias_sum, up_sum, up_bias_sum, down_sum, down_bias_sum,
    )


def solution(mesh):
    both = ("dp", "feat")
    rows = P("dp", "feat", None)
    in_specs = (
        rows, P(), P(), P(), P(), P(None, None, "feat"), P(), P(), P(), P(), P(), P(), P(), P(),
        P("dp", None, None), rows,
    )
    out_specs = (
        rows, rows, P(both), P(both), P(both, None), P(both), P(both, None), P(both), P(both),
        P(both), P(both, None), P(both), P(both, None), P(both),
    )
    return jax.shard_map(
        per_device, mesh=mesh, in_specs=in_specs, out_specs=out_specs, check_vma=False
    )
```

```python
import math

import jax
import jax.numpy as jnp
from jax import lax
from jax.experimental import pallas as pl
from jax.experimental.pallas import tpu as pltpu
from jax.sharding import PartitionSpec as P

HD = 64
FEAT = 256
BLOCK = 64
NBUCK = 4
GROUP = 4
CHUNK = 256
STATES = NBUCK * HD + 16
FAR = 16384.0
VMEM = 60 * 1024 * 1024

F32 = jnp.float32
BF16 = jnp.bfloat16
MESH = pl.DeviceIdType.MESH


def mat(left, right):
    return jnp.dot(left, right, preferred_element_type=F32)


def mat_nt(left, right):
    return lax.dot_general(left, right, (((1,), (1,)), ((), ())), preferred_element_type=F32)


def mat_tn(left, right):
    return lax.dot_general(left, right, (((0,), (0,)), ((), ())), preferred_element_type=F32)


def row_stats(values):
    row_mean = jnp.mean(values, axis=-1, keepdims=True)
    centered = values - row_mean
    scale = lax.rsqrt(jnp.mean(centered * centered, axis=-1, keepdims=True) + 1e-05)
    return (centered * scale, scale)


def norm_back(cotangent, normed, scale):
    mean_one = jnp.mean(cotangent, axis=-1, keepdims=True)
    mean_two = jnp.mean(cotangent * normed, axis=-1, keepdims=True)
    return scale * (cotangent - mean_one - normed * mean_two)


def features(vectors, draws):
    wide = vectors.astype(F32)
    square = jnp.sum(wide * wide, axis=0, keepdims=True) * (0.5 / math.sqrt(HD))
    return jnp.exp(mat_tn(draws, vectors) - (square + 0.5 * math.log(FEAT)))


def spread(rows, marks):
    return [rows * marks[u : u + 1] for u in range(NBUCK)]


def pick(stacked, marks):
    total = stacked[0:HD] * marks[0:1]
    for u in range(1, NBUCK):
        total = total + stacked[u * HD : (u + 1) * HD] * marks[u : u + 1]
    return total


def away_marks(hot):
    live = (lax.broadcasted_iota(jnp.int32, hot.shape, 0) < NBUCK).astype(F32)
    return live - hot.astype(F32)


def partner(own, r):
    x, core = own // 2, own % 2
    if r & 2:
        x = 1 - x
    if r & 1:
        core = 1 - core
    return 2 * x + core


def aligned(count):
    return -(-count // 16) * 16


def remote(src, dst, send, recv, place):
    return pltpu.make_async_remote_copy(
        src_ref=src, dst_ref=dst, send_sem=send, recv_sem=recv, device_id=place, device_id_type=MESH
    )


def head_rows(h, kind, heads):
    return pl.ds(pl.multiple_of((kind * heads + h) * HD, HD), HD)


def attend_kernel(
    bucket, hidden, gain, shift, weight_any, bias_ref, draws_in,
    parts_any, mix_any, proj_out, state_out, mixed_out, den_out, hot_out, weight_out, draws_out,
    parts, mix_land, mix_send, raw, bias_scr, draws_land,
    query_scr, key_scr, value_scr, low_scr, gather_scr,
    raw_sem, part_send, part_recv, draw_send, draw_recv, mix_send_sem, mix_recv_sem, out_sem,
):
    s, h = pl.program_id(0), pl.program_id(1)
    seqs, rows, model = hidden.shape
    heads = draws_out.shape[0]
    total = GROUP * rows
    width = heads * HD
    own = lax.axis_index("feat")
    near, across = {"feat": partner(own, 1)}, {"feat": partner(own, 2)}

    def part_copy(q, kind):
        src, dst, place = ((0, 1, near), (0, 2, across), (2, 3, near))[kind]
        return remote(
            parts.at[q, src], parts.at[q, dst], part_send.at[q, kind], part_recv.at[q, kind], place
        )

    def draw_copy(r):
        other = partner(own, r)
        return remote(
            draws_in.at[pl.ds(other * heads, heads)], draws_land.at[r - 1],
            draw_send.at[r - 1], draw_recv.at[r - 1], {"feat": other},
        )

    def mix_copy(q, r):
        return remote(
            mix_send.at[q, r], mix_land.at[q, r], mix_send_sem.at[q, r - 1],
            mix_recv_sem.at[q, r - 1], {"feat": partner(own, r)},
        )

    def raw_copy(j):
        cols = pl.ds(pl.multiple_of(j * model + (own // 2) * 2 * width, 2 * width), 2 * width)
        return pltpu.make_async_copy(weight_any.at[:, cols], raw.at[j], raw_sem.at[j])

    def out_copy(q):
        return pltpu.make_async_copy(parts.at[q], parts_any.at[q], out_sem.at[q])

    @pl.when((s == 0) & (h == 0))
    def _():
        for j in range(3):
            raw_copy(j).start()
        barrier = pltpu.get_barrier_semaphore()
        for r in (1, 2, 3):
            pl.semaphore_signal(
                barrier, inc=1, device_id={"feat": partner(own, r)}, device_id_type=MESH
            )
        first = row_stats(hidden[0].astype(F32))[0] * gain[...] + shift[...]
        parts[0, 0] = first.astype(BF16)
        pl.semaphore_wait(barrier, 3)
        part_copy(0, 1).start()
        part_copy(0, 0).start()
        for r in (1, 2, 3):
            draw_copy(r).start()
        for q in range(1, seqs):
            normed = row_stats(hidden[q].astype(F32))[0] * gain[...] + shift[...]
            parts[q, 0] = normed.astype(BF16)
            part_copy(q, 1).start()
            part_copy(q, 0).start()
        core = own % 2
        for j in range(3):
            raw_copy(j).wait()
            piece = raw[j].astype(F32)
            piece = jnp.where(core == 0, piece[:, 0:width], piece[:, width:])
            weight_out[j * width : (j + 1) * width] = piece.T.astype(BF16)
            cols = pl.ds(pl.multiple_of(j * model + (own // 2) * 2 * width, 2 * width), 2 * width)
            pair = jnp.broadcast_to(bias_ref[:, cols], (128, 2 * width))
            pair = jnp.where(core == 0, pair[:, 0:width], pair[:, width:])
            bias_scr[j * width : (j + 1) * width] = pair.T
        part_copy(0, 1).wait_recv()
        part_copy(0, 2).start()
        for r in (1, 2, 3):
            draw_copy(r).wait_recv()
        mine = draws_in[pl.ds(own * heads, heads)]
        draws_out[...] = jnp.concatenate(
            [mine] + [draws_land[r - 1] for r in (1, 2, 3)], axis=2
        )

    @pl.when(h == 0)
    def _():
        per = rows // BLOCK
        lanes = lax.broadcasted_iota(jnp.int32, (16, total), 1) // BLOCK
        level = lax.broadcasted_iota(jnp.int32, (16, total), 0)
        ids = jnp.full((16, total), -1, jnp.int32)
        for r in range(GROUP):
            for i in range(per):
                ids = jnp.where(
                    lanes == r * per + i, bucket[s, partner(own, r) * per + i], ids
                )
        hot_out[...] = (ids == level).astype(F32).astype(BF16)

        def project(r):
            cols = slice(r * rows, (r + 1) * rows)
            piece = mat_nt(weight_out[...], parts[s, r]) + bias_scr[:, 0:1]
            proj_out[:, cols] = piece.astype(BF16)

        project(0)
        part_copy(s, 0).wait_recv()
        project(1)
        project(2)
        part_copy(s, 2).wait_recv()
        project(3)
        out_copy(s).start()

    query = proj_out[head_rows(h, 0, heads)]
    key = proj_out[head_rows(h, 1, heads)]
    value = proj_out[head_rows(h, 2, heads)]
    draws = draws_out[h]
    hot = hot_out[...]
    hot_wide = hot.astype(F32)
    away = away_marks(hot).astype(BF16)
    phi_q = features(query, draws).astype(BF16)
    phi_k = features(key, draws).astype(BF16)
    spread_value = jnp.concatenate(spread(value, away) + [away], axis=0)
    state = mat_nt(spread_value, phi_k).astype(BF16)
    state_out[...] = state
    low = mat(state, phi_q)
    low_scr[0:HD] = pick(low, hot_wide)
    low_den = jnp.sum(low[NBUCK * HD :] * hot_wide, axis=0, keepdims=True)
    low_scr[HD : HD + 8] = jnp.broadcast_to(low_den, (8, total))
    query_scr[...] = jnp.concatenate([query * (1.0 / math.sqrt(HD)), hot], axis=0).astype(BF16)
    key_scr[...] = jnp.concatenate([key, away * -FAR], axis=0).astype(F32).T.astype(BF16)
    value_scr[0:HD] = value
    value_scr[HD:] = jnp.ones((16, total), BF16)

    for c in range(total // CHUNK):
        cols = slice(c * CHUNK, (c + 1) * CHUNK)
        weights = jnp.exp(mat(key_scr[...], query_scr[:, cols])).astype(BF16)
        exact = mat(value_scr[...], weights)
        den = low_scr[HD : HD + 8, cols] + exact[HD : HD + 8]
        mixed = (low_scr[0:HD, cols] + exact[0:HD]) / den[0:1]
        mixed_out[:, cols] = mixed
        den_out[:, cols] = den
        gather_scr[pl.ds(pl.multiple_of(h * HD, HD), HD), cols] = mixed

    @pl.when(h == heads - 1)
    def _():
        for r in range(GROUP):
            piece = gather_scr[:, r * rows : (r + 1) * rows].T.astype(BF16)
            if r == 0:
                mix_land[s, 0] = piece
            else:
                mix_send[s, r] = piece
                mix_copy(s, r).start()

        @pl.when(s < seqs - 1)
        def _():
            part_copy(s + 1, 1).wait_recv()
            part_copy(s + 1, 2).start()

    @pl.when((s == seqs - 1) & (h == heads - 1))
    def _():
        for q in range(seqs):
            for r in (1, 2, 3):
                mix_copy(q, r).wait_recv()
        done = pltpu.make_async_copy(mix_land, mix_any, out_sem.at[seqs])
        done.start()
        for q in range(seqs):
            for kind in range(3):
                part_copy(q, kind).wait_send()
            for r in (1, 2, 3):
                mix_copy(q, r).wait_send()
            out_copy(q).wait()
        for r in (1, 2, 3):
            draw_copy(r).wait_send()
        done.wait()


def attend(bucket, hidden, gain, shift, weight, bias, draws):
    seqs, rows, model = hidden.shape
    heads = draws.shape[0] // GROUP
    width = heads * HD
    total = GROUP * rows
    whole = lambda *shape: pl.BlockSpec(shape, lambda s, h: (0,) * len(shape))
    by_seq = lambda *shape: pl.BlockSpec((None,) + shape, lambda s, h: (s,) + (0,) * len(shape))
    by_head = lambda *shape: pl.BlockSpec(
        (None, None) + shape, lambda s, h: (s, h) + (0,) * len(shape)
    )
    anywhere = pl.BlockSpec(memory_space=pl.ANY)
    return pl.pallas_call(
        attend_kernel,
        grid=(seqs, heads),
        out_shape=(
            jax.ShapeDtypeStruct((seqs, GROUP, rows, model), BF16),
            jax.ShapeDtypeStruct((seqs, GROUP, rows, width), BF16),
            jax.ShapeDtypeStruct((seqs, 3 * width, total), BF16),
            jax.ShapeDtypeStruct((seqs, heads, STATES, FEAT), BF16),
            jax.ShapeDtypeStruct((seqs, heads, HD, total), F32),
            jax.ShapeDtypeStruct((seqs, heads, 8, total), F32),
            jax.ShapeDtypeStruct((seqs, 16, total), BF16),
            jax.ShapeDtypeStruct((3 * width, model), BF16),
            jax.ShapeDtypeStruct((heads, HD, FEAT), BF16),
        ),
        in_specs=[
            pl.BlockSpec(memory_space=pltpu.SMEM),
            whole(seqs, rows, model), whole(1, model), whole(1, model), anywhere,
            whole(1, 3 * model), whole(*draws.shape),
        ],
        out_specs=(
            anywhere, anywhere, by_seq(3 * width, total), by_head(STATES, FEAT), by_head(HD, total),
            by_head(8, total), by_seq(16, total), whole(3 * width, model), whole(heads, HD, FEAT),
        ),
        scratch_shapes=[
            pltpu.VMEM((seqs, GROUP, rows, model), BF16),
            pltpu.VMEM((seqs, GROUP, rows, width), BF16),
            pltpu.VMEM((seqs, GROUP, rows, width), BF16),
            pltpu.VMEM((3, model, 2 * width), BF16),
            pltpu.VMEM((3 * width, 128), F32),
            pltpu.VMEM((3, heads, HD, draws.shape[2]), BF16),
            pltpu.VMEM((HD + 16, total), BF16),
            pltpu.VMEM((total, HD + 16), BF16),
            pltpu.VMEM((HD + 16, total), BF16),
            pltpu.VMEM((HD + 8, total), F32),
            pltpu.VMEM((width, total), F32),
            pltpu.SemaphoreType.DMA((3,)),
            pltpu.SemaphoreType.DMA((seqs, 3)),
            pltpu.SemaphoreType.DMA((seqs, 3)),
            pltpu.SemaphoreType.DMA((3,)),
            pltpu.SemaphoreType.DMA((3,)),
            pltpu.SemaphoreType.DMA((seqs, 3)),
            pltpu.SemaphoreType.DMA((seqs, 3)),
            pltpu.SemaphoreType.DMA((seqs + 1,)),
        ],
        compiler_params=pltpu.CompilerParams(
            vmem_limit_bytes=VMEM, collective_id=1, has_side_effects=True
        ),
        cost_estimate=pl.CostEstimate(
            flops=24_000_000_000, bytes_accessed=20_000_000, transcendentals=0
        ),
        name="attend",
    )(bucket, hidden, gain, shift, weight, bias, draws)


def block_kernel(
    direct, parts_ref, hidden, grad, out_w, rows_ref, up_b, up, down,
    layer_out, resid_out, mixed_grad, down_out, up_out, tail_out,
    mixed, resid_scr, in_scr, in_t, acc_out, acc_in, act_scr, pre_scr, vec_scr,
):
    step = pl.program_id(0)
    model = hidden.shape[1]
    count = hidden.shape[0] // CHUNK
    spans = [slice(c * CHUNK, (c + 1) * CHUNK) for c in range(count)]
    subs = [slice(u * model, (u + 1) * model) for u in range(up.shape[1] // model)]
    owners = tail_out.shape[0]
    small = model // owners

    @pl.when(step == 0)
    def _():
        own = lax.axis_index("feat")
        for c, span in enumerate(spans):
            pieces = [parts_ref[c, r] for r in range(GROUP)]
            pieces = [jnp.where(own % 2 == 1, pieces[r ^ 1], pieces[r]) for r in range(GROUP)]
            pieces = [jnp.where(own // 2 == 1, pieces[r ^ 2], pieces[r]) for r in range(GROUP)]
            mixed[span] = jnp.concatenate(pieces, axis=1)
            resid = hidden[span].astype(F32) + mat(mixed[span], out_w[...]) + rows_ref[0:1]
            resid_scr[span] = resid
            normed, _ = row_stats(resid)
            inner = normed * rows_ref[1:2] + rows_ref[2:3]
            in_scr[span] = inner.astype(BF16)
            in_t[:, span] = inner.T.astype(BF16)
        acc_out[...] = jnp.zeros_like(acc_out)
        acc_in[...] = jnp.zeros_like(acc_in)

    slope = math.sqrt(2.0 / math.pi)
    up_terms = []
    for u, sub in enumerate(subs):
        total = jnp.zeros((1, model), F32)
        for span in spans:
            pre = mat(in_scr[span], up[:, sub]) + up_b[:, sub]
            square = pre * pre
            tanh = jnp.tanh(pre * (slope + (slope * 0.044715) * square))
            half = 0.5 * (1.0 + tanh)
            act = (pre * half).astype(BF16)
            bend = half + (0.5 * pre) * (1.0 - tanh * tanh) * (
                slope + (3.0 * slope * 0.044715) * square
            )
            pre_grad = mat_nt(grad[span], down[sub]) * bend
            total = total + jnp.sum(pre_grad, axis=0, keepdims=True)
            pre_low = pre_grad.astype(BF16)
            act_scr[span] = act
            pre_scr[span] = pre_low
            acc_out[span] += mat(act, down[sub])
            acc_in[span] += mat_nt(pre_low, up[:, sub])
        vec_scr[pl.ds(4 + step * len(subs) + u, 1)] = total
        down_term = mat_tn(act_scr[...], grad[...])
        up_term = mat(in_t[...], pre_scr[...])
        if direct:
            share = down_out.shape[1]
            for i in range(model // share):
                down_out[u * (model // share) + i] = down_term[
                    i * share : (i + 1) * share
                ].astype(BF16)
            up_terms.append(up_term)
        else:
            down_out[sub] = down_term.astype(BF16)
            up_out[:, sub] = up_term.astype(BF16)
    if direct:
        for i in range(owners):
            own_rows = slice(i * small, (i + 1) * small)
            up_out[i] = jnp.concatenate([term[own_rows] for term in up_terms], axis=0).astype(BF16)

    @pl.when(step == pl.num_programs(0) - 1)
    def _():
        sums = [jnp.zeros((1, model), F32) for _ in range(4)]
        for span in spans:
            resid = resid_scr[span]
            layer_out[span] = (resid + acc_out[span] + rows_ref[3:4]).astype(BF16)
            normed, scale = row_stats(resid)
            inner_grad = acc_in[span]
            wide = grad[span].astype(F32)
            resid_grad = wide + norm_back(inner_grad * rows_ref[1:2], normed, scale)
            resid_out[span] = resid_grad
            low = resid_grad.astype(BF16)
            in_scr[span] = low
            for i, term in enumerate((wide, resid_grad, inner_grad * normed, inner_grad)):
                sums[i] = sums[i] + jnp.sum(term, axis=0, keepdims=True)
            back = mat_nt(low, out_w[...]).astype(BF16)
            part = model // GROUP
            for a in range(GROUP):
                mixed_grad[a, span] = back[:, a * part : (a + 1) * part]
        for i in range(4):
            vec_scr[i : i + 1] = sums[i]
        out_term = mat_tn(mixed[...], in_scr[...])
        fill = tail_out.shape[1] - small - 8
        extra = [jnp.zeros((fill, model), F32)] if fill else []
        for i in range(owners):
            tail_out[i] = jnp.concatenate(
                [out_term[i * small : (i + 1) * small], vec_scr[...]] + extra, axis=0
            ).astype(BF16)


def block_layer(parts, hidden, grad, out_w, rows_in, up_b, up, down, devices):
    tokens, model = hidden.shape
    ff = up.shape[1]
    steps = 2
    tile = ff // steps
    small, share = model // devices, ff // devices
    direct = small % 8 == 0 and share % 16 == 0
    tail_rows = aligned(small + 8)
    single = pl.Buffered(1)
    whole = lambda *shape: pl.BlockSpec(
        shape, lambda t: (0,) * len(shape), pipeline_mode=single
    )
    part = model // GROUP
    if direct:
        grad_shapes = (
            jax.ShapeDtypeStruct((devices, share, model), BF16),
            jax.ShapeDtypeStruct((devices, ff // model * small, model), BF16),
        )
        grad_specs = (
            pl.BlockSpec((devices // steps, share, model), lambda t: (t, 0, 0)),
            pl.BlockSpec((devices, tile // model * small, model), lambda t: (0, t, 0)),
        )
    else:
        grad_shapes = (
            jax.ShapeDtypeStruct((ff, model), BF16),
            jax.ShapeDtypeStruct((model, ff), BF16),
        )
        grad_specs = (
            pl.BlockSpec((tile, model), lambda t: (t, 0)),
            pl.BlockSpec((model, tile), lambda t: (0, t)),
        )
    layer_out, resid_grad, mixed_grad, down_grad, up_grad, tail = pl.pallas_call(
        lambda *refs: block_kernel(direct, *refs),
        grid=(steps,),
        out_shape=(
            jax.ShapeDtypeStruct((tokens, model), BF16),
            jax.ShapeDtypeStruct((tokens, model), F32),
            jax.ShapeDtypeStruct((GROUP, tokens, part), BF16),
        )
        + grad_shapes
        + (jax.ShapeDtypeStruct((devices, tail_rows, model), BF16),),
        in_specs=[
            whole(*parts.shape), whole(tokens, model), whole(tokens, model), whole(model, model),
            whole(8, model),
            pl.BlockSpec((1, tile), lambda t: (0, t)),
            pl.BlockSpec((model, tile), lambda t: (0, t)),
            pl.BlockSpec((tile, model), lambda t: (t, 0)),
        ],
        out_specs=(whole(tokens, model), whole(tokens, model), whole(GROUP, tokens, part))
        + grad_specs
        + (whole(devices, tail_rows, model),),
        scratch_shapes=[
            pltpu.VMEM((tokens, model), BF16),
            pltpu.VMEM((tokens, model), F32),
            pltpu.VMEM((tokens, model), BF16),
            pltpu.VMEM((model, tokens), BF16),
            pltpu.VMEM((tokens, model), F32),
            pltpu.VMEM((tokens, model), F32),
            pltpu.VMEM((tokens, model), BF16),
            pltpu.VMEM((tokens, model), BF16),
            pltpu.VMEM((8, model), F32),
        ],
        compiler_params=pltpu.CompilerParams(vmem_limit_bytes=VMEM),
        cost_estimate=pl.CostEstimate(
            flops=26_000_000_000, bytes_accessed=30_000_000, transcendentals=0
        ),
        name="block_layer",
    )(parts, hidden, grad, out_w, rows_in, up_b, up, down)
    if not direct:
        fit = lambda a: jnp.pad(a, ((0, 0), (0, aligned(a.shape[1]) - a.shape[1]), (0, 0)))
        down_grad = fit(down_grad.reshape(devices, share, model))
        up_grad = up_grad.reshape(devices, small, ff // model, model).transpose(0, 2, 1, 3)
        up_grad = fit(up_grad.reshape(devices, ff // model * small, model))
    return layer_out, resid_grad, mixed_grad, down_grad, up_grad, tail


def attend_back_kernel(
    dp_size, x_ref, mixed_grad, weight, draws_ref, hot_ref, proj, state_ref, mixed_ref, den_ref,
    hidden, resid_grad, gain, down_any, up_any, tail_any,
    input_out, ring_out, proj_out,
    grad_scr, query_scr, key_scr, num_scr, value_scr, soft_scr, score_scr, exact_scr, proj_scr,
    grad_land, near_send, near_land, far_keep, far_send, far_land,
    mine, met, ring_land, cross_land,
    weight_acc, first_send, last_send, first_land, last_land, part_send, part_land,
    grad_sems, near_sems, far_sems, mine_sem, met_sems, ring_sems, cross_sems, own_sems, part_sems,
):
    s, h = pl.program_id(0), pl.program_id(1)
    seqs, heads = pl.num_programs(0), pl.num_programs(1)
    rows, model = x_ref.shape[1], x_ref.shape[2]
    head_count = proj_scr.shape[0] // (3 * HD)
    width = head_count * HD
    total = GROUP * rows
    root = 1.0 / math.sqrt(HD)
    own, me = lax.axis_index("feat"), lax.axis_index("dp")
    own_x, own_core = own // 2, own % 2
    near, across = {"feat": partner(own, 1)}, {"feat": partner(own, 2)}
    last = (s == seqs - 1) & (h == heads - 1)

    def grad_copy(q, r):
        other = partner(own, r)
        return remote(
            mixed_grad.at[other, pl.ds(q * rows, rows)], grad_land.at[q, r - 1],
            grad_sems.at[0, q, r - 1], grad_sems.at[1, q, r - 1], {"feat": other},
        )

    def near_copy(q, i):
        return remote(
            near_send.at[i], near_land.at[q, i], near_sems.at[0, q, i], near_sems.at[1, q, i], near
        )

    def far_copy(q):
        return remote(far_send, far_land.at[q], far_sems.at[0, q], far_sems.at[1, q], across)

    odd = me % 2
    half = dp_size // 2
    spot = (1 - odd) * (me // 2) + odd * (dp_size - 1 - me // 2)

    def at_spot(p):
        p = lax.rem(p + dp_size, dp_size)
        upper = p // half
        return (1 - upper) * (2 * p) + upper * (2 * (dp_size - 1 - p) + 1)

    def chunk(k, way):
        return at_spot(spot - 1 - k) if way == 0 else at_spot(lax.rem(spot + 1 + k, dp_size))

    sources = (down_any, up_any, tail_any)
    lengths = [ref.shape[1] for ref in sources]
    starts = [sum(lengths[:i]) for i in range(3)]

    def owner(k, way, core):
        return chunk(k, way) * GROUP + 2 * way + core

    def mine_copy(k, way, i):
        return pltpu.make_async_copy(
            sources[i].at[owner(k, way, own_core)],
            mine.at[k, way, pl.ds(starts[i], lengths[i])],
            mine_sem.at[k, way, i],
        )

    def met_copy(k, way, i):
        return remote(
            sources[i].at[owner(k, way, 1 - own_core)],
            met.at[k, way, pl.ds(starts[i], lengths[i])],
            met_sems.at[0, k, way, i], met_sems.at[1, k, way, i], near,
        )

    def ring_copy(k, way):
        place = at_spot(spot + 1) if way == 0 else at_spot(spot - 1)
        return remote(
            mine.at[k, way], ring_land.at[k, way], ring_sems.at[0, k, way], ring_sems.at[1, k, way],
            {"dp": place},
        )

    def cross_copy():
        return remote(
            mine.at[dp_size - 1, 1 - own_x], cross_land, cross_sems.at[0], cross_sems.at[1], across
        )

    def ring_step(k, carry):
        @pl.when(k < dp_size)
        def _():
            for way in range(2):
                for i in range(3):
                    mine_copy(k, way, i).wait()
                    met_copy(k, way, i).wait_recv()
                base = mine[k, way].astype(F32) + met[k, way].astype(F32)

                @pl.when(k == 0)
                def _():
                    mine[k, way] = base.astype(BF16)

                @pl.when(k > 0)
                def _():
                    ring_copy(k - 1, way).wait_recv()
                    mine[k, way] = (base + ring_land[k - 1, way].astype(F32)).astype(BF16)

                @pl.when(k < dp_size - 1)
                def _():
                    ring_copy(k, way).start()

            @pl.when(k == dp_size - 1)
            def _():
                cross_copy().start()

        @pl.when(k == dp_size)
        def _():
            cross_copy().wait_recv()
            ring_out[...] = mine[dp_size - 1, own_x].astype(F32) + cross_land[...].astype(F32)

        return carry

    def own_copy(k, which):
        to = lax.rem(me + k, dp_size)
        src, dst = ((first_send, first_land), (last_send, last_land))[which]
        return remote(
            src.at[to], dst.at[k], own_sems.at[0, which, k], own_sems.at[1, which, k], {"dp": to}
        )

    def part_copy(r):
        other = partner(own, r)
        return remote(
            part_send.at[other], part_land.at[r - 1], part_sems.at[0, r - 1],
            part_sems.at[1, r - 1], {"feat": other},
        )

    def stage(send, lanes):
        base = model // dp_size
        turned = weight_acc[lanes].T
        fill = turned[model : model + send.shape[1] - base]
        for c in range(dp_size):
            send[c] = jnp.concatenate([turned[c * base : (c + 1) * base], fill], axis=0).astype(BF16)

    def begin_own(which):
        def start(k, carry):
            own_copy(k, which).start()
            return carry

        lax.fori_loop(1, dp_size, start, 0)

    def seq_span(q):
        return pl.ds(pl.multiple_of(q * rows, rows), rows)

    def add_near(q):
        near_copy(q, 1).wait_recv()

        @pl.when(q > 0)
        def _():
            far_copy(q - 1).wait_send()

        far_send[...] = (far_keep[1] + near_land[q, 1].astype(F32)).astype(BF16)
        far_copy(q).start()
        near_copy(q, 0).wait_recv()
        input_out[seq_span(q)] = far_keep[0] + near_land[q, 0].astype(F32)

    def finish(q):
        far_copy(q).wait_recv()
        span = seq_span(q)
        attn_grad = input_out[span] + far_land[q].astype(F32)
        normed, scale = row_stats(hidden[q].astype(F32))
        input_out[span] = resid_grad[span] + norm_back(attn_grad * gain[...], normed, scale)

    @pl.when((s == 0) & (h == 0))
    def _():
        barrier = pltpu.get_barrier_semaphore()
        for r in (1, 2, 3):
            pl.semaphore_signal(
                barrier, inc=1, device_id={"feat": partner(own, r)}, device_id_type=MESH
            )

        def greet(k, carry):
            pl.semaphore_signal(
                barrier, inc=1, device_id={"dp": lax.rem(me + k, dp_size)}, device_id_type=MESH
            )
            return carry

        lax.fori_loop(1, dp_size, greet, 0)
        pl.semaphore_wait(barrier, 3 + dp_size - 1)
        for q in range(grad_land.shape[0]):
            for r in (2, 3, 1):
                grad_copy(q, r).start()

        def begin(k, carry):
            for way in range(2):
                for i in range(3):
                    mine_copy(k, way, i).start()
                    met_copy(k, way, i).start()
            return carry

        lax.fori_loop(0, dp_size, begin, 0)
        weight_acc[...] = jnp.zeros_like(weight_acc)

    @pl.when((s > 0) & (h == 0))
    def _():
        add_near(s - 1)

    @pl.when(h == 0)
    def _():
        span = pl.ds(pl.multiple_of(s * rows, rows), rows)
        grad_scr[:, 0:rows] = mixed_grad[own, span].astype(F32).T
        for r in (1, 2, 3):
            grad_copy(s, r).wait_recv()
            grad_scr[:, r * rows : (r + 1) * rows] = grad_land[s, r - 1].astype(F32).T

    query = proj[head_rows(h, 0, head_count)]
    key = proj[head_rows(h, 1, head_count)]
    value = proj[head_rows(h, 2, head_count)]
    draws = draws_ref[...]
    draws_ext = jnp.concatenate([draws, jnp.ones((16, FEAT), BF16)], axis=0)
    hot = hot_ref[...]
    away_wide = away_marks(hot)
    away = away_wide.astype(BF16)
    inverse = 1.0 / den_ref[0:1]
    head_grad = grad_scr[pl.ds(pl.multiple_of(h * HD, HD), HD)]
    grad_num = (head_grad * inverse).astype(BF16)
    grad_den = -jnp.sum(head_grad * mixed_ref[...], axis=0, keepdims=True) * inverse
    den_rows = jnp.broadcast_to(grad_den, (16, total)).astype(BF16)
    spread_grad = jnp.concatenate(spread(grad_num, hot) + [den_rows * hot], axis=0)
    spread_value = jnp.concatenate(spread(value, away) + [away], axis=0)

    wide_q = features(query, draws)
    state_grad = mat_nt(spread_grad, wide_q.astype(BF16)).astype(BF16)
    scaled_q = mat_tn(state_ref[...], spread_grad) * wide_q
    back_q = mat(draws_ext, scaled_q.astype(BF16))
    query_grad = back_q[0:HD] - query.astype(F32) * (back_q[HD : HD + 1] * root)

    wide_k = features(key, draws)
    scaled_k = mat_tn(state_grad, spread_value) * wide_k
    back_k = mat(draws_ext, scaled_k.astype(BF16))
    key_grad = back_k[0:HD] - key.astype(F32) * (back_k[HD : HD + 1] * root)
    value_grad = pick(mat(state_grad[0 : NBUCK * HD], wide_k.astype(BF16)), away_wide)

    query_scr[...] = jnp.concatenate([query * root, hot], axis=0).astype(BF16)
    key_scr[...] = jnp.concatenate([key, away * -FAR], axis=0).astype(F32).T.astype(BF16)
    one = (lax.broadcasted_iota(jnp.int32, hot.shape, 0) < 1).astype(F32).astype(BF16)
    num_scr[...] = jnp.concatenate([grad_num, den_rows], axis=0)
    value_scr[...] = jnp.concatenate([value, one], axis=0).astype(F32).T.astype(BF16)

    for c in range(total // CHUNK):
        cols = slice(c * CHUNK, (c + 1) * CHUNK)
        soft = jnp.exp(mat(key_scr[...], query_scr[:, cols]))
        soft_scr[:, cols] = soft.astype(BF16)
        score = (mat(value_scr[...], num_scr[:, cols]) * soft).astype(BF16)
        score_scr[:, cols] = score
        exact_scr[:, cols] = mat(proj[head_rows(h, 1, head_count)], score)
    query_grad = query_grad + exact_scr[...] * root
    pair = jnp.concatenate([query, grad_num], axis=0).astype(F32).T
    lane = lax.broadcasted_iota(jnp.int32, pair.shape, 1)
    left = jnp.where(lane < HD, pair, 0.0).astype(BF16)
    right = jnp.where(lane < HD, 0.0, pair).astype(BF16)
    exact_pair = (mat(score_scr[...], left) + mat(soft_scr[...], right)).T
    key_grad = key_grad + exact_pair[0:HD] * root
    value_grad = value_grad + exact_pair[HD:]
    for kind, term in enumerate((query_grad, key_grad, value_grad)):
        low = term.astype(BF16)
        proj_scr[head_rows(h, kind, head_count)] = low
        weight_grad = mat(low[:, 0:rows], x_ref[0])
        for r in (1, 2, 3):
            weight_grad = weight_grad + mat(low[:, r * rows : (r + 1) * rows], x_ref[r])
        span = pl.ds(pl.multiple_of((h * 3 + kind) * HD, HD), HD)
        weight_acc[span, 0:model] += weight_grad
        weight_acc[span, model:] += jnp.broadcast_to(
            jnp.sum(term, axis=1, keepdims=True), (HD, 128)
        )

    @pl.when(h == heads - 1)
    def _():
        @pl.when(s > 0)
        def _():
            for i in range(2):
                near_copy(s - 1, i).wait_send()

        for r in (3, 1, 2, 0):
            term = mat_tn(proj_scr[:, r * rows : (r + 1) * rows], weight[...])
            if r % 2:
                near_send[r // 2] = term.astype(BF16)
                near_copy(s, r // 2).start()
            else:
                far_keep[r // 2] = term

    @pl.when((s == seqs - 1) & (h == heads - 2))
    def _():
        stage(first_send, slice(0, first_send.shape[2]))
        begin_own(0)

    @pl.when(last)
    def _():
        stage(last_send, slice(first_send.shape[2], 3 * width))
        begin_own(1)

    turn = s * heads + h
    count = seqs * heads
    steps = dp_size + 1
    lax.fori_loop(turn * steps // count, (turn + 1) * steps // count, ring_step, 0)

    @pl.when(last)
    def _():
        add_near(s)
        for q in range(grad_land.shape[0] - 1):
            finish(q)

        def arrive(k, carry):
            for which in range(2):
                own_copy(k, which).wait_recv()
            return carry

        lax.fori_loop(1, dp_size, arrive, 0)
        sums = []
        for send, land in ((first_send, first_land), (last_send, last_land)):
            sums.append(
                lax.fori_loop(
                    1, dp_size, lambda k, t: t + land[k].astype(F32), send[me].astype(F32)
                )
            )
        joined = jnp.concatenate(sums, axis=1)
        base = model // dp_size
        small = base // GROUP
        fill = jnp.broadcast_to(
            joined[base : base + 1], (part_send.shape[1] - small, joined.shape[1])
        )
        for a in range(GROUP):
            part_send[a] = jnp.concatenate(
                [joined[a * small : (a + 1) * small], fill], axis=0
            ).astype(BF16)
        for r in (2, 3, 1):
            part_copy(r).start()
        finish(s)
        proj_out[own] = part_send[own].astype(F32)
        for r in (1, 2, 3):
            part_copy(r).wait_recv()
            proj_out[partner(own, r)] = part_land[r - 1].astype(F32)

        for q in range(grad_land.shape[0]):
            for r in (1, 2, 3):
                grad_copy(q, r).wait_send()
        for i in range(2):
            near_copy(s, i).wait_send()
        far_copy(s).wait_send()
        for r in (1, 2, 3):
            part_copy(r).wait_send()
        cross_copy().wait_send()

        def leave(k, carry):
            for way in range(2):
                for i in range(3):
                    met_copy(k, way, i).wait_send()
            return carry

        lax.fori_loop(0, dp_size, leave, 0)

        def leave_ring(k, carry):
            for way in range(2):
                ring_copy(k, way).wait_send()
            for which in range(2):
                own_copy(k + 1, which).wait_send()
            return carry

        lax.fori_loop(0, dp_size - 1, leave_ring, 0)


def attend_back(
    dp_size, parts, mixed_grad, weight, draws, hot, proj, state, mixed, den, hidden, resid_grad,
    gain, down_grad, up_grad, tail,
):
    seqs, _, rows, model = parts.shape
    heads = draws.shape[0]
    width = heads * HD
    total = GROUP * rows
    n = dp_size
    ring_rows = down_grad.shape[1] + up_grad.shape[1] + tail.shape[1]
    own_rows = aligned(model // n + 1)
    part_rows = aligned(model // (n * GROUP) + 1)
    early = (heads - 1) * 3 * HD
    single = pl.Buffered(1)
    whole = lambda *shape: pl.BlockSpec(
        shape, lambda s, h: (0,) * len(shape), pipeline_mode=single
    )
    mode = single if n > 16 else None
    by_seq = lambda *shape: pl.BlockSpec(
        (None,) + shape, lambda s, h: (s,) + (0,) * len(shape), pipeline_mode=mode
    )
    by_head = lambda *shape: pl.BlockSpec(
        (None, None) + shape, lambda s, h: (s, h) + (0,) * len(shape)
    )
    anywhere = pl.BlockSpec(memory_space=pl.ANY)
    dma = pltpu.SemaphoreType.DMA
    return pl.pallas_call(
        lambda *refs: attend_back_kernel(dp_size, *refs),
        grid=(seqs, heads),
        out_shape=(
            jax.ShapeDtypeStruct((seqs * rows, model), F32),
            jax.ShapeDtypeStruct((ring_rows, model), F32),
            jax.ShapeDtypeStruct((GROUP, part_rows, 3 * width), F32),
        ),
        in_specs=[
            by_seq(GROUP, rows, model), whole(*mixed_grad.shape), whole(3 * width, model),
            pl.BlockSpec((None, HD, FEAT), lambda s, h: (h, 0, 0)),
            by_seq(16, total), by_seq(3 * width, total), by_head(STATES, FEAT), by_head(HD, total),
            by_head(8, total), whole(seqs, rows, model), whole(seqs * rows, model), whole(1, model),
            anywhere, anywhere, anywhere,
        ],
        out_specs=(
            whole(seqs * rows, model), whole(ring_rows, model), whole(GROUP, part_rows, 3 * width),
        ),
        scratch_shapes=[
            pltpu.VMEM((width, total), F32),
            pltpu.VMEM((HD + 16, total), BF16),
            pltpu.VMEM((total, HD + 16), BF16),
            pltpu.VMEM((HD + 16, total), BF16),
            pltpu.VMEM((total, HD + 16), BF16),
            pltpu.VMEM((total, total), BF16),
            pltpu.VMEM((total, total), BF16),
            pltpu.VMEM((HD, total), F32),
            pltpu.VMEM((3 * width, total), BF16),
            pltpu.VMEM((seqs, 3, rows, width), BF16),
            pltpu.VMEM((2, rows, model), BF16),
            pltpu.VMEM((seqs, 2, rows, model), BF16),
            pltpu.VMEM((2, rows, model), F32),
            pltpu.VMEM((rows, model), BF16),
            pltpu.VMEM((seqs, rows, model), BF16),
            pltpu.VMEM((n, 2, ring_rows, model), BF16),
            pltpu.VMEM((n, 2, ring_rows, model), BF16),
            pltpu.VMEM((n - 1, 2, ring_rows, model), BF16),
            pltpu.VMEM((ring_rows, model), BF16),
            pltpu.VMEM((3 * width, model + 128), F32),
            pltpu.VMEM((n, own_rows, early), BF16),
            pltpu.VMEM((n, own_rows, 3 * width - early), BF16),
            pltpu.VMEM((n, own_rows, early), BF16),
            pltpu.VMEM((n, own_rows, 3 * width - early), BF16),
            pltpu.VMEM((GROUP, part_rows, 3 * width), BF16),
            pltpu.VMEM((3, part_rows, 3 * width), BF16),
            dma((2, seqs, 3)),
            dma((2, seqs, 2)),
            dma((2, seqs)),
            dma((n, 2, 3)),
            dma((2, n, 2, 3)),
            dma((2, n - 1, 2)),
            dma((2,)),
            dma((2, 2, n)),
            dma((2, 3)),
        ],
        compiler_params=pltpu.CompilerParams(
            vmem_limit_bytes=VMEM + (3 * 1024 * 1024 if n > 16 else 0), collective_id=2, has_side_effects=True
        ),
        cost_estimate=pl.CostEstimate(
            flops=48_000_000_000, bytes_accessed=40_000_000, transcendentals=0
        ),
        name="attend_back",
    )(
        parts, mixed_grad, weight, draws, hot, proj, state, mixed, den, hidden, resid_grad, gain,
        down_grad, up_grad, tail,
    )


def per_device(
    hidden_in, norm1_gain, norm1_bias, qkv_weight, qkv_bias, feature_draws, out_weight, out_bias,
    norm2_gain, norm2_bias, up_weight, up_bias, down_weight, down_bias, block_bucket, out_grad,
):
    seqs, rows, model = hidden_in.shape
    ff = up_weight.shape[1]
    dp_size = lax.axis_size("dp")
    devices = dp_size * GROUP
    small, share = model // devices, ff // devices
    heads = feature_draws.shape[0] // GROUP
    flat = (seqs * rows, model)

    parts, mixed_parts, proj, state, mixed, den, hot, own_weight, own_draws = attend(
        block_bucket.reshape(seqs, -1), hidden_in, norm1_gain.reshape(1, model),
        norm1_bias.reshape(1, model), qkv_weight, qkv_bias.reshape(1, 3 * model), feature_draws,
    )
    zero = jnp.zeros_like(out_bias)
    rows_in = jnp.stack([out_bias, norm2_gain, norm2_bias, down_bias, zero, zero, zero, zero])
    layer_out, resid_grad, mixed_grad, down_grad, up_grad, tail = block_layer(
        mixed_parts, hidden_in.reshape(flat), out_grad.reshape(flat), out_weight, rows_in,
        up_bias.reshape(1, ff), up_weight, down_weight, devices,
    )
    input_grad, sums, proj_sums = attend_back(
        dp_size, parts, mixed_grad, own_weight, own_draws, hot, proj, state, mixed, den, hidden_in,
        resid_grad, norm1_gain.reshape(1, model), down_grad, up_grad, tail,
    )

    index = lax.axis_index("dp") * GROUP + lax.axis_index("feat")
    own_slice = lambda values, size: lax.dynamic_slice_in_dim(values, index * size, size, 0)
    down_sum = sums[:share]
    up_sum = sums[down_grad.shape[1] :][: share].reshape(ff // model, small, model)
    up_sum = up_sum.transpose(1, 0, 2).reshape(small, ff)
    rest = sums[down_grad.shape[1] + up_grad.shape[1] :]
    out_weight_sum, vectors = rest[:small], rest[small : small + 8]
    down_bias_sum, out_bias_sum, norm2_gain_sum, norm2_bias_sum = [
        own_slice(vectors[i], small) for i in range(4)
    ]
    up_bias_sum = own_slice(vectors[4:].reshape(ff), share)
    grid = proj_sums[:, : small + 1].reshape(GROUP, small + 1, heads, 3, HD)
    grid = grid.transpose(1, 3, 0, 2, 4).reshape(small + 1, 3 * model)
    qkv_weight_sum, bias_sum = grid[:-1], grid[-1]
    weight_rows = own_slice(qkv_weight, small).astype(F32)
    norm1_bias_sum = jnp.sum(weight_rows * bias_sum, axis=1)
    norm1_gain_sum = jnp.sum(weight_rows * qkv_weight_sum, axis=1)
    norm1_gain_sum = (norm1_gain_sum - own_slice(norm1_bias, small) * norm1_bias_sum) / own_slice(
        norm1_gain, small
    )
    qkv_bias_sum = own_slice(bias_sum, 3 * model // devices)
    return (
        layer_out.reshape(hidden_in.shape), input_grad.reshape(hidden_in.shape), norm1_gain_sum,
        norm1_bias_sum, qkv_weight_sum, qkv_bias_sum, out_weight_sum, out_bias_sum, norm2_gain_sum,
        norm2_bias_sum, up_sum, up_bias_sum, down_sum, down_bias_sum,
    )


def solution(mesh):
    both = ("dp", "feat")
    rows = P("dp", "feat", None)
    in_specs = (
        rows, P(), P(), P(), P(), P(None, None, "feat"), P(), P(), P(), P(), P(), P(), P(), P(),
        P("dp", None, None), rows,
    )
    out_specs = (
        rows, rows, P(both), P(both), P(both, None), P(both), P(both, None), P(both), P(both),
        P(both), P(both, None), P(both), P(both, None), P(both),
    )
    return jax.shard_map(
        per_device, mesh=mesh, in_specs=in_specs, out_specs=out_specs, check_vma=False
    )
```

```python
import math

import jax
import jax.numpy as jnp
from jax import lax
from jax.experimental import pallas as pl
from jax.experimental.pallas import tpu as pltpu
from jax.sharding import PartitionSpec as P

HD = 64
FEAT = 256
BLOCK = 64
NBUCK = 4
GROUP = 4
CHUNK = 256
STATES = NBUCK * HD + 16
FAR = 16384.0
VMEM = 60 * 1024 * 1024

F32 = jnp.float32
BF16 = jnp.bfloat16
MESH = pl.DeviceIdType.MESH


def mat(left, right):
    return jnp.dot(left, right, preferred_element_type=F32)


def mat_nt(left, right):
    return lax.dot_general(left, right, (((1,), (1,)), ((), ())), preferred_element_type=F32)


def mat_tn(left, right):
    return lax.dot_general(left, right, (((0,), (0,)), ((), ())), preferred_element_type=F32)


def row_stats(values):
    row_mean = jnp.mean(values, axis=-1, keepdims=True)
    centered = values - row_mean
    scale = lax.rsqrt(jnp.mean(centered * centered, axis=-1, keepdims=True) + 1e-05)
    return (centered * scale, scale)


def norm_back(cotangent, normed, scale):
    mean_one = jnp.mean(cotangent, axis=-1, keepdims=True)
    mean_two = jnp.mean(cotangent * normed, axis=-1, keepdims=True)
    return scale * (cotangent - mean_one - normed * mean_two)


def features(vectors, draws):
    wide = vectors.astype(F32)
    square = jnp.sum(wide * wide, axis=0, keepdims=True) * (0.5 / math.sqrt(HD))
    return jnp.exp(mat_tn(draws, vectors) - (square + 0.5 * math.log(FEAT)))


def spread(rows, marks):
    return [rows * marks[u : u + 1] for u in range(NBUCK)]


def pick(stacked, marks):
    total = stacked[0:HD] * marks[0:1]
    for u in range(1, NBUCK):
        total = total + stacked[u * HD : (u + 1) * HD] * marks[u : u + 1]
    return total


def away_marks(hot):
    live = (lax.broadcasted_iota(jnp.int32, hot.shape, 0) < NBUCK).astype(F32)
    return live - hot.astype(F32)


def partner(own, r):
    x, core = own // 2, own % 2
    if r & 2:
        x = 1 - x
    if r & 1:
        core = 1 - core
    return 2 * x + core


def as_row(ref):
    return ref[...].reshape(1, ref.shape[0])


def aligned(count):
    return -(-count // 16) * 16


def remote(src, dst, send, recv, place):
    return pltpu.make_async_remote_copy(
        src_ref=src, dst_ref=dst, send_sem=send, recv_sem=recv, device_id=place, device_id_type=MESH
    )


def head_rows(h, kind, heads):
    return pl.ds(pl.multiple_of((kind * heads + h) * HD, HD), HD)


def attend_kernel(
    bucket, hidden, gain_ref, shift_ref, bias_ref, weight_any, draws_in,
    parts_any, mix_any, proj_out, state_out, mixed_out, den_out, hot_out, weight_out, draws_out,
    soft_out, phi_q_out, phi_k_out,
    parts, mix_land, mix_send, raw, bias_row, bias_scr, draws_land,
    query_scr, key_scr, value_scr, low_scr, gather_scr,
    raw_sem, part_send, part_recv, draw_send, draw_recv, mix_send_sem, mix_recv_sem, out_sem,
):
    s, h = pl.program_id(0), pl.program_id(1)
    seqs, rows, model = hidden.shape
    heads = draws_out.shape[0]
    total = GROUP * rows
    width = heads * HD
    own = lax.axis_index("feat")
    near, across = {"feat": partner(own, 1)}, {"feat": partner(own, 2)}

    def part_copy(q, kind):
        src, dst, place = ((0, 1, near), (0, 2, across), (2, 3, near))[kind]
        return remote(
            parts.at[q, src], parts.at[q, dst], part_send.at[q, kind], part_recv.at[q, kind], place
        )

    def draw_copy(r):
        other = partner(own, r)
        return remote(
            draws_in.at[pl.ds(other * heads, heads)], draws_land.at[r - 1],
            draw_send.at[r - 1], draw_recv.at[r - 1], {"feat": other},
        )

    def mix_copy(q, r):
        return remote(
            mix_send.at[q, r], mix_land.at[q, r], mix_send_sem.at[q, r - 1],
            mix_recv_sem.at[q, r - 1], {"feat": partner(own, r)},
        )

    def raw_copy(j):
        cols = pl.ds(pl.multiple_of(j * model + (own // 2) * 2 * width, 2 * width), 2 * width)
        return pltpu.make_async_copy(weight_any.at[:, cols], raw.at[j], raw_sem.at[j])

    def out_copy(q):
        return pltpu.make_async_copy(parts.at[q], parts_any.at[q], out_sem.at[q])

    @pl.when((s == 0) & (h == 0))
    def _():
        for j in range(3):
            raw_copy(j).start()
        barrier = pltpu.get_barrier_semaphore()
        for r in (1, 2, 3):
            pl.semaphore_signal(
                barrier, inc=1, device_id={"feat": partner(own, r)}, device_id_type=MESH
            )
        gain, shift = as_row(gain_ref), as_row(shift_ref)
        first = row_stats(hidden[0].astype(F32))[0] * gain + shift
        parts[0, 0] = first.astype(BF16)
        pl.semaphore_wait(barrier, 3)
        part_copy(0, 1).start()
        part_copy(0, 0).start()
        for r in (1, 2, 3):
            draw_copy(r).start()
        for q in range(1, seqs):
            normed = row_stats(hidden[q].astype(F32))[0] * gain + shift
            parts[q, 0] = normed.astype(BF16)
        core = own % 2
        bias_row[...] = as_row(bias_ref)
        for j in range(3):
            raw_copy(j).wait()
            piece = raw[j].astype(F32)
            piece = jnp.where(core == 0, piece[:, 0:width], piece[:, width:])
            weight_out[j * width : (j + 1) * width] = piece.T.astype(BF16)
            cols = pl.ds(pl.multiple_of(j * model + (own // 2) * 2 * width, 2 * width), 2 * width)
            pair = jnp.broadcast_to(bias_row[:, cols], (128, 2 * width))
            pair = jnp.where(core == 0, pair[:, 0:width], pair[:, width:])
            bias_scr[j * width : (j + 1) * width] = pair.T
        part_copy(0, 1).wait_recv()
        part_copy(0, 2).start()
        part_copy(1, 1).start()
        part_copy(1, 0).start()
        for r in (1, 2, 3):
            draw_copy(r).wait_recv()
        mine = draws_in[pl.ds(own * heads, heads)]
        draws_out[...] = jnp.concatenate(
            [mine] + [draws_land[r - 1] for r in (1, 2, 3)], axis=2
        )

    @pl.when(h == 0)
    def _():
        per = rows // BLOCK
        lanes = lax.broadcasted_iota(jnp.int32, (16, total), 1) // BLOCK
        level = lax.broadcasted_iota(jnp.int32, (16, total), 0)
        ids = jnp.full((16, total), -1, jnp.int32)
        for r in range(GROUP):
            for i in range(per):
                ids = jnp.where(
                    lanes == r * per + i, bucket[s, partner(own, r) * per + i, 0], ids
                )
        hot_out[...] = (ids == level).astype(F32).astype(BF16)

        def project(r):
            cols = slice(r * rows, (r + 1) * rows)
            piece = mat_nt(weight_out[...], parts[s, r]) + bias_scr[:, 0:1]
            proj_out[:, cols] = piece.astype(BF16)

        project(0)
        part_copy(s, 0).wait_recv()
        project(1)
        project(2)
        part_copy(s, 2).wait_recv()
        project(3)
        out_copy(s).start()

    @pl.when((s > 0) & (s < seqs - 1) & (h == 0))
    def _():
        part_copy(s + 1, 1).start()
        part_copy(s + 1, 0).start()

    query = proj_out[head_rows(h, 0, heads)]
    key = proj_out[head_rows(h, 1, heads)]
    value = proj_out[head_rows(h, 2, heads)]
    draws = draws_out[h]
    hot = hot_out[...]
    hot_wide = hot.astype(F32)
    away = away_marks(hot).astype(BF16)
    phi_q = features(query, draws).astype(BF16)
    phi_k = features(key, draws).astype(BF16)
    phi_q_out[...] = phi_q
    phi_k_out[...] = phi_k
    spread_value = jnp.concatenate(spread(value, away) + [away], axis=0)
    state = mat_nt(spread_value, phi_k).astype(BF16)
    state_out[...] = state
    low = mat(state, phi_q)
    low_scr[0:HD] = pick(low, hot_wide)
    low_den = jnp.sum(low[NBUCK * HD :] * hot_wide, axis=0, keepdims=True)
    low_scr[HD : HD + 8] = jnp.broadcast_to(low_den, (8, total))
    query_scr[...] = jnp.concatenate([query * (1.0 / math.sqrt(HD)), hot], axis=0).astype(BF16)
    key_scr[...] = jnp.concatenate([key, away * -FAR], axis=0).astype(F32).T.astype(BF16)
    value_scr[0:HD] = value
    value_scr[HD:] = jnp.ones((16, total), BF16)

    for c in range(total // CHUNK):
        cols = slice(c * CHUNK, (c + 1) * CHUNK)
        weights = jnp.exp(mat(key_scr[...], query_scr[:, cols])).astype(BF16)
        soft_out[:, cols] = weights
        exact = mat(value_scr[...], weights)
        den = low_scr[HD : HD + 8, cols] + exact[HD : HD + 8]
        mixed = (low_scr[0:HD, cols] + exact[0:HD]) / den[0:1]
        mixed_out[:, cols] = mixed
        den_out[:, cols] = den
        gather_scr[pl.ds(pl.multiple_of(h * HD, HD), HD), cols] = mixed

    @pl.when(h == heads - 1)
    def _():
        for r in range(GROUP):
            piece = gather_scr[:, r * rows : (r + 1) * rows].T.astype(BF16)
            if r == 0:
                mix_land[s, 0] = piece
            else:
                mix_send[s, r] = piece
                mix_copy(s, r).start()

        @pl.when(s < seqs - 1)
        def _():
            part_copy(s + 1, 1).wait_recv()
            part_copy(s + 1, 2).start()

    @pl.when((s == seqs - 1) & (h == heads - 1))
    def _():
        for q in range(seqs):
            for r in (1, 2, 3):
                mix_copy(q, r).wait_recv()
        done = pltpu.make_async_copy(mix_land, mix_any, out_sem.at[seqs])
        done.start()
        for q in range(seqs):
            for kind in range(3):
                part_copy(q, kind).wait_send()
            for r in (1, 2, 3):
                mix_copy(q, r).wait_send()
            out_copy(q).wait()
        for r in (1, 2, 3):
            draw_copy(r).wait_send()
        done.wait()


def attend(bucket, hidden, gain, shift, bias, weight, draws):
    seqs, rows, model = hidden.shape
    heads = draws.shape[0] // GROUP
    width = heads * HD
    total = GROUP * rows
    whole = lambda *shape: pl.BlockSpec(shape, lambda s, h: (0,) * len(shape))
    by_seq = lambda *shape: pl.BlockSpec((None,) + shape, lambda s, h: (s,) + (0,) * len(shape))
    by_head = lambda *shape: pl.BlockSpec(
        (None, None) + shape, lambda s, h: (s, h) + (0,) * len(shape)
    )
    anywhere = pl.BlockSpec(memory_space=pl.ANY)
    return pl.pallas_call(
        attend_kernel,
        grid=(seqs, heads),
        out_shape=(
            jax.ShapeDtypeStruct((seqs, GROUP, rows, model), BF16),
            jax.ShapeDtypeStruct((seqs, GROUP, rows, width), BF16),
            jax.ShapeDtypeStruct((seqs, 3 * width, total), BF16),
            jax.ShapeDtypeStruct((seqs, heads, STATES, FEAT), BF16),
            jax.ShapeDtypeStruct((seqs, heads, HD, total), F32),
            jax.ShapeDtypeStruct((seqs, heads, 8, total), F32),
            jax.ShapeDtypeStruct((seqs, 16, total), BF16),
            jax.ShapeDtypeStruct((3 * width, model), BF16),
            jax.ShapeDtypeStruct((heads, HD, FEAT), BF16),
            jax.ShapeDtypeStruct((seqs, heads, total, total), BF16),
            jax.ShapeDtypeStruct((seqs, heads, FEAT, total), BF16),
            jax.ShapeDtypeStruct((seqs, heads, FEAT, total), BF16),
        ),
        in_specs=[
            pl.BlockSpec(memory_space=pltpu.SMEM),
            whole(seqs, rows, model), whole(model), whole(model), whole(3 * model), anywhere,
            whole(*draws.shape),
        ],
        out_specs=(
            anywhere, anywhere, by_seq(3 * width, total), by_head(STATES, FEAT), by_head(HD, total),
            by_head(8, total), by_seq(16, total), whole(3 * width, model), whole(heads, HD, FEAT),
            by_head(total, total), by_head(FEAT, total), by_head(FEAT, total),
        ),
        scratch_shapes=[
            pltpu.VMEM((seqs, GROUP, rows, model), BF16),
            pltpu.VMEM((seqs, GROUP, rows, width), BF16),
            pltpu.VMEM((seqs, GROUP, rows, width), BF16),
            pltpu.VMEM((3, model, 2 * width), BF16),
            pltpu.VMEM((1, 3 * model), F32),
            pltpu.VMEM((3 * width, 128), F32),
            pltpu.VMEM((3, heads, HD, draws.shape[2]), BF16),
            pltpu.VMEM((HD + 16, total), BF16),
            pltpu.VMEM((total, HD + 16), BF16),
            pltpu.VMEM((HD + 16, total), BF16),
            pltpu.VMEM((HD + 8, total), F32),
            pltpu.VMEM((width, total), F32),
            pltpu.SemaphoreType.DMA((3,)),
            pltpu.SemaphoreType.DMA((seqs, 3)),
            pltpu.SemaphoreType.DMA((seqs, 3)),
            pltpu.SemaphoreType.DMA((3,)),
            pltpu.SemaphoreType.DMA((3,)),
            pltpu.SemaphoreType.DMA((seqs, 3)),
            pltpu.SemaphoreType.DMA((seqs, 3)),
            pltpu.SemaphoreType.DMA((seqs + 1,)),
        ],
        compiler_params=pltpu.CompilerParams(
            vmem_limit_bytes=VMEM, collective_id=1, has_side_effects=True
        ),
        cost_estimate=pl.CostEstimate(
            flops=24_000_000_000, bytes_accessed=20_000_000, transcendentals=0
        ),
        name="attend",
    )(bucket, hidden, gain, shift, bias, weight, draws)


def block_kernel(
    direct, parts_ref, hidden, grad, out_w, out_b, gain_ref, shift_ref, down_b, up_b, up, down,
    layer_out, resid_out, mixed_grad, down_out, up_out, tail_out,
    mixed, resid_scr, in_scr, in_t, acc_out, acc_in, act_scr, pre_scr, vec_scr, bias_row,
):
    step = pl.program_id(0)
    model = hidden.shape[1]
    count = hidden.shape[0] // CHUNK
    spans = [slice(c * CHUNK, (c + 1) * CHUNK) for c in range(count)]
    subs = [slice(u * model, (u + 1) * model) for u in range(up.shape[1] // model)]
    owners = tail_out.shape[0]
    small = model // owners

    @pl.when(step == 0)
    def _():
        own = lax.axis_index("feat")
        for c, span in enumerate(spans):
            pieces = [parts_ref[c, r] for r in range(GROUP)]
            pieces = [jnp.where(own % 2 == 1, pieces[r ^ 1], pieces[r]) for r in range(GROUP)]
            pieces = [jnp.where(own // 2 == 1, pieces[r ^ 2], pieces[r]) for r in range(GROUP)]
            mixed[span] = jnp.concatenate(pieces, axis=1)
            resid = hidden[span].astype(F32) + mat(mixed[span], out_w[...]) + as_row(out_b)
            resid_scr[span] = resid
            normed, _ = row_stats(resid)
            inner = normed * as_row(gain_ref) + as_row(shift_ref)
            in_scr[span] = inner.astype(BF16)
            in_t[:, span] = inner.T.astype(BF16)
        acc_out[...] = jnp.zeros_like(acc_out)
        acc_in[...] = jnp.zeros_like(acc_in)
        bias_row[...] = as_row(up_b)

    slope = math.sqrt(2.0 / math.pi)
    up_terms = []
    for u, sub in enumerate(subs):
        total = jnp.zeros((1, model), F32)
        place = (step * len(subs) + u) * model
        up_bias = bias_row[:, pl.ds(pl.multiple_of(place, model), model)]
        for span in spans:
            pre = mat(in_scr[span], up[:, sub]) + up_bias
            square = pre * pre
            tanh = jnp.tanh(pre * (slope + (slope * 0.044715) * square))
            half = 0.5 * (1.0 + tanh)
            act = (pre * half).astype(BF16)
            bend = half + (0.5 * pre) * (1.0 - tanh * tanh) * (
                slope + (3.0 * slope * 0.044715) * square
            )
            pre_grad = mat_nt(grad[span], down[sub]) * bend
            total = total + jnp.sum(pre_grad, axis=0, keepdims=True)
            pre_low = pre_grad.astype(BF16)
            act_scr[span] = act
            pre_scr[span] = pre_low
            acc_out[span] += mat(act, down[sub])
            acc_in[span] += mat_nt(pre_low, up[:, sub])
        vec_scr[pl.ds(4 + step * len(subs) + u, 1)] = total
        down_term = mat_tn(act_scr[...], grad[...])
        up_term = mat(in_t[...], pre_scr[...])
        if direct:
            share = down_out.shape[1]
            for i in range(model // share):
                down_out[u * (model // share) + i] = down_term[
                    i * share : (i + 1) * share
                ].astype(BF16)
            up_terms.append(up_term)
        else:
            down_out[sub] = down_term.astype(BF16)
            up_out[:, sub] = up_term.astype(BF16)
    if direct:
        for i in range(owners):
            own_rows = slice(i * small, (i + 1) * small)
            up_out[i] = jnp.concatenate([term[own_rows] for term in up_terms], axis=0).astype(BF16)

    @pl.when(step == pl.num_programs(0) - 1)
    def _():
        sums = [jnp.zeros((1, model), F32) for _ in range(4)]
        for span in spans:
            resid = resid_scr[span]
            layer_out[span] = (resid + acc_out[span] + as_row(down_b)).astype(BF16)
            normed, scale = row_stats(resid)
            inner_grad = acc_in[span]
            wide = grad[span].astype(F32)
            resid_grad = wide + norm_back(inner_grad * as_row(gain_ref), normed, scale)
            resid_out[span] = resid_grad
            low = resid_grad.astype(BF16)
            in_scr[span] = low
            for i, term in enumerate((wide, resid_grad, inner_grad * normed, inner_grad)):
                sums[i] = sums[i] + jnp.sum(term, axis=0, keepdims=True)
            back = mat_nt(low, out_w[...]).astype(BF16)
            part = model // GROUP
            for a in range(GROUP):
                mixed_grad[a, span] = back[:, a * part : (a + 1) * part]
        for i in range(4):
            vec_scr[i : i + 1] = sums[i]
        out_term = mat_tn(mixed[...], in_scr[...])
        fill = tail_out.shape[1] - small - 8
        extra = [jnp.zeros((fill, model), F32)] if fill else []
        for i in range(owners):
            tail_out[i] = jnp.concatenate(
                [out_term[i * small : (i + 1) * small], vec_scr[...]] + extra, axis=0
            ).astype(BF16)


def block_layer(parts, hidden, grad, out_w, out_b, gain, shift, down_b, up_b, up, down, devices):
    tokens, model = hidden.shape
    ff = up.shape[1]
    steps = 2
    tile = ff // steps
    small, share = model // devices, ff // devices
    direct = small % 8 == 0 and share % 16 == 0
    tail_rows = aligned(small + 8)
    single = pl.Buffered(1)
    whole = lambda *shape: pl.BlockSpec(
        shape, lambda t: (0,) * len(shape), pipeline_mode=single
    )
    part = model // GROUP
    if direct:
        grad_shapes = (
            jax.ShapeDtypeStruct((devices, share, model), BF16),
            jax.ShapeDtypeStruct((devices, ff // model * small, model), BF16),
        )
        grad_specs = (
            pl.BlockSpec((devices // steps, share, model), lambda t: (t, 0, 0)),
            pl.BlockSpec((devices, tile // model * small, model), lambda t: (0, t, 0)),
        )
    else:
        grad_shapes = (
            jax.ShapeDtypeStruct((ff, model), BF16),
            jax.ShapeDtypeStruct((model, ff), BF16),
        )
        grad_specs = (
            pl.BlockSpec((tile, model), lambda t: (t, 0)),
            pl.BlockSpec((model, tile), lambda t: (0, t)),
        )
    layer_out, resid_grad, mixed_grad, down_grad, up_grad, tail = pl.pallas_call(
        lambda *refs: block_kernel(direct, *refs),
        grid=(steps,),
        out_shape=(
            jax.ShapeDtypeStruct((tokens, model), BF16),
            jax.ShapeDtypeStruct((tokens, model), F32),
            jax.ShapeDtypeStruct((GROUP, tokens, part), BF16),
        )
        + grad_shapes
        + (jax.ShapeDtypeStruct((devices, tail_rows, model), BF16),),
        in_specs=[
            whole(*parts.shape), whole(tokens, model), whole(tokens, model), whole(model, model),
            whole(model), whole(model), whole(model), whole(model), whole(ff),
            pl.BlockSpec((model, tile), lambda t: (0, t)),
            pl.BlockSpec((tile, model), lambda t: (t, 0)),
        ],
        out_specs=(whole(tokens, model), whole(tokens, model), whole(GROUP, tokens, part))
        + grad_specs
        + (whole(devices, tail_rows, model),),
        scratch_shapes=[
            pltpu.VMEM((tokens, model), BF16),
            pltpu.VMEM((tokens, model), F32),
            pltpu.VMEM((tokens, model), BF16),
            pltpu.VMEM((model, tokens), BF16),
            pltpu.VMEM((tokens, model), F32),
            pltpu.VMEM((tokens, model), F32),
            pltpu.VMEM((tokens, model), BF16),
            pltpu.VMEM((tokens, model), BF16),
            pltpu.VMEM((8, model), F32),
            pltpu.VMEM((1, ff), F32),
        ],
        compiler_params=pltpu.CompilerParams(vmem_limit_bytes=VMEM),
        cost_estimate=pl.CostEstimate(
            flops=26_000_000_000, bytes_accessed=30_000_000, transcendentals=0
        ),
        name="block_layer",
    )(parts, hidden, grad, out_w, out_b, gain, shift, down_b, up_b, up, down)
    if not direct:
        fit = lambda a: jnp.pad(a, ((0, 0), (0, aligned(a.shape[1]) - a.shape[1]), (0, 0)))
        down_grad = fit(down_grad.reshape(devices, share, model))
        up_grad = up_grad.reshape(devices, small, ff // model, model).transpose(0, 2, 1, 3)
        up_grad = fit(up_grad.reshape(devices, ff // model * small, model))
    return layer_out, resid_grad, mixed_grad, down_grad, up_grad, tail


def attend_back_kernel(
    dp_size, x_ref, mixed_grad, weight, draws_ref, hot_ref, proj, state_ref, mixed_ref, den_ref,
    soft_ref, phi_q_ref, phi_k_ref, down_any, up_any, tail_any,
    attn_out, ring_out, proj_out,
    grad_scr, num_scr, value_scr, score_scr, exact_scr, proj_scr,
    grad_land, near_send, near_land, far_keep, far_send, far_land,
    mine, met, ring_land, cross_land,
    weight_acc, own_send, pair_land, own_mid, own_land, part_send, part_land,
    grad_sems, near_sems, far_sems, mine_sem, met_sems, ring_sems, cross_sems, pair_sems, own_sems,
    part_sems,
):
    s, h = pl.program_id(0), pl.program_id(1)
    seqs, heads = pl.num_programs(0), pl.num_programs(1)
    rows, model = x_ref.shape[1], x_ref.shape[2]
    head_count = proj_scr.shape[0] // (3 * HD)
    width = head_count * HD
    total = GROUP * rows
    root = 1.0 / math.sqrt(HD)
    own, me = lax.axis_index("feat"), lax.axis_index("dp")
    own_x, own_core = own // 2, own % 2
    near, across = {"feat": partner(own, 1)}, {"feat": partner(own, 2)}
    last = (s == seqs - 1) & (h == heads - 1)

    def grad_copy(q, r):
        other = partner(own, r)
        return remote(
            mixed_grad.at[other, pl.ds(q * rows, rows)], grad_land.at[q, r - 1],
            grad_sems.at[0, q, r - 1], grad_sems.at[1, q, r - 1], {"feat": other},
        )

    def near_copy(q, i):
        return remote(
            near_send.at[i], near_land.at[q, i], near_sems.at[0, q, i], near_sems.at[1, q, i], near
        )

    def far_copy(q):
        return remote(far_send, far_land.at[q], far_sems.at[0, q], far_sems.at[1, q], across)

    odd = me % 2
    half = dp_size // 2
    spot = (1 - odd) * (me // 2) + odd * (dp_size - 1 - me // 2)

    def at_spot(p):
        p = lax.rem(p + dp_size, dp_size)
        upper = p // half
        return (1 - upper) * (2 * p) + upper * (2 * (dp_size - 1 - p) + 1)

    def chunk(k, way):
        return at_spot(spot - 1 - k) if way == 0 else at_spot(lax.rem(spot + 1 + k, dp_size))

    sources = (down_any, up_any, tail_any)
    lengths = [ref.shape[1] for ref in sources]
    starts = [sum(lengths[:i]) for i in range(3)]

    def owner(k, way, core):
        return chunk(k, way) * GROUP + 2 * way + core

    def mine_copy(k, way, i):
        return pltpu.make_async_copy(
            sources[i].at[owner(k, way, own_core)],
            mine.at[k, way, pl.ds(starts[i], lengths[i])],
            mine_sem.at[k, way, i],
        )

    def met_copy(k, way, i):
        return remote(
            sources[i].at[owner(k, way, 1 - own_core)],
            met.at[k, way, pl.ds(starts[i], lengths[i])],
            met_sems.at[0, k, way, i], met_sems.at[1, k, way, i], near,
        )

    def ring_copy(k, way):
        place = at_spot(spot + 1) if way == 0 else at_spot(spot - 1)
        return remote(
            mine.at[k, way], ring_land.at[k, way], ring_sems.at[0, k, way], ring_sems.at[1, k, way],
            {"dp": place},
        )

    def cross_copy():
        return remote(
            mine.at[dp_size - 1, 1 - own_x], cross_land, cross_sems.at[0], cross_sems.at[1], across
        )

    def begin_pieces(k):
        for way in range(2):
            for i in range(3):
                met_copy(k, way, i).start()
                mine_copy(k, way, i).start()

    def ring_step(k, carry):
        @pl.when(k + 2 < dp_size)
        def _():
            begin_pieces(k + 2)

        @pl.when(k < dp_size)
        def _():
            for way in range(2):
                for i in range(3):
                    mine_copy(k, way, i).wait()
                    met_copy(k, way, i).wait_recv()
                base = mine[k, way].astype(F32) + met[k, way].astype(F32)

                @pl.when(k == 0)
                def _():
                    mine[k, way] = base.astype(BF16)

                @pl.when(k > 0)
                def _():
                    ring_copy(k - 1, way).wait_recv()
                    mine[k, way] = (base + ring_land[k - 1, way].astype(F32)).astype(BF16)

                @pl.when(k < dp_size - 1)
                def _():
                    ring_copy(k, way).start()

            @pl.when(k == dp_size - 1)
            def _():
                cross_copy().start()

        @pl.when(k == dp_size)
        def _():
            cross_copy().wait_recv()
            ring_out[...] = mine[dp_size - 1, own_x].astype(F32) + cross_land[...].astype(F32)

        return carry

    parity, pair = me % 2, me // 2
    mate = me + 1 - 2 * parity

    def pair_copy(q):
        return remote(
            own_send.at[q, 1 - parity], pair_land.at[q], pair_sems.at[0, q], pair_sems.at[1, q],
            {"dp": mate},
        )

    def own_copy(q, k):
        to = lax.rem(pair + k, half)
        return remote(
            own_mid.at[q, to], own_land.at[q, k], own_sems.at[0, q, k], own_sems.at[1, q, k],
            {"dp": 2 * to + parity},
        )

    def begin_own(q):
        base = model // dp_size
        turned = weight_acc[pl.ds(pl.multiple_of(q * 3 * HD, 3 * HD), 3 * HD)].T
        fill = turned[model : model + own_send.shape[3] - base]
        for c in range(dp_size):
            own_send[q, c % 2, c // 2] = jnp.concatenate(
                [turned[c * base : (c + 1) * base], fill], axis=0
            ).astype(BF16)
        pair_copy(q).start()

    def relay_own(q):
        pair_copy(q).wait_recv()
        own_mid[q] = (own_send[q, parity].astype(F32) + pair_land[q].astype(F32)).astype(BF16)

        def start(k, carry):
            own_copy(q, k).start()
            return carry

        lax.fori_loop(1, half, start, 0)

    def part_copy(r):
        other = partner(own, r)
        return remote(
            part_send.at[other], part_land.at[r - 1], part_sems.at[0, r - 1],
            part_sems.at[1, r - 1], {"feat": other},
        )

    def seq_span(q):
        return pl.ds(pl.multiple_of(q * rows, rows), rows)

    def add_near(q):
        near_copy(q, 1).wait_recv()

        @pl.when(q > 0)
        def _():
            far_copy(q - 1).wait_send()

        far_send[...] = (far_keep[1] + near_land[q, 1].astype(F32)).astype(BF16)
        far_copy(q).start()
        near_copy(q, 0).wait_recv()
        attn_out[seq_span(q)] = far_keep[0] + near_land[q, 0].astype(F32)

    def finish(q):
        far_copy(q).wait_recv()
        span = seq_span(q)
        attn_out[span] = attn_out[span] + far_land[q].astype(F32)

    @pl.when((s == 0) & (h == 0))
    def _():
        barrier = pltpu.get_barrier_semaphore()
        for r in (1, 2, 3):
            pl.semaphore_signal(
                barrier, inc=1, device_id={"feat": partner(own, r)}, device_id_type=MESH
            )

        def greet(k, carry):
            pl.semaphore_signal(
                barrier, inc=1, device_id={"dp": lax.rem(me + k, dp_size)}, device_id_type=MESH
            )
            return carry

        lax.fori_loop(1, dp_size, greet, 0)
        pl.semaphore_wait(barrier, 3 + dp_size - 1)
        for r in (2, 3, 1):
            grad_copy(0, r).start()
        for k in range(2):
            begin_pieces(k)
        weight_acc[...] = jnp.zeros_like(weight_acc)

    @pl.when(h == 0)
    def _():
        span = pl.ds(pl.multiple_of(s * rows, rows), rows)
        grad_scr[:, 0:rows] = mixed_grad[own, span].astype(F32).T
        for r in (1, 2, 3):
            grad_copy(s, r).wait_recv()
            grad_scr[:, r * rows : (r + 1) * rows] = grad_land[s, r - 1].astype(F32).T

        @pl.when(s < seqs - 1)
        def _():
            for r in (2, 3, 1):
                grad_copy(s + 1, r).start()

    query = proj[head_rows(h, 0, head_count)]
    key = proj[head_rows(h, 1, head_count)]
    value = proj[head_rows(h, 2, head_count)]
    draws = draws_ref[...]
    draws_ext = jnp.concatenate([draws, jnp.ones((16, FEAT), BF16)], axis=0)
    hot = hot_ref[...]
    away_wide = away_marks(hot)
    away = away_wide.astype(BF16)
    inverse = 1.0 / den_ref[0:1]
    head_grad = grad_scr[pl.ds(pl.multiple_of(h * HD, HD), HD)]
    grad_num = (head_grad * inverse).astype(BF16)
    grad_den = -jnp.sum(head_grad * mixed_ref[...], axis=0, keepdims=True) * inverse
    den_rows = jnp.broadcast_to(grad_den, (16, total)).astype(BF16)
    spread_grad = jnp.concatenate(spread(grad_num, hot) + [den_rows * hot], axis=0)
    spread_value = jnp.concatenate(spread(value, away) + [away], axis=0)

    phi_q = phi_q_ref[...]
    state_grad = mat_nt(spread_grad, phi_q).astype(BF16)
    scaled_q = mat_tn(state_ref[...], spread_grad) * phi_q.astype(F32)
    back_q = mat(draws_ext, scaled_q.astype(BF16))
    query_grad = back_q[0:HD] - query.astype(F32) * (back_q[HD : HD + 1] * root)

    phi_k = phi_k_ref[...]
    scaled_k = mat_tn(state_grad, spread_value) * phi_k.astype(F32)
    back_k = mat(draws_ext, scaled_k.astype(BF16))
    key_grad = back_k[0:HD] - key.astype(F32) * (back_k[HD : HD + 1] * root)
    value_grad = pick(mat(state_grad[0 : NBUCK * HD], phi_k), away_wide)

    one = (lax.broadcasted_iota(jnp.int32, hot.shape, 0) < 1).astype(F32).astype(BF16)
    num_scr[...] = jnp.concatenate([grad_num, den_rows], axis=0)
    value_scr[...] = jnp.concatenate([value, one], axis=0).astype(F32).T.astype(BF16)

    for c in range(total // CHUNK):
        cols = slice(c * CHUNK, (c + 1) * CHUNK)
        score = mat(value_scr[...], num_scr[:, cols]) * soft_ref[:, cols].astype(F32)
        score = score.astype(BF16)
        score_scr[:, cols] = score
        exact_scr[:, cols] = mat(proj[head_rows(h, 1, head_count)], score)
    query_grad = query_grad + exact_scr[...] * root
    joint = jnp.concatenate([query, grad_num], axis=0).astype(F32).T
    lane = lax.broadcasted_iota(jnp.int32, joint.shape, 1)
    left = jnp.where(lane < HD, joint, 0.0).astype(BF16)
    right = jnp.where(lane < HD, 0.0, joint).astype(BF16)
    exact_pair = (mat(score_scr[...], left) + mat(soft_ref[...], right)).T
    key_grad = key_grad + exact_pair[0:HD] * root
    value_grad = value_grad + exact_pair[HD:]
    wide_grad = jnp.concatenate([query_grad, key_grad, value_grad], axis=0)
    low_grad = wide_grad.astype(BF16)
    for kind in range(3):
        proj_scr[head_rows(h, kind, head_count)] = low_grad[kind * HD : (kind + 1) * HD]
    weight_grad = mat(low_grad[:, 0:rows], x_ref[0])
    for r in (1, 2, 3):
        weight_grad = weight_grad + mat(low_grad[:, r * rows : (r + 1) * rows], x_ref[r])
    span = pl.ds(pl.multiple_of(h * 3 * HD, 3 * HD), 3 * HD)
    weight_acc[span, 0:model] += weight_grad
    weight_acc[span, model:] += jnp.broadcast_to(
        jnp.sum(wide_grad, axis=1, keepdims=True), (3 * HD, 128)
    )

    @pl.when((s > 0) & (h == 0))
    def _():
        add_near(s - 1)

    @pl.when(h == heads - 1)
    def _():
        @pl.when(s > 0)
        def _():
            for i in range(2):
                near_copy(s - 1, i).wait_send()

        for r in (3, 1, 2, 0):
            term = mat_tn(proj_scr[:, r * rows : (r + 1) * rows], weight[...])
            if r % 2:
                near_send[r // 2] = term.astype(BF16)
                near_copy(s, r // 2).start()
            else:
                far_keep[r // 2] = term

    @pl.when(s == seqs - 1)
    def _():
        begin_own(h)

        @pl.when(h > 0)
        def _():
            relay_own(h - 1)

    turn = s * heads + h
    count = seqs * heads
    steps = dp_size + 1
    lax.fori_loop(turn * steps // count, (turn + 1) * steps // count, ring_step, 0)

    @pl.when(last)
    def _():
        add_near(s)
        relay_own(h)
        for q in range(grad_land.shape[0] - 1):
            finish(q)

        sums = []
        for q in range(head_count):

            def arrive(k, carry):
                own_copy(q, k).wait_recv()
                return carry + own_land[q, k].astype(F32)

            sums.append(lax.fori_loop(1, half, arrive, own_mid[q, pair].astype(F32)))
        joined = jnp.concatenate(sums, axis=1)
        base = model // dp_size
        small = base // GROUP
        fill = jnp.broadcast_to(
            joined[base : base + 1], (part_send.shape[1] - small, joined.shape[1])
        )
        for a in range(GROUP):
            part_send[a] = jnp.concatenate(
                [joined[a * small : (a + 1) * small], fill], axis=0
            ).astype(BF16)
        for r in (2, 3, 1):
            part_copy(r).start()
        finish(s)
        proj_out[own] = part_send[own].astype(F32)
        for r in (1, 2, 3):
            part_copy(r).wait_recv()
            proj_out[partner(own, r)] = part_land[r - 1].astype(F32)

        for q in range(grad_land.shape[0]):
            for r in (1, 2, 3):
                grad_copy(q, r).wait_send()
        for i in range(2):
            near_copy(s, i).wait_send()
        far_copy(s).wait_send()
        for r in (1, 2, 3):
            part_copy(r).wait_send()
        cross_copy().wait_send()

        def leave(k, carry):
            for way in range(2):
                for i in range(3):
                    met_copy(k, way, i).wait_send()
            return carry

        lax.fori_loop(0, dp_size, leave, 0)

        def leave_ring(k, carry):
            for way in range(2):
                ring_copy(k, way).wait_send()
            return carry

        lax.fori_loop(0, dp_size - 1, leave_ring, 0)
        for q in range(head_count):
            pair_copy(q).wait_send()

            def leave_own(k, carry):
                own_copy(q, k).wait_send()
                return carry

            lax.fori_loop(1, half, leave_own, 0)


def attend_back(
    dp_size, parts, mixed_grad, weight, draws, hot, proj, state, mixed, den, soft, phi_q, phi_k,
    down_grad, up_grad, tail,
):
    seqs, _, rows, model = parts.shape
    heads = draws.shape[0]
    width = heads * HD
    total = GROUP * rows
    n = dp_size
    ring_rows = down_grad.shape[1] + up_grad.shape[1] + tail.shape[1]
    own_rows = aligned(model // n + 1)
    part_rows = aligned(model // (n * GROUP) + 1)
    single = pl.Buffered(1)
    whole = lambda *shape: pl.BlockSpec(
        shape, lambda s, h: (0,) * len(shape), pipeline_mode=single
    )
    mode = single if n > 16 else None
    by_seq = lambda *shape: pl.BlockSpec(
        (None,) + shape, lambda s, h: (s,) + (0,) * len(shape), pipeline_mode=mode
    )
    by_head = lambda *shape: pl.BlockSpec(
        (None, None) + shape, lambda s, h: (s, h) + (0,) * len(shape), pipeline_mode=mode
    )
    anywhere = pl.BlockSpec(memory_space=pl.ANY)
    dma = pltpu.SemaphoreType.DMA
    return pl.pallas_call(
        lambda *refs: attend_back_kernel(dp_size, *refs),
        grid=(seqs, heads),
        out_shape=(
            jax.ShapeDtypeStruct((seqs * rows, model), F32),
            jax.ShapeDtypeStruct((ring_rows, model), F32),
            jax.ShapeDtypeStruct((GROUP, part_rows, 3 * width), F32),
        ),
        in_specs=[
            by_seq(GROUP, rows, model), whole(*mixed_grad.shape), whole(3 * width, model),
            pl.BlockSpec((None, HD, FEAT), lambda s, h: (h, 0, 0)),
            by_seq(16, total), by_seq(3 * width, total), by_head(STATES, FEAT), by_head(HD, total),
            by_head(8, total), by_head(total, total), by_head(FEAT, total), by_head(FEAT, total),
            anywhere, anywhere, anywhere,
        ],
        out_specs=(
            whole(seqs * rows, model), whole(ring_rows, model), whole(GROUP, part_rows, 3 * width),
        ),
        scratch_shapes=[
            pltpu.VMEM((width, total), F32),
            pltpu.VMEM((HD + 16, total), BF16),
            pltpu.VMEM((total, HD + 16), BF16),
            pltpu.VMEM((total, total), BF16),
            pltpu.VMEM((HD, total), F32),
            pltpu.VMEM((3 * width, total), BF16),
            pltpu.VMEM((seqs, 3, rows, width), BF16),
            pltpu.VMEM((2, rows, model), BF16),
            pltpu.VMEM((seqs, 2, rows, model), BF16),
            pltpu.VMEM((2, rows, model), F32),
            pltpu.VMEM((rows, model), BF16),
            pltpu.VMEM((seqs, rows, model), BF16),
            pltpu.VMEM((n, 2, ring_rows, model), BF16),
            pltpu.VMEM((n, 2, ring_rows, model), BF16),
            pltpu.VMEM((n - 1, 2, ring_rows, model), BF16),
            pltpu.VMEM((ring_rows, model), BF16),
            pltpu.VMEM((3 * width, model + 128), F32),
            pltpu.VMEM((heads, 2, n // 2, own_rows, 3 * HD), BF16),
            pltpu.VMEM((heads, n // 2, own_rows, 3 * HD), BF16),
            pltpu.VMEM((heads, n // 2, own_rows, 3 * HD), BF16),
            pltpu.VMEM((heads, n // 2, own_rows, 3 * HD), BF16),
            pltpu.VMEM((GROUP, part_rows, 3 * width), BF16),
            pltpu.VMEM((3, part_rows, 3 * width), BF16),
            dma((2, seqs, 3)),
            dma((2, seqs, 2)),
            dma((2, seqs)),
            dma((n, 2, 3)),
            dma((2, n, 2, 3)),
            dma((2, n - 1, 2)),
            dma((2,)),
            dma((2, heads)),
            dma((2, heads, n // 2)),
            dma((2, 3)),
        ],
        compiler_params=pltpu.CompilerParams(
            vmem_limit_bytes=VMEM + (3 * 1024 * 1024 if n > 16 else 0), collective_id=2, has_side_effects=True
        ),
        cost_estimate=pl.CostEstimate(
            flops=48_000_000_000, bytes_accessed=40_000_000, transcendentals=0
        ),
        name="attend_back",
    )(
        parts, mixed_grad, weight, draws, hot, proj, state, mixed, den, soft, phi_q, phi_k,
        down_grad, up_grad, tail,
    )


def finish_kernel(
    starts, heads, attn_grad, resid_grad, hidden, sums, proj_sums, weight_rows, gain_ref, shift_ref,
    input_out, norm1_gain_out, norm1_bias_out, qkv_out, qkv_bias_out, out_out, out_bias_out,
    norm2_gain_out, norm2_bias_out, up_out, up_bias_out, down_out, down_bias_out,
):
    gain, shift = as_row(gain_ref), as_row(shift_ref)
    normed, scale = row_stats(hidden[...].astype(F32))
    input_out[...] = resid_grad[...] + norm_back(attn_grad[...] * gain, normed, scale)

    @pl.when(pl.program_id(0) == 0)
    def _():
        index = lax.axis_index("dp") * GROUP + lax.axis_index("feat")
        small, model = out_out.shape
        share = down_out.shape[0]
        ff = up_out.shape[1]

        def own(row, size):
            length = row.shape[1]
            wide = jnp.broadcast_to(row, (8, length))
            back = lax.rem(length - lax.rem(index * size, length), length)
            return pltpu.roll(wide, back, 1)[0:1, 0:size]

        down_out[...] = sums[0:share]
        first = starts[0]
        up_out[...] = jnp.concatenate(
            [sums[first + i * small : first + (i + 1) * small] for i in range(ff // model)], axis=1
        )
        first = starts[0] + starts[1]
        out_out[...] = sums[first : first + small]
        totals = first + small
        for i, out in enumerate((down_bias_out, out_bias_out, norm2_gain_out, norm2_bias_out)):
            out[...] = own(sums[totals + i : totals + i + 1], small).reshape(small)
        per_row = model // share
        level = index // per_row
        row = jnp.zeros((1, model), F32)
        for i in range(ff // model):
            row = jnp.where(level == i, sums[totals + 4 + i : totals + 5 + i], row)
        up_bias_out[...] = own(row, share).reshape(share)

        pieces = []
        for kind in range(3):
            for f in range(GROUP):
                for h in range(heads):
                    lanes = slice((h * 3 + kind) * HD, (h * 3 + kind + 1) * HD)
                    pieces.append(proj_sums[f, 0 : small + 1, lanes])
        grid = jnp.concatenate(pieces, axis=1)
        weight_sum, bias_sum = grid[0:small], grid[small : small + 1]
        qkv_out[...] = weight_sum
        qkv_bias_out[...] = own(bias_sum, 3 * small).reshape(3 * small)
        wide = weight_rows[...].astype(F32)

        def to_row(column):
            column = jnp.concatenate(
                [column, jnp.zeros((-small % 128, 1), F32)], axis=0
            )
            return jnp.broadcast_to(column, (column.shape[0], 128)).T[0:1, 0:small]

        bias_grad = to_row(jnp.sum(wide * bias_sum, axis=1, keepdims=True))
        gain_grad = to_row(jnp.sum(wide * weight_sum, axis=1, keepdims=True))
        norm1_bias_out[...] = bias_grad.reshape(small)
        gain_grad = (gain_grad - own(shift, small) * bias_grad) / own(gain, small)
        norm1_gain_out[...] = gain_grad.reshape(small)


def finish_all(
    attn_grad, resid_grad, hidden, sums, proj_sums, weight_rows, gain, shift, starts, devices, ff,
    heads,
):
    seqs, rows, model = hidden.shape
    small, share = model // devices, ff // devices
    whole = lambda *shape: pl.BlockSpec(shape, lambda s: (0,) * len(shape))
    by_seq = pl.BlockSpec((rows, model), lambda s: (s, 0))
    shapes = (
        (small,), (small,), (small, 3 * model), (3 * small,), (small, model), (small,), (small,),
        (small,), (small, ff), (share,), (share, model), (small,),
    )
    return pl.pallas_call(
        lambda *refs: finish_kernel(starts, heads, *refs),
        grid=(seqs,),
        out_shape=(jax.ShapeDtypeStruct((seqs * rows, model), F32),)
        + tuple(jax.ShapeDtypeStruct(shape, F32) for shape in shapes),
        in_specs=[
            by_seq, by_seq, pl.BlockSpec((None, rows, model), lambda s: (s, 0, 0)),
            whole(*sums.shape), whole(*proj_sums.shape), whole(*weight_rows.shape), whole(model),
            whole(model),
        ],
        out_specs=(by_seq,) + tuple(whole(*shape) for shape in shapes),
        compiler_params=pltpu.CompilerParams(vmem_limit_bytes=VMEM),
        name="finish_all",
    )(attn_grad, resid_grad, hidden, sums, proj_sums, weight_rows, gain, shift)


def per_device(
    hidden_in, norm1_gain, norm1_bias, qkv_weight, qkv_bias, feature_draws, out_weight, out_bias,
    norm2_gain, norm2_bias, up_weight, up_bias, down_weight, down_bias, block_bucket, out_grad,
):
    seqs, rows, model = hidden_in.shape
    ff = up_weight.shape[1]
    dp_size = lax.axis_size("dp")
    devices = dp_size * GROUP
    small = model // devices
    heads = feature_draws.shape[0] // GROUP
    flat = (seqs * rows, model)

    (
        parts, mixed_parts, proj, state, mixed, den, hot, own_weight, own_draws, soft, phi_q, phi_k,
    ) = attend(
        block_bucket, hidden_in, norm1_gain, norm1_bias, qkv_bias, qkv_weight, feature_draws
    )
    layer_out, resid_grad, mixed_grad, down_grad, up_grad, tail = block_layer(
        mixed_parts, hidden_in.reshape(flat), out_grad.reshape(flat), out_weight, out_bias,
        norm2_gain, norm2_bias, down_bias, up_bias, up_weight, down_weight, devices,
    )
    attn_grad, sums, proj_sums = attend_back(
        dp_size, parts, mixed_grad, own_weight, own_draws, hot, proj, state, mixed, den, soft,
        phi_q, phi_k, down_grad, up_grad, tail,
    )
    index = lax.axis_index("dp") * GROUP + lax.axis_index("feat")
    weight_rows = lax.dynamic_slice_in_dim(qkv_weight, index * small, small, 0)
    (
        input_grad, norm1_gain_sum, norm1_bias_sum, qkv_weight_sum, qkv_bias_sum, out_weight_sum,
        out_bias_sum, norm2_gain_sum, norm2_bias_sum, up_sum, up_bias_sum, down_sum, down_bias_sum,
    ) = finish_all(
        attn_grad, resid_grad, hidden_in, sums, proj_sums, weight_rows, norm1_gain, norm1_bias,
        (down_grad.shape[1], up_grad.shape[1]), devices, ff, heads,
    )
    return (
        layer_out.reshape(hidden_in.shape), input_grad.reshape(hidden_in.shape), norm1_gain_sum,
        norm1_bias_sum, qkv_weight_sum, qkv_bias_sum, out_weight_sum, out_bias_sum, norm2_gain_sum,
        norm2_bias_sum, up_sum, up_bias_sum, down_sum, down_bias_sum,
    )


def solution(mesh):
    both = ("dp", "feat")
    rows = P("dp", "feat", None)
    in_specs = (
        rows, P(), P(), P(), P(), P(None, None, "feat"), P(), P(), P(), P(), P(), P(), P(), P(),
        P("dp", None, None), rows,
    )
    out_specs = (
        rows, rows, P(both), P(both), P(both, None), P(both), P(both, None), P(both), P(both),
        P(both), P(both, None), P(both), P(both, None), P(both),
    )
    return jax.shard_map(
        per_device, mesh=mesh, in_specs=in_specs, out_specs=out_specs, check_vma=False
    )
```

```python
import math

import jax
import jax.numpy as jnp
from jax import lax
from jax.experimental import pallas as pl
from jax.experimental.pallas import tpu as pltpu
from jax.sharding import PartitionSpec as P

HD = 64
FEAT = 256
BLOCK = 64
NBUCK = 4
GROUP = 4
CHUNK = 256
STATES = NBUCK * HD + 16
FAR = 16384.0
VMEM = 60 * 1024 * 1024

F32 = jnp.float32
BF16 = jnp.bfloat16
MESH = pl.DeviceIdType.MESH


def mat(left, right):
    return jnp.dot(left, right, preferred_element_type=F32)


def mat_nt(left, right):
    return lax.dot_general(left, right, (((1,), (1,)), ((), ())), preferred_element_type=F32)


def mat_tn(left, right):
    return lax.dot_general(left, right, (((0,), (0,)), ((), ())), preferred_element_type=F32)


def row_stats(values):
    row_mean = jnp.mean(values, axis=-1, keepdims=True)
    centered = values - row_mean
    scale = lax.rsqrt(jnp.mean(centered * centered, axis=-1, keepdims=True) + 1e-05)
    return (centered * scale, scale)


def norm_back(cotangent, normed, scale):
    mean_one = jnp.mean(cotangent, axis=-1, keepdims=True)
    mean_two = jnp.mean(cotangent * normed, axis=-1, keepdims=True)
    return scale * (cotangent - mean_one - normed * mean_two)


def features(vectors, draws):
    wide = vectors.astype(F32)
    square = jnp.sum(wide * wide, axis=0, keepdims=True) * (0.5 / math.sqrt(HD))
    return jnp.exp(mat_tn(draws, vectors) - (square + 0.5 * math.log(FEAT)))


def spread(rows, marks):
    return [rows * marks[u : u + 1] for u in range(NBUCK)]


def pick(stacked, marks):
    total = stacked[0:HD] * marks[0:1]
    for u in range(1, NBUCK):
        total = total + stacked[u * HD : (u + 1) * HD] * marks[u : u + 1]
    return total


def away_marks(hot):
    live = (lax.broadcasted_iota(jnp.int32, hot.shape, 0) < NBUCK).astype(F32)
    return live - hot.astype(F32)


def partner(own, r):
    x, core = own // 2, own % 2
    if r & 2:
        x = 1 - x
    if r & 1:
        core = 1 - core
    return 2 * x + core


def as_row(ref):
    return ref[...].reshape(1, ref.shape[0])


def aligned(count):
    return -(-count // 16) * 16


def remote(src, dst, send, recv, place):
    return pltpu.make_async_remote_copy(
        src_ref=src, dst_ref=dst, send_sem=send, recv_sem=recv, device_id=place, device_id_type=MESH
    )


def head_rows(h, kind, heads):
    return pl.ds(pl.multiple_of((kind * heads + h) * HD, HD), HD)


def attend_kernel(
    bucket, hidden, gain_ref, shift_ref, bias_ref, weight_any, draws_in,
    parts_any, mix_any, proj_out, state_out, mixed_out, den_out, hot_out, weight_out, draws_out,
    soft_out, phi_q_out, phi_k_out,
    parts, mix_land, mix_send, raw, bias_row, bias_scr, draws_land,
    query_scr, key_scr, value_scr, low_scr, gather_scr,
    raw_sem, part_send, part_recv, draw_send, draw_recv, mix_send_sem, mix_recv_sem, out_sem,
):
    s, h = pl.program_id(0), pl.program_id(1)
    seqs, rows, model = hidden.shape
    heads = draws_out.shape[0]
    total = GROUP * rows
    width = heads * HD
    own = lax.axis_index("feat")
    near, across = {"feat": partner(own, 1)}, {"feat": partner(own, 2)}

    def part_copy(q, kind):
        src, dst, place = ((0, 1, near), (0, 2, across), (2, 3, near))[kind]
        return remote(
            parts.at[q, src], parts.at[q, dst], part_send.at[q, kind], part_recv.at[q, kind], place
        )

    def draw_copy(r):
        other = partner(own, r)
        return remote(
            draws_in.at[pl.ds(other * heads, heads)], draws_land.at[r - 1],
            draw_send.at[r - 1], draw_recv.at[r - 1], {"feat": other},
        )

    def mix_copy(q, r):
        return remote(
            mix_send.at[q, r], mix_land.at[q, r], mix_send_sem.at[q, r - 1],
            mix_recv_sem.at[q, r - 1], {"feat": partner(own, r)},
        )

    def raw_copy(j):
        cols = pl.ds(pl.multiple_of(j * model + (own // 2) * 2 * width, 2 * width), 2 * width)
        return pltpu.make_async_copy(weight_any.at[:, cols], raw.at[j], raw_sem.at[j])

    def out_copy(q):
        return pltpu.make_async_copy(parts.at[q], parts_any.at[q], out_sem.at[q])

    @pl.when((s == 0) & (h == 0))
    def _():
        for j in range(3):
            raw_copy(j).start()
        barrier = pltpu.get_barrier_semaphore()
        for r in (1, 2, 3):
            pl.semaphore_signal(
                barrier, inc=1, device_id={"feat": partner(own, r)}, device_id_type=MESH
            )
        gain, shift = as_row(gain_ref), as_row(shift_ref)
        first = row_stats(hidden[0].astype(F32))[0] * gain + shift
        parts[0, 0] = first.astype(BF16)
        pl.semaphore_wait(barrier, 3)
        part_copy(0, 1).start()
        part_copy(0, 0).start()
        for r in (1, 2, 3):
            draw_copy(r).start()
        for q in range(1, seqs):
            normed = row_stats(hidden[q].astype(F32))[0] * gain + shift
            parts[q, 0] = normed.astype(BF16)
            part_copy(q, 1).start()
            part_copy(q, 0).start()
        core = own % 2
        bias_row[...] = as_row(bias_ref)
        for j in range(3):
            raw_copy(j).wait()
            piece = raw[j].astype(F32)
            piece = jnp.where(core == 0, piece[:, 0:width], piece[:, width:])
            weight_out[j * width : (j + 1) * width] = piece.T.astype(BF16)
            cols = pl.ds(pl.multiple_of(j * model + (own // 2) * 2 * width, 2 * width), 2 * width)
            pair = jnp.broadcast_to(bias_row[:, cols], (128, 2 * width))
            pair = jnp.where(core == 0, pair[:, 0:width], pair[:, width:])
            bias_scr[j * width : (j + 1) * width] = pair.T
        part_copy(0, 1).wait_recv()
        part_copy(0, 2).start()
        for r in (1, 2, 3):
            draw_copy(r).wait_recv()
        mine = draws_in[pl.ds(own * heads, heads)]
        draws_out[...] = jnp.concatenate(
            [mine] + [draws_land[r - 1] for r in (1, 2, 3)], axis=2
        )

    @pl.when(h == 0)
    def _():
        per = rows // BLOCK
        lanes = lax.broadcasted_iota(jnp.int32, (16, total), 1) // BLOCK
        level = lax.broadcasted_iota(jnp.int32, (16, total), 0)
        ids = jnp.full((16, total), -1, jnp.int32)
        for r in range(GROUP):
            for i in range(per):
                ids = jnp.where(
                    lanes == r * per + i, bucket[s, partner(own, r) * per + i, 0], ids
                )
        hot_out[...] = (ids == level).astype(F32).astype(BF16)

        def project(r):
            cols = slice(r * rows, (r + 1) * rows)
            piece = mat_nt(weight_out[...], parts[s, r]) + bias_scr[:, 0:1]
            proj_out[:, cols] = piece.astype(BF16)

        project(0)
        part_copy(s, 0).wait_recv()
        project(1)
        project(2)
        part_copy(s, 2).wait_recv()
        project(3)
        out_copy(s).start()

    query = proj_out[head_rows(h, 0, heads)]
    key = proj_out[head_rows(h, 1, heads)]
    value = proj_out[head_rows(h, 2, heads)]
    draws = draws_out[h]
    hot = hot_out[...]
    hot_wide = hot.astype(F32)
    away = away_marks(hot).astype(BF16)
    phi_q = features(query, draws).astype(BF16)
    phi_k = features(key, draws).astype(BF16)
    phi_q_out[...] = phi_q
    phi_k_out[...] = phi_k
    spread_value = jnp.concatenate(spread(value, away) + [away], axis=0)
    state = mat_nt(spread_value, phi_k).astype(BF16)
    state_out[...] = state
    low = mat(state, phi_q)
    low_scr[0:HD] = pick(low, hot_wide)
    low_den = jnp.sum(low[NBUCK * HD :] * hot_wide, axis=0, keepdims=True)
    low_scr[HD : HD + 8] = jnp.broadcast_to(low_den, (8, total))
    query_scr[...] = jnp.concatenate([query * (1.0 / math.sqrt(HD)), hot], axis=0).astype(BF16)
    key_scr[...] = jnp.concatenate([key, away * -FAR], axis=0).astype(F32).T.astype(BF16)
    value_scr[0:HD] = value
    value_scr[HD:] = jnp.ones((16, total), BF16)

    for c in range(total // CHUNK):
        cols = slice(c * CHUNK, (c + 1) * CHUNK)
        weights = jnp.exp(mat(key_scr[...], query_scr[:, cols])).astype(BF16)
        soft_out[:, cols] = weights
        exact = mat(value_scr[...], weights)
        den = low_scr[HD : HD + 8, cols] + exact[HD : HD + 8]
        mixed = (low_scr[0:HD, cols] + exact[0:HD]) / den[0:1]
        mixed_out[:, cols] = mixed
        den_out[:, cols] = den
        gather_scr[pl.ds(pl.multiple_of(h * HD, HD), HD), cols] = mixed

    @pl.when((h == heads - 2) & (s < seqs - 1))
    def _():
        part_copy(s + 1, 1).wait_recv()
        part_copy(s + 1, 2).start()

    @pl.when(h == heads - 1)
    def _():
        for r in range(GROUP):
            piece = gather_scr[:, r * rows : (r + 1) * rows].T.astype(BF16)
            if r == 0:
                mix_land[s, 0] = piece
            else:
                mix_send[s, r] = piece
                mix_copy(s, r).start()

    @pl.when((s == seqs - 1) & (h == heads - 1))
    def _():
        for q in range(seqs):
            for r in (1, 2, 3):
                mix_copy(q, r).wait_recv()
        done = pltpu.make_async_copy(mix_land, mix_any, out_sem.at[seqs])
        done.start()
        for q in range(seqs):
            for kind in range(3):
                part_copy(q, kind).wait_send()
            for r in (1, 2, 3):
                mix_copy(q, r).wait_send()
            out_copy(q).wait()
        for r in (1, 2, 3):
            draw_copy(r).wait_send()
        done.wait()


def attend(bucket, hidden, gain, shift, bias, weight, draws):
    seqs, rows, model = hidden.shape
    heads = draws.shape[0] // GROUP
    width = heads * HD
    total = GROUP * rows
    whole = lambda *shape: pl.BlockSpec(shape, lambda s, h: (0,) * len(shape))
    by_seq = lambda *shape: pl.BlockSpec((None,) + shape, lambda s, h: (s,) + (0,) * len(shape))
    by_head = lambda *shape: pl.BlockSpec(
        (None, None) + shape, lambda s, h: (s, h) + (0,) * len(shape)
    )
    anywhere = pl.BlockSpec(memory_space=pl.ANY)
    return pl.pallas_call(
        attend_kernel,
        grid=(seqs, heads),
        out_shape=(
            jax.ShapeDtypeStruct((seqs, GROUP, rows, model), BF16),
            jax.ShapeDtypeStruct((seqs, GROUP, rows, width), BF16),
            jax.ShapeDtypeStruct((seqs, 3 * width, total), BF16),
            jax.ShapeDtypeStruct((seqs, heads, STATES, FEAT), BF16),
            jax.ShapeDtypeStruct((seqs, heads, HD, total), F32),
            jax.ShapeDtypeStruct((seqs, heads, 8, total), F32),
            jax.ShapeDtypeStruct((seqs, 16, total), BF16),
            jax.ShapeDtypeStruct((3 * width, model), BF16),
            jax.ShapeDtypeStruct((heads, HD, FEAT), BF16),
            jax.ShapeDtypeStruct((seqs, heads, total, total), BF16),
            jax.ShapeDtypeStruct((seqs, heads, FEAT, total), BF16),
            jax.ShapeDtypeStruct((seqs, heads, FEAT, total), BF16),
        ),
        in_specs=[
            pl.BlockSpec(memory_space=pltpu.SMEM),
            whole(seqs, rows, model), whole(model), whole(model), whole(3 * model), anywhere,
            whole(*draws.shape),
        ],
        out_specs=(
            anywhere, anywhere, by_seq(3 * width, total), by_head(STATES, FEAT), by_head(HD, total),
            by_head(8, total), by_seq(16, total), whole(3 * width, model), whole(heads, HD, FEAT),
            by_head(total, total), by_head(FEAT, total), by_head(FEAT, total),
        ),
        scratch_shapes=[
            pltpu.VMEM((seqs, GROUP, rows, model), BF16),
            pltpu.VMEM((seqs, GROUP, rows, width), BF16),
            pltpu.VMEM((seqs, GROUP, rows, width), BF16),
            pltpu.VMEM((3, model, 2 * width), BF16),
            pltpu.VMEM((1, 3 * model), F32),
            pltpu.VMEM((3 * width, 128), F32),
            pltpu.VMEM((3, heads, HD, draws.shape[2]), BF16),
            pltpu.VMEM((HD + 16, total), BF16),
            pltpu.VMEM((total, HD + 16), BF16),
            pltpu.VMEM((HD + 16, total), BF16),
            pltpu.VMEM((HD + 8, total), F32),
            pltpu.VMEM((width, total), F32),
            pltpu.SemaphoreType.DMA((3,)),
            pltpu.SemaphoreType.DMA((seqs, 3)),
            pltpu.SemaphoreType.DMA((seqs, 3)),
            pltpu.SemaphoreType.DMA((3,)),
            pltpu.SemaphoreType.DMA((3,)),
            pltpu.SemaphoreType.DMA((seqs, 3)),
            pltpu.SemaphoreType.DMA((seqs, 3)),
            pltpu.SemaphoreType.DMA((seqs + 1,)),
        ],
        compiler_params=pltpu.CompilerParams(
            vmem_limit_bytes=VMEM, collective_id=1, has_side_effects=True
        ),
        cost_estimate=pl.CostEstimate(
            flops=24_000_000_000, bytes_accessed=20_000_000, transcendentals=0
        ),
        name="attend",
    )(bucket, hidden, gain, shift, bias, weight, draws)


def block_kernel(
    direct, parts_ref, hidden, grad, out_w, out_b, gain_ref, shift_ref, down_b, up_b, up, down,
    layer_out, resid_out, mixed_grad, down_out, up_out, tail_out,
    mixed, resid_scr, in_scr, in_t, acc_out, acc_in, act_scr, pre_scr, vec_scr, bias_row,
):
    step = pl.program_id(0)
    model = hidden.shape[1]
    count = hidden.shape[0] // CHUNK
    spans = [slice(c * CHUNK, (c + 1) * CHUNK) for c in range(count)]
    subs = [slice(u * model, (u + 1) * model) for u in range(up.shape[1] // model)]
    owners = tail_out.shape[0]
    small = model // owners

    @pl.when(step == 0)
    def _():
        own = lax.axis_index("feat")
        for c, span in enumerate(spans):
            pieces = [parts_ref[c, r] for r in range(GROUP)]
            pieces = [jnp.where(own % 2 == 1, pieces[r ^ 1], pieces[r]) for r in range(GROUP)]
            pieces = [jnp.where(own // 2 == 1, pieces[r ^ 2], pieces[r]) for r in range(GROUP)]
            mixed[span] = jnp.concatenate(pieces, axis=1)
            resid = hidden[span].astype(F32) + mat(mixed[span], out_w[...]) + as_row(out_b)
            resid_scr[span] = resid
            normed, _ = row_stats(resid)
            inner = normed * as_row(gain_ref) + as_row(shift_ref)
            in_scr[span] = inner.astype(BF16)
            in_t[:, span] = inner.T.astype(BF16)
        acc_out[...] = jnp.zeros_like(acc_out)
        acc_in[...] = jnp.zeros_like(acc_in)
        bias_row[...] = as_row(up_b)

    slope = math.sqrt(2.0 / math.pi)
    up_terms = []
    for u, sub in enumerate(subs):
        total = jnp.zeros((1, model), F32)
        place = (step * len(subs) + u) * model
        up_bias = bias_row[:, pl.ds(pl.multiple_of(place, model), model)]
        for span in spans:
            pre = mat(in_scr[span], up[:, sub]) + up_bias
            square = pre * pre
            tanh = jnp.tanh(pre * (slope + (slope * 0.044715) * square))
            half = 0.5 * (1.0 + tanh)
            act = (pre * half).astype(BF16)
            bend = half + (0.5 * pre) * (1.0 - tanh * tanh) * (
                slope + (3.0 * slope * 0.044715) * square
            )
            pre_grad = mat_nt(grad[span], down[sub]) * bend
            total = total + jnp.sum(pre_grad, axis=0, keepdims=True)
            pre_low = pre_grad.astype(BF16)
            act_scr[span] = act
            pre_scr[span] = pre_low
            acc_out[span] += mat(act, down[sub])
            acc_in[span] += mat_nt(pre_low, up[:, sub])
        vec_scr[pl.ds(4 + step * len(subs) + u, 1)] = total
        down_term = mat_tn(act_scr[...], grad[...])
        up_term = mat(in_t[...], pre_scr[...])
        if direct:
            share = down_out.shape[1]
            for i in range(model // share):
                down_out[u * (model // share) + i] = down_term[
                    i * share : (i + 1) * share
                ].astype(BF16)
            up_terms.append(up_term)
        else:
            down_out[sub] = down_term.astype(BF16)
            up_out[:, sub] = up_term.astype(BF16)
    if direct:
        for i in range(owners):
            own_rows = slice(i * small, (i + 1) * small)
            up_out[i] = jnp.concatenate([term[own_rows] for term in up_terms], axis=0).astype(BF16)

    @pl.when(step == pl.num_programs(0) - 1)
    def _():
        sums = [jnp.zeros((1, model), F32) for _ in range(4)]
        for span in spans:
            resid = resid_scr[span]
            layer_out[span] = (resid + acc_out[span] + as_row(down_b)).astype(BF16)
            normed, scale = row_stats(resid)
            inner_grad = acc_in[span]
            wide = grad[span].astype(F32)
            resid_grad = wide + norm_back(inner_grad * as_row(gain_ref), normed, scale)
            resid_out[span] = resid_grad
            low = resid_grad.astype(BF16)
            in_scr[span] = low
            for i, term in enumerate((wide, resid_grad, inner_grad * normed, inner_grad)):
                sums[i] = sums[i] + jnp.sum(term, axis=0, keepdims=True)
            back = mat_nt(low, out_w[...]).astype(BF16)
            part = model // GROUP
            for a in range(GROUP):
                mixed_grad[a, span] = back[:, a * part : (a + 1) * part]
        for i in range(4):
            vec_scr[i : i + 1] = sums[i]
        out_term = mat_tn(mixed[...], in_scr[...])
        fill = tail_out.shape[1] - small - 8
        extra = [jnp.zeros((fill, model), F32)] if fill else []
        for i in range(owners):
            tail_out[i] = jnp.concatenate(
                [out_term[i * small : (i + 1) * small], vec_scr[...]] + extra, axis=0
            ).astype(BF16)


def block_layer(parts, hidden, grad, out_w, out_b, gain, shift, down_b, up_b, up, down, devices):
    tokens, model = hidden.shape
    ff = up.shape[1]
    steps = 2
    tile = ff // steps
    small, share = model // devices, ff // devices
    direct = small % 8 == 0 and share % 16 == 0
    tail_rows = aligned(small + 8)
    single = pl.Buffered(1)
    whole = lambda *shape: pl.BlockSpec(
        shape, lambda t: (0,) * len(shape), pipeline_mode=single
    )
    part = model // GROUP
    if direct:
        grad_shapes = (
            jax.ShapeDtypeStruct((devices, share, model), BF16),
            jax.ShapeDtypeStruct((devices, ff // model * small, model), BF16),
        )
        grad_specs = (
            pl.BlockSpec((devices // steps, share, model), lambda t: (t, 0, 0)),
            pl.BlockSpec((devices, tile // model * small, model), lambda t: (0, t, 0)),
        )
    else:
        grad_shapes = (
            jax.ShapeDtypeStruct((ff, model), BF16),
            jax.ShapeDtypeStruct((model, ff), BF16),
        )
        grad_specs = (
            pl.BlockSpec((tile, model), lambda t: (t, 0)),
            pl.BlockSpec((model, tile), lambda t: (0, t)),
        )
    layer_out, resid_grad, mixed_grad, down_grad, up_grad, tail = pl.pallas_call(
        lambda *refs: block_kernel(direct, *refs),
        grid=(steps,),
        out_shape=(
            jax.ShapeDtypeStruct((tokens, model), BF16),
            jax.ShapeDtypeStruct((tokens, model), F32),
            jax.ShapeDtypeStruct((GROUP, tokens, part), BF16),
        )
        + grad_shapes
        + (jax.ShapeDtypeStruct((devices, tail_rows, model), BF16),),
        in_specs=[
            whole(*parts.shape), whole(tokens, model), whole(tokens, model), whole(model, model),
            whole(model), whole(model), whole(model), whole(model), whole(ff),
            pl.BlockSpec((model, tile), lambda t: (0, t)),
            pl.BlockSpec((tile, model), lambda t: (t, 0)),
        ],
        out_specs=(whole(tokens, model), whole(tokens, model), whole(GROUP, tokens, part))
        + grad_specs
        + (whole(devices, tail_rows, model),),
        scratch_shapes=[
            pltpu.VMEM((tokens, model), BF16),
            pltpu.VMEM((tokens, model), F32),
            pltpu.VMEM((tokens, model), BF16),
            pltpu.VMEM((model, tokens), BF16),
            pltpu.VMEM((tokens, model), F32),
            pltpu.VMEM((tokens, model), F32),
            pltpu.VMEM((tokens, model), BF16),
            pltpu.VMEM((tokens, model), BF16),
            pltpu.VMEM((8, model), F32),
            pltpu.VMEM((1, ff), F32),
        ],
        compiler_params=pltpu.CompilerParams(vmem_limit_bytes=VMEM),
        cost_estimate=pl.CostEstimate(
            flops=26_000_000_000, bytes_accessed=30_000_000, transcendentals=0
        ),
        name="block_layer",
    )(parts, hidden, grad, out_w, out_b, gain, shift, down_b, up_b, up, down)
    if not direct:
        fit = lambda a: jnp.pad(a, ((0, 0), (0, aligned(a.shape[1]) - a.shape[1]), (0, 0)))
        down_grad = fit(down_grad.reshape(devices, share, model))
        up_grad = up_grad.reshape(devices, small, ff // model, model).transpose(0, 2, 1, 3)
        up_grad = fit(up_grad.reshape(devices, ff // model * small, model))
    return layer_out, resid_grad, mixed_grad, down_grad, up_grad, tail


def attend_back_kernel(
    dp_size, x_ref, mixed_grad, weight, draws_ref, hot_ref, proj, state_ref, mixed_ref, den_ref,
    soft_ref, phi_q_ref, phi_k_ref, down_any, up_any, tail_any,
    attn_out, ring_out, proj_out,
    grad_scr, num_scr, value_scr, score_scr, exact_scr, proj_scr,
    grad_land, near_send, near_land, far_keep, far_send, far_land,
    mine, met, ring_land, cross_land,
    weight_acc, own_send, pair_land, own_mid, own_land, part_send, part_land,
    grad_sems, near_sems, far_sems, mine_sem, met_sems, ring_sems, cross_sems, pair_sems, own_sems,
    part_sems,
):
    s, h = pl.program_id(0), pl.program_id(1)
    seqs, heads = pl.num_programs(0), pl.num_programs(1)
    rows, model = x_ref.shape[1], x_ref.shape[2]
    head_count = proj_scr.shape[0] // (3 * HD)
    width = head_count * HD
    total = GROUP * rows
    root = 1.0 / math.sqrt(HD)
    own, me = lax.axis_index("feat"), lax.axis_index("dp")
    own_x, own_core = own // 2, own % 2
    near, across = {"feat": partner(own, 1)}, {"feat": partner(own, 2)}
    last = (s == seqs - 1) & (h == heads - 1)

    def grad_copy(q, r):
        other = partner(own, r)
        return remote(
            mixed_grad.at[other, pl.ds(q * rows, rows)], grad_land.at[q, r - 1],
            grad_sems.at[0, q, r - 1], grad_sems.at[1, q, r - 1], {"feat": other},
        )

    def near_copy(q, i):
        return remote(
            near_send.at[i], near_land.at[q, i], near_sems.at[0, q, i], near_sems.at[1, q, i], near
        )

    def far_copy(q):
        return remote(far_send, far_land.at[q], far_sems.at[0, q], far_sems.at[1, q], across)

    odd = me % 2
    half = dp_size // 2
    spot = (1 - odd) * (me // 2) + odd * (dp_size - 1 - me // 2)

    def at_spot(p):
        p = lax.rem(p + dp_size, dp_size)
        upper = p // half
        return (1 - upper) * (2 * p) + upper * (2 * (dp_size - 1 - p) + 1)

    def chunk(k, way):
        return at_spot(spot - 1 - k) if way == 0 else at_spot(lax.rem(spot + 1 + k, dp_size))

    sources = (down_any, up_any, tail_any)
    lengths = [ref.shape[1] for ref in sources]
    starts = [sum(lengths[:i]) for i in range(3)]

    def owner(k, way, core):
        return chunk(k, way) * GROUP + 2 * way + core

    def mine_copy(k, way, i):
        return pltpu.make_async_copy(
            sources[i].at[owner(k, way, own_core)],
            mine.at[k, way, pl.ds(starts[i], lengths[i])],
            mine_sem.at[k, way, i],
        )

    def met_copy(k, way, i):
        return remote(
            sources[i].at[owner(k, way, 1 - own_core)],
            met.at[k, way, pl.ds(starts[i], lengths[i])],
            met_sems.at[0, k, way, i], met_sems.at[1, k, way, i], near,
        )

    cut = aligned(mine.shape[2] // 2)
    halves = (pl.ds(0, cut), pl.ds(cut, mine.shape[2] - cut))

    def ring_copy(k, way, part):
        place = at_spot(spot + 1) if way == 0 else at_spot(spot - 1)
        return remote(
            mine.at[k, way, halves[part]], ring_land.at[k, way, halves[part]],
            ring_sems.at[0, k, way, part], ring_sems.at[1, k, way, part], {"dp": place},
        )

    def cross_copy(part):
        return remote(
            mine.at[dp_size - 1, 1 - own_x, halves[part]], cross_land.at[halves[part]],
            cross_sems.at[0, part], cross_sems.at[1, part], across,
        )

    def begin_pieces(k):
        for way in range(2):
            for i in range(3):
                met_copy(k, way, i).start()
                mine_copy(k, way, i).start()

    def ring_step(k, part):
        span = halves[part]
        if part == 0:

            @pl.when(k + 2 < dp_size)
            def _():
                begin_pieces(k + 2)

        @pl.when(k < dp_size)
        def _():
            for way in range(2):
                if part == 0:
                    for i in range(3):
                        mine_copy(k, way, i).wait()
                        met_copy(k, way, i).wait_recv()

                @pl.when(k == 0)
                def _():
                    base = mine[k, way, span].astype(F32) + met[k, way, span].astype(F32)
                    mine[k, way, span] = base.astype(BF16)

                @pl.when(k > 0)
                def _():
                    ring_copy(k - 1, way, part).wait_recv()
                    base = mine[k, way, span].astype(F32) + met[k, way, span].astype(F32)
                    base = base + ring_land[k - 1, way, span].astype(F32)
                    mine[k, way, span] = base.astype(BF16)

                @pl.when(k < dp_size - 1)
                def _():
                    ring_copy(k, way, part).start()

            @pl.when(k == dp_size - 1)
            def _():
                cross_copy(part).start()

        @pl.when(k == dp_size)
        def _():
            cross_copy(part).wait_recv()
            ring_out[span] = mine[dp_size - 1, own_x, span].astype(F32) + cross_land[span].astype(F32)

    def ring_turn(part):
        turn = s * heads + h
        count = seqs * heads
        steps = dp_size + 1

        def body(k, carry):
            ring_step(k, part)
            return carry

        lax.fori_loop(turn * steps // count, (turn + 1) * steps // count, body, 0)

    parity, pair = me % 2, me // 2
    mate = me + 1 - 2 * parity

    def pair_copy(q):
        return remote(
            own_send.at[q, 1 - parity], pair_land.at[q], pair_sems.at[0, q], pair_sems.at[1, q],
            {"dp": mate},
        )

    def own_copy(q, k):
        to = lax.rem(pair + k, half)
        return remote(
            own_mid.at[q, to], own_land.at[q, k], own_sems.at[0, q, k], own_sems.at[1, q, k],
            {"dp": 2 * to + parity},
        )

    def begin_own(q):
        base = model // dp_size
        turned = weight_acc[pl.ds(pl.multiple_of(q * 3 * HD, 3 * HD), 3 * HD)].T
        fill = turned[model : model + own_send.shape[3] - base]
        for c in range(dp_size):
            own_send[q, c % 2, c // 2] = jnp.concatenate(
                [turned[c * base : (c + 1) * base], fill], axis=0
            ).astype(BF16)
        pair_copy(q).start()

    def relay_own(q):
        pair_copy(q).wait_recv()
        own_mid[q] = (own_send[q, parity].astype(F32) + pair_land[q].astype(F32)).astype(BF16)

        def start(k, carry):
            own_copy(q, k).start()
            return carry

        lax.fori_loop(1, half, start, 0)

    def part_copy(r):
        other = partner(own, r)
        return remote(
            part_send.at[other], part_land.at[r - 1], part_sems.at[0, r - 1],
            part_sems.at[1, r - 1], {"feat": other},
        )

    def seq_span(q):
        return pl.ds(pl.multiple_of(q * rows, rows), rows)

    def add_near(q):
        near_copy(q, 1).wait_recv()

        @pl.when(q > 0)
        def _():
            far_copy(q - 1).wait_send()

        far_send[...] = (far_keep[1] + near_land[q, 1].astype(F32)).astype(BF16)
        far_copy(q).start()
        near_copy(q, 0).wait_recv()
        attn_out[seq_span(q)] = far_keep[0] + near_land[q, 0].astype(F32)

    def finish(q):
        far_copy(q).wait_recv()
        span = seq_span(q)
        attn_out[span] = attn_out[span] + far_land[q].astype(F32)

    @pl.when((s == 0) & (h == 0))
    def _():
        barrier = pltpu.get_barrier_semaphore()
        for r in (1, 2, 3):
            pl.semaphore_signal(
                barrier, inc=1, device_id={"feat": partner(own, r)}, device_id_type=MESH
            )

        def greet(k, carry):
            pl.semaphore_signal(
                barrier, inc=1, device_id={"dp": lax.rem(me + k, dp_size)}, device_id_type=MESH
            )
            return carry

        lax.fori_loop(1, dp_size, greet, 0)
        pl.semaphore_wait(barrier, 3 + dp_size - 1)
        for q in range(grad_land.shape[0]):
            for r in (2, 3, 1):
                grad_copy(q, r).start()
        for k in range(2):
            begin_pieces(k)
        weight_acc[...] = jnp.zeros_like(weight_acc)

    @pl.when(h == 0)
    def _():
        span = pl.ds(pl.multiple_of(s * rows, rows), rows)
        grad_scr[:, 0:rows] = mixed_grad[own, span].astype(F32).T
        for r in (1, 2, 3):
            grad_copy(s, r).wait_recv()
            grad_scr[:, r * rows : (r + 1) * rows] = grad_land[s, r - 1].astype(F32).T

    query = proj[head_rows(h, 0, head_count)]
    key = proj[head_rows(h, 1, head_count)]
    value = proj[head_rows(h, 2, head_count)]
    draws = draws_ref[...]
    draws_ext = jnp.concatenate([draws, jnp.ones((16, FEAT), BF16)], axis=0)
    hot = hot_ref[...]
    away_wide = away_marks(hot)
    away = away_wide.astype(BF16)
    inverse = 1.0 / den_ref[0:1]
    head_grad = grad_scr[pl.ds(pl.multiple_of(h * HD, HD), HD)]
    grad_num = (head_grad * inverse).astype(BF16)
    grad_den = -jnp.sum(head_grad * mixed_ref[...], axis=0, keepdims=True) * inverse
    den_rows = jnp.broadcast_to(grad_den, (16, total)).astype(BF16)
    spread_grad = jnp.concatenate(spread(grad_num, hot) + [den_rows * hot], axis=0)
    spread_value = jnp.concatenate(spread(value, away) + [away], axis=0)

    phi_q = phi_q_ref[...]
    state_grad = mat_nt(spread_grad, phi_q).astype(BF16)
    scaled_q = mat_tn(state_ref[...], spread_grad) * phi_q.astype(F32)
    back_q = mat(draws_ext, scaled_q.astype(BF16))
    query_grad = back_q[0:HD] - query.astype(F32) * (back_q[HD : HD + 1] * root)

    phi_k = phi_k_ref[...]
    scaled_k = mat_tn(state_grad, spread_value) * phi_k.astype(F32)
    back_k = mat(draws_ext, scaled_k.astype(BF16))
    key_grad = back_k[0:HD] - key.astype(F32) * (back_k[HD : HD + 1] * root)
    value_grad = pick(mat(state_grad[0 : NBUCK * HD], phi_k), away_wide)

    ring_turn(0)
    one = (lax.broadcasted_iota(jnp.int32, hot.shape, 0) < 1).astype(F32).astype(BF16)
    num_scr[...] = jnp.concatenate([grad_num, den_rows], axis=0)
    value_scr[...] = jnp.concatenate([value, one], axis=0).astype(F32).T.astype(BF16)

    for c in range(total // CHUNK):
        cols = slice(c * CHUNK, (c + 1) * CHUNK)
        score = mat(value_scr[...], num_scr[:, cols]) * soft_ref[:, cols].astype(F32)
        score = score.astype(BF16)
        score_scr[:, cols] = score
        exact_scr[:, cols] = mat(proj[head_rows(h, 1, head_count)], score)
    query_grad = query_grad + exact_scr[...] * root
    joint = jnp.concatenate([query, grad_num], axis=0).astype(F32).T
    lane = lax.broadcasted_iota(jnp.int32, joint.shape, 1)
    left = jnp.where(lane < HD, joint, 0.0).astype(BF16)
    right = jnp.where(lane < HD, 0.0, joint).astype(BF16)
    exact_pair = (mat(score_scr[...], left) + mat(soft_ref[...], right)).T
    key_grad = key_grad + exact_pair[0:HD] * root
    value_grad = value_grad + exact_pair[HD:]
    wide_grad = jnp.concatenate([query_grad, key_grad, value_grad], axis=0)
    low_grad = wide_grad.astype(BF16)
    for kind in range(3):
        proj_scr[head_rows(h, kind, head_count)] = low_grad[kind * HD : (kind + 1) * HD]
    weight_grad = mat(low_grad[:, 0:rows], x_ref[0])
    for r in (1, 2, 3):
        weight_grad = weight_grad + mat(low_grad[:, r * rows : (r + 1) * rows], x_ref[r])
    span = pl.ds(pl.multiple_of(h * 3 * HD, 3 * HD), 3 * HD)
    weight_acc[span, 0:model] += weight_grad
    weight_acc[span, model:] += jnp.broadcast_to(
        jnp.sum(wide_grad, axis=1, keepdims=True), (3 * HD, 128)
    )

    @pl.when(s == seqs - 1)
    def _():
        begin_own(h)

        @pl.when(h > 0)
        def _():
            relay_own(h - 1)

    @pl.when((s > 0) & (h == 0))
    def _():
        add_near(s - 1)

    @pl.when(h == heads - 1)
    def _():
        @pl.when(s > 0)
        def _():
            for i in range(2):
                near_copy(s - 1, i).wait_send()

        for r in (3, 1, 2, 0):
            term = mat_tn(proj_scr[:, r * rows : (r + 1) * rows], weight[...])
            if r % 2:
                near_send[r // 2] = term.astype(BF16)
                near_copy(s, r // 2).start()
            else:
                far_keep[r // 2] = term

    ring_turn(1)

    @pl.when(last)
    def _():
        add_near(s)
        relay_own(h)
        for q in range(grad_land.shape[0] - 1):
            finish(q)

        sums = []
        for q in range(head_count):

            def arrive(k, carry):
                own_copy(q, k).wait_recv()
                return carry + own_land[q, k].astype(F32)

            sums.append(lax.fori_loop(1, half, arrive, own_mid[q, pair].astype(F32)))
        joined = jnp.concatenate(sums, axis=1)
        base = model // dp_size
        small = base // GROUP
        fill = jnp.broadcast_to(
            joined[base : base + 1], (part_send.shape[1] - small, joined.shape[1])
        )
        for a in range(GROUP):
            part_send[a] = jnp.concatenate(
                [joined[a * small : (a + 1) * small], fill], axis=0
            ).astype(BF16)
        for r in (2, 3, 1):
            part_copy(r).start()
        finish(s)
        proj_out[own] = part_send[own].astype(F32)
        for r in (1, 2, 3):
            part_copy(r).wait_recv()
            proj_out[partner(own, r)] = part_land[r - 1].astype(F32)

        for q in range(grad_land.shape[0]):
            for r in (1, 2, 3):
                grad_copy(q, r).wait_send()
        for i in range(2):
            near_copy(s, i).wait_send()
        far_copy(s).wait_send()
        for r in (1, 2, 3):
            part_copy(r).wait_send()
        for part in range(2):
            cross_copy(part).wait_send()

        def leave(k, carry):
            for way in range(2):
                for i in range(3):
                    met_copy(k, way, i).wait_send()
            return carry

        lax.fori_loop(0, dp_size, leave, 0)

        def leave_ring(k, carry):
            for way in range(2):
                for part in range(2):
                    ring_copy(k, way, part).wait_send()
            return carry

        lax.fori_loop(0, dp_size - 1, leave_ring, 0)
        for q in range(head_count):
            pair_copy(q).wait_send()

            def leave_own(k, carry):
                own_copy(q, k).wait_send()
                return carry

            lax.fori_loop(1, half, leave_own, 0)


def attend_back(
    dp_size, parts, mixed_grad, weight, draws, hot, proj, state, mixed, den, soft, phi_q, phi_k,
    down_grad, up_grad, tail,
):
    seqs, _, rows, model = parts.shape
    heads = draws.shape[0]
    width = heads * HD
    total = GROUP * rows
    n = dp_size
    ring_rows = down_grad.shape[1] + up_grad.shape[1] + tail.shape[1]
    own_rows = aligned(model // n + 1)
    part_rows = aligned(model // (n * GROUP) + 1)
    single = pl.Buffered(1)
    whole = lambda *shape: pl.BlockSpec(
        shape, lambda s, h: (0,) * len(shape), pipeline_mode=single
    )
    mode = single if n > 16 else None
    by_seq = lambda *shape: pl.BlockSpec(
        (None,) + shape, lambda s, h: (s,) + (0,) * len(shape), pipeline_mode=mode
    )
    by_head = lambda *shape: pl.BlockSpec(
        (None, None) + shape, lambda s, h: (s, h) + (0,) * len(shape), pipeline_mode=mode
    )
    anywhere = pl.BlockSpec(memory_space=pl.ANY)
    dma = pltpu.SemaphoreType.DMA
    return pl.pallas_call(
        lambda *refs: attend_back_kernel(dp_size, *refs),
        grid=(seqs, heads),
        out_shape=(
            jax.ShapeDtypeStruct((seqs * rows, model), F32),
            jax.ShapeDtypeStruct((ring_rows, model), F32),
            jax.ShapeDtypeStruct((GROUP, part_rows, 3 * width), F32),
        ),
        in_specs=[
            by_seq(GROUP, rows, model), whole(*mixed_grad.shape), whole(3 * width, model),
            pl.BlockSpec((None, HD, FEAT), lambda s, h: (h, 0, 0)),
            by_seq(16, total), by_seq(3 * width, total), by_head(STATES, FEAT), by_head(HD, total),
            by_head(8, total), by_head(total, total), by_head(FEAT, total), by_head(FEAT, total),
            anywhere, anywhere, anywhere,
        ],
        out_specs=(
            whole(seqs * rows, model), whole(ring_rows, model), whole(GROUP, part_rows, 3 * width),
        ),
        scratch_shapes=[
            pltpu.VMEM((width, total), F32),
            pltpu.VMEM((HD + 16, total), BF16),
            pltpu.VMEM((total, HD + 16), BF16),
            pltpu.VMEM((total, total), BF16),
            pltpu.VMEM((HD, total), F32),
            pltpu.VMEM((3 * width, total), BF16),
            pltpu.VMEM((seqs, 3, rows, width), BF16),
            pltpu.VMEM((2, rows, model), BF16),
            pltpu.VMEM((seqs, 2, rows, model), BF16),
            pltpu.VMEM((2, rows, model), F32),
            pltpu.VMEM((rows, model), BF16),
            pltpu.VMEM((seqs, rows, model), BF16),
            pltpu.VMEM((n, 2, ring_rows, model), BF16),
            pltpu.VMEM((n, 2, ring_rows, model), BF16),
            pltpu.VMEM((n - 1, 2, ring_rows, model), BF16),
            pltpu.VMEM((ring_rows, model), BF16),
            pltpu.VMEM((3 * width, model + 128), F32),
            pltpu.VMEM((heads, 2, n // 2, own_rows, 3 * HD), BF16),
            pltpu.VMEM((heads, n // 2, own_rows, 3 * HD), BF16),
            pltpu.VMEM((heads, n // 2, own_rows, 3 * HD), BF16),
            pltpu.VMEM((heads, n // 2, own_rows, 3 * HD), BF16),
            pltpu.VMEM((GROUP, part_rows, 3 * width), BF16),
            pltpu.VMEM((3, part_rows, 3 * width), BF16),
            dma((2, seqs, 3)),
            dma((2, seqs, 2)),
            dma((2, seqs)),
            dma((n, 2, 3)),
            dma((2, n, 2, 3)),
            dma((2, n - 1, 2, 2)),
            dma((2, 2)),
            dma((2, heads)),
            dma((2, heads, n // 2)),
            dma((2, 3)),
        ],
        compiler_params=pltpu.CompilerParams(
            vmem_limit_bytes=VMEM + (3 * 1024 * 1024 if n > 16 else 0), collective_id=2, has_side_effects=True
        ),
        cost_estimate=pl.CostEstimate(
            flops=48_000_000_000, bytes_accessed=40_000_000, transcendentals=0
        ),
        name="attend_back",
    )(
        parts, mixed_grad, weight, draws, hot, proj, state, mixed, den, soft, phi_q, phi_k,
        down_grad, up_grad, tail,
    )


def finish_kernel(
    starts, heads, attn_grad, resid_grad, hidden, sums, proj_sums, weight_rows, gain_ref, shift_ref,
    input_out, norm1_gain_out, norm1_bias_out, qkv_out, qkv_bias_out, out_out, out_bias_out,
    norm2_gain_out, norm2_bias_out, up_out, up_bias_out, down_out, down_bias_out,
):
    gain, shift = as_row(gain_ref), as_row(shift_ref)
    normed, scale = row_stats(hidden[...].astype(F32))
    input_out[...] = resid_grad[...] + norm_back(attn_grad[...] * gain, normed, scale)

    @pl.when(pl.program_id(0) == 0)
    def _():
        index = lax.axis_index("dp") * GROUP + lax.axis_index("feat")
        small, model = out_out.shape
        share = down_out.shape[0]
        ff = up_out.shape[1]

        def own(row, size):
            length = row.shape[1]
            wide = jnp.broadcast_to(row, (8, length))
            back = lax.rem(length - lax.rem(index * size, length), length)
            return pltpu.roll(wide, back, 1)[0:1, 0:size]

        down_out[...] = sums[0:share]
        first = starts[0]
        up_out[...] = jnp.concatenate(
            [sums[first + i * small : first + (i + 1) * small] for i in range(ff // model)], axis=1
        )
        first = starts[0] + starts[1]
        out_out[...] = sums[first : first + small]
        totals = first + small
        for i, out in enumerate((down_bias_out, out_bias_out, norm2_gain_out, norm2_bias_out)):
            out[...] = own(sums[totals + i : totals + i + 1], small).reshape(small)
        per_row = model // share
        level = index // per_row
        row = jnp.zeros((1, model), F32)
        for i in range(ff // model):
            row = jnp.where(level == i, sums[totals + 4 + i : totals + 5 + i], row)
        up_bias_out[...] = own(row, share).reshape(share)

        pieces = []
        for kind in range(3):
            for f in range(GROUP):
                for h in range(heads):
                    lanes = slice((h * 3 + kind) * HD, (h * 3 + kind + 1) * HD)
                    pieces.append(proj_sums[f, 0 : small + 1, lanes])
        grid = jnp.concatenate(pieces, axis=1)
        weight_sum, bias_sum = grid[0:small], grid[small : small + 1]
        qkv_out[...] = weight_sum
        qkv_bias_out[...] = own(bias_sum, 3 * small).reshape(3 * small)
        wide = weight_rows[...].astype(F32)

        def to_row(column):
            column = jnp.concatenate(
                [column, jnp.zeros((-small % 128, 1), F32)], axis=0
            )
            return jnp.broadcast_to(column, (column.shape[0], 128)).T[0:1, 0:small]

        bias_grad = to_row(jnp.sum(wide * bias_sum, axis=1, keepdims=True))
        gain_grad = to_row(jnp.sum(wide * weight_sum, axis=1, keepdims=True))
        norm1_bias_out[...] = bias_grad.reshape(small)
        gain_grad = (gain_grad - own(shift, small) * bias_grad) / own(gain, small)
        norm1_gain_out[...] = gain_grad.reshape(small)


def finish_all(
    attn_grad, resid_grad, hidden, sums, proj_sums, weight_rows, gain, shift, starts, devices, ff,
    heads,
):
    seqs, rows, model = hidden.shape
    small, share = model // devices, ff // devices
    whole = lambda *shape: pl.BlockSpec(shape, lambda s: (0,) * len(shape))
    by_seq = pl.BlockSpec((rows, model), lambda s: (s, 0))
    shapes = (
        (small,), (small,), (small, 3 * model), (3 * small,), (small, model), (small,), (small,),
        (small,), (small, ff), (share,), (share, model), (small,),
    )
    return pl.pallas_call(
        lambda *refs: finish_kernel(starts, heads, *refs),
        grid=(seqs,),
        out_shape=(jax.ShapeDtypeStruct((seqs * rows, model), F32),)
        + tuple(jax.ShapeDtypeStruct(shape, F32) for shape in shapes),
        in_specs=[
            by_seq, by_seq, pl.BlockSpec((None, rows, model), lambda s: (s, 0, 0)),
            whole(*sums.shape), whole(*proj_sums.shape), whole(*weight_rows.shape), whole(model),
            whole(model),
        ],
        out_specs=(by_seq,) + tuple(whole(*shape) for shape in shapes),
        compiler_params=pltpu.CompilerParams(vmem_limit_bytes=VMEM),
        name="finish_all",
    )(attn_grad, resid_grad, hidden, sums, proj_sums, weight_rows, gain, shift)


def per_device(
    hidden_in, norm1_gain, norm1_bias, qkv_weight, qkv_bias, feature_draws, out_weight, out_bias,
    norm2_gain, norm2_bias, up_weight, up_bias, down_weight, down_bias, block_bucket, out_grad,
):
    seqs, rows, model = hidden_in.shape
    ff = up_weight.shape[1]
    dp_size = lax.axis_size("dp")
    devices = dp_size * GROUP
    small = model // devices
    heads = feature_draws.shape[0] // GROUP
    flat = (seqs * rows, model)

    (
        parts, mixed_parts, proj, state, mixed, den, hot, own_weight, own_draws, soft, phi_q, phi_k,
    ) = attend(
        block_bucket, hidden_in, norm1_gain, norm1_bias, qkv_bias, qkv_weight, feature_draws
    )
    layer_out, resid_grad, mixed_grad, down_grad, up_grad, tail = block_layer(
        mixed_parts, hidden_in.reshape(flat), out_grad.reshape(flat), out_weight, out_bias,
        norm2_gain, norm2_bias, down_bias, up_bias, up_weight, down_weight, devices,
    )
    attn_grad, sums, proj_sums = attend_back(
        dp_size, parts, mixed_grad, own_weight, own_draws, hot, proj, state, mixed, den, soft,
        phi_q, phi_k, down_grad, up_grad, tail,
    )
    index = lax.axis_index("dp") * GROUP + lax.axis_index("feat")
    weight_rows = lax.dynamic_slice_in_dim(qkv_weight, index * small, small, 0)
    (
        input_grad, norm1_gain_sum, norm1_bias_sum, qkv_weight_sum, qkv_bias_sum, out_weight_sum,
        out_bias_sum, norm2_gain_sum, norm2_bias_sum, up_sum, up_bias_sum, down_sum, down_bias_sum,
    ) = finish_all(
        attn_grad, resid_grad, hidden_in, sums, proj_sums, weight_rows, norm1_gain, norm1_bias,
        (down_grad.shape[1], up_grad.shape[1]), devices, ff, heads,
    )
    return (
        layer_out.reshape(hidden_in.shape), input_grad.reshape(hidden_in.shape), norm1_gain_sum,
        norm1_bias_sum, qkv_weight_sum, qkv_bias_sum, out_weight_sum, out_bias_sum, norm2_gain_sum,
        norm2_bias_sum, up_sum, up_bias_sum, down_sum, down_bias_sum,
    )


def solution(mesh):
    both = ("dp", "feat")
    rows = P("dp", "feat", None)
    in_specs = (
        rows, P(), P(), P(), P(), P(None, None, "feat"), P(), P(), P(), P(), P(), P(), P(), P(),
        P("dp", None, None), rows,
    )
    out_specs = (
        rows, rows, P(both), P(both), P(both, None), P(both), P(both, None), P(both), P(both),
        P(both), P(both, None), P(both), P(both, None), P(both),
    )
    return jax.shard_map(
        per_device, mesh=mesh, in_specs=in_specs, out_specs=out_specs, check_vma=False
    )
```

```python
import math

import jax
import jax.numpy as jnp
from jax import lax
from jax.experimental import pallas as pl
from jax.experimental.pallas import tpu as pltpu
from jax.sharding import PartitionSpec as P

HD = 64
FEAT = 256
BLOCK = 64
NBUCK = 4
GROUP = 4
CHUNK = 256
STATES = NBUCK * HD + 16
FAR = 16384.0
VMEM = 60 * 1024 * 1024

F32 = jnp.float32
BF16 = jnp.bfloat16
MESH = pl.DeviceIdType.MESH


def mat(left, right):
    return jnp.dot(left, right, preferred_element_type=F32)


def mat_nt(left, right):
    return lax.dot_general(left, right, (((1,), (1,)), ((), ())), preferred_element_type=F32)


def mat_tn(left, right):
    return lax.dot_general(left, right, (((0,), (0,)), ((), ())), preferred_element_type=F32)


def row_stats(values):
    row_mean = jnp.mean(values, axis=-1, keepdims=True)
    centered = values - row_mean
    scale = lax.rsqrt(jnp.mean(centered * centered, axis=-1, keepdims=True) + 1e-05)
    return (centered * scale, scale)


def norm_back(cotangent, normed, scale):
    mean_one = jnp.mean(cotangent, axis=-1, keepdims=True)
    mean_two = jnp.mean(cotangent * normed, axis=-1, keepdims=True)
    return scale * (cotangent - mean_one - normed * mean_two)


def features(vectors, draws):
    wide = vectors.astype(F32)
    square = jnp.sum(wide * wide, axis=0, keepdims=True) * (0.5 / math.sqrt(HD))
    return jnp.exp(mat_tn(draws, vectors) - (square + 0.5 * math.log(FEAT)))


def spread(rows, marks):
    return [rows * marks[u : u + 1] for u in range(NBUCK)]


def pick(stacked, marks):
    total = stacked[0:HD] * marks[0:1]
    for u in range(1, NBUCK):
        total = total + stacked[u * HD : (u + 1) * HD] * marks[u : u + 1]
    return total


def away_marks(hot):
    live = (lax.broadcasted_iota(jnp.int32, hot.shape, 0) < NBUCK).astype(F32)
    return live - hot.astype(F32)


def partner(own, r):
    x, core = own // 2, own % 2
    if r & 2:
        x = 1 - x
    if r & 1:
        core = 1 - core
    return 2 * x + core


def as_row(ref):
    return ref[...].reshape(1, ref.shape[0])


def aligned(count):
    return -(-count // 16) * 16


def remote(src, dst, send, recv, place):
    return pltpu.make_async_remote_copy(
        src_ref=src, dst_ref=dst, send_sem=send, recv_sem=recv, device_id=place, device_id_type=MESH
    )


def head_rows(h, kind, heads):
    return pl.ds(pl.multiple_of((kind * heads + h) * HD, HD), HD)


def attend_kernel(
    bucket, hidden, gain_ref, shift_ref, bias_ref, weight_any, draws_in,
    parts_any, mix_any, proj_out, state_out, mixed_out, den_out, hot_out, weight_out, draws_out,
    soft_out, phi_q_out, phi_k_out,
    parts, mix_land, mix_send, raw, bias_row, bias_scr, draws_land,
    query_scr, key_scr, value_scr, low_scr, gather_scr,
    raw_sem, part_send, part_recv, draw_send, draw_recv, mix_send_sem, mix_recv_sem, out_sem,
):
    s, h = pl.program_id(0), pl.program_id(1)
    seqs, rows, model = hidden.shape
    heads = draws_out.shape[0]
    total = GROUP * rows
    width = heads * HD
    own = lax.axis_index("feat")
    near, across = {"feat": partner(own, 1)}, {"feat": partner(own, 2)}

    def part_copy(q, kind):
        src, dst, place = ((0, 1, near), (0, 2, across), (2, 3, near))[kind]
        return remote(
            parts.at[q, src], parts.at[q, dst], part_send.at[q, kind], part_recv.at[q, kind], place
        )

    def draw_copy(r):
        other = partner(own, r)
        return remote(
            draws_in.at[pl.ds(other * heads, heads)], draws_land.at[r - 1],
            draw_send.at[r - 1], draw_recv.at[r - 1], {"feat": other},
        )

    def mix_copy(q, r):
        return remote(
            mix_send.at[q, r], mix_land.at[q, r], mix_send_sem.at[q, r - 1],
            mix_recv_sem.at[q, r - 1], {"feat": partner(own, r)},
        )

    def raw_copy(j):
        cols = pl.ds(pl.multiple_of(j * model + (own // 2) * 2 * width, 2 * width), 2 * width)
        return pltpu.make_async_copy(weight_any.at[:, cols], raw.at[j], raw_sem.at[j])

    def out_copy(q):
        return pltpu.make_async_copy(parts.at[q], parts_any.at[q], out_sem.at[q])

    @pl.when((s == 0) & (h == 0))
    def _():
        for j in range(3):
            raw_copy(j).start()
        barrier = pltpu.get_barrier_semaphore()
        for r in (1, 2, 3):
            pl.semaphore_signal(
                barrier, inc=1, device_id={"feat": partner(own, r)}, device_id_type=MESH
            )
        gain, shift = as_row(gain_ref), as_row(shift_ref)
        first = row_stats(hidden[0].astype(F32))[0] * gain + shift
        parts[0, 0] = first.astype(BF16)
        pl.semaphore_wait(barrier, 3)
        part_copy(0, 1).start()
        part_copy(0, 0).start()
        for r in (1, 2, 3):
            draw_copy(r).start()
        for q in range(1, seqs):
            normed = row_stats(hidden[q].astype(F32))[0] * gain + shift
            parts[q, 0] = normed.astype(BF16)
            part_copy(q, 1).start()
            part_copy(q, 0).start()
        core = own % 2
        bias_row[...] = as_row(bias_ref)
        for j in range(3):
            raw_copy(j).wait()
            piece = raw[j].astype(F32)
            piece = jnp.where(core == 0, piece[:, 0:width], piece[:, width:])
            weight_out[j * width : (j + 1) * width] = piece.T.astype(BF16)
            cols = pl.ds(pl.multiple_of(j * model + (own // 2) * 2 * width, 2 * width), 2 * width)
            pair = jnp.broadcast_to(bias_row[:, cols], (128, 2 * width))
            pair = jnp.where(core == 0, pair[:, 0:width], pair[:, width:])
            bias_scr[j * width : (j + 1) * width] = pair.T
        part_copy(0, 1).wait_recv()
        part_copy(0, 2).start()
        for r in (1, 2, 3):
            draw_copy(r).wait_recv()
        mine = draws_in[pl.ds(own * heads, heads)]
        draws_out[...] = jnp.concatenate(
            [mine] + [draws_land[r - 1] for r in (1, 2, 3)], axis=2
        )

    @pl.when(h == 0)
    def _():
        per = rows // BLOCK
        lanes = lax.broadcasted_iota(jnp.int32, (16, total), 1) // BLOCK
        level = lax.broadcasted_iota(jnp.int32, (16, total), 0)
        ids = jnp.full((16, total), -1, jnp.int32)
        for r in range(GROUP):
            for i in range(per):
                ids = jnp.where(
                    lanes == r * per + i, bucket[s, partner(own, r) * per + i, 0], ids
                )
        hot_out[...] = (ids == level).astype(F32).astype(BF16)

        def project(r):
            cols = slice(r * rows, (r + 1) * rows)
            piece = mat_nt(weight_out[...], parts[s, r]) + bias_scr[:, 0:1]
            proj_out[:, cols] = piece.astype(BF16)

        project(0)
        part_copy(s, 0).wait_recv()
        project(1)
        project(2)
        part_copy(s, 2).wait_recv()
        project(3)
        out_copy(s).start()

    query = proj_out[head_rows(h, 0, heads)]
    key = proj_out[head_rows(h, 1, heads)]
    value = proj_out[head_rows(h, 2, heads)]
    draws = draws_out[h]
    hot = hot_out[...]
    hot_wide = hot.astype(F32)
    away = away_marks(hot).astype(BF16)
    phi_q = features(query, draws).astype(BF16)
    phi_k = features(key, draws).astype(BF16)
    phi_q_out[...] = phi_q
    phi_k_out[...] = phi_k
    spread_value = jnp.concatenate(spread(value, away) + [away], axis=0)
    state = mat_nt(spread_value, phi_k).astype(BF16)
    state_out[...] = state
    low = mat(state, phi_q)
    low_scr[0:HD] = pick(low, hot_wide)
    low_den = jnp.sum(low[NBUCK * HD :] * hot_wide, axis=0, keepdims=True)
    low_scr[HD : HD + 8] = jnp.broadcast_to(low_den, (8, total))
    query_scr[...] = jnp.concatenate([query * (1.0 / math.sqrt(HD)), hot], axis=0).astype(BF16)
    key_scr[...] = jnp.concatenate([key, away * -FAR], axis=0).astype(F32).T.astype(BF16)
    value_scr[0:HD] = value
    value_scr[HD:] = jnp.ones((16, total), BF16)

    for c in range(total // CHUNK):
        cols = slice(c * CHUNK, (c + 1) * CHUNK)
        weights = jnp.exp(mat(key_scr[...], query_scr[:, cols])).astype(BF16)
        soft_out[:, cols] = weights
        exact = mat(value_scr[...], weights)
        den = low_scr[HD : HD + 8, cols] + exact[HD : HD + 8]
        mixed = (low_scr[0:HD, cols] + exact[0:HD]) / den[0:1]
        mixed_out[:, cols] = mixed
        den_out[:, cols] = den
        gather_scr[pl.ds(pl.multiple_of(h * HD, HD), HD), cols] = mixed

    @pl.when((h == heads - 2) & (s < seqs - 1))
    def _():
        part_copy(s + 1, 1).wait_recv()
        part_copy(s + 1, 2).start()

    @pl.when(h == heads - 1)
    def _():
        for r in range(GROUP):
            piece = gather_scr[:, r * rows : (r + 1) * rows].T.astype(BF16)
            if r == 0:
                mix_land[s, 0] = piece
            else:
                mix_send[s, r] = piece
                mix_copy(s, r).start()

    @pl.when((s == seqs - 1) & (h == heads - 1))
    def _():
        for q in range(seqs):
            for r in (1, 2, 3):
                mix_copy(q, r).wait_recv()
        done = pltpu.make_async_copy(mix_land, mix_any, out_sem.at[seqs])
        done.start()
        for q in range(seqs):
            for kind in range(3):
                part_copy(q, kind).wait_send()
            for r in (1, 2, 3):
                mix_copy(q, r).wait_send()
            out_copy(q).wait()
        for r in (1, 2, 3):
            draw_copy(r).wait_send()
        done.wait()


def attend(bucket, hidden, gain, shift, bias, weight, draws):
    seqs, rows, model = hidden.shape
    heads = draws.shape[0] // GROUP
    width = heads * HD
    total = GROUP * rows
    whole = lambda *shape: pl.BlockSpec(shape, lambda s, h: (0,) * len(shape))
    by_seq = lambda *shape: pl.BlockSpec((None,) + shape, lambda s, h: (s,) + (0,) * len(shape))
    by_head = lambda *shape: pl.BlockSpec(
        (None, None) + shape, lambda s, h: (s, h) + (0,) * len(shape)
    )
    anywhere = pl.BlockSpec(memory_space=pl.ANY)
    return pl.pallas_call(
        attend_kernel,
        grid=(seqs, heads),
        out_shape=(
            jax.ShapeDtypeStruct((seqs, GROUP, rows, model), BF16),
            jax.ShapeDtypeStruct((seqs, GROUP, rows, width), BF16),
            jax.ShapeDtypeStruct((seqs, 3 * width, total), BF16),
            jax.ShapeDtypeStruct((seqs, heads, STATES, FEAT), BF16),
            jax.ShapeDtypeStruct((seqs, heads, HD, total), F32),
            jax.ShapeDtypeStruct((seqs, heads, 8, total), F32),
            jax.ShapeDtypeStruct((seqs, 16, total), BF16),
            jax.ShapeDtypeStruct((3 * width, model), BF16),
            jax.ShapeDtypeStruct((heads, HD, FEAT), BF16),
            jax.ShapeDtypeStruct((seqs, heads, total, total), BF16),
            jax.ShapeDtypeStruct((seqs, heads, FEAT, total), BF16),
            jax.ShapeDtypeStruct((seqs, heads, FEAT, total), BF16),
        ),
        in_specs=[
            pl.BlockSpec(memory_space=pltpu.SMEM),
            whole(seqs, rows, model), whole(model), whole(model), whole(3 * model), anywhere,
            whole(*draws.shape),
        ],
        out_specs=(
            anywhere, anywhere, by_seq(3 * width, total), by_head(STATES, FEAT), by_head(HD, total),
            by_head(8, total), by_seq(16, total), whole(3 * width, model), whole(heads, HD, FEAT),
            by_head(total, total), by_head(FEAT, total), by_head(FEAT, total),
        ),
        scratch_shapes=[
            pltpu.VMEM((seqs, GROUP, rows, model), BF16),
            pltpu.VMEM((seqs, GROUP, rows, width), BF16),
            pltpu.VMEM((seqs, GROUP, rows, width), BF16),
            pltpu.VMEM((3, model, 2 * width), BF16),
            pltpu.VMEM((1, 3 * model), F32),
            pltpu.VMEM((3 * width, 128), F32),
            pltpu.VMEM((3, heads, HD, draws.shape[2]), BF16),
            pltpu.VMEM((HD + 16, total), BF16),
            pltpu.VMEM((total, HD + 16), BF16),
            pltpu.VMEM((HD + 16, total), BF16),
            pltpu.VMEM((HD + 8, total), F32),
            pltpu.VMEM((width, total), F32),
            pltpu.SemaphoreType.DMA((3,)),
            pltpu.SemaphoreType.DMA((seqs, 3)),
            pltpu.SemaphoreType.DMA((seqs, 3)),
            pltpu.SemaphoreType.DMA((3,)),
            pltpu.SemaphoreType.DMA((3,)),
            pltpu.SemaphoreType.DMA((seqs, 3)),
            pltpu.SemaphoreType.DMA((seqs, 3)),
            pltpu.SemaphoreType.DMA((seqs + 1,)),
        ],
        compiler_params=pltpu.CompilerParams(
            vmem_limit_bytes=VMEM, collective_id=1, has_side_effects=True
        ),
        cost_estimate=pl.CostEstimate(
            flops=24_000_000_000, bytes_accessed=20_000_000, transcendentals=0
        ),
        name="attend",
    )(bucket, hidden, gain, shift, bias, weight, draws)


def block_kernel(
    direct, parts_ref, hidden, grad, out_w, out_b, gain_ref, shift_ref, down_b, up_b, up, down,
    layer_out, resid_out, mixed_grad, down_out, up_out, tail_out,
    mixed, resid_scr, in_scr, in_t, acc_out, acc_in, act_scr, pre_scr, vec_scr, bias_row,
):
    step = pl.program_id(0)
    model = hidden.shape[1]
    count = hidden.shape[0] // CHUNK
    spans = [slice(c * CHUNK, (c + 1) * CHUNK) for c in range(count)]
    subs = [slice(u * model, (u + 1) * model) for u in range(up.shape[1] // model)]
    owners = tail_out.shape[0]
    small = model // owners

    @pl.when(step == 0)
    def _():
        own = lax.axis_index("feat")
        for c, span in enumerate(spans):
            pieces = [parts_ref[c, r] for r in range(GROUP)]
            pieces = [jnp.where(own % 2 == 1, pieces[r ^ 1], pieces[r]) for r in range(GROUP)]
            pieces = [jnp.where(own // 2 == 1, pieces[r ^ 2], pieces[r]) for r in range(GROUP)]
            mixed[span] = jnp.concatenate(pieces, axis=1)
            resid = hidden[span].astype(F32) + mat(mixed[span], out_w[...]) + as_row(out_b)
            resid_scr[span] = resid
            normed, _ = row_stats(resid)
            inner = normed * as_row(gain_ref) + as_row(shift_ref)
            in_scr[span] = inner.astype(BF16)
            in_t[:, span] = inner.T.astype(BF16)
        acc_out[...] = jnp.zeros_like(acc_out)
        acc_in[...] = jnp.zeros_like(acc_in)
        bias_row[...] = as_row(up_b)

    slope = math.sqrt(2.0 / math.pi)
    up_terms = []
    for u, sub in enumerate(subs):
        total = jnp.zeros((1, model), F32)
        place = (step * len(subs) + u) * model
        up_bias = bias_row[:, pl.ds(pl.multiple_of(place, model), model)]
        for span in spans:
            pre = mat(in_scr[span], up[:, sub]) + up_bias
            square = pre * pre
            tanh = jnp.tanh(pre * (slope + (slope * 0.044715) * square))
            half = 0.5 * (1.0 + tanh)
            act = (pre * half).astype(BF16)
            bend = half + (0.5 * pre) * (1.0 - tanh * tanh) * (
                slope + (3.0 * slope * 0.044715) * square
            )
            pre_grad = mat_nt(grad[span], down[sub]) * bend
            total = total + jnp.sum(pre_grad, axis=0, keepdims=True)
            pre_low = pre_grad.astype(BF16)
            act_scr[span] = act
            pre_scr[span] = pre_low
            acc_out[span] += mat(act, down[sub])
            acc_in[span] += mat_nt(pre_low, up[:, sub])
        vec_scr[pl.ds(4 + step * len(subs) + u, 1)] = total
        down_term = mat_tn(act_scr[...], grad[...])
        up_term = mat(in_t[...], pre_scr[...])
        if direct:
            share = down_out.shape[1]
            for i in range(model // share):
                down_out[u * (model // share) + i] = down_term[
                    i * share : (i + 1) * share
                ].astype(BF16)
            up_terms.append(up_term)
        else:
            down_out[sub] = down_term.astype(BF16)
            up_out[:, sub] = up_term.astype(BF16)
    if direct:
        for i in range(owners):
            own_rows = slice(i * small, (i + 1) * small)
            up_out[i] = jnp.concatenate([term[own_rows] for term in up_terms], axis=0).astype(BF16)

    @pl.when(step == pl.num_programs(0) - 1)
    def _():
        sums = [jnp.zeros((1, model), F32) for _ in range(4)]
        for span in spans:
            resid = resid_scr[span]
            layer_out[span] = (resid + acc_out[span] + as_row(down_b)).astype(BF16)
            normed, scale = row_stats(resid)
            inner_grad = acc_in[span]
            wide = grad[span].astype(F32)
            resid_grad = wide + norm_back(inner_grad * as_row(gain_ref), normed, scale)
            resid_out[span] = resid_grad
            low = resid_grad.astype(BF16)
            in_scr[span] = low
            for i, term in enumerate((wide, resid_grad, inner_grad * normed, inner_grad)):
                sums[i] = sums[i] + jnp.sum(term, axis=0, keepdims=True)
            back = mat_nt(low, out_w[...]).astype(BF16)
            part = model // GROUP
            for a in range(GROUP):
                mixed_grad[a, span] = back[:, a * part : (a + 1) * part]
        for i in range(4):
            vec_scr[i : i + 1] = sums[i]
        out_term = mat_tn(mixed[...], in_scr[...])
        fill = tail_out.shape[1] - small - 8
        extra = [jnp.zeros((fill, model), F32)] if fill else []
        for i in range(owners):
            tail_out[i] = jnp.concatenate(
                [out_term[i * small : (i + 1) * small], vec_scr[...]] + extra, axis=0
            ).astype(BF16)


def block_layer(parts, hidden, grad, out_w, out_b, gain, shift, down_b, up_b, up, down, devices):
    tokens, model = hidden.shape
    ff = up.shape[1]
    steps = 2
    tile = ff // steps
    small, share = model // devices, ff // devices
    direct = small % 8 == 0 and share % 16 == 0
    tail_rows = aligned(small + 8)
    single = pl.Buffered(1)
    whole = lambda *shape: pl.BlockSpec(
        shape, lambda t: (0,) * len(shape), pipeline_mode=single
    )
    part = model // GROUP
    if direct:
        grad_shapes = (
            jax.ShapeDtypeStruct((devices, share, model), BF16),
            jax.ShapeDtypeStruct((devices, ff // model * small, model), BF16),
        )
        grad_specs = (
            pl.BlockSpec((devices // steps, share, model), lambda t: (t, 0, 0)),
            pl.BlockSpec((devices, tile // model * small, model), lambda t: (0, t, 0)),
        )
    else:
        grad_shapes = (
            jax.ShapeDtypeStruct((ff, model), BF16),
            jax.ShapeDtypeStruct((model, ff), BF16),
        )
        grad_specs = (
            pl.BlockSpec((tile, model), lambda t: (t, 0)),
            pl.BlockSpec((model, tile), lambda t: (0, t)),
        )
    layer_out, resid_grad, mixed_grad, down_grad, up_grad, tail = pl.pallas_call(
        lambda *refs: block_kernel(direct, *refs),
        grid=(steps,),
        out_shape=(
            jax.ShapeDtypeStruct((tokens, model), BF16),
            jax.ShapeDtypeStruct((tokens, model), F32),
            jax.ShapeDtypeStruct((GROUP, tokens, part), BF16),
        )
        + grad_shapes
        + (jax.ShapeDtypeStruct((devices, tail_rows, model), BF16),),
        in_specs=[
            whole(*parts.shape), whole(tokens, model), whole(tokens, model), whole(model, model),
            whole(model), whole(model), whole(model), whole(model), whole(ff),
            pl.BlockSpec((model, tile), lambda t: (0, t)),
            pl.BlockSpec((tile, model), lambda t: (t, 0)),
        ],
        out_specs=(whole(tokens, model), whole(tokens, model), whole(GROUP, tokens, part))
        + grad_specs
        + (whole(devices, tail_rows, model),),
        scratch_shapes=[
            pltpu.VMEM((tokens, model), BF16),
            pltpu.VMEM((tokens, model), F32),
            pltpu.VMEM((tokens, model), BF16),
            pltpu.VMEM((model, tokens), BF16),
            pltpu.VMEM((tokens, model), F32),
            pltpu.VMEM((tokens, model), F32),
            pltpu.VMEM((tokens, model), BF16),
            pltpu.VMEM((tokens, model), BF16),
            pltpu.VMEM((8, model), F32),
            pltpu.VMEM((1, ff), F32),
        ],
        compiler_params=pltpu.CompilerParams(vmem_limit_bytes=VMEM),
        cost_estimate=pl.CostEstimate(
            flops=26_000_000_000, bytes_accessed=30_000_000, transcendentals=0
        ),
        name="block_layer",
    )(parts, hidden, grad, out_w, out_b, gain, shift, down_b, up_b, up, down)
    if not direct:
        fit = lambda a: jnp.pad(a, ((0, 0), (0, aligned(a.shape[1]) - a.shape[1]), (0, 0)))
        down_grad = fit(down_grad.reshape(devices, share, model))
        up_grad = up_grad.reshape(devices, small, ff // model, model).transpose(0, 2, 1, 3)
        up_grad = fit(up_grad.reshape(devices, ff // model * small, model))
    return layer_out, resid_grad, mixed_grad, down_grad, up_grad, tail


def attend_back_kernel(
    dp_size, x_ref, mixed_grad, weight, draws_ref, hot_ref, proj, state_ref, mixed_ref, den_ref,
    soft_ref, phi_q_ref, phi_k_ref, down_any, up_any, tail_any,
    attn_out, ring_out, proj_out,
    grad_scr, num_scr, value_scr, score_scr, exact_scr, proj_scr,
    grad_land, near_send, near_land, far_keep, far_send, far_land,
    mine, met, ring_land, cross_land,
    weight_acc, own_send, pair_land, own_mid, own_land, part_send, part_land,
    grad_sems, near_sems, far_sems, mine_sem, met_sems, ring_sems, cross_sems, pair_sems, own_sems,
    part_sems,
):
    s, h = pl.program_id(0), pl.program_id(1)
    seqs, heads = pl.num_programs(0), pl.num_programs(1)
    rows, model = x_ref.shape[1], x_ref.shape[2]
    head_count = proj_scr.shape[0] // (3 * HD)
    width = head_count * HD
    total = GROUP * rows
    root = 1.0 / math.sqrt(HD)
    own, me = lax.axis_index("feat"), lax.axis_index("dp")
    own_x, own_core = own // 2, own % 2
    near, across = {"feat": partner(own, 1)}, {"feat": partner(own, 2)}
    last = (s == seqs - 1) & (h == heads - 1)

    def grad_copy(q, r):
        other = partner(own, r)
        return remote(
            mixed_grad.at[other, pl.ds(q * rows, rows)], grad_land.at[q, r - 1],
            grad_sems.at[0, q, r - 1], grad_sems.at[1, q, r - 1], {"feat": other},
        )

    def near_copy(q, i):
        return remote(
            near_send.at[i], near_land.at[q, i], near_sems.at[0, q, i], near_sems.at[1, q, i], near
        )

    def far_copy(q):
        return remote(far_send, far_land.at[q], far_sems.at[0, q], far_sems.at[1, q], across)

    odd = me % 2
    half = dp_size // 2
    spot = (1 - odd) * (me // 2) + odd * (dp_size - 1 - me // 2)

    def at_spot(p):
        p = lax.rem(p + dp_size, dp_size)
        upper = p // half
        return (1 - upper) * (2 * p) + upper * (2 * (dp_size - 1 - p) + 1)

    def chunk(k, way):
        return at_spot(spot - 1 - k) if way == 0 else at_spot(lax.rem(spot + 1 + k, dp_size))

    sources = (down_any, up_any, tail_any)
    lengths = [ref.shape[1] for ref in sources]
    starts = [sum(lengths[:i]) for i in range(3)]

    def owner(k, way, core):
        return chunk(k, way) * GROUP + 2 * way + core

    def mine_copy(k, way, i):
        return pltpu.make_async_copy(
            sources[i].at[owner(k, way, own_core)],
            mine.at[k, way, pl.ds(starts[i], lengths[i])],
            mine_sem.at[k, way, i],
        )

    def met_copy(k, way, i):
        return remote(
            sources[i].at[owner(k, way, 1 - own_core)],
            met.at[k, way, pl.ds(starts[i], lengths[i])],
            met_sems.at[0, k, way, i], met_sems.at[1, k, way, i], near,
        )

    cut = aligned(mine.shape[2] // 2)
    halves = (pl.ds(0, cut), pl.ds(cut, mine.shape[2] - cut))

    def ring_copy(k, way, part):
        place = at_spot(spot + 1) if way == 0 else at_spot(spot - 1)
        return remote(
            mine.at[k, way, halves[part]], ring_land.at[k, way, halves[part]],
            ring_sems.at[0, k, way, part], ring_sems.at[1, k, way, part], {"dp": place},
        )

    def cross_copy(part):
        return remote(
            mine.at[dp_size - 1, 1 - own_x, halves[part]], cross_land.at[halves[part]],
            cross_sems.at[0, part], cross_sems.at[1, part], across,
        )

    def begin_pieces(k):
        for way in range(2):
            for i in range(3):
                met_copy(k, way, i).start()
                mine_copy(k, way, i).start()

    def ring_step(k, part):
        span = halves[part]
        if part == 0:

            @pl.when(k + 2 < dp_size)
            def _():
                begin_pieces(k + 2)

        @pl.when(k < dp_size)
        def _():
            for way in range(2):
                if part == 0:
                    for i in range(3):
                        mine_copy(k, way, i).wait()
                        met_copy(k, way, i).wait_recv()

                @pl.when(k == 0)
                def _():
                    base = mine[k, way, span].astype(F32) + met[k, way, span].astype(F32)
                    mine[k, way, span] = base.astype(BF16)

                @pl.when(k > 0)
                def _():
                    ring_copy(k - 1, way, part).wait_recv()
                    base = mine[k, way, span].astype(F32) + met[k, way, span].astype(F32)
                    base = base + ring_land[k - 1, way, span].astype(F32)
                    mine[k, way, span] = base.astype(BF16)

                @pl.when(k < dp_size - 1)
                def _():
                    ring_copy(k, way, part).start()

            @pl.when(k == dp_size - 1)
            def _():
                cross_copy(part).start()

        @pl.when(k == dp_size)
        def _():
            cross_copy(part).wait_recv()
            ring_out[span] = mine[dp_size - 1, own_x, span].astype(F32) + cross_land[span].astype(F32)

    def ring_turn(part, late=0):
        turn = s * heads + h + late
        count = seqs * heads + 2
        steps = dp_size + 1

        def body(k, carry):
            ring_step(k, part)
            return carry

        lax.fori_loop(turn * steps // count, (turn + 1) * steps // count, body, 0)

    parity, pair = me % 2, me // 2
    mate = me + 1 - 2 * parity

    def pair_copy(q):
        return remote(
            own_send.at[q, 1 - parity], pair_land.at[q], pair_sems.at[0, q], pair_sems.at[1, q],
            {"dp": mate},
        )

    def own_copy(q, k):
        to = lax.rem(pair + k, half)
        return remote(
            own_mid.at[q, to], own_land.at[q, k], own_sems.at[0, q, k], own_sems.at[1, q, k],
            {"dp": 2 * to + parity},
        )

    def begin_own(q):
        base = model // dp_size
        turned = weight_acc[pl.ds(pl.multiple_of(q * 3 * HD, 3 * HD), 3 * HD)].T
        fill = turned[model : model + own_send.shape[3] - base]
        for c in range(dp_size):
            own_send[q, c % 2, c // 2] = jnp.concatenate(
                [turned[c * base : (c + 1) * base], fill], axis=0
            ).astype(BF16)
        pair_copy(q).start()

    def relay_own(q):
        pair_copy(q).wait_recv()
        own_mid[q] = (own_send[q, parity].astype(F32) + pair_land[q].astype(F32)).astype(BF16)

        def start(k, carry):
            own_copy(q, k).start()
            return carry

        lax.fori_loop(1, half, start, 0)

    def part_copy(r):
        other = partner(own, r)
        return remote(
            part_send.at[other], part_land.at[r - 1], part_sems.at[0, r - 1],
            part_sems.at[1, r - 1], {"feat": other},
        )

    def seq_span(q):
        return pl.ds(pl.multiple_of(q * rows, rows), rows)

    def add_near(q):
        near_copy(q, 1).wait_recv()

        @pl.when(q > 0)
        def _():
            far_copy(q - 1).wait_send()

        far_send[...] = (far_keep[1] + near_land[q, 1].astype(F32)).astype(BF16)
        far_copy(q).start()
        near_copy(q, 0).wait_recv()
        attn_out[seq_span(q)] = far_keep[0] + near_land[q, 0].astype(F32)

    def finish(q):
        far_copy(q).wait_recv()
        span = seq_span(q)
        attn_out[span] = attn_out[span] + far_land[q].astype(F32)

    @pl.when((s == 0) & (h == 0))
    def _():
        barrier = pltpu.get_barrier_semaphore()
        for r in (1, 2, 3):
            pl.semaphore_signal(
                barrier, inc=1, device_id={"feat": partner(own, r)}, device_id_type=MESH
            )

        def greet(k, carry):
            pl.semaphore_signal(
                barrier, inc=1, device_id={"dp": lax.rem(me + k, dp_size)}, device_id_type=MESH
            )
            return carry

        lax.fori_loop(1, dp_size, greet, 0)
        pl.semaphore_wait(barrier, 3 + dp_size - 1)
        for q in range(grad_land.shape[0]):
            for r in (2, 3, 1):
                grad_copy(q, r).start()
        for k in range(2):
            begin_pieces(k)
        weight_acc[...] = jnp.zeros_like(weight_acc)

    @pl.when(h == 0)
    def _():
        span = pl.ds(pl.multiple_of(s * rows, rows), rows)
        grad_scr[:, 0:rows] = mixed_grad[own, span].astype(F32).T
        for r in (1, 2, 3):
            grad_copy(s, r).wait_recv()
            grad_scr[:, r * rows : (r + 1) * rows] = grad_land[s, r - 1].astype(F32).T

    query = proj[head_rows(h, 0, head_count)]
    key = proj[head_rows(h, 1, head_count)]
    value = proj[head_rows(h, 2, head_count)]
    draws = draws_ref[...]
    draws_ext = jnp.concatenate([draws, jnp.ones((16, FEAT), BF16)], axis=0)
    hot = hot_ref[...]
    away_wide = away_marks(hot)
    away = away_wide.astype(BF16)
    inverse = 1.0 / den_ref[0:1]
    head_grad = grad_scr[pl.ds(pl.multiple_of(h * HD, HD), HD)]
    grad_num = (head_grad * inverse).astype(BF16)
    grad_den = -jnp.sum(head_grad * mixed_ref[...], axis=0, keepdims=True) * inverse
    den_rows = jnp.broadcast_to(grad_den, (16, total)).astype(BF16)
    spread_grad = jnp.concatenate(spread(grad_num, hot) + [den_rows * hot], axis=0)
    spread_value = jnp.concatenate(spread(value, away) + [away], axis=0)

    phi_q = phi_q_ref[...]
    state_grad = mat_nt(spread_grad, phi_q).astype(BF16)
    scaled_q = mat_tn(state_ref[...], spread_grad) * phi_q.astype(F32)
    back_q = mat(draws_ext, scaled_q.astype(BF16))
    query_grad = back_q[0:HD] - query.astype(F32) * (back_q[HD : HD + 1] * root)

    phi_k = phi_k_ref[...]
    scaled_k = mat_tn(state_grad, spread_value) * phi_k.astype(F32)
    back_k = mat(draws_ext, scaled_k.astype(BF16))
    key_grad = back_k[0:HD] - key.astype(F32) * (back_k[HD : HD + 1] * root)
    value_grad = pick(mat(state_grad[0 : NBUCK * HD], phi_k), away_wide)

    ring_turn(0)
    one = (lax.broadcasted_iota(jnp.int32, hot.shape, 0) < 1).astype(F32).astype(BF16)
    num_scr[...] = jnp.concatenate([grad_num, den_rows], axis=0)
    value_scr[...] = jnp.concatenate([value, one], axis=0).astype(F32).T.astype(BF16)

    for c in range(total // CHUNK):
        cols = slice(c * CHUNK, (c + 1) * CHUNK)
        score = mat(value_scr[...], num_scr[:, cols]) * soft_ref[:, cols].astype(F32)
        score = score.astype(BF16)
        score_scr[:, cols] = score
        exact_scr[:, cols] = mat(proj[head_rows(h, 1, head_count)], score)
    query_grad = query_grad + exact_scr[...] * root
    joint = jnp.concatenate([query, grad_num], axis=0).astype(F32).T
    lane = lax.broadcasted_iota(jnp.int32, joint.shape, 1)
    left = jnp.where(lane < HD, joint, 0.0).astype(BF16)
    right = jnp.where(lane < HD, 0.0, joint).astype(BF16)
    exact_pair = (mat(score_scr[...], left) + mat(soft_ref[...], right)).T
    key_grad = key_grad + exact_pair[0:HD] * root
    value_grad = value_grad + exact_pair[HD:]
    wide_grad = jnp.concatenate([query_grad, key_grad, value_grad], axis=0)
    low_grad = wide_grad.astype(BF16)
    for kind in range(3):
        proj_scr[head_rows(h, kind, head_count)] = low_grad[kind * HD : (kind + 1) * HD]
    weight_grad = mat(low_grad[:, 0:rows], x_ref[0])
    for r in (1, 2, 3):
        weight_grad = weight_grad + mat(low_grad[:, r * rows : (r + 1) * rows], x_ref[r])
    span = pl.ds(pl.multiple_of(h * 3 * HD, 3 * HD), 3 * HD)
    weight_acc[span, 0:model] += weight_grad
    weight_acc[span, model:] += jnp.broadcast_to(
        jnp.sum(wide_grad, axis=1, keepdims=True), (3 * HD, 128)
    )

    @pl.when(s == seqs - 1)
    def _():
        begin_own(h)

        @pl.when(h > 0)
        def _():
            relay_own(h - 1)

    @pl.when((s > 0) & (h == 0))
    def _():
        add_near(s - 1)

    @pl.when(h == heads - 1)
    def _():
        @pl.when(s > 0)
        def _():
            for i in range(2):
                near_copy(s - 1, i).wait_send()

        for r in (3, 1, 2, 0):
            term = mat_tn(proj_scr[:, r * rows : (r + 1) * rows], weight[...])
            if r % 2:
                near_send[r // 2] = term.astype(BF16)
                near_copy(s, r // 2).start()
            else:
                far_keep[r // 2] = term

    ring_turn(1)

    @pl.when(last)
    def _():
        add_near(s)
        relay_own(h)
        for q in range(grad_land.shape[0] - 1):
            finish(q)
        ring_turn(0, 1)
        ring_turn(1, 1)

        sums = []
        for q in range(head_count):

            def arrive(k, carry):
                own_copy(q, k).wait_recv()
                return carry + own_land[q, k].astype(F32)

            sums.append(lax.fori_loop(1, half, arrive, own_mid[q, pair].astype(F32)))
        joined = jnp.concatenate(sums, axis=1)
        base = model // dp_size
        small = base // GROUP
        fill = jnp.broadcast_to(
            joined[base : base + 1], (part_send.shape[1] - small, joined.shape[1])
        )
        for a in range(GROUP):
            part_send[a] = jnp.concatenate(
                [joined[a * small : (a + 1) * small], fill], axis=0
            ).astype(BF16)
        for r in (2, 3, 1):
            part_copy(r).start()
        finish(s)
        ring_turn(0, 2)
        ring_turn(1, 2)
        proj_out[own] = part_send[own].astype(F32)
        for r in (1, 2, 3):
            part_copy(r).wait_recv()
            proj_out[partner(own, r)] = part_land[r - 1].astype(F32)

        for q in range(grad_land.shape[0]):
            for r in (1, 2, 3):
                grad_copy(q, r).wait_send()
        for i in range(2):
            near_copy(s, i).wait_send()
        far_copy(s).wait_send()
        for r in (1, 2, 3):
            part_copy(r).wait_send()
        for part in range(2):
            cross_copy(part).wait_send()

        def leave(k, carry):
            for way in range(2):
                for i in range(3):
                    met_copy(k, way, i).wait_send()
            return carry

        lax.fori_loop(0, dp_size, leave, 0)

        def leave_ring(k, carry):
            for way in range(2):
                for part in range(2):
                    ring_copy(k, way, part).wait_send()
            return carry

        lax.fori_loop(0, dp_size - 1, leave_ring, 0)
        for q in range(head_count):
            pair_copy(q).wait_send()

            def leave_own(k, carry):
                own_copy(q, k).wait_send()
                return carry

            lax.fori_loop(1, half, leave_own, 0)


def attend_back(
    dp_size, parts, mixed_grad, weight, draws, hot, proj, state, mixed, den, soft, phi_q, phi_k,
    down_grad, up_grad, tail,
):
    seqs, _, rows, model = parts.shape
    heads = draws.shape[0]
    width = heads * HD
    total = GROUP * rows
    n = dp_size
    ring_rows = down_grad.shape[1] + up_grad.shape[1] + tail.shape[1]
    own_rows = aligned(model // n + 1)
    part_rows = aligned(model // (n * GROUP) + 1)
    single = pl.Buffered(1)
    whole = lambda *shape: pl.BlockSpec(
        shape, lambda s, h: (0,) * len(shape), pipeline_mode=single
    )
    mode = single if n > 16 else None
    by_seq = lambda *shape: pl.BlockSpec(
        (None,) + shape, lambda s, h: (s,) + (0,) * len(shape), pipeline_mode=mode
    )
    by_head = lambda *shape: pl.BlockSpec(
        (None, None) + shape, lambda s, h: (s, h) + (0,) * len(shape), pipeline_mode=mode
    )
    anywhere = pl.BlockSpec(memory_space=pl.ANY)
    dma = pltpu.SemaphoreType.DMA
    return pl.pallas_call(
        lambda *refs: attend_back_kernel(dp_size, *refs),
        grid=(seqs, heads),
        out_shape=(
            jax.ShapeDtypeStruct((seqs * rows, model), F32),
            jax.ShapeDtypeStruct((ring_rows, model), F32),
            jax.ShapeDtypeStruct((GROUP, part_rows, 3 * width), F32),
        ),
        in_specs=[
            by_seq(GROUP, rows, model), whole(*mixed_grad.shape), whole(3 * width, model),
            pl.BlockSpec((None, HD, FEAT), lambda s, h: (h, 0, 0)),
            by_seq(16, total), by_seq(3 * width, total), by_head(STATES, FEAT), by_head(HD, total),
            by_head(8, total), by_head(total, total), by_head(FEAT, total), by_head(FEAT, total),
            anywhere, anywhere, anywhere,
        ],
        out_specs=(
            whole(seqs * rows, model), whole(ring_rows, model), whole(GROUP, part_rows, 3 * width),
        ),
        scratch_shapes=[
            pltpu.VMEM((width, total), F32),
            pltpu.VMEM((HD + 16, total), BF16),
            pltpu.VMEM((total, HD + 16), BF16),
            pltpu.VMEM((total, total), BF16),
            pltpu.VMEM((HD, total), F32),
            pltpu.VMEM((3 * width, total), BF16),
            pltpu.VMEM((seqs, 3, rows, width), BF16),
            pltpu.VMEM((2, rows, model), BF16),
            pltpu.VMEM((seqs, 2, rows, model), BF16),
            pltpu.VMEM((2, rows, model), F32),
            pltpu.VMEM((rows, model), BF16),
            pltpu.VMEM((seqs, rows, model), BF16),
            pltpu.VMEM((n, 2, ring_rows, model), BF16),
            pltpu.VMEM((n, 2, ring_rows, model), BF16),
            pltpu.VMEM((n - 1, 2, ring_rows, model), BF16),
            pltpu.VMEM((ring_rows, model), BF16),
            pltpu.VMEM((3 * width, model + 128), F32),
            pltpu.VMEM((heads, 2, n // 2, own_rows, 3 * HD), BF16),
            pltpu.VMEM((heads, n // 2, own_rows, 3 * HD), BF16),
            pltpu.VMEM((heads, n // 2, own_rows, 3 * HD), BF16),
            pltpu.VMEM((heads, n // 2, own_rows, 3 * HD), BF16),
            pltpu.VMEM((GROUP, part_rows, 3 * width), BF16),
            pltpu.VMEM((3, part_rows, 3 * width), BF16),
            dma((2, seqs, 3)),
            dma((2, seqs, 2)),
            dma((2, seqs)),
            dma((n, 2, 3)),
            dma((2, n, 2, 3)),
            dma((2, n - 1, 2, 2)),
            dma((2, 2)),
            dma((2, heads)),
            dma((2, heads, n // 2)),
            dma((2, 3)),
        ],
        compiler_params=pltpu.CompilerParams(
            vmem_limit_bytes=VMEM + (3 * 1024 * 1024 if n > 16 else 0), collective_id=2, has_side_effects=True
        ),
        cost_estimate=pl.CostEstimate(
            flops=48_000_000_000, bytes_accessed=40_000_000, transcendentals=0
        ),
        name="attend_back",
    )(
        parts, mixed_grad, weight, draws, hot, proj, state, mixed, den, soft, phi_q, phi_k,
        down_grad, up_grad, tail,
    )


def finish_kernel(
    starts, heads, attn_grad, resid_grad, hidden, sums, proj_sums, weight_rows, gain_ref, shift_ref,
    input_out, norm1_gain_out, norm1_bias_out, qkv_out, qkv_bias_out, out_out, out_bias_out,
    norm2_gain_out, norm2_bias_out, up_out, up_bias_out, down_out, down_bias_out,
):
    gain, shift = as_row(gain_ref), as_row(shift_ref)
    normed, scale = row_stats(hidden[...].astype(F32))
    input_out[...] = resid_grad[...] + norm_back(attn_grad[...] * gain, normed, scale)

    @pl.when(pl.program_id(0) == 0)
    def _():
        index = lax.axis_index("dp") * GROUP + lax.axis_index("feat")
        small, model = out_out.shape
        share = down_out.shape[0]
        ff = up_out.shape[1]

        def own(row, size):
            length = row.shape[1]
            wide = jnp.broadcast_to(row, (8, length))
            back = lax.rem(length - lax.rem(index * size, length), length)
            return pltpu.roll(wide, back, 1)[0:1, 0:size]

        down_out[...] = sums[0:share]
        first = starts[0]
        up_out[...] = jnp.concatenate(
            [sums[first + i * small : first + (i + 1) * small] for i in range(ff // model)], axis=1
        )
        first = starts[0] + starts[1]
        out_out[...] = sums[first : first + small]
        totals = first + small
        for i, out in enumerate((down_bias_out, out_bias_out, norm2_gain_out, norm2_bias_out)):
            out[...] = own(sums[totals + i : totals + i + 1], small).reshape(small)
        per_row = model // share
        level = index // per_row
        row = jnp.zeros((1, model), F32)
        for i in range(ff // model):
            row = jnp.where(level == i, sums[totals + 4 + i : totals + 5 + i], row)
        up_bias_out[...] = own(row, share).reshape(share)

        pieces = []
        for kind in range(3):
            for f in range(GROUP):
                for h in range(heads):
                    lanes = slice((h * 3 + kind) * HD, (h * 3 + kind + 1) * HD)
                    pieces.append(proj_sums[f, 0 : small + 1, lanes])
        grid = jnp.concatenate(pieces, axis=1)
        weight_sum, bias_sum = grid[0:small], grid[small : small + 1]
        qkv_out[...] = weight_sum
        qkv_bias_out[...] = own(bias_sum, 3 * small).reshape(3 * small)
        wide = weight_rows[...].astype(F32)

        def to_row(column):
            column = jnp.concatenate(
                [column, jnp.zeros((-small % 128, 1), F32)], axis=0
            )
            return jnp.broadcast_to(column, (column.shape[0], 128)).T[0:1, 0:small]

        bias_grad = to_row(jnp.sum(wide * bias_sum, axis=1, keepdims=True))
        gain_grad = to_row(jnp.sum(wide * weight_sum, axis=1, keepdims=True))
        norm1_bias_out[...] = bias_grad.reshape(small)
        gain_grad = (gain_grad - own(shift, small) * bias_grad) / own(gain, small)
        norm1_gain_out[...] = gain_grad.reshape(small)


def finish_all(
    attn_grad, resid_grad, hidden, sums, proj_sums, weight_rows, gain, shift, starts, devices, ff,
    heads,
):
    seqs, rows, model = hidden.shape
    small, share = model // devices, ff // devices
    whole = lambda *shape: pl.BlockSpec(shape, lambda s: (0,) * len(shape))
    by_seq = pl.BlockSpec((rows, model), lambda s: (s, 0))
    shapes = (
        (small,), (small,), (small, 3 * model), (3 * small,), (small, model), (small,), (small,),
        (small,), (small, ff), (share,), (share, model), (small,),
    )
    return pl.pallas_call(
        lambda *refs: finish_kernel(starts, heads, *refs),
        grid=(seqs,),
        out_shape=(jax.ShapeDtypeStruct((seqs * rows, model), F32),)
        + tuple(jax.ShapeDtypeStruct(shape, F32) for shape in shapes),
        in_specs=[
            by_seq, by_seq, pl.BlockSpec((None, rows, model), lambda s: (s, 0, 0)),
            whole(*sums.shape), whole(*proj_sums.shape), whole(*weight_rows.shape), whole(model),
            whole(model),
        ],
        out_specs=(by_seq,) + tuple(whole(*shape) for shape in shapes),
        compiler_params=pltpu.CompilerParams(vmem_limit_bytes=VMEM),
        name="finish_all",
    )(attn_grad, resid_grad, hidden, sums, proj_sums, weight_rows, gain, shift)


def per_device(
    hidden_in, norm1_gain, norm1_bias, qkv_weight, qkv_bias, feature_draws, out_weight, out_bias,
    norm2_gain, norm2_bias, up_weight, up_bias, down_weight, down_bias, block_bucket, out_grad,
):
    seqs, rows, model = hidden_in.shape
    ff = up_weight.shape[1]
    dp_size = lax.axis_size("dp")
    devices = dp_size * GROUP
    small = model // devices
    heads = feature_draws.shape[0] // GROUP
    flat = (seqs * rows, model)

    (
        parts, mixed_parts, proj, state, mixed, den, hot, own_weight, own_draws, soft, phi_q, phi_k,
    ) = attend(
        block_bucket, hidden_in, norm1_gain, norm1_bias, qkv_bias, qkv_weight, feature_draws
    )
    layer_out, resid_grad, mixed_grad, down_grad, up_grad, tail = block_layer(
        mixed_parts, hidden_in.reshape(flat), out_grad.reshape(flat), out_weight, out_bias,
        norm2_gain, norm2_bias, down_bias, up_bias, up_weight, down_weight, devices,
    )
    attn_grad, sums, proj_sums = attend_back(
        dp_size, parts, mixed_grad, own_weight, own_draws, hot, proj, state, mixed, den, soft,
        phi_q, phi_k, down_grad, up_grad, tail,
    )
    index = lax.axis_index("dp") * GROUP + lax.axis_index("feat")
    weight_rows = lax.dynamic_slice_in_dim(qkv_weight, index * small, small, 0)
    (
        input_grad, norm1_gain_sum, norm1_bias_sum, qkv_weight_sum, qkv_bias_sum, out_weight_sum,
        out_bias_sum, norm2_gain_sum, norm2_bias_sum, up_sum, up_bias_sum, down_sum, down_bias_sum,
    ) = finish_all(
        attn_grad, resid_grad, hidden_in, sums, proj_sums, weight_rows, norm1_gain, norm1_bias,
        (down_grad.shape[1], up_grad.shape[1]), devices, ff, heads,
    )
    return (
        layer_out.reshape(hidden_in.shape), input_grad.reshape(hidden_in.shape), norm1_gain_sum,
        norm1_bias_sum, qkv_weight_sum, qkv_bias_sum, out_weight_sum, out_bias_sum, norm2_gain_sum,
        norm2_bias_sum, up_sum, up_bias_sum, down_sum, down_bias_sum,
    )


def solution(mesh):
    both = ("dp", "feat")
    rows = P("dp", "feat", None)
    in_specs = (
        rows, P(), P(), P(), P(), P(None, None, "feat"), P(), P(), P(), P(), P(), P(), P(), P(),
        P("dp", None, None), rows,
    )
    out_specs = (
        rows, rows, P(both), P(both), P(both, None), P(both), P(both, None), P(both), P(both),
        P(both), P(both, None), P(both), P(both, None), P(both),
    )
    return jax.shard_map(
        per_device, mesh=mesh, in_specs=in_specs, out_specs=out_specs, check_vma=False
    )
```

```python
import math

import jax
import jax.numpy as jnp
from jax import lax
from jax.experimental import pallas as pl
from jax.experimental.pallas import tpu as pltpu
from jax.sharding import PartitionSpec as P

HD = 64
FEAT = 256
BLOCK = 64
NBUCK = 4
GROUP = 4
CHUNK = 256
STATES = NBUCK * HD + 16
FAR = 16384.0
VMEM = 60 * 1024 * 1024

F32 = jnp.float32
BF16 = jnp.bfloat16
MESH = pl.DeviceIdType.MESH


def mat(left, right):
    return jnp.dot(left, right, preferred_element_type=F32)


def mat_nt(left, right):
    return lax.dot_general(left, right, (((1,), (1,)), ((), ())), preferred_element_type=F32)


def mat_tn(left, right):
    return lax.dot_general(left, right, (((0,), (0,)), ((), ())), preferred_element_type=F32)


def row_stats(values):
    row_mean = jnp.mean(values, axis=-1, keepdims=True)
    centered = values - row_mean
    scale = lax.rsqrt(jnp.mean(centered * centered, axis=-1, keepdims=True) + 1e-05)
    return (centered * scale, scale)


def norm_back(cotangent, normed, scale):
    mean_one = jnp.mean(cotangent, axis=-1, keepdims=True)
    mean_two = jnp.mean(cotangent * normed, axis=-1, keepdims=True)
    return scale * (cotangent - mean_one - normed * mean_two)


def features(vectors, draws):
    wide = vectors.astype(F32)
    square = jnp.sum(wide * wide, axis=0, keepdims=True) * (0.5 / math.sqrt(HD))
    return jnp.exp(mat_tn(draws, vectors) - (square + 0.5 * math.log(FEAT)))


def spread(rows, marks):
    return [rows * marks[u : u + 1] for u in range(NBUCK)]


def pick(stacked, marks):
    total = stacked[0:HD] * marks[0:1]
    for u in range(1, NBUCK):
        total = total + stacked[u * HD : (u + 1) * HD] * marks[u : u + 1]
    return total


def away_marks(hot):
    live = (lax.broadcasted_iota(jnp.int32, hot.shape, 0) < NBUCK).astype(F32)
    return live - hot.astype(F32)


def partner(own, r):
    x, core = own // 2, own % 2
    if r & 2:
        x = 1 - x
    if r & 1:
        core = 1 - core
    return 2 * x + core


def as_row(ref):
    return ref[...].reshape(1, ref.shape[0])


def aligned(count):
    return -(-count // 16) * 16


def remote(src, dst, send, recv, place):
    return pltpu.make_async_remote_copy(
        src_ref=src, dst_ref=dst, send_sem=send, recv_sem=recv, device_id=place, device_id_type=MESH
    )


def head_rows(h, kind, heads):
    return pl.ds(pl.multiple_of((kind * heads + h) * HD, HD), HD)


def attend_kernel(
    bucket, hidden, gain_ref, shift_ref, bias_ref, weight_any, draws_in,
    parts_any, mix_any, proj_out, state_out, mixed_out, den_out, hot_out, weight_out, draws_out,
    soft_out, phi_q_out, phi_k_out,
    parts, mix_land, mix_send, raw, bias_row, bias_scr, draws_land,
    query_scr, key_scr, value_scr, low_scr, gather_scr,
    raw_sem, part_send, part_recv, draw_send, draw_recv, mix_send_sem, mix_recv_sem, out_sem,
):
    s, h = pl.program_id(0), pl.program_id(1)
    seqs, rows, model = hidden.shape
    heads = draws_out.shape[0]
    total = GROUP * rows
    width = heads * HD
    own = lax.axis_index("feat")
    near, across = {"feat": partner(own, 1)}, {"feat": partner(own, 2)}

    def part_copy(q, kind):
        src, dst, place = ((0, 1, near), (0, 2, across), (2, 3, near))[kind]
        return remote(
            parts.at[q, src], parts.at[q, dst], part_send.at[q, kind], part_recv.at[q, kind], place
        )

    def draw_copy(r):
        other = partner(own, r)
        return remote(
            draws_in.at[pl.ds(other * heads, heads)], draws_land.at[r - 1],
            draw_send.at[r - 1], draw_recv.at[r - 1], {"feat": other},
        )

    def mix_copy(q, r):
        return remote(
            mix_send.at[q, r], mix_land.at[q, r], mix_send_sem.at[q, r - 1],
            mix_recv_sem.at[q, r - 1], {"feat": partner(own, r)},
        )

    def raw_copy(j):
        cols = pl.ds(pl.multiple_of(j * model + (own // 2) * 2 * width, 2 * width), 2 * width)
        return pltpu.make_async_copy(weight_any.at[:, cols], raw.at[j], raw_sem.at[j])

    def out_copy(q):
        return pltpu.make_async_copy(parts.at[q], parts_any.at[q], out_sem.at[q])

    @pl.when((s == 0) & (h == 0))
    def _():
        for j in range(3):
            raw_copy(j).start()
        barrier = pltpu.get_barrier_semaphore()
        for r in (1, 2, 3):
            pl.semaphore_signal(
                barrier, inc=1, device_id={"feat": partner(own, r)}, device_id_type=MESH
            )
        gain, shift = as_row(gain_ref), as_row(shift_ref)
        first = row_stats(hidden[0].astype(F32))[0] * gain + shift
        parts[0, 0] = first.astype(BF16)
        pl.semaphore_wait(barrier, 3)
        part_copy(0, 1).start()
        part_copy(0, 0).start()
        for r in (1, 2, 3):
            draw_copy(r).start()
        for q in range(1, seqs):
            normed = row_stats(hidden[q].astype(F32))[0] * gain + shift
            parts[q, 0] = normed.astype(BF16)
            part_copy(q, 1).start()
            part_copy(q, 0).start()
        core = own % 2
        bias_row[...] = as_row(bias_ref)
        for j in range(3):
            raw_copy(j).wait()
            piece = raw[j].astype(F32)
            piece = jnp.where(core == 0, piece[:, 0:width], piece[:, width:])
            weight_out[j * width : (j + 1) * width] = piece.T.astype(BF16)
            cols = pl.ds(pl.multiple_of(j * model + (own // 2) * 2 * width, 2 * width), 2 * width)
            pair = jnp.broadcast_to(bias_row[:, cols], (128, 2 * width))
            pair = jnp.where(core == 0, pair[:, 0:width], pair[:, width:])
            bias_scr[j * width : (j + 1) * width] = pair.T
        part_copy(0, 1).wait_recv()
        part_copy(0, 2).start()
        for r in (1, 2, 3):
            draw_copy(r).wait_recv()
        mine = draws_in[pl.ds(own * heads, heads)]
        draws_out[...] = jnp.concatenate(
            [mine] + [draws_land[r - 1] for r in (1, 2, 3)], axis=2
        )

    @pl.when(h == 0)
    def _():
        per = rows // BLOCK
        lanes = lax.broadcasted_iota(jnp.int32, (16, total), 1) // BLOCK
        level = lax.broadcasted_iota(jnp.int32, (16, total), 0)
        ids = jnp.full((16, total), -1, jnp.int32)
        for r in range(GROUP):
            for i in range(per):
                ids = jnp.where(
                    lanes == r * per + i, bucket[s, partner(own, r) * per + i, 0], ids
                )
        hot_out[...] = (ids == level).astype(F32).astype(BF16)

        def project(r):
            cols = slice(r * rows, (r + 1) * rows)
            piece = mat_nt(weight_out[...], parts[s, r]) + bias_scr[:, 0:1]
            proj_out[:, cols] = piece.astype(BF16)

        project(0)
        part_copy(s, 0).wait_recv()
        project(1)
        project(2)
        part_copy(s, 2).wait_recv()
        project(3)
        out_copy(s).start()

    query = proj_out[head_rows(h, 0, heads)]
    key = proj_out[head_rows(h, 1, heads)]
    value = proj_out[head_rows(h, 2, heads)]
    draws = draws_out[h]
    hot = hot_out[...]
    hot_wide = hot.astype(F32)
    away = away_marks(hot).astype(BF16)
    phi_q = features(query, draws).astype(BF16)
    phi_k = features(key, draws).astype(BF16)
    phi_q_out[...] = phi_q
    phi_k_out[...] = phi_k
    spread_value = jnp.concatenate(spread(value, away) + [away], axis=0)
    state = mat_nt(spread_value, phi_k).astype(BF16)
    state_out[...] = state
    low = mat(state, phi_q)
    low_scr[0:HD] = pick(low, hot_wide)
    low_den = jnp.sum(low[NBUCK * HD :] * hot_wide, axis=0, keepdims=True)
    low_scr[HD : HD + 8] = jnp.broadcast_to(low_den, (8, total))
    query_scr[...] = jnp.concatenate([query * (1.0 / math.sqrt(HD)), hot], axis=0).astype(BF16)
    key_scr[...] = jnp.concatenate([key, away * -FAR], axis=0).astype(F32).T.astype(BF16)
    value_scr[0:HD] = value
    value_scr[HD:] = jnp.ones((16, total), BF16)

    for c in range(total // CHUNK):
        cols = slice(c * CHUNK, (c + 1) * CHUNK)
        weights = jnp.exp(mat(key_scr[...], query_scr[:, cols])).astype(BF16)
        soft_out[:, cols] = weights
        exact = mat(value_scr[...], weights)
        den = low_scr[HD : HD + 8, cols] + exact[HD : HD + 8]
        mixed = (low_scr[0:HD, cols] + exact[0:HD]) / den[0:1]
        mixed_out[:, cols] = mixed
        den_out[:, cols] = den
        gather_scr[pl.ds(pl.multiple_of(h * HD, HD), HD), cols] = mixed

    @pl.when((h == heads - 2) & (s < seqs - 1))
    def _():
        part_copy(s + 1, 1).wait_recv()
        part_copy(s + 1, 2).start()

    @pl.when(h == heads - 1)
    def _():
        for r in range(GROUP):
            piece = gather_scr[:, r * rows : (r + 1) * rows].T.astype(BF16)
            if r == 0:
                mix_land[s, 0] = piece
            else:
                mix_send[s, r] = piece
                mix_copy(s, r).start()

    @pl.when((s == seqs - 1) & (h == heads - 1))
    def _():
        for q in range(seqs):
            for r in (1, 2, 3):
                mix_copy(q, r).wait_recv()
        done = pltpu.make_async_copy(mix_land, mix_any, out_sem.at[seqs])
        done.start()
        for q in range(seqs):
            for kind in range(3):
                part_copy(q, kind).wait_send()
            for r in (1, 2, 3):
                mix_copy(q, r).wait_send()
            out_copy(q).wait()
        for r in (1, 2, 3):
            draw_copy(r).wait_send()
        done.wait()


def attend(bucket, hidden, gain, shift, bias, weight, draws):
    seqs, rows, model = hidden.shape
    heads = draws.shape[0] // GROUP
    width = heads * HD
    total = GROUP * rows
    whole = lambda *shape: pl.BlockSpec(shape, lambda s, h: (0,) * len(shape))
    by_seq = lambda *shape: pl.BlockSpec((None,) + shape, lambda s, h: (s,) + (0,) * len(shape))
    by_head = lambda *shape: pl.BlockSpec(
        (None, None) + shape, lambda s, h: (s, h) + (0,) * len(shape)
    )
    anywhere = pl.BlockSpec(memory_space=pl.ANY)
    return pl.pallas_call(
        attend_kernel,
        grid=(seqs, heads),
        out_shape=(
            jax.ShapeDtypeStruct((seqs, GROUP, rows, model), BF16),
            jax.ShapeDtypeStruct((seqs, GROUP, rows, width), BF16),
            jax.ShapeDtypeStruct((seqs, 3 * width, total), BF16),
            jax.ShapeDtypeStruct((seqs, heads, STATES, FEAT), BF16),
            jax.ShapeDtypeStruct((seqs, heads, HD, total), F32),
            jax.ShapeDtypeStruct((seqs, heads, 8, total), F32),
            jax.ShapeDtypeStruct((seqs, 16, total), BF16),
            jax.ShapeDtypeStruct((3 * width, model), BF16),
            jax.ShapeDtypeStruct((heads, HD, FEAT), BF16),
            jax.ShapeDtypeStruct((seqs, heads, total, total), BF16),
            jax.ShapeDtypeStruct((seqs, heads, FEAT, total), BF16),
            jax.ShapeDtypeStruct((seqs, heads, FEAT, total), BF16),
        ),
        in_specs=[
            pl.BlockSpec(memory_space=pltpu.SMEM),
            whole(seqs, rows, model), whole(model), whole(model), whole(3 * model), anywhere,
            whole(*draws.shape),
        ],
        out_specs=(
            anywhere, anywhere, by_seq(3 * width, total), by_head(STATES, FEAT), by_head(HD, total),
            by_head(8, total), by_seq(16, total), whole(3 * width, model), whole(heads, HD, FEAT),
            by_head(total, total), by_head(FEAT, total), by_head(FEAT, total),
        ),
        scratch_shapes=[
            pltpu.VMEM((seqs, GROUP, rows, model), BF16),
            pltpu.VMEM((seqs, GROUP, rows, width), BF16),
            pltpu.VMEM((seqs, GROUP, rows, width), BF16),
            pltpu.VMEM((3, model, 2 * width), BF16),
            pltpu.VMEM((1, 3 * model), F32),
            pltpu.VMEM((3 * width, 128), F32),
            pltpu.VMEM((3, heads, HD, draws.shape[2]), BF16),
            pltpu.VMEM((HD + 16, total), BF16),
            pltpu.VMEM((total, HD + 16), BF16),
            pltpu.VMEM((HD + 16, total), BF16),
            pltpu.VMEM((HD + 8, total), F32),
            pltpu.VMEM((width, total), F32),
            pltpu.SemaphoreType.DMA((3,)),
            pltpu.SemaphoreType.DMA((seqs, 3)),
            pltpu.SemaphoreType.DMA((seqs, 3)),
            pltpu.SemaphoreType.DMA((3,)),
            pltpu.SemaphoreType.DMA((3,)),
            pltpu.SemaphoreType.DMA((seqs, 3)),
            pltpu.SemaphoreType.DMA((seqs, 3)),
            pltpu.SemaphoreType.DMA((seqs + 1,)),
        ],
        compiler_params=pltpu.CompilerParams(
            vmem_limit_bytes=VMEM, collective_id=1, has_side_effects=True
        ),
        cost_estimate=pl.CostEstimate(
            flops=24_000_000_000, bytes_accessed=20_000_000, transcendentals=0
        ),
        name="attend",
    )(bucket, hidden, gain, shift, bias, weight, draws)


def block_kernel(
    direct, parts_ref, hidden, grad, out_w, out_b, gain_ref, shift_ref, down_b, up_b, up, down,
    layer_out, resid_out, mixed_grad, down_out, up_out, tail_out,
    mixed, resid_scr, in_scr, in_t, acc_out, acc_in, act_scr, pre_scr, vec_scr, bias_row,
):
    step = pl.program_id(0)
    model = hidden.shape[1]
    count = hidden.shape[0] // CHUNK
    spans = [slice(c * CHUNK, (c + 1) * CHUNK) for c in range(count)]
    subs = [slice(u * model, (u + 1) * model) for u in range(up.shape[1] // model)]
    owners = tail_out.shape[0]
    small = model // owners

    @pl.when(step == 0)
    def _():
        own = lax.axis_index("feat")
        for c, span in enumerate(spans):
            pieces = [parts_ref[c, r] for r in range(GROUP)]
            pieces = [jnp.where(own % 2 == 1, pieces[r ^ 1], pieces[r]) for r in range(GROUP)]
            pieces = [jnp.where(own // 2 == 1, pieces[r ^ 2], pieces[r]) for r in range(GROUP)]
            mixed[span] = jnp.concatenate(pieces, axis=1)
            resid = hidden[span].astype(F32) + mat(mixed[span], out_w[...]) + as_row(out_b)
            resid_scr[span] = resid
            normed, _ = row_stats(resid)
            inner = normed * as_row(gain_ref) + as_row(shift_ref)
            in_scr[span] = inner.astype(BF16)
            in_t[:, span] = inner.T.astype(BF16)
        acc_out[...] = jnp.zeros_like(acc_out)
        acc_in[...] = jnp.zeros_like(acc_in)
        bias_row[...] = as_row(up_b)

    slope = math.sqrt(2.0 / math.pi)
    up_terms = []
    for u, sub in enumerate(subs):
        total = jnp.zeros((1, model), F32)
        place = (step * len(subs) + u) * model
        up_bias = bias_row[:, pl.ds(pl.multiple_of(place, model), model)]
        for span in spans:
            pre = mat(in_scr[span], up[:, sub]) + up_bias
            square = pre * pre
            tanh = jnp.tanh(pre * (slope + (slope * 0.044715) * square))
            half = 0.5 * (1.0 + tanh)
            act = (pre * half).astype(BF16)
            bend = half + (0.5 * pre) * (1.0 - tanh * tanh) * (
                slope + (3.0 * slope * 0.044715) * square
            )
            pre_grad = mat_nt(grad[span], down[sub]) * bend
            total = total + jnp.sum(pre_grad, axis=0, keepdims=True)
            pre_low = pre_grad.astype(BF16)
            act_scr[span] = act
            pre_scr[span] = pre_low
            acc_out[span] += mat(act, down[sub])
            acc_in[span] += mat_nt(pre_low, up[:, sub])
        vec_scr[pl.ds(4 + step * len(subs) + u, 1)] = total
        down_term = mat_tn(act_scr[...], grad[...])
        up_term = mat(in_t[...], pre_scr[...])
        if direct:
            share = down_out.shape[1]
            for i in range(model // share):
                down_out[u * (model // share) + i] = down_term[
                    i * share : (i + 1) * share
                ].astype(BF16)
            up_terms.append(up_term)
        else:
            down_out[sub] = down_term.astype(BF16)
            up_out[:, sub] = up_term.astype(BF16)
    if direct:
        for i in range(owners):
            own_rows = slice(i * small, (i + 1) * small)
            up_out[i] = jnp.concatenate([term[own_rows] for term in up_terms], axis=0).astype(BF16)

    @pl.when(step == pl.num_programs(0) - 1)
    def _():
        sums = [jnp.zeros((1, model), F32) for _ in range(4)]
        for span in spans:
            resid = resid_scr[span]
            layer_out[span] = (resid + acc_out[span] + as_row(down_b)).astype(BF16)
            normed, scale = row_stats(resid)
            inner_grad = acc_in[span]
            wide = grad[span].astype(F32)
            resid_grad = wide + norm_back(inner_grad * as_row(gain_ref), normed, scale)
            resid_out[span] = resid_grad
            low = resid_grad.astype(BF16)
            in_scr[span] = low
            for i, term in enumerate((wide, resid_grad, inner_grad * normed, inner_grad)):
                sums[i] = sums[i] + jnp.sum(term, axis=0, keepdims=True)
            back = mat_nt(low, out_w[...]).astype(BF16)
            part = model // GROUP
            for a in range(GROUP):
                mixed_grad[a, span] = back[:, a * part : (a + 1) * part]
        for i in range(4):
            vec_scr[i : i + 1] = sums[i]
        out_term = mat_tn(mixed[...], in_scr[...])
        fill = tail_out.shape[1] - small - 8
        extra = [jnp.zeros((fill, model), F32)] if fill else []
        for i in range(owners):
            tail_out[i] = jnp.concatenate(
                [out_term[i * small : (i + 1) * small], vec_scr[...]] + extra, axis=0
            ).astype(BF16)


def block_layer(parts, hidden, grad, out_w, out_b, gain, shift, down_b, up_b, up, down, devices):
    tokens, model = hidden.shape
    ff = up.shape[1]
    steps = 2
    tile = ff // steps
    small, share = model // devices, ff // devices
    direct = small % 8 == 0 and share % 16 == 0
    tail_rows = aligned(small + 8)
    single = pl.Buffered(1)
    whole = lambda *shape: pl.BlockSpec(
        shape, lambda t: (0,) * len(shape), pipeline_mode=single
    )
    part = model // GROUP
    if direct:
        grad_shapes = (
            jax.ShapeDtypeStruct((devices, share, model), BF16),
            jax.ShapeDtypeStruct((devices, ff // model * small, model), BF16),
        )
        grad_specs = (
            pl.BlockSpec((devices // steps, share, model), lambda t: (t, 0, 0)),
            pl.BlockSpec((devices, tile // model * small, model), lambda t: (0, t, 0)),
        )
    else:
        grad_shapes = (
            jax.ShapeDtypeStruct((ff, model), BF16),
            jax.ShapeDtypeStruct((model, ff), BF16),
        )
        grad_specs = (
            pl.BlockSpec((tile, model), lambda t: (t, 0)),
            pl.BlockSpec((model, tile), lambda t: (0, t)),
        )
    layer_out, resid_grad, mixed_grad, down_grad, up_grad, tail = pl.pallas_call(
        lambda *refs: block_kernel(direct, *refs),
        grid=(steps,),
        out_shape=(
            jax.ShapeDtypeStruct((tokens, model), BF16),
            jax.ShapeDtypeStruct((tokens, model), F32),
            jax.ShapeDtypeStruct((GROUP, tokens, part), BF16),
        )
        + grad_shapes
        + (jax.ShapeDtypeStruct((devices, tail_rows, model), BF16),),
        in_specs=[
            whole(*parts.shape), whole(tokens, model), whole(tokens, model), whole(model, model),
            whole(model), whole(model), whole(model), whole(model), whole(ff),
            pl.BlockSpec((model, tile), lambda t: (0, t)),
            pl.BlockSpec((tile, model), lambda t: (t, 0)),
        ],
        out_specs=(whole(tokens, model), whole(tokens, model), whole(GROUP, tokens, part))
        + grad_specs
        + (whole(devices, tail_rows, model),),
        scratch_shapes=[
            pltpu.VMEM((tokens, model), BF16),
            pltpu.VMEM((tokens, model), F32),
            pltpu.VMEM((tokens, model), BF16),
            pltpu.VMEM((model, tokens), BF16),
            pltpu.VMEM((tokens, model), F32),
            pltpu.VMEM((tokens, model), F32),
            pltpu.VMEM((tokens, model), BF16),
            pltpu.VMEM((tokens, model), BF16),
            pltpu.VMEM((8, model), F32),
            pltpu.VMEM((1, ff), F32),
        ],
        compiler_params=pltpu.CompilerParams(vmem_limit_bytes=VMEM),
        cost_estimate=pl.CostEstimate(
            flops=26_000_000_000, bytes_accessed=30_000_000, transcendentals=0
        ),
        name="block_layer",
    )(parts, hidden, grad, out_w, out_b, gain, shift, down_b, up_b, up, down)
    if not direct:
        fit = lambda a: jnp.pad(a, ((0, 0), (0, aligned(a.shape[1]) - a.shape[1]), (0, 0)))
        down_grad = fit(down_grad.reshape(devices, share, model))
        up_grad = up_grad.reshape(devices, small, ff // model, model).transpose(0, 2, 1, 3)
        up_grad = fit(up_grad.reshape(devices, ff // model * small, model))
    return layer_out, resid_grad, mixed_grad, down_grad, up_grad, tail


def attend_back_kernel(
    dp_size, x_ref, mixed_grad, weight, draws_ref, hot_ref, proj, state_ref, mixed_ref, den_ref,
    soft_ref, phi_q_ref, phi_k_ref, down_any, up_any, tail_any,
    attn_out, ring_out, proj_out,
    grad_scr, num_scr, value_scr, score_scr, exact_scr, proj_scr,
    grad_land, near_send, near_land, far_keep, far_send, far_land,
    mine, met, ring_land, cross_land,
    weight_acc, own_send, pair_land, own_mid, own_land, part_send, part_land,
    grad_sems, near_sems, far_sems, mine_sem, met_sems, ring_sems, cross_sems, pair_sems, own_sems,
    part_sems,
):
    s, h = pl.program_id(0), pl.program_id(1)
    seqs, heads = pl.num_programs(0), pl.num_programs(1)
    rows, model = x_ref.shape[1], x_ref.shape[2]
    head_count = proj_scr.shape[0] // (3 * HD)
    width = head_count * HD
    total = GROUP * rows
    root = 1.0 / math.sqrt(HD)
    own, me = lax.axis_index("feat"), lax.axis_index("dp")
    own_x, own_core = own // 2, own % 2
    near, across = {"feat": partner(own, 1)}, {"feat": partner(own, 2)}
    last = (s == seqs - 1) & (h == heads - 1)

    def grad_copy(q, r):
        other = partner(own, r)
        return remote(
            mixed_grad.at[other, pl.ds(q * rows, rows)], grad_land.at[q, r - 1],
            grad_sems.at[0, q, r - 1], grad_sems.at[1, q, r - 1], {"feat": other},
        )

    def near_copy(q, i):
        return remote(
            near_send.at[i], near_land.at[q, i], near_sems.at[0, q, i], near_sems.at[1, q, i], near
        )

    def far_copy(q):
        return remote(far_send, far_land.at[q], far_sems.at[0, q], far_sems.at[1, q], across)

    odd = me % 2
    half = dp_size // 2
    spot = (1 - odd) * (me // 2) + odd * (dp_size - 1 - me // 2)

    def at_spot(p):
        p = lax.rem(p + dp_size, dp_size)
        upper = p // half
        return (1 - upper) * (2 * p) + upper * (2 * (dp_size - 1 - p) + 1)

    def chunk(k, way):
        return at_spot(spot - 1 - k) if way == 0 else at_spot(lax.rem(spot + 1 + k, dp_size))

    sources = (down_any, up_any, tail_any)
    lengths = [ref.shape[1] for ref in sources]
    starts = [sum(lengths[:i]) for i in range(3)]

    def owner(k, way, core):
        return chunk(k, way) * GROUP + 2 * way + core

    def mine_copy(k, way, i):
        return pltpu.make_async_copy(
            sources[i].at[owner(k, way, own_core)],
            mine.at[k, way, pl.ds(starts[i], lengths[i])],
            mine_sem.at[k, way, i],
        )

    def met_copy(k, way, i):
        return remote(
            sources[i].at[owner(k, way, 1 - own_core)],
            met.at[k, way, pl.ds(starts[i], lengths[i])],
            met_sems.at[0, k, way, i], met_sems.at[1, k, way, i], near,
        )

    cut = aligned(mine.shape[2] // 2)
    halves = (pl.ds(0, cut), pl.ds(cut, mine.shape[2] - cut))

    def ring_copy(k, way, part):
        place = at_spot(spot + 1) if way == 0 else at_spot(spot - 1)
        return remote(
            mine.at[k, way, halves[part]], ring_land.at[k, way, halves[part]],
            ring_sems.at[0, k, way, part], ring_sems.at[1, k, way, part], {"dp": place},
        )

    def cross_copy(part):
        return remote(
            mine.at[dp_size - 1, 1 - own_x, halves[part]], cross_land.at[halves[part]],
            cross_sems.at[0, part], cross_sems.at[1, part], across,
        )

    def begin_pieces(k):
        for way in range(2):
            for i in range(3):
                met_copy(k, way, i).start()
                mine_copy(k, way, i).start()

    def ring_step(k, part):
        span = halves[part]
        if part == 0:

            @pl.when(k + 2 < dp_size)
            def _():
                begin_pieces(k + 2)

        @pl.when(k < dp_size)
        def _():
            for way in range(2):
                if part == 0:
                    for i in range(3):
                        mine_copy(k, way, i).wait()
                        met_copy(k, way, i).wait_recv()

                @pl.when(k == 0)
                def _():
                    base = mine[k, way, span].astype(F32) + met[k, way, span].astype(F32)
                    mine[k, way, span] = base.astype(BF16)

                @pl.when(k > 0)
                def _():
                    ring_copy(k - 1, way, part).wait_recv()
                    base = mine[k, way, span].astype(F32) + met[k, way, span].astype(F32)
                    base = base + ring_land[k - 1, way, span].astype(F32)
                    mine[k, way, span] = base.astype(BF16)

                @pl.when(k < dp_size - 1)
                def _():
                    ring_copy(k, way, part).start()

            @pl.when(k == dp_size - 1)
            def _():
                cross_copy(part).start()

        @pl.when(k == dp_size)
        def _():
            cross_copy(part).wait_recv()
            ring_out[span] = mine[dp_size - 1, own_x, span].astype(F32) + cross_land[span].astype(F32)

    def ring_turn(part):
        turn = s * heads + h
        count = seqs * heads
        steps = dp_size + 1

        def body(k, carry):
            ring_step(k, part)
            return carry

        lax.fori_loop(turn * steps // count, (turn + 1) * steps // count, body, 0)

    parity, pair = me % 2, me // 2
    mate = me + 1 - 2 * parity

    def pair_copy(q):
        return remote(
            own_send.at[q, 1 - parity], pair_land.at[q], pair_sems.at[0, q], pair_sems.at[1, q],
            {"dp": mate},
        )

    def own_copy(q, k):
        to = lax.rem(pair + k, half)
        return remote(
            own_mid.at[q, to], own_land.at[q, k], own_sems.at[0, q, k], own_sems.at[1, q, k],
            {"dp": 2 * to + parity},
        )

    def begin_own(q):
        base = model // dp_size
        turned = weight_acc[pl.ds(pl.multiple_of(q * 3 * HD, 3 * HD), 3 * HD)].T
        fill = turned[model : model + own_send.shape[3] - base]
        for c in range(dp_size):
            own_send[q, c % 2, c // 2] = jnp.concatenate(
                [turned[c * base : (c + 1) * base], fill], axis=0
            ).astype(BF16)
        pair_copy(q).start()

    def relay_own(q):
        pair_copy(q).wait_recv()
        own_mid[q] = (own_send[q, parity].astype(F32) + pair_land[q].astype(F32)).astype(BF16)

        def start(k, carry):
            own_copy(q, k).start()
            return carry

        lax.fori_loop(1, half, start, 0)

    def part_copy(r):
        other = partner(own, r)
        return remote(
            part_send.at[other], part_land.at[r - 1], part_sems.at[0, r - 1],
            part_sems.at[1, r - 1], {"feat": other},
        )

    def seq_span(q):
        return pl.ds(pl.multiple_of(q * rows, rows), rows)

    def add_near(q):
        near_copy(q, 1).wait_recv()

        @pl.when(q > 0)
        def _():
            far_copy(q - 1).wait_send()

        far_send[...] = (far_keep[1] + near_land[q, 1].astype(F32)).astype(BF16)
        far_copy(q).start()
        near_copy(q, 0).wait_recv()
        attn_out[seq_span(q)] = far_keep[0] + near_land[q, 0].astype(F32)

    def finish(q):
        far_copy(q).wait_recv()
        span = seq_span(q)
        attn_out[span] = attn_out[span] + far_land[q].astype(F32)

    @pl.when((s == 0) & (h == 0))
    def _():
        barrier = pltpu.get_barrier_semaphore()
        for r in (1, 2, 3):
            pl.semaphore_signal(
                barrier, inc=1, device_id={"feat": partner(own, r)}, device_id_type=MESH
            )

        def greet(k, carry):
            pl.semaphore_signal(
                barrier, inc=1, device_id={"dp": lax.rem(me + k, dp_size)}, device_id_type=MESH
            )
            return carry

        lax.fori_loop(1, dp_size, greet, 0)
        pl.semaphore_wait(barrier, 3 + dp_size - 1)
        for q in range(grad_land.shape[0]):
            for r in (2, 3, 1):
                grad_copy(q, r).start()
        for k in range(2):
            begin_pieces(k)
        weight_acc[...] = jnp.zeros_like(weight_acc)

    @pl.when(h == 0)
    def _():
        span = pl.ds(pl.multiple_of(s * rows, rows), rows)
        grad_scr[:, 0:rows] = mixed_grad[own, span].astype(F32).T
        for r in (1, 2, 3):
            grad_copy(s, r).wait_recv()
            grad_scr[:, r * rows : (r + 1) * rows] = grad_land[s, r - 1].astype(F32).T

    query = proj[head_rows(h, 0, head_count)]
    key = proj[head_rows(h, 1, head_count)]
    value = proj[head_rows(h, 2, head_count)]
    draws = draws_ref[...]
    draws_ext = jnp.concatenate([draws, jnp.ones((16, FEAT), BF16)], axis=0)
    hot = hot_ref[...]
    away_wide = away_marks(hot)
    away = away_wide.astype(BF16)
    inverse = 1.0 / den_ref[0:1]
    head_grad = grad_scr[pl.ds(pl.multiple_of(h * HD, HD), HD)]
    grad_num = (head_grad * inverse).astype(BF16)
    grad_den = -jnp.sum(head_grad * mixed_ref[...], axis=0, keepdims=True) * inverse
    den_rows = jnp.broadcast_to(grad_den, (16, total)).astype(BF16)
    spread_grad = jnp.concatenate(spread(grad_num, hot) + [den_rows * hot], axis=0)
    spread_value = jnp.concatenate(spread(value, away) + [away], axis=0)

    phi_q = phi_q_ref[...]
    state_grad = mat_nt(spread_grad, phi_q).astype(BF16)
    scaled_q = mat_tn(state_ref[...], spread_grad) * phi_q.astype(F32)
    back_q = mat(draws_ext, scaled_q.astype(BF16))
    query_grad = back_q[0:HD] - query.astype(F32) * (back_q[HD : HD + 1] * root)

    phi_k = phi_k_ref[...]
    scaled_k = mat_tn(state_grad, spread_value) * phi_k.astype(F32)
    back_k = mat(draws_ext, scaled_k.astype(BF16))
    key_grad = back_k[0:HD] - key.astype(F32) * (back_k[HD : HD + 1] * root)
    value_grad = pick(mat(state_grad[0 : NBUCK * HD], phi_k), away_wide)

    ring_turn(0)
    one = (lax.broadcasted_iota(jnp.int32, hot.shape, 0) < 1).astype(F32).astype(BF16)
    num_scr[...] = jnp.concatenate([grad_num, den_rows], axis=0)
    value_scr[...] = jnp.concatenate([value, one], axis=0).astype(F32).T.astype(BF16)

    for c in range(total // CHUNK):
        cols = slice(c * CHUNK, (c + 1) * CHUNK)
        score = mat(value_scr[...], num_scr[:, cols]) * soft_ref[:, cols].astype(F32)
        score = score.astype(BF16)
        score_scr[:, cols] = score
        exact_scr[:, cols] = mat(proj[head_rows(h, 1, head_count)], score)
    query_grad = query_grad + exact_scr[...] * root
    key_grad = key_grad + mat_nt(query, score_scr[...]) * root
    value_grad = value_grad + mat_nt(grad_num, soft_ref[...])
    wide_grad = jnp.concatenate([query_grad, key_grad, value_grad], axis=0)
    low_grad = wide_grad.astype(BF16)
    for kind in range(3):
        proj_scr[head_rows(h, kind, head_count)] = low_grad[kind * HD : (kind + 1) * HD]
    weight_grad = mat(low_grad[:, 0:rows], x_ref[0])
    for r in (1, 2, 3):
        weight_grad = weight_grad + mat(low_grad[:, r * rows : (r + 1) * rows], x_ref[r])
    span = pl.ds(pl.multiple_of(h * 3 * HD, 3 * HD), 3 * HD)
    weight_acc[span, 0:model] += weight_grad
    weight_acc[span, model:] += jnp.broadcast_to(
        jnp.sum(wide_grad, axis=1, keepdims=True), (3 * HD, 128)
    )

    @pl.when(s == seqs - 1)
    def _():
        begin_own(h)

        @pl.when(h > 0)
        def _():
            relay_own(h - 1)

    @pl.when((s > 0) & (h == 0))
    def _():
        add_near(s - 1)

    @pl.when(h == heads - 1)
    def _():
        @pl.when(s > 0)
        def _():
            for i in range(2):
                near_copy(s - 1, i).wait_send()

        for r in (3, 1, 2, 0):
            term = mat_tn(proj_scr[:, r * rows : (r + 1) * rows], weight[...])
            if r % 2:
                near_send[r // 2] = term.astype(BF16)
                near_copy(s, r // 2).start()
            else:
                far_keep[r // 2] = term

    ring_turn(1)

    @pl.when(last)
    def _():
        add_near(s)
        relay_own(h)
        for q in range(grad_land.shape[0] - 1):
            finish(q)

        sums = []
        for q in range(head_count):

            def arrive(k, carry):
                own_copy(q, k).wait_recv()
                return carry + own_land[q, k].astype(F32)

            sums.append(lax.fori_loop(1, half, arrive, own_mid[q, pair].astype(F32)))
        joined = jnp.concatenate(sums, axis=1)
        base = model // dp_size
        small = base // GROUP
        fill = jnp.broadcast_to(
            joined[base : base + 1], (part_send.shape[1] - small, joined.shape[1])
        )
        for a in range(GROUP):
            part_send[a] = jnp.concatenate(
                [joined[a * small : (a + 1) * small], fill], axis=0
            ).astype(BF16)
        for r in (2, 3, 1):
            part_copy(r).start()
        finish(s)
        proj_out[own] = part_send[own].astype(F32)
        for r in (1, 2, 3):
            part_copy(r).wait_recv()
            proj_out[partner(own, r)] = part_land[r - 1].astype(F32)

        for q in range(grad_land.shape[0]):
            for r in (1, 2, 3):
                grad_copy(q, r).wait_send()
        for i in range(2):
            near_copy(s, i).wait_send()
        far_copy(s).wait_send()
        for r in (1, 2, 3):
            part_copy(r).wait_send()
        for part in range(2):
            cross_copy(part).wait_send()

        def leave(k, carry):
            for way in range(2):
                for i in range(3):
                    met_copy(k, way, i).wait_send()
            return carry

        lax.fori_loop(0, dp_size, leave, 0)

        def leave_ring(k, carry):
            for way in range(2):
                for part in range(2):
                    ring_copy(k, way, part).wait_send()
            return carry

        lax.fori_loop(0, dp_size - 1, leave_ring, 0)
        for q in range(head_count):
            pair_copy(q).wait_send()

            def leave_own(k, carry):
                own_copy(q, k).wait_send()
                return carry

            lax.fori_loop(1, half, leave_own, 0)


def attend_back(
    dp_size, parts, mixed_grad, weight, draws, hot, proj, state, mixed, den, soft, phi_q, phi_k,
    down_grad, up_grad, tail,
):
    seqs, _, rows, model = parts.shape
    heads = draws.shape[0]
    width = heads * HD
    total = GROUP * rows
    n = dp_size
    ring_rows = down_grad.shape[1] + up_grad.shape[1] + tail.shape[1]
    own_rows = aligned(model // n + 1)
    part_rows = aligned(model // (n * GROUP) + 1)
    single = pl.Buffered(1)
    whole = lambda *shape: pl.BlockSpec(
        shape, lambda s, h: (0,) * len(shape), pipeline_mode=single
    )
    mode = single if n > 16 else None
    by_seq = lambda *shape: pl.BlockSpec(
        (None,) + shape, lambda s, h: (s,) + (0,) * len(shape), pipeline_mode=mode
    )
    by_head = lambda *shape: pl.BlockSpec(
        (None, None) + shape, lambda s, h: (s, h) + (0,) * len(shape), pipeline_mode=mode
    )
    anywhere = pl.BlockSpec(memory_space=pl.ANY)
    dma = pltpu.SemaphoreType.DMA
    return pl.pallas_call(
        lambda *refs: attend_back_kernel(dp_size, *refs),
        grid=(seqs, heads),
        out_shape=(
            jax.ShapeDtypeStruct((seqs * rows, model), F32),
            jax.ShapeDtypeStruct((ring_rows, model), F32),
            jax.ShapeDtypeStruct((GROUP, part_rows, 3 * width), F32),
        ),
        in_specs=[
            by_seq(GROUP, rows, model), whole(*mixed_grad.shape), whole(3 * width, model),
            pl.BlockSpec((None, HD, FEAT), lambda s, h: (h, 0, 0)),
            by_seq(16, total), by_seq(3 * width, total), by_head(STATES, FEAT), by_head(HD, total),
            by_head(8, total), by_head(total, total), by_head(FEAT, total), by_head(FEAT, total),
            anywhere, anywhere, anywhere,
        ],
        out_specs=(
            whole(seqs * rows, model), whole(ring_rows, model), whole(GROUP, part_rows, 3 * width),
        ),
        scratch_shapes=[
            pltpu.VMEM((width, total), F32),
            pltpu.VMEM((HD + 16, total), BF16),
            pltpu.VMEM((total, HD + 16), BF16),
            pltpu.VMEM((total, total), BF16),
            pltpu.VMEM((HD, total), F32),
            pltpu.VMEM((3 * width, total), BF16),
            pltpu.VMEM((seqs, 3, rows, width), BF16),
            pltpu.VMEM((2, rows, model), BF16),
            pltpu.VMEM((seqs, 2, rows, model), BF16),
            pltpu.VMEM((2, rows, model), F32),
            pltpu.VMEM((rows, model), BF16),
            pltpu.VMEM((seqs, rows, model), BF16),
            pltpu.VMEM((n, 2, ring_rows, model), BF16),
            pltpu.VMEM((n, 2, ring_rows, model), BF16),
            pltpu.VMEM((n - 1, 2, ring_rows, model), BF16),
            pltpu.VMEM((ring_rows, model), BF16),
            pltpu.VMEM((3 * width, model + 128), F32),
            pltpu.VMEM((heads, 2, n // 2, own_rows, 3 * HD), BF16),
            pltpu.VMEM((heads, n // 2, own_rows, 3 * HD), BF16),
            pltpu.VMEM((heads, n // 2, own_rows, 3 * HD), BF16),
            pltpu.VMEM((heads, n // 2, own_rows, 3 * HD), BF16),
            pltpu.VMEM((GROUP, part_rows, 3 * width), BF16),
            pltpu.VMEM((3, part_rows, 3 * width), BF16),
            dma((2, seqs, 3)),
            dma((2, seqs, 2)),
            dma((2, seqs)),
            dma((n, 2, 3)),
            dma((2, n, 2, 3)),
            dma((2, n - 1, 2, 2)),
            dma((2, 2)),
            dma((2, heads)),
            dma((2, heads, n // 2)),
            dma((2, 3)),
        ],
        compiler_params=pltpu.CompilerParams(
            vmem_limit_bytes=VMEM + (3 * 1024 * 1024 if n > 16 else 0), collective_id=2, has_side_effects=True
        ),
        cost_estimate=pl.CostEstimate(
            flops=48_000_000_000, bytes_accessed=40_000_000, transcendentals=0
        ),
        name="attend_back",
    )(
        parts, mixed_grad, weight, draws, hot, proj, state, mixed, den, soft, phi_q, phi_k,
        down_grad, up_grad, tail,
    )


def finish_kernel(
    starts, heads, attn_grad, resid_grad, hidden, sums, proj_sums, weight_rows, gain_ref, shift_ref,
    input_out, norm1_gain_out, norm1_bias_out, qkv_out, qkv_bias_out, out_out, out_bias_out,
    norm2_gain_out, norm2_bias_out, up_out, up_bias_out, down_out, down_bias_out,
):
    gain, shift = as_row(gain_ref), as_row(shift_ref)
    normed, scale = row_stats(hidden[...].astype(F32))
    input_out[...] = resid_grad[...] + norm_back(attn_grad[...] * gain, normed, scale)

    @pl.when(pl.program_id(0) == 0)
    def _():
        index = lax.axis_index("dp") * GROUP + lax.axis_index("feat")
        small, model = out_out.shape
        share = down_out.shape[0]
        ff = up_out.shape[1]

        def own(row, size):
            length = row.shape[1]
            wide = jnp.broadcast_to(row, (8, length))
            back = lax.rem(length - lax.rem(index * size, length), length)
            return pltpu.roll(wide, back, 1)[0:1, 0:size]

        down_out[...] = sums[0:share]
        first = starts[0]
        up_out[...] = jnp.concatenate(
            [sums[first + i * small : first + (i + 1) * small] for i in range(ff // model)], axis=1
        )
        first = starts[0] + starts[1]
        out_out[...] = sums[first : first + small]
        totals = first + small
        for i, out in enumerate((down_bias_out, out_bias_out, norm2_gain_out, norm2_bias_out)):
            out[...] = own(sums[totals + i : totals + i + 1], small).reshape(small)
        per_row = model // share
        level = index // per_row
        row = jnp.zeros((1, model), F32)
        for i in range(ff // model):
            row = jnp.where(level == i, sums[totals + 4 + i : totals + 5 + i], row)
        up_bias_out[...] = own(row, share).reshape(share)

        pieces = []
        for kind in range(3):
            for f in range(GROUP):
                for h in range(heads):
                    lanes = slice((h * 3 + kind) * HD, (h * 3 + kind + 1) * HD)
                    pieces.append(proj_sums[f, 0 : small + 1, lanes])
        grid = jnp.concatenate(pieces, axis=1)
        weight_sum, bias_sum = grid[0:small], grid[small : small + 1]
        qkv_out[...] = weight_sum
        qkv_bias_out[...] = own(bias_sum, 3 * small).reshape(3 * small)
        wide = weight_rows[...].astype(F32)

        def to_row(column):
            column = jnp.concatenate(
                [column, jnp.zeros((-small % 128, 1), F32)], axis=0
            )
            return jnp.broadcast_to(column, (column.shape[0], 128)).T[0:1, 0:small]

        bias_grad = to_row(jnp.sum(wide * bias_sum, axis=1, keepdims=True))
        gain_grad = to_row(jnp.sum(wide * weight_sum, axis=1, keepdims=True))
        norm1_bias_out[...] = bias_grad.reshape(small)
        gain_grad = (gain_grad - own(shift, small) * bias_grad) / own(gain, small)
        norm1_gain_out[...] = gain_grad.reshape(small)


def finish_all(
    attn_grad, resid_grad, hidden, sums, proj_sums, weight_rows, gain, shift, starts, devices, ff,
    heads,
):
    seqs, rows, model = hidden.shape
    small, share = model // devices, ff // devices
    whole = lambda *shape: pl.BlockSpec(shape, lambda s: (0,) * len(shape))
    by_seq = pl.BlockSpec((rows, model), lambda s: (s, 0))
    shapes = (
        (small,), (small,), (small, 3 * model), (3 * small,), (small, model), (small,), (small,),
        (small,), (small, ff), (share,), (share, model), (small,),
    )
    return pl.pallas_call(
        lambda *refs: finish_kernel(starts, heads, *refs),
        grid=(seqs,),
        out_shape=(jax.ShapeDtypeStruct((seqs * rows, model), F32),)
        + tuple(jax.ShapeDtypeStruct(shape, F32) for shape in shapes),
        in_specs=[
            by_seq, by_seq, pl.BlockSpec((None, rows, model), lambda s: (s, 0, 0)),
            whole(*sums.shape), whole(*proj_sums.shape), whole(*weight_rows.shape), whole(model),
            whole(model),
        ],
        out_specs=(by_seq,) + tuple(whole(*shape) for shape in shapes),
        compiler_params=pltpu.CompilerParams(vmem_limit_bytes=VMEM),
        name="finish_all",
    )(attn_grad, resid_grad, hidden, sums, proj_sums, weight_rows, gain, shift)


def per_device(
    hidden_in, norm1_gain, norm1_bias, qkv_weight, qkv_bias, feature_draws, out_weight, out_bias,
    norm2_gain, norm2_bias, up_weight, up_bias, down_weight, down_bias, block_bucket, out_grad,
):
    seqs, rows, model = hidden_in.shape
    ff = up_weight.shape[1]
    dp_size = lax.axis_size("dp")
    devices = dp_size * GROUP
    small = model // devices
    heads = feature_draws.shape[0] // GROUP
    flat = (seqs * rows, model)

    (
        parts, mixed_parts, proj, state, mixed, den, hot, own_weight, own_draws, soft, phi_q, phi_k,
    ) = attend(
        block_bucket, hidden_in, norm1_gain, norm1_bias, qkv_bias, qkv_weight, feature_draws
    )
    layer_out, resid_grad, mixed_grad, down_grad, up_grad, tail = block_layer(
        mixed_parts, hidden_in.reshape(flat), out_grad.reshape(flat), out_weight, out_bias,
        norm2_gain, norm2_bias, down_bias, up_bias, up_weight, down_weight, devices,
    )
    attn_grad, sums, proj_sums = attend_back(
        dp_size, parts, mixed_grad, own_weight, own_draws, hot, proj, state, mixed, den, soft,
        phi_q, phi_k, down_grad, up_grad, tail,
    )
    index = lax.axis_index("dp") * GROUP + lax.axis_index("feat")
    weight_rows = lax.dynamic_slice_in_dim(qkv_weight, index * small, small, 0)
    (
        input_grad, norm1_gain_sum, norm1_bias_sum, qkv_weight_sum, qkv_bias_sum, out_weight_sum,
        out_bias_sum, norm2_gain_sum, norm2_bias_sum, up_sum, up_bias_sum, down_sum, down_bias_sum,
    ) = finish_all(
        attn_grad, resid_grad, hidden_in, sums, proj_sums, weight_rows, norm1_gain, norm1_bias,
        (down_grad.shape[1], up_grad.shape[1]), devices, ff, heads,
    )
    return (
        layer_out.reshape(hidden_in.shape), input_grad.reshape(hidden_in.shape), norm1_gain_sum,
        norm1_bias_sum, qkv_weight_sum, qkv_bias_sum, out_weight_sum, out_bias_sum, norm2_gain_sum,
        norm2_bias_sum, up_sum, up_bias_sum, down_sum, down_bias_sum,
    )


def solution(mesh):
    both = ("dp", "feat")
    rows = P("dp", "feat", None)
    in_specs = (
        rows, P(), P(), P(), P(), P(None, None, "feat"), P(), P(), P(), P(), P(), P(), P(), P(),
        P("dp", None, None), rows,
    )
    out_specs = (
        rows, rows, P(both), P(both), P(both, None), P(both), P(both, None), P(both), P(both),
        P(both), P(both, None), P(both), P(both, None), P(both),
    )
    return jax.shard_map(
        per_device, mesh=mesh, in_specs=in_specs, out_specs=out_specs, check_vma=False
    )
```

```python
import math

import jax
import jax.numpy as jnp
from jax import lax
from jax.experimental import pallas as pl
from jax.experimental.pallas import tpu as pltpu
from jax.sharding import PartitionSpec as P

HD = 64
FEAT = 256
BLOCK = 64
NBUCK = 4
GROUP = 4
CHUNK = 256
STATES = NBUCK * HD + 16
FAR = 16384.0
VMEM = 60 * 1024 * 1024

F32 = jnp.float32
BF16 = jnp.bfloat16
MESH = pl.DeviceIdType.MESH


def mat(left, right):
    return jnp.dot(left, right, preferred_element_type=F32)


def mat_nt(left, right):
    return lax.dot_general(left, right, (((1,), (1,)), ((), ())), preferred_element_type=F32)


def mat_tn(left, right):
    return lax.dot_general(left, right, (((0,), (0,)), ((), ())), preferred_element_type=F32)


def row_stats(values):
    row_mean = jnp.mean(values, axis=-1, keepdims=True)
    centered = values - row_mean
    scale = lax.rsqrt(jnp.mean(centered * centered, axis=-1, keepdims=True) + 1e-05)
    return (centered * scale, scale)


def norm_back(cotangent, normed, scale):
    mean_one = jnp.mean(cotangent, axis=-1, keepdims=True)
    mean_two = jnp.mean(cotangent * normed, axis=-1, keepdims=True)
    return scale * (cotangent - mean_one - normed * mean_two)


def features(vectors, draws):
    wide = vectors.astype(F32)
    square = jnp.sum(wide * wide, axis=0, keepdims=True) * (0.5 / math.sqrt(HD))
    return jnp.exp(mat_tn(draws, vectors) - (square + 0.5 * math.log(FEAT)))


def spread(rows, marks):
    return [rows * marks[u : u + 1] for u in range(NBUCK)]


def pick(stacked, marks):
    total = stacked[0:HD] * marks[0:1]
    for u in range(1, NBUCK):
        total = total + stacked[u * HD : (u + 1) * HD] * marks[u : u + 1]
    return total


def away_marks(hot):
    live = (lax.broadcasted_iota(jnp.int32, hot.shape, 0) < NBUCK).astype(F32)
    return live - hot.astype(F32)


def partner(own, r):
    x, core = own // 2, own % 2
    if r & 2:
        x = 1 - x
    if r & 1:
        core = 1 - core
    return 2 * x + core


def as_row(ref):
    return ref[...].reshape(1, ref.shape[0])


def aligned(count):
    return -(-count // 16) * 16


def remote(src, dst, send, recv, place):
    return pltpu.make_async_remote_copy(
        src_ref=src, dst_ref=dst, send_sem=send, recv_sem=recv, device_id=place, device_id_type=MESH
    )


def head_rows(h, kind, heads):
    return pl.ds(pl.multiple_of((kind * heads + h) * HD, HD), HD)


def attend_kernel(
    bucket, hidden, gain_ref, shift_ref, bias_ref, weight_any, draws_in,
    parts_any, mix_any, proj_out, state_out, mixed_out, den_out, hot_out, weight_out, draws_out,
    soft_out, phi_q_out, phi_k_out,
    parts, mix_land, mix_send, raw, bias_row, bias_scr, draws_land,
    query_scr, key_scr, value_scr, low_scr, gather_scr,
    raw_sem, part_send, part_recv, draw_send, draw_recv, mix_send_sem, mix_recv_sem, out_sem,
):
    s, h = pl.program_id(0), pl.program_id(1)
    seqs, rows, model = hidden.shape
    heads = draws_out.shape[0]
    total = GROUP * rows
    width = heads * HD
    own = lax.axis_index("feat")
    near, across = {"feat": partner(own, 1)}, {"feat": partner(own, 2)}

    def part_copy(q, kind):
        src, dst, place = ((0, 1, near), (0, 2, across), (2, 3, near))[kind]
        return remote(
            parts.at[q, src], parts.at[q, dst], part_send.at[q, kind], part_recv.at[q, kind], place
        )

    def draw_copy(r):
        other = partner(own, r)
        return remote(
            draws_in.at[pl.ds(other * heads, heads)], draws_land.at[r - 1],
            draw_send.at[r - 1], draw_recv.at[r - 1], {"feat": other},
        )

    def mix_copy(q, r):
        return remote(
            mix_send.at[q, r], mix_land.at[q, r], mix_send_sem.at[q, r - 1],
            mix_recv_sem.at[q, r - 1], {"feat": partner(own, r)},
        )

    def raw_copy(j):
        cols = pl.ds(pl.multiple_of(j * model + (own // 2) * 2 * width, 2 * width), 2 * width)
        return pltpu.make_async_copy(weight_any.at[:, cols], raw.at[j], raw_sem.at[j])

    def out_copy(q):
        return pltpu.make_async_copy(parts.at[q], parts_any.at[q], out_sem.at[q])

    @pl.when((s == 0) & (h == 0))
    def _():
        for j in range(3):
            raw_copy(j).start()
        barrier = pltpu.get_barrier_semaphore()
        for r in (1, 2, 3):
            pl.semaphore_signal(
                barrier, inc=1, device_id={"feat": partner(own, r)}, device_id_type=MESH
            )
        gain, shift = as_row(gain_ref), as_row(shift_ref)
        first = row_stats(hidden[0].astype(F32))[0] * gain + shift
        parts[0, 0] = first.astype(BF16)
        pl.semaphore_wait(barrier, 3)
        part_copy(0, 1).start()
        part_copy(0, 0).start()
        for r in (1, 2, 3):
            draw_copy(r).start()
        for q in range(1, seqs):
            normed = row_stats(hidden[q].astype(F32))[0] * gain + shift
            parts[q, 0] = normed.astype(BF16)
            part_copy(q, 1).start()
            part_copy(q, 0).start()
        core = own % 2
        bias_row[...] = as_row(bias_ref)
        for j in range(3):
            raw_copy(j).wait()
            piece = raw[j].astype(F32)
            piece = jnp.where(core == 0, piece[:, 0:width], piece[:, width:])
            weight_out[j * width : (j + 1) * width] = piece.T.astype(BF16)
            cols = pl.ds(pl.multiple_of(j * model + (own // 2) * 2 * width, 2 * width), 2 * width)
            pair = jnp.broadcast_to(bias_row[:, cols], (128, 2 * width))
            pair = jnp.where(core == 0, pair[:, 0:width], pair[:, width:])
            bias_scr[j * width : (j + 1) * width] = pair.T
        part_copy(0, 1).wait_recv()
        part_copy(0, 2).start()
        for r in (1, 2, 3):
            draw_copy(r).wait_recv()
        mine = draws_in[pl.ds(own * heads, heads)]
        draws_out[...] = jnp.concatenate(
            [mine] + [draws_land[r - 1] for r in (1, 2, 3)], axis=2
        )

    @pl.when(h == 0)
    def _():
        per = rows // BLOCK
        lanes = lax.broadcasted_iota(jnp.int32, (16, total), 1) // BLOCK
        level = lax.broadcasted_iota(jnp.int32, (16, total), 0)
        ids = jnp.full((16, total), -1, jnp.int32)
        for r in range(GROUP):
            for i in range(per):
                ids = jnp.where(
                    lanes == r * per + i, bucket[s, partner(own, r) * per + i, 0], ids
                )
        hot_out[...] = (ids == level).astype(F32).astype(BF16)

        def project(r):
            cols = slice(r * rows, (r + 1) * rows)
            piece = mat_nt(weight_out[...], parts[s, r]) + bias_scr[:, 0:1]
            proj_out[:, cols] = piece.astype(BF16)

        project(0)
        part_copy(s, 0).wait_recv()
        project(1)
        project(2)
        part_copy(s, 2).wait_recv()
        project(3)
        out_copy(s).start()

    query = proj_out[head_rows(h, 0, heads)]
    key = proj_out[head_rows(h, 1, heads)]
    value = proj_out[head_rows(h, 2, heads)]
    draws = draws_out[h]
    hot = hot_out[...]
    hot_wide = hot.astype(F32)
    away = away_marks(hot).astype(BF16)
    phi_q = features(query, draws).astype(BF16)
    phi_k = features(key, draws).astype(BF16)
    phi_q_out[...] = phi_q
    phi_k_out[...] = phi_k
    spread_value = jnp.concatenate(spread(value, away) + [away], axis=0)
    state = mat_nt(spread_value, phi_k).astype(BF16)
    state_out[...] = state
    low = mat(state, phi_q)
    low_scr[0:HD] = pick(low, hot_wide)
    low_den = jnp.sum(low[NBUCK * HD :] * hot_wide, axis=0, keepdims=True)
    low_scr[HD : HD + 8] = jnp.broadcast_to(low_den, (8, total))
    query_scr[...] = jnp.concatenate([query * (1.0 / math.sqrt(HD)), hot], axis=0).astype(BF16)
    key_scr[...] = jnp.concatenate([key, away * -FAR], axis=0).astype(F32).T.astype(BF16)
    value_scr[0:HD] = value
    value_scr[HD:] = jnp.ones((16, total), BF16)

    score = mat(key_scr[...], query_scr[:, 0:CHUNK])
    for c in range(total // CHUNK):
        cols = slice(c * CHUNK, (c + 1) * CHUNK)
        ahead = slice((c + 1) * CHUNK, (c + 2) * CHUNK)
        later = mat(key_scr[...], query_scr[:, ahead]) if ahead.stop <= total else None
        weights = jnp.exp(score).astype(BF16)
        score = later
        soft_out[:, cols] = weights
        exact = mat(value_scr[...], weights)
        den = low_scr[HD : HD + 8, cols] + exact[HD : HD + 8]
        mixed = (low_scr[0:HD, cols] + exact[0:HD]) / den[0:1]
        mixed_out[:, cols] = mixed
        den_out[:, cols] = den
        gather_scr[pl.ds(pl.multiple_of(h * HD, HD), HD), cols] = mixed

    @pl.when((h == heads - 2) & (s < seqs - 1))
    def _():
        part_copy(s + 1, 1).wait_recv()
        part_copy(s + 1, 2).start()

    @pl.when(h == heads - 1)
    def _():
        for r in range(GROUP):
            piece = gather_scr[:, r * rows : (r + 1) * rows].T.astype(BF16)
            if r == 0:
                mix_land[s, 0] = piece
            else:
                mix_send[s, r] = piece
                mix_copy(s, r).start()

    @pl.when((s == seqs - 1) & (h == heads - 1))
    def _():
        for q in range(seqs):
            for r in (1, 2, 3):
                mix_copy(q, r).wait_recv()
        done = pltpu.make_async_copy(mix_land, mix_any, out_sem.at[seqs])
        done.start()
        for q in range(seqs):
            for kind in range(3):
                part_copy(q, kind).wait_send()
            for r in (1, 2, 3):
                mix_copy(q, r).wait_send()
            out_copy(q).wait()
        for r in (1, 2, 3):
            draw_copy(r).wait_send()
        done.wait()


def attend(bucket, hidden, gain, shift, bias, weight, draws):
    seqs, rows, model = hidden.shape
    heads = draws.shape[0] // GROUP
    width = heads * HD
    total = GROUP * rows
    whole = lambda *shape: pl.BlockSpec(shape, lambda s, h: (0,) * len(shape))
    by_seq = lambda *shape: pl.BlockSpec((None,) + shape, lambda s, h: (s,) + (0,) * len(shape))
    by_head = lambda *shape: pl.BlockSpec(
        (None, None) + shape, lambda s, h: (s, h) + (0,) * len(shape)
    )
    anywhere = pl.BlockSpec(memory_space=pl.ANY)
    return pl.pallas_call(
        attend_kernel,
        grid=(seqs, heads),
        out_shape=(
            jax.ShapeDtypeStruct((seqs, GROUP, rows, model), BF16),
            jax.ShapeDtypeStruct((seqs, GROUP, rows, width), BF16),
            jax.ShapeDtypeStruct((seqs, 3 * width, total), BF16),
            jax.ShapeDtypeStruct((seqs, heads, STATES, FEAT), BF16),
            jax.ShapeDtypeStruct((seqs, heads, HD, total), F32),
            jax.ShapeDtypeStruct((seqs, heads, 8, total), F32),
            jax.ShapeDtypeStruct((seqs, 16, total), BF16),
            jax.ShapeDtypeStruct((3 * width, model), BF16),
            jax.ShapeDtypeStruct((heads, HD, FEAT), BF16),
            jax.ShapeDtypeStruct((seqs, heads, total, total), BF16),
            jax.ShapeDtypeStruct((seqs, heads, FEAT, total), BF16),
            jax.ShapeDtypeStruct((seqs, heads, FEAT, total), BF16),
        ),
        in_specs=[
            pl.BlockSpec(memory_space=pltpu.SMEM),
            whole(seqs, rows, model), whole(model), whole(model), whole(3 * model), anywhere,
            whole(*draws.shape),
        ],
        out_specs=(
            anywhere, anywhere, by_seq(3 * width, total), by_head(STATES, FEAT), by_head(HD, total),
            by_head(8, total), by_seq(16, total), whole(3 * width, model), whole(heads, HD, FEAT),
            by_head(total, total), by_head(FEAT, total), by_head(FEAT, total),
        ),
        scratch_shapes=[
            pltpu.VMEM((seqs, GROUP, rows, model), BF16),
            pltpu.VMEM((seqs, GROUP, rows, width), BF16),
            pltpu.VMEM((seqs, GROUP, rows, width), BF16),
            pltpu.VMEM((3, model, 2 * width), BF16),
            pltpu.VMEM((1, 3 * model), F32),
            pltpu.VMEM((3 * width, 128), F32),
            pltpu.VMEM((3, heads, HD, draws.shape[2]), BF16),
            pltpu.VMEM((HD + 16, total), BF16),
            pltpu.VMEM((total, HD + 16), BF16),
            pltpu.VMEM((HD + 16, total), BF16),
            pltpu.VMEM((HD + 8, total), F32),
            pltpu.VMEM((width, total), F32),
            pltpu.SemaphoreType.DMA((3,)),
            pltpu.SemaphoreType.DMA((seqs, 3)),
            pltpu.SemaphoreType.DMA((seqs, 3)),
            pltpu.SemaphoreType.DMA((3,)),
            pltpu.SemaphoreType.DMA((3,)),
            pltpu.SemaphoreType.DMA((seqs, 3)),
            pltpu.SemaphoreType.DMA((seqs, 3)),
            pltpu.SemaphoreType.DMA((seqs + 1,)),
        ],
        compiler_params=pltpu.CompilerParams(
            vmem_limit_bytes=VMEM, collective_id=1, has_side_effects=True
        ),
        cost_estimate=pl.CostEstimate(
            flops=24_000_000_000, bytes_accessed=20_000_000, transcendentals=0
        ),
        name="attend",
    )(bucket, hidden, gain, shift, bias, weight, draws)


def block_kernel(
    direct, parts_ref, hidden, grad, out_w, out_b, gain_ref, shift_ref, down_b, up_b, up, down,
    layer_out, resid_out, grads_any, down_any, up_any, tail_any,
    mixed, resid_scr, in_scr, in_t, acc_out, acc_in, act_scr, pre_scr, vec_scr, bias_row,
    down_vm, up_vm, tail_vm, grads_send, grads_land, send_sem, recv_sem, out_sem,
):
    step = pl.program_id(0)
    model = hidden.shape[1]
    count = hidden.shape[0] // CHUNK
    tiles = act_scr.shape[0]
    spans = [slice(c * CHUNK, (c + 1) * CHUNK) for c in range(count)]
    owners = tail_vm.shape[0]
    small = model // owners
    own = lax.axis_index("feat")
    barrier = pltpu.get_barrier_semaphore()

    def swap_groups(pieces):
        pieces = [jnp.where(own % 2 == 1, pieces[r ^ 1], pieces[r]) for r in range(GROUP)]
        return [jnp.where(own // 2 == 1, pieces[r ^ 2], pieces[r]) for r in range(GROUP)]

    def grad_copy(c, r):
        return remote(
            grads_send.at[c, r - 1], grads_land.at[c, r], send_sem.at[c, r - 1],
            recv_sem.at[c, r - 1], {"feat": partner(own, r)},
        )

    def out_copy(i):
        src, dst = (
            (down_vm, down_any), (up_vm, up_any), (tail_vm, tail_any), (grads_land, grads_any)
        )[i]
        return pltpu.make_async_copy(src, dst, out_sem.at[i])

    @pl.when(step == 0)
    def _():
        for r in (1, 2, 3):
            pl.semaphore_signal(
                barrier, inc=1, device_id={"feat": partner(own, r)}, device_id_type=MESH
            )
        for c, span in enumerate(spans):
            pieces = swap_groups([parts_ref[c, r] for r in range(GROUP)])
            mixed[span] = jnp.concatenate(pieces, axis=1)
            resid = hidden[span].astype(F32) + mat(mixed[span], out_w[...]) + as_row(out_b)
            resid_scr[span] = resid
            normed, _ = row_stats(resid)
            inner = normed * as_row(gain_ref) + as_row(shift_ref)
            in_scr[span] = inner.astype(BF16)
            in_t[:, span] = inner.T.astype(BF16)
        acc_out[...] = jnp.zeros_like(acc_out)
        acc_in[...] = jnp.zeros_like(acc_in)
        bias_row[...] = as_row(up_b)

    slope = math.sqrt(2.0 / math.pi)
    total = jnp.zeros((1, model), F32)
    up_bias = bias_row[:, pl.ds(pl.multiple_of(step * model, model), model)]
    for span in spans:
        pre = mat(in_scr[span], up[...]) + up_bias
        square = pre * pre
        tanh = jnp.tanh(pre * (slope + (slope * 0.044715) * square))
        half = 0.5 * (1.0 + tanh)
        act = (pre * half).astype(BF16)
        bend = half + (0.5 * pre) * (1.0 - tanh * tanh) * (
            slope + (3.0 * slope * 0.044715) * square
        )
        pre_grad = mat_nt(grad[span], down[...]) * bend
        total = total + jnp.sum(pre_grad, axis=0, keepdims=True)
        pre_low = pre_grad.astype(BF16)
        act_scr[step, span] = act
        pre_scr[step, span] = pre_low
        acc_out[span] += mat(act, down[...])
        acc_in[span] += mat_nt(pre_low, up[...])
    vec_scr[pl.ds(4 + step, 1)] = total

    @pl.when(step == pl.num_programs(0) - 1)
    def _():
        pl.semaphore_wait(barrier, 3)
        sums = [jnp.zeros((1, model), F32) for _ in range(4)]
        part = model // GROUP
        for c, span in enumerate(spans):
            resid = resid_scr[span]
            normed, scale = row_stats(resid)
            inner_grad = acc_in[span]
            wide = grad[span].astype(F32)
            resid_grad = wide + norm_back(inner_grad * as_row(gain_ref), normed, scale)
            resid_out[span] = resid_grad
            low = resid_grad.astype(BF16)
            in_scr[span] = low
            back = mat_nt(low, out_w[...]).astype(BF16)
            pieces = swap_groups([back[:, a * part : (a + 1) * part] for a in range(GROUP)])
            grads_land[c, 0] = pieces[0]
            for r in (2, 3, 1):
                grads_send[c, r - 1] = pieces[r]
                grad_copy(c, r).start()
            layer_out[span] = (resid + acc_out[span] + as_row(down_b)).astype(BF16)
            for i, term in enumerate((wide, resid_grad, inner_grad * normed, inner_grad)):
                sums[i] = sums[i] + jnp.sum(term, axis=0, keepdims=True)
        for i in range(4):
            vec_scr[i : i + 1] = sums[i]
        for t in range(tiles):
            down_term = mat_tn(act_scr[t], grad[...])
            if direct:
                share = down_vm.shape[1]
                for i in range(model // share):
                    down_vm[t * (model // share) + i] = down_term[
                        i * share : (i + 1) * share
                    ].astype(BF16)
            else:
                down_vm[t * model : (t + 1) * model] = down_term.astype(BF16)
        out_copy(0).start()
        for t in range(0, tiles, 2):
            terms = [mat(in_t[...], pre_scr[t]), mat(in_t[...], pre_scr[t + 1])]
            if direct:
                for i in range(owners):
                    own_rows = slice(i * small, (i + 1) * small)
                    up_vm[i, t * small : (t + 2) * small] = jnp.concatenate(
                        [term[own_rows] for term in terms], axis=0
                    ).astype(BF16)
            else:
                for u, term in enumerate(terms):
                    up_vm[:, (t + u) * model : (t + u + 1) * model] = term.astype(BF16)
        out_copy(1).start()
        out_term = mat_tn(mixed[...], in_scr[...])
        fill = tail_vm.shape[1] - small - 8
        extra = [jnp.zeros((fill, model), F32)] if fill else []
        for i in range(owners):
            tail_vm[i] = jnp.concatenate(
                [out_term[i * small : (i + 1) * small], vec_scr[...]] + extra, axis=0
            ).astype(BF16)
        out_copy(2).start()
        for c in range(count):
            for r in (1, 2, 3):
                grad_copy(c, r).wait_recv()
        out_copy(3).start()
        for c in range(count):
            for r in (1, 2, 3):
                grad_copy(c, r).wait_send()
        for i in range(4):
            out_copy(i).wait()


def block_layer(parts, hidden, grad, out_w, out_b, gain, shift, down_b, up_b, up, down, devices):
    tokens, model = hidden.shape
    ff = up.shape[1]
    steps = ff // model
    seqs = parts.shape[0]
    small, share = model // devices, ff // devices
    direct = small % 8 == 0 and share % 16 == 0
    tail_rows = aligned(small + 8)
    single = pl.Buffered(1)
    whole = lambda *shape: pl.BlockSpec(
        shape, lambda t: (0,) * len(shape), pipeline_mode=single
    )
    anywhere = pl.BlockSpec(memory_space=pl.ANY)
    if direct:
        down_shape, up_shape = (devices, share, model), (devices, steps * small, model)
    else:
        down_shape, up_shape = (ff, model), (model, ff)
    tail_shape = (devices, tail_rows, model)
    layer_out, resid_grad, grads, down_grad, up_grad, tail = pl.pallas_call(
        lambda *refs: block_kernel(direct, *refs),
        grid=(steps,),
        out_shape=(
            jax.ShapeDtypeStruct((tokens, model), BF16),
            jax.ShapeDtypeStruct((tokens, model), F32),
            jax.ShapeDtypeStruct(parts.shape, BF16),
            jax.ShapeDtypeStruct(down_shape, BF16),
            jax.ShapeDtypeStruct(up_shape, BF16),
            jax.ShapeDtypeStruct(tail_shape, BF16),
        ),
        in_specs=[
            whole(*parts.shape), whole(tokens, model), whole(tokens, model), whole(model, model),
            whole(model), whole(model), whole(model), whole(model), whole(ff),
            pl.BlockSpec((model, model), lambda t: (0, t)),
            pl.BlockSpec((model, model), lambda t: (t, 0)),
        ],
        out_specs=(
            whole(tokens, model), whole(tokens, model), anywhere, anywhere, anywhere, anywhere,
        ),
        scratch_shapes=[
            pltpu.VMEM((tokens, model), BF16),
            pltpu.VMEM((tokens, model), F32),
            pltpu.VMEM((tokens, model), BF16),
            pltpu.VMEM((model, tokens), BF16),
            pltpu.VMEM((tokens, model), F32),
            pltpu.VMEM((tokens, model), F32),
            pltpu.VMEM((steps, tokens, model), BF16),
            pltpu.VMEM((steps, tokens, model), BF16),
            pltpu.VMEM((8, model), F32),
            pltpu.VMEM((1, ff), F32),
            pltpu.VMEM(down_shape, BF16),
            pltpu.VMEM(up_shape, BF16),
            pltpu.VMEM(tail_shape, BF16),
            pltpu.VMEM((seqs, 3) + parts.shape[2:], BF16),
            pltpu.VMEM(parts.shape, BF16),
            pltpu.SemaphoreType.DMA((seqs, 3)),
            pltpu.SemaphoreType.DMA((seqs, 3)),
            pltpu.SemaphoreType.DMA((4,)),
        ],
        compiler_params=pltpu.CompilerParams(
            vmem_limit_bytes=VMEM, collective_id=3, has_side_effects=True
        ),
        cost_estimate=pl.CostEstimate(
            flops=26_000_000_000, bytes_accessed=30_000_000, transcendentals=0
        ),
        name="block_layer",
    )(parts, hidden, grad, out_w, out_b, gain, shift, down_b, up_b, up, down)
    if not direct:
        fit = lambda a: jnp.pad(a, ((0, 0), (0, aligned(a.shape[1]) - a.shape[1]), (0, 0)))
        down_grad = fit(down_grad.reshape(devices, share, model))
        up_grad = up_grad.reshape(devices, small, ff // model, model).transpose(0, 2, 1, 3)
        up_grad = fit(up_grad.reshape(devices, ff // model * small, model))
    return layer_out, resid_grad, grads, down_grad, up_grad, tail


def attend_back_kernel(
    dp_size, x_ref, grads_ref, weight, draws_ref, hot_ref, proj, state_ref, mixed_ref, den_ref,
    soft_ref, phi_q_ref, phi_k_ref, down_any, up_any, tail_any,
    attn_out, ring_out, proj_out,
    grad_scr, num_scr, value_scr, score_scr, exact_scr, proj_scr,
    near_send, near_land, far_keep, far_send, far_land,
    mine, met, ring_land, cross_land,
    weight_acc, own_send, pair_land, own_mid, own_land, part_send, part_land,
    near_sems, far_sems, mine_sem, met_sems, ring_sems, cross_sems, pair_sems, own_sems,
    part_sems,
):
    s, h = pl.program_id(0), pl.program_id(1)
    seqs, heads = pl.num_programs(0), pl.num_programs(1)
    rows, model = x_ref.shape[1], x_ref.shape[2]
    head_count = proj_scr.shape[0] // (3 * HD)
    width = head_count * HD
    total = GROUP * rows
    root = 1.0 / math.sqrt(HD)
    own, me = lax.axis_index("feat"), lax.axis_index("dp")
    own_x, own_core = own // 2, own % 2
    near, across = {"feat": partner(own, 1)}, {"feat": partner(own, 2)}
    last = (s == seqs - 1) & (h == heads - 1)

    def near_copy(q, i):
        return remote(
            near_send.at[i], near_land.at[q, i], near_sems.at[0, q, i], near_sems.at[1, q, i], near
        )

    def far_copy(q):
        return remote(far_send, far_land.at[q], far_sems.at[0, q], far_sems.at[1, q], across)

    odd = me % 2
    half = dp_size // 2
    spot = (1 - odd) * (me // 2) + odd * (dp_size - 1 - me // 2)

    def at_spot(p):
        p = lax.rem(p + dp_size, dp_size)
        upper = p // half
        return (1 - upper) * (2 * p) + upper * (2 * (dp_size - 1 - p) + 1)

    def chunk(k, way):
        return at_spot(spot - 1 - k) if way == 0 else at_spot(lax.rem(spot + 1 + k, dp_size))

    sources = (down_any, up_any, tail_any)
    lengths = [ref.shape[1] for ref in sources]
    starts = [sum(lengths[:i]) for i in range(3)]

    def owner(k, way, core):
        return chunk(k, way) * GROUP + 2 * way + core

    def mine_copy(k, way, i):
        return pltpu.make_async_copy(
            sources[i].at[owner(k, way, own_core)],
            mine.at[k, way, pl.ds(starts[i], lengths[i])],
            mine_sem.at[k, way, i],
        )

    def met_copy(k, way, i):
        return remote(
            sources[i].at[owner(k, way, 1 - own_core)],
            met.at[k, way, pl.ds(starts[i], lengths[i])],
            met_sems.at[0, k, way, i], met_sems.at[1, k, way, i], near,
        )

    cut = aligned(mine.shape[2] // 2)
    halves = (pl.ds(0, cut), pl.ds(cut, mine.shape[2] - cut))

    def ring_copy(k, way, part):
        place = at_spot(spot + 1) if way == 0 else at_spot(spot - 1)
        return remote(
            mine.at[k, way, halves[part]], ring_land.at[k, way, halves[part]],
            ring_sems.at[0, k, way, part], ring_sems.at[1, k, way, part], {"dp": place},
        )

    def cross_copy(part):
        return remote(
            mine.at[dp_size - 1, 1 - own_x, halves[part]], cross_land.at[halves[part]],
            cross_sems.at[0, part], cross_sems.at[1, part], across,
        )

    def begin_pieces(k):
        for way in range(2):
            for i in range(3):
                met_copy(k, way, i).start()
                mine_copy(k, way, i).start()

    def ring_step(k, part):
        span = halves[part]
        if part == 0:

            @pl.when(k + 2 < dp_size)
            def _():
                begin_pieces(k + 2)

        @pl.when(k < dp_size)
        def _():
            for way in range(2):
                if part == 0:
                    for i in range(3):
                        mine_copy(k, way, i).wait()
                        met_copy(k, way, i).wait_recv()

                @pl.when(k == 0)
                def _():
                    base = mine[k, way, span].astype(F32) + met[k, way, span].astype(F32)
                    mine[k, way, span] = base.astype(BF16)

                @pl.when(k > 0)
                def _():
                    ring_copy(k - 1, way, part).wait_recv()
                    base = mine[k, way, span].astype(F32) + met[k, way, span].astype(F32)
                    base = base + ring_land[k - 1, way, span].astype(F32)
                    mine[k, way, span] = base.astype(BF16)

                @pl.when(k < dp_size - 1)
                def _():
                    ring_copy(k, way, part).start()

            @pl.when(k == dp_size - 1)
            def _():
                cross_copy(part).start()

        @pl.when(k == dp_size)
        def _():
            cross_copy(part).wait_recv()
            ring_out[span] = mine[dp_size - 1, own_x, span].astype(F32) + cross_land[span].astype(F32)

    def ring_turn(part):
        turn = s * heads + h
        count = seqs * heads
        steps = dp_size + 1

        def body(k, carry):
            ring_step(k, part)
            return carry

        lax.fori_loop(turn * steps // count, (turn + 1) * steps // count, body, 0)

    parity, pair = me % 2, me // 2
    mate = me + 1 - 2 * parity

    def pair_copy(q):
        return remote(
            own_send.at[q, 1 - parity], pair_land.at[q], pair_sems.at[0, q], pair_sems.at[1, q],
            {"dp": mate},
        )

    def own_copy(q, k):
        to = lax.rem(pair + k, half)
        return remote(
            own_mid.at[q, to], own_land.at[q, k], own_sems.at[0, q, k], own_sems.at[1, q, k],
            {"dp": 2 * to + parity},
        )

    def begin_own(q):
        base = model // dp_size
        turned = weight_acc[pl.ds(pl.multiple_of(q * 3 * HD, 3 * HD), 3 * HD)].T
        fill = turned[model : model + own_send.shape[3] - base]
        for c in range(dp_size):
            own_send[q, c % 2, c // 2] = jnp.concatenate(
                [turned[c * base : (c + 1) * base], fill], axis=0
            ).astype(BF16)
        pair_copy(q).start()

    def relay_own(q):
        pair_copy(q).wait_recv()
        own_mid[q] = (own_send[q, parity].astype(F32) + pair_land[q].astype(F32)).astype(BF16)

        def start(k, carry):
            own_copy(q, k).start()
            return carry

        lax.fori_loop(1, half, start, 0)

    def part_copy(r):
        other = partner(own, r)
        return remote(
            part_send.at[other], part_land.at[r - 1], part_sems.at[0, r - 1],
            part_sems.at[1, r - 1], {"feat": other},
        )

    def seq_span(q):
        return pl.ds(pl.multiple_of(q * rows, rows), rows)

    def add_near(q):
        near_copy(q, 1).wait_recv()

        @pl.when(q > 0)
        def _():
            far_copy(q - 1).wait_send()

        far_send[...] = (far_keep[1] + near_land[q, 1].astype(F32)).astype(BF16)
        far_copy(q).start()
        near_copy(q, 0).wait_recv()
        attn_out[seq_span(q)] = far_keep[0] + near_land[q, 0].astype(F32)

    def finish(q):
        far_copy(q).wait_recv()
        span = seq_span(q)
        attn_out[span] = attn_out[span] + far_land[q].astype(F32)

    @pl.when((s == 0) & (h == 0))
    def _():
        barrier = pltpu.get_barrier_semaphore()
        for r in (1, 2, 3):
            pl.semaphore_signal(
                barrier, inc=1, device_id={"feat": partner(own, r)}, device_id_type=MESH
            )

        def greet(k, carry):
            pl.semaphore_signal(
                barrier, inc=1, device_id={"dp": lax.rem(me + k, dp_size)}, device_id_type=MESH
            )
            return carry

        lax.fori_loop(1, dp_size, greet, 0)
        pl.semaphore_wait(barrier, 3 + dp_size - 1)
        for k in range(2):
            begin_pieces(k)
        weight_acc[...] = jnp.zeros_like(weight_acc)

    @pl.when(h == 0)
    def _():
        for r in range(GROUP):
            grad_scr[:, r * rows : (r + 1) * rows] = grads_ref[r].astype(F32).T

    query = proj[head_rows(h, 0, head_count)]
    key = proj[head_rows(h, 1, head_count)]
    value = proj[head_rows(h, 2, head_count)]
    draws = draws_ref[...]
    draws_ext = jnp.concatenate([draws, jnp.ones((16, FEAT), BF16)], axis=0)
    hot = hot_ref[...]
    away_wide = away_marks(hot)
    away = away_wide.astype(BF16)
    inverse = 1.0 / den_ref[0:1]
    head_grad = grad_scr[pl.ds(pl.multiple_of(h * HD, HD), HD)]
    grad_num = (head_grad * inverse).astype(BF16)
    grad_den = -jnp.sum(head_grad * mixed_ref[...], axis=0, keepdims=True) * inverse
    den_rows = jnp.broadcast_to(grad_den, (16, total)).astype(BF16)
    spread_grad = jnp.concatenate(spread(grad_num, hot) + [den_rows * hot], axis=0)
    spread_value = jnp.concatenate(spread(value, away) + [away], axis=0)

    phi_q = phi_q_ref[...]
    state_grad = mat_nt(spread_grad, phi_q).astype(BF16)
    scaled_q = mat_tn(state_ref[...], spread_grad) * phi_q.astype(F32)
    back_q = mat(draws_ext, scaled_q.astype(BF16))
    query_grad = back_q[0:HD] - query.astype(F32) * (back_q[HD : HD + 1] * root)

    phi_k = phi_k_ref[...]
    scaled_k = mat_tn(state_grad, spread_value) * phi_k.astype(F32)
    back_k = mat(draws_ext, scaled_k.astype(BF16))
    key_grad = back_k[0:HD] - key.astype(F32) * (back_k[HD : HD + 1] * root)
    value_grad = pick(mat(state_grad[0 : NBUCK * HD], phi_k), away_wide)

    ring_turn(0)
    one = (lax.broadcasted_iota(jnp.int32, hot.shape, 0) < 1).astype(F32).astype(BF16)
    num_scr[...] = jnp.concatenate([grad_num, den_rows], axis=0)
    value_scr[...] = jnp.concatenate([value, one], axis=0).astype(F32).T.astype(BF16)

    for c in range(total // CHUNK):
        cols = slice(c * CHUNK, (c + 1) * CHUNK)
        score = mat(value_scr[...], num_scr[:, cols]) * soft_ref[:, cols].astype(F32)
        score = score.astype(BF16)
        score_scr[:, cols] = score
        exact_scr[:, cols] = mat(proj[head_rows(h, 1, head_count)], score)
    query_grad = query_grad + exact_scr[...] * root
    key_grad = key_grad + mat_nt(query, score_scr[...]) * root
    value_grad = value_grad + mat_nt(grad_num, soft_ref[...])
    wide_grad = jnp.concatenate([query_grad, key_grad, value_grad], axis=0)
    low_grad = wide_grad.astype(BF16)
    for kind in range(3):
        proj_scr[head_rows(h, kind, head_count)] = low_grad[kind * HD : (kind + 1) * HD]
    weight_grad = mat(low_grad[:, 0:rows], x_ref[0])
    for r in (1, 2, 3):
        weight_grad = weight_grad + mat(low_grad[:, r * rows : (r + 1) * rows], x_ref[r])
    span = pl.ds(pl.multiple_of(h * 3 * HD, 3 * HD), 3 * HD)
    weight_acc[span, 0:model] += weight_grad
    weight_acc[span, model:] += jnp.broadcast_to(
        jnp.sum(wide_grad, axis=1, keepdims=True), (3 * HD, 128)
    )

    @pl.when(s == seqs - 1)
    def _():
        begin_own(h)

        @pl.when(h > 0)
        def _():
            relay_own(h - 1)

    @pl.when((s > 0) & (h == 0))
    def _():
        add_near(s - 1)

    @pl.when(h == heads - 1)
    def _():
        @pl.when(s > 0)
        def _():
            for i in range(2):
                near_copy(s - 1, i).wait_send()

        for r in (3, 1, 2, 0):
            term = mat_tn(proj_scr[:, r * rows : (r + 1) * rows], weight[...])
            if r % 2:
                near_send[r // 2] = term.astype(BF16)
                near_copy(s, r // 2).start()
            else:
                far_keep[r // 2] = term

    ring_turn(1)

    @pl.when(last)
    def _():
        add_near(s)
        relay_own(h)
        for q in range(near_land.shape[0] - 1):
            finish(q)

        sums = []
        for q in range(head_count):

            def arrive(k, carry):
                own_copy(q, k).wait_recv()
                return carry + own_land[q, k].astype(F32)

            sums.append(lax.fori_loop(1, half, arrive, own_mid[q, pair].astype(F32)))
        joined = jnp.concatenate(sums, axis=1)
        base = model // dp_size
        small = base // GROUP
        fill = jnp.broadcast_to(
            joined[base : base + 1], (part_send.shape[1] - small, joined.shape[1])
        )
        for a in range(GROUP):
            part_send[a] = jnp.concatenate(
                [joined[a * small : (a + 1) * small], fill], axis=0
            ).astype(BF16)
        for r in (2, 3, 1):
            part_copy(r).start()
        finish(s)
        proj_out[own] = part_send[own].astype(F32)
        for r in (1, 2, 3):
            part_copy(r).wait_recv()
            proj_out[partner(own, r)] = part_land[r - 1].astype(F32)

        for i in range(2):
            near_copy(s, i).wait_send()
        far_copy(s).wait_send()
        for r in (1, 2, 3):
            part_copy(r).wait_send()
        for part in range(2):
            cross_copy(part).wait_send()

        def leave(k, carry):
            for way in range(2):
                for i in range(3):
                    met_copy(k, way, i).wait_send()
            return carry

        lax.fori_loop(0, dp_size, leave, 0)

        def leave_ring(k, carry):
            for way in range(2):
                for part in range(2):
                    ring_copy(k, way, part).wait_send()
            return carry

        lax.fori_loop(0, dp_size - 1, leave_ring, 0)
        for q in range(head_count):
            pair_copy(q).wait_send()

            def leave_own(k, carry):
                own_copy(q, k).wait_send()
                return carry

            lax.fori_loop(1, half, leave_own, 0)


def attend_back(
    dp_size, parts, grads, weight, draws, hot, proj, state, mixed, den, soft, phi_q, phi_k,
    down_grad, up_grad, tail,
):
    seqs, _, rows, model = parts.shape
    heads = draws.shape[0]
    width = heads * HD
    total = GROUP * rows
    n = dp_size
    ring_rows = down_grad.shape[1] + up_grad.shape[1] + tail.shape[1]
    own_rows = aligned(model // n + 1)
    part_rows = aligned(model // (n * GROUP) + 1)
    single = pl.Buffered(1)
    whole = lambda *shape: pl.BlockSpec(
        shape, lambda s, h: (0,) * len(shape), pipeline_mode=single
    )
    mode = single if n > 16 else None
    by_seq = lambda *shape: pl.BlockSpec(
        (None,) + shape, lambda s, h: (s,) + (0,) * len(shape), pipeline_mode=mode
    )
    by_head = lambda *shape: pl.BlockSpec(
        (None, None) + shape, lambda s, h: (s, h) + (0,) * len(shape), pipeline_mode=mode
    )
    anywhere = pl.BlockSpec(memory_space=pl.ANY)
    dma = pltpu.SemaphoreType.DMA
    return pl.pallas_call(
        lambda *refs: attend_back_kernel(dp_size, *refs),
        grid=(seqs, heads),
        out_shape=(
            jax.ShapeDtypeStruct((seqs * rows, model), F32),
            jax.ShapeDtypeStruct((ring_rows, model), F32),
            jax.ShapeDtypeStruct((GROUP, part_rows, 3 * width), F32),
        ),
        in_specs=[
            by_seq(GROUP, rows, model), by_seq(GROUP, rows, width), whole(3 * width, model),
            pl.BlockSpec((None, HD, FEAT), lambda s, h: (h, 0, 0)),
            by_seq(16, total), by_seq(3 * width, total), by_head(STATES, FEAT), by_head(HD, total),
            by_head(8, total), by_head(total, total), by_head(FEAT, total), by_head(FEAT, total),
            anywhere, anywhere, anywhere,
        ],
        out_specs=(
            whole(seqs * rows, model), whole(ring_rows, model), whole(GROUP, part_rows, 3 * width),
        ),
        scratch_shapes=[
            pltpu.VMEM((width, total), F32),
            pltpu.VMEM((HD + 16, total), BF16),
            pltpu.VMEM((total, HD + 16), BF16),
            pltpu.VMEM((total, total), BF16),
            pltpu.VMEM((HD, total), F32),
            pltpu.VMEM((3 * width, total), BF16),
            pltpu.VMEM((2, rows, model), BF16),
            pltpu.VMEM((seqs, 2, rows, model), BF16),
            pltpu.VMEM((2, rows, model), F32),
            pltpu.VMEM((rows, model), BF16),
            pltpu.VMEM((seqs, rows, model), BF16),
            pltpu.VMEM((n, 2, ring_rows, model), BF16),
            pltpu.VMEM((n, 2, ring_rows, model), BF16),
            pltpu.VMEM((n - 1, 2, ring_rows, model), BF16),
            pltpu.VMEM((ring_rows, model), BF16),
            pltpu.VMEM((3 * width, model + 128), F32),
            pltpu.VMEM((heads, 2, n // 2, own_rows, 3 * HD), BF16),
            pltpu.VMEM((heads, n // 2, own_rows, 3 * HD), BF16),
            pltpu.VMEM((heads, n // 2, own_rows, 3 * HD), BF16),
            pltpu.VMEM((heads, n // 2, own_rows, 3 * HD), BF16),
            pltpu.VMEM((GROUP, part_rows, 3 * width), BF16),
            pltpu.VMEM((3, part_rows, 3 * width), BF16),
            dma((2, seqs, 2)),
            dma((2, seqs)),
            dma((n, 2, 3)),
            dma((2, n, 2, 3)),
            dma((2, n - 1, 2, 2)),
            dma((2, 2)),
            dma((2, heads)),
            dma((2, heads, n // 2)),
            dma((2, 3)),
        ],
        compiler_params=pltpu.CompilerParams(
            vmem_limit_bytes=VMEM + (3 * 1024 * 1024 if n > 16 else 0), collective_id=2, has_side_effects=True
        ),
        cost_estimate=pl.CostEstimate(
            flops=48_000_000_000, bytes_accessed=40_000_000, transcendentals=0
        ),
        name="attend_back",
    )(
        parts, grads, weight, draws, hot, proj, state, mixed, den, soft, phi_q, phi_k, down_grad,
        up_grad, tail,
    )


def finish_kernel(
    starts, heads, attn_grad, resid_grad, hidden, sums, proj_sums, weight_rows, gain_ref, shift_ref,
    input_out, norm1_gain_out, norm1_bias_out, qkv_out, qkv_bias_out, out_out, out_bias_out,
    norm2_gain_out, norm2_bias_out, up_out, up_bias_out, down_out, down_bias_out,
):
    gain, shift = as_row(gain_ref), as_row(shift_ref)
    normed, scale = row_stats(hidden[...].astype(F32))
    input_out[...] = resid_grad[...] + norm_back(attn_grad[...] * gain, normed, scale)

    @pl.when(pl.program_id(0) == 0)
    def _():
        index = lax.axis_index("dp") * GROUP + lax.axis_index("feat")
        small, model = out_out.shape
        share = down_out.shape[0]
        ff = up_out.shape[1]

        def own(row, size):
            length = row.shape[1]
            wide = jnp.broadcast_to(row, (8, length))
            back = lax.rem(length - lax.rem(index * size, length), length)
            return pltpu.roll(wide, back, 1)[0:1, 0:size]

        down_out[...] = sums[0:share]
        first = starts[0]
        up_out[...] = jnp.concatenate(
            [sums[first + i * small : first + (i + 1) * small] for i in range(ff // model)], axis=1
        )
        first = starts[0] + starts[1]
        out_out[...] = sums[first : first + small]
        totals = first + small
        for i, out in enumerate((down_bias_out, out_bias_out, norm2_gain_out, norm2_bias_out)):
            out[...] = own(sums[totals + i : totals + i + 1], small).reshape(small)
        per_row = model // share
        level = index // per_row
        row = jnp.zeros((1, model), F32)
        for i in range(ff // model):
            row = jnp.where(level == i, sums[totals + 4 + i : totals + 5 + i], row)
        up_bias_out[...] = own(row, share).reshape(share)

        pieces = []
        for kind in range(3):
            for f in range(GROUP):
                for h in range(heads):
                    lanes = slice((h * 3 + kind) * HD, (h * 3 + kind + 1) * HD)
                    pieces.append(proj_sums[f, 0 : small + 1, lanes])
        grid = jnp.concatenate(pieces, axis=1)
        weight_sum, bias_sum = grid[0:small], grid[small : small + 1]
        qkv_out[...] = weight_sum
        qkv_bias_out[...] = own(bias_sum, 3 * small).reshape(3 * small)
        wide = weight_rows[...].astype(F32)

        def to_row(column):
            column = jnp.concatenate(
                [column, jnp.zeros((-small % 128, 1), F32)], axis=0
            )
            return jnp.broadcast_to(column, (column.shape[0], 128)).T[0:1, 0:small]

        bias_grad = to_row(jnp.sum(wide * bias_sum, axis=1, keepdims=True))
        gain_grad = to_row(jnp.sum(wide * weight_sum, axis=1, keepdims=True))
        norm1_bias_out[...] = bias_grad.reshape(small)
        gain_grad = (gain_grad - own(shift, small) * bias_grad) / own(gain, small)
        norm1_gain_out[...] = gain_grad.reshape(small)


def finish_all(
    attn_grad, resid_grad, hidden, sums, proj_sums, weight_rows, gain, shift, starts, devices, ff,
    heads,
):
    seqs, rows, model = hidden.shape
    small, share = model // devices, ff // devices
    whole = lambda *shape: pl.BlockSpec(shape, lambda s: (0,) * len(shape))
    by_seq = pl.BlockSpec((rows, model), lambda s: (s, 0))
    shapes = (
        (small,), (small,), (small, 3 * model), (3 * small,), (small, model), (small,), (small,),
        (small,), (small, ff), (share,), (share, model), (small,),
    )
    return pl.pallas_call(
        lambda *refs: finish_kernel(starts, heads, *refs),
        grid=(seqs,),
        out_shape=(jax.ShapeDtypeStruct((seqs * rows, model), F32),)
        + tuple(jax.ShapeDtypeStruct(shape, F32) for shape in shapes),
        in_specs=[
            by_seq, by_seq, pl.BlockSpec((None, rows, model), lambda s: (s, 0, 0)),
            whole(*sums.shape), whole(*proj_sums.shape), whole(*weight_rows.shape), whole(model),
            whole(model),
        ],
        out_specs=(by_seq,) + tuple(whole(*shape) for shape in shapes),
        compiler_params=pltpu.CompilerParams(vmem_limit_bytes=VMEM),
        name="finish_all",
    )(attn_grad, resid_grad, hidden, sums, proj_sums, weight_rows, gain, shift)


def per_device(
    hidden_in, norm1_gain, norm1_bias, qkv_weight, qkv_bias, feature_draws, out_weight, out_bias,
    norm2_gain, norm2_bias, up_weight, up_bias, down_weight, down_bias, block_bucket, out_grad,
):
    seqs, rows, model = hidden_in.shape
    ff = up_weight.shape[1]
    dp_size = lax.axis_size("dp")
    devices = dp_size * GROUP
    small = model // devices
    heads = feature_draws.shape[0] // GROUP
    flat = (seqs * rows, model)

    (
        parts, mixed_parts, proj, state, mixed, den, hot, own_weight, own_draws, soft, phi_q, phi_k,
    ) = attend(
        block_bucket, hidden_in, norm1_gain, norm1_bias, qkv_bias, qkv_weight, feature_draws
    )
    layer_out, resid_grad, grads, down_grad, up_grad, tail = block_layer(
        mixed_parts, hidden_in.reshape(flat), out_grad.reshape(flat), out_weight, out_bias,
        norm2_gain, norm2_bias, down_bias, up_bias, up_weight, down_weight, devices,
    )
    attn_grad, sums, proj_sums = attend_back(
        dp_size, parts, grads, own_weight, own_draws, hot, proj, state, mixed, den, soft,
        phi_q, phi_k, down_grad, up_grad, tail,
    )
    index = lax.axis_index("dp") * GROUP + lax.axis_index("feat")
    weight_rows = lax.dynamic_slice_in_dim(qkv_weight, index * small, small, 0)
    (
        input_grad, norm1_gain_sum, norm1_bias_sum, qkv_weight_sum, qkv_bias_sum, out_weight_sum,
        out_bias_sum, norm2_gain_sum, norm2_bias_sum, up_sum, up_bias_sum, down_sum, down_bias_sum,
    ) = finish_all(
        attn_grad, resid_grad, hidden_in, sums, proj_sums, weight_rows, norm1_gain, norm1_bias,
        (down_grad.shape[1], up_grad.shape[1]), devices, ff, heads,
    )
    return (
        layer_out.reshape(hidden_in.shape), input_grad.reshape(hidden_in.shape), norm1_gain_sum,
        norm1_bias_sum, qkv_weight_sum, qkv_bias_sum, out_weight_sum, out_bias_sum, norm2_gain_sum,
        norm2_bias_sum, up_sum, up_bias_sum, down_sum, down_bias_sum,
    )


def solution(mesh):
    both = ("dp", "feat")
    rows = P("dp", "feat", None)
    in_specs = (
        rows, P(), P(), P(), P(), P(None, None, "feat"), P(), P(), P(), P(), P(), P(), P(), P(),
        P("dp", None, None), rows,
    )
    out_specs = (
        rows, rows, P(both), P(both), P(both, None), P(both), P(both, None), P(both), P(both),
        P(both), P(both, None), P(both), P(both, None), P(both),
    )
    return jax.shard_map(
        per_device, mesh=mesh, in_specs=in_specs, out_specs=out_specs, check_vma=False
    )
```

```python
import math

import jax
import jax.numpy as jnp
from jax import lax
from jax.experimental import pallas as pl
from jax.experimental.pallas import tpu as pltpu
from jax.sharding import PartitionSpec as P

HD = 64
FEAT = 256
BLOCK = 64
NBUCK = 4
GROUP = 4
CHUNK = 256
STATES = NBUCK * HD + 16
FAR = 16384.0
VMEM = 60 * 1024 * 1024

F32 = jnp.float32
BF16 = jnp.bfloat16
MESH = pl.DeviceIdType.MESH


def mat(left, right):
    return jnp.dot(left, right, preferred_element_type=F32)


def mat_nt(left, right):
    return lax.dot_general(left, right, (((1,), (1,)), ((), ())), preferred_element_type=F32)


def mat_tn(left, right):
    return lax.dot_general(left, right, (((0,), (0,)), ((), ())), preferred_element_type=F32)


def row_stats(values):
    row_mean = jnp.mean(values, axis=-1, keepdims=True)
    centered = values - row_mean
    scale = lax.rsqrt(jnp.mean(centered * centered, axis=-1, keepdims=True) + 1e-05)
    return (centered * scale, scale)


def norm_back(cotangent, normed, scale):
    mean_one = jnp.mean(cotangent, axis=-1, keepdims=True)
    mean_two = jnp.mean(cotangent * normed, axis=-1, keepdims=True)
    return scale * (cotangent - mean_one - normed * mean_two)


def features(vectors, draws):
    wide = vectors.astype(F32)
    square = jnp.sum(wide * wide, axis=0, keepdims=True) * (0.5 / math.sqrt(HD))
    return jnp.exp(mat_tn(draws, vectors) - (square + 0.5 * math.log(FEAT)))


def spread(rows, marks):
    return [rows * marks[u : u + 1] for u in range(NBUCK)]


def pick(stacked, marks):
    total = stacked[0:HD] * marks[0:1]
    for u in range(1, NBUCK):
        total = total + stacked[u * HD : (u + 1) * HD] * marks[u : u + 1]
    return total


def away_marks(hot):
    live = (lax.broadcasted_iota(jnp.int32, hot.shape, 0) < NBUCK).astype(F32)
    return live - hot.astype(F32)


def partner(own, r):
    x, core = own // 2, own % 2
    if r & 2:
        x = 1 - x
    if r & 1:
        core = 1 - core
    return 2 * x + core


def as_row(ref):
    return ref[...].reshape(1, ref.shape[0])


def aligned(count):
    return -(-count // 16) * 16


def remote(src, dst, send, recv, place):
    return pltpu.make_async_remote_copy(
        src_ref=src, dst_ref=dst, send_sem=send, recv_sem=recv, device_id=place, device_id_type=MESH
    )


def head_rows(h, kind, heads):
    return pl.ds(pl.multiple_of((kind * heads + h) * HD, HD), HD)


def attend_kernel(
    bucket, hidden, gain_ref, shift_ref, bias_ref, weight_any, draws_in,
    parts_any, mix_any, proj_out, state_out, mixed_out, den_out, hot_out, weight_out, draws_out,
    soft_out, phi_q_out, phi_k_out,
    parts, mix_land, mix_send, raw, bias_row, bias_scr, draws_land,
    query_scr, key_scr, value_scr, low_scr, gather_scr,
    raw_sem, part_send, part_recv, draw_send, draw_recv, mix_send_sem, mix_recv_sem, out_sem,
):
    s, h = pl.program_id(0), pl.program_id(1)
    seqs, rows, model = hidden.shape
    heads = draws_out.shape[0]
    total = GROUP * rows
    width = heads * HD
    own = lax.axis_index("feat")
    near, across = {"feat": partner(own, 1)}, {"feat": partner(own, 2)}

    def part_copy(q, kind):
        src, dst, place = ((0, 1, near), (0, 2, across), (2, 3, near))[kind]
        return remote(
            parts.at[q, src], parts.at[q, dst], part_send.at[q, kind], part_recv.at[q, kind], place
        )

    def draw_copy(r):
        other = partner(own, r)
        return remote(
            draws_in.at[pl.ds(other * heads, heads)], draws_land.at[r - 1],
            draw_send.at[r - 1], draw_recv.at[r - 1], {"feat": other},
        )

    def mix_copy(q, r):
        return remote(
            mix_send.at[q, r], mix_land.at[q, r], mix_send_sem.at[q, r - 1],
            mix_recv_sem.at[q, r - 1], {"feat": partner(own, r)},
        )

    def raw_copy(j):
        cols = pl.ds(pl.multiple_of(j * model + (own // 2) * 2 * width, 2 * width), 2 * width)
        return pltpu.make_async_copy(weight_any.at[:, cols], raw.at[j], raw_sem.at[j])

    def out_copy(q):
        return pltpu.make_async_copy(parts.at[q], parts_any.at[q], out_sem.at[q])

    @pl.when((s == 0) & (h == 0))
    def _():
        for j in range(3):
            raw_copy(j).start()
        barrier = pltpu.get_barrier_semaphore()
        for r in (1, 2, 3):
            pl.semaphore_signal(
                barrier, inc=1, device_id={"feat": partner(own, r)}, device_id_type=MESH
            )
        gain, shift = as_row(gain_ref), as_row(shift_ref)
        first = row_stats(hidden[0].astype(F32))[0] * gain + shift
        parts[0, 0] = first.astype(BF16)
        pl.semaphore_wait(barrier, 3)
        part_copy(0, 1).start()
        part_copy(0, 0).start()
        for r in (1, 2, 3):
            draw_copy(r).start()
        for q in range(1, seqs):
            normed = row_stats(hidden[q].astype(F32))[0] * gain + shift
            parts[q, 0] = normed.astype(BF16)
            part_copy(q, 1).start()
            part_copy(q, 0).start()
        core = own % 2
        bias_row[...] = as_row(bias_ref)
        for j in range(3):
            raw_copy(j).wait()
            piece = raw[j].astype(F32)
            piece = jnp.where(core == 0, piece[:, 0:width], piece[:, width:])
            weight_out[j * width : (j + 1) * width] = piece.T.astype(BF16)
            cols = pl.ds(pl.multiple_of(j * model + (own // 2) * 2 * width, 2 * width), 2 * width)
            pair = jnp.broadcast_to(bias_row[:, cols], (128, 2 * width))
            pair = jnp.where(core == 0, pair[:, 0:width], pair[:, width:])
            bias_scr[j * width : (j + 1) * width] = pair.T
        part_copy(0, 1).wait_recv()
        part_copy(0, 2).start()
        for r in (1, 2, 3):
            draw_copy(r).wait_recv()
        mine = draws_in[pl.ds(own * heads, heads)]
        draws_out[...] = jnp.concatenate(
            [mine] + [draws_land[r - 1] for r in (1, 2, 3)], axis=2
        )

    @pl.when(h == 0)
    def _():
        per = rows // BLOCK
        lanes = lax.broadcasted_iota(jnp.int32, (16, total), 1) // BLOCK
        level = lax.broadcasted_iota(jnp.int32, (16, total), 0)
        ids = jnp.full((16, total), -1, jnp.int32)
        for r in range(GROUP):
            for i in range(per):
                ids = jnp.where(
                    lanes == r * per + i, bucket[s, partner(own, r) * per + i, 0], ids
                )
        hot_out[...] = (ids == level).astype(F32).astype(BF16)

        def project(r):
            cols = slice(r * rows, (r + 1) * rows)
            piece = mat_nt(weight_out[...], parts[s, r]) + bias_scr[:, 0:1]
            proj_out[:, cols] = piece.astype(BF16)

        project(0)
        part_copy(s, 0).wait_recv()
        project(1)
        project(2)
        part_copy(s, 2).wait_recv()
        project(3)
        out_copy(s).start()

    query = proj_out[head_rows(h, 0, heads)]
    key = proj_out[head_rows(h, 1, heads)]
    value = proj_out[head_rows(h, 2, heads)]
    draws = draws_out[h]
    hot = hot_out[...]
    hot_wide = hot.astype(F32)
    away = away_marks(hot).astype(BF16)
    phi_q = features(query, draws).astype(BF16)
    phi_k = features(key, draws).astype(BF16)
    phi_q_out[...] = phi_q
    phi_k_out[...] = phi_k
    spread_value = jnp.concatenate(spread(value, away) + [away], axis=0)
    state = mat_nt(spread_value, phi_k).astype(BF16)
    state_out[...] = state
    low = mat(state, phi_q)
    low_scr[0:HD] = pick(low, hot_wide)
    low_den = jnp.sum(low[NBUCK * HD :] * hot_wide, axis=0, keepdims=True)
    low_scr[HD : HD + 8] = jnp.broadcast_to(low_den, (8, total))
    query_scr[...] = jnp.concatenate([query * (1.0 / math.sqrt(HD)), hot], axis=0).astype(BF16)
    key_scr[...] = jnp.concatenate([key, away * -FAR], axis=0).astype(F32).T.astype(BF16)
    value_scr[0:HD] = value
    value_scr[HD:] = jnp.ones((16, total), BF16)

    score = mat(key_scr[...], query_scr[:, 0:CHUNK])
    for c in range(total // CHUNK):
        cols = slice(c * CHUNK, (c + 1) * CHUNK)
        ahead = slice((c + 1) * CHUNK, (c + 2) * CHUNK)
        later = mat(key_scr[...], query_scr[:, ahead]) if ahead.stop <= total else None
        weights = jnp.exp(score).astype(BF16)
        score = later
        soft_out[:, cols] = weights
        exact = mat(value_scr[...], weights)
        den = low_scr[HD : HD + 8, cols] + exact[HD : HD + 8]
        mixed = (low_scr[0:HD, cols] + exact[0:HD]) / den[0:1]
        mixed_out[:, cols] = mixed
        den_out[:, cols] = den
        gather_scr[pl.ds(pl.multiple_of(h * HD, HD), HD), cols] = mixed

    @pl.when((h == heads - 2) & (s < seqs - 1))
    def _():
        part_copy(s + 1, 1).wait_recv()
        part_copy(s + 1, 2).start()

    @pl.when(h == heads - 1)
    def _():
        for r in range(GROUP):
            piece = gather_scr[:, r * rows : (r + 1) * rows].T.astype(BF16)
            if r == 0:
                mix_land[s, 0] = piece
            else:
                mix_send[s, r] = piece
                mix_copy(s, r).start()

    @pl.when((s == seqs - 1) & (h == heads - 1))
    def _():
        for q in range(seqs):
            for r in (1, 2, 3):
                mix_copy(q, r).wait_recv()
        done = pltpu.make_async_copy(mix_land, mix_any, out_sem.at[seqs])
        done.start()
        for q in range(seqs):
            for kind in range(3):
                part_copy(q, kind).wait_send()
            for r in (1, 2, 3):
                mix_copy(q, r).wait_send()
            out_copy(q).wait()
        for r in (1, 2, 3):
            draw_copy(r).wait_send()
        done.wait()


def attend(bucket, hidden, gain, shift, bias, weight, draws):
    seqs, rows, model = hidden.shape
    heads = draws.shape[0] // GROUP
    width = heads * HD
    total = GROUP * rows
    whole = lambda *shape: pl.BlockSpec(shape, lambda s, h: (0,) * len(shape))
    by_seq = lambda *shape: pl.BlockSpec((None,) + shape, lambda s, h: (s,) + (0,) * len(shape))
    by_head = lambda *shape: pl.BlockSpec(
        (None, None) + shape, lambda s, h: (s, h) + (0,) * len(shape)
    )
    anywhere = pl.BlockSpec(memory_space=pl.ANY)
    return pl.pallas_call(
        attend_kernel,
        grid=(seqs, heads),
        out_shape=(
            jax.ShapeDtypeStruct((seqs, GROUP, rows, model), BF16),
            jax.ShapeDtypeStruct((seqs, GROUP, rows, width), BF16),
            jax.ShapeDtypeStruct((seqs, 3 * width, total), BF16),
            jax.ShapeDtypeStruct((seqs, heads, STATES, FEAT), BF16),
            jax.ShapeDtypeStruct((seqs, heads, HD, total), F32),
            jax.ShapeDtypeStruct((seqs, heads, 8, total), F32),
            jax.ShapeDtypeStruct((seqs, 16, total), BF16),
            jax.ShapeDtypeStruct((3 * width, model), BF16),
            jax.ShapeDtypeStruct((heads, HD, FEAT), BF16),
            jax.ShapeDtypeStruct((seqs, heads, total, total), BF16),
            jax.ShapeDtypeStruct((seqs, heads, FEAT, total), BF16),
            jax.ShapeDtypeStruct((seqs, heads, FEAT, total), BF16),
        ),
        in_specs=[
            pl.BlockSpec(memory_space=pltpu.SMEM),
            whole(seqs, rows, model), whole(model), whole(model), whole(3 * model), anywhere,
            whole(*draws.shape),
        ],
        out_specs=(
            anywhere, anywhere, by_seq(3 * width, total), by_head(STATES, FEAT), by_head(HD, total),
            by_head(8, total), by_seq(16, total), whole(3 * width, model), whole(heads, HD, FEAT),
            by_head(total, total), by_head(FEAT, total), by_head(FEAT, total),
        ),
        scratch_shapes=[
            pltpu.VMEM((seqs, GROUP, rows, model), BF16),
            pltpu.VMEM((seqs, GROUP, rows, width), BF16),
            pltpu.VMEM((seqs, GROUP, rows, width), BF16),
            pltpu.VMEM((3, model, 2 * width), BF16),
            pltpu.VMEM((1, 3 * model), F32),
            pltpu.VMEM((3 * width, 128), F32),
            pltpu.VMEM((3, heads, HD, draws.shape[2]), BF16),
            pltpu.VMEM((HD + 16, total), BF16),
            pltpu.VMEM((total, HD + 16), BF16),
            pltpu.VMEM((HD + 16, total), BF16),
            pltpu.VMEM((HD + 8, total), F32),
            pltpu.VMEM((width, total), F32),
            pltpu.SemaphoreType.DMA((3,)),
            pltpu.SemaphoreType.DMA((seqs, 3)),
            pltpu.SemaphoreType.DMA((seqs, 3)),
            pltpu.SemaphoreType.DMA((3,)),
            pltpu.SemaphoreType.DMA((3,)),
            pltpu.SemaphoreType.DMA((seqs, 3)),
            pltpu.SemaphoreType.DMA((seqs, 3)),
            pltpu.SemaphoreType.DMA((seqs + 1,)),
        ],
        compiler_params=pltpu.CompilerParams(
            vmem_limit_bytes=VMEM, collective_id=1, has_side_effects=True
        ),
        cost_estimate=pl.CostEstimate(
            flops=24_000_000_000, bytes_accessed=20_000_000, transcendentals=0
        ),
        name="attend",
    )(bucket, hidden, gain, shift, bias, weight, draws)


def block_kernel(
    direct, parts_ref, hidden, grad, out_w, out_b, gain_ref, shift_ref, down_b, up_b, up, down,
    layer_out, resid_out, grads_any, first_any, down_any, up_any, tail_any,
    mixed, resid_scr, in_scr, in_t, acc_out, acc_in, act_scr, pre_scr, vec_scr, bias_row,
    down_vm, up_vm, tail_vm, grads_vm, first_land, send_sem, recv_sem, out_sem,
):
    step = pl.program_id(0)
    model = hidden.shape[1]
    count = hidden.shape[0] // CHUNK
    tiles = act_scr.shape[0]
    spans = [slice(c * CHUNK, (c + 1) * CHUNK) for c in range(count)]
    owners = tail_vm.shape[0]
    small = model // owners
    own = lax.axis_index("feat")
    barrier = pltpu.get_barrier_semaphore()

    def swap_groups(pieces):
        pieces = [jnp.where(own % 2 == 1, pieces[r ^ 1], pieces[r]) for r in range(GROUP)]
        return [jnp.where(own // 2 == 1, pieces[r ^ 2], pieces[r]) for r in range(GROUP)]

    def grad_copy(r):
        return remote(
            grads_vm.at[0, r], first_land.at[r - 1], send_sem.at[r - 1], recv_sem.at[r - 1],
            {"feat": partner(own, r)},
        )

    def out_copy(i):
        src, dst = (
            (down_vm, down_any), (up_vm, up_any), (tail_vm, tail_any), (grads_vm, grads_any),
            (first_land, first_any),
        )[i]
        return pltpu.make_async_copy(src, dst, out_sem.at[i])

    @pl.when(step == 0)
    def _():
        for r in (1, 2, 3):
            pl.semaphore_signal(
                barrier, inc=1, device_id={"feat": partner(own, r)}, device_id_type=MESH
            )
        for c, span in enumerate(spans):
            pieces = swap_groups([parts_ref[c, r] for r in range(GROUP)])
            mixed[span] = jnp.concatenate(pieces, axis=1)
            resid = hidden[span].astype(F32) + mat(mixed[span], out_w[...]) + as_row(out_b)
            resid_scr[span] = resid
            normed, _ = row_stats(resid)
            inner = normed * as_row(gain_ref) + as_row(shift_ref)
            in_scr[span] = inner.astype(BF16)
            in_t[:, span] = inner.T.astype(BF16)
        acc_out[...] = jnp.zeros_like(acc_out)
        acc_in[...] = jnp.zeros_like(acc_in)
        bias_row[...] = as_row(up_b)

    slope = math.sqrt(2.0 / math.pi)
    total = jnp.zeros((1, model), F32)
    up_bias = bias_row[:, pl.ds(pl.multiple_of(step * model, model), model)]
    for span in spans:
        pre = mat(in_scr[span], up[...]) + up_bias
        square = pre * pre
        tanh = jnp.tanh(pre * (slope + (slope * 0.044715) * square))
        half = 0.5 * (1.0 + tanh)
        act = (pre * half).astype(BF16)
        bend = half + (0.5 * pre) * (1.0 - tanh * tanh) * (
            slope + (3.0 * slope * 0.044715) * square
        )
        pre_grad = mat_nt(grad[span], down[...]) * bend
        total = total + jnp.sum(pre_grad, axis=0, keepdims=True)
        pre_low = pre_grad.astype(BF16)
        act_scr[step, span] = act
        pre_scr[step, span] = pre_low
        acc_out[span] += mat(act, down[...])
        acc_in[span] += mat_nt(pre_low, up[...])
    vec_scr[pl.ds(4 + step, 1)] = total

    @pl.when(step == pl.num_programs(0) - 1)
    def _():
        pl.semaphore_wait(barrier, 3)
        sums = [jnp.zeros((1, model), F32) for _ in range(4)]
        part = model // GROUP
        for c, span in enumerate(spans):
            resid = resid_scr[span]
            normed, scale = row_stats(resid)
            inner_grad = acc_in[span]
            wide = grad[span].astype(F32)
            resid_grad = wide + norm_back(inner_grad * as_row(gain_ref), normed, scale)
            resid_out[span] = resid_grad
            low = resid_grad.astype(BF16)
            in_scr[span] = low
            back = mat_nt(low, out_w[...]).astype(BF16)
            pieces = swap_groups([back[:, a * part : (a + 1) * part] for a in range(GROUP)])
            for r in (2, 3, 1, 0):
                grads_vm[c, r] = pieces[r]
                if c == 0 and r:
                    grad_copy(r).start()
            layer_out[span] = (resid + acc_out[span] + as_row(down_b)).astype(BF16)
            for i, term in enumerate((wide, resid_grad, inner_grad * normed, inner_grad)):
                sums[i] = sums[i] + jnp.sum(term, axis=0, keepdims=True)
        out_copy(3).start()
        for i in range(4):
            vec_scr[i : i + 1] = sums[i]
        for t in range(tiles):
            down_term = mat_tn(act_scr[t], grad[...])
            if direct:
                share = down_vm.shape[1]
                for i in range(model // share):
                    down_vm[t * (model // share) + i] = down_term[
                        i * share : (i + 1) * share
                    ].astype(BF16)
            else:
                down_vm[t * model : (t + 1) * model] = down_term.astype(BF16)
        out_copy(0).start()
        for t in range(0, tiles, 2):
            terms = [mat(in_t[...], pre_scr[t]), mat(in_t[...], pre_scr[t + 1])]
            if direct:
                for i in range(owners):
                    own_rows = slice(i * small, (i + 1) * small)
                    up_vm[i, t * small : (t + 2) * small] = jnp.concatenate(
                        [term[own_rows] for term in terms], axis=0
                    ).astype(BF16)
            else:
                for u, term in enumerate(terms):
                    up_vm[:, (t + u) * model : (t + u + 1) * model] = term.astype(BF16)
        out_copy(1).start()
        out_term = mat_tn(mixed[...], in_scr[...])
        fill = tail_vm.shape[1] - small - 8
        extra = [jnp.zeros((fill, model), F32)] if fill else []
        for i in range(owners):
            tail_vm[i] = jnp.concatenate(
                [out_term[i * small : (i + 1) * small], vec_scr[...]] + extra, axis=0
            ).astype(BF16)
        out_copy(2).start()
        for r in (1, 2, 3):
            grad_copy(r).wait_recv()
        out_copy(4).start()
        for r in (1, 2, 3):
            grad_copy(r).wait_send()
        for i in range(5):
            out_copy(i).wait()


def block_layer(parts, hidden, grad, out_w, out_b, gain, shift, down_b, up_b, up, down, devices):
    tokens, model = hidden.shape
    ff = up.shape[1]
    steps = ff // model
    seqs = parts.shape[0]
    small, share = model // devices, ff // devices
    direct = small % 8 == 0 and share % 16 == 0
    tail_rows = aligned(small + 8)
    single = pl.Buffered(1)
    whole = lambda *shape: pl.BlockSpec(
        shape, lambda t: (0,) * len(shape), pipeline_mode=single
    )
    anywhere = pl.BlockSpec(memory_space=pl.ANY)
    if direct:
        down_shape, up_shape = (devices, share, model), (devices, steps * small, model)
    else:
        down_shape, up_shape = (ff, model), (model, ff)
    tail_shape = (devices, tail_rows, model)
    layer_out, resid_grad, grads, first, down_grad, up_grad, tail = pl.pallas_call(
        lambda *refs: block_kernel(direct, *refs),
        grid=(steps,),
        out_shape=(
            jax.ShapeDtypeStruct((tokens, model), BF16),
            jax.ShapeDtypeStruct((tokens, model), F32),
            jax.ShapeDtypeStruct(parts.shape, BF16),
            jax.ShapeDtypeStruct((3,) + parts.shape[2:], BF16),
            jax.ShapeDtypeStruct(down_shape, BF16),
            jax.ShapeDtypeStruct(up_shape, BF16),
            jax.ShapeDtypeStruct(tail_shape, BF16),
        ),
        in_specs=[
            whole(*parts.shape), whole(tokens, model), whole(tokens, model), whole(model, model),
            whole(model), whole(model), whole(model), whole(model), whole(ff),
            pl.BlockSpec((model, model), lambda t: (0, t)),
            pl.BlockSpec((model, model), lambda t: (t, 0)),
        ],
        out_specs=(
            whole(tokens, model), whole(tokens, model), anywhere, anywhere, anywhere, anywhere,
            anywhere,
        ),
        scratch_shapes=[
            pltpu.VMEM((tokens, model), BF16),
            pltpu.VMEM((tokens, model), F32),
            pltpu.VMEM((tokens, model), BF16),
            pltpu.VMEM((model, tokens), BF16),
            pltpu.VMEM((tokens, model), F32),
            pltpu.VMEM((tokens, model), F32),
            pltpu.VMEM((steps, tokens, model), BF16),
            pltpu.VMEM((steps, tokens, model), BF16),
            pltpu.VMEM((8, model), F32),
            pltpu.VMEM((1, ff), F32),
            pltpu.VMEM(down_shape, BF16),
            pltpu.VMEM(up_shape, BF16),
            pltpu.VMEM(tail_shape, BF16),
            pltpu.VMEM(parts.shape, BF16),
            pltpu.VMEM((3,) + parts.shape[2:], BF16),
            pltpu.SemaphoreType.DMA((3,)),
            pltpu.SemaphoreType.DMA((3,)),
            pltpu.SemaphoreType.DMA((5,)),
        ],
        compiler_params=pltpu.CompilerParams(
            vmem_limit_bytes=VMEM, collective_id=3, has_side_effects=True
        ),
        cost_estimate=pl.CostEstimate(
            flops=26_000_000_000, bytes_accessed=30_000_000, transcendentals=0
        ),
        name="block_layer",
    )(parts, hidden, grad, out_w, out_b, gain, shift, down_b, up_b, up, down)
    if not direct:
        fit = lambda a: jnp.pad(a, ((0, 0), (0, aligned(a.shape[1]) - a.shape[1]), (0, 0)))
        down_grad = fit(down_grad.reshape(devices, share, model))
        up_grad = up_grad.reshape(devices, small, ff // model, model).transpose(0, 2, 1, 3)
        up_grad = fit(up_grad.reshape(devices, ff // model * small, model))
    return layer_out, resid_grad, grads, first, down_grad, up_grad, tail


def attend_back_kernel(
    dp_size, split_up, x_ref, grads_ref, first_ref, weight, draws_ref, hot_ref, proj, state_ref, mixed_ref, den_ref,
    soft_ref, phi_q_ref, phi_k_ref, down_any, up_any, tail_any,
    attn_out, ring_out, proj_out,
    grad_scr, num_scr, value_scr, score_scr, exact_scr, proj_scr,
    grad_land, near_send, near_land, far_keep, far_send, far_land,
    mine, met, ring_land, cross_land, up_mine, up_met, up_cross, up_land,
    weight_acc, own_send, pair_land, own_mid, own_land, part_send, part_land,
    grad_sems, near_sems, far_sems, mine_sem, met_sems, ring_sems, cross_sems, pair_sems, own_sems,
    part_sems, up_mine_sem, up_met_sems, up_cross_sems, up_ring_sems,
):
    s, h = pl.program_id(0), pl.program_id(1)
    seqs, heads = pl.num_programs(0), pl.num_programs(1)
    rows, model = x_ref.shape[1], x_ref.shape[2]
    head_count = proj_scr.shape[0] // (3 * HD)
    width = head_count * HD
    total = GROUP * rows
    root = 1.0 / math.sqrt(HD)
    own, me = lax.axis_index("feat"), lax.axis_index("dp")
    own_x, own_core = own // 2, own % 2
    near, across = {"feat": partner(own, 1)}, {"feat": partner(own, 2)}
    last = (s == seqs - 1) & (h == heads - 1)

    def grad_copy(q, r):
        return remote(
            grads_ref.at[q, r], grad_land.at[q - 1, r - 1], grad_sems.at[0, q - 1, r - 1],
            grad_sems.at[1, q - 1, r - 1], {"feat": partner(own, r)},
        )

    def near_copy(q, i):
        return remote(
            near_send.at[i], near_land.at[q, i], near_sems.at[0, q, i], near_sems.at[1, q, i], near
        )

    def far_copy(q):
        return remote(far_send, far_land.at[q], far_sems.at[0, q], far_sems.at[1, q], across)

    odd = me % 2
    half = dp_size // 2
    spot = (1 - odd) * (me // 2) + odd * (dp_size - 1 - me // 2)

    def at_spot(p):
        p = lax.rem(p + dp_size, dp_size)
        upper = p // half
        return (1 - upper) * (2 * p) + upper * (2 * (dp_size - 1 - p) + 1)

    def chunk(k, way):
        return at_spot(spot - 1 - k) if way == 0 else at_spot(lax.rem(spot + 1 + k, dp_size))

    sources = (down_any, tail_any) if split_up else (down_any, up_any, tail_any)
    lengths = [ref.shape[1] for ref in sources]
    starts = [sum(lengths[:i]) for i in range(len(sources))]

    def owner(k, way, core):
        return chunk(k, way) * GROUP + 2 * way + core

    def mine_copy(k, way, i):
        return pltpu.make_async_copy(
            sources[i].at[owner(k, way, own_core)],
            mine.at[k, way, pl.ds(starts[i], lengths[i])],
            mine_sem.at[k, way, i],
        )

    def met_copy(k, way, i):
        return remote(
            sources[i].at[owner(k, way, 1 - own_core)],
            met.at[k, way, pl.ds(starts[i], lengths[i])],
            met_sems.at[0, k, way, i], met_sems.at[1, k, way, i], near,
        )

    def ring_copy(k, way):
        place = at_spot(spot + 1) if way == 0 else at_spot(spot - 1)
        return remote(
            mine.at[k, way], ring_land.at[k, way], ring_sems.at[0, k, way], ring_sems.at[1, k, way],
            {"dp": place},
        )

    def cross_copy():
        return remote(
            mine.at[dp_size - 1, 1 - own_x], cross_land, cross_sems.at[0], cross_sems.at[1], across
        )

    up_rows = up_mine.shape[3]

    def up_mine_copy(k, way, x):
        return pltpu.make_async_copy(
            up_any.at[chunk(k, way) * GROUP + 2 * x + own_core, pl.ds(way * up_rows, up_rows)],
            up_mine.at[k, way, x], up_mine_sem.at[k, way, x],
        )

    def up_met_copy(k, way, x):
        return remote(
            up_any.at[chunk(k, way) * GROUP + 2 * x + 1 - own_core, pl.ds(way * up_rows, up_rows)],
            up_met.at[k, way, x], up_met_sems.at[0, k, way, x], up_met_sems.at[1, k, way, x], near,
        )

    def up_cross_copy(k, way):
        return remote(
            up_mine.at[k, way, 1 - own_x], up_cross.at[k, way], up_cross_sems.at[0, k, way],
            up_cross_sems.at[1, k, way], across,
        )

    def up_ring_copy(k, way):
        place = at_spot(spot + 1) if way == 0 else at_spot(spot - 1)
        return remote(
            up_mine.at[k, way, own_x], up_land.at[k, way], up_ring_sems.at[0, k, way],
            up_ring_sems.at[1, k, way], {"dp": place},
        )

    def begin_pieces(k):
        for way in range(2):
            for i in range(len(sources)):
                met_copy(k, way, i).start()
                mine_copy(k, way, i).start()
            if split_up:
                for x in range(2):
                    up_met_copy(k, way, x).start()
                    up_mine_copy(k, way, x).start()

    def ring_step(k, carry):
        @pl.when(k + 2 < dp_size)
        def _():
            begin_pieces(k + 2)

        @pl.when(k < dp_size)
        def _():
            for way in range(2):
                for i in range(len(sources)):
                    mine_copy(k, way, i).wait()
                    met_copy(k, way, i).wait_recv()

                @pl.when(k == 0)
                def _():
                    base = mine[k, way].astype(F32) + met[k, way].astype(F32)
                    mine[k, way] = base.astype(BF16)

                @pl.when(k > 0)
                def _():
                    ring_copy(k - 1, way).wait_recv()
                    base = mine[k, way].astype(F32) + met[k, way].astype(F32)
                    base = base + ring_land[k - 1, way].astype(F32)
                    mine[k, way] = base.astype(BF16)

                @pl.when(k < dp_size - 1)
                def _():
                    ring_copy(k, way).start()

                if split_up:
                    for x in range(2):
                        up_mine_copy(k, way, x).wait()
                        up_met_copy(k, way, x).wait_recv()
                    base = up_mine[k, way].astype(F32) + up_met[k, way].astype(F32)
                    up_mine[k, way] = base.astype(BF16)
                    up_cross_copy(k, way).start()

            @pl.when(k == dp_size - 1)
            def _():
                cross_copy().start()

        @pl.when(k == dp_size)
        def _():
            cross_copy().wait_recv()
            ring_out[0 : mine.shape[2]] = mine[dp_size - 1, own_x].astype(F32) + cross_land[
                ...
            ].astype(F32)

        return carry

    def up_step(after, carry):
        k = after - 1

        @pl.when(k >= 0)
        def _():
            for way in range(2):
                up_cross_copy(k, way).wait_recv()
                base = up_mine[k, way, own_x].astype(F32) + up_cross[k, way].astype(F32)

                @pl.when(k == 0)
                def _():
                    up_mine[k, way, own_x] = base.astype(BF16)

                @pl.when(k > 0)
                def _():
                    up_ring_copy(k - 1, way).wait_recv()
                    up_mine[k, way, own_x] = (base + up_land[k - 1, way].astype(F32)).astype(BF16)

                @pl.when(k < dp_size - 1)
                def _():
                    up_ring_copy(k, way).start()

                @pl.when(k == dp_size - 1)
                def _():
                    first = mine.shape[2] + way * up_rows
                    ring_out[first : first + up_rows] = up_mine[k, way, own_x].astype(F32)

        return carry

    def ring_turn(body):
        turn = s * heads + h
        count = seqs * heads
        steps = dp_size + 1
        lax.fori_loop(turn * steps // count, (turn + 1) * steps // count, body, 0)

    parity, pair = me % 2, me // 2
    mate = me + 1 - 2 * parity

    def pair_copy(q):
        return remote(
            own_send.at[q, 1 - parity], pair_land.at[q], pair_sems.at[0, q], pair_sems.at[1, q],
            {"dp": mate},
        )

    def own_copy(q, k):
        to = lax.rem(pair + k, half)
        return remote(
            own_mid.at[q, to], own_land.at[q, k], own_sems.at[0, q, k], own_sems.at[1, q, k],
            {"dp": 2 * to + parity},
        )

    def begin_own(q):
        base = model // dp_size
        turned = weight_acc[pl.ds(pl.multiple_of(q * 3 * HD, 3 * HD), 3 * HD)].T
        fill = turned[model : model + own_send.shape[3] - base]
        for c in range(dp_size):
            own_send[q, c % 2, c // 2] = jnp.concatenate(
                [turned[c * base : (c + 1) * base], fill], axis=0
            ).astype(BF16)
        pair_copy(q).start()

    def relay_own(q):
        pair_copy(q).wait_recv()
        own_mid[q] = (own_send[q, parity].astype(F32) + pair_land[q].astype(F32)).astype(BF16)

        def start(k, carry):
            own_copy(q, k).start()
            return carry

        lax.fori_loop(1, half, start, 0)

    def part_copy(r):
        other = partner(own, r)
        return remote(
            part_send.at[other], part_land.at[r - 1], part_sems.at[0, r - 1],
            part_sems.at[1, r - 1], {"feat": other},
        )

    def seq_span(q):
        return pl.ds(pl.multiple_of(q * rows, rows), rows)

    def add_near(q):
        near_copy(q, 1).wait_recv()

        @pl.when(q > 0)
        def _():
            far_copy(q - 1).wait_send()

        far_send[...] = (far_keep[1] + near_land[q, 1].astype(F32)).astype(BF16)
        far_copy(q).start()
        near_copy(q, 0).wait_recv()
        attn_out[seq_span(q)] = far_keep[0] + near_land[q, 0].astype(F32)

    def finish(q):
        far_copy(q).wait_recv()
        span = seq_span(q)
        attn_out[span] = attn_out[span] + far_land[q].astype(F32)

    @pl.when((s == 0) & (h == 0))
    def _():
        barrier = pltpu.get_barrier_semaphore()
        for r in (1, 2, 3):
            pl.semaphore_signal(
                barrier, inc=1, device_id={"feat": partner(own, r)}, device_id_type=MESH
            )

        def greet(k, carry):
            pl.semaphore_signal(
                barrier, inc=1, device_id={"dp": lax.rem(me + k, dp_size)}, device_id_type=MESH
            )
            return carry

        lax.fori_loop(1, dp_size, greet, 0)
        pl.semaphore_wait(barrier, 3 + dp_size - 1)
        for q in range(1, near_land.shape[0]):
            for r in (2, 3, 1):
                grad_copy(q, r).start()
        for k in range(2):
            begin_pieces(k)
        weight_acc[...] = jnp.zeros_like(weight_acc)

    @pl.when(h == 0)
    def _():
        grad_scr[:, 0:rows] = grads_ref[s, 0].astype(F32).T

        @pl.when(s == 0)
        def _():
            for r in (1, 2, 3):
                grad_scr[:, r * rows : (r + 1) * rows] = first_ref[r - 1].astype(F32).T

        @pl.when(s > 0)
        def _():
            for r in (1, 2, 3):
                grad_copy(s, r).wait_recv()
                grad_scr[:, r * rows : (r + 1) * rows] = grad_land[s - 1, r - 1].astype(F32).T

    query = proj[head_rows(h, 0, head_count)]
    key = proj[head_rows(h, 1, head_count)]
    value = proj[head_rows(h, 2, head_count)]
    draws = draws_ref[...]
    draws_ext = jnp.concatenate([draws, jnp.ones((16, FEAT), BF16)], axis=0)
    hot = hot_ref[...]
    away_wide = away_marks(hot)
    away = away_wide.astype(BF16)
    inverse = 1.0 / den_ref[0:1]
    head_grad = grad_scr[pl.ds(pl.multiple_of(h * HD, HD), HD)]
    grad_num = (head_grad * inverse).astype(BF16)
    grad_den = -jnp.sum(head_grad * mixed_ref[...], axis=0, keepdims=True) * inverse
    den_rows = jnp.broadcast_to(grad_den, (16, total)).astype(BF16)
    spread_grad = jnp.concatenate(spread(grad_num, hot) + [den_rows * hot], axis=0)
    spread_value = jnp.concatenate(spread(value, away) + [away], axis=0)

    phi_q = phi_q_ref[...]
    state_grad = mat_nt(spread_grad, phi_q).astype(BF16)
    scaled_q = mat_tn(state_ref[...], spread_grad) * phi_q.astype(F32)
    back_q = mat(draws_ext, scaled_q.astype(BF16))
    query_grad = back_q[0:HD] - query.astype(F32) * (back_q[HD : HD + 1] * root)

    phi_k = phi_k_ref[...]
    scaled_k = mat_tn(state_grad, spread_value) * phi_k.astype(F32)
    back_k = mat(draws_ext, scaled_k.astype(BF16))
    key_grad = back_k[0:HD] - key.astype(F32) * (back_k[HD : HD + 1] * root)
    value_grad = pick(mat(state_grad[0 : NBUCK * HD], phi_k), away_wide)

    ring_turn(ring_step)
    one = (lax.broadcasted_iota(jnp.int32, hot.shape, 0) < 1).astype(F32).astype(BF16)
    num_scr[...] = jnp.concatenate([grad_num, den_rows], axis=0)
    value_scr[...] = jnp.concatenate([value, one], axis=0).astype(F32).T.astype(BF16)

    for c in range(total // CHUNK):
        cols = slice(c * CHUNK, (c + 1) * CHUNK)
        score = mat(value_scr[...], num_scr[:, cols]) * soft_ref[:, cols].astype(F32)
        score = score.astype(BF16)
        score_scr[:, cols] = score
        exact_scr[:, cols] = mat(proj[head_rows(h, 1, head_count)], score)
    query_grad = query_grad + exact_scr[...] * root
    key_grad = key_grad + mat_nt(query, score_scr[...]) * root
    value_grad = value_grad + mat_nt(grad_num, soft_ref[...])
    wide_grad = jnp.concatenate([query_grad, key_grad, value_grad], axis=0)
    low_grad = wide_grad.astype(BF16)
    for kind in range(3):
        proj_scr[head_rows(h, kind, head_count)] = low_grad[kind * HD : (kind + 1) * HD]
    weight_grad = mat(low_grad[:, 0:rows], x_ref[0])
    for r in (1, 2, 3):
        weight_grad = weight_grad + mat(low_grad[:, r * rows : (r + 1) * rows], x_ref[r])
    span = pl.ds(pl.multiple_of(h * 3 * HD, 3 * HD), 3 * HD)
    weight_acc[span, 0:model] += weight_grad
    weight_acc[span, model:] += jnp.broadcast_to(
        jnp.sum(wide_grad, axis=1, keepdims=True), (3 * HD, 128)
    )

    @pl.when(s == seqs - 1)
    def _():
        begin_own(h)

        @pl.when(h > 0)
        def _():
            relay_own(h - 1)

    @pl.when((s > 0) & (h == 0))
    def _():
        add_near(s - 1)

    @pl.when(h == heads - 1)
    def _():
        @pl.when(s > 0)
        def _():
            for i in range(2):
                near_copy(s - 1, i).wait_send()

        for r in (3, 1, 2, 0):
            term = mat_tn(proj_scr[:, r * rows : (r + 1) * rows], weight[...])
            if r % 2:
                near_send[r // 2] = term.astype(BF16)
                near_copy(s, r // 2).start()
            else:
                far_keep[r // 2] = term

    if split_up:
        ring_turn(up_step)

    @pl.when(last)
    def _():
        add_near(s)
        relay_own(h)
        for q in range(near_land.shape[0] - 1):
            finish(q)

        sums = []
        for q in range(head_count):

            def arrive(k, carry):
                own_copy(q, k).wait_recv()
                return carry + own_land[q, k].astype(F32)

            sums.append(lax.fori_loop(1, half, arrive, own_mid[q, pair].astype(F32)))
        joined = jnp.concatenate(sums, axis=1)
        base = model // dp_size
        small = base // GROUP
        fill = jnp.broadcast_to(
            joined[base : base + 1], (part_send.shape[1] - small, joined.shape[1])
        )
        for a in range(GROUP):
            part_send[a] = jnp.concatenate(
                [joined[a * small : (a + 1) * small], fill], axis=0
            ).astype(BF16)
        for r in (2, 3, 1):
            part_copy(r).start()
        finish(s)
        proj_out[own] = part_send[own].astype(F32)
        for r in (1, 2, 3):
            part_copy(r).wait_recv()
            proj_out[partner(own, r)] = part_land[r - 1].astype(F32)

        for i in range(2):
            near_copy(s, i).wait_send()
        far_copy(s).wait_send()
        for r in (1, 2, 3):
            part_copy(r).wait_send()
        cross_copy().wait_send()
        for q in range(1, near_land.shape[0]):
            for r in (1, 2, 3):
                grad_copy(q, r).wait_send()

        def leave(k, carry):
            for way in range(2):
                for i in range(len(sources)):
                    met_copy(k, way, i).wait_send()
                if split_up:
                    for x in range(2):
                        up_met_copy(k, way, x).wait_send()
                    up_cross_copy(k, way).wait_send()
            return carry

        lax.fori_loop(0, dp_size, leave, 0)

        def leave_ring(k, carry):
            for way in range(2):
                ring_copy(k, way).wait_send()
                if split_up:
                    up_ring_copy(k, way).wait_send()
            return carry

        lax.fori_loop(0, dp_size - 1, leave_ring, 0)
        for q in range(head_count):
            pair_copy(q).wait_send()

            def leave_own(k, carry):
                own_copy(q, k).wait_send()
                return carry

            lax.fori_loop(1, half, leave_own, 0)


def attend_back(
    dp_size, parts, grads, first, weight, draws, hot, proj, state, mixed, den, soft, phi_q, phi_k,
    down_grad, up_grad, tail,
):
    seqs, _, rows, model = parts.shape
    heads = draws.shape[0]
    width = heads * HD
    total = GROUP * rows
    n = dp_size
    up_rows = up_grad.shape[1] // 2
    split_up = up_rows % 16 == 0
    all_rows = down_grad.shape[1] + up_grad.shape[1] + tail.shape[1]
    ring_rows = all_rows - 2 * up_rows if split_up else all_rows
    if not split_up:
        up_rows = 16
    up_n = n if split_up else 1
    own_rows = aligned(model // n + 1)
    part_rows = aligned(model // (n * GROUP) + 1)
    single = pl.Buffered(1)
    whole = lambda *shape: pl.BlockSpec(
        shape, lambda s, h: (0,) * len(shape), pipeline_mode=single
    )
    mode = single if n > 16 else None
    by_seq = lambda *shape: pl.BlockSpec(
        (None,) + shape, lambda s, h: (s,) + (0,) * len(shape), pipeline_mode=mode
    )
    by_head = lambda *shape: pl.BlockSpec(
        (None, None) + shape, lambda s, h: (s, h) + (0,) * len(shape), pipeline_mode=mode
    )
    anywhere = pl.BlockSpec(memory_space=pl.ANY)
    dma = pltpu.SemaphoreType.DMA
    results = pl.pallas_call(
        lambda *refs: attend_back_kernel(dp_size, split_up, *refs),
        grid=(seqs, heads),
        out_shape=(
            jax.ShapeDtypeStruct((seqs * rows, model), F32),
            jax.ShapeDtypeStruct((all_rows, model), F32),
            jax.ShapeDtypeStruct((GROUP, part_rows, 3 * width), F32),
        ),
        in_specs=[
            by_seq(GROUP, rows, model), whole(*grads.shape), whole(*first.shape),
            whole(3 * width, model),
            pl.BlockSpec((None, HD, FEAT), lambda s, h: (h, 0, 0)),
            by_seq(16, total), by_seq(3 * width, total), by_head(STATES, FEAT), by_head(HD, total),
            by_head(8, total), by_head(total, total), by_head(FEAT, total), by_head(FEAT, total),
            anywhere, anywhere, anywhere,
        ],
        out_specs=(
            whole(seqs * rows, model), whole(all_rows, model), whole(GROUP, part_rows, 3 * width),
        ),
        scratch_shapes=[
            pltpu.VMEM((width, total), F32),
            pltpu.VMEM((HD + 16, total), BF16),
            pltpu.VMEM((total, HD + 16), BF16),
            pltpu.VMEM((total, total), BF16),
            pltpu.VMEM((HD, total), F32),
            pltpu.VMEM((3 * width, total), BF16),
            pltpu.VMEM((seqs - 1, 3, rows, width), BF16),
            pltpu.VMEM((2, rows, model), BF16),
            pltpu.VMEM((seqs, 2, rows, model), BF16),
            pltpu.VMEM((2, rows, model), F32),
            pltpu.VMEM((rows, model), BF16),
            pltpu.VMEM((seqs, rows, model), BF16),
            pltpu.VMEM((n, 2, ring_rows, model), BF16),
            pltpu.VMEM((n, 2, ring_rows, model), BF16),
            pltpu.VMEM((n - 1, 2, ring_rows, model), BF16),
            pltpu.VMEM((ring_rows, model), BF16),
            pltpu.VMEM((up_n, 2, 2, up_rows, model), BF16),
            pltpu.VMEM((up_n, 2, 2, up_rows, model), BF16),
            pltpu.VMEM((up_n, 2, up_rows, model), BF16),
            pltpu.VMEM((up_n, 2, up_rows, model), BF16),
            pltpu.VMEM((3 * width, model + 128), F32),
            pltpu.VMEM((heads, 2, n // 2, own_rows, 3 * HD), BF16),
            pltpu.VMEM((heads, n // 2, own_rows, 3 * HD), BF16),
            pltpu.VMEM((heads, n // 2, own_rows, 3 * HD), BF16),
            pltpu.VMEM((heads, n // 2, own_rows, 3 * HD), BF16),
            pltpu.VMEM((GROUP, part_rows, 3 * width), BF16),
            pltpu.VMEM((3, part_rows, 3 * width), BF16),
            dma((2, seqs - 1, 3)),
            dma((2, seqs, 2)),
            dma((2, seqs)),
            dma((n, 2, 3)),
            dma((2, n, 2, 3)),
            dma((2, n - 1, 2)),
            dma((2,)),
            dma((2, heads)),
            dma((2, heads, n // 2)),
            dma((2, 3)),
            dma((up_n, 2, 2)),
            dma((2, up_n, 2, 2)),
            dma((2, up_n, 2)),
            dma((2, up_n, 2)),
        ],
        compiler_params=pltpu.CompilerParams(
            vmem_limit_bytes=VMEM + (3 * 1024 * 1024 if n > 16 else 0), collective_id=2, has_side_effects=True
        ),
        cost_estimate=pl.CostEstimate(
            flops=48_000_000_000, bytes_accessed=40_000_000, transcendentals=0
        ),
        name="attend_back",
    )(
        parts, grads, first, weight, draws, hot, proj, state, mixed, den, soft, phi_q, phi_k,
        down_grad, up_grad, tail,
    )
    low = down_grad.shape[1]
    starts = (ring_rows, low) if split_up else (low, low + up_grad.shape[1])
    return results + (starts,)


def finish_kernel(
    starts, heads, attn_grad, resid_grad, hidden, sums, proj_sums, weight_rows, gain_ref, shift_ref,
    input_out, norm1_gain_out, norm1_bias_out, qkv_out, qkv_bias_out, out_out, out_bias_out,
    norm2_gain_out, norm2_bias_out, up_out, up_bias_out, down_out, down_bias_out,
):
    gain, shift = as_row(gain_ref), as_row(shift_ref)
    normed, scale = row_stats(hidden[...].astype(F32))
    input_out[...] = resid_grad[...] + norm_back(attn_grad[...] * gain, normed, scale)

    @pl.when(pl.program_id(0) == 0)
    def _():
        index = lax.axis_index("dp") * GROUP + lax.axis_index("feat")
        small, model = out_out.shape
        share = down_out.shape[0]
        ff = up_out.shape[1]

        def own(row, size):
            length = row.shape[1]
            wide = jnp.broadcast_to(row, (8, length))
            back = lax.rem(length - lax.rem(index * size, length), length)
            return pltpu.roll(wide, back, 1)[0:1, 0:size]

        down_out[...] = sums[0:share]
        first = starts[0]
        up_out[...] = jnp.concatenate(
            [sums[first + i * small : first + (i + 1) * small] for i in range(ff // model)], axis=1
        )
        first = starts[1]
        out_out[...] = sums[first : first + small]
        totals = first + small
        for i, out in enumerate((down_bias_out, out_bias_out, norm2_gain_out, norm2_bias_out)):
            out[...] = own(sums[totals + i : totals + i + 1], small).reshape(small)
        per_row = model // share
        level = index // per_row
        row = jnp.zeros((1, model), F32)
        for i in range(ff // model):
            row = jnp.where(level == i, sums[totals + 4 + i : totals + 5 + i], row)
        up_bias_out[...] = own(row, share).reshape(share)

        pieces = []
        for kind in range(3):
            for f in range(GROUP):
                for h in range(heads):
                    lanes = slice((h * 3 + kind) * HD, (h * 3 + kind + 1) * HD)
                    pieces.append(proj_sums[f, 0 : small + 1, lanes])
        grid = jnp.concatenate(pieces, axis=1)
        weight_sum, bias_sum = grid[0:small], grid[small : small + 1]
        qkv_out[...] = weight_sum
        qkv_bias_out[...] = own(bias_sum, 3 * small).reshape(3 * small)
        wide = weight_rows[...].astype(F32)

        def to_row(column):
            column = jnp.concatenate(
                [column, jnp.zeros((-small % 128, 1), F32)], axis=0
            )
            return jnp.broadcast_to(column, (column.shape[0], 128)).T[0:1, 0:small]

        bias_grad = to_row(jnp.sum(wide * bias_sum, axis=1, keepdims=True))
        gain_grad = to_row(jnp.sum(wide * weight_sum, axis=1, keepdims=True))
        norm1_bias_out[...] = bias_grad.reshape(small)
        gain_grad = (gain_grad - own(shift, small) * bias_grad) / own(gain, small)
        norm1_gain_out[...] = gain_grad.reshape(small)


def finish_all(
    attn_grad, resid_grad, hidden, sums, proj_sums, weight_rows, gain, shift, starts, devices, ff,
    heads,
):
    seqs, rows, model = hidden.shape
    small, share = model // devices, ff // devices
    whole = lambda *shape: pl.BlockSpec(shape, lambda s: (0,) * len(shape))
    by_seq = pl.BlockSpec((rows, model), lambda s: (s, 0))
    shapes = (
        (small,), (small,), (small, 3 * model), (3 * small,), (small, model), (small,), (small,),
        (small,), (small, ff), (share,), (share, model), (small,),
    )
    return pl.pallas_call(
        lambda *refs: finish_kernel(starts, heads, *refs),
        grid=(seqs,),
        out_shape=(jax.ShapeDtypeStruct((seqs * rows, model), F32),)
        + tuple(jax.ShapeDtypeStruct(shape, F32) for shape in shapes),
        in_specs=[
            by_seq, by_seq, pl.BlockSpec((None, rows, model), lambda s: (s, 0, 0)),
            whole(*sums.shape), whole(*proj_sums.shape), whole(*weight_rows.shape), whole(model),
            whole(model),
        ],
        out_specs=(by_seq,) + tuple(whole(*shape) for shape in shapes),
        compiler_params=pltpu.CompilerParams(vmem_limit_bytes=VMEM),
        name="finish_all",
    )(attn_grad, resid_grad, hidden, sums, proj_sums, weight_rows, gain, shift)


def per_device(
    hidden_in, norm1_gain, norm1_bias, qkv_weight, qkv_bias, feature_draws, out_weight, out_bias,
    norm2_gain, norm2_bias, up_weight, up_bias, down_weight, down_bias, block_bucket, out_grad,
):
    seqs, rows, model = hidden_in.shape
    ff = up_weight.shape[1]
    dp_size = lax.axis_size("dp")
    devices = dp_size * GROUP
    small = model // devices
    heads = feature_draws.shape[0] // GROUP
    flat = (seqs * rows, model)

    (
        parts, mixed_parts, proj, state, mixed, den, hot, own_weight, own_draws, soft, phi_q, phi_k,
    ) = attend(
        block_bucket, hidden_in, norm1_gain, norm1_bias, qkv_bias, qkv_weight, feature_draws
    )
    layer_out, resid_grad, grads, first, down_grad, up_grad, tail = block_layer(
        mixed_parts, hidden_in.reshape(flat), out_grad.reshape(flat), out_weight, out_bias,
        norm2_gain, norm2_bias, down_bias, up_bias, up_weight, down_weight, devices,
    )
    attn_grad, sums, proj_sums, starts = attend_back(
        dp_size, parts, grads, first, own_weight, own_draws, hot, proj, state, mixed, den, soft,
        phi_q, phi_k, down_grad, up_grad, tail,
    )
    index = lax.axis_index("dp") * GROUP + lax.axis_index("feat")
    weight_rows = lax.dynamic_slice_in_dim(qkv_weight, index * small, small, 0)
    (
        input_grad, norm1_gain_sum, norm1_bias_sum, qkv_weight_sum, qkv_bias_sum, out_weight_sum,
        out_bias_sum, norm2_gain_sum, norm2_bias_sum, up_sum, up_bias_sum, down_sum, down_bias_sum,
    ) = finish_all(
        attn_grad, resid_grad, hidden_in, sums, proj_sums, weight_rows, norm1_gain, norm1_bias,
        starts, devices, ff, heads,
    )
    return (
        layer_out.reshape(hidden_in.shape), input_grad.reshape(hidden_in.shape), norm1_gain_sum,
        norm1_bias_sum, qkv_weight_sum, qkv_bias_sum, out_weight_sum, out_bias_sum, norm2_gain_sum,
        norm2_bias_sum, up_sum, up_bias_sum, down_sum, down_bias_sum,
    )


def solution(mesh):
    both = ("dp", "feat")
    rows = P("dp", "feat", None)
    in_specs = (
        rows, P(), P(), P(), P(), P(None, None, "feat"), P(), P(), P(), P(), P(), P(), P(), P(),
        P("dp", None, None), rows,
    )
    out_specs = (
        rows, rows, P(both), P(both), P(both, None), P(both), P(both, None), P(both), P(both),
        P(both), P(both, None), P(both), P(both, None), P(both),
    )
    return jax.shard_map(
        per_device, mesh=mesh, in_specs=in_specs, out_specs=out_specs, check_vma=False
    )
```

```python
import math

import jax
import jax.numpy as jnp
from jax import lax
from jax.experimental import pallas as pl
from jax.experimental.pallas import tpu as pltpu
from jax.sharding import PartitionSpec as P

HD = 64
FEAT = 256
BLOCK = 64
NBUCK = 4
GROUP = 4
CHUNK = 256
STATES = NBUCK * HD + 16
FAR = 16384.0
VMEM = 60 * 1024 * 1024

F32 = jnp.float32
BF16 = jnp.bfloat16
MESH = pl.DeviceIdType.MESH


def mat(left, right):
    return jnp.dot(left, right, preferred_element_type=F32)


def mat_nt(left, right):
    return lax.dot_general(left, right, (((1,), (1,)), ((), ())), preferred_element_type=F32)


def mat_tn(left, right):
    return lax.dot_general(left, right, (((0,), (0,)), ((), ())), preferred_element_type=F32)


def row_stats(values):
    row_mean = jnp.mean(values, axis=-1, keepdims=True)
    centered = values - row_mean
    scale = lax.rsqrt(jnp.mean(centered * centered, axis=-1, keepdims=True) + 1e-05)
    return (centered * scale, scale)


def norm_back(cotangent, normed, scale):
    mean_one = jnp.mean(cotangent, axis=-1, keepdims=True)
    mean_two = jnp.mean(cotangent * normed, axis=-1, keepdims=True)
    return scale * (cotangent - mean_one - normed * mean_two)


def features(vectors, draws):
    wide = vectors.astype(F32)
    square = jnp.sum(wide * wide, axis=0, keepdims=True) * (0.5 / math.sqrt(HD))
    return jnp.exp(mat_tn(draws, vectors) - (square + 0.5 * math.log(FEAT)))


def spread(rows, marks):
    return [rows * marks[u : u + 1] for u in range(NBUCK)]


def pick(stacked, marks):
    total = stacked[0:HD] * marks[0:1]
    for u in range(1, NBUCK):
        total = total + stacked[u * HD : (u + 1) * HD] * marks[u : u + 1]
    return total


def away_marks(hot):
    live = (lax.broadcasted_iota(jnp.int32, hot.shape, 0) < NBUCK).astype(F32)
    return live - hot.astype(F32)


def partner(own, r):
    x, core = own // 2, own % 2
    if r & 2:
        x = 1 - x
    if r & 1:
        core = 1 - core
    return 2 * x + core


def as_row(ref):
    return ref[...].reshape(1, ref.shape[0])


def aligned(count):
    return -(-count // 16) * 16


def remote(src, dst, send, recv, place):
    return pltpu.make_async_remote_copy(
        src_ref=src, dst_ref=dst, send_sem=send, recv_sem=recv, device_id=place, device_id_type=MESH
    )


def head_rows(h, kind, heads):
    return pl.ds(pl.multiple_of((kind * heads + h) * HD, HD), HD)


def attend_kernel(
    bucket, hidden, gain_ref, shift_ref, bias_ref, weight_any, draws_in,
    parts_any, mix_any, proj_out, state_out, mixed_out, den_out, hot_out, weight_out, draws_out,
    soft_out, phi_q_out, phi_k_out,
    parts, mix_land, mix_send, raw, bias_row, bias_scr, draws_land,
    query_scr, key_scr, value_scr, low_scr, gather_scr,
    raw_sem, part_send, part_recv, draw_send, draw_recv, mix_send_sem, mix_recv_sem, out_sem,
):
    s, h = pl.program_id(0), pl.program_id(1)
    seqs, rows, model = hidden.shape
    heads = draws_out.shape[0]
    total = GROUP * rows
    width = heads * HD
    own = lax.axis_index("feat")
    near, across = {"feat": partner(own, 1)}, {"feat": partner(own, 2)}

    def part_copy(q, kind):
        src, dst, place = ((0, 1, near), (0, 2, across), (2, 3, near))[kind]
        return remote(
            parts.at[q, src], parts.at[q, dst], part_send.at[q, kind], part_recv.at[q, kind], place
        )

    def draw_copy(r):
        other = partner(own, r)
        return remote(
            draws_in.at[pl.ds(other * heads, heads)], draws_land.at[r - 1],
            draw_send.at[r - 1], draw_recv.at[r - 1], {"feat": other},
        )

    def mix_copy(q, r):
        return remote(
            mix_send.at[q, r], mix_land.at[q, r], mix_send_sem.at[q, r - 1],
            mix_recv_sem.at[q, r - 1], {"feat": partner(own, r)},
        )

    def raw_copy(j):
        cols = pl.ds(pl.multiple_of(j * model + (own // 2) * 2 * width, 2 * width), 2 * width)
        return pltpu.make_async_copy(weight_any.at[:, cols], raw.at[j], raw_sem.at[j])

    def out_copy(q):
        return pltpu.make_async_copy(parts.at[q], parts_any.at[q], out_sem.at[q])

    @pl.when((s == 0) & (h == 0))
    def _():
        for j in range(3):
            raw_copy(j).start()
        barrier = pltpu.get_barrier_semaphore()
        for r in (1, 2, 3):
            pl.semaphore_signal(
                barrier, inc=1, device_id={"feat": partner(own, r)}, device_id_type=MESH
            )
        gain, shift = as_row(gain_ref), as_row(shift_ref)
        first = row_stats(hidden[0].astype(F32))[0] * gain + shift
        parts[0, 0] = first.astype(BF16)
        pl.semaphore_wait(barrier, 3)
        part_copy(0, 1).start()
        part_copy(0, 0).start()
        for r in (1, 2, 3):
            draw_copy(r).start()
        for q in range(1, seqs):
            normed = row_stats(hidden[q].astype(F32))[0] * gain + shift
            parts[q, 0] = normed.astype(BF16)
            part_copy(q, 1).start()
            part_copy(q, 0).start()
        core = own % 2
        bias_row[...] = as_row(bias_ref)
        for j in range(3):
            raw_copy(j).wait()
            piece = raw[j].astype(F32)
            piece = jnp.where(core == 0, piece[:, 0:width], piece[:, width:])
            weight_out[j * width : (j + 1) * width] = piece.T.astype(BF16)
            cols = pl.ds(pl.multiple_of(j * model + (own // 2) * 2 * width, 2 * width), 2 * width)
            pair = jnp.broadcast_to(bias_row[:, cols], (128, 2 * width))
            pair = jnp.where(core == 0, pair[:, 0:width], pair[:, width:])
            bias_scr[j * width : (j + 1) * width] = pair.T
        part_copy(0, 1).wait_recv()
        part_copy(0, 2).start()
        for r in (1, 2, 3):
            draw_copy(r).wait_recv()
        mine = draws_in[pl.ds(own * heads, heads)]
        draws_out[...] = jnp.concatenate(
            [mine] + [draws_land[r - 1] for r in (1, 2, 3)], axis=2
        )

    @pl.when(h == 0)
    def _():
        per = rows // BLOCK
        lanes = lax.broadcasted_iota(jnp.int32, (16, total), 1) // BLOCK
        level = lax.broadcasted_iota(jnp.int32, (16, total), 0)
        ids = jnp.full((16, total), -1, jnp.int32)
        for r in range(GROUP):
            for i in range(per):
                ids = jnp.where(
                    lanes == r * per + i, bucket[s, partner(own, r) * per + i, 0], ids
                )
        hot_out[...] = (ids == level).astype(F32).astype(BF16)

        def project(r):
            cols = slice(r * rows, (r + 1) * rows)
            piece = mat_nt(weight_out[...], parts[s, r]) + bias_scr[:, 0:1]
            proj_out[:, cols] = piece.astype(BF16)

        project(0)
        part_copy(s, 0).wait_recv()
        project(1)
        project(2)
        part_copy(s, 2).wait_recv()
        project(3)
        out_copy(s).start()

    query = proj_out[head_rows(h, 0, heads)]
    key = proj_out[head_rows(h, 1, heads)]
    value = proj_out[head_rows(h, 2, heads)]
    draws = draws_out[h]
    hot = hot_out[...]
    hot_wide = hot.astype(F32)
    away = away_marks(hot).astype(BF16)
    phi_q = features(query, draws).astype(BF16)
    phi_k = features(key, draws).astype(BF16)
    phi_q_out[...] = phi_q
    phi_k_out[...] = phi_k
    spread_value = jnp.concatenate(spread(value, away) + [away], axis=0)
    state = mat_nt(spread_value, phi_k).astype(BF16)
    state_out[...] = state
    low = mat(state, phi_q)
    low_scr[0:HD] = pick(low, hot_wide)
    low_den = jnp.sum(low[NBUCK * HD :] * hot_wide, axis=0, keepdims=True)
    low_scr[HD : HD + 8] = jnp.broadcast_to(low_den, (8, total))
    query_scr[...] = jnp.concatenate([query * (1.0 / math.sqrt(HD)), hot], axis=0).astype(BF16)
    key_scr[...] = jnp.concatenate([key, away * -FAR], axis=0).astype(F32).T.astype(BF16)
    value_scr[0:HD] = value
    value_scr[HD:] = jnp.ones((16, total), BF16)

    score = mat(key_scr[...], query_scr[:, 0:CHUNK])
    for c in range(total // CHUNK):
        cols = slice(c * CHUNK, (c + 1) * CHUNK)
        ahead = slice((c + 1) * CHUNK, (c + 2) * CHUNK)
        later = mat(key_scr[...], query_scr[:, ahead]) if ahead.stop <= total else None
        weights = jnp.exp(score).astype(BF16)
        score = later
        soft_out[:, cols] = weights
        exact = mat(value_scr[...], weights)
        den = low_scr[HD : HD + 8, cols] + exact[HD : HD + 8]
        mixed = (low_scr[0:HD, cols] + exact[0:HD]) / den[0:1]
        mixed_out[:, cols] = mixed
        den_out[:, cols] = den
        gather_scr[pl.ds(pl.multiple_of(h * HD, HD), HD), cols] = mixed

    @pl.when((h == heads - 2) & (s < seqs - 1))
    def _():
        part_copy(s + 1, 1).wait_recv()
        part_copy(s + 1, 2).start()

    @pl.when(h == heads - 1)
    def _():
        for r in range(GROUP):
            piece = gather_scr[:, r * rows : (r + 1) * rows].T.astype(BF16)
            if r == 0:
                mix_land[s, 0] = piece
            else:
                mix_send[s, r] = piece
                mix_copy(s, r).start()

    @pl.when((s == seqs - 1) & (h == heads - 1))
    def _():
        for q in range(seqs):
            for r in (1, 2, 3):
                mix_copy(q, r).wait_recv()
        done = pltpu.make_async_copy(mix_land, mix_any, out_sem.at[seqs])
        done.start()
        for q in range(seqs):
            for kind in range(3):
                part_copy(q, kind).wait_send()
            for r in (1, 2, 3):
                mix_copy(q, r).wait_send()
            out_copy(q).wait()
        for r in (1, 2, 3):
            draw_copy(r).wait_send()
        done.wait()


def attend(bucket, hidden, gain, shift, bias, weight, draws):
    seqs, rows, model = hidden.shape
    heads = draws.shape[0] // GROUP
    width = heads * HD
    total = GROUP * rows
    whole = lambda *shape: pl.BlockSpec(shape, lambda s, h: (0,) * len(shape))
    by_seq = lambda *shape: pl.BlockSpec((None,) + shape, lambda s, h: (s,) + (0,) * len(shape))
    by_head = lambda *shape: pl.BlockSpec(
        (None, None) + shape, lambda s, h: (s, h) + (0,) * len(shape)
    )
    anywhere = pl.BlockSpec(memory_space=pl.ANY)
    return pl.pallas_call(
        attend_kernel,
        grid=(seqs, heads),
        out_shape=(
            jax.ShapeDtypeStruct((seqs, GROUP, rows, model), BF16),
            jax.ShapeDtypeStruct((seqs, GROUP, rows, width), BF16),
            jax.ShapeDtypeStruct((seqs, 3 * width, total), BF16),
            jax.ShapeDtypeStruct((seqs, heads, STATES, FEAT), BF16),
            jax.ShapeDtypeStruct((seqs, heads, HD, total), F32),
            jax.ShapeDtypeStruct((seqs, heads, 8, total), F32),
            jax.ShapeDtypeStruct((seqs, 16, total), BF16),
            jax.ShapeDtypeStruct((3 * width, model), BF16),
            jax.ShapeDtypeStruct((heads, HD, FEAT), BF16),
            jax.ShapeDtypeStruct((seqs, heads, total, total), BF16),
            jax.ShapeDtypeStruct((seqs, heads, FEAT, total), BF16),
            jax.ShapeDtypeStruct((seqs, heads, FEAT, total), BF16),
        ),
        in_specs=[
            pl.BlockSpec(memory_space=pltpu.SMEM),
            whole(seqs, rows, model), whole(model), whole(model), whole(3 * model), anywhere,
            whole(*draws.shape),
        ],
        out_specs=(
            anywhere, anywhere, by_seq(3 * width, total), by_head(STATES, FEAT), by_head(HD, total),
            by_head(8, total), by_seq(16, total), whole(3 * width, model), whole(heads, HD, FEAT),
            by_head(total, total), by_head(FEAT, total), by_head(FEAT, total),
        ),
        scratch_shapes=[
            pltpu.VMEM((seqs, GROUP, rows, model), BF16),
            pltpu.VMEM((seqs, GROUP, rows, width), BF16),
            pltpu.VMEM((seqs, GROUP, rows, width), BF16),
            pltpu.VMEM((3, model, 2 * width), BF16),
            pltpu.VMEM((1, 3 * model), F32),
            pltpu.VMEM((3 * width, 128), F32),
            pltpu.VMEM((3, heads, HD, draws.shape[2]), BF16),
            pltpu.VMEM((HD + 16, total), BF16),
            pltpu.VMEM((total, HD + 16), BF16),
            pltpu.VMEM((HD + 16, total), BF16),
            pltpu.VMEM((HD + 8, total), F32),
            pltpu.VMEM((width, total), F32),
            pltpu.SemaphoreType.DMA((3,)),
            pltpu.SemaphoreType.DMA((seqs, 3)),
            pltpu.SemaphoreType.DMA((seqs, 3)),
            pltpu.SemaphoreType.DMA((3,)),
            pltpu.SemaphoreType.DMA((3,)),
            pltpu.SemaphoreType.DMA((seqs, 3)),
            pltpu.SemaphoreType.DMA((seqs, 3)),
            pltpu.SemaphoreType.DMA((seqs + 1,)),
        ],
        compiler_params=pltpu.CompilerParams(
            vmem_limit_bytes=VMEM, collective_id=1, has_side_effects=True
        ),
        cost_estimate=pl.CostEstimate(
            flops=24_000_000_000, bytes_accessed=20_000_000, transcendentals=0
        ),
        name="attend",
    )(bucket, hidden, gain, shift, bias, weight, draws)


def block_kernel(
    direct, parts_ref, hidden, grad, out_w, out_b, gain_ref, shift_ref, down_b, up_b, up, down,
    layer_out, resid_out, grads_any, first_any, slab_any, down_any, up_any, tail_any,
    mixed, resid_scr, in_scr, in_t, acc_out, acc_in, act_scr, pre_scr, vec_scr, bias_row,
    slab_vm, down_vm, up_vm, tail_vm, grads_vm, first_land, send_sem, recv_sem, out_sem,
):
    step = pl.program_id(0)
    model = hidden.shape[1]
    count = hidden.shape[0] // CHUNK
    tiles = act_scr.shape[0]
    spans = [slice(c * CHUNK, (c + 1) * CHUNK) for c in range(count)]
    owners = slab_vm.shape[0] if direct else tail_vm.shape[0]
    small = model // owners
    share = tiles * small
    own = lax.axis_index("feat")
    barrier = pltpu.get_barrier_semaphore()

    def swap_groups(pieces):
        pieces = [jnp.where(own % 2 == 1, pieces[r ^ 1], pieces[r]) for r in range(GROUP)]
        return [jnp.where(own // 2 == 1, pieces[r ^ 2], pieces[r]) for r in range(GROUP)]

    def grad_copy(r):
        return remote(
            grads_vm.at[0, r], first_land.at[r - 1], send_sem.at[r - 1], recv_sem.at[r - 1],
            {"feat": partner(own, r)},
        )

    def out_copy(i):
        pieces = [(down_vm, down_any), (up_vm, up_any), (tail_vm, tail_any)]
        if direct:
            cuts = (0, share, 2 * share, slab_vm.shape[1])
            pieces = [
                (slab_vm.at[:, pl.ds(low, high - low)], slab_any.at[:, pl.ds(low, high - low)])
                for low, high in zip(cuts, cuts[1:])
            ]
        src, dst = (
            *pieces, (grads_vm, grads_any), (first_land, first_any),
        )[i]
        return pltpu.make_async_copy(src, dst, out_sem.at[i])

    @pl.when(step == 0)
    def _():
        for r in (1, 2, 3):
            pl.semaphore_signal(
                barrier, inc=1, device_id={"feat": partner(own, r)}, device_id_type=MESH
            )
        for c, span in enumerate(spans):
            pieces = swap_groups([parts_ref[c, r] for r in range(GROUP)])
            mixed[span] = jnp.concatenate(pieces, axis=1)
            resid = hidden[span].astype(F32) + mat(mixed[span], out_w[...]) + as_row(out_b)
            resid_scr[span] = resid
            normed, _ = row_stats(resid)
            inner = normed * as_row(gain_ref) + as_row(shift_ref)
            in_scr[span] = inner.astype(BF16)
            in_t[:, span] = inner.T.astype(BF16)
        acc_out[...] = jnp.zeros_like(acc_out)
        acc_in[...] = jnp.zeros_like(acc_in)
        bias_row[...] = as_row(up_b)

    slope = math.sqrt(2.0 / math.pi)
    total = jnp.zeros((1, model), F32)
    up_bias = bias_row[:, pl.ds(pl.multiple_of(step * model, model), model)]
    for span in spans:
        pre = mat(in_scr[span], up[...]) + up_bias
        square = pre * pre
        tanh = jnp.tanh(pre * (slope + (slope * 0.044715) * square))
        half = 0.5 * (1.0 + tanh)
        act = (pre * half).astype(BF16)
        bend = half + (0.5 * pre) * (1.0 - tanh * tanh) * (
            slope + (3.0 * slope * 0.044715) * square
        )
        pre_grad = mat_nt(grad[span], down[...]) * bend
        total = total + jnp.sum(pre_grad, axis=0, keepdims=True)
        pre_low = pre_grad.astype(BF16)
        act_scr[step, span] = act
        pre_scr[step, span] = pre_low
        acc_out[span] += mat(act, down[...])
        acc_in[span] += mat_nt(pre_low, up[...])
    vec_scr[pl.ds(4 + step, 1)] = total

    @pl.when(step == pl.num_programs(0) - 1)
    def _():
        pl.semaphore_wait(barrier, 3)
        sums = [jnp.zeros((1, model), F32) for _ in range(4)]
        part = model // GROUP
        for c, span in enumerate(spans):
            resid = resid_scr[span]
            normed, scale = row_stats(resid)
            inner_grad = acc_in[span]
            wide = grad[span].astype(F32)
            resid_grad = wide + norm_back(inner_grad * as_row(gain_ref), normed, scale)
            resid_out[span] = resid_grad
            low = resid_grad.astype(BF16)
            in_scr[span] = low
            back = mat_nt(low, out_w[...]).astype(BF16)
            pieces = swap_groups([back[:, a * part : (a + 1) * part] for a in range(GROUP)])
            for r in (2, 3, 1, 0):
                grads_vm[c, r] = pieces[r]
                if c == 0 and r:
                    grad_copy(r).start()
            layer_out[span] = (resid + acc_out[span] + as_row(down_b)).astype(BF16)
            for i, term in enumerate((wide, resid_grad, inner_grad * normed, inner_grad)):
                sums[i] = sums[i] + jnp.sum(term, axis=0, keepdims=True)
        out_copy(3).start()
        for i in range(4):
            vec_scr[i : i + 1] = sums[i]
        for t in range(tiles):
            down_term = mat_tn(act_scr[t], grad[...])
            if direct:
                for i in range(model // share):
                    slab_vm[t * (model // share) + i, 0:share] = down_term[
                        i * share : (i + 1) * share
                    ].astype(BF16)
            else:
                down_vm[t * model : (t + 1) * model] = down_term.astype(BF16)
        out_copy(0).start()
        for t in range(0, tiles, 2):
            terms = [mat(in_t[...], pre_scr[t]), mat(in_t[...], pre_scr[t + 1])]
            if direct:
                for i in range(owners):
                    own_rows = slice(i * small, (i + 1) * small)
                    slab_vm[i, share + t * small : share + (t + 2) * small] = jnp.concatenate(
                        [term[own_rows] for term in terms], axis=0
                    ).astype(BF16)
            else:
                for u, term in enumerate(terms):
                    up_vm[:, (t + u) * model : (t + u + 1) * model] = term.astype(BF16)
        out_copy(1).start()
        out_term = mat_tn(mixed[...], in_scr[...])
        fill = aligned(small + 8) - small - 8
        extra = [jnp.zeros((fill, model), F32)] if fill else []
        for i in range(owners):
            rest = jnp.concatenate(
                [out_term[i * small : (i + 1) * small], vec_scr[...]] + extra, axis=0
            ).astype(BF16)
            if direct:
                slab_vm[i, 2 * share :] = rest
            else:
                tail_vm[i] = rest
        out_copy(2).start()
        for r in (1, 2, 3):
            grad_copy(r).wait_recv()
        out_copy(4).start()
        for r in (1, 2, 3):
            grad_copy(r).wait_send()
        for i in range(5):
            out_copy(i).wait()


def block_layer(parts, hidden, grad, out_w, out_b, gain, shift, down_b, up_b, up, down, devices):
    tokens, model = hidden.shape
    ff = up.shape[1]
    steps = ff // model
    seqs = parts.shape[0]
    small, share = model // devices, ff // devices
    direct = small % 8 == 0 and share % 16 == 0
    tail_rows = aligned(small + 8)
    single = pl.Buffered(1)
    whole = lambda *shape: pl.BlockSpec(
        shape, lambda t: (0,) * len(shape), pipeline_mode=single
    )
    anywhere = pl.BlockSpec(memory_space=pl.ANY)
    unused = (16, 128)
    slab_shape, down_shape, up_shape, tail_shape = (
        ((devices, 2 * share + tail_rows, model), unused, unused, unused) if direct
        else (unused, (ff, model), (model, ff), (devices, tail_rows, model))
    )
    layer_out, resid_grad, grads, first, slab, down_grad, up_grad, tail = pl.pallas_call(
        lambda *refs: block_kernel(direct, *refs),
        grid=(steps,),
        out_shape=(
            jax.ShapeDtypeStruct((tokens, model), BF16),
            jax.ShapeDtypeStruct((tokens, model), F32),
            jax.ShapeDtypeStruct(parts.shape, BF16),
            jax.ShapeDtypeStruct((3,) + parts.shape[2:], BF16),
            jax.ShapeDtypeStruct(slab_shape, BF16),
            jax.ShapeDtypeStruct(down_shape, BF16),
            jax.ShapeDtypeStruct(up_shape, BF16),
            jax.ShapeDtypeStruct(tail_shape, BF16),
        ),
        in_specs=[
            whole(*parts.shape), whole(tokens, model), whole(tokens, model), whole(model, model),
            whole(model), whole(model), whole(model), whole(model), whole(ff),
            pl.BlockSpec((model, model), lambda t: (0, t)),
            pl.BlockSpec((model, model), lambda t: (t, 0)),
        ],
        out_specs=(
            whole(tokens, model), whole(tokens, model), anywhere, anywhere, anywhere, anywhere,
            anywhere, anywhere,
        ),
        scratch_shapes=[
            pltpu.VMEM((tokens, model), BF16),
            pltpu.VMEM((tokens, model), F32),
            pltpu.VMEM((tokens, model), BF16),
            pltpu.VMEM((model, tokens), BF16),
            pltpu.VMEM((tokens, model), F32),
            pltpu.VMEM((tokens, model), F32),
            pltpu.VMEM((steps, tokens, model), BF16),
            pltpu.VMEM((steps, tokens, model), BF16),
            pltpu.VMEM((8, model), F32),
            pltpu.VMEM((1, ff), F32),
            pltpu.VMEM(slab_shape, BF16),
            pltpu.VMEM(down_shape, BF16),
            pltpu.VMEM(up_shape, BF16),
            pltpu.VMEM(tail_shape, BF16),
            pltpu.VMEM(parts.shape, BF16),
            pltpu.VMEM((3,) + parts.shape[2:], BF16),
            pltpu.SemaphoreType.DMA((3,)),
            pltpu.SemaphoreType.DMA((3,)),
            pltpu.SemaphoreType.DMA((5,)),
        ],
        compiler_params=pltpu.CompilerParams(
            vmem_limit_bytes=VMEM, collective_id=3, has_side_effects=True
        ),
        cost_estimate=pl.CostEstimate(
            flops=26_000_000_000, bytes_accessed=30_000_000, transcendentals=0
        ),
        name="block_layer",
    )(parts, hidden, grad, out_w, out_b, gain, shift, down_b, up_b, up, down)
    if not direct:
        fit = lambda a: jnp.pad(a, ((0, 0), (0, aligned(a.shape[1]) - a.shape[1]), (0, 0)))
        down_grad = fit(down_grad.reshape(devices, share, model))
        up_grad = up_grad.reshape(devices, small, ff // model, model).transpose(0, 2, 1, 3)
        up_grad = fit(up_grad.reshape(devices, ff // model * small, model))
        slab = jnp.concatenate([down_grad, up_grad, tail], axis=1)
    return layer_out, resid_grad, grads, first, slab


def attend_back_kernel(
    dp_size, x_ref, grads_ref, first_ref, weight, draws_ref, hot_ref, proj, state_ref, mixed_ref, den_ref,
    soft_ref, phi_q_ref, phi_k_ref, slab_any,
    attn_out, ring_out, proj_out,
    grad_scr, num_scr, value_scr, score_scr, exact_scr, proj_scr,
    grad_land, near_send, near_land, far_keep, far_send, far_land,
    mine, met, ring_land, cross_land,
    weight_acc, own_send, pair_land, own_mid, own_land, part_send, part_land,
    grad_sems, near_sems, far_sems, mine_sem, met_send, met_sems, ring_send, ring_sems, cross_sems,
    pair_sems, own_send_sem, own_sems,
    part_sems,
):
    s, h = pl.program_id(0), pl.program_id(1)
    seqs, heads = pl.num_programs(0), pl.num_programs(1)
    rows, model = x_ref.shape[1], x_ref.shape[2]
    head_count = proj_scr.shape[0] // (3 * HD)
    width = head_count * HD
    total = GROUP * rows
    root = 1.0 / math.sqrt(HD)
    own, me = lax.axis_index("feat"), lax.axis_index("dp")
    own_x, own_core = own // 2, own % 2
    near, across = {"feat": partner(own, 1)}, {"feat": partner(own, 2)}
    last = (s == seqs - 1) & (h == heads - 1)

    def grad_copy(q, r):
        return remote(
            grads_ref.at[q, r], grad_land.at[q - 1, r - 1], grad_sems.at[0, q - 1, r - 1],
            grad_sems.at[1, q - 1, r - 1], {"feat": partner(own, r)},
        )

    def near_copy(q, i):
        return remote(
            near_send.at[i], near_land.at[q, i], near_sems.at[0, q, i], near_sems.at[1, q, i], near
        )

    def far_copy(q):
        return remote(far_send, far_land.at[q], far_sems.at[0, q], far_sems.at[1, q], across)

    half = dp_size // 2
    parity, pair = lax.rem(me, 2), lax.div(me, 2)
    spot = pair + parity * (dp_size - 1 - 2 * pair)

    def at_spot(p):
        p = lax.rem(p + dp_size, dp_size)
        upper = lax.div(p, half)
        return 2 * p + upper * (2 * dp_size - 1 - 4 * p)

    places = ({"dp": at_spot(spot + 1)}, {"dp": at_spot(spot - 1)})

    def chunk(k, way):
        return at_spot(spot - 1 - k) if way == 0 else at_spot(spot + 1 + k)

    def mine_copy(k, way, owner):
        return pltpu.make_async_copy(
            slab_any.at[owner + own_core], mine.at[k, way], mine_sem.at[k, way]
        )

    def met_copy(k, way, owner):
        return remote(
            slab_any.at[owner + 1 - own_core], met.at[k, way], met_send, met_sems.at[k, way], near
        )

    cut = aligned(mine.shape[2] // 2)
    halves = (pl.ds(0, cut), pl.ds(cut, mine.shape[2] - cut))

    def ring_copy(k, way, part):
        return remote(
            mine.at[k, way, halves[part]], ring_land.at[k, way, halves[part]], ring_send,
            ring_sems.at[k, way, part], places[way],
        )

    def cross_copy(part):
        return remote(
            mine.at[dp_size - 1, 1 - own_x, halves[part]], cross_land.at[halves[part]],
            cross_sems.at[0, part], cross_sems.at[1, part], across,
        )

    def begin_pieces(k):
        for way in range(2):
            owner = chunk(k, way) * GROUP + 2 * way
            met_copy(k, way, owner).start()
            mine_copy(k, way, owner).start()

    def ring_step(k, part):
        span = halves[part]
        if part == 0:

            @pl.when(k + 2 < dp_size)
            def _():
                begin_pieces(k + 2)

        @pl.when(k < dp_size)
        def _():
            for way in range(2):
                if part == 0:
                    mine_copy(k, way, 0).wait()
                    met_copy(k, way, 0).wait_recv()

                @pl.when(k == 0)
                def _():
                    base = mine[k, way, span].astype(F32) + met[k, way, span].astype(F32)
                    mine[k, way, span] = base.astype(BF16)

                @pl.when(k > 0)
                def _():
                    ring_copy(k - 1, way, part).wait_recv()
                    base = mine[k, way, span].astype(F32) + met[k, way, span].astype(F32)
                    base = base + ring_land[k - 1, way, span].astype(F32)
                    mine[k, way, span] = base.astype(BF16)

                @pl.when(k < dp_size - 1)
                def _():
                    ring_copy(k, way, part).start()

            @pl.when(k == dp_size - 1)
            def _():
                cross_copy(part).start()

        @pl.when(k == dp_size)
        def _():
            cross_copy(part).wait_recv()
            ring_out[span] = mine[dp_size - 1, own_x, span].astype(F32) + cross_land[span].astype(F32)

    def ring_turn(part):
        turn = s * heads + h
        count = seqs * heads
        steps = dp_size + 1

        def body(k, carry):
            ring_step(k, part)
            return carry

        lax.fori_loop(lax.div(turn * steps, count), lax.div((turn + 1) * steps, count), body, 0)

    mate = me + 1 - 2 * parity

    def pair_copy(q):
        return remote(
            own_send.at[q, 1 - parity], pair_land.at[q], pair_sems.at[0, q], pair_sems.at[1, q],
            {"dp": mate},
        )

    def own_copy(q, k):
        to = lax.rem(pair + k, half)
        return remote(
            own_mid.at[q, to], own_land.at[q, k], own_send_sem, own_sems.at[q, k],
            {"dp": 2 * to + parity},
        )

    def begin_own(q):
        base = model // dp_size
        turned = weight_acc[pl.ds(pl.multiple_of(q * 3 * HD, 3 * HD), 3 * HD)].T
        fill = turned[model : model + own_send.shape[3] - base]
        for c in range(dp_size):
            own_send[q, c % 2, c // 2] = jnp.concatenate(
                [turned[c * base : (c + 1) * base], fill], axis=0
            ).astype(BF16)
        pair_copy(q).start()

    def relay_own(q):
        pair_copy(q).wait_recv()
        own_mid[q] = (own_send[q, parity].astype(F32) + pair_land[q].astype(F32)).astype(BF16)

        def start(k, carry):
            own_copy(q, k).start()
            return carry

        lax.fori_loop(1, half, start, 0)

    def part_copy(r):
        other = partner(own, r)
        return remote(
            part_send.at[other], part_land.at[r - 1], part_sems.at[0, r - 1],
            part_sems.at[1, r - 1], {"feat": other},
        )

    def seq_span(q):
        return pl.ds(pl.multiple_of(q * rows, rows), rows)

    def add_near(q):
        near_copy(q, 1).wait_recv()

        @pl.when(q > 0)
        def _():
            far_copy(q - 1).wait_send()

        far_send[...] = (far_keep[1] + near_land[q, 1].astype(F32)).astype(BF16)
        far_copy(q).start()
        near_copy(q, 0).wait_recv()
        attn_out[seq_span(q)] = far_keep[0] + near_land[q, 0].astype(F32)

    def finish(q):
        far_copy(q).wait_recv()
        span = seq_span(q)
        attn_out[span] = attn_out[span] + far_land[q].astype(F32)

    @pl.when((s == 0) & (h == 0))
    def _():
        barrier = pltpu.get_barrier_semaphore()
        for r in (1, 2, 3):
            pl.semaphore_signal(
                barrier, inc=1, device_id={"feat": partner(own, r)}, device_id_type=MESH
            )

        def greet(k, carry):
            pl.semaphore_signal(
                barrier, inc=1, device_id={"dp": lax.rem(me + k, dp_size)}, device_id_type=MESH
            )
            return carry

        lax.fori_loop(1, dp_size, greet, 0)
        pl.semaphore_wait(barrier, 3 + dp_size - 1)
        for q in range(1, near_land.shape[0]):
            for r in (2, 3, 1):
                grad_copy(q, r).start()
        for k in range(2):
            begin_pieces(k)
        weight_acc[...] = jnp.zeros_like(weight_acc)

    @pl.when(h == 0)
    def _():
        grad_scr[:, 0:rows] = grads_ref[s, 0].astype(F32).T

        @pl.when(s == 0)
        def _():
            for r in (1, 2, 3):
                grad_scr[:, r * rows : (r + 1) * rows] = first_ref[r - 1].astype(F32).T

        @pl.when(s > 0)
        def _():
            for r in (1, 2, 3):
                grad_copy(s, r).wait_recv()
                grad_scr[:, r * rows : (r + 1) * rows] = grad_land[s - 1, r - 1].astype(F32).T

    query = proj[head_rows(h, 0, head_count)]
    key = proj[head_rows(h, 1, head_count)]
    value = proj[head_rows(h, 2, head_count)]
    draws = draws_ref[...]
    draws_ext = jnp.concatenate([draws, jnp.ones((16, FEAT), BF16)], axis=0)
    hot = hot_ref[...]
    away_wide = away_marks(hot)
    away = away_wide.astype(BF16)
    inverse = 1.0 / den_ref[0:1]
    head_grad = grad_scr[pl.ds(pl.multiple_of(h * HD, HD), HD)]
    grad_num = (head_grad * inverse).astype(BF16)
    grad_den = -jnp.sum(head_grad * mixed_ref[...], axis=0, keepdims=True) * inverse
    den_rows = jnp.broadcast_to(grad_den, (16, total)).astype(BF16)
    spread_grad = jnp.concatenate(spread(grad_num, hot) + [den_rows * hot], axis=0)
    spread_value = jnp.concatenate(spread(value, away) + [away], axis=0)

    phi_q = phi_q_ref[...]
    state_grad = mat_nt(spread_grad, phi_q).astype(BF16)
    scaled_q = mat_tn(state_ref[...], spread_grad) * phi_q.astype(F32)
    back_q = mat(draws_ext, scaled_q.astype(BF16))
    query_grad = back_q[0:HD] - query.astype(F32) * (back_q[HD : HD + 1] * root)

    phi_k = phi_k_ref[...]
    scaled_k = mat_tn(state_grad, spread_value) * phi_k.astype(F32)
    back_k = mat(draws_ext, scaled_k.astype(BF16))
    key_grad = back_k[0:HD] - key.astype(F32) * (back_k[HD : HD + 1] * root)
    value_grad = pick(mat(state_grad[0 : NBUCK * HD], phi_k), away_wide)

    ring_turn(0)
    one = (lax.broadcasted_iota(jnp.int32, hot.shape, 0) < 1).astype(F32).astype(BF16)
    num_scr[...] = jnp.concatenate([grad_num, den_rows], axis=0)
    value_scr[...] = jnp.concatenate([value, one], axis=0).astype(F32).T.astype(BF16)

    for c in range(total // CHUNK):
        cols = slice(c * CHUNK, (c + 1) * CHUNK)
        score = mat(value_scr[...], num_scr[:, cols]) * soft_ref[:, cols].astype(F32)
        score = score.astype(BF16)
        score_scr[:, cols] = score
        exact_scr[:, cols] = mat(proj[head_rows(h, 1, head_count)], score)
    query_grad = query_grad + exact_scr[...] * root
    key_grad = key_grad + mat_nt(query, score_scr[...]) * root
    value_grad = value_grad + mat_nt(grad_num, soft_ref[...])
    wide_grad = jnp.concatenate([query_grad, key_grad, value_grad], axis=0)
    low_grad = wide_grad.astype(BF16)
    for kind in range(3):
        proj_scr[head_rows(h, kind, head_count)] = low_grad[kind * HD : (kind + 1) * HD]
    weight_grad = mat(low_grad[:, 0:rows], x_ref[0])
    for r in (1, 2, 3):
        weight_grad = weight_grad + mat(low_grad[:, r * rows : (r + 1) * rows], x_ref[r])
    span = pl.ds(pl.multiple_of(h * 3 * HD, 3 * HD), 3 * HD)
    weight_acc[span, 0:model] += weight_grad
    weight_acc[span, model:] += jnp.broadcast_to(
        jnp.sum(wide_grad, axis=1, keepdims=True), (3 * HD, 128)
    )

    @pl.when(s == seqs - 1)
    def _():
        begin_own(h)

        @pl.when(h > 0)
        def _():
            relay_own(h - 1)

    @pl.when((s > 0) & (h == 0))
    def _():
        add_near(s - 1)

    @pl.when(h == heads - 1)
    def _():
        @pl.when(s > 0)
        def _():
            for i in range(2):
                near_copy(s - 1, i).wait_send()

        for r in (3, 1, 2, 0):
            term = mat_tn(proj_scr[:, r * rows : (r + 1) * rows], weight[...])
            if r % 2:
                near_send[r // 2] = term.astype(BF16)
                near_copy(s, r // 2).start()
            else:
                far_keep[r // 2] = term

    ring_turn(1)

    @pl.when(last)
    def _():
        add_near(s)
        relay_own(h)
        for q in range(near_land.shape[0] - 1):
            finish(q)

        sums = []
        for q in range(head_count):

            def arrive(k, carry):
                own_copy(q, k).wait_recv()
                return carry + own_land[q, k].astype(F32)

            sums.append(lax.fori_loop(1, half, arrive, own_mid[q, pair].astype(F32)))
        joined = jnp.concatenate(sums, axis=1)
        base = model // dp_size
        small = base // GROUP
        fill = jnp.broadcast_to(
            joined[base : base + 1], (part_send.shape[1] - small, joined.shape[1])
        )
        for a in range(GROUP):
            part_send[a] = jnp.concatenate(
                [joined[a * small : (a + 1) * small], fill], axis=0
            ).astype(BF16)
        for r in (2, 3, 1):
            part_copy(r).start()
        finish(s)
        proj_out[own] = part_send[own].astype(F32)
        for r in (1, 2, 3):
            part_copy(r).wait_recv()
            proj_out[partner(own, r)] = part_land[r - 1].astype(F32)

        for i in range(2):
            near_copy(s, i).wait_send()
        far_copy(s).wait_send()
        for r in (1, 2, 3):
            part_copy(r).wait_send()
        for part in range(2):
            cross_copy(part).wait_send()
        for q in range(1, near_land.shape[0]):
            for r in (1, 2, 3):
                grad_copy(q, r).wait_send()
        for q in range(head_count):
            pair_copy(q).wait_send()
        every = pl.ds(0, half - 1)
        if half > 1:
            remote(
                own_mid.at[:, every], own_land.at[:, every], own_send_sem, own_sems.at[0, 0],
                {"dp": mate},
            ).wait_send()
        remote(
            mine.at[pl.ds(0, dp_size - 1)], ring_land, ring_send, ring_sems.at[0, 0, 0], places[0]
        ).wait_send()
        remote(mine, met, met_send, met_sems.at[0, 0], near).wait_send()


def attend_back(
    dp_size, parts, grads, first, weight, draws, hot, proj, state, mixed, den, soft, phi_q, phi_k,
    slab,
):
    seqs, _, rows, model = parts.shape
    heads = draws.shape[0]
    width = heads * HD
    total = GROUP * rows
    n = dp_size
    ring_rows = slab.shape[1]
    own_rows = aligned(model // n + 1)
    part_rows = aligned(model // (n * GROUP) + 1)
    single = pl.Buffered(1)
    whole = lambda *shape: pl.BlockSpec(
        shape, lambda s, h: (0,) * len(shape), pipeline_mode=single
    )
    mode = single if n > 16 else None
    by_seq = lambda *shape: pl.BlockSpec(
        (None,) + shape, lambda s, h: (s,) + (0,) * len(shape), pipeline_mode=mode
    )
    by_head = lambda *shape: pl.BlockSpec(
        (None, None) + shape, lambda s, h: (s, h) + (0,) * len(shape), pipeline_mode=mode
    )
    anywhere = pl.BlockSpec(memory_space=pl.ANY)
    dma = pltpu.SemaphoreType.DMA
    return pl.pallas_call(
        lambda *refs: attend_back_kernel(dp_size, *refs),
        grid=(seqs, heads),
        out_shape=(
            jax.ShapeDtypeStruct((seqs * rows, model), F32),
            jax.ShapeDtypeStruct((ring_rows, model), F32),
            jax.ShapeDtypeStruct((GROUP, part_rows, 3 * width), F32),
        ),
        in_specs=[
            by_seq(GROUP, rows, model), whole(*grads.shape), whole(*first.shape),
            whole(3 * width, model),
            pl.BlockSpec((None, HD, FEAT), lambda s, h: (h, 0, 0)),
            by_seq(16, total), by_seq(3 * width, total), by_head(STATES, FEAT), by_head(HD, total),
            by_head(8, total), by_head(total, total), by_head(FEAT, total), by_head(FEAT, total),
            anywhere,
        ],
        out_specs=(
            whole(seqs * rows, model), whole(ring_rows, model), whole(GROUP, part_rows, 3 * width),
        ),
        scratch_shapes=[
            pltpu.VMEM((width, total), F32),
            pltpu.VMEM((HD + 16, total), BF16),
            pltpu.VMEM((total, HD + 16), BF16),
            pltpu.VMEM((total, total), BF16),
            pltpu.VMEM((HD, total), F32),
            pltpu.VMEM((3 * width, total), BF16),
            pltpu.VMEM((seqs - 1, 3, rows, width), BF16),
            pltpu.VMEM((2, rows, model), BF16),
            pltpu.VMEM((seqs, 2, rows, model), BF16),
            pltpu.VMEM((2, rows, model), F32),
            pltpu.VMEM((rows, model), BF16),
            pltpu.VMEM((seqs, rows, model), BF16),
            pltpu.VMEM((n, 2, ring_rows, model), BF16),
            pltpu.VMEM((n, 2, ring_rows, model), BF16),
            pltpu.VMEM((n - 1, 2, ring_rows, model), BF16),
            pltpu.VMEM((ring_rows, model), BF16),
            pltpu.VMEM((3 * width, model + 128), F32),
            pltpu.VMEM((heads, 2, n // 2, own_rows, 3 * HD), BF16),
            pltpu.VMEM((heads, n // 2, own_rows, 3 * HD), BF16),
            pltpu.VMEM((heads, n // 2, own_rows, 3 * HD), BF16),
            pltpu.VMEM((heads, n // 2, own_rows, 3 * HD), BF16),
            pltpu.VMEM((GROUP, part_rows, 3 * width), BF16),
            pltpu.VMEM((3, part_rows, 3 * width), BF16),
            dma((2, seqs - 1, 3)),
            dma((2, seqs, 2)),
            dma((2, seqs)),
            dma((n, 2)),
            dma,
            dma((n, 2)),
            dma,
            dma((n - 1, 2, 2)),
            dma((2, 2)),
            dma((2, heads)),
            dma,
            dma((heads, n // 2)),
            dma((2, 3)),
        ],
        compiler_params=pltpu.CompilerParams(
            vmem_limit_bytes=VMEM + (3 * 1024 * 1024 if n > 16 else 0), collective_id=2, has_side_effects=True
        ),
        cost_estimate=pl.CostEstimate(
            flops=48_000_000_000, bytes_accessed=40_000_000, transcendentals=0
        ),
        name="attend_back",
    )(
        parts, grads, first, weight, draws, hot, proj, state, mixed, den, soft, phi_q, phi_k, slab,
    )


def finish_kernel(
    starts, heads, attn_grad, resid_grad, hidden, sums, proj_sums, weight_rows, gain_ref, shift_ref,
    input_out, norm1_gain_out, norm1_bias_out, qkv_out, qkv_bias_out, out_out, out_bias_out,
    norm2_gain_out, norm2_bias_out, up_out, up_bias_out, down_out, down_bias_out,
):
    gain, shift = as_row(gain_ref), as_row(shift_ref)
    normed, scale = row_stats(hidden[...].astype(F32))
    input_out[...] = resid_grad[...] + norm_back(attn_grad[...] * gain, normed, scale)

    @pl.when(pl.program_id(0) == 0)
    def _():
        index = lax.axis_index("dp") * GROUP + lax.axis_index("feat")
        small, model = out_out.shape
        share = down_out.shape[0]
        ff = up_out.shape[1]

        def own(row, size):
            length = row.shape[1]
            wide = jnp.broadcast_to(row, (8, length))
            back = lax.rem(length - lax.rem(index * size, length), length)
            return pltpu.roll(wide, back, 1)[0:1, 0:size]

        down_out[...] = sums[0:share]
        first = starts[0]
        up_out[...] = jnp.concatenate(
            [sums[first + i * small : first + (i + 1) * small] for i in range(ff // model)], axis=1
        )
        first = starts[1]
        out_out[...] = sums[first : first + small]
        totals = first + small
        for i, out in enumerate((down_bias_out, out_bias_out, norm2_gain_out, norm2_bias_out)):
            out[...] = own(sums[totals + i : totals + i + 1], small).reshape(small)
        per_row = model // share
        level = index // per_row
        row = jnp.zeros((1, model), F32)
        for i in range(ff // model):
            row = jnp.where(level == i, sums[totals + 4 + i : totals + 5 + i], row)
        up_bias_out[...] = own(row, share).reshape(share)

        pieces = []
        for kind in range(3):
            for f in range(GROUP):
                for h in range(heads):
                    lanes = slice((h * 3 + kind) * HD, (h * 3 + kind + 1) * HD)
                    pieces.append(proj_sums[f, 0 : small + 1, lanes])
        grid = jnp.concatenate(pieces, axis=1)
        weight_sum, bias_sum = grid[0:small], grid[small : small + 1]
        qkv_out[...] = weight_sum
        qkv_bias_out[...] = own(bias_sum, 3 * small).reshape(3 * small)
        wide = weight_rows[...].astype(F32)

        def to_row(column):
            column = jnp.concatenate(
                [column, jnp.zeros((-small % 128, 1), F32)], axis=0
            )
            return jnp.broadcast_to(column, (column.shape[0], 128)).T[0:1, 0:small]

        bias_grad = to_row(jnp.sum(wide * bias_sum, axis=1, keepdims=True))
        gain_grad = to_row(jnp.sum(wide * weight_sum, axis=1, keepdims=True))
        norm1_bias_out[...] = bias_grad.reshape(small)
        gain_grad = (gain_grad - own(shift, small) * bias_grad) / own(gain, small)
        norm1_gain_out[...] = gain_grad.reshape(small)


def finish_all(
    attn_grad, resid_grad, hidden, sums, proj_sums, weight_rows, gain, shift, devices, ff, heads,
):
    seqs, rows, model = hidden.shape
    small, share = model // devices, ff // devices
    starts = (aligned(share), 2 * aligned(share))
    whole = lambda *shape: pl.BlockSpec(shape, lambda s: (0,) * len(shape))
    by_seq = pl.BlockSpec((rows, model), lambda s: (s, 0))
    shapes = (
        (small,), (small,), (small, 3 * model), (3 * small,), (small, model), (small,), (small,),
        (small,), (small, ff), (share,), (share, model), (small,),
    )
    return pl.pallas_call(
        lambda *refs: finish_kernel(starts, heads, *refs),
        grid=(seqs,),
        out_shape=(jax.ShapeDtypeStruct((seqs * rows, model), F32),)
        + tuple(jax.ShapeDtypeStruct(shape, F32) for shape in shapes),
        in_specs=[
            by_seq, by_seq, pl.BlockSpec((None, rows, model), lambda s: (s, 0, 0)),
            whole(*sums.shape), whole(*proj_sums.shape), whole(*weight_rows.shape), whole(model),
            whole(model),
        ],
        out_specs=(by_seq,) + tuple(whole(*shape) for shape in shapes),
        compiler_params=pltpu.CompilerParams(vmem_limit_bytes=VMEM),
        name="finish_all",
    )(attn_grad, resid_grad, hidden, sums, proj_sums, weight_rows, gain, shift)


def per_device(
    hidden_in, norm1_gain, norm1_bias, qkv_weight, qkv_bias, feature_draws, out_weight, out_bias,
    norm2_gain, norm2_bias, up_weight, up_bias, down_weight, down_bias, block_bucket, out_grad,
):
    seqs, rows, model = hidden_in.shape
    ff = up_weight.shape[1]
    dp_size = lax.axis_size("dp")
    devices = dp_size * GROUP
    small = model // devices
    heads = feature_draws.shape[0] // GROUP
    flat = (seqs * rows, model)

    (
        parts, mixed_parts, proj, state, mixed, den, hot, own_weight, own_draws, soft, phi_q, phi_k,
    ) = attend(
        block_bucket, hidden_in, norm1_gain, norm1_bias, qkv_bias, qkv_weight, feature_draws
    )
    layer_out, resid_grad, grads, first, slab = block_layer(
        mixed_parts, hidden_in.reshape(flat), out_grad.reshape(flat), out_weight, out_bias,
        norm2_gain, norm2_bias, down_bias, up_bias, up_weight, down_weight, devices,
    )
    attn_grad, sums, proj_sums = attend_back(
        dp_size, parts, grads, first, own_weight, own_draws, hot, proj, state, mixed, den, soft,
        phi_q, phi_k, slab,
    )
    index = lax.axis_index("dp") * GROUP + lax.axis_index("feat")
    weight_rows = lax.dynamic_slice_in_dim(qkv_weight, index * small, small, 0)
    (
        input_grad, norm1_gain_sum, norm1_bias_sum, qkv_weight_sum, qkv_bias_sum, out_weight_sum,
        out_bias_sum, norm2_gain_sum, norm2_bias_sum, up_sum, up_bias_sum, down_sum, down_bias_sum,
    ) = finish_all(
        attn_grad, resid_grad, hidden_in, sums, proj_sums, weight_rows, norm1_gain, norm1_bias,
        devices, ff, heads,
    )
    return (
        layer_out.reshape(hidden_in.shape), input_grad.reshape(hidden_in.shape), norm1_gain_sum,
        norm1_bias_sum, qkv_weight_sum, qkv_bias_sum, out_weight_sum, out_bias_sum, norm2_gain_sum,
        norm2_bias_sum, up_sum, up_bias_sum, down_sum, down_bias_sum,
    )


def solution(mesh):
    both = ("dp", "feat")
    rows = P("dp", "feat", None)
    in_specs = (
        rows, P(), P(), P(), P(), P(None, None, "feat"), P(), P(), P(), P(), P(), P(), P(), P(),
        P("dp", None, None), rows,
    )
    out_specs = (
        rows, rows, P(both), P(both), P(both, None), P(both), P(both, None), P(both), P(both),
        P(both), P(both, None), P(both), P(both, None), P(both),
    )
    return jax.shard_map(
        per_device, mesh=mesh, in_specs=in_specs, out_specs=out_specs, check_vma=False
    )
```

```python
import math

import jax
import jax.numpy as jnp
from jax import lax
from jax.experimental import pallas as pl
from jax.experimental.pallas import tpu as pltpu
from jax.sharding import PartitionSpec as P

HD = 64
FEAT = 256
BLOCK = 64
NBUCK = 4
GROUP = 4
CHUNK = 256
STATES = NBUCK * HD + 16
FAR = 16384.0
VMEM = 60 * 1024 * 1024

F32 = jnp.float32
BF16 = jnp.bfloat16
MESH = pl.DeviceIdType.MESH


def mat(left, right):
    return jnp.dot(left, right, preferred_element_type=F32)


def mat_nt(left, right):
    return lax.dot_general(left, right, (((1,), (1,)), ((), ())), preferred_element_type=F32)


def mat_tn(left, right):
    return lax.dot_general(left, right, (((0,), (0,)), ((), ())), preferred_element_type=F32)


def row_stats(values):
    row_mean = jnp.mean(values, axis=-1, keepdims=True)
    centered = values - row_mean
    scale = lax.rsqrt(jnp.mean(centered * centered, axis=-1, keepdims=True) + 1e-05)
    return (centered * scale, scale)


def norm_back(cotangent, normed, scale):
    mean_one = jnp.mean(cotangent, axis=-1, keepdims=True)
    mean_two = jnp.mean(cotangent * normed, axis=-1, keepdims=True)
    return scale * (cotangent - mean_one - normed * mean_two)


def features(vectors, draws):
    wide = vectors.astype(F32)
    square = jnp.sum(wide * wide, axis=0, keepdims=True) * (0.5 / math.sqrt(HD))
    return jnp.exp(mat_tn(draws, vectors) - (square + 0.5 * math.log(FEAT)))


def spread(rows, marks):
    return [rows * marks[u : u + 1] for u in range(NBUCK)]


def pick(stacked, marks):
    total = stacked[0:HD] * marks[0:1]
    for u in range(1, NBUCK):
        total = total + stacked[u * HD : (u + 1) * HD] * marks[u : u + 1]
    return total


def away_marks(hot):
    live = (lax.broadcasted_iota(jnp.int32, hot.shape, 0) < NBUCK).astype(F32)
    return live - hot.astype(F32)


def partner(own, r):
    x, core = own // 2, own % 2
    if r & 2:
        x = 1 - x
    if r & 1:
        core = 1 - core
    return 2 * x + core


def as_row(ref):
    return ref[...].reshape(1, ref.shape[0])


def aligned(count):
    return -(-count // 16) * 16


def remote(src, dst, send, recv, place):
    return pltpu.make_async_remote_copy(
        src_ref=src, dst_ref=dst, send_sem=send, recv_sem=recv, device_id=place, device_id_type=MESH
    )


def head_rows(h, kind, heads):
    return pl.ds(pl.multiple_of((kind * heads + h) * HD, HD), HD)


def attend_kernel(
    bucket, hidden, gain_ref, shift_ref, bias_ref, weight_any, draws_in,
    parts_any, mix_any, proj_out, state_out, mixed_out, den_out, hot_out, weight_out, draws_out,
    soft_out, phi_q_out, phi_k_out,
    parts, mix_land, mix_send, raw, bias_row, bias_scr, draws_land,
    query_scr, key_scr, value_scr, low_scr, gather_scr,
    raw_sem, part_send, part_recv, draw_send, draw_recv, mix_send_sem, mix_recv_sem, out_sem,
):
    s, h = pl.program_id(0), pl.program_id(1)
    seqs, rows, model = hidden.shape
    heads = draws_out.shape[0]
    total = GROUP * rows
    width = heads * HD
    own = lax.axis_index("feat")
    near, across = {"feat": partner(own, 1)}, {"feat": partner(own, 2)}

    def part_copy(q, kind):
        src, dst, place = ((0, 1, near), (0, 2, across), (2, 3, near))[kind]
        return remote(
            parts.at[q, src], parts.at[q, dst], part_send.at[q, kind], part_recv.at[q, kind], place
        )

    def draw_copy(r):
        other = partner(own, r)
        return remote(
            draws_in.at[pl.ds(other * heads, heads)], draws_land.at[r - 1],
            draw_send.at[r - 1], draw_recv.at[r - 1], {"feat": other},
        )

    def mix_copy(q, r):
        return remote(
            mix_send.at[q, r], mix_land.at[q, r], mix_send_sem.at[q, r - 1],
            mix_recv_sem.at[q, r - 1], {"feat": partner(own, r)},
        )

    def raw_copy(j):
        cols = pl.ds(pl.multiple_of(j * model + (own // 2) * 2 * width, 2 * width), 2 * width)
        return pltpu.make_async_copy(weight_any.at[:, cols], raw.at[j], raw_sem.at[j])

    def out_copy(q):
        return pltpu.make_async_copy(parts.at[q], parts_any.at[q], out_sem.at[q])

    @pl.when((s == 0) & (h == 0))
    def _():
        for j in range(3):
            raw_copy(j).start()
        barrier = pltpu.get_barrier_semaphore()
        for r in (1, 2, 3):
            pl.semaphore_signal(
                barrier, inc=1, device_id={"feat": partner(own, r)}, device_id_type=MESH
            )
        gain, shift = as_row(gain_ref), as_row(shift_ref)
        first = row_stats(hidden[0].astype(F32))[0] * gain + shift
        parts[0, 0] = first.astype(BF16)
        pl.semaphore_wait(barrier, 3)
        part_copy(0, 1).start()
        part_copy(0, 0).start()
        for r in (1, 2, 3):
            draw_copy(r).start()
        for q in range(1, seqs):
            normed = row_stats(hidden[q].astype(F32))[0] * gain + shift
            parts[q, 0] = normed.astype(BF16)
            part_copy(q, 1).start()
            part_copy(q, 0).start()
        core = own % 2
        bias_row[...] = as_row(bias_ref)
        for j in range(3):
            raw_copy(j).wait()
            piece = raw[j].astype(F32)
            piece = jnp.where(core == 0, piece[:, 0:width], piece[:, width:])
            weight_out[j * width : (j + 1) * width] = piece.T.astype(BF16)
            cols = pl.ds(pl.multiple_of(j * model + (own // 2) * 2 * width, 2 * width), 2 * width)
            pair = jnp.broadcast_to(bias_row[:, cols], (128, 2 * width))
            pair = jnp.where(core == 0, pair[:, 0:width], pair[:, width:])
            bias_scr[j * width : (j + 1) * width] = pair.T
        part_copy(0, 1).wait_recv()
        part_copy(0, 2).start()
        for r in (1, 2, 3):
            draw_copy(r).wait_recv()
        mine = draws_in[pl.ds(own * heads, heads)]
        draws_out[...] = jnp.concatenate(
            [mine] + [draws_land[r - 1] for r in (1, 2, 3)], axis=2
        )

    @pl.when(h == 0)
    def _():
        per = rows // BLOCK
        lanes = lax.broadcasted_iota(jnp.int32, (16, total), 1) // BLOCK
        level = lax.broadcasted_iota(jnp.int32, (16, total), 0)
        ids = jnp.full((16, total), -1, jnp.int32)
        for r in range(GROUP):
            for i in range(per):
                ids = jnp.where(
                    lanes == r * per + i, bucket[s, partner(own, r) * per + i, 0], ids
                )
        hot_out[...] = (ids == level).astype(F32).astype(BF16)

        def project(r):
            cols = slice(r * rows, (r + 1) * rows)
            piece = mat_nt(weight_out[...], parts[s, r]) + bias_scr[:, 0:1]
            proj_out[:, cols] = piece.astype(BF16)

        project(0)
        part_copy(s, 0).wait_recv()
        project(1)
        project(2)
        part_copy(s, 2).wait_recv()
        project(3)
        out_copy(s).start()

    query = proj_out[head_rows(h, 0, heads)]
    key = proj_out[head_rows(h, 1, heads)]
    value = proj_out[head_rows(h, 2, heads)]
    draws = draws_out[h]
    hot = hot_out[...]
    hot_wide = hot.astype(F32)
    away = away_marks(hot).astype(BF16)
    phi_q = features(query, draws).astype(BF16)
    phi_k = features(key, draws).astype(BF16)
    phi_q_out[...] = phi_q
    phi_k_out[...] = phi_k
    spread_value = jnp.concatenate(spread(value, away) + [away], axis=0)
    state = mat_nt(spread_value, phi_k).astype(BF16)
    state_out[...] = state
    low = mat(state, phi_q)
    low_scr[0:HD] = pick(low, hot_wide)
    low_den = jnp.sum(low[NBUCK * HD :] * hot_wide, axis=0, keepdims=True)
    low_scr[HD : HD + 8] = jnp.broadcast_to(low_den, (8, total))
    query_scr[...] = jnp.concatenate([query * (1.0 / math.sqrt(HD)), hot], axis=0).astype(BF16)
    key_scr[...] = jnp.concatenate([key, away * -FAR], axis=0).astype(F32).T.astype(BF16)
    value_scr[0:HD] = value
    value_scr[HD:] = jnp.ones((16, total), BF16)

    score = mat(key_scr[...], query_scr[:, 0:CHUNK])
    for c in range(total // CHUNK):
        cols = slice(c * CHUNK, (c + 1) * CHUNK)
        ahead = slice((c + 1) * CHUNK, (c + 2) * CHUNK)
        later = mat(key_scr[...], query_scr[:, ahead]) if ahead.stop <= total else None
        weights = jnp.exp(score).astype(BF16)
        score = later
        soft_out[:, cols] = weights
        exact = mat(value_scr[...], weights)
        den = low_scr[HD : HD + 8, cols] + exact[HD : HD + 8]
        mixed = (low_scr[0:HD, cols] + exact[0:HD]) / den[0:1]
        mixed_out[:, cols] = mixed
        den_out[:, cols] = den
        gather_scr[pl.ds(pl.multiple_of(h * HD, HD), HD), cols] = mixed

    @pl.when((h == heads - 2) & (s < seqs - 1))
    def _():
        part_copy(s + 1, 1).wait_recv()
        part_copy(s + 1, 2).start()

    @pl.when(h == heads - 1)
    def _():
        for r in range(GROUP):
            piece = gather_scr[:, r * rows : (r + 1) * rows].T.astype(BF16)
            if r == 0:
                mix_land[s, 0] = piece
            else:
                mix_send[s, r] = piece
                mix_copy(s, r).start()

    @pl.when((s == seqs - 1) & (h == heads - 1))
    def _():
        for q in range(seqs):
            for r in (1, 2, 3):
                mix_copy(q, r).wait_recv()
        done = pltpu.make_async_copy(mix_land, mix_any, out_sem.at[seqs])
        done.start()
        for q in range(seqs):
            for kind in range(3):
                part_copy(q, kind).wait_send()
            for r in (1, 2, 3):
                mix_copy(q, r).wait_send()
            out_copy(q).wait()
        for r in (1, 2, 3):
            draw_copy(r).wait_send()
        done.wait()


def attend(bucket, hidden, gain, shift, bias, weight, draws):
    seqs, rows, model = hidden.shape
    heads = draws.shape[0] // GROUP
    width = heads * HD
    total = GROUP * rows
    whole = lambda *shape: pl.BlockSpec(shape, lambda s, h: (0,) * len(shape))
    by_seq = lambda *shape: pl.BlockSpec((None,) + shape, lambda s, h: (s,) + (0,) * len(shape))
    by_head = lambda *shape: pl.BlockSpec(
        (None, None) + shape, lambda s, h: (s, h) + (0,) * len(shape)
    )
    anywhere = pl.BlockSpec(memory_space=pl.ANY)
    return pl.pallas_call(
        attend_kernel,
        grid=(seqs, heads),
        out_shape=(
            jax.ShapeDtypeStruct((seqs, GROUP, rows, model), BF16),
            jax.ShapeDtypeStruct((seqs, GROUP, rows, width), BF16),
            jax.ShapeDtypeStruct((seqs, 3 * width, total), BF16),
            jax.ShapeDtypeStruct((seqs, heads, STATES, FEAT), BF16),
            jax.ShapeDtypeStruct((seqs, heads, HD, total), F32),
            jax.ShapeDtypeStruct((seqs, heads, 8, total), F32),
            jax.ShapeDtypeStruct((seqs, 16, total), BF16),
            jax.ShapeDtypeStruct((3 * width, model), BF16),
            jax.ShapeDtypeStruct((heads, HD, FEAT), BF16),
            jax.ShapeDtypeStruct((seqs, heads, total, total), BF16),
            jax.ShapeDtypeStruct((seqs, heads, FEAT, total), BF16),
            jax.ShapeDtypeStruct((seqs, heads, FEAT, total), BF16),
        ),
        in_specs=[
            pl.BlockSpec(memory_space=pltpu.SMEM),
            whole(seqs, rows, model), whole(model), whole(model), whole(3 * model), anywhere,
            whole(*draws.shape),
        ],
        out_specs=(
            anywhere, anywhere, by_seq(3 * width, total), by_head(STATES, FEAT), by_head(HD, total),
            by_head(8, total), by_seq(16, total), whole(3 * width, model), whole(heads, HD, FEAT),
            by_head(total, total), by_head(FEAT, total), by_head(FEAT, total),
        ),
        scratch_shapes=[
            pltpu.VMEM((seqs, GROUP, rows, model), BF16),
            pltpu.VMEM((seqs, GROUP, rows, width), BF16),
            pltpu.VMEM((seqs, GROUP, rows, width), BF16),
            pltpu.VMEM((3, model, 2 * width), BF16),
            pltpu.VMEM((1, 3 * model), F32),
            pltpu.VMEM((3 * width, 128), F32),
            pltpu.VMEM((3, heads, HD, draws.shape[2]), BF16),
            pltpu.VMEM((HD + 16, total), BF16),
            pltpu.VMEM((total, HD + 16), BF16),
            pltpu.VMEM((HD + 16, total), BF16),
            pltpu.VMEM((HD + 8, total), F32),
            pltpu.VMEM((width, total), F32),
            pltpu.SemaphoreType.DMA((3,)),
            pltpu.SemaphoreType.DMA((seqs, 3)),
            pltpu.SemaphoreType.DMA((seqs, 3)),
            pltpu.SemaphoreType.DMA((3,)),
            pltpu.SemaphoreType.DMA((3,)),
            pltpu.SemaphoreType.DMA((seqs, 3)),
            pltpu.SemaphoreType.DMA((seqs, 3)),
            pltpu.SemaphoreType.DMA((seqs + 1,)),
        ],
        compiler_params=pltpu.CompilerParams(
            vmem_limit_bytes=VMEM, collective_id=1, has_side_effects=True
        ),
        cost_estimate=pl.CostEstimate(
            flops=24_000_000_000, bytes_accessed=20_000_000, transcendentals=0
        ),
        name="attend",
    )(bucket, hidden, gain, shift, bias, weight, draws)


def block_kernel(
    direct, parts_ref, hidden, grad, out_w, out_b, gain_ref, shift_ref, down_b, up_b, up, down,
    layer_out, resid_out, grads_any, first_any, slab_any, down_any, up_any, tail_any,
    mixed, resid_scr, in_scr, in_t, acc_out, acc_in, act_scr, pre_scr, vec_scr, bias_row,
    slab_vm, down_vm, up_vm, tail_vm, grads_vm, first_land, send_sem, recv_sem, out_sem,
):
    step = pl.program_id(0)
    model = hidden.shape[1]
    count = hidden.shape[0] // CHUNK
    tiles = act_scr.shape[0]
    spans = [slice(c * CHUNK, (c + 1) * CHUNK) for c in range(count)]
    owners = slab_vm.shape[0] if direct else tail_vm.shape[0]
    small = model // owners
    share = tiles * small
    own = lax.axis_index("feat")
    barrier = pltpu.get_barrier_semaphore()

    def swap_groups(pieces):
        pieces = [jnp.where(own % 2 == 1, pieces[r ^ 1], pieces[r]) for r in range(GROUP)]
        return [jnp.where(own // 2 == 1, pieces[r ^ 2], pieces[r]) for r in range(GROUP)]

    def grad_copy(r):
        return remote(
            grads_vm.at[0, r], first_land.at[r - 1], send_sem.at[r - 1], recv_sem.at[r - 1],
            {"feat": partner(own, r)},
        )

    def out_copy(i):
        pieces = [(down_vm, down_any), (up_vm, up_any), (tail_vm, tail_any)]
        if direct:
            cuts = (0, share, 2 * share, slab_vm.shape[1])
            pieces = [
                (slab_vm.at[:, pl.ds(low, high - low)], slab_any.at[:, pl.ds(low, high - low)])
                for low, high in zip(cuts, cuts[1:])
            ]
        src, dst = (
            *pieces, (grads_vm, grads_any), (first_land, first_any),
        )[i]
        return pltpu.make_async_copy(src, dst, out_sem.at[i])

    @pl.when(step == 0)
    def _():
        for r in (1, 2, 3):
            pl.semaphore_signal(
                barrier, inc=1, device_id={"feat": partner(own, r)}, device_id_type=MESH
            )
        for c, span in enumerate(spans):
            pieces = swap_groups([parts_ref[c, r] for r in range(GROUP)])
            mixed[span] = jnp.concatenate(pieces, axis=1)
            resid = hidden[span].astype(F32) + mat(mixed[span], out_w[...]) + as_row(out_b)
            resid_scr[span] = resid
            normed, _ = row_stats(resid)
            inner = normed * as_row(gain_ref) + as_row(shift_ref)
            in_scr[span] = inner.astype(BF16)
            in_t[:, span] = inner.T.astype(BF16)
        acc_out[...] = jnp.zeros_like(acc_out)
        acc_in[...] = jnp.zeros_like(acc_in)
        bias_row[...] = as_row(up_b)

    slope = math.sqrt(2.0 / math.pi)
    total = jnp.zeros((1, model), F32)
    up_bias = bias_row[:, pl.ds(pl.multiple_of(step * model, model), model)]
    products = lambda span: (mat(in_scr[span], up[...]), mat_nt(grad[span], down[...]))
    later = products(spans[0])
    for c, span in enumerate(spans):
        pre, act_grad = later
        if c + 1 < count:
            later = products(spans[c + 1])
        pre = pre + up_bias
        square = pre * pre
        tanh = jnp.tanh(pre * (slope + (slope * 0.044715) * square))
        half = 0.5 * (1.0 + tanh)
        act = (pre * half).astype(BF16)
        bend = half + (0.5 * pre) * (1.0 - tanh * tanh) * (
            slope + (3.0 * slope * 0.044715) * square
        )
        pre_grad = act_grad * bend
        total = total + jnp.sum(pre_grad, axis=0, keepdims=True)
        pre_low = pre_grad.astype(BF16)
        act_scr[step, span] = act
        pre_scr[step, span] = pre_low
        acc_out[span] += mat(act, down[...])
        acc_in[span] += mat_nt(pre_low, up[...])
    vec_scr[pl.ds(4 + step, 1)] = total

    @pl.when(step == pl.num_programs(0) - 1)
    def _():
        pl.semaphore_wait(barrier, 3)
        sums = [jnp.zeros((1, model), F32) for _ in range(4)]
        part = model // GROUP
        for c, span in enumerate(spans):
            resid = resid_scr[span]
            normed, scale = row_stats(resid)
            inner_grad = acc_in[span]
            wide = grad[span].astype(F32)
            resid_grad = wide + norm_back(inner_grad * as_row(gain_ref), normed, scale)
            resid_out[span] = resid_grad
            low = resid_grad.astype(BF16)
            in_scr[span] = low
            back = mat_nt(low, out_w[...]).astype(BF16)
            pieces = swap_groups([back[:, a * part : (a + 1) * part] for a in range(GROUP)])
            for r in (2, 3, 1, 0):
                grads_vm[c, r] = pieces[r]
                if c == 0 and r:
                    grad_copy(r).start()
            layer_out[span] = (resid + acc_out[span] + as_row(down_b)).astype(BF16)
            for i, term in enumerate((wide, resid_grad, inner_grad * normed, inner_grad)):
                sums[i] = sums[i] + jnp.sum(term, axis=0, keepdims=True)
        out_copy(3).start()
        for i in range(4):
            vec_scr[i : i + 1] = sums[i]
        for t in range(tiles):
            down_term = mat_tn(act_scr[t], grad[...])
            if direct:
                for i in range(model // share):
                    slab_vm[t * (model // share) + i, 0:share] = down_term[
                        i * share : (i + 1) * share
                    ].astype(BF16)
            else:
                down_vm[t * model : (t + 1) * model] = down_term.astype(BF16)
        out_copy(0).start()
        for t in range(0, tiles, 2):
            terms = [mat(in_t[...], pre_scr[t]), mat(in_t[...], pre_scr[t + 1])]
            if direct:
                for i in range(owners):
                    own_rows = slice(i * small, (i + 1) * small)
                    slab_vm[i, share + t * small : share + (t + 2) * small] = jnp.concatenate(
                        [term[own_rows] for term in terms], axis=0
                    ).astype(BF16)
            else:
                for u, term in enumerate(terms):
                    up_vm[:, (t + u) * model : (t + u + 1) * model] = term.astype(BF16)
        out_copy(1).start()
        out_term = mat_tn(mixed[...], in_scr[...])
        fill = aligned(small + 8) - small - 8
        extra = [jnp.zeros((fill, model), F32)] if fill else []
        for i in range(owners):
            rest = jnp.concatenate(
                [out_term[i * small : (i + 1) * small], vec_scr[...]] + extra, axis=0
            ).astype(BF16)
            if direct:
                slab_vm[i, 2 * share :] = rest
            else:
                tail_vm[i] = rest
        out_copy(2).start()
        for r in (1, 2, 3):
            grad_copy(r).wait_recv()
        out_copy(4).start()
        for r in (1, 2, 3):
            grad_copy(r).wait_send()
        for i in range(5):
            out_copy(i).wait()


def block_layer(parts, hidden, grad, out_w, out_b, gain, shift, down_b, up_b, up, down, devices):
    tokens, model = hidden.shape
    ff = up.shape[1]
    steps = ff // model
    seqs = parts.shape[0]
    small, share = model // devices, ff // devices
    direct = small % 8 == 0 and share % 16 == 0
    tail_rows = aligned(small + 8)
    single = pl.Buffered(1)
    whole = lambda *shape: pl.BlockSpec(
        shape, lambda t: (0,) * len(shape), pipeline_mode=single
    )
    anywhere = pl.BlockSpec(memory_space=pl.ANY)
    unused = (16, 128)
    slab_shape, down_shape, up_shape, tail_shape = (
        ((devices, 2 * share + tail_rows, model), unused, unused, unused) if direct
        else (unused, (ff, model), (model, ff), (devices, tail_rows, model))
    )
    layer_out, resid_grad, grads, first, slab, down_grad, up_grad, tail = pl.pallas_call(
        lambda *refs: block_kernel(direct, *refs),
        grid=(steps,),
        out_shape=(
            jax.ShapeDtypeStruct((tokens, model), BF16),
            jax.ShapeDtypeStruct((tokens, model), F32),
            jax.ShapeDtypeStruct(parts.shape, BF16),
            jax.ShapeDtypeStruct((3,) + parts.shape[2:], BF16),
            jax.ShapeDtypeStruct(slab_shape, BF16),
            jax.ShapeDtypeStruct(down_shape, BF16),
            jax.ShapeDtypeStruct(up_shape, BF16),
            jax.ShapeDtypeStruct(tail_shape, BF16),
        ),
        in_specs=[
            whole(*parts.shape), whole(tokens, model), whole(tokens, model), whole(model, model),
            whole(model), whole(model), whole(model), whole(model), whole(ff),
            pl.BlockSpec((model, model), lambda t: (0, t)),
            pl.BlockSpec((model, model), lambda t: (t, 0)),
        ],
        out_specs=(
            whole(tokens, model), whole(tokens, model), anywhere, anywhere, anywhere, anywhere,
            anywhere, anywhere,
        ),
        scratch_shapes=[
            pltpu.VMEM((tokens, model), BF16),
            pltpu.VMEM((tokens, model), F32),
            pltpu.VMEM((tokens, model), BF16),
            pltpu.VMEM((model, tokens), BF16),
            pltpu.VMEM((tokens, model), F32),
            pltpu.VMEM((tokens, model), F32),
            pltpu.VMEM((steps, tokens, model), BF16),
            pltpu.VMEM((steps, tokens, model), BF16),
            pltpu.VMEM((8, model), F32),
            pltpu.VMEM((1, ff), F32),
            pltpu.VMEM(slab_shape, BF16),
            pltpu.VMEM(down_shape, BF16),
            pltpu.VMEM(up_shape, BF16),
            pltpu.VMEM(tail_shape, BF16),
            pltpu.VMEM(parts.shape, BF16),
            pltpu.VMEM((3,) + parts.shape[2:], BF16),
            pltpu.SemaphoreType.DMA((3,)),
            pltpu.SemaphoreType.DMA((3,)),
            pltpu.SemaphoreType.DMA((5,)),
        ],
        compiler_params=pltpu.CompilerParams(
            vmem_limit_bytes=VMEM, collective_id=3, has_side_effects=True
        ),
        cost_estimate=pl.CostEstimate(
            flops=26_000_000_000, bytes_accessed=30_000_000, transcendentals=0
        ),
        name="block_layer",
    )(parts, hidden, grad, out_w, out_b, gain, shift, down_b, up_b, up, down)
    if not direct:
        fit = lambda a: jnp.pad(a, ((0, 0), (0, aligned(a.shape[1]) - a.shape[1]), (0, 0)))
        down_grad = fit(down_grad.reshape(devices, share, model))
        up_grad = up_grad.reshape(devices, small, ff // model, model).transpose(0, 2, 1, 3)
        up_grad = fit(up_grad.reshape(devices, ff // model * small, model))
        slab = jnp.concatenate([down_grad, up_grad, tail], axis=1)
    return layer_out, resid_grad, grads, first, slab


def attend_back_kernel(
    dp_size, x_ref, grads_ref, first_ref, weight, draws_ref, hot_ref, proj, state_ref, mixed_ref, den_ref,
    soft_ref, phi_q_ref, phi_k_ref, slab_any,
    attn_out, ring_out, proj_out,
    grad_scr, num_scr, value_scr, score_scr, exact_scr, proj_scr,
    grad_land, near_send, near_land, far_keep, far_send, far_land,
    mine, met, ring_land, cross_land,
    weight_acc, own_send, pair_land, own_mid, own_land, part_send, part_land,
    grad_sems, near_sems, far_sems, mine_sem, met_send, met_sems, ring_send, ring_sems, cross_sems,
    pair_sems, own_send_sem, own_sems,
    part_sems,
):
    s, h = pl.program_id(0), pl.program_id(1)
    seqs, heads = pl.num_programs(0), pl.num_programs(1)
    rows, model = x_ref.shape[1], x_ref.shape[2]
    head_count = proj_scr.shape[0] // (3 * HD)
    width = head_count * HD
    total = GROUP * rows
    root = 1.0 / math.sqrt(HD)
    own, me = lax.axis_index("feat"), lax.axis_index("dp")
    own_x, own_core = own // 2, own % 2
    near, across = {"feat": partner(own, 1)}, {"feat": partner(own, 2)}
    last = (s == seqs - 1) & (h == heads - 1)

    def grad_copy(q, r):
        return remote(
            grads_ref.at[q, r], grad_land.at[q - 1, r - 1], grad_sems.at[0, q - 1, r - 1],
            grad_sems.at[1, q - 1, r - 1], {"feat": partner(own, r)},
        )

    def near_copy(q, i):
        return remote(
            near_send.at[i], near_land.at[q, i], near_sems.at[0, q, i], near_sems.at[1, q, i], near
        )

    def far_copy(q):
        return remote(far_send, far_land.at[q], far_sems.at[0, q], far_sems.at[1, q], across)

    half = dp_size // 2
    parity, pair = lax.rem(me, 2), lax.div(me, 2)
    spot = pair + parity * (dp_size - 1 - 2 * pair)

    def at_spot(p):
        p = lax.rem(p + dp_size, dp_size)
        upper = lax.div(p, half)
        return 2 * p + upper * (2 * dp_size - 1 - 4 * p)

    places = ({"dp": at_spot(spot + 1)}, {"dp": at_spot(spot - 1)})

    def chunk(k, way):
        return at_spot(spot - 1 - k) if way == 0 else at_spot(spot + 1 + k)

    def mine_copy(k, way, owner):
        return pltpu.make_async_copy(
            slab_any.at[owner + own_core], mine.at[k, way], mine_sem.at[k, way]
        )

    def met_copy(k, way, owner):
        return remote(
            slab_any.at[owner + 1 - own_core], met.at[k, way], met_send, met_sems.at[k, way], near
        )

    cut = aligned(mine.shape[2] // 2)
    halves = (pl.ds(0, cut), pl.ds(cut, mine.shape[2] - cut))

    def ring_copy(k, way, part):
        return remote(
            mine.at[k, way, halves[part]], ring_land.at[k, way, halves[part]], ring_send,
            ring_sems.at[k, way, part], places[way],
        )

    def cross_copy(part):
        return remote(
            mine.at[dp_size - 1, 1 - own_x, halves[part]], cross_land.at[halves[part]],
            cross_sems.at[0, part], cross_sems.at[1, part], across,
        )

    def begin_pieces(k):
        for way in range(2):
            owner = chunk(k, way) * GROUP + 2 * way
            met_copy(k, way, owner).start()
            mine_copy(k, way, owner).start()

    def ring_step(k, part):
        span = halves[part]
        if part == 0:

            @pl.when(k + 2 < dp_size)
            def _():
                begin_pieces(k + 2)

        @pl.when(k < dp_size)
        def _():
            for way in range(2):
                if part == 0:
                    mine_copy(k, way, 0).wait()
                    met_copy(k, way, 0).wait_recv()

                @pl.when(k == 0)
                def _():
                    base = mine[k, way, span].astype(F32) + met[k, way, span].astype(F32)
                    mine[k, way, span] = base.astype(BF16)

                @pl.when(k > 0)
                def _():
                    ring_copy(k - 1, way, part).wait_recv()
                    base = mine[k, way, span].astype(F32) + met[k, way, span].astype(F32)
                    base = base + ring_land[k - 1, way, span].astype(F32)
                    mine[k, way, span] = base.astype(BF16)

                @pl.when(k < dp_size - 1)
                def _():
                    ring_copy(k, way, part).start()

            @pl.when(k == dp_size - 1)
            def _():
                cross_copy(part).start()

        @pl.when(k == dp_size)
        def _():
            cross_copy(part).wait_recv()
            ring_out[span] = mine[dp_size - 1, own_x, span].astype(F32) + cross_land[span].astype(F32)

    def ring_turn(part):
        turn = s * heads + h
        count = seqs * heads
        steps = dp_size + 1

        def body(k, carry):
            ring_step(k, part)
            return carry

        lax.fori_loop(lax.div(turn * steps, count), lax.div((turn + 1) * steps, count), body, 0)

    mate = me + 1 - 2 * parity

    def pair_copy(q):
        return remote(
            own_send.at[q, 1 - parity], pair_land.at[q], pair_sems.at[0, q], pair_sems.at[1, q],
            {"dp": mate},
        )

    def own_copy(q, k):
        to = lax.rem(pair + k, half)
        return remote(
            own_mid.at[q, to], own_land.at[q, k], own_send_sem, own_sems.at[q, k],
            {"dp": 2 * to + parity},
        )

    def begin_own(q):
        base = model // dp_size
        turned = weight_acc[pl.ds(pl.multiple_of(q * 3 * HD, 3 * HD), 3 * HD)].T
        fill = turned[model : model + own_send.shape[3] - base]
        for c in range(dp_size):
            own_send[q, c % 2, c // 2] = jnp.concatenate(
                [turned[c * base : (c + 1) * base], fill], axis=0
            ).astype(BF16)
        pair_copy(q).start()

    def relay_own(q):
        pair_copy(q).wait_recv()
        own_mid[q] = (own_send[q, parity].astype(F32) + pair_land[q].astype(F32)).astype(BF16)

        def start(k, carry):
            own_copy(q, k).start()
            return carry

        lax.fori_loop(1, half, start, 0)

    def part_copy(r):
        other = partner(own, r)
        return remote(
            part_send.at[other], part_land.at[r - 1], part_sems.at[0, r - 1],
            part_sems.at[1, r - 1], {"feat": other},
        )

    def seq_span(q):
        return pl.ds(pl.multiple_of(q * rows, rows), rows)

    def add_near(q):
        near_copy(q, 1).wait_recv()

        @pl.when(q > 0)
        def _():
            far_copy(q - 1).wait_send()

        far_send[...] = (far_keep[1] + near_land[q, 1].astype(F32)).astype(BF16)
        far_copy(q).start()
        near_copy(q, 0).wait_recv()
        attn_out[seq_span(q)] = far_keep[0] + near_land[q, 0].astype(F32)

    def finish(q):
        far_copy(q).wait_recv()
        span = seq_span(q)
        attn_out[span] = attn_out[span] + far_land[q].astype(F32)

    @pl.when((s == 0) & (h == 0))
    def _():
        barrier = pltpu.get_barrier_semaphore()
        for r in (1, 2, 3):
            pl.semaphore_signal(
                barrier, inc=1, device_id={"feat": partner(own, r)}, device_id_type=MESH
            )

        def greet(k, carry):
            pl.semaphore_signal(
                barrier, inc=1, device_id={"dp": lax.rem(me + k, dp_size)}, device_id_type=MESH
            )
            return carry

        lax.fori_loop(1, dp_size, greet, 0)
        pl.semaphore_wait(barrier, 3 + dp_size - 1)
        for q in range(1, near_land.shape[0]):
            for r in (2, 3, 1):
                grad_copy(q, r).start()
        for k in range(2):
            begin_pieces(k)
        weight_acc[...] = jnp.zeros_like(weight_acc)

    @pl.when(h == 0)
    def _():
        grad_scr[:, 0:rows] = grads_ref[s, 0].astype(F32).T

        @pl.when(s == 0)
        def _():
            for r in (1, 2, 3):
                grad_scr[:, r * rows : (r + 1) * rows] = first_ref[r - 1].astype(F32).T

        @pl.when(s > 0)
        def _():
            for r in (1, 2, 3):
                grad_copy(s, r).wait_recv()
                grad_scr[:, r * rows : (r + 1) * rows] = grad_land[s - 1, r - 1].astype(F32).T

    query = proj[head_rows(h, 0, head_count)]
    key = proj[head_rows(h, 1, head_count)]
    value = proj[head_rows(h, 2, head_count)]
    draws = draws_ref[...]
    draws_ext = jnp.concatenate([draws, jnp.ones((16, FEAT), BF16)], axis=0)
    hot = hot_ref[...]
    away_wide = away_marks(hot)
    away = away_wide.astype(BF16)
    inverse = 1.0 / den_ref[0:1]
    head_grad = grad_scr[pl.ds(pl.multiple_of(h * HD, HD), HD)]
    grad_num = (head_grad * inverse).astype(BF16)
    grad_den = -jnp.sum(head_grad * mixed_ref[...], axis=0, keepdims=True) * inverse
    den_rows = jnp.broadcast_to(grad_den, (16, total)).astype(BF16)
    spread_grad = jnp.concatenate(spread(grad_num, hot) + [den_rows * hot], axis=0)
    spread_value = jnp.concatenate(spread(value, away) + [away], axis=0)

    phi_q, phi_k = phi_q_ref[...], phi_k_ref[...]
    state_grad = mat_nt(spread_grad, phi_q).astype(BF16)
    phi_q_grad = mat_tn(state_ref[...], spread_grad)
    phi_k_grad = mat_tn(state_grad, spread_value)
    value_low = mat(state_grad[0 : NBUCK * HD], phi_k)
    scaled_q = (phi_q_grad * phi_q.astype(F32)).astype(BF16)
    back_q = mat(draws_ext, scaled_q)
    scaled_k = (phi_k_grad * phi_k.astype(F32)).astype(BF16)
    back_k = mat(draws_ext, scaled_k)
    value_grad = pick(value_low, away_wide)
    query_grad = back_q[0:HD] - query.astype(F32) * (back_q[HD : HD + 1] * root)
    key_grad = back_k[0:HD] - key.astype(F32) * (back_k[HD : HD + 1] * root)

    ring_turn(0)
    one = (lax.broadcasted_iota(jnp.int32, hot.shape, 0) < 1).astype(F32).astype(BF16)
    num_scr[...] = jnp.concatenate([grad_num, den_rows], axis=0)
    value_scr[...] = jnp.concatenate([value, one], axis=0).astype(F32).T.astype(BF16)

    later = mat(value_scr[...], num_scr[:, 0:CHUNK])
    for c in range(total // CHUNK):
        cols = slice(c * CHUNK, (c + 1) * CHUNK)
        ahead = slice((c + 1) * CHUNK, (c + 2) * CHUNK)
        score = later
        later = mat(value_scr[...], num_scr[:, ahead]) if ahead.stop <= total else None
        score = (score * soft_ref[:, cols].astype(F32)).astype(BF16)
        score_scr[:, cols] = score
        exact_scr[:, cols] = mat(proj[head_rows(h, 1, head_count)], score)
    query_grad = query_grad + exact_scr[...] * root
    key_grad = key_grad + mat_nt(query, score_scr[...]) * root
    value_grad = value_grad + mat_nt(grad_num, soft_ref[...])
    wide_grad = jnp.concatenate([query_grad, key_grad, value_grad], axis=0)
    low_grad = wide_grad.astype(BF16)
    for kind in range(3):
        proj_scr[head_rows(h, kind, head_count)] = low_grad[kind * HD : (kind + 1) * HD]
    weight_grad = mat(low_grad[:, 0:rows], x_ref[0])
    for r in (1, 2, 3):
        weight_grad = weight_grad + mat(low_grad[:, r * rows : (r + 1) * rows], x_ref[r])
    span = pl.ds(pl.multiple_of(h * 3 * HD, 3 * HD), 3 * HD)
    weight_acc[span, 0:model] += weight_grad
    weight_acc[span, model:] += jnp.broadcast_to(
        jnp.sum(wide_grad, axis=1, keepdims=True), (3 * HD, 128)
    )

    @pl.when((s > 0) & (h == 0))
    def _():
        add_near(s - 1)

    @pl.when(h == heads - 1)
    def _():
        @pl.when(s > 0)
        def _():
            for i in range(2):
                near_copy(s - 1, i).wait_send()

        for r in (3, 1, 2, 0):
            term = mat_tn(proj_scr[:, r * rows : (r + 1) * rows], weight[...])
            if r % 2:
                near_send[r // 2] = term.astype(BF16)
                near_copy(s, r // 2).start()
            else:
                far_keep[r // 2] = term

    @pl.when(s == seqs - 1)
    def _():
        begin_own(h)

        @pl.when(h > 0)
        def _():
            relay_own(h - 1)

    ring_turn(1)

    @pl.when(last)
    def _():
        add_near(s)
        relay_own(h)
        for q in range(near_land.shape[0] - 1):
            finish(q)

        sums = []
        for q in range(head_count):

            def arrive(k, carry):
                own_copy(q, k).wait_recv()
                return carry + own_land[q, k].astype(F32)

            sums.append(lax.fori_loop(1, half, arrive, own_mid[q, pair].astype(F32)))
        joined = jnp.concatenate(sums, axis=1)
        base = model // dp_size
        small = base // GROUP
        fill = jnp.broadcast_to(
            joined[base : base + 1], (part_send.shape[1] - small, joined.shape[1])
        )
        for a in range(GROUP):
            part_send[a] = jnp.concatenate(
                [joined[a * small : (a + 1) * small], fill], axis=0
            ).astype(BF16)
        for r in (2, 3, 1):
            part_copy(r).start()
        finish(s)
        proj_out[own] = part_send[own].astype(F32)
        for r in (1, 2, 3):
            part_copy(r).wait_recv()
            proj_out[partner(own, r)] = part_land[r - 1].astype(F32)

        for i in range(2):
            near_copy(s, i).wait_send()
        far_copy(s).wait_send()
        for r in (1, 2, 3):
            part_copy(r).wait_send()
        for part in range(2):
            cross_copy(part).wait_send()
        for q in range(1, near_land.shape[0]):
            for r in (1, 2, 3):
                grad_copy(q, r).wait_send()
        for q in range(head_count):
            pair_copy(q).wait_send()
        every = pl.ds(0, half - 1)
        if half > 1:
            remote(
                own_mid.at[:, every], own_land.at[:, every], own_send_sem, own_sems.at[0, 0],
                {"dp": mate},
            ).wait_send()
        remote(
            mine.at[pl.ds(0, dp_size - 1)], ring_land, ring_send, ring_sems.at[0, 0, 0], places[0]
        ).wait_send()
        remote(mine, met, met_send, met_sems.at[0, 0], near).wait_send()


def attend_back(
    dp_size, parts, grads, first, weight, draws, hot, proj, state, mixed, den, soft, phi_q, phi_k,
    slab,
):
    seqs, _, rows, model = parts.shape
    heads = draws.shape[0]
    width = heads * HD
    total = GROUP * rows
    n = dp_size
    ring_rows = slab.shape[1]
    own_rows = aligned(model // n + 1)
    part_rows = aligned(model // (n * GROUP) + 1)
    single = pl.Buffered(1)
    whole = lambda *shape: pl.BlockSpec(
        shape, lambda s, h: (0,) * len(shape), pipeline_mode=single
    )
    mode = single if n > 16 else None
    by_seq = lambda *shape: pl.BlockSpec(
        (None,) + shape, lambda s, h: (s,) + (0,) * len(shape), pipeline_mode=mode
    )
    by_head = lambda *shape: pl.BlockSpec(
        (None, None) + shape, lambda s, h: (s, h) + (0,) * len(shape), pipeline_mode=mode
    )
    anywhere = pl.BlockSpec(memory_space=pl.ANY)
    dma = pltpu.SemaphoreType.DMA
    return pl.pallas_call(
        lambda *refs: attend_back_kernel(dp_size, *refs),
        grid=(seqs, heads),
        out_shape=(
            jax.ShapeDtypeStruct((seqs * rows, model), F32),
            jax.ShapeDtypeStruct((ring_rows, model), F32),
            jax.ShapeDtypeStruct((GROUP, part_rows, 3 * width), F32),
        ),
        in_specs=[
            by_seq(GROUP, rows, model), whole(*grads.shape), whole(*first.shape),
            whole(3 * width, model),
            pl.BlockSpec((None, HD, FEAT), lambda s, h: (h, 0, 0)),
            by_seq(16, total), by_seq(3 * width, total), by_head(STATES, FEAT), by_head(HD, total),
            by_head(8, total), by_head(total, total), by_head(FEAT, total), by_head(FEAT, total),
            anywhere,
        ],
        out_specs=(
            whole(seqs * rows, model), whole(ring_rows, model), whole(GROUP, part_rows, 3 * width),
        ),
        scratch_shapes=[
            pltpu.VMEM((width, total), F32),
            pltpu.VMEM((HD + 16, total), BF16),
            pltpu.VMEM((total, HD + 16), BF16),
            pltpu.VMEM((total, total), BF16),
            pltpu.VMEM((HD, total), F32),
            pltpu.VMEM((3 * width, total), BF16),
            pltpu.VMEM((seqs - 1, 3, rows, width), BF16),
            pltpu.VMEM((2, rows, model), BF16),
            pltpu.VMEM((seqs, 2, rows, model), BF16),
            pltpu.VMEM((2, rows, model), F32),
            pltpu.VMEM((rows, model), BF16),
            pltpu.VMEM((seqs, rows, model), BF16),
            pltpu.VMEM((n, 2, ring_rows, model), BF16),
            pltpu.VMEM((n, 2, ring_rows, model), BF16),
            pltpu.VMEM((n - 1, 2, ring_rows, model), BF16),
            pltpu.VMEM((ring_rows, model), BF16),
            pltpu.VMEM((3 * width, model + 128), F32),
            pltpu.VMEM((heads, 2, n // 2, own_rows, 3 * HD), BF16),
            pltpu.VMEM((heads, n // 2, own_rows, 3 * HD), BF16),
            pltpu.VMEM((heads, n // 2, own_rows, 3 * HD), BF16),
            pltpu.VMEM((heads, n // 2, own_rows, 3 * HD), BF16),
            pltpu.VMEM((GROUP, part_rows, 3 * width), BF16),
            pltpu.VMEM((3, part_rows, 3 * width), BF16),
            dma((2, seqs - 1, 3)),
            dma((2, seqs, 2)),
            dma((2, seqs)),
            dma((n, 2)),
            dma,
            dma((n, 2)),
            dma,
            dma((n - 1, 2, 2)),
            dma((2, 2)),
            dma((2, heads)),
            dma,
            dma((heads, n // 2)),
            dma((2, 3)),
        ],
        compiler_params=pltpu.CompilerParams(
            vmem_limit_bytes=VMEM + (3 * 1024 * 1024 if n > 16 else 0), collective_id=2, has_side_effects=True
        ),
        cost_estimate=pl.CostEstimate(
            flops=48_000_000_000, bytes_accessed=40_000_000, transcendentals=0
        ),
        name="attend_back",
    )(
        parts, grads, first, weight, draws, hot, proj, state, mixed, den, soft, phi_q, phi_k, slab,
    )


def finish_kernel(
    starts, heads, attn_grad, resid_grad, hidden, sums, proj_sums, weight_rows, gain_ref, shift_ref,
    input_out, norm1_gain_out, norm1_bias_out, qkv_out, qkv_bias_out, out_out, out_bias_out,
    norm2_gain_out, norm2_bias_out, up_out, up_bias_out, down_out, down_bias_out,
):
    gain, shift = as_row(gain_ref), as_row(shift_ref)
    normed, scale = row_stats(hidden[...].astype(F32))
    input_out[...] = resid_grad[...] + norm_back(attn_grad[...] * gain, normed, scale)

    @pl.when(pl.program_id(0) == 0)
    def _():
        index = lax.axis_index("dp") * GROUP + lax.axis_index("feat")
        small, model = out_out.shape
        share = down_out.shape[0]
        ff = up_out.shape[1]

        def own(row, size):
            length = row.shape[1]
            wide = jnp.broadcast_to(row, (8, length))
            back = lax.rem(length - lax.rem(index * size, length), length)
            return pltpu.roll(wide, back, 1)[0:1, 0:size]

        down_out[...] = sums[0:share]
        first = starts[0]
        up_out[...] = jnp.concatenate(
            [sums[first + i * small : first + (i + 1) * small] for i in range(ff // model)], axis=1
        )
        first = starts[1]
        out_out[...] = sums[first : first + small]
        totals = first + small
        for i, out in enumerate((down_bias_out, out_bias_out, norm2_gain_out, norm2_bias_out)):
            out[...] = own(sums[totals + i : totals + i + 1], small).reshape(small)
        per_row = model // share
        level = index // per_row
        row = jnp.zeros((1, model), F32)
        for i in range(ff // model):
            row = jnp.where(level == i, sums[totals + 4 + i : totals + 5 + i], row)
        up_bias_out[...] = own(row, share).reshape(share)

        pieces = []
        for kind in range(3):
            for f in range(GROUP):
                for h in range(heads):
                    lanes = slice((h * 3 + kind) * HD, (h * 3 + kind + 1) * HD)
                    pieces.append(proj_sums[f, 0 : small + 1, lanes])
        grid = jnp.concatenate(pieces, axis=1)
        weight_sum, bias_sum = grid[0:small], grid[small : small + 1]
        qkv_out[...] = weight_sum
        qkv_bias_out[...] = own(bias_sum, 3 * small).reshape(3 * small)
        wide = weight_rows[...].astype(F32)

        def to_row(column):
            column = jnp.concatenate(
                [column, jnp.zeros((-small % 128, 1), F32)], axis=0
            )
            return jnp.broadcast_to(column, (column.shape[0], 128)).T[0:1, 0:small]

        bias_grad = to_row(jnp.sum(wide * bias_sum, axis=1, keepdims=True))
        gain_grad = to_row(jnp.sum(wide * weight_sum, axis=1, keepdims=True))
        norm1_bias_out[...] = bias_grad.reshape(small)
        gain_grad = (gain_grad - own(shift, small) * bias_grad) / own(gain, small)
        norm1_gain_out[...] = gain_grad.reshape(small)


def finish_all(
    attn_grad, resid_grad, hidden, sums, proj_sums, weight_rows, gain, shift, devices, ff, heads,
):
    seqs, rows, model = hidden.shape
    small, share = model // devices, ff // devices
    starts = (aligned(share), 2 * aligned(share))
    whole = lambda *shape: pl.BlockSpec(shape, lambda s: (0,) * len(shape))
    by_seq = pl.BlockSpec((rows, model), lambda s: (s, 0))
    shapes = (
        (small,), (small,), (small, 3 * model), (3 * small,), (small, model), (small,), (small,),
        (small,), (small, ff), (share,), (share, model), (small,),
    )
    return pl.pallas_call(
        lambda *refs: finish_kernel(starts, heads, *refs),
        grid=(seqs,),
        out_shape=(jax.ShapeDtypeStruct((seqs * rows, model), F32),)
        + tuple(jax.ShapeDtypeStruct(shape, F32) for shape in shapes),
        in_specs=[
            by_seq, by_seq, pl.BlockSpec((None, rows, model), lambda s: (s, 0, 0)),
            whole(*sums.shape), whole(*proj_sums.shape), whole(*weight_rows.shape), whole(model),
            whole(model),
        ],
        out_specs=(by_seq,) + tuple(whole(*shape) for shape in shapes),
        compiler_params=pltpu.CompilerParams(vmem_limit_bytes=VMEM),
        name="finish_all",
    )(attn_grad, resid_grad, hidden, sums, proj_sums, weight_rows, gain, shift)


def per_device(
    hidden_in, norm1_gain, norm1_bias, qkv_weight, qkv_bias, feature_draws, out_weight, out_bias,
    norm2_gain, norm2_bias, up_weight, up_bias, down_weight, down_bias, block_bucket, out_grad,
):
    seqs, rows, model = hidden_in.shape
    ff = up_weight.shape[1]
    dp_size = lax.axis_size("dp")
    devices = dp_size * GROUP
    small = model // devices
    heads = feature_draws.shape[0] // GROUP
    flat = (seqs * rows, model)

    (
        parts, mixed_parts, proj, state, mixed, den, hot, own_weight, own_draws, soft, phi_q, phi_k,
    ) = attend(
        block_bucket, hidden_in, norm1_gain, norm1_bias, qkv_bias, qkv_weight, feature_draws
    )
    layer_out, resid_grad, grads, first, slab = block_layer(
        mixed_parts, hidden_in.reshape(flat), out_grad.reshape(flat), out_weight, out_bias,
        norm2_gain, norm2_bias, down_bias, up_bias, up_weight, down_weight, devices,
    )
    attn_grad, sums, proj_sums = attend_back(
        dp_size, parts, grads, first, own_weight, own_draws, hot, proj, state, mixed, den, soft,
        phi_q, phi_k, slab,
    )
    index = lax.axis_index("dp") * GROUP + lax.axis_index("feat")
    weight_rows = lax.dynamic_slice_in_dim(qkv_weight, index * small, small, 0)
    (
        input_grad, norm1_gain_sum, norm1_bias_sum, qkv_weight_sum, qkv_bias_sum, out_weight_sum,
        out_bias_sum, norm2_gain_sum, norm2_bias_sum, up_sum, up_bias_sum, down_sum, down_bias_sum,
    ) = finish_all(
        attn_grad, resid_grad, hidden_in, sums, proj_sums, weight_rows, norm1_gain, norm1_bias,
        devices, ff, heads,
    )
    return (
        layer_out.reshape(hidden_in.shape), input_grad.reshape(hidden_in.shape), norm1_gain_sum,
        norm1_bias_sum, qkv_weight_sum, qkv_bias_sum, out_weight_sum, out_bias_sum, norm2_gain_sum,
        norm2_bias_sum, up_sum, up_bias_sum, down_sum, down_bias_sum,
    )


def solution(mesh):
    both = ("dp", "feat")
    rows = P("dp", "feat", None)
    in_specs = (
        rows, P(), P(), P(), P(), P(None, None, "feat"), P(), P(), P(), P(), P(), P(), P(), P(),
        P("dp", None, None), rows,
    )
    out_specs = (
        rows, rows, P(both), P(both), P(both, None), P(both), P(both, None), P(both), P(both),
        P(both), P(both, None), P(both), P(both, None), P(both),
    )
    return jax.shard_map(
        per_device, mesh=mesh, in_specs=in_specs, out_specs=out_specs, check_vma=False
    )
```

```python
import math

import jax
import jax.numpy as jnp
from jax import lax
from jax.experimental import pallas as pl
from jax.experimental.pallas import tpu as pltpu
from jax.sharding import PartitionSpec as P

HD = 64
FEAT = 256
BLOCK = 64
NBUCK = 4
GROUP = 4
CHUNK = 256
STATES = NBUCK * HD + 16
FAR = 16384.0
VMEM = 60 * 1024 * 1024

F32 = jnp.float32
BF16 = jnp.bfloat16
MESH = pl.DeviceIdType.MESH


def mat(left, right):
    return jnp.dot(left, right, preferred_element_type=F32)


def mat_nt(left, right):
    return lax.dot_general(left, right, (((1,), (1,)), ((), ())), preferred_element_type=F32)


def mat_tn(left, right):
    return lax.dot_general(left, right, (((0,), (0,)), ((), ())), preferred_element_type=F32)


def row_stats(values):
    row_mean = jnp.mean(values, axis=-1, keepdims=True)
    centered = values - row_mean
    scale = lax.rsqrt(jnp.mean(centered * centered, axis=-1, keepdims=True) + 1e-05)
    return (centered * scale, scale)


def norm_back(cotangent, normed, scale):
    mean_one = jnp.mean(cotangent, axis=-1, keepdims=True)
    mean_two = jnp.mean(cotangent * normed, axis=-1, keepdims=True)
    return scale * (cotangent - mean_one - normed * mean_two)


def features(vectors, draws):
    wide = vectors.astype(F32)
    square = jnp.sum(wide * wide, axis=0, keepdims=True) * (0.5 / math.sqrt(HD))
    return jnp.exp(mat_tn(draws, vectors) - (square + 0.5 * math.log(FEAT)))


def spread(rows, marks):
    return [rows * marks[u : u + 1] for u in range(NBUCK)]


def pick(stacked, marks):
    total = stacked[0:HD] * marks[0:1]
    for u in range(1, NBUCK):
        total = total + stacked[u * HD : (u + 1) * HD] * marks[u : u + 1]
    return total


def away_marks(hot):
    live = (lax.broadcasted_iota(jnp.int32, hot.shape, 0) < NBUCK).astype(F32)
    return live - hot.astype(F32)


def partner(own, r):
    x, core = own // 2, own % 2
    if r & 2:
        x = 1 - x
    if r & 1:
        core = 1 - core
    return 2 * x + core


def as_row(ref):
    return ref[...].reshape(1, ref.shape[0])


def aligned(count):
    return -(-count // 16) * 16


def remote(src, dst, send, recv, place):
    return pltpu.make_async_remote_copy(
        src_ref=src, dst_ref=dst, send_sem=send, recv_sem=recv, device_id=place, device_id_type=MESH
    )


def head_rows(h, kind, heads):
    return pl.ds(pl.multiple_of((kind * heads + h) * HD, HD), HD)


def attend_kernel(
    bucket, hidden, gain_ref, shift_ref, bias_ref, weight_any, draws_in, grad, down_any,
    parts_any, mix_any, act_grad_any, proj_out, state_out, mixed_out, den_out, hot_out, weight_out, draws_out,
    soft_out, phi_q_out, phi_k_out,
    parts, mix_land, mix_send, raw, bias_row, bias_scr, draws_land, down_vm, act_grad,
    query_scr, key_scr, value_scr, low_scr,
    raw_sem, part_send, part_recv, draw_send, draw_recv, mix_send_sem, mix_recv_sem, out_sem,
    down_sem, act_sem,
):
    s, h = pl.program_id(0), pl.program_id(1)
    seqs, rows, model = hidden.shape
    heads = draws_out.shape[0]
    total = GROUP * rows
    width = heads * HD
    own = lax.axis_index("feat")
    near, across = {"feat": partner(own, 1)}, {"feat": partner(own, 2)}

    def part_copy(q, kind):
        src, dst, place = ((0, 1, near), (0, 2, across), (2, 3, near))[kind]
        return remote(
            parts.at[q, src], parts.at[q, dst], part_send.at[q, kind], part_recv.at[q, kind], place
        )

    def draw_copy(r):
        other = partner(own, r)
        return remote(
            draws_in.at[pl.ds(other * heads, heads)], draws_land.at[r - 1],
            draw_send.at[r - 1], draw_recv.at[r - 1], {"feat": other},
        )

    def mix_copy(q, g, r):
        span = pl.ds(pl.multiple_of(g * HD, HD), HD)
        return remote(
            mix_send.at[q, r - 1, span], mix_land.at[q, r, span], mix_send_sem.at[q, g, r - 1],
            mix_recv_sem.at[q, g, r - 1], {"feat": partner(own, r)},
        )

    down_copy = pltpu.make_async_copy(down_any, down_vm, down_sem)
    act_copy = pltpu.make_async_copy(act_grad, act_grad_any, act_sem)

    def raw_copy(j):
        cols = pl.ds(pl.multiple_of(j * model + (own // 2) * 2 * width, 2 * width), 2 * width)
        return pltpu.make_async_copy(weight_any.at[:, cols], raw.at[j], raw_sem.at[j])

    def out_copy(q):
        return pltpu.make_async_copy(parts.at[q], parts_any.at[q], out_sem.at[q])

    @pl.when((s == 0) & (h == 0))
    def _():
        for j in range(3):
            raw_copy(j).start()
        down_copy.start()
        barrier = pltpu.get_barrier_semaphore()
        for r in (1, 2, 3):
            pl.semaphore_signal(
                barrier, inc=1, device_id={"feat": partner(own, r)}, device_id_type=MESH
            )
        gain, shift = as_row(gain_ref), as_row(shift_ref)
        first = row_stats(hidden[0].astype(F32))[0] * gain + shift
        parts[0, 0] = first.astype(BF16)
        pl.semaphore_wait(barrier, 3)
        part_copy(0, 1).start()
        part_copy(0, 0).start()
        for r in (1, 2, 3):
            draw_copy(r).start()
        for q in range(1, seqs):
            normed = row_stats(hidden[q].astype(F32))[0] * gain + shift
            parts[q, 0] = normed.astype(BF16)
            part_copy(q, 1).start()
            part_copy(q, 0).start()
        core = own % 2
        bias_row[...] = as_row(bias_ref)
        for j in range(3):
            raw_copy(j).wait()
            piece = raw[j].astype(F32)
            piece = jnp.where(core == 0, piece[:, 0:width], piece[:, width:])
            weight_out[j * width : (j + 1) * width] = piece.T.astype(BF16)
            cols = pl.ds(pl.multiple_of(j * model + (own // 2) * 2 * width, 2 * width), 2 * width)
            pair = jnp.broadcast_to(bias_row[:, cols], (128, 2 * width))
            pair = jnp.where(core == 0, pair[:, 0:width], pair[:, width:])
            bias_scr[j * width : (j + 1) * width] = pair.T
        down_copy.wait()
        for t in range(act_grad.shape[0]):
            tile = down_vm[t * model : (t + 1) * model]
            for q in range(seqs):
                act_grad[t, q * rows : (q + 1) * rows] = mat_nt(grad[q], tile).astype(BF16)
        act_copy.start()
        part_copy(0, 1).wait_recv()
        part_copy(0, 2).start()
        for r in (1, 2, 3):
            draw_copy(r).wait_recv()
        mine = draws_in[pl.ds(own * heads, heads)]
        draws_out[...] = jnp.concatenate(
            [mine] + [draws_land[r - 1] for r in (1, 2, 3)], axis=2
        )

    @pl.when(h == 0)
    def _():
        per = rows // BLOCK
        lanes = lax.broadcasted_iota(jnp.int32, (16, total), 1) // BLOCK
        level = lax.broadcasted_iota(jnp.int32, (16, total), 0)
        ids = jnp.full((16, total), -1, jnp.int32)
        for r in range(GROUP):
            for i in range(per):
                ids = jnp.where(
                    lanes == r * per + i, bucket[s, partner(own, r) * per + i, 0], ids
                )
        hot_out[...] = (ids == level).astype(F32).astype(BF16)

        def project(r):
            cols = slice(r * rows, (r + 1) * rows)
            piece = mat_nt(weight_out[...], parts[s, r]) + bias_scr[:, 0:1]
            proj_out[:, cols] = piece.astype(BF16)

        project(0)
        part_copy(s, 0).wait_recv()
        project(1)
        project(2)
        part_copy(s, 2).wait_recv()
        project(3)
        out_copy(s).start()

    query = proj_out[head_rows(h, 0, heads)]
    key = proj_out[head_rows(h, 1, heads)]
    value = proj_out[head_rows(h, 2, heads)]
    draws = draws_out[h]
    hot = hot_out[...]
    hot_wide = hot.astype(F32)
    away = away_marks(hot).astype(BF16)
    phi_q = features(query, draws).astype(BF16)
    phi_k = features(key, draws).astype(BF16)
    phi_q_out[...] = phi_q
    phi_k_out[...] = phi_k
    spread_value = jnp.concatenate(spread(value, away) + [away], axis=0)
    state = mat_nt(spread_value, phi_k).astype(BF16)
    state_out[...] = state
    low = mat(state, phi_q)
    low_scr[0:HD] = pick(low, hot_wide)
    low_den = jnp.sum(low[NBUCK * HD :] * hot_wide, axis=0, keepdims=True)
    low_scr[HD : HD + 8] = jnp.broadcast_to(low_den, (8, total))
    query_scr[...] = jnp.concatenate([query * (1.0 / math.sqrt(HD)), hot], axis=0).astype(BF16)
    key_scr[...] = jnp.concatenate([key, away * -FAR], axis=0).astype(F32).T.astype(BF16)
    value_scr[0:HD] = value
    value_scr[HD:] = jnp.ones((16, total), BF16)

    head_span = pl.ds(pl.multiple_of(h * HD, HD), HD)
    score = mat(key_scr[...], query_scr[:, 0:CHUNK])
    for c in range(total // CHUNK):
        cols = slice(c * CHUNK, (c + 1) * CHUNK)
        ahead = slice((c + 1) * CHUNK, (c + 2) * CHUNK)
        later = mat(key_scr[...], query_scr[:, ahead]) if ahead.stop <= total else None
        weights = jnp.exp(score).astype(BF16)
        score = later
        soft_out[:, cols] = weights
        exact = mat(value_scr[...], weights)
        den = low_scr[HD : HD + 8, cols] + exact[HD : HD + 8]
        mixed = (low_scr[0:HD, cols] + exact[0:HD]) / den[0:1]
        mixed_out[:, cols] = mixed
        den_out[:, cols] = den
        mixed_low = mixed.astype(BF16)
        for r in range(GROUP):
            low_col, high_col = max(cols.start, r * rows), min(cols.stop, (r + 1) * rows)
            if low_col < high_col:
                piece = mixed_low[:, low_col - cols.start : high_col - cols.start]
                inner = slice(low_col - r * rows, high_col - r * rows)
                if r:
                    mix_send[s, r - 1, head_span, inner] = piece
                else:
                    mix_land[s, 0, head_span, inner] = piece
    for r in (2, 3, 1):
        mix_copy(s, h, r).start()

    @pl.when((h == heads - 2) & (s < seqs - 1))
    def _():
        part_copy(s + 1, 1).wait_recv()
        part_copy(s + 1, 2).start()

    @pl.when((s == seqs - 1) & (h == heads - 1))
    def _():
        for q in range(seqs):
            for g in range(heads):
                for r in (1, 2, 3):
                    mix_copy(q, g, r).wait_recv()
        done = pltpu.make_async_copy(mix_land, mix_any, out_sem.at[seqs])
        done.start()
        for q in range(seqs):
            for kind in range(3):
                part_copy(q, kind).wait_send()
            for g in range(heads):
                for r in (1, 2, 3):
                    mix_copy(q, g, r).wait_send()
            out_copy(q).wait()
        act_copy.wait()
        for r in (1, 2, 3):
            draw_copy(r).wait_send()
        done.wait()


def attend(bucket, hidden, gain, shift, bias, weight, draws, grad, down):
    seqs, rows, model = hidden.shape
    tiles = down.shape[0] // model
    heads = draws.shape[0] // GROUP
    width = heads * HD
    total = GROUP * rows
    whole = lambda *shape: pl.BlockSpec(shape, lambda s, h: (0,) * len(shape))
    by_seq = lambda *shape: pl.BlockSpec((None,) + shape, lambda s, h: (s,) + (0,) * len(shape))
    by_head = lambda *shape: pl.BlockSpec(
        (None, None) + shape, lambda s, h: (s, h) + (0,) * len(shape)
    )
    anywhere = pl.BlockSpec(memory_space=pl.ANY)
    return pl.pallas_call(
        attend_kernel,
        grid=(seqs, heads),
        out_shape=(
            jax.ShapeDtypeStruct((seqs, GROUP, rows, model), BF16),
            jax.ShapeDtypeStruct((seqs, GROUP, width, rows), BF16),
            jax.ShapeDtypeStruct((tiles, seqs * rows, model), BF16),
            jax.ShapeDtypeStruct((seqs, 3 * width, total), BF16),
            jax.ShapeDtypeStruct((seqs, heads, STATES, FEAT), BF16),
            jax.ShapeDtypeStruct((seqs, heads, HD, total), F32),
            jax.ShapeDtypeStruct((seqs, heads, 8, total), F32),
            jax.ShapeDtypeStruct((seqs, 16, total), BF16),
            jax.ShapeDtypeStruct((3 * width, model), BF16),
            jax.ShapeDtypeStruct((heads, HD, FEAT), BF16),
            jax.ShapeDtypeStruct((seqs, heads, total, total), BF16),
            jax.ShapeDtypeStruct((seqs, heads, FEAT, total), BF16),
            jax.ShapeDtypeStruct((seqs, heads, FEAT, total), BF16),
        ),
        in_specs=[
            pl.BlockSpec(memory_space=pltpu.SMEM),
            whole(seqs, rows, model), whole(model), whole(model), whole(3 * model), anywhere,
            whole(*draws.shape), whole(seqs, rows, model), anywhere,
        ],
        out_specs=(
            anywhere, anywhere, anywhere, by_seq(3 * width, total), by_head(STATES, FEAT), by_head(HD, total),
            by_head(8, total), by_seq(16, total), whole(3 * width, model), whole(heads, HD, FEAT),
            by_head(total, total), by_head(FEAT, total), by_head(FEAT, total),
        ),
        scratch_shapes=[
            pltpu.VMEM((seqs, GROUP, rows, model), BF16),
            pltpu.VMEM((seqs, GROUP, width, rows), BF16),
            pltpu.VMEM((seqs, 3, width, rows), BF16),
            pltpu.VMEM((3, model, 2 * width), BF16),
            pltpu.VMEM((1, 3 * model), F32),
            pltpu.VMEM((3 * width, 128), F32),
            pltpu.VMEM((3, heads, HD, draws.shape[2]), BF16),
            pltpu.VMEM(down.shape, BF16),
            pltpu.VMEM((tiles, seqs * rows, model), BF16),
            pltpu.VMEM((HD + 16, total), BF16),
            pltpu.VMEM((total, HD + 16), BF16),
            pltpu.VMEM((HD + 16, total), BF16),
            pltpu.VMEM((HD + 8, total), F32),
            pltpu.SemaphoreType.DMA((3,)),
            pltpu.SemaphoreType.DMA((seqs, 3)),
            pltpu.SemaphoreType.DMA((seqs, 3)),
            pltpu.SemaphoreType.DMA((3,)),
            pltpu.SemaphoreType.DMA((3,)),
            pltpu.SemaphoreType.DMA((seqs, heads, 3)),
            pltpu.SemaphoreType.DMA((seqs, heads, 3)),
            pltpu.SemaphoreType.DMA((seqs + 1,)),
            pltpu.SemaphoreType.DMA,
            pltpu.SemaphoreType.DMA,
        ],
        compiler_params=pltpu.CompilerParams(
            vmem_limit_bytes=VMEM, collective_id=1, has_side_effects=True
        ),
        cost_estimate=pl.CostEstimate(
            flops=24_000_000_000, bytes_accessed=20_000_000, transcendentals=0
        ),
        name="attend",
    )(bucket, hidden, gain, shift, bias, weight, draws, grad, down)


def block_kernel(
    direct, parts_ref, hidden, grad, out_w, out_b, gain_ref, shift_ref, down_b, up_b, up, down,
    act_grad_ref,
    layer_out, resid_out, grads_any, first_any, slab_any, down_any, up_any, tail_any,
    mixed_t, resid_scr, in_scr, in_t, acc_out, acc_in, act_scr, pre_scr, vec_scr, bias_row, back_t,
    slab_vm, down_vm, up_vm, tail_vm, grads_vm, first_land, send_sem, recv_sem, out_sem,
):
    step = pl.program_id(0)
    model = hidden.shape[1]
    count = hidden.shape[0] // CHUNK
    tiles = act_scr.shape[0]
    spans = [slice(c * CHUNK, (c + 1) * CHUNK) for c in range(count)]
    owners = slab_vm.shape[0] if direct else tail_vm.shape[0]
    small = model // owners
    share = tiles * small
    own = lax.axis_index("feat")
    barrier = pltpu.get_barrier_semaphore()

    part = model // GROUP

    def group_rows(r):
        return pl.ds(pl.multiple_of(partner(own, r) * part, part), part)

    def grad_copy(r):
        return remote(
            grads_vm.at[0, r], first_land.at[r - 1], send_sem.at[r - 1], recv_sem.at[r - 1],
            {"feat": partner(own, r)},
        )

    def out_copy(i):
        pieces = [(down_vm, down_any), (up_vm, up_any), (tail_vm, tail_any)]
        if direct:
            cuts = (0, share, 2 * share, slab_vm.shape[1])
            pieces = [
                (slab_vm.at[:, pl.ds(low, high - low)], slab_any.at[:, pl.ds(low, high - low)])
                for low, high in zip(cuts, cuts[1:])
            ]
        src, dst = (
            *pieces, (grads_vm, grads_any), (first_land, first_any),
        )[i]
        return pltpu.make_async_copy(src, dst, out_sem.at[i])

    @pl.when(step == 0)
    def _():
        for r in (1, 2, 3):
            pl.semaphore_signal(
                barrier, inc=1, device_id={"feat": partner(own, r)}, device_id_type=MESH
            )
        for c, span in enumerate(spans):
            for r in range(GROUP):
                mixed_t[group_rows(r), span] = parts_ref[c, r]
            resid = hidden[span].astype(F32) + mat_tn(mixed_t[:, span], out_w[...]) + as_row(out_b)
            resid_scr[span] = resid
            normed, _ = row_stats(resid)
            inner = normed * as_row(gain_ref) + as_row(shift_ref)
            in_scr[span] = inner.astype(BF16)
            in_t[:, span] = inner.T.astype(BF16)
        acc_out[...] = jnp.zeros_like(acc_out)
        acc_in[...] = jnp.zeros_like(acc_in)
        bias_row[...] = as_row(up_b)

    slope = math.sqrt(2.0 / math.pi)
    total = jnp.zeros((1, model), F32)
    up_bias = bias_row[:, pl.ds(pl.multiple_of(step * model, model), model)]
    for span in spans:
        pre = mat(in_scr[span], up[...]) + up_bias
        square = pre * pre
        tanh = jnp.tanh(pre * (slope + (slope * 0.044715) * square))
        half = 0.5 * (1.0 + tanh)
        act = (pre * half).astype(BF16)
        bend = half + (0.5 * pre) * (1.0 - tanh * tanh) * (
            slope + (3.0 * slope * 0.044715) * square
        )
        pre_grad = act_grad_ref[span].astype(F32) * bend
        total = total + jnp.sum(pre_grad, axis=0, keepdims=True)
        pre_low = pre_grad.astype(BF16)
        act_scr[step, span] = act
        pre_scr[step, span] = pre_low
        acc_out[span] += mat(act, down[...])
        acc_in[span] += mat_nt(pre_low, up[...])
    vec_scr[pl.ds(4 + step, 1)] = total

    @pl.when(step == pl.num_programs(0) - 1)
    def _():
        pl.semaphore_wait(barrier, 3)
        sums = [jnp.zeros((1, model), F32) for _ in range(4)]
        for c, span in enumerate(spans):
            resid = resid_scr[span]
            normed, scale = row_stats(resid)
            inner_grad = acc_in[span]
            wide = grad[span].astype(F32)
            resid_grad = wide + norm_back(inner_grad * as_row(gain_ref), normed, scale)
            resid_out[span] = resid_grad
            low = resid_grad.astype(BF16)
            in_scr[span] = low
            back_t[...] = mat_nt(out_w[...], low).astype(BF16)
            for r in (2, 3, 1, 0):
                grads_vm[c, r] = back_t[group_rows(r)]
                if c == 0 and r:
                    grad_copy(r).start()
            layer_out[span] = (resid + acc_out[span] + as_row(down_b)).astype(BF16)
            for i, term in enumerate((wide, resid_grad, inner_grad * normed, inner_grad)):
                sums[i] = sums[i] + jnp.sum(term, axis=0, keepdims=True)
        out_copy(3).start()
        for i in range(4):
            vec_scr[i : i + 1] = sums[i]
        for t in range(tiles):
            down_term = mat_tn(act_scr[t], grad[...])
            if direct:
                for i in range(model // share):
                    slab_vm[t * (model // share) + i, 0:share] = down_term[
                        i * share : (i + 1) * share
                    ].astype(BF16)
            else:
                down_vm[t * model : (t + 1) * model] = down_term.astype(BF16)
        out_copy(0).start()
        for t in range(0, tiles, 2):
            terms = [mat(in_t[...], pre_scr[t]), mat(in_t[...], pre_scr[t + 1])]
            if direct:
                for i in range(owners):
                    own_rows = slice(i * small, (i + 1) * small)
                    slab_vm[i, share + t * small : share + (t + 2) * small] = jnp.concatenate(
                        [term[own_rows] for term in terms], axis=0
                    ).astype(BF16)
            else:
                for u, term in enumerate(terms):
                    up_vm[:, (t + u) * model : (t + u + 1) * model] = term.astype(BF16)
        out_copy(1).start()
        out_term = mat(mixed_t[...], in_scr[...])
        fill = aligned(small + 8) - small - 8
        extra = [jnp.zeros((fill, model), F32)] if fill else []
        for i in range(owners):
            rest = jnp.concatenate(
                [out_term[i * small : (i + 1) * small], vec_scr[...]] + extra, axis=0
            ).astype(BF16)
            if direct:
                slab_vm[i, 2 * share :] = rest
            else:
                tail_vm[i] = rest
        out_copy(2).start()
        for r in (1, 2, 3):
            grad_copy(r).wait_recv()
        out_copy(4).start()
        for r in (1, 2, 3):
            grad_copy(r).wait_send()
        for i in range(5):
            out_copy(i).wait()


def block_layer(
    parts, hidden, grad, out_w, out_b, gain, shift, down_b, up_b, up, down, act_grad, devices
):
    tokens, model = hidden.shape
    ff = up.shape[1]
    steps = ff // model
    seqs = parts.shape[0]
    small, share = model // devices, ff // devices
    direct = small % 8 == 0 and share % 16 == 0
    tail_rows = aligned(small + 8)
    single = pl.Buffered(1)
    whole = lambda *shape: pl.BlockSpec(
        shape, lambda t: (0,) * len(shape), pipeline_mode=single
    )
    anywhere = pl.BlockSpec(memory_space=pl.ANY)
    unused = (16, 128)
    slab_shape, down_shape, up_shape, tail_shape = (
        ((devices, 2 * share + tail_rows, model), unused, unused, unused) if direct
        else (unused, (ff, model), (model, ff), (devices, tail_rows, model))
    )
    layer_out, resid_grad, grads, first, slab, down_grad, up_grad, tail = pl.pallas_call(
        lambda *refs: block_kernel(direct, *refs),
        grid=(steps,),
        out_shape=(
            jax.ShapeDtypeStruct((tokens, model), BF16),
            jax.ShapeDtypeStruct((tokens, model), F32),
            jax.ShapeDtypeStruct(parts.shape, BF16),
            jax.ShapeDtypeStruct((3,) + parts.shape[2:], BF16),
            jax.ShapeDtypeStruct(slab_shape, BF16),
            jax.ShapeDtypeStruct(down_shape, BF16),
            jax.ShapeDtypeStruct(up_shape, BF16),
            jax.ShapeDtypeStruct(tail_shape, BF16),
        ),
        in_specs=[
            whole(*parts.shape), whole(tokens, model), whole(tokens, model), whole(model, model),
            whole(model), whole(model), whole(model), whole(model), whole(ff),
            pl.BlockSpec((model, model), lambda t: (0, t)),
            pl.BlockSpec((model, model), lambda t: (t, 0)),
            pl.BlockSpec((None, tokens, model), lambda t: (t, 0, 0)),
        ],
        out_specs=(
            whole(tokens, model), whole(tokens, model), anywhere, anywhere, anywhere, anywhere,
            anywhere, anywhere,
        ),
        scratch_shapes=[
            pltpu.VMEM((model, tokens), BF16),
            pltpu.VMEM((tokens, model), F32),
            pltpu.VMEM((tokens, model), BF16),
            pltpu.VMEM((model, tokens), BF16),
            pltpu.VMEM((tokens, model), F32),
            pltpu.VMEM((tokens, model), F32),
            pltpu.VMEM((steps, tokens, model), BF16),
            pltpu.VMEM((steps, tokens, model), BF16),
            pltpu.VMEM((8, model), F32),
            pltpu.VMEM((1, ff), F32),
            pltpu.VMEM((model, CHUNK), BF16),
            pltpu.VMEM(slab_shape, BF16),
            pltpu.VMEM(down_shape, BF16),
            pltpu.VMEM(up_shape, BF16),
            pltpu.VMEM(tail_shape, BF16),
            pltpu.VMEM(parts.shape, BF16),
            pltpu.VMEM((3,) + parts.shape[2:], BF16),
            pltpu.SemaphoreType.DMA((3,)),
            pltpu.SemaphoreType.DMA((3,)),
            pltpu.SemaphoreType.DMA((5,)),
        ],
        compiler_params=pltpu.CompilerParams(
            vmem_limit_bytes=VMEM, collective_id=3, has_side_effects=True
        ),
        cost_estimate=pl.CostEstimate(
            flops=26_000_000_000, bytes_accessed=30_000_000, transcendentals=0
        ),
        name="block_layer",
    )(parts, hidden, grad, out_w, out_b, gain, shift, down_b, up_b, up, down, act_grad)
    if not direct:
        fit = lambda a: jnp.pad(a, ((0, 0), (0, aligned(a.shape[1]) - a.shape[1]), (0, 0)))
        down_grad = fit(down_grad.reshape(devices, share, model))
        up_grad = up_grad.reshape(devices, small, ff // model, model).transpose(0, 2, 1, 3)
        up_grad = fit(up_grad.reshape(devices, ff // model * small, model))
        slab = jnp.concatenate([down_grad, up_grad, tail], axis=1)
    return layer_out, resid_grad, grads, first, slab


def attend_back_kernel(
    dp_size, x_ref, grads_ref, first_ref, weight, draws_ref, hot_ref, proj, state_ref, mixed_ref, den_ref,
    soft_ref, phi_q_ref, phi_k_ref, slab_any,
    attn_out, ring_out, proj_out,
    grad_scr, num_scr, value_scr, score_scr, exact_scr, proj_scr,
    grad_land, near_send, near_land, far_keep, far_send, far_land,
    mine, met, ring_land, cross_land,
    weight_acc, own_send, pair_land, own_mid, own_land, part_send, part_land,
    grad_sems, near_sems, far_sems, mine_sem, met_send, met_sems, ring_send, ring_sems, cross_sems,
    pair_sems, own_send_sem, own_sems,
    part_sems,
):
    s, h = pl.program_id(0), pl.program_id(1)
    seqs, heads = pl.num_programs(0), pl.num_programs(1)
    rows, model = x_ref.shape[1], x_ref.shape[2]
    head_count = proj_scr.shape[0] // (3 * HD)
    width = head_count * HD
    total = GROUP * rows
    root = 1.0 / math.sqrt(HD)
    own, me = lax.axis_index("feat"), lax.axis_index("dp")
    own_x, own_core = own // 2, own % 2
    near, across = {"feat": partner(own, 1)}, {"feat": partner(own, 2)}
    last = (s == seqs - 1) & (h == heads - 1)

    def grad_copy(q, r):
        return remote(
            grads_ref.at[q, r], grad_land.at[q - 1, r - 1], grad_sems.at[0, q - 1, r - 1],
            grad_sems.at[1, q - 1, r - 1], {"feat": partner(own, r)},
        )

    def near_copy(q, i):
        return remote(
            near_send.at[i], near_land.at[q, i], near_sems.at[0, q, i], near_sems.at[1, q, i], near
        )

    def far_copy(q):
        return remote(far_send, far_land.at[q], far_sems.at[0, q], far_sems.at[1, q], across)

    half = dp_size // 2
    parity, pair = lax.rem(me, 2), lax.div(me, 2)
    spot = pair + parity * (dp_size - 1 - 2 * pair)

    def at_spot(p):
        p = lax.rem(p + dp_size, dp_size)
        upper = lax.div(p, half)
        return 2 * p + upper * (2 * dp_size - 1 - 4 * p)

    places = ({"dp": at_spot(spot + 1)}, {"dp": at_spot(spot - 1)})

    def chunk(k, way):
        return at_spot(spot - 1 - k) if way == 0 else at_spot(spot + 1 + k)

    def mine_copy(k, way, owner):
        return pltpu.make_async_copy(
            slab_any.at[owner + own_core], mine.at[k, way], mine_sem.at[k, way]
        )

    def met_copy(k, way, owner):
        return remote(
            slab_any.at[owner + 1 - own_core], met.at[k, way], met_send, met_sems.at[k, way], near
        )

    cut = aligned(mine.shape[2] // 2)
    halves = (pl.ds(0, cut), pl.ds(cut, mine.shape[2] - cut))

    def ring_copy(k, way, part):
        return remote(
            mine.at[k, way, halves[part]], ring_land.at[k, way, halves[part]], ring_send,
            ring_sems.at[k, way, part], places[way],
        )

    def cross_copy(part):
        return remote(
            mine.at[dp_size - 1, 1 - own_x, halves[part]], cross_land.at[halves[part]],
            cross_sems.at[0, part], cross_sems.at[1, part], across,
        )

    def begin_pieces(k):
        for way in range(2):
            owner = chunk(k, way) * GROUP + 2 * way
            met_copy(k, way, owner).start()
            mine_copy(k, way, owner).start()

    def ring_step(k, part):
        span = halves[part]
        if part == 0:

            @pl.when(k + 2 < dp_size)
            def _():
                begin_pieces(k + 2)

        @pl.when(k < dp_size)
        def _():
            for way in range(2):
                if part == 0:
                    mine_copy(k, way, 0).wait()
                    met_copy(k, way, 0).wait_recv()

                @pl.when(k == 0)
                def _():
                    base = mine[k, way, span].astype(F32) + met[k, way, span].astype(F32)
                    mine[k, way, span] = base.astype(BF16)

                @pl.when(k > 0)
                def _():
                    ring_copy(k - 1, way, part).wait_recv()
                    base = mine[k, way, span].astype(F32) + met[k, way, span].astype(F32)
                    base = base + ring_land[k - 1, way, span].astype(F32)
                    mine[k, way, span] = base.astype(BF16)

                @pl.when(k < dp_size - 1)
                def _():
                    ring_copy(k, way, part).start()

            @pl.when(k == dp_size - 1)
            def _():
                cross_copy(part).start()

        @pl.when(k == dp_size)
        def _():
            cross_copy(part).wait_recv()
            ring_out[span] = mine[dp_size - 1, own_x, span].astype(F32) + cross_land[span].astype(F32)

    def ring_turn(part):
        turn = s * heads + h
        count = seqs * heads
        steps = dp_size + 1

        def body(k, carry):
            ring_step(k, part)
            return carry

        lax.fori_loop(lax.div(turn * steps, count), lax.div((turn + 1) * steps, count), body, 0)

    mate = me + 1 - 2 * parity

    def pair_copy(q):
        return remote(
            own_send.at[q, 1 - parity], pair_land.at[q], pair_sems.at[0, q], pair_sems.at[1, q],
            {"dp": mate},
        )

    def own_copy(q, k):
        to = lax.rem(pair + k, half)
        return remote(
            own_mid.at[q, to], own_land.at[q, k], own_send_sem, own_sems.at[q, k],
            {"dp": 2 * to + parity},
        )

    def begin_own(q):
        base = model // dp_size
        turned = weight_acc[pl.ds(pl.multiple_of(q * 3 * HD, 3 * HD), 3 * HD)].T
        fill = turned[model : model + own_send.shape[3] - base]
        for c in range(dp_size):
            own_send[q, c % 2, c // 2] = jnp.concatenate(
                [turned[c * base : (c + 1) * base], fill], axis=0
            ).astype(BF16)
        pair_copy(q).start()

    def relay_own(q):
        pair_copy(q).wait_recv()
        own_mid[q] = (own_send[q, parity].astype(F32) + pair_land[q].astype(F32)).astype(BF16)

        def start(k, carry):
            own_copy(q, k).start()
            return carry

        lax.fori_loop(1, half, start, 0)

    def part_copy(r):
        other = partner(own, r)
        return remote(
            part_send.at[other], part_land.at[r - 1], part_sems.at[0, r - 1],
            part_sems.at[1, r - 1], {"feat": other},
        )

    def seq_span(q):
        return pl.ds(pl.multiple_of(q * rows, rows), rows)

    def add_near(q):
        near_copy(q, 1).wait_recv()

        @pl.when(q > 0)
        def _():
            far_copy(q - 1).wait_send()

        far_send[...] = (far_keep[1] + near_land[q, 1].astype(F32)).astype(BF16)
        far_copy(q).start()
        near_copy(q, 0).wait_recv()
        attn_out[seq_span(q)] = far_keep[0] + near_land[q, 0].astype(F32)

    def finish(q):
        far_copy(q).wait_recv()
        span = seq_span(q)
        attn_out[span] = attn_out[span] + far_land[q].astype(F32)

    @pl.when((s == 0) & (h == 0))
    def _():
        barrier = pltpu.get_barrier_semaphore()
        for r in (1, 2, 3):
            pl.semaphore_signal(
                barrier, inc=1, device_id={"feat": partner(own, r)}, device_id_type=MESH
            )

        def greet(k, carry):
            pl.semaphore_signal(
                barrier, inc=1, device_id={"dp": lax.rem(me + k, dp_size)}, device_id_type=MESH
            )
            return carry

        lax.fori_loop(1, dp_size, greet, 0)
        pl.semaphore_wait(barrier, 3 + dp_size - 1)
        for q in range(1, near_land.shape[0]):
            for r in (2, 3, 1):
                grad_copy(q, r).start()
        for k in range(2):
            begin_pieces(k)
        weight_acc[...] = jnp.zeros_like(weight_acc)

    @pl.when(h == 0)
    def _():
        grad_scr[:, 0:rows] = grads_ref[s, 0].astype(F32)

        @pl.when(s == 0)
        def _():
            for r in (1, 2, 3):
                grad_scr[:, r * rows : (r + 1) * rows] = first_ref[r - 1].astype(F32)

        @pl.when(s > 0)
        def _():
            for r in (1, 2, 3):
                grad_copy(s, r).wait_recv()
                grad_scr[:, r * rows : (r + 1) * rows] = grad_land[s - 1, r - 1].astype(F32)

    query = proj[head_rows(h, 0, head_count)]
    key = proj[head_rows(h, 1, head_count)]
    value = proj[head_rows(h, 2, head_count)]
    draws = draws_ref[...]
    draws_ext = jnp.concatenate([draws, jnp.ones((16, FEAT), BF16)], axis=0)
    hot = hot_ref[...]
    away_wide = away_marks(hot)
    away = away_wide.astype(BF16)
    inverse = 1.0 / den_ref[0:1]
    head_grad = grad_scr[pl.ds(pl.multiple_of(h * HD, HD), HD)]
    grad_num = (head_grad * inverse).astype(BF16)
    grad_den = -jnp.sum(head_grad * mixed_ref[...], axis=0, keepdims=True) * inverse
    den_rows = jnp.broadcast_to(grad_den, (16, total)).astype(BF16)
    spread_grad = jnp.concatenate(spread(grad_num, hot) + [den_rows * hot], axis=0)
    spread_value = jnp.concatenate(spread(value, away) + [away], axis=0)

    phi_q, phi_k = phi_q_ref[...], phi_k_ref[...]
    state_grad = mat_nt(spread_grad, phi_q).astype(BF16)
    phi_q_grad = mat_tn(state_ref[...], spread_grad)
    phi_k_grad = mat_tn(state_grad, spread_value)
    value_low = mat(state_grad[0 : NBUCK * HD], phi_k)
    scaled_q = (phi_q_grad * phi_q.astype(F32)).astype(BF16)
    back_q = mat(draws_ext, scaled_q)
    scaled_k = (phi_k_grad * phi_k.astype(F32)).astype(BF16)
    back_k = mat(draws_ext, scaled_k)
    value_grad = pick(value_low, away_wide)
    query_grad = back_q[0:HD] - query.astype(F32) * (back_q[HD : HD + 1] * root)
    key_grad = back_k[0:HD] - key.astype(F32) * (back_k[HD : HD + 1] * root)

    ring_turn(0)
    one = (lax.broadcasted_iota(jnp.int32, hot.shape, 0) < 1).astype(F32).astype(BF16)
    num_scr[...] = jnp.concatenate([grad_num, den_rows], axis=0)
    value_scr[...] = jnp.concatenate([value, one], axis=0).astype(F32).T.astype(BF16)

    later = mat(value_scr[...], num_scr[:, 0:CHUNK])
    for c in range(total // CHUNK):
        cols = slice(c * CHUNK, (c + 1) * CHUNK)
        ahead = slice((c + 1) * CHUNK, (c + 2) * CHUNK)
        score = later
        later = mat(value_scr[...], num_scr[:, ahead]) if ahead.stop <= total else None
        score = (score * soft_ref[:, cols].astype(F32)).astype(BF16)
        score_scr[:, cols] = score
        exact_scr[:, cols] = mat(proj[head_rows(h, 1, head_count)], score)
    query_grad = query_grad + exact_scr[...] * root
    key_grad = key_grad + mat_nt(query, score_scr[...]) * root
    value_grad = value_grad + mat_nt(grad_num, soft_ref[...])
    wide_grad = jnp.concatenate([query_grad, key_grad, value_grad], axis=0)
    low_grad = wide_grad.astype(BF16)
    for kind in range(3):
        proj_scr[head_rows(h, kind, head_count)] = low_grad[kind * HD : (kind + 1) * HD]
    weight_grad = mat(low_grad[:, 0:rows], x_ref[0])
    for r in (1, 2, 3):
        weight_grad = weight_grad + mat(low_grad[:, r * rows : (r + 1) * rows], x_ref[r])
    span = pl.ds(pl.multiple_of(h * 3 * HD, 3 * HD), 3 * HD)
    weight_acc[span, 0:model] += weight_grad
    weight_acc[span, model:] += jnp.broadcast_to(
        jnp.sum(wide_grad, axis=1, keepdims=True), (3 * HD, 128)
    )

    @pl.when((s > 0) & (h == 0))
    def _():
        add_near(s - 1)

    @pl.when(h == heads - 1)
    def _():
        @pl.when(s > 0)
        def _():
            for i in range(2):
                near_copy(s - 1, i).wait_send()

        for r in (3, 1, 2, 0):
            term = mat_tn(proj_scr[:, r * rows : (r + 1) * rows], weight[...])
            if r % 2:
                near_send[r // 2] = term.astype(BF16)
                near_copy(s, r // 2).start()
            else:
                far_keep[r // 2] = term

    @pl.when(s == seqs - 1)
    def _():
        begin_own(h)

        @pl.when(h > 0)
        def _():
            relay_own(h - 1)

    ring_turn(1)

    @pl.when(last)
    def _():
        add_near(s)
        relay_own(h)
        for q in range(near_land.shape[0] - 1):
            finish(q)

        sums = []
        for q in range(head_count):

            def arrive(k, carry):
                own_copy(q, k).wait_recv()
                return carry + own_land[q, k].astype(F32)

            sums.append(lax.fori_loop(1, half, arrive, own_mid[q, pair].astype(F32)))
        joined = jnp.concatenate(sums, axis=1)
        base = model // dp_size
        small = base // GROUP
        fill = jnp.broadcast_to(
            joined[base : base + 1], (part_send.shape[1] - small, joined.shape[1])
        )
        for a in range(GROUP):
            part_send[a] = jnp.concatenate(
                [joined[a * small : (a + 1) * small], fill], axis=0
            ).astype(BF16)
        for r in (2, 3, 1):
            part_copy(r).start()
        finish(s)
        proj_out[own] = part_send[own].astype(F32)
        for r in (1, 2, 3):
            part_copy(r).wait_recv()
            proj_out[partner(own, r)] = part_land[r - 1].astype(F32)

        for i in range(2):
            near_copy(s, i).wait_send()
        far_copy(s).wait_send()
        for r in (1, 2, 3):
            part_copy(r).wait_send()
        for part in range(2):
            cross_copy(part).wait_send()
        for q in range(1, near_land.shape[0]):
            for r in (1, 2, 3):
                grad_copy(q, r).wait_send()
        for q in range(head_count):
            pair_copy(q).wait_send()
        every = pl.ds(0, half - 1)
        if half > 1:
            remote(
                own_mid.at[:, every], own_land.at[:, every], own_send_sem, own_sems.at[0, 0],
                {"dp": mate},
            ).wait_send()
        remote(
            mine.at[pl.ds(0, dp_size - 1)], ring_land, ring_send, ring_sems.at[0, 0, 0], places[0]
        ).wait_send()
        remote(mine, met, met_send, met_sems.at[0, 0], near).wait_send()


def attend_back(
    dp_size, parts, grads, first, weight, draws, hot, proj, state, mixed, den, soft, phi_q, phi_k,
    slab,
):
    seqs, _, rows, model = parts.shape
    heads = draws.shape[0]
    width = heads * HD
    total = GROUP * rows
    n = dp_size
    ring_rows = slab.shape[1]
    own_rows = aligned(model // n + 1)
    part_rows = aligned(model // (n * GROUP) + 1)
    single = pl.Buffered(1)
    whole = lambda *shape: pl.BlockSpec(
        shape, lambda s, h: (0,) * len(shape), pipeline_mode=single
    )
    mode = single if n > 16 else None
    by_seq = lambda *shape: pl.BlockSpec(
        (None,) + shape, lambda s, h: (s,) + (0,) * len(shape), pipeline_mode=mode
    )
    by_head = lambda *shape: pl.BlockSpec(
        (None, None) + shape, lambda s, h: (s, h) + (0,) * len(shape), pipeline_mode=mode
    )
    anywhere = pl.BlockSpec(memory_space=pl.ANY)
    dma = pltpu.SemaphoreType.DMA
    return pl.pallas_call(
        lambda *refs: attend_back_kernel(dp_size, *refs),
        grid=(seqs, heads),
        out_shape=(
            jax.ShapeDtypeStruct((seqs * rows, model), F32),
            jax.ShapeDtypeStruct((ring_rows, model), F32),
            jax.ShapeDtypeStruct((GROUP, part_rows, 3 * width), F32),
        ),
        in_specs=[
            by_seq(GROUP, rows, model), whole(*grads.shape), whole(*first.shape),
            whole(3 * width, model),
            pl.BlockSpec((None, HD, FEAT), lambda s, h: (h, 0, 0)),
            by_seq(16, total), by_seq(3 * width, total), by_head(STATES, FEAT), by_head(HD, total),
            by_head(8, total), by_head(total, total), by_head(FEAT, total), by_head(FEAT, total),
            anywhere,
        ],
        out_specs=(
            whole(seqs * rows, model), whole(ring_rows, model), whole(GROUP, part_rows, 3 * width),
        ),
        scratch_shapes=[
            pltpu.VMEM((width, total), F32),
            pltpu.VMEM((HD + 16, total), BF16),
            pltpu.VMEM((total, HD + 16), BF16),
            pltpu.VMEM((total, total), BF16),
            pltpu.VMEM((HD, total), F32),
            pltpu.VMEM((3 * width, total), BF16),
            pltpu.VMEM((seqs - 1, 3, width, rows), BF16),
            pltpu.VMEM((2, rows, model), BF16),
            pltpu.VMEM((seqs, 2, rows, model), BF16),
            pltpu.VMEM((2, rows, model), F32),
            pltpu.VMEM((rows, model), BF16),
            pltpu.VMEM((seqs, rows, model), BF16),
            pltpu.VMEM((n, 2, ring_rows, model), BF16),
            pltpu.VMEM((n, 2, ring_rows, model), BF16),
            pltpu.VMEM((n - 1, 2, ring_rows, model), BF16),
            pltpu.VMEM((ring_rows, model), BF16),
            pltpu.VMEM((3 * width, model + 128), F32),
            pltpu.VMEM((heads, 2, n // 2, own_rows, 3 * HD), BF16),
            pltpu.VMEM((heads, n // 2, own_rows, 3 * HD), BF16),
            pltpu.VMEM((heads, n // 2, own_rows, 3 * HD), BF16),
            pltpu.VMEM((heads, n // 2, own_rows, 3 * HD), BF16),
            pltpu.VMEM((GROUP, part_rows, 3 * width), BF16),
            pltpu.VMEM((3, part_rows, 3 * width), BF16),
            dma((2, seqs - 1, 3)),
            dma((2, seqs, 2)),
            dma((2, seqs)),
            dma((n, 2)),
            dma,
            dma((n, 2)),
            dma,
            dma((n - 1, 2, 2)),
            dma((2, 2)),
            dma((2, heads)),
            dma,
            dma((heads, n // 2)),
            dma((2, 3)),
        ],
        compiler_params=pltpu.CompilerParams(
            vmem_limit_bytes=VMEM + (3 * 1024 * 1024 if n > 16 else 0), collective_id=2, has_side_effects=True
        ),
        cost_estimate=pl.CostEstimate(
            flops=48_000_000_000, bytes_accessed=40_000_000, transcendentals=0
        ),
        name="attend_back",
    )(
        parts, grads, first, weight, draws, hot, proj, state, mixed, den, soft, phi_q, phi_k, slab,
    )


def finish_kernel(
    starts, heads, attn_grad, resid_grad, hidden, sums, proj_sums, weight_any, gain_ref, shift_ref,
    input_out, norm1_gain_out, norm1_bias_out, qkv_out, qkv_bias_out, out_out, out_bias_out,
    norm2_gain_out, norm2_bias_out, up_out, up_bias_out, down_out, down_bias_out,
    weight_vm, weight_sem,
):
    gain, shift = as_row(gain_ref), as_row(shift_ref)
    index = lax.axis_index("dp") * GROUP + lax.axis_index("feat")
    small, model = out_out.shape
    window = weight_vm.shape[0]
    begin = jnp.minimum(lax.div(index * small, 16) * 16, model - window)
    weight_copy = pltpu.make_async_copy(
        weight_any.at[pl.ds(pl.multiple_of(begin, 16), window)], weight_vm, weight_sem
    )

    @pl.when(pl.program_id(0) == 0)
    def _():
        weight_copy.start()

    normed, scale = row_stats(hidden[...].astype(F32))
    input_out[...] = resid_grad[...] + norm_back(attn_grad[...] * gain, normed, scale)

    @pl.when(pl.program_id(0) == 0)
    def _():
        share = down_out.shape[0]
        ff = up_out.shape[1]

        def own(row, size):
            length = row.shape[1]
            wide = jnp.broadcast_to(row, (8, length))
            back = lax.rem(length - lax.rem(index * size, length), length)
            return pltpu.roll(wide, back, 1)[0:1, 0:size]

        down_out[...] = sums[0:share]
        first = starts[0]
        up_out[...] = jnp.concatenate(
            [sums[first + i * small : first + (i + 1) * small] for i in range(ff // model)], axis=1
        )
        first = starts[1]
        out_out[...] = sums[first : first + small]
        totals = first + small
        for i, out in enumerate((down_bias_out, out_bias_out, norm2_gain_out, norm2_bias_out)):
            out[...] = own(sums[totals + i : totals + i + 1], small).reshape(small)
        per_row = model // share
        level = index // per_row
        row = jnp.zeros((1, model), F32)
        for i in range(ff // model):
            row = jnp.where(level == i, sums[totals + 4 + i : totals + 5 + i], row)
        up_bias_out[...] = own(row, share).reshape(share)

        pieces = []
        for kind in range(3):
            for f in range(GROUP):
                for h in range(heads):
                    lanes = slice((h * 3 + kind) * HD, (h * 3 + kind + 1) * HD)
                    pieces.append(proj_sums[f, 0 : small + 1, lanes])
        grid = jnp.concatenate(pieces, axis=1)
        weight_sum, bias_sum = grid[0:small], grid[small : small + 1]
        qkv_out[...] = weight_sum
        qkv_bias_out[...] = own(bias_sum, 3 * small).reshape(3 * small)
        weight_copy.wait()
        near_rows = weight_vm[...].astype(F32)
        step = math.gcd(small, 16)
        wide = near_rows[0:small]
        for offset in range(step, window - small + 1, step):
            wide = jnp.where(
                index * small - begin == offset, near_rows[offset : offset + small], wide
            )

        def to_row(column):
            column = jnp.concatenate(
                [column, jnp.zeros((-small % 128, 1), F32)], axis=0
            )
            return jnp.broadcast_to(column, (column.shape[0], 128)).T[0:1, 0:small]

        bias_grad = to_row(jnp.sum(wide * bias_sum, axis=1, keepdims=True))
        gain_grad = to_row(jnp.sum(wide * weight_sum, axis=1, keepdims=True))
        norm1_bias_out[...] = bias_grad.reshape(small)
        gain_grad = (gain_grad - own(shift, small) * bias_grad) / own(gain, small)
        norm1_gain_out[...] = gain_grad.reshape(small)


def finish_all(
    attn_grad, resid_grad, hidden, sums, proj_sums, weight, gain, shift, devices, ff, heads,
):
    seqs, rows, model = hidden.shape
    small, share = model // devices, ff // devices
    starts = (aligned(share), 2 * aligned(share))
    whole = lambda *shape: pl.BlockSpec(shape, lambda s: (0,) * len(shape))
    by_seq = pl.BlockSpec((rows, model), lambda s: (s, 0))
    shapes = (
        (small,), (small,), (small, 3 * model), (3 * small,), (small, model), (small,), (small,),
        (small,), (small, ff), (share,), (share, model), (small,),
    )
    return pl.pallas_call(
        lambda *refs: finish_kernel(starts, heads, *refs),
        grid=(seqs,),
        out_shape=(jax.ShapeDtypeStruct((seqs * rows, model), F32),)
        + tuple(jax.ShapeDtypeStruct(shape, F32) for shape in shapes),
        in_specs=[
            by_seq, by_seq, pl.BlockSpec((None, rows, model), lambda s: (s, 0, 0)),
            whole(*sums.shape), whole(*proj_sums.shape), pl.BlockSpec(memory_space=pl.ANY), whole(model),
            whole(model),
        ],
        out_specs=(by_seq,) + tuple(whole(*shape) for shape in shapes),
        scratch_shapes=[
            pltpu.VMEM((aligned(small) + 16, 3 * model), BF16), pltpu.SemaphoreType.DMA,
        ],
        compiler_params=pltpu.CompilerParams(vmem_limit_bytes=VMEM),
        name="finish_all",
    )(attn_grad, resid_grad, hidden, sums, proj_sums, weight, gain, shift)


def per_device(
    hidden_in, norm1_gain, norm1_bias, qkv_weight, qkv_bias, feature_draws, out_weight, out_bias,
    norm2_gain, norm2_bias, up_weight, up_bias, down_weight, down_bias, block_bucket, out_grad,
):
    seqs, rows, model = hidden_in.shape
    ff = up_weight.shape[1]
    dp_size = lax.axis_size("dp")
    devices = dp_size * GROUP
    heads = feature_draws.shape[0] // GROUP
    flat = (seqs * rows, model)

    (
        parts, mixed_parts, act_grad, proj, state, mixed, den, hot, own_weight, own_draws, soft,
        phi_q, phi_k,
    ) = attend(
        block_bucket, hidden_in, norm1_gain, norm1_bias, qkv_bias, qkv_weight, feature_draws,
        out_grad, down_weight,
    )
    layer_out, resid_grad, grads, first, slab = block_layer(
        mixed_parts, hidden_in.reshape(flat), out_grad.reshape(flat), out_weight, out_bias,
        norm2_gain, norm2_bias, down_bias, up_bias, up_weight, down_weight, act_grad, devices,
    )
    attn_grad, sums, proj_sums = attend_back(
        dp_size, parts, grads, first, own_weight, own_draws, hot, proj, state, mixed, den, soft,
        phi_q, phi_k, slab,
    )
    (
        input_grad, norm1_gain_sum, norm1_bias_sum, qkv_weight_sum, qkv_bias_sum, out_weight_sum,
        out_bias_sum, norm2_gain_sum, norm2_bias_sum, up_sum, up_bias_sum, down_sum, down_bias_sum,
    ) = finish_all(
        attn_grad, resid_grad, hidden_in, sums, proj_sums, qkv_weight, norm1_gain, norm1_bias,
        devices, ff, heads,
    )
    return (
        layer_out.reshape(hidden_in.shape), input_grad.reshape(hidden_in.shape), norm1_gain_sum,
        norm1_bias_sum, qkv_weight_sum, qkv_bias_sum, out_weight_sum, out_bias_sum, norm2_gain_sum,
        norm2_bias_sum, up_sum, up_bias_sum, down_sum, down_bias_sum,
    )


def solution(mesh):
    both = ("dp", "feat")
    rows = P("dp", "feat", None)
    in_specs = (
        rows, P(), P(), P(), P(), P(None, None, "feat"), P(), P(), P(), P(), P(), P(), P(), P(),
        P("dp", None, None), rows,
    )
    out_specs = (
        rows, rows, P(both), P(both), P(both, None), P(both), P(both, None), P(both), P(both),
        P(both), P(both, None), P(both), P(both, None), P(both),
    )
    return jax.shard_map(
        per_device, mesh=mesh, in_specs=in_specs, out_specs=out_specs, check_vma=False
    )
```

```python
import math

import jax
import jax.numpy as jnp
from jax import lax
from jax.experimental import pallas as pl
from jax.experimental.pallas import tpu as pltpu
from jax.sharding import PartitionSpec as P

HD = 64
FEAT = 256
BLOCK = 64
NBUCK = 4
GROUP = 4
CHUNK = 256
STATES = NBUCK * HD + 16
FAR = 16384.0
VMEM = 60 * 1024 * 1024

F32 = jnp.float32
BF16 = jnp.bfloat16
MESH = pl.DeviceIdType.MESH


def mat(left, right):
    return jnp.dot(left, right, preferred_element_type=F32)


def mat_nt(left, right):
    return lax.dot_general(left, right, (((1,), (1,)), ((), ())), preferred_element_type=F32)


def mat_tn(left, right):
    return lax.dot_general(left, right, (((0,), (0,)), ((), ())), preferred_element_type=F32)


def row_stats(values):
    row_mean = jnp.mean(values, axis=-1, keepdims=True)
    centered = values - row_mean
    scale = lax.rsqrt(jnp.mean(centered * centered, axis=-1, keepdims=True) + 1e-05)
    return (centered * scale, scale)


def norm_back(cotangent, normed, scale):
    mean_one = jnp.mean(cotangent, axis=-1, keepdims=True)
    mean_two = jnp.mean(cotangent * normed, axis=-1, keepdims=True)
    return scale * (cotangent - mean_one - normed * mean_two)


def features(vectors, draws):
    wide = vectors.astype(F32)
    square = jnp.sum(wide * wide, axis=0, keepdims=True) * (0.5 / math.sqrt(HD))
    return jnp.exp(mat_tn(draws, vectors) - (square + 0.5 * math.log(FEAT)))


def spread(rows, marks):
    return [rows * marks[u : u + 1] for u in range(NBUCK)]


def pick(stacked, marks):
    total = stacked[0:HD] * marks[0:1]
    for u in range(1, NBUCK):
        total = total + stacked[u * HD : (u + 1) * HD] * marks[u : u + 1]
    return total


def away_marks(hot):
    live = (lax.broadcasted_iota(jnp.int32, hot.shape, 0) < NBUCK).astype(F32)
    return live - hot.astype(F32)


def partner(own, r):
    x, core = own // 2, own % 2
    if r & 2:
        x = 1 - x
    if r & 1:
        core = 1 - core
    return 2 * x + core


def as_row(ref):
    return ref[...].reshape(1, ref.shape[0])


def aligned(count):
    return -(-count // 16) * 16


def remote(src, dst, send, recv, place):
    return pltpu.make_async_remote_copy(
        src_ref=src, dst_ref=dst, send_sem=send, recv_sem=recv, device_id=place, device_id_type=MESH
    )


def head_rows(h, kind, heads):
    return pl.ds(pl.multiple_of((kind * heads + h) * HD, HD), HD)


def attend_kernel(
    bucket, hidden, gain_ref, shift_ref, bias_ref, weight_any, draws_in, grad, down_any,
    parts_any, mix_any, act_grad_any, proj_out, state_out, mixed_out, den_out, hot_out, weight_out, draws_out,
    soft_out, phi_q_out, phi_k_out,
    parts, mix_land, mix_send, raw, bias_row, bias_scr, draws_land, down_vm, act_grad,
    query_scr, key_scr, value_scr, low_scr,
    raw_sem, part_send, part_recv, draw_send, draw_recv, mix_send_sem, mix_recv_sem, out_sem,
    down_sem, act_sem,
):
    s, h = pl.program_id(0), pl.program_id(1)
    seqs, rows, model = hidden.shape
    heads = draws_out.shape[0]
    total = GROUP * rows
    width = heads * HD
    own = lax.axis_index("feat")
    near, across = {"feat": partner(own, 1)}, {"feat": partner(own, 2)}

    def part_copy(q, kind):
        src, dst, place = ((0, 1, near), (0, 2, across), (2, 3, near))[kind]
        return remote(
            parts.at[q, src], parts.at[q, dst], part_send.at[q, kind], part_recv.at[q, kind], place
        )

    def draw_copy(r):
        other = partner(own, r)
        return remote(
            draws_in.at[pl.ds(other * heads, heads)], draws_land.at[r - 1],
            draw_send.at[r - 1], draw_recv.at[r - 1], {"feat": other},
        )

    def mix_copy(q, g, r):
        span = pl.ds(pl.multiple_of(g * HD, HD), HD)
        return remote(
            mix_send.at[q, r - 1, span], mix_land.at[q, r, span], mix_send_sem.at[q, g, r - 1],
            mix_recv_sem.at[q, g, r - 1], {"feat": partner(own, r)},
        )

    down_copy = pltpu.make_async_copy(down_any, down_vm, down_sem)
    act_copy = pltpu.make_async_copy(act_grad, act_grad_any, act_sem)

    def raw_copy(j):
        cols = pl.ds(pl.multiple_of(j * model + (own // 2) * 2 * width, 2 * width), 2 * width)
        return pltpu.make_async_copy(weight_any.at[:, cols], raw.at[j], raw_sem.at[j])

    def out_copy(q):
        return pltpu.make_async_copy(parts.at[q], parts_any.at[q], out_sem.at[q])

    @pl.when((s == 0) & (h == 0))
    def _():
        for j in range(3):
            raw_copy(j).start()
        down_copy.start()
        barrier = pltpu.get_barrier_semaphore()
        for r in (1, 2, 3):
            pl.semaphore_signal(
                barrier, inc=1, device_id={"feat": partner(own, r)}, device_id_type=MESH
            )
        gain, shift = as_row(gain_ref), as_row(shift_ref)
        first = row_stats(hidden[0].astype(F32))[0] * gain + shift
        parts[0, 0] = first.astype(BF16)
        pl.semaphore_wait(barrier, 3)
        part_copy(0, 1).start()
        part_copy(0, 0).start()
        for r in (1, 2, 3):
            draw_copy(r).start()
        for q in range(1, seqs):
            normed = row_stats(hidden[q].astype(F32))[0] * gain + shift
            parts[q, 0] = normed.astype(BF16)
            part_copy(q, 1).start()
            part_copy(q, 0).start()
        core = own % 2
        bias_row[...] = as_row(bias_ref)
        for j in range(3):
            raw_copy(j).wait()
            piece = raw[j].astype(F32)
            piece = jnp.where(core == 0, piece[:, 0:width], piece[:, width:])
            weight_out[j * width : (j + 1) * width] = piece.T.astype(BF16)
            cols = pl.ds(pl.multiple_of(j * model + (own // 2) * 2 * width, 2 * width), 2 * width)
            pair = jnp.broadcast_to(bias_row[:, cols], (128, 2 * width))
            pair = jnp.where(core == 0, pair[:, 0:width], pair[:, width:])
            bias_scr[j * width : (j + 1) * width] = pair.T
        down_copy.wait()
        for t in range(act_grad.shape[0]):
            tile = down_vm[t * model : (t + 1) * model]
            act_grad[t] = mat_nt(grad[...], tile).astype(BF16)
        act_copy.start()
        part_copy(0, 1).wait_recv()
        part_copy(0, 2).start()
        for r in (1, 2, 3):
            draw_copy(r).wait_recv()
        mine = draws_in[pl.ds(own * heads, heads)]
        draws_out[...] = jnp.concatenate(
            [mine] + [draws_land[r - 1] for r in (1, 2, 3)], axis=2
        )

    @pl.when(h == 0)
    def _():
        per = rows // BLOCK
        lanes = lax.broadcasted_iota(jnp.int32, (16, total), 1) // BLOCK
        level = lax.broadcasted_iota(jnp.int32, (16, total), 0)
        ids = jnp.full((16, total), -1, jnp.int32)
        for r in range(GROUP):
            for i in range(per):
                ids = jnp.where(
                    lanes == r * per + i, bucket[s, partner(own, r) * per + i, 0], ids
                )
        hot_out[...] = (ids == level).astype(F32).astype(BF16)

        def project(r):
            cols = slice(r * rows, (r + 1) * rows)
            piece = mat_nt(weight_out[...], parts[s, r]) + bias_scr[:, 0:1]
            proj_out[:, cols] = piece.astype(BF16)

        project(0)
        part_copy(s, 0).wait_recv()
        project(1)
        project(2)
        part_copy(s, 2).wait_recv()
        project(3)
        out_copy(s).start()

    query = proj_out[head_rows(h, 0, heads)]
    key = proj_out[head_rows(h, 1, heads)]
    value = proj_out[head_rows(h, 2, heads)]
    draws = draws_out[h]
    hot = hot_out[...]
    hot_wide = hot.astype(F32)
    away = away_marks(hot).astype(BF16)
    phi_q = features(query, draws).astype(BF16)
    phi_k = features(key, draws).astype(BF16)
    phi_q_out[...] = phi_q
    phi_k_out[...] = phi_k
    spread_value = jnp.concatenate(spread(value, away) + [away], axis=0)
    state = mat_nt(spread_value, phi_k).astype(BF16)
    state_out[...] = state
    low = mat(state, phi_q)
    low_scr[0:HD] = pick(low, hot_wide)
    low_den = jnp.sum(low[NBUCK * HD :] * hot_wide, axis=0, keepdims=True)
    low_scr[HD : HD + 8] = jnp.broadcast_to(low_den, (8, total))
    query_scr[...] = jnp.concatenate([query * (1.0 / math.sqrt(HD)), hot], axis=0).astype(BF16)
    key_scr[...] = jnp.concatenate([key, away * -FAR], axis=0).astype(F32).T.astype(BF16)
    value_scr[0:HD] = value
    value_scr[HD:] = jnp.ones((16, total), BF16)

    head_span = pl.ds(pl.multiple_of(h * HD, HD), HD)
    score = mat(key_scr[...], query_scr[:, 0:CHUNK])
    for c in range(total // CHUNK):
        cols = slice(c * CHUNK, (c + 1) * CHUNK)
        ahead = slice((c + 1) * CHUNK, (c + 2) * CHUNK)
        later = mat(key_scr[...], query_scr[:, ahead]) if ahead.stop <= total else None
        weights = jnp.exp(score).astype(BF16)
        score = later
        soft_out[:, cols] = weights
        exact = mat(value_scr[...], weights)
        den = low_scr[HD : HD + 8, cols] + exact[HD : HD + 8]
        mixed = (low_scr[0:HD, cols] + exact[0:HD]) / den[0:1]
        mixed_out[:, cols] = mixed
        den_out[:, cols] = den
        mixed_low = mixed.astype(BF16)
        for r in range(GROUP):
            low_col, high_col = max(cols.start, r * rows), min(cols.stop, (r + 1) * rows)
            if low_col < high_col:
                piece = mixed_low[:, low_col - cols.start : high_col - cols.start]
                inner = slice(low_col - r * rows, high_col - r * rows)
                if r:
                    mix_send[s, r - 1, head_span, inner] = piece
                else:
                    mix_land[s, 0, head_span, inner] = piece
    for r in (2, 3, 1):
        mix_copy(s, h, r).start()

    @pl.when((h == heads - 2) & (s < seqs - 1))
    def _():
        part_copy(s + 1, 1).wait_recv()
        part_copy(s + 1, 2).start()

    @pl.when((s == seqs - 1) & (h == heads - 1))
    def _():
        for q in range(seqs):
            for g in range(heads):
                for r in (1, 2, 3):
                    mix_copy(q, g, r).wait_recv()
        done = pltpu.make_async_copy(mix_land, mix_any, out_sem.at[seqs])
        done.start()
        for q in range(seqs):
            for kind in range(3):
                part_copy(q, kind).wait_send()
            for g in range(heads):
                for r in (1, 2, 3):
                    mix_copy(q, g, r).wait_send()
            out_copy(q).wait()
        act_copy.wait()
        for r in (1, 2, 3):
            draw_copy(r).wait_send()
        done.wait()


def attend(bucket, hidden, gain, shift, bias, weight, draws, grad, down):
    seqs, rows, model = hidden.shape
    tiles = down.shape[0] // model
    heads = draws.shape[0] // GROUP
    width = heads * HD
    total = GROUP * rows
    whole = lambda *shape: pl.BlockSpec(shape, lambda s, h: (0,) * len(shape))
    by_seq = lambda *shape: pl.BlockSpec((None,) + shape, lambda s, h: (s,) + (0,) * len(shape))
    by_head = lambda *shape: pl.BlockSpec(
        (None, None) + shape, lambda s, h: (s, h) + (0,) * len(shape)
    )
    anywhere = pl.BlockSpec(memory_space=pl.ANY)
    return pl.pallas_call(
        attend_kernel,
        grid=(seqs, heads),
        out_shape=(
            jax.ShapeDtypeStruct((seqs, GROUP, rows, model), BF16),
            jax.ShapeDtypeStruct((seqs, GROUP, width, rows), BF16),
            jax.ShapeDtypeStruct((tiles, seqs * rows, model), BF16),
            jax.ShapeDtypeStruct((seqs, 3 * width, total), BF16),
            jax.ShapeDtypeStruct((seqs, heads, STATES, FEAT), BF16),
            jax.ShapeDtypeStruct((seqs, heads, HD, total), F32),
            jax.ShapeDtypeStruct((seqs, heads, 8, total), F32),
            jax.ShapeDtypeStruct((seqs, 16, total), BF16),
            jax.ShapeDtypeStruct((3 * width, model), BF16),
            jax.ShapeDtypeStruct((heads, HD, FEAT), BF16),
            jax.ShapeDtypeStruct((seqs, heads, total, total), BF16),
            jax.ShapeDtypeStruct((seqs, heads, FEAT, total), BF16),
            jax.ShapeDtypeStruct((seqs, heads, FEAT, total), BF16),
        ),
        in_specs=[
            pl.BlockSpec(memory_space=pltpu.SMEM),
            whole(seqs, rows, model), whole(model), whole(model), whole(3 * model), anywhere,
            whole(*draws.shape), whole(seqs * rows, model), anywhere,
        ],
        out_specs=(
            anywhere, anywhere, anywhere, by_seq(3 * width, total), by_head(STATES, FEAT), by_head(HD, total),
            by_head(8, total), by_seq(16, total), whole(3 * width, model), whole(heads, HD, FEAT),
            by_head(total, total), by_head(FEAT, total), by_head(FEAT, total),
        ),
        scratch_shapes=[
            pltpu.VMEM((seqs, GROUP, rows, model), BF16),
            pltpu.VMEM((seqs, GROUP, width, rows), BF16),
            pltpu.VMEM((seqs, 3, width, rows), BF16),
            pltpu.VMEM((3, model, 2 * width), BF16),
            pltpu.VMEM((1, 3 * model), F32),
            pltpu.VMEM((3 * width, 128), F32),
            pltpu.VMEM((3, heads, HD, draws.shape[2]), BF16),
            pltpu.VMEM(down.shape, BF16),
            pltpu.VMEM((tiles, seqs * rows, model), BF16),
            pltpu.VMEM((HD + 16, total), BF16),
            pltpu.VMEM((total, HD + 16), BF16),
            pltpu.VMEM((HD + 16, total), BF16),
            pltpu.VMEM((HD + 8, total), F32),
            pltpu.SemaphoreType.DMA((3,)),
            pltpu.SemaphoreType.DMA((seqs, 3)),
            pltpu.SemaphoreType.DMA((seqs, 3)),
            pltpu.SemaphoreType.DMA((3,)),
            pltpu.SemaphoreType.DMA((3,)),
            pltpu.SemaphoreType.DMA((seqs, heads, 3)),
            pltpu.SemaphoreType.DMA((seqs, heads, 3)),
            pltpu.SemaphoreType.DMA((seqs + 1,)),
            pltpu.SemaphoreType.DMA,
            pltpu.SemaphoreType.DMA,
        ],
        compiler_params=pltpu.CompilerParams(
            vmem_limit_bytes=VMEM, collective_id=1, has_side_effects=True
        ),
        cost_estimate=pl.CostEstimate(
            flops=24_000_000_000, bytes_accessed=20_000_000, transcendentals=0
        ),
        name="attend",
    )(bucket, hidden, gain, shift, bias, weight, draws, grad, down)


def block_kernel(
    direct, parts_ref, hidden, grad, out_w, out_b, gain_ref, shift_ref, down_b, up_b, up, down,
    act_grad_ref,
    layer_out, resid_out, grads_any, first_any, slab_any, down_any, up_any, tail_any,
    mixed_t, resid_scr, in_scr, in_t, acc_out, acc_in, act_scr, pre_scr, vec_scr, bias_row, back_t, pre_scr32,
    slab_vm, down_vm, up_vm, tail_vm, grads_vm, first_land, send_sem, recv_sem, out_sem,
):
    step = pl.program_id(0)
    model = hidden.shape[1]
    count = hidden.shape[0] // CHUNK
    tiles = act_scr.shape[0]
    spans = [slice(c * CHUNK, (c + 1) * CHUNK) for c in range(count)]
    owners = slab_vm.shape[0] if direct else tail_vm.shape[0]
    small = model // owners
    share = tiles * small
    own = lax.axis_index("feat")
    barrier = pltpu.get_barrier_semaphore()

    part = model // GROUP

    def group_rows(r):
        return pl.ds(pl.multiple_of(partner(own, r) * part, part), part)

    def grad_copy(r):
        return remote(
            grads_vm.at[0, r], first_land.at[r - 1], send_sem.at[r - 1], recv_sem.at[r - 1],
            {"feat": partner(own, r)},
        )

    def out_copy(i):
        pieces = [(down_vm, down_any), (up_vm, up_any), (tail_vm, tail_any)]
        if direct:
            cuts = (0, share, 2 * share, slab_vm.shape[1])
            pieces = [
                (slab_vm.at[:, pl.ds(low, high - low)], slab_any.at[:, pl.ds(low, high - low)])
                for low, high in zip(cuts, cuts[1:])
            ]
        src, dst = (
            *pieces, (grads_vm, grads_any), (first_land, first_any),
        )[i]
        return pltpu.make_async_copy(src, dst, out_sem.at[i])

    @pl.when(step == 0)
    def _():
        for r in (1, 2, 3):
            pl.semaphore_signal(
                barrier, inc=1, device_id={"feat": partner(own, r)}, device_id_type=MESH
            )
        for c, span in enumerate(spans):
            for r in range(GROUP):
                mixed_t[group_rows(r), span] = parts_ref[c, r]
            resid = hidden[span].astype(F32) + mat_tn(mixed_t[:, span], out_w[...]) + as_row(out_b)
            resid_scr[span] = resid
            normed, _ = row_stats(resid)
            inner = normed * as_row(gain_ref) + as_row(shift_ref)
            in_scr[span] = inner.astype(BF16)
            in_t[:, span] = inner.T.astype(BF16)
        acc_out[...] = jnp.zeros_like(acc_out)
        acc_in[...] = jnp.zeros_like(acc_in)
        bias_row[...] = as_row(up_b)

    slope = math.sqrt(2.0 / math.pi)
    total = jnp.zeros((1, model), F32)
    up_bias = bias_row[:, pl.ds(pl.multiple_of(step * model, model), model)]
    pre_scr32[...] = mat(in_scr[...], up[...]) + up_bias
    for span in spans:
        pre = pre_scr32[span]
        square = pre * pre
        tanh = jnp.tanh(pre * (slope + (slope * 0.044715) * square))
        half = 0.5 * (1.0 + tanh)
        act = (pre * half).astype(BF16)
        bend = half + (0.5 * pre) * (1.0 - tanh * tanh) * (
            slope + (3.0 * slope * 0.044715) * square
        )
        pre_grad = act_grad_ref[span].astype(F32) * bend
        total = total + jnp.sum(pre_grad, axis=0, keepdims=True)
        pre_low = pre_grad.astype(BF16)
        act_scr[step, span] = act
        pre_scr[step, span] = pre_low
    acc_out[...] += mat(act_scr[step], down[...])
    acc_in[...] += mat_nt(pre_scr[step], up[...])
    vec_scr[pl.ds(4 + step, 1)] = total

    @pl.when(step == pl.num_programs(0) - 1)
    def _():
        pl.semaphore_wait(barrier, 3)
        sums = [jnp.zeros((1, model), F32) for _ in range(4)]
        for c, span in enumerate(spans):
            resid = resid_scr[span]
            normed, scale = row_stats(resid)
            inner_grad = acc_in[span]
            wide = grad[span].astype(F32)
            resid_grad = wide + norm_back(inner_grad * as_row(gain_ref), normed, scale)
            resid_out[span] = resid_grad
            low = resid_grad.astype(BF16)
            in_scr[span] = low
            back_t[...] = mat_nt(out_w[...], low).astype(BF16)
            for r in (2, 3, 1, 0):
                grads_vm[c, r] = back_t[group_rows(r)]
                if c == 0 and r:
                    grad_copy(r).start()
            layer_out[span] = (resid + acc_out[span] + as_row(down_b)).astype(BF16)
            for i, term in enumerate((wide, resid_grad, inner_grad * normed, inner_grad)):
                sums[i] = sums[i] + jnp.sum(term, axis=0, keepdims=True)
        out_copy(3).start()
        for i in range(4):
            vec_scr[i : i + 1] = sums[i]
        for t in range(tiles):
            down_term = mat_tn(act_scr[t], grad[...])
            if direct:
                for i in range(model // share):
                    slab_vm[t * (model // share) + i, 0:share] = down_term[
                        i * share : (i + 1) * share
                    ].astype(BF16)
            else:
                down_vm[t * model : (t + 1) * model] = down_term.astype(BF16)
        out_copy(0).start()
        for t in range(0, tiles, 2):
            terms = [mat(in_t[...], pre_scr[t]), mat(in_t[...], pre_scr[t + 1])]
            if direct:
                for i in range(owners):
                    own_rows = slice(i * small, (i + 1) * small)
                    slab_vm[i, share + t * small : share + (t + 2) * small] = jnp.concatenate(
                        [term[own_rows] for term in terms], axis=0
                    ).astype(BF16)
            else:
                for u, term in enumerate(terms):
                    up_vm[:, (t + u) * model : (t + u + 1) * model] = term.astype(BF16)
        out_copy(1).start()
        out_term = mat(mixed_t[...], in_scr[...])
        fill = aligned(small + 8) - small - 8
        extra = [jnp.zeros((fill, model), F32)] if fill else []
        for i in range(owners):
            rest = jnp.concatenate(
                [out_term[i * small : (i + 1) * small], vec_scr[...]] + extra, axis=0
            ).astype(BF16)
            if direct:
                slab_vm[i, 2 * share :] = rest
            else:
                tail_vm[i] = rest
        out_copy(2).start()
        for r in (1, 2, 3):
            grad_copy(r).wait_recv()
        out_copy(4).start()
        for r in (1, 2, 3):
            grad_copy(r).wait_send()
        for i in range(5):
            out_copy(i).wait()


def block_layer(
    parts, hidden, grad, out_w, out_b, gain, shift, down_b, up_b, up, down, act_grad, devices
):
    tokens, model = hidden.shape
    ff = up.shape[1]
    steps = ff // model
    seqs = parts.shape[0]
    small, share = model // devices, ff // devices
    direct = small % 8 == 0 and share % 16 == 0
    tail_rows = aligned(small + 8)
    single = pl.Buffered(1)
    whole = lambda *shape: pl.BlockSpec(
        shape, lambda t: (0,) * len(shape), pipeline_mode=single
    )
    anywhere = pl.BlockSpec(memory_space=pl.ANY)
    unused = (16, 128)
    slab_shape, down_shape, up_shape, tail_shape = (
        ((devices, 2 * share + tail_rows, model), unused, unused, unused) if direct
        else (unused, (ff, model), (model, ff), (devices, tail_rows, model))
    )
    layer_out, resid_grad, grads, first, slab, down_grad, up_grad, tail = pl.pallas_call(
        lambda *refs: block_kernel(direct, *refs),
        grid=(steps,),
        out_shape=(
            jax.ShapeDtypeStruct((tokens, model), BF16),
            jax.ShapeDtypeStruct((tokens, model), F32),
            jax.ShapeDtypeStruct(parts.shape, BF16),
            jax.ShapeDtypeStruct((3,) + parts.shape[2:], BF16),
            jax.ShapeDtypeStruct(slab_shape, BF16),
            jax.ShapeDtypeStruct(down_shape, BF16),
            jax.ShapeDtypeStruct(up_shape, BF16),
            jax.ShapeDtypeStruct(tail_shape, BF16),
        ),
        in_specs=[
            whole(*parts.shape), whole(tokens, model), whole(tokens, model), whole(model, model),
            whole(model), whole(model), whole(model), whole(model), whole(ff),
            pl.BlockSpec((model, model), lambda t: (0, t)),
            pl.BlockSpec((model, model), lambda t: (t, 0)),
            pl.BlockSpec((None, tokens, model), lambda t: (t, 0, 0)),
        ],
        out_specs=(
            whole(tokens, model), whole(tokens, model), anywhere, anywhere, anywhere, anywhere,
            anywhere, anywhere,
        ),
        scratch_shapes=[
            pltpu.VMEM((model, tokens), BF16),
            pltpu.VMEM((tokens, model), F32),
            pltpu.VMEM((tokens, model), BF16),
            pltpu.VMEM((model, tokens), BF16),
            pltpu.VMEM((tokens, model), F32),
            pltpu.VMEM((tokens, model), F32),
            pltpu.VMEM((steps, tokens, model), BF16),
            pltpu.VMEM((steps, tokens, model), BF16),
            pltpu.VMEM((8, model), F32),
            pltpu.VMEM((1, ff), F32),
            pltpu.VMEM((model, CHUNK), BF16),
            pltpu.VMEM((tokens, model), F32),
            pltpu.VMEM(slab_shape, BF16),
            pltpu.VMEM(down_shape, BF16),
            pltpu.VMEM(up_shape, BF16),
            pltpu.VMEM(tail_shape, BF16),
            pltpu.VMEM(parts.shape, BF16),
            pltpu.VMEM((3,) + parts.shape[2:], BF16),
            pltpu.SemaphoreType.DMA((3,)),
            pltpu.SemaphoreType.DMA((3,)),
            pltpu.SemaphoreType.DMA((5,)),
        ],
        compiler_params=pltpu.CompilerParams(
            vmem_limit_bytes=VMEM, collective_id=3, has_side_effects=True
        ),
        cost_estimate=pl.CostEstimate(
            flops=26_000_000_000, bytes_accessed=30_000_000, transcendentals=0
        ),
        name="block_layer",
    )(parts, hidden, grad, out_w, out_b, gain, shift, down_b, up_b, up, down, act_grad)
    if not direct:
        fit = lambda a: jnp.pad(a, ((0, 0), (0, aligned(a.shape[1]) - a.shape[1]), (0, 0)))
        down_grad = fit(down_grad.reshape(devices, share, model))
        up_grad = up_grad.reshape(devices, small, ff // model, model).transpose(0, 2, 1, 3)
        up_grad = fit(up_grad.reshape(devices, ff // model * small, model))
        slab = jnp.concatenate([down_grad, up_grad, tail], axis=1)
    return layer_out, resid_grad, grads, first, slab


def attend_back_kernel(
    dp_size, x_ref, grads_ref, first_ref, weight, draws_ref, hot_ref, proj, state_ref, mixed_ref, den_ref,
    soft_ref, phi_q_ref, phi_k_ref, slab_any,
    attn_out, ring_out, proj_out,
    grad_scr, num_scr, value_scr, score_scr, exact_scr, proj_scr,
    grad_land, near_send, near_land, far_keep, far_send, far_land,
    mine, met, ring_land, cross_land,
    weight_acc, own_send, pair_land, own_mid, own_land, part_send, part_land,
    grad_sems, near_sems, far_sems, mine_sem, met_send, met_sems, ring_send, ring_sems, cross_sems,
    pair_sems, own_send_sem, own_sems,
    part_sems,
):
    s, h = pl.program_id(0), pl.program_id(1)
    seqs, heads = pl.num_programs(0), pl.num_programs(1)
    rows, model = x_ref.shape[1], x_ref.shape[2]
    head_count = proj_scr.shape[0] // (3 * HD)
    width = head_count * HD
    total = GROUP * rows
    root = 1.0 / math.sqrt(HD)
    own, me = lax.axis_index("feat"), lax.axis_index("dp")
    own_x, own_core = own // 2, own % 2
    near, across = {"feat": partner(own, 1)}, {"feat": partner(own, 2)}
    last = (s == seqs - 1) & (h == heads - 1)

    def grad_copy(q, r):
        return remote(
            grads_ref.at[q, r], grad_land.at[q - 1, r - 1], grad_sems.at[0, q - 1, r - 1],
            grad_sems.at[1, q - 1, r - 1], {"feat": partner(own, r)},
        )

    def near_copy(q, i):
        return remote(
            near_send.at[i], near_land.at[q, i], near_sems.at[0, q, i], near_sems.at[1, q, i], near
        )

    def far_copy(q):
        return remote(far_send, far_land.at[q], far_sems.at[0, q], far_sems.at[1, q], across)

    half = dp_size // 2
    parity, pair = lax.rem(me, 2), lax.div(me, 2)
    spot = pair + parity * (dp_size - 1 - 2 * pair)

    def at_spot(p):
        p = lax.rem(p + dp_size, dp_size)
        upper = lax.div(p, half)
        return 2 * p + upper * (2 * dp_size - 1 - 4 * p)

    places = ({"dp": at_spot(spot + 1)}, {"dp": at_spot(spot - 1)})

    def chunk(k, way):
        return at_spot(spot - 1 - k) if way == 0 else at_spot(spot + 1 + k)

    def mine_copy(k, way, owner):
        return pltpu.make_async_copy(
            slab_any.at[owner + own_core], mine.at[k, way], mine_sem.at[k, way]
        )

    def met_copy(k, way, owner):
        return remote(
            slab_any.at[owner + 1 - own_core], met.at[k, way], met_send, met_sems.at[k, way], near
        )

    cut = aligned(mine.shape[2] // 2)
    halves = (pl.ds(0, cut), pl.ds(cut, mine.shape[2] - cut))

    def ring_copy(k, way, part):
        return remote(
            mine.at[k, way, halves[part]], ring_land.at[k, way, halves[part]], ring_send,
            ring_sems.at[k, way, part], places[way],
        )

    def cross_copy(part):
        return remote(
            mine.at[dp_size - 1, 1 - own_x, halves[part]], cross_land.at[halves[part]],
            cross_sems.at[0, part], cross_sems.at[1, part], across,
        )

    def begin_pieces(k):
        for way in range(2):
            owner = chunk(k, way) * GROUP + 2 * way
            met_copy(k, way, owner).start()
            mine_copy(k, way, owner).start()

    def ring_step(k, part):
        span = halves[part]
        if part == 0:

            @pl.when(k + 2 < dp_size)
            def _():
                begin_pieces(k + 2)

        @pl.when(k < dp_size)
        def _():
            for way in range(2):
                if part == 0:
                    mine_copy(k, way, 0).wait()
                    met_copy(k, way, 0).wait_recv()

                @pl.when(k == 0)
                def _():
                    base = mine[k, way, span].astype(F32) + met[k, way, span].astype(F32)
                    mine[k, way, span] = base.astype(BF16)

                @pl.when(k > 0)
                def _():
                    ring_copy(k - 1, way, part).wait_recv()
                    base = mine[k, way, span].astype(F32) + met[k, way, span].astype(F32)
                    base = base + ring_land[k - 1, way, span].astype(F32)
                    mine[k, way, span] = base.astype(BF16)

                @pl.when(k < dp_size - 1)
                def _():
                    ring_copy(k, way, part).start()

            @pl.when(k == dp_size - 1)
            def _():
                cross_copy(part).start()

        @pl.when(k == dp_size)
        def _():
            cross_copy(part).wait_recv()
            ring_out[span] = mine[dp_size - 1, own_x, span].astype(F32) + cross_land[span].astype(F32)

    def ring_turn(part):
        turn = s * heads + h
        count = seqs * heads
        steps = dp_size + 1

        def body(k, carry):
            ring_step(k, part)
            return carry

        lax.fori_loop(lax.div(turn * steps, count), lax.div((turn + 1) * steps, count), body, 0)

    mate = me + 1 - 2 * parity

    def pair_copy(q):
        return remote(
            own_send.at[q, 1 - parity], pair_land.at[q], pair_sems.at[0, q], pair_sems.at[1, q],
            {"dp": mate},
        )

    def own_copy(q, k):
        to = lax.rem(pair + k, half)
        return remote(
            own_mid.at[q, to], own_land.at[q, k], own_send_sem, own_sems.at[q, k],
            {"dp": 2 * to + parity},
        )

    def begin_own(q):
        base = model // dp_size
        turned = weight_acc[pl.ds(pl.multiple_of(q * 3 * HD, 3 * HD), 3 * HD)].T
        fill = turned[model : model + own_send.shape[3] - base]
        for c in range(dp_size):
            own_send[q, c % 2, c // 2] = jnp.concatenate(
                [turned[c * base : (c + 1) * base], fill], axis=0
            ).astype(BF16)
        pair_copy(q).start()

    def relay_own(q):
        pair_copy(q).wait_recv()
        own_mid[q] = (own_send[q, parity].astype(F32) + pair_land[q].astype(F32)).astype(BF16)

        def start(k, carry):
            own_copy(q, k).start()
            return carry

        lax.fori_loop(1, half, start, 0)

    def part_copy(r):
        other = partner(own, r)
        return remote(
            part_send.at[other], part_land.at[r - 1], part_sems.at[0, r - 1],
            part_sems.at[1, r - 1], {"feat": other},
        )

    def seq_span(q):
        return pl.ds(pl.multiple_of(q * rows, rows), rows)

    def add_near(q):
        near_copy(q, 1).wait_recv()

        @pl.when(q > 0)
        def _():
            far_copy(q - 1).wait_send()

        far_send[...] = (far_keep[1] + near_land[q, 1].astype(F32)).astype(BF16)
        far_copy(q).start()
        near_copy(q, 0).wait_recv()
        attn_out[seq_span(q)] = far_keep[0] + near_land[q, 0].astype(F32)

    def finish(q):
        far_copy(q).wait_recv()
        span = seq_span(q)
        attn_out[span] = attn_out[span] + far_land[q].astype(F32)

    @pl.when((s == 0) & (h == 0))
    def _():
        barrier = pltpu.get_barrier_semaphore()
        for r in (1, 2, 3):
            pl.semaphore_signal(
                barrier, inc=1, device_id={"feat": partner(own, r)}, device_id_type=MESH
            )

        def greet(k, carry):
            pl.semaphore_signal(
                barrier, inc=1, device_id={"dp": lax.rem(me + k, dp_size)}, device_id_type=MESH
            )
            return carry

        lax.fori_loop(1, dp_size, greet, 0)
        pl.semaphore_wait(barrier, 3 + dp_size - 1)
        for q in range(1, near_land.shape[0]):
            for r in (2, 3, 1):
                grad_copy(q, r).start()
        for k in range(2):
            begin_pieces(k)
        weight_acc[...] = jnp.zeros_like(weight_acc)

    @pl.when(h == 0)
    def _():
        grad_scr[:, 0:rows] = grads_ref[s, 0].astype(F32)

        @pl.when(s == 0)
        def _():
            for r in (1, 2, 3):
                grad_scr[:, r * rows : (r + 1) * rows] = first_ref[r - 1].astype(F32)

        @pl.when(s > 0)
        def _():
            for r in (1, 2, 3):
                grad_copy(s, r).wait_recv()
                grad_scr[:, r * rows : (r + 1) * rows] = grad_land[s - 1, r - 1].astype(F32)

    query = proj[head_rows(h, 0, head_count)]
    key = proj[head_rows(h, 1, head_count)]
    value = proj[head_rows(h, 2, head_count)]
    draws = draws_ref[...]
    draws_ext = jnp.concatenate([draws, jnp.ones((16, FEAT), BF16)], axis=0)
    hot = hot_ref[...]
    away_wide = away_marks(hot)
    away = away_wide.astype(BF16)
    inverse = 1.0 / den_ref[0:1]
    head_grad = grad_scr[pl.ds(pl.multiple_of(h * HD, HD), HD)]
    grad_num = (head_grad * inverse).astype(BF16)
    grad_den = -jnp.sum(head_grad * mixed_ref[...], axis=0, keepdims=True) * inverse
    den_rows = jnp.broadcast_to(grad_den, (16, total)).astype(BF16)
    spread_grad = jnp.concatenate(spread(grad_num, hot) + [den_rows * hot], axis=0)
    spread_value = jnp.concatenate(spread(value, away) + [away], axis=0)

    phi_q, phi_k = phi_q_ref[...], phi_k_ref[...]
    state_grad = mat_nt(spread_grad, phi_q).astype(BF16)
    phi_q_grad = mat_tn(state_ref[...], spread_grad)
    phi_k_grad = mat_tn(state_grad, spread_value)
    value_low = mat(state_grad[0 : NBUCK * HD], phi_k)
    scaled_q = (phi_q_grad * phi_q.astype(F32)).astype(BF16)
    back_q = mat(draws_ext, scaled_q)
    scaled_k = (phi_k_grad * phi_k.astype(F32)).astype(BF16)
    back_k = mat(draws_ext, scaled_k)
    value_grad = pick(value_low, away_wide)
    query_grad = back_q[0:HD] - query.astype(F32) * (back_q[HD : HD + 1] * root)
    key_grad = back_k[0:HD] - key.astype(F32) * (back_k[HD : HD + 1] * root)

    ring_turn(0)
    one = (lax.broadcasted_iota(jnp.int32, hot.shape, 0) < 1).astype(F32).astype(BF16)
    num_scr[...] = jnp.concatenate([grad_num, den_rows], axis=0)
    value_scr[...] = jnp.concatenate([value, one], axis=0).astype(F32).T.astype(BF16)

    later = mat(value_scr[...], num_scr[:, 0:CHUNK])
    for c in range(total // CHUNK):
        cols = slice(c * CHUNK, (c + 1) * CHUNK)
        ahead = slice((c + 1) * CHUNK, (c + 2) * CHUNK)
        score = later
        later = mat(value_scr[...], num_scr[:, ahead]) if ahead.stop <= total else None
        score = (score * soft_ref[:, cols].astype(F32)).astype(BF16)
        score_scr[:, cols] = score
        exact_scr[:, cols] = mat(proj[head_rows(h, 1, head_count)], score)
    query_grad = query_grad + exact_scr[...] * root
    key_grad = key_grad + mat_nt(query, score_scr[...]) * root
    value_grad = value_grad + mat_nt(grad_num, soft_ref[...])
    wide_grad = jnp.concatenate([query_grad, key_grad, value_grad], axis=0)
    low_grad = wide_grad.astype(BF16)
    for kind in range(3):
        proj_scr[head_rows(h, kind, head_count)] = low_grad[kind * HD : (kind + 1) * HD]
    span = pl.ds(pl.multiple_of(h * 3 * HD, 3 * HD), 3 * HD)

    def times_x(grads):
        total_grad = mat(grads[:, 0:rows], x_ref[0])
        for r in (1, 2, 3):
            total_grad = total_grad + mat(grads[:, r * rows : (r + 1) * rows], x_ref[r])
        return total_grad

    @pl.when(s == seqs - 1)
    def _():
        weight_acc[span, 0:model] += times_x(low_grad)

    @pl.when((s < seqs - 1) & (h == heads - 1))
    def _():
        every = times_x(proj_scr[...])
        for g in range(head_count):
            for kind in range(3):
                low_row = (kind * head_count + g) * HD
                rows_to = slice((g * 3 + kind) * HD, (g * 3 + kind + 1) * HD)
                weight_acc[rows_to, 0:model] += every[low_row : low_row + HD]

    weight_acc[span, model:] += jnp.broadcast_to(
        jnp.sum(wide_grad, axis=1, keepdims=True), (3 * HD, 128)
    )

    @pl.when((s > 0) & (h == 0))
    def _():
        add_near(s - 1)

    @pl.when(h == heads - 1)
    def _():
        @pl.when(s > 0)
        def _():
            for i in range(2):
                near_copy(s - 1, i).wait_send()

        terms = mat_tn(proj_scr[...], weight[...])
        for r in (3, 1, 2, 0):
            term = terms[r * rows : (r + 1) * rows]
            if r % 2:
                near_send[r // 2] = term.astype(BF16)
                near_copy(s, r // 2).start()
            else:
                far_keep[r // 2] = term

    @pl.when(s == seqs - 1)
    def _():
        begin_own(h)

        @pl.when(h > 0)
        def _():
            relay_own(h - 1)

    ring_turn(1)

    @pl.when(last)
    def _():
        add_near(s)
        relay_own(h)
        for q in range(near_land.shape[0] - 1):
            finish(q)

        sums = []
        for q in range(head_count):

            def arrive(k, carry):
                own_copy(q, k).wait_recv()
                return carry + own_land[q, k].astype(F32)

            sums.append(lax.fori_loop(1, half, arrive, own_mid[q, pair].astype(F32)))
        joined = jnp.concatenate(sums, axis=1)
        base = model // dp_size
        small = base // GROUP
        fill = jnp.broadcast_to(
            joined[base : base + 1], (part_send.shape[1] - small, joined.shape[1])
        )
        for a in range(GROUP):
            part_send[a] = jnp.concatenate(
                [joined[a * small : (a + 1) * small], fill], axis=0
            ).astype(BF16)
        for r in (2, 3, 1):
            part_copy(r).start()
        finish(s)
        proj_out[own] = part_send[own].astype(F32)
        for r in (1, 2, 3):
            part_copy(r).wait_recv()
            proj_out[partner(own, r)] = part_land[r - 1].astype(F32)

        for i in range(2):
            near_copy(s, i).wait_send()
        far_copy(s).wait_send()
        for r in (1, 2, 3):
            part_copy(r).wait_send()
        for part in range(2):
            cross_copy(part).wait_send()
        for q in range(1, near_land.shape[0]):
            for r in (1, 2, 3):
                grad_copy(q, r).wait_send()
        for q in range(head_count):
            pair_copy(q).wait_send()
        every = pl.ds(0, half - 1)
        if half > 1:
            remote(
                own_mid.at[:, every], own_land.at[:, every], own_send_sem, own_sems.at[0, 0],
                {"dp": mate},
            ).wait_send()
        remote(
            mine.at[pl.ds(0, dp_size - 1)], ring_land, ring_send, ring_sems.at[0, 0, 0], places[0]
        ).wait_send()
        remote(mine, met, met_send, met_sems.at[0, 0], near).wait_send()


def attend_back(
    dp_size, parts, grads, first, weight, draws, hot, proj, state, mixed, den, soft, phi_q, phi_k,
    slab,
):
    seqs, _, rows, model = parts.shape
    heads = draws.shape[0]
    width = heads * HD
    total = GROUP * rows
    n = dp_size
    ring_rows = slab.shape[1]
    own_rows = aligned(model // n + 1)
    part_rows = aligned(model // (n * GROUP) + 1)
    single = pl.Buffered(1)
    whole = lambda *shape: pl.BlockSpec(
        shape, lambda s, h: (0,) * len(shape), pipeline_mode=single
    )
    mode = single if n > 16 else None
    by_seq = lambda *shape: pl.BlockSpec(
        (None,) + shape, lambda s, h: (s,) + (0,) * len(shape), pipeline_mode=mode
    )
    by_head = lambda *shape: pl.BlockSpec(
        (None, None) + shape, lambda s, h: (s, h) + (0,) * len(shape), pipeline_mode=mode
    )
    anywhere = pl.BlockSpec(memory_space=pl.ANY)
    dma = pltpu.SemaphoreType.DMA
    return pl.pallas_call(
        lambda *refs: attend_back_kernel(dp_size, *refs),
        grid=(seqs, heads),
        out_shape=(
            jax.ShapeDtypeStruct((seqs * rows, model), F32),
            jax.ShapeDtypeStruct((ring_rows, model), F32),
            jax.ShapeDtypeStruct((GROUP, part_rows, 3 * width), F32),
        ),
        in_specs=[
            by_seq(GROUP, rows, model), whole(*grads.shape), whole(*first.shape),
            whole(3 * width, model),
            pl.BlockSpec((None, HD, FEAT), lambda s, h: (h, 0, 0)),
            by_seq(16, total), by_seq(3 * width, total), by_head(STATES, FEAT), by_head(HD, total),
            by_head(8, total), by_head(total, total), by_head(FEAT, total), by_head(FEAT, total),
            anywhere,
        ],
        out_specs=(
            whole(seqs * rows, model), whole(ring_rows, model), whole(GROUP, part_rows, 3 * width),
        ),
        scratch_shapes=[
            pltpu.VMEM((width, total), F32),
            pltpu.VMEM((HD + 16, total), BF16),
            pltpu.VMEM((total, HD + 16), BF16),
            pltpu.VMEM((total, total), BF16),
            pltpu.VMEM((HD, total), F32),
            pltpu.VMEM((3 * width, total), BF16),
            pltpu.VMEM((seqs - 1, 3, width, rows), BF16),
            pltpu.VMEM((2, rows, model), BF16),
            pltpu.VMEM((seqs, 2, rows, model), BF16),
            pltpu.VMEM((2, rows, model), F32),
            pltpu.VMEM((rows, model), BF16),
            pltpu.VMEM((seqs, rows, model), BF16),
            pltpu.VMEM((n, 2, ring_rows, model), BF16),
            pltpu.VMEM((n, 2, ring_rows, model), BF16),
            pltpu.VMEM((n - 1, 2, ring_rows, model), BF16),
            pltpu.VMEM((ring_rows, model), BF16),
            pltpu.VMEM((3 * width, model + 128), F32),
            pltpu.VMEM((heads, 2, n // 2, own_rows, 3 * HD), BF16),
            pltpu.VMEM((heads, n // 2, own_rows, 3 * HD), BF16),
            pltpu.VMEM((heads, n // 2, own_rows, 3 * HD), BF16),
            pltpu.VMEM((heads, n // 2, own_rows, 3 * HD), BF16),
            pltpu.VMEM((GROUP, part_rows, 3 * width), BF16),
            pltpu.VMEM((3, part_rows, 3 * width), BF16),
            dma((2, seqs - 1, 3)),
            dma((2, seqs, 2)),
            dma((2, seqs)),
            dma((n, 2)),
            dma,
            dma((n, 2)),
            dma,
            dma((n - 1, 2, 2)),
            dma((2, 2)),
            dma((2, heads)),
            dma,
            dma((heads, n // 2)),
            dma((2, 3)),
        ],
        compiler_params=pltpu.CompilerParams(
            vmem_limit_bytes=VMEM + (3 * 1024 * 1024 if n > 16 else 0), collective_id=2, has_side_effects=True
        ),
        cost_estimate=pl.CostEstimate(
            flops=48_000_000_000, bytes_accessed=40_000_000, transcendentals=0
        ),
        name="attend_back",
    )(
        parts, grads, first, weight, draws, hot, proj, state, mixed, den, soft, phi_q, phi_k, slab,
    )


def finish_kernel(
    starts, heads, attn_grad, resid_grad, hidden, sums, proj_sums, weight_any, gain_ref, shift_ref,
    input_out, norm1_gain_out, norm1_bias_out, qkv_out, qkv_bias_out, out_out, out_bias_out,
    norm2_gain_out, norm2_bias_out, up_out, up_bias_out, down_out, down_bias_out,
    weight_vm, weight_sem,
):
    gain, shift = as_row(gain_ref), as_row(shift_ref)
    index = lax.axis_index("dp") * GROUP + lax.axis_index("feat")
    small, model = out_out.shape
    window = weight_vm.shape[0]
    begin = jnp.minimum(lax.div(index * small, 16) * 16, model - window)
    weight_copy = pltpu.make_async_copy(
        weight_any.at[pl.ds(pl.multiple_of(begin, 16), window)], weight_vm, weight_sem
    )

    @pl.when(pl.program_id(0) == 0)
    def _():
        weight_copy.start()

    normed, scale = row_stats(hidden[...].astype(F32))
    input_out[...] = resid_grad[...] + norm_back(attn_grad[...] * gain, normed, scale)

    @pl.when(pl.program_id(0) == 0)
    def _():
        share = down_out.shape[0]
        ff = up_out.shape[1]

        def own(row, size):
            length = row.shape[1]
            wide = jnp.broadcast_to(row, (8, length))
            back = lax.rem(length - lax.rem(index * size, length), length)
            return pltpu.roll(wide, back, 1)[0:1, 0:size]

        down_out[...] = sums[0:share]
        first = starts[0]
        up_out[...] = jnp.concatenate(
            [sums[first + i * small : first + (i + 1) * small] for i in range(ff // model)], axis=1
        )
        first = starts[1]
        out_out[...] = sums[first : first + small]
        totals = first + small
        for i, out in enumerate((down_bias_out, out_bias_out, norm2_gain_out, norm2_bias_out)):
            out[...] = own(sums[totals + i : totals + i + 1], small).reshape(small)
        per_row = model // share
        level = index // per_row
        row = jnp.zeros((1, model), F32)
        for i in range(ff // model):
            row = jnp.where(level == i, sums[totals + 4 + i : totals + 5 + i], row)
        up_bias_out[...] = own(row, share).reshape(share)

        pieces = []
        for kind in range(3):
            for f in range(GROUP):
                for h in range(heads):
                    lanes = slice((h * 3 + kind) * HD, (h * 3 + kind + 1) * HD)
                    pieces.append(proj_sums[f, 0 : small + 1, lanes])
        grid = jnp.concatenate(pieces, axis=1)
        weight_sum, bias_sum = grid[0:small], grid[small : small + 1]
        qkv_out[...] = weight_sum
        qkv_bias_out[...] = own(bias_sum, 3 * small).reshape(3 * small)
        weight_copy.wait()
        near_rows = weight_vm[...].astype(F32)
        step = math.gcd(small, 16)
        wide = near_rows[0:small]
        for offset in range(step, window - small + 1, step):
            wide = jnp.where(
                index * small - begin == offset, near_rows[offset : offset + small], wide
            )

        def to_row(column):
            column = jnp.concatenate(
                [column, jnp.zeros((-small % 128, 1), F32)], axis=0
            )
            return jnp.broadcast_to(column, (column.shape[0], 128)).T[0:1, 0:small]

        bias_grad = to_row(jnp.sum(wide * bias_sum, axis=1, keepdims=True))
        gain_grad = to_row(jnp.sum(wide * weight_sum, axis=1, keepdims=True))
        norm1_bias_out[...] = bias_grad.reshape(small)
        gain_grad = (gain_grad - own(shift, small) * bias_grad) / own(gain, small)
        norm1_gain_out[...] = gain_grad.reshape(small)


def finish_all(
    attn_grad, resid_grad, hidden, sums, proj_sums, weight, gain, shift, devices, ff, heads,
):
    seqs, rows, model = hidden.shape
    small, share = model // devices, ff // devices
    starts = (aligned(share), 2 * aligned(share))
    whole = lambda *shape: pl.BlockSpec(shape, lambda s: (0,) * len(shape))
    by_seq = pl.BlockSpec((rows, model), lambda s: (s, 0))
    shapes = (
        (small,), (small,), (small, 3 * model), (3 * small,), (small, model), (small,), (small,),
        (small,), (small, ff), (share,), (share, model), (small,),
    )
    return pl.pallas_call(
        lambda *refs: finish_kernel(starts, heads, *refs),
        grid=(seqs,),
        out_shape=(jax.ShapeDtypeStruct((seqs * rows, model), F32),)
        + tuple(jax.ShapeDtypeStruct(shape, F32) for shape in shapes),
        in_specs=[
            by_seq, by_seq, pl.BlockSpec((None, rows, model), lambda s: (s, 0, 0)),
            whole(*sums.shape), whole(*proj_sums.shape), pl.BlockSpec(memory_space=pl.ANY), whole(model),
            whole(model),
        ],
        out_specs=(by_seq,) + tuple(whole(*shape) for shape in shapes),
        scratch_shapes=[
            pltpu.VMEM((aligned(small) + 16, 3 * model), BF16), pltpu.SemaphoreType.DMA,
        ],
        compiler_params=pltpu.CompilerParams(vmem_limit_bytes=VMEM),
        name="finish_all",
    )(attn_grad, resid_grad, hidden, sums, proj_sums, weight, gain, shift)


def per_device(
    hidden_in, norm1_gain, norm1_bias, qkv_weight, qkv_bias, feature_draws, out_weight, out_bias,
    norm2_gain, norm2_bias, up_weight, up_bias, down_weight, down_bias, block_bucket, out_grad,
):
    seqs, rows, model = hidden_in.shape
    ff = up_weight.shape[1]
    dp_size = lax.axis_size("dp")
    devices = dp_size * GROUP
    heads = feature_draws.shape[0] // GROUP
    flat = (seqs * rows, model)

    (
        parts, mixed_parts, act_grad, proj, state, mixed, den, hot, own_weight, own_draws, soft,
        phi_q, phi_k,
    ) = attend(
        block_bucket, hidden_in, norm1_gain, norm1_bias, qkv_bias, qkv_weight, feature_draws,
        out_grad.reshape(flat), down_weight,
    )
    layer_out, resid_grad, grads, first, slab = block_layer(
        mixed_parts, hidden_in.reshape(flat), out_grad.reshape(flat), out_weight, out_bias,
        norm2_gain, norm2_bias, down_bias, up_bias, up_weight, down_weight, act_grad, devices,
    )
    attn_grad, sums, proj_sums = attend_back(
        dp_size, parts, grads, first, own_weight, own_draws, hot, proj, state, mixed, den, soft,
        phi_q, phi_k, slab,
    )
    (
        input_grad, norm1_gain_sum, norm1_bias_sum, qkv_weight_sum, qkv_bias_sum, out_weight_sum,
        out_bias_sum, norm2_gain_sum, norm2_bias_sum, up_sum, up_bias_sum, down_sum, down_bias_sum,
    ) = finish_all(
        attn_grad, resid_grad, hidden_in, sums, proj_sums, qkv_weight, norm1_gain, norm1_bias,
        devices, ff, heads,
    )
    return (
        layer_out.reshape(hidden_in.shape), input_grad.reshape(hidden_in.shape), norm1_gain_sum,
        norm1_bias_sum, qkv_weight_sum, qkv_bias_sum, out_weight_sum, out_bias_sum, norm2_gain_sum,
        norm2_bias_sum, up_sum, up_bias_sum, down_sum, down_bias_sum,
    )


def solution(mesh):
    both = ("dp", "feat")
    rows = P("dp", "feat", None)
    in_specs = (
        rows, P(), P(), P(), P(), P(None, None, "feat"), P(), P(), P(), P(), P(), P(), P(), P(),
        P("dp", None, None), rows,
    )
    out_specs = (
        rows, rows, P(both), P(both), P(both, None), P(both), P(both, None), P(both), P(both),
        P(both), P(both, None), P(both), P(both, None), P(both),
    )
    return jax.shard_map(
        per_device, mesh=mesh, in_specs=in_specs, out_specs=out_specs, check_vma=False
    )
```

```python
import math

import jax
import jax.numpy as jnp
from jax import lax
from jax.experimental import pallas as pl
from jax.experimental.pallas import tpu as pltpu
from jax.sharding import PartitionSpec as P

HD = 64
FEAT = 256
BLOCK = 64
NBUCK = 4
GROUP = 4
CHUNK = 256
STATES = NBUCK * HD + 16
FAR = 16384.0
VMEM = 60 * 1024 * 1024

F32 = jnp.float32
BF16 = jnp.bfloat16
MESH = pl.DeviceIdType.MESH


def mat(left, right):
    return jnp.dot(left, right, preferred_element_type=F32)


def mat_nt(left, right):
    return lax.dot_general(left, right, (((1,), (1,)), ((), ())), preferred_element_type=F32)


def mat_tn(left, right):
    return lax.dot_general(left, right, (((0,), (0,)), ((), ())), preferred_element_type=F32)


def row_stats(values):
    row_mean = jnp.mean(values, axis=-1, keepdims=True)
    centered = values - row_mean
    scale = lax.rsqrt(jnp.mean(centered * centered, axis=-1, keepdims=True) + 1e-05)
    return (centered * scale, scale)


def norm_back(cotangent, normed, scale):
    mean_one = jnp.mean(cotangent, axis=-1, keepdims=True)
    mean_two = jnp.mean(cotangent * normed, axis=-1, keepdims=True)
    return scale * (cotangent - mean_one - normed * mean_two)


def features(vectors, draws):
    wide = vectors.astype(F32)
    square = jnp.sum(wide * wide, axis=0, keepdims=True) * (0.5 / math.sqrt(HD))
    return jnp.exp(mat_tn(draws, vectors) - (square + 0.5 * math.log(FEAT)))


def spread(rows, marks):
    return [rows * marks[u : u + 1] for u in range(NBUCK)]


def pick(stacked, marks):
    total = stacked[0:HD] * marks[0:1]
    for u in range(1, NBUCK):
        total = total + stacked[u * HD : (u + 1) * HD] * marks[u : u + 1]
    return total


def away_marks(hot):
    live = (lax.broadcasted_iota(jnp.int32, hot.shape, 0) < NBUCK).astype(F32)
    return live - hot.astype(F32)


def partner(own, r):
    x, core = own // 2, own % 2
    if r & 2:
        x = 1 - x
    if r & 1:
        core = 1 - core
    return 2 * x + core


def as_row(ref):
    return ref[...].reshape(1, ref.shape[0])


def aligned(count):
    return -(-count // 16) * 16


def remote(src, dst, send, recv, place):
    return pltpu.make_async_remote_copy(
        src_ref=src, dst_ref=dst, send_sem=send, recv_sem=recv, device_id=place, device_id_type=MESH
    )


def head_rows(h, kind, heads):
    return pl.ds(pl.multiple_of((kind * heads + h) * HD, HD), HD)


def attend_kernel(
    bucket, hidden, gain_ref, shift_ref, bias_ref, weight_any, draws_in, grad, down_any,
    parts_any, mix_any, act_grad_any, proj_out, state_out, mixed_out, den_out, hot_out, weight_out, draws_out,
    soft_out, phi_q_out, phi_k_out,
    parts, mix_land, mix_send, raw, bias_row, bias_scr, draws_land, down_vm, act_grad,
    query_scr, key_scr, value_scr, low_scr,
    raw_sem, part_send, part_recv, draw_send, draw_recv, mix_send_sem, mix_recv_sem, out_sem,
    down_sem, act_sem,
):
    s, h = pl.program_id(0), pl.program_id(1)
    seqs, rows, model = hidden.shape
    heads = draws_out.shape[0]
    total = GROUP * rows
    width = heads * HD
    own = lax.axis_index("feat")
    near, across = {"feat": partner(own, 1)}, {"feat": partner(own, 2)}

    def part_copy(q, kind):
        src, dst, place = ((0, 1, near), (0, 2, across), (2, 3, near))[kind]
        return remote(
            parts.at[q, src], parts.at[q, dst], part_send.at[q, kind], part_recv.at[q, kind], place
        )

    def draw_copy(r):
        other = partner(own, r)
        return remote(
            draws_in.at[pl.ds(other * heads, heads)], draws_land.at[r - 1],
            draw_send.at[r - 1], draw_recv.at[r - 1], {"feat": other},
        )

    def mix_copy(q, g, r):
        span = pl.ds(pl.multiple_of(g * HD, HD), HD)
        return remote(
            mix_send.at[q, r - 1, span], mix_land.at[q, r, span], mix_send_sem.at[q, g, r - 1],
            mix_recv_sem.at[q, g, r - 1], {"feat": partner(own, r)},
        )

    down_copy = pltpu.make_async_copy(down_any, down_vm, down_sem)
    act_copy = pltpu.make_async_copy(act_grad, act_grad_any, act_sem)

    def raw_copy(j):
        cols = pl.ds(pl.multiple_of(j * model + (own // 2) * 2 * width, 2 * width), 2 * width)
        return pltpu.make_async_copy(weight_any.at[:, cols], raw.at[j], raw_sem.at[j])

    def out_copy(q):
        return pltpu.make_async_copy(parts.at[q], parts_any.at[q], out_sem.at[q])

    @pl.when((s == 0) & (h == 0))
    def _():
        for j in range(3):
            raw_copy(j).start()
        down_copy.start()
        barrier = pltpu.get_barrier_semaphore()
        for r in (1, 2, 3):
            pl.semaphore_signal(
                barrier, inc=1, device_id={"feat": partner(own, r)}, device_id_type=MESH
            )
        gain, shift = as_row(gain_ref), as_row(shift_ref)
        first = row_stats(hidden[0].astype(F32))[0] * gain + shift
        parts[0, 0] = first.astype(BF16)
        pl.semaphore_wait(barrier, 3)
        part_copy(0, 1).start()
        part_copy(0, 0).start()
        for r in (1, 2, 3):
            draw_copy(r).start()
        for q in range(1, seqs):
            normed = row_stats(hidden[q].astype(F32))[0] * gain + shift
            parts[q, 0] = normed.astype(BF16)
            part_copy(q, 1).start()
            part_copy(q, 0).start()
        core = own % 2
        bias_row[...] = as_row(bias_ref)
        for j in range(3):
            raw_copy(j).wait()
            piece = raw[j].astype(F32)
            piece = jnp.where(core == 0, piece[:, 0:width], piece[:, width:])
            weight_out[j * width : (j + 1) * width] = piece.T.astype(BF16)
            cols = pl.ds(pl.multiple_of(j * model + (own // 2) * 2 * width, 2 * width), 2 * width)
            pair = jnp.broadcast_to(bias_row[:, cols], (128, 2 * width))
            pair = jnp.where(core == 0, pair[:, 0:width], pair[:, width:])
            bias_scr[j * width : (j + 1) * width] = pair.T
        down_copy.wait()
        for t in range(act_grad.shape[0]):
            tile = down_vm[t * model : (t + 1) * model]
            for q in range(seqs):
                act_grad[t, q * rows : (q + 1) * rows] = mat_nt(grad[q], tile).astype(BF16)
        act_copy.start()
        part_copy(0, 1).wait_recv()
        part_copy(0, 2).start()
        for r in (1, 2, 3):
            draw_copy(r).wait_recv()
        mine = draws_in[pl.ds(own * heads, heads)]
        draws_out[...] = jnp.concatenate(
            [mine] + [draws_land[r - 1] for r in (1, 2, 3)], axis=2
        )

    @pl.when(h == 0)
    def _():
        per = rows // BLOCK
        lanes = lax.broadcasted_iota(jnp.int32, (16, total), 1) // BLOCK
        level = lax.broadcasted_iota(jnp.int32, (16, total), 0)
        ids = jnp.full((16, total), -1, jnp.int32)
        for r in range(GROUP):
            for i in range(per):
                ids = jnp.where(
                    lanes == r * per + i, bucket[s, partner(own, r) * per + i, 0], ids
                )
        hot_out[...] = (ids == level).astype(F32).astype(BF16)

        def project(r):
            cols = slice(r * rows, (r + 1) * rows)
            piece = mat_nt(weight_out[...], parts[s, r]) + bias_scr[:, 0:1]
            proj_out[:, cols] = piece.astype(BF16)

        project(0)
        part_copy(s, 0).wait_recv()
        project(1)
        project(2)
        part_copy(s, 2).wait_recv()
        project(3)
        out_copy(s).start()

    query = proj_out[head_rows(h, 0, heads)]
    key = proj_out[head_rows(h, 1, heads)]
    value = proj_out[head_rows(h, 2, heads)]
    draws = draws_out[h]
    hot = hot_out[...]
    hot_wide = hot.astype(F32)
    away = away_marks(hot).astype(BF16)
    phi_q = features(query, draws).astype(BF16)
    phi_k = features(key, draws).astype(BF16)
    phi_q_out[...] = phi_q
    phi_k_out[...] = phi_k
    spread_value = jnp.concatenate(spread(value, away) + [away], axis=0)
    state = mat_nt(spread_value, phi_k).astype(BF16)
    state_out[...] = state
    low = mat(state, phi_q)
    low_scr[0:HD] = pick(low, hot_wide)
    low_den = jnp.sum(low[NBUCK * HD :] * hot_wide, axis=0, keepdims=True)
    low_scr[HD : HD + 8] = jnp.broadcast_to(low_den, (8, total))
    query_scr[...] = jnp.concatenate([query * (1.0 / math.sqrt(HD)), hot], axis=0).astype(BF16)
    key_scr[...] = jnp.concatenate([key, away * -FAR], axis=0).astype(F32).T.astype(BF16)
    value_scr[0:HD] = value
    value_scr[HD:] = jnp.ones((16, total), BF16)

    head_span = pl.ds(pl.multiple_of(h * HD, HD), HD)
    score = mat(key_scr[...], query_scr[:, 0:CHUNK])
    for c in range(total // CHUNK):
        cols = slice(c * CHUNK, (c + 1) * CHUNK)
        ahead = slice((c + 1) * CHUNK, (c + 2) * CHUNK)
        later = mat(key_scr[...], query_scr[:, ahead]) if ahead.stop <= total else None
        weights = jnp.exp(score).astype(BF16)
        score = later
        soft_out[:, cols] = weights
        exact = mat(value_scr[...], weights)
        den = low_scr[HD : HD + 8, cols] + exact[HD : HD + 8]
        mixed = (low_scr[0:HD, cols] + exact[0:HD]) / den[0:1]
        mixed_out[:, cols] = mixed
        den_out[:, cols] = den
        mixed_low = mixed.astype(BF16)
        for r in range(GROUP):
            low_col, high_col = max(cols.start, r * rows), min(cols.stop, (r + 1) * rows)
            if low_col < high_col:
                piece = mixed_low[:, low_col - cols.start : high_col - cols.start]
                inner = slice(low_col - r * rows, high_col - r * rows)
                if r:
                    mix_send[s, r - 1, head_span, inner] = piece
                else:
                    mix_land[s, 0, head_span, inner] = piece
    for r in (2, 3, 1):
        mix_copy(s, h, r).start()

    @pl.when((h == heads - 2) & (s < seqs - 1))
    def _():
        part_copy(s + 1, 1).wait_recv()
        part_copy(s + 1, 2).start()

    @pl.when((s == seqs - 1) & (h == heads - 1))
    def _():
        for q in range(seqs):
            for g in range(heads):
                for r in (1, 2, 3):
                    mix_copy(q, g, r).wait_recv()
        done = pltpu.make_async_copy(mix_land, mix_any, out_sem.at[seqs])
        done.start()
        for q in range(seqs):
            for kind in range(3):
                part_copy(q, kind).wait_send()
            for g in range(heads):
                for r in (1, 2, 3):
                    mix_copy(q, g, r).wait_send()
            out_copy(q).wait()
        act_copy.wait()
        for r in (1, 2, 3):
            draw_copy(r).wait_send()
        done.wait()


def attend(bucket, hidden, gain, shift, bias, weight, draws, grad, down):
    seqs, rows, model = hidden.shape
    tiles = down.shape[0] // model
    heads = draws.shape[0] // GROUP
    width = heads * HD
    total = GROUP * rows
    whole = lambda *shape: pl.BlockSpec(shape, lambda s, h: (0,) * len(shape))
    by_seq = lambda *shape: pl.BlockSpec((None,) + shape, lambda s, h: (s,) + (0,) * len(shape))
    by_head = lambda *shape: pl.BlockSpec(
        (None, None) + shape, lambda s, h: (s, h) + (0,) * len(shape)
    )
    anywhere = pl.BlockSpec(memory_space=pl.ANY)
    return pl.pallas_call(
        attend_kernel,
        grid=(seqs, heads),
        out_shape=(
            jax.ShapeDtypeStruct((seqs, GROUP, rows, model), BF16),
            jax.ShapeDtypeStruct((seqs, GROUP, width, rows), BF16),
            jax.ShapeDtypeStruct((tiles, seqs * rows, model), BF16),
            jax.ShapeDtypeStruct((seqs, 3 * width, total), BF16),
            jax.ShapeDtypeStruct((seqs, heads, STATES, FEAT), BF16),
            jax.ShapeDtypeStruct((seqs, heads, HD, total), F32),
            jax.ShapeDtypeStruct((seqs, heads, 8, total), F32),
            jax.ShapeDtypeStruct((seqs, 16, total), BF16),
            jax.ShapeDtypeStruct((3 * width, model), BF16),
            jax.ShapeDtypeStruct((heads, HD, FEAT), BF16),
            jax.ShapeDtypeStruct((seqs, heads, total, total), BF16),
            jax.ShapeDtypeStruct((seqs, heads, FEAT, total), BF16),
            jax.ShapeDtypeStruct((seqs, heads, FEAT, total), BF16),
        ),
        in_specs=[
            pl.BlockSpec(memory_space=pltpu.SMEM),
            whole(seqs, rows, model), whole(model), whole(model), whole(3 * model), anywhere,
            whole(*draws.shape), whole(seqs, rows, model), anywhere,
        ],
        out_specs=(
            anywhere, anywhere, anywhere, by_seq(3 * width, total), by_head(STATES, FEAT), by_head(HD, total),
            by_head(8, total), by_seq(16, total), whole(3 * width, model), whole(heads, HD, FEAT),
            by_head(total, total), by_head(FEAT, total), by_head(FEAT, total),
        ),
        scratch_shapes=[
            pltpu.VMEM((seqs, GROUP, rows, model), BF16),
            pltpu.VMEM((seqs, GROUP, width, rows), BF16),
            pltpu.VMEM((seqs, 3, width, rows), BF16),
            pltpu.VMEM((3, model, 2 * width), BF16),
            pltpu.VMEM((1, 3 * model), F32),
            pltpu.VMEM((3 * width, 128), F32),
            pltpu.VMEM((3, heads, HD, draws.shape[2]), BF16),
            pltpu.VMEM(down.shape, BF16),
            pltpu.VMEM((tiles, seqs * rows, model), BF16),
            pltpu.VMEM((HD + 16, total), BF16),
            pltpu.VMEM((total, HD + 16), BF16),
            pltpu.VMEM((HD + 16, total), BF16),
            pltpu.VMEM((HD + 8, total), F32),
            pltpu.SemaphoreType.DMA((3,)),
            pltpu.SemaphoreType.DMA((seqs, 3)),
            pltpu.SemaphoreType.DMA((seqs, 3)),
            pltpu.SemaphoreType.DMA((3,)),
            pltpu.SemaphoreType.DMA((3,)),
            pltpu.SemaphoreType.DMA((seqs, heads, 3)),
            pltpu.SemaphoreType.DMA((seqs, heads, 3)),
            pltpu.SemaphoreType.DMA((seqs + 1,)),
            pltpu.SemaphoreType.DMA,
            pltpu.SemaphoreType.DMA,
        ],
        compiler_params=pltpu.CompilerParams(
            vmem_limit_bytes=VMEM, collective_id=1, has_side_effects=True
        ),
        cost_estimate=pl.CostEstimate(
            flops=24_000_000_000, bytes_accessed=20_000_000, transcendentals=0
        ),
        name="attend",
    )(bucket, hidden, gain, shift, bias, weight, draws, grad, down)


def block_kernel(
    direct, parts_ref, hidden, grad, out_w, out_b, gain_ref, shift_ref, down_b, up_b, up, down,
    act_grad_ref,
    layer_out, resid_out, grads_any, first_any, slab_any, down_any, up_any, tail_any,
    mixed_t, resid_scr, in_scr, in_t, acc_out, acc_in, act_scr, pre_scr, vec_scr, bias_row, back_t,
    slab_vm, down_vm, up_vm, tail_vm, grads_vm, first_land, send_sem, recv_sem, out_sem,
):
    step = pl.program_id(0)
    model = hidden.shape[1]
    count = hidden.shape[0] // CHUNK
    tiles = act_scr.shape[0]
    spans = [slice(c * CHUNK, (c + 1) * CHUNK) for c in range(count)]
    owners = slab_vm.shape[0] if direct else tail_vm.shape[0]
    small = model // owners
    share = tiles * small
    own = lax.axis_index("feat")
    barrier = pltpu.get_barrier_semaphore()

    part = model // GROUP

    def group_rows(r):
        return pl.ds(pl.multiple_of(partner(own, r) * part, part), part)

    def grad_copy(r):
        return remote(
            grads_vm.at[0, r], first_land.at[r - 1], send_sem.at[r - 1], recv_sem.at[r - 1],
            {"feat": partner(own, r)},
        )

    def out_copy(i):
        pieces = [(down_vm, down_any), (up_vm, up_any), (tail_vm, tail_any)]
        if direct:
            cuts = (0, share, 2 * share, slab_vm.shape[1])
            pieces = [
                (slab_vm.at[:, pl.ds(low, high - low)], slab_any.at[:, pl.ds(low, high - low)])
                for low, high in zip(cuts, cuts[1:])
            ]
        src, dst = (
            *pieces, (grads_vm, grads_any), (first_land, first_any),
        )[i]
        return pltpu.make_async_copy(src, dst, out_sem.at[i])

    @pl.when(step == 0)
    def _():
        for r in (1, 2, 3):
            pl.semaphore_signal(
                barrier, inc=1, device_id={"feat": partner(own, r)}, device_id_type=MESH
            )
        for c, span in enumerate(spans):
            for r in range(GROUP):
                mixed_t[group_rows(r), span] = parts_ref[c, r]
            resid = hidden[span].astype(F32) + mat_tn(mixed_t[:, span], out_w[...]) + as_row(out_b)
            resid_scr[span] = resid
            normed, _ = row_stats(resid)
            inner = normed * as_row(gain_ref) + as_row(shift_ref)
            in_scr[span] = inner.astype(BF16)
            in_t[:, span] = inner.T.astype(BF16)
        acc_out[...] = jnp.zeros_like(acc_out)
        acc_in[...] = jnp.zeros_like(acc_in)
        bias_row[...] = as_row(up_b)

    slope = math.sqrt(2.0 / math.pi)
    total = jnp.zeros((1, model), F32)
    up_bias = bias_row[:, pl.ds(pl.multiple_of(step * model, model), model)]
    for span in spans:
        pre = mat(in_scr[span], up[...]) + up_bias
        square = pre * pre
        tanh = jnp.tanh(pre * (slope + (slope * 0.044715) * square))
        half = 0.5 * (1.0 + tanh)
        act = (pre * half).astype(BF16)
        bend = half + (0.5 * pre) * (1.0 - tanh * tanh) * (
            slope + (3.0 * slope * 0.044715) * square
        )
        pre_grad = act_grad_ref[span].astype(F32) * bend
        total = total + jnp.sum(pre_grad, axis=0, keepdims=True)
        pre_low = pre_grad.astype(BF16)
        act_scr[step, span] = act
        pre_scr[step, span] = pre_low
        acc_out[span] += mat(act, down[...])
        acc_in[span] += mat_nt(pre_low, up[...])
    vec_scr[pl.ds(4 + step, 1)] = total

    @pl.when(step == pl.num_programs(0) - 1)
    def _():
        pl.semaphore_wait(barrier, 3)
        sums = [jnp.zeros((1, model), F32) for _ in range(4)]
        for c, span in enumerate(spans):
            resid = resid_scr[span]
            normed, scale = row_stats(resid)
            inner_grad = acc_in[span]
            wide = grad[span].astype(F32)
            resid_grad = wide + norm_back(inner_grad * as_row(gain_ref), normed, scale)
            resid_out[span] = resid_grad
            low = resid_grad.astype(BF16)
            in_scr[span] = low
            back_t[...] = mat_nt(out_w[...], low).astype(BF16)
            for r in (2, 3, 1, 0):
                grads_vm[c, r] = back_t[group_rows(r)]
                if c == 0 and r:
                    grad_copy(r).start()
            layer_out[span] = (resid + acc_out[span] + as_row(down_b)).astype(BF16)
            for i, term in enumerate((wide, resid_grad, inner_grad * normed, inner_grad)):
                sums[i] = sums[i] + jnp.sum(term, axis=0, keepdims=True)
        out_copy(3).start()
        for i in range(4):
            vec_scr[i : i + 1] = sums[i]
        for t in range(tiles):
            down_term = mat_tn(act_scr[t], grad[...])
            if direct:
                for i in range(model // share):
                    slab_vm[t * (model // share) + i, 0:share] = down_term[
                        i * share : (i + 1) * share
                    ].astype(BF16)
            else:
                down_vm[t * model : (t + 1) * model] = down_term.astype(BF16)
        out_copy(0).start()
        for t in range(0, tiles, 2):
            terms = [mat(in_t[...], pre_scr[t]), mat(in_t[...], pre_scr[t + 1])]
            if direct:
                for i in range(owners):
                    own_rows = slice(i * small, (i + 1) * small)
                    slab_vm[i, share + t * small : share + (t + 2) * small] = jnp.concatenate(
                        [term[own_rows] for term in terms], axis=0
                    ).astype(BF16)
            else:
                for u, term in enumerate(terms):
                    up_vm[:, (t + u) * model : (t + u + 1) * model] = term.astype(BF16)
        out_copy(1).start()
        out_term = mat(mixed_t[...], in_scr[...])
        fill = aligned(small + 8) - small - 8
        extra = [jnp.zeros((fill, model), F32)] if fill else []
        for i in range(owners):
            rest = jnp.concatenate(
                [out_term[i * small : (i + 1) * small], vec_scr[...]] + extra, axis=0
            ).astype(BF16)
            if direct:
                slab_vm[i, 2 * share :] = rest
            else:
                tail_vm[i] = rest
        out_copy(2).start()
        for r in (1, 2, 3):
            grad_copy(r).wait_recv()
        out_copy(4).start()
        for r in (1, 2, 3):
            grad_copy(r).wait_send()
        for i in range(5):
            out_copy(i).wait()


def block_layer(
    parts, hidden, grad, out_w, out_b, gain, shift, down_b, up_b, up, down, act_grad, devices
):
    tokens, model = hidden.shape
    ff = up.shape[1]
    steps = ff // model
    seqs = parts.shape[0]
    small, share = model // devices, ff // devices
    direct = small % 8 == 0 and share % 16 == 0
    tail_rows = aligned(small + 8)
    single = pl.Buffered(1)
    whole = lambda *shape: pl.BlockSpec(
        shape, lambda t: (0,) * len(shape), pipeline_mode=single
    )
    anywhere = pl.BlockSpec(memory_space=pl.ANY)
    unused = (16, 128)
    slab_shape, down_shape, up_shape, tail_shape = (
        ((devices, 2 * share + tail_rows, model), unused, unused, unused) if direct
        else (unused, (ff, model), (model, ff), (devices, tail_rows, model))
    )
    layer_out, resid_grad, grads, first, slab, down_grad, up_grad, tail = pl.pallas_call(
        lambda *refs: block_kernel(direct, *refs),
        grid=(steps,),
        out_shape=(
            jax.ShapeDtypeStruct((tokens, model), BF16),
            jax.ShapeDtypeStruct((tokens, model), F32),
            jax.ShapeDtypeStruct(parts.shape, BF16),
            jax.ShapeDtypeStruct((3,) + parts.shape[2:], BF16),
            jax.ShapeDtypeStruct(slab_shape, BF16),
            jax.ShapeDtypeStruct(down_shape, BF16),
            jax.ShapeDtypeStruct(up_shape, BF16),
            jax.ShapeDtypeStruct(tail_shape, BF16),
        ),
        in_specs=[
            whole(*parts.shape), whole(tokens, model), whole(tokens, model), whole(model, model),
            whole(model), whole(model), whole(model), whole(model), whole(ff),
            pl.BlockSpec((model, model), lambda t: (0, t)),
            pl.BlockSpec((model, model), lambda t: (t, 0)),
            pl.BlockSpec((None, tokens, model), lambda t: (t, 0, 0)),
        ],
        out_specs=(
            whole(tokens, model), whole(tokens, model), anywhere, anywhere, anywhere, anywhere,
            anywhere, anywhere,
        ),
        scratch_shapes=[
            pltpu.VMEM((model, tokens), BF16),
            pltpu.VMEM((tokens, model), F32),
            pltpu.VMEM((tokens, model), BF16),
            pltpu.VMEM((model, tokens), BF16),
            pltpu.VMEM((tokens, model), F32),
            pltpu.VMEM((tokens, model), F32),
            pltpu.VMEM((steps, tokens, model), BF16),
            pltpu.VMEM((steps, tokens, model), BF16),
            pltpu.VMEM((8, model), F32),
            pltpu.VMEM((1, ff), F32),
            pltpu.VMEM((model, CHUNK), BF16),
            pltpu.VMEM(slab_shape, BF16),
            pltpu.VMEM(down_shape, BF16),
            pltpu.VMEM(up_shape, BF16),
            pltpu.VMEM(tail_shape, BF16),
            pltpu.VMEM(parts.shape, BF16),
            pltpu.VMEM((3,) + parts.shape[2:], BF16),
            pltpu.SemaphoreType.DMA((3,)),
            pltpu.SemaphoreType.DMA((3,)),
            pltpu.SemaphoreType.DMA((5,)),
        ],
        compiler_params=pltpu.CompilerParams(
            vmem_limit_bytes=VMEM, collective_id=3, has_side_effects=True
        ),
        cost_estimate=pl.CostEstimate(
            flops=26_000_000_000, bytes_accessed=30_000_000, transcendentals=0
        ),
        name="block_layer",
    )(parts, hidden, grad, out_w, out_b, gain, shift, down_b, up_b, up, down, act_grad)
    if not direct:
        fit = lambda a: jnp.pad(a, ((0, 0), (0, aligned(a.shape[1]) - a.shape[1]), (0, 0)))
        down_grad = fit(down_grad.reshape(devices, share, model))
        up_grad = up_grad.reshape(devices, small, ff // model, model).transpose(0, 2, 1, 3)
        up_grad = fit(up_grad.reshape(devices, ff // model * small, model))
        slab = jnp.concatenate([down_grad, up_grad, tail], axis=1)
    return layer_out, resid_grad, grads, first, slab


def attend_back_kernel(
    dp_size, x_ref, grads_ref, first_ref, weight, draws_ref, hot_ref, proj, state_ref, mixed_ref, den_ref,
    soft_ref, phi_q_ref, phi_k_ref, slab_any,
    attn_out, ring_out, proj_out,
    grad_scr, num_scr, value_scr, score_scr, exact_scr, proj_scr,
    grad_land, near_send, near_land, far_keep, far_send, far_land,
    mine, met, ring_land, cross_land,
    weight_acc, own_send, pair_land, own_mid, own_land, part_send, part_land,
    grad_sems, near_sems, far_sems, mine_sem, met_send, met_sems, ring_send, ring_sems, cross_sems,
    pair_sems, own_send_sem, own_sems,
    part_sems,
):
    s, h = pl.program_id(0), pl.program_id(1)
    seqs, heads = pl.num_programs(0), pl.num_programs(1)
    rows, model = x_ref.shape[1], x_ref.shape[2]
    head_count = proj_scr.shape[0] // (3 * HD)
    width = head_count * HD
    total = GROUP * rows
    root = 1.0 / math.sqrt(HD)
    own, me = lax.axis_index("feat"), lax.axis_index("dp")
    own_x, own_core = own // 2, own % 2
    near, across = {"feat": partner(own, 1)}, {"feat": partner(own, 2)}
    last = (s == seqs - 1) & (h == heads - 1)

    def grad_copy(q, r):
        return remote(
            grads_ref.at[q, r], grad_land.at[q - 1, r - 1], grad_sems.at[0, q - 1, r - 1],
            grad_sems.at[1, q - 1, r - 1], {"feat": partner(own, r)},
        )

    def near_copy(q, i):
        return remote(
            near_send.at[i], near_land.at[q, i], near_sems.at[0, q, i], near_sems.at[1, q, i], near
        )

    def far_copy(q):
        return remote(far_send, far_land.at[q], far_sems.at[0, q], far_sems.at[1, q], across)

    half = dp_size // 2
    parity, pair = lax.rem(me, 2), lax.div(me, 2)
    spot = pair + parity * (dp_size - 1 - 2 * pair)

    def at_spot(p):
        p = lax.rem(p + dp_size, dp_size)
        upper = lax.div(p, half)
        return 2 * p + upper * (2 * dp_size - 1 - 4 * p)

    places = ({"dp": at_spot(spot + 1)}, {"dp": at_spot(spot - 1)})

    def chunk(k, way):
        return at_spot(spot - 1 - k) if way == 0 else at_spot(spot + 1 + k)

    def mine_copy(k, way, owner):
        return pltpu.make_async_copy(
            slab_any.at[owner + own_core], mine.at[k, way], mine_sem.at[k, way]
        )

    def met_copy(k, way, owner):
        return remote(
            slab_any.at[owner + 1 - own_core], met.at[k, way], met_send, met_sems.at[k, way], near
        )

    cut = aligned(mine.shape[2] // 2)
    halves = (pl.ds(0, cut), pl.ds(cut, mine.shape[2] - cut))

    def ring_copy(k, way, part):
        return remote(
            mine.at[k, way, halves[part]], ring_land.at[k, way, halves[part]], ring_send,
            ring_sems.at[k, way, part], places[way],
        )

    def cross_copy(part):
        return remote(
            mine.at[dp_size - 1, 1 - own_x, halves[part]], cross_land.at[halves[part]],
            cross_sems.at[0, part], cross_sems.at[1, part], across,
        )

    def begin_pieces(k):
        for way in range(2):
            owner = chunk(k, way) * GROUP + 2 * way
            met_copy(k, way, owner).start()
            mine_copy(k, way, owner).start()

    def ring_step(k, part):
        span = halves[part]
        if part == 0:

            @pl.when(k + 2 < dp_size)
            def _():
                begin_pieces(k + 2)

        @pl.when(k < dp_size)
        def _():
            for way in range(2):
                if part == 0:
                    mine_copy(k, way, 0).wait()
                    met_copy(k, way, 0).wait_recv()

                @pl.when(k == 0)
                def _():
                    base = mine[k, way, span].astype(F32) + met[k, way, span].astype(F32)
                    mine[k, way, span] = base.astype(BF16)

                @pl.when(k > 0)
                def _():
                    ring_copy(k - 1, way, part).wait_recv()
                    base = mine[k, way, span].astype(F32) + met[k, way, span].astype(F32)
                    base = base + ring_land[k - 1, way, span].astype(F32)
                    mine[k, way, span] = base.astype(BF16)

                @pl.when(k < dp_size - 1)
                def _():
                    ring_copy(k, way, part).start()

            @pl.when(k == dp_size - 1)
            def _():
                cross_copy(part).start()

        @pl.when(k == dp_size)
        def _():
            cross_copy(part).wait_recv()
            ring_out[span] = mine[dp_size - 1, own_x, span].astype(F32) + cross_land[span].astype(F32)

    def ring_turn(part):
        turn = s * heads + h
        count = seqs * heads
        steps = dp_size + 1

        def body(k, carry):
            ring_step(k, part)
            return carry

        lax.fori_loop(lax.div(turn * steps, count), lax.div((turn + 1) * steps, count), body, 0)

    mate = me + 1 - 2 * parity

    def pair_copy(q):
        return remote(
            own_send.at[q, 1 - parity], pair_land.at[q], pair_sems.at[0, q], pair_sems.at[1, q],
            {"dp": mate},
        )

    def own_copy(q, k):
        to = lax.rem(pair + k, half)
        return remote(
            own_mid.at[q, to], own_land.at[q, k], own_send_sem, own_sems.at[q, k],
            {"dp": 2 * to + parity},
        )

    base = model // dp_size

    def folded(values):
        middle = values.shape[0] // 2
        return jnp.concatenate([values[0:middle], values[middle:]], axis=1)

    def begin_own(q):
        turned = weight_acc[pl.ds(pl.multiple_of(q * 3 * HD, 3 * HD), 3 * HD)].T
        biases = turned[model : model + 16]
        blank = own_send.shape[3] - base - base // 2 - 16
        extra = [jnp.zeros((blank, 2 * HD), F32)] if blank else []
        for c in range(dp_size):
            block = turned[c * base : (c + 1) * base]
            own_send[q, c % 2, c // 2] = jnp.concatenate(
                [
                    block[:, 0 : 2 * HD], folded(block[:, 2 * HD :]), biases[0:8, 0 : 2 * HD],
                    folded(biases[:, 2 * HD :]),
                ] + extra,
                axis=0,
            ).astype(BF16)
        pair_copy(q).start()

    def relay_own(q):
        pair_copy(q).wait_recv()
        own_mid[q] = (own_send[q, parity].astype(F32) + pair_land[q].astype(F32)).astype(BF16)

        def start(k, carry):
            own_copy(q, k).start()
            return carry

        lax.fori_loop(1, half, start, 0)

    def part_copy(r):
        other = partner(own, r)
        return remote(
            part_send.at[other], part_land.at[r - 1], part_sems.at[0, r - 1],
            part_sems.at[1, r - 1], {"feat": other},
        )

    def seq_span(q):
        return pl.ds(pl.multiple_of(q * rows, rows), rows)

    def add_near(q):
        near_copy(q, 1).wait_recv()

        @pl.when(q > 0)
        def _():
            far_copy(q - 1).wait_send()

        far_send[...] = (far_keep[1] + near_land[q, 1].astype(F32)).astype(BF16)
        far_copy(q).start()
        near_copy(q, 0).wait_recv()
        attn_out[seq_span(q)] = far_keep[0] + near_land[q, 0].astype(F32)

    def finish(q):
        far_copy(q).wait_recv()
        span = seq_span(q)
        attn_out[span] = attn_out[span] + far_land[q].astype(F32)

    @pl.when((s == 0) & (h == 0))
    def _():
        barrier = pltpu.get_barrier_semaphore()
        for r in (1, 2, 3):
            pl.semaphore_signal(
                barrier, inc=1, device_id={"feat": partner(own, r)}, device_id_type=MESH
            )

        def greet(k, carry):
            pl.semaphore_signal(
                barrier, inc=1, device_id={"dp": lax.rem(me + k, dp_size)}, device_id_type=MESH
            )
            return carry

        lax.fori_loop(1, dp_size, greet, 0)
        pl.semaphore_wait(barrier, 3 + dp_size - 1)
        for q in range(1, near_land.shape[0]):
            for r in (2, 3, 1):
                grad_copy(q, r).start()
        for k in range(2):
            begin_pieces(k)
        weight_acc[...] = jnp.zeros_like(weight_acc)

    @pl.when(h == 0)
    def _():
        grad_scr[:, 0:rows] = grads_ref[s, 0].astype(F32)

        @pl.when(s == 0)
        def _():
            for r in (1, 2, 3):
                grad_scr[:, r * rows : (r + 1) * rows] = first_ref[r - 1].astype(F32)

        @pl.when(s > 0)
        def _():
            for r in (1, 2, 3):
                grad_copy(s, r).wait_recv()
                grad_scr[:, r * rows : (r + 1) * rows] = grad_land[s - 1, r - 1].astype(F32)

    query = proj[head_rows(h, 0, head_count)]
    key = proj[head_rows(h, 1, head_count)]
    value = proj[head_rows(h, 2, head_count)]
    draws = draws_ref[...]
    draws_ext = jnp.concatenate([draws, jnp.ones((16, FEAT), BF16)], axis=0)
    hot = hot_ref[...]
    away_wide = away_marks(hot)
    away = away_wide.astype(BF16)
    inverse = 1.0 / den_ref[0:1]
    head_grad = grad_scr[pl.ds(pl.multiple_of(h * HD, HD), HD)]
    grad_num = (head_grad * inverse).astype(BF16)
    grad_den = -jnp.sum(head_grad * mixed_ref[...], axis=0, keepdims=True) * inverse
    den_rows = jnp.broadcast_to(grad_den, (16, total)).astype(BF16)
    spread_grad = jnp.concatenate(spread(grad_num, hot) + [den_rows * hot], axis=0)
    spread_value = jnp.concatenate(spread(value, away) + [away], axis=0)

    phi_q, phi_k = phi_q_ref[...], phi_k_ref[...]
    state_grad = mat_nt(spread_grad, phi_q).astype(BF16)
    phi_q_grad = mat_tn(state_ref[...], spread_grad)
    phi_k_grad = mat_tn(state_grad, spread_value)
    value_low = mat(state_grad[0 : NBUCK * HD], phi_k)
    scaled_q = (phi_q_grad * phi_q.astype(F32)).astype(BF16)
    back_q = mat(draws_ext, scaled_q)
    scaled_k = (phi_k_grad * phi_k.astype(F32)).astype(BF16)
    back_k = mat(draws_ext, scaled_k)
    value_grad = pick(value_low, away_wide)
    query_grad = back_q[0:HD] - query.astype(F32) * (back_q[HD : HD + 1] * root)
    key_grad = back_k[0:HD] - key.astype(F32) * (back_k[HD : HD + 1] * root)

    ring_turn(0)
    one = (lax.broadcasted_iota(jnp.int32, hot.shape, 0) < 1).astype(F32).astype(BF16)
    num_scr[...] = jnp.concatenate([grad_num, den_rows], axis=0)
    value_scr[...] = jnp.concatenate([value, one], axis=0).astype(F32).T.astype(BF16)

    later = mat(value_scr[...], num_scr[:, 0:CHUNK])
    for c in range(total // CHUNK):
        cols = slice(c * CHUNK, (c + 1) * CHUNK)
        ahead = slice((c + 1) * CHUNK, (c + 2) * CHUNK)
        score = later
        later = mat(value_scr[...], num_scr[:, ahead]) if ahead.stop <= total else None
        score = (score * soft_ref[:, cols].astype(F32)).astype(BF16)
        score_scr[:, cols] = score
        exact_scr[:, cols] = mat(proj[head_rows(h, 1, head_count)], score)
    query_grad = query_grad + exact_scr[...] * root
    key_grad = key_grad + mat_nt(query, score_scr[...]) * root
    value_grad = value_grad + mat_nt(grad_num, soft_ref[...])
    wide_grad = jnp.concatenate([query_grad, key_grad, value_grad], axis=0)
    low_grad = wide_grad.astype(BF16)
    for kind in range(3):
        proj_scr[head_rows(h, kind, head_count)] = low_grad[kind * HD : (kind + 1) * HD]
    weight_grad = mat(low_grad[:, 0:rows], x_ref[0])
    for r in (1, 2, 3):
        weight_grad = weight_grad + mat(low_grad[:, r * rows : (r + 1) * rows], x_ref[r])
    span = pl.ds(pl.multiple_of(h * 3 * HD, 3 * HD), 3 * HD)
    weight_acc[span, 0:model] += weight_grad
    weight_acc[span, model:] += jnp.broadcast_to(
        jnp.sum(wide_grad, axis=1, keepdims=True), (3 * HD, 128)
    )

    @pl.when(s == seqs - 1)
    def _():
        begin_own(h)

        @pl.when(h > 0)
        def _():
            relay_own(h - 1)

    @pl.when((s > 0) & (h == 0))
    def _():
        add_near(s - 1)

    @pl.when(h == heads - 1)
    def _():
        @pl.when(s > 0)
        def _():
            for i in range(2):
                near_copy(s - 1, i).wait_send()

        for r in (3, 1, 2, 0):
            term = mat_tn(proj_scr[:, r * rows : (r + 1) * rows], weight[...])
            if r % 2:
                near_send[r // 2] = term.astype(BF16)
                near_copy(s, r // 2).start()
            else:
                far_keep[r // 2] = term

    ring_turn(1)

    @pl.when(last)
    def _():
        add_near(s)
        relay_own(h)
        for q in range(near_land.shape[0] - 1):
            finish(q)

        sums = []
        for q in range(head_count):

            def arrive(k, carry):
                own_copy(q, k).wait_recv()
                return carry + own_land[q, k].astype(F32)

            sums.append(lax.fori_loop(1, half, arrive, own_mid[q, pair].astype(F32)))
        blocks, biases = [], []
        end = base + base // 2
        for total_sum in sums:
            value_rows = total_sum[base:end]
            value_rows = jnp.concatenate([value_rows[:, 0:HD], value_rows[:, HD:]], axis=0)
            blocks += [total_sum[0:base], value_rows]
            biases += [total_sum[end : end + 1], total_sum[end + 8 : end + 9, 0:HD]]
        joined = jnp.concatenate(blocks, axis=1)
        small = base // GROUP
        fill = jnp.broadcast_to(
            jnp.concatenate(biases, axis=1), (part_send.shape[1] - small, joined.shape[1])
        )
        for a in range(GROUP):
            part_send[a] = jnp.concatenate(
                [joined[a * small : (a + 1) * small], fill], axis=0
            ).astype(BF16)
        for r in (2, 3, 1):
            part_copy(r).start()
        finish(s)
        proj_out[own] = part_send[own].astype(F32)
        for r in (1, 2, 3):
            part_copy(r).wait_recv()
            proj_out[partner(own, r)] = part_land[r - 1].astype(F32)

        for i in range(2):
            near_copy(s, i).wait_send()
        far_copy(s).wait_send()
        for r in (1, 2, 3):
            part_copy(r).wait_send()
        for part in range(2):
            cross_copy(part).wait_send()
        for q in range(1, near_land.shape[0]):
            for r in (1, 2, 3):
                grad_copy(q, r).wait_send()
        for q in range(head_count):
            pair_copy(q).wait_send()
        every = pl.ds(0, half - 1)
        if half > 1:
            remote(
                own_mid.at[:, every], own_land.at[:, every], own_send_sem, own_sems.at[0, 0],
                {"dp": mate},
            ).wait_send()
        remote(
            mine.at[pl.ds(0, dp_size - 1)], ring_land, ring_send, ring_sems.at[0, 0, 0], places[0]
        ).wait_send()
        remote(mine, met, met_send, met_sems.at[0, 0], near).wait_send()


def attend_back(
    dp_size, parts, grads, first, weight, draws, hot, proj, state, mixed, den, soft, phi_q, phi_k,
    slab,
):
    seqs, _, rows, model = parts.shape
    heads = draws.shape[0]
    width = heads * HD
    total = GROUP * rows
    n = dp_size
    ring_rows = slab.shape[1]
    own_rows = aligned(model // n + model // n // 2 + 16)
    part_rows = aligned(model // (n * GROUP) + 1)
    single = pl.Buffered(1)
    whole = lambda *shape: pl.BlockSpec(
        shape, lambda s, h: (0,) * len(shape), pipeline_mode=single
    )
    mode = single if n > 16 else None
    by_seq = lambda *shape: pl.BlockSpec(
        (None,) + shape, lambda s, h: (s,) + (0,) * len(shape), pipeline_mode=mode
    )
    by_head = lambda *shape: pl.BlockSpec(
        (None, None) + shape, lambda s, h: (s, h) + (0,) * len(shape), pipeline_mode=mode
    )
    anywhere = pl.BlockSpec(memory_space=pl.ANY)
    dma = pltpu.SemaphoreType.DMA
    return pl.pallas_call(
        lambda *refs: attend_back_kernel(dp_size, *refs),
        grid=(seqs, heads),
        out_shape=(
            jax.ShapeDtypeStruct((seqs * rows, model), F32),
            jax.ShapeDtypeStruct((ring_rows, model), F32),
            jax.ShapeDtypeStruct((GROUP, part_rows, 3 * width), F32),
        ),
        in_specs=[
            by_seq(GROUP, rows, model), whole(*grads.shape), whole(*first.shape),
            whole(3 * width, model),
            pl.BlockSpec((None, HD, FEAT), lambda s, h: (h, 0, 0)),
            by_seq(16, total), by_seq(3 * width, total), by_head(STATES, FEAT), by_head(HD, total),
            by_head(8, total), by_head(total, total), by_head(FEAT, total), by_head(FEAT, total),
            anywhere,
        ],
        out_specs=(
            whole(seqs * rows, model), whole(ring_rows, model), whole(GROUP, part_rows, 3 * width),
        ),
        scratch_shapes=[
            pltpu.VMEM((width, total), F32),
            pltpu.VMEM((HD + 16, total), BF16),
            pltpu.VMEM((total, HD + 16), BF16),
            pltpu.VMEM((total, total), BF16),
            pltpu.VMEM((HD, total), F32),
            pltpu.VMEM((3 * width, total), BF16),
            pltpu.VMEM((seqs - 1, 3, width, rows), BF16),
            pltpu.VMEM((2, rows, model), BF16),
            pltpu.VMEM((seqs, 2, rows, model), BF16),
            pltpu.VMEM((2, rows, model), F32),
            pltpu.VMEM((rows, model), BF16),
            pltpu.VMEM((seqs, rows, model), BF16),
            pltpu.VMEM((n, 2, ring_rows, model), BF16),
            pltpu.VMEM((n, 2, ring_rows, model), BF16),
            pltpu.VMEM((n - 1, 2, ring_rows, model), BF16),
            pltpu.VMEM((ring_rows, model), BF16),
            pltpu.VMEM((3 * width, model + 128), F32),
            pltpu.VMEM((heads, 2, n // 2, own_rows, 2 * HD), BF16),
            pltpu.VMEM((heads, n // 2, own_rows, 2 * HD), BF16),
            pltpu.VMEM((heads, n // 2, own_rows, 2 * HD), BF16),
            pltpu.VMEM((heads, n // 2, own_rows, 2 * HD), BF16),
            pltpu.VMEM((GROUP, part_rows, 3 * width), BF16),
            pltpu.VMEM((3, part_rows, 3 * width), BF16),
            dma((2, seqs - 1, 3)),
            dma((2, seqs, 2)),
            dma((2, seqs)),
            dma((n, 2)),
            dma,
            dma((n, 2)),
            dma,
            dma((n - 1, 2, 2)),
            dma((2, 2)),
            dma((2, heads)),
            dma,
            dma((heads, n // 2)),
            dma((2, 3)),
        ],
        compiler_params=pltpu.CompilerParams(
            vmem_limit_bytes=VMEM + (3 * 1024 * 1024 if n > 16 else 0), collective_id=2, has_side_effects=True
        ),
        cost_estimate=pl.CostEstimate(
            flops=48_000_000_000, bytes_accessed=40_000_000, transcendentals=0
        ),
        name="attend_back",
    )(
        parts, grads, first, weight, draws, hot, proj, state, mixed, den, soft, phi_q, phi_k, slab,
    )


def finish_kernel(
    starts, heads, attn_grad, resid_grad, hidden, sums, proj_sums, weight_any, gain_ref, shift_ref,
    input_out, norm1_gain_out, norm1_bias_out, qkv_out, qkv_bias_out, out_out, out_bias_out,
    norm2_gain_out, norm2_bias_out, up_out, up_bias_out, down_out, down_bias_out,
    weight_vm, weight_sem,
):
    gain, shift = as_row(gain_ref), as_row(shift_ref)
    index = lax.axis_index("dp") * GROUP + lax.axis_index("feat")
    small, model = out_out.shape
    window = weight_vm.shape[0]
    begin = jnp.minimum(lax.div(index * small, 16) * 16, model - window)
    weight_copy = pltpu.make_async_copy(
        weight_any.at[pl.ds(pl.multiple_of(begin, 16), window)], weight_vm, weight_sem
    )

    @pl.when(pl.program_id(0) == 0)
    def _():
        weight_copy.start()

    normed, scale = row_stats(hidden[...].astype(F32))
    input_out[...] = resid_grad[...] + norm_back(attn_grad[...] * gain, normed, scale)

    @pl.when(pl.program_id(0) == 0)
    def _():
        share = down_out.shape[0]
        ff = up_out.shape[1]

        def own(row, size):
            length = row.shape[1]
            wide = jnp.broadcast_to(row, (8, length))
            back = lax.rem(length - lax.rem(index * size, length), length)
            return pltpu.roll(wide, back, 1)[0:1, 0:size]

        down_out[...] = sums[0:share]
        first = starts[0]
        up_out[...] = jnp.concatenate(
            [sums[first + i * small : first + (i + 1) * small] for i in range(ff // model)], axis=1
        )
        first = starts[1]
        out_out[...] = sums[first : first + small]
        totals = first + small
        for i, out in enumerate((down_bias_out, out_bias_out, norm2_gain_out, norm2_bias_out)):
            out[...] = own(sums[totals + i : totals + i + 1], small).reshape(small)
        per_row = model // share
        level = index // per_row
        row = jnp.zeros((1, model), F32)
        for i in range(ff // model):
            row = jnp.where(level == i, sums[totals + 4 + i : totals + 5 + i], row)
        up_bias_out[...] = own(row, share).reshape(share)

        pieces = []
        for kind in range(3):
            for f in range(GROUP):
                for h in range(heads):
                    lanes = slice((h * 3 + kind) * HD, (h * 3 + kind + 1) * HD)
                    pieces.append(proj_sums[f, 0 : small + 1, lanes])
        grid = jnp.concatenate(pieces, axis=1)
        weight_sum, bias_sum = grid[0:small], grid[small : small + 1]
        qkv_out[...] = weight_sum
        qkv_bias_out[...] = own(bias_sum, 3 * small).reshape(3 * small)
        weight_copy.wait()
        near_rows = weight_vm[...].astype(F32)
        step = math.gcd(small, 16)
        wide = near_rows[0:small]
        for offset in range(step, window - small + 1, step):
            wide = jnp.where(
                index * small - begin == offset, near_rows[offset : offset + small], wide
            )

        def to_row(column):
            column = jnp.concatenate(
                [column, jnp.zeros((-small % 128, 1), F32)], axis=0
            )
            return jnp.broadcast_to(column, (column.shape[0], 128)).T[0:1, 0:small]

        bias_grad = to_row(jnp.sum(wide * bias_sum, axis=1, keepdims=True))
        gain_grad = to_row(jnp.sum(wide * weight_sum, axis=1, keepdims=True))
        norm1_bias_out[...] = bias_grad.reshape(small)
        gain_grad = (gain_grad - own(shift, small) * bias_grad) / own(gain, small)
        norm1_gain_out[...] = gain_grad.reshape(small)


def finish_all(
    attn_grad, resid_grad, hidden, sums, proj_sums, weight, gain, shift, devices, ff, heads,
):
    seqs, rows, model = hidden.shape
    small, share = model // devices, ff // devices
    starts = (aligned(share), 2 * aligned(share))
    whole = lambda *shape: pl.BlockSpec(shape, lambda s: (0,) * len(shape))
    by_seq = pl.BlockSpec((rows, model), lambda s: (s, 0))
    shapes = (
        (small,), (small,), (small, 3 * model), (3 * small,), (small, model), (small,), (small,),
        (small,), (small, ff), (share,), (share, model), (small,),
    )
    return pl.pallas_call(
        lambda *refs: finish_kernel(starts, heads, *refs),
        grid=(seqs,),
        out_shape=(jax.ShapeDtypeStruct((seqs * rows, model), F32),)
        + tuple(jax.ShapeDtypeStruct(shape, F32) for shape in shapes),
        in_specs=[
            by_seq, by_seq, pl.BlockSpec((None, rows, model), lambda s: (s, 0, 0)),
            whole(*sums.shape), whole(*proj_sums.shape), pl.BlockSpec(memory_space=pl.ANY), whole(model),
            whole(model),
        ],
        out_specs=(by_seq,) + tuple(whole(*shape) for shape in shapes),
        scratch_shapes=[
            pltpu.VMEM((aligned(small) + 16, 3 * model), BF16), pltpu.SemaphoreType.DMA,
        ],
        compiler_params=pltpu.CompilerParams(vmem_limit_bytes=VMEM),
        name="finish_all",
    )(attn_grad, resid_grad, hidden, sums, proj_sums, weight, gain, shift)


def per_device(
    hidden_in, norm1_gain, norm1_bias, qkv_weight, qkv_bias, feature_draws, out_weight, out_bias,
    norm2_gain, norm2_bias, up_weight, up_bias, down_weight, down_bias, block_bucket, out_grad,
):
    seqs, rows, model = hidden_in.shape
    ff = up_weight.shape[1]
    dp_size = lax.axis_size("dp")
    devices = dp_size * GROUP
    heads = feature_draws.shape[0] // GROUP
    flat = (seqs * rows, model)

    (
        parts, mixed_parts, act_grad, proj, state, mixed, den, hot, own_weight, own_draws, soft,
        phi_q, phi_k,
    ) = attend(
        block_bucket, hidden_in, norm1_gain, norm1_bias, qkv_bias, qkv_weight, feature_draws,
        out_grad, down_weight,
    )
    layer_out, resid_grad, grads, first, slab = block_layer(
        mixed_parts, hidden_in.reshape(flat), out_grad.reshape(flat), out_weight, out_bias,
        norm2_gain, norm2_bias, down_bias, up_bias, up_weight, down_weight, act_grad, devices,
    )
    attn_grad, sums, proj_sums = attend_back(
        dp_size, parts, grads, first, own_weight, own_draws, hot, proj, state, mixed, den, soft,
        phi_q, phi_k, slab,
    )
    (
        input_grad, norm1_gain_sum, norm1_bias_sum, qkv_weight_sum, qkv_bias_sum, out_weight_sum,
        out_bias_sum, norm2_gain_sum, norm2_bias_sum, up_sum, up_bias_sum, down_sum, down_bias_sum,
    ) = finish_all(
        attn_grad, resid_grad, hidden_in, sums, proj_sums, qkv_weight, norm1_gain, norm1_bias,
        devices, ff, heads,
    )
    return (
        layer_out.reshape(hidden_in.shape), input_grad.reshape(hidden_in.shape), norm1_gain_sum,
        norm1_bias_sum, qkv_weight_sum, qkv_bias_sum, out_weight_sum, out_bias_sum, norm2_gain_sum,
        norm2_bias_sum, up_sum, up_bias_sum, down_sum, down_bias_sum,
    )


def solution(mesh):
    both = ("dp", "feat")
    rows = P("dp", "feat", None)
    in_specs = (
        rows, P(), P(), P(), P(), P(None, None, "feat"), P(), P(), P(), P(), P(), P(), P(), P(),
        P("dp", None, None), rows,
    )
    out_specs = (
        rows, rows, P(both), P(both), P(both, None), P(both), P(both, None), P(both), P(both),
        P(both), P(both, None), P(both), P(both, None), P(both),
    )
    return jax.shard_map(
        per_device, mesh=mesh, in_specs=in_specs, out_specs=out_specs, check_vma=False
    )
```

```python
import math

import jax
import jax.numpy as jnp
from jax import lax
from jax.experimental import pallas as pl
from jax.experimental.pallas import tpu as pltpu
from jax.sharding import PartitionSpec as P

HD = 64
FEAT = 256
BLOCK = 64
NBUCK = 4
GROUP = 4
CHUNK = 256
STATES = NBUCK * HD + 16
FAR = 16384.0
VMEM = 60 * 1024 * 1024

F32 = jnp.float32
BF16 = jnp.bfloat16
MESH = pl.DeviceIdType.MESH


def mat(left, right):
    return jnp.dot(left, right, preferred_element_type=F32)


def mat_nt(left, right):
    return lax.dot_general(left, right, (((1,), (1,)), ((), ())), preferred_element_type=F32)


def mat_tn(left, right):
    return lax.dot_general(left, right, (((0,), (0,)), ((), ())), preferred_element_type=F32)


def row_stats(values):
    row_mean = jnp.mean(values, axis=-1, keepdims=True)
    centered = values - row_mean
    scale = lax.rsqrt(jnp.mean(centered * centered, axis=-1, keepdims=True) + 1e-05)
    return (centered * scale, scale)


def norm_back(cotangent, normed, scale):
    mean_one = jnp.mean(cotangent, axis=-1, keepdims=True)
    mean_two = jnp.mean(cotangent * normed, axis=-1, keepdims=True)
    return scale * (cotangent - mean_one - normed * mean_two)


def features(vectors, draws):
    wide = vectors.astype(F32)
    square = jnp.sum(wide * wide, axis=0, keepdims=True) * (0.5 / math.sqrt(HD))
    return jnp.exp(mat_tn(draws, vectors) - (square + 0.5 * math.log(FEAT)))


def spread(rows, marks):
    return [rows * marks[u : u + 1] for u in range(NBUCK)]


def pick(stacked, marks):
    total = stacked[0:HD] * marks[0:1]
    for u in range(1, NBUCK):
        total = total + stacked[u * HD : (u + 1) * HD] * marks[u : u + 1]
    return total


def away_marks(hot):
    live = (lax.broadcasted_iota(jnp.int32, hot.shape, 0) < NBUCK).astype(F32)
    return live - hot.astype(F32)


def partner(own, r):
    x, core = own // 2, own % 2
    if r & 2:
        x = 1 - x
    if r & 1:
        core = 1 - core
    return 2 * x + core


def as_row(ref):
    return ref[...].reshape(1, ref.shape[0])


def aligned(count):
    return -(-count // 16) * 16


def remote(src, dst, send, recv, place):
    return pltpu.make_async_remote_copy(
        src_ref=src, dst_ref=dst, send_sem=send, recv_sem=recv, device_id=place, device_id_type=MESH
    )


def head_rows(h, kind, heads):
    return pl.ds(pl.multiple_of((kind * heads + h) * HD, HD), HD)


def attend_kernel(
    bucket, hidden, gain_ref, shift_ref, bias_ref, weight_any, draws_in, grad, down_any,
    parts_any, mix_any, act_grad_any, proj_out, state_out, mixed_out, den_out, hot_out, weight_out, draws_out,
    soft_out, phi_q_out, phi_k_out,
    parts, mix_land, mix_send, raw, bias_row, bias_scr, draws_land, down_vm, act_grad,
    query_scr, key_scr, value_scr, low_scr,
    raw_sem, part_send, part_recv, draw_send, draw_recv, mix_send_sem, mix_recv_sem, out_sem,
    down_sem, act_sem,
):
    s, h = pl.program_id(0), pl.program_id(1)
    seqs, rows, model = hidden.shape
    heads = draws_out.shape[0]
    total = GROUP * rows
    width = heads * HD
    own = lax.axis_index("feat")
    near, across = {"feat": partner(own, 1)}, {"feat": partner(own, 2)}

    def part_copy(q, kind):
        src, dst, place = ((0, 1, near), (0, 2, across), (2, 3, near))[kind]
        return remote(
            parts.at[q, src], parts.at[q, dst], part_send.at[q, kind], part_recv.at[q, kind], place
        )

    def draw_copy(r):
        other = partner(own, r)
        return remote(
            draws_in.at[pl.ds(other * heads, heads)], draws_land.at[r - 1],
            draw_send.at[r - 1], draw_recv.at[r - 1], {"feat": other},
        )

    def mix_copy(q, g, r):
        span = pl.ds(pl.multiple_of(g * HD, HD), HD)
        return remote(
            mix_send.at[q, r - 1, span], mix_land.at[q, r, span], mix_send_sem.at[q, g, r - 1],
            mix_recv_sem.at[q, g, r - 1], {"feat": partner(own, r)},
        )

    down_copy = pltpu.make_async_copy(down_any, down_vm, down_sem)
    act_copy = pltpu.make_async_copy(act_grad, act_grad_any, act_sem)

    def raw_copy(j):
        cols = pl.ds(pl.multiple_of(j * model + (own // 2) * 2 * width, 2 * width), 2 * width)
        return pltpu.make_async_copy(weight_any.at[:, cols], raw.at[j], raw_sem.at[j])

    def out_copy(q):
        return pltpu.make_async_copy(parts.at[q], parts_any.at[q], out_sem.at[q])

    @pl.when((s == 0) & (h == 0))
    def _():
        for j in range(3):
            raw_copy(j).start()
        down_copy.start()
        barrier = pltpu.get_barrier_semaphore()
        for r in (1, 2, 3):
            pl.semaphore_signal(
                barrier, inc=1, device_id={"feat": partner(own, r)}, device_id_type=MESH
            )
        gain, shift = as_row(gain_ref), as_row(shift_ref)
        first = row_stats(hidden[0].astype(F32))[0] * gain + shift
        parts[0, 0] = first.astype(BF16)
        pl.semaphore_wait(barrier, 3)
        part_copy(0, 1).start()
        part_copy(0, 0).start()
        for r in (1, 2, 3):
            draw_copy(r).start()
        for q in range(1, seqs):
            normed = row_stats(hidden[q].astype(F32))[0] * gain + shift
            parts[q, 0] = normed.astype(BF16)
            part_copy(q, 1).start()
            part_copy(q, 0).start()
        core = own % 2
        bias_row[...] = as_row(bias_ref)
        for j in range(3):
            raw_copy(j).wait()
            piece = raw[j].astype(F32)
            piece = jnp.where(core == 0, piece[:, 0:width], piece[:, width:])
            weight_out[j * width : (j + 1) * width] = piece.T.astype(BF16)
            cols = pl.ds(pl.multiple_of(j * model + (own // 2) * 2 * width, 2 * width), 2 * width)
            pair = jnp.broadcast_to(bias_row[:, cols], (128, 2 * width))
            pair = jnp.where(core == 0, pair[:, 0:width], pair[:, width:])
            bias_scr[j * width : (j + 1) * width] = pair.T
        down_copy.wait()
        for t in range(act_grad.shape[0]):
            tile = down_vm[t * model : (t + 1) * model]
            for q in range(seqs):
                act_grad[t, q * rows : (q + 1) * rows] = mat_nt(grad[q], tile).astype(BF16)
        act_copy.start()
        part_copy(0, 1).wait_recv()
        part_copy(0, 2).start()
        for r in (1, 2, 3):
            draw_copy(r).wait_recv()
        mine = draws_in[pl.ds(own * heads, heads)]
        draws_out[...] = jnp.concatenate(
            [mine] + [draws_land[r - 1] for r in (1, 2, 3)], axis=2
        )

    @pl.when(h == 0)
    def _():
        per = rows // BLOCK
        lanes = lax.broadcasted_iota(jnp.int32, (16, total), 1) // BLOCK
        level = lax.broadcasted_iota(jnp.int32, (16, total), 0)
        ids = jnp.full((16, total), -1, jnp.int32)
        for r in range(GROUP):
            for i in range(per):
                ids = jnp.where(
                    lanes == r * per + i, bucket[s, partner(own, r) * per + i, 0], ids
                )
        hot_out[...] = (ids == level).astype(F32).astype(BF16)

        def project(r):
            cols = slice(r * rows, (r + 1) * rows)
            piece = mat_nt(weight_out[...], parts[s, r]) + bias_scr[:, 0:1]
            proj_out[:, cols] = piece.astype(BF16)

        project(0)
        part_copy(s, 0).wait_recv()
        project(1)
        project(2)
        part_copy(s, 2).wait_recv()
        project(3)
        out_copy(s).start()

    query = proj_out[head_rows(h, 0, heads)]
    key = proj_out[head_rows(h, 1, heads)]
    value = proj_out[head_rows(h, 2, heads)]
    draws = draws_out[h]
    hot = hot_out[...]
    hot_wide = hot.astype(F32)
    away = away_marks(hot).astype(BF16)
    phi_q = features(query, draws).astype(BF16)
    phi_k = features(key, draws).astype(BF16)
    phi_q_out[...] = phi_q
    phi_k_out[...] = phi_k
    spread_value = jnp.concatenate(spread(value, away) + [away], axis=0)
    state = mat_nt(spread_value, phi_k).astype(BF16)
    state_out[...] = state
    low = mat(state, phi_q)
    low_scr[0:HD] = pick(low, hot_wide)
    low_den = jnp.sum(low[NBUCK * HD :] * hot_wide, axis=0, keepdims=True)
    low_scr[HD : HD + 8] = jnp.broadcast_to(low_den, (8, total))
    query_scr[...] = jnp.concatenate([query * (1.0 / math.sqrt(HD)), hot], axis=0).astype(BF16)
    key_scr[...] = jnp.concatenate([key, away * -FAR], axis=0).astype(F32).T.astype(BF16)
    value_scr[0:HD] = value
    value_scr[HD:] = jnp.ones((16, total), BF16)

    head_span = pl.ds(pl.multiple_of(h * HD, HD), HD)
    score = mat(key_scr[...], query_scr[:, 0:CHUNK])
    for c in range(total // CHUNK):
        cols = slice(c * CHUNK, (c + 1) * CHUNK)
        ahead = slice((c + 1) * CHUNK, (c + 2) * CHUNK)
        later = mat(key_scr[...], query_scr[:, ahead]) if ahead.stop <= total else None
        weights = jnp.exp(score).astype(BF16)
        score = later
        soft_out[:, cols] = weights
        exact = mat(value_scr[...], weights)
        den = low_scr[HD : HD + 8, cols] + exact[HD : HD + 8]
        mixed = (low_scr[0:HD, cols] + exact[0:HD]) / den[0:1]
        mixed_out[:, cols] = mixed
        den_out[:, cols] = den
        mixed_low = mixed.astype(BF16)
        for r in range(GROUP):
            low_col, high_col = max(cols.start, r * rows), min(cols.stop, (r + 1) * rows)
            if low_col < high_col:
                piece = mixed_low[:, low_col - cols.start : high_col - cols.start]
                inner = slice(low_col - r * rows, high_col - r * rows)
                if r:
                    mix_send[s, r - 1, head_span, inner] = piece
                else:
                    mix_land[s, 0, head_span, inner] = piece
    for r in (2, 3, 1):
        mix_copy(s, h, r).start()

    @pl.when((h == heads - 2) & (s < seqs - 1))
    def _():
        part_copy(s + 1, 1).wait_recv()
        part_copy(s + 1, 2).start()

    @pl.when((s == seqs - 1) & (h == heads - 1))
    def _():
        for q in range(seqs):
            for g in range(heads):
                for r in (1, 2, 3):
                    mix_copy(q, g, r).wait_recv()
        done = pltpu.make_async_copy(mix_land, mix_any, out_sem.at[seqs])
        done.start()
        for q in range(seqs):
            for kind in range(3):
                part_copy(q, kind).wait_send()
            for g in range(heads):
                for r in (1, 2, 3):
                    mix_copy(q, g, r).wait_send()
            out_copy(q).wait()
        act_copy.wait()
        for r in (1, 2, 3):
            draw_copy(r).wait_send()
        done.wait()


def attend(bucket, hidden, gain, shift, bias, weight, draws, grad, down):
    seqs, rows, model = hidden.shape
    tiles = down.shape[0] // model
    heads = draws.shape[0] // GROUP
    width = heads * HD
    total = GROUP * rows
    whole = lambda *shape: pl.BlockSpec(shape, lambda s, h: (0,) * len(shape))
    by_seq = lambda *shape: pl.BlockSpec((None,) + shape, lambda s, h: (s,) + (0,) * len(shape))
    by_head = lambda *shape: pl.BlockSpec(
        (None, None) + shape, lambda s, h: (s, h) + (0,) * len(shape)
    )
    anywhere = pl.BlockSpec(memory_space=pl.ANY)
    return pl.pallas_call(
        attend_kernel,
        grid=(seqs, heads),
        out_shape=(
            jax.ShapeDtypeStruct((seqs, GROUP, rows, model), BF16),
            jax.ShapeDtypeStruct((seqs, GROUP, width, rows), BF16),
            jax.ShapeDtypeStruct((tiles, seqs * rows, model), BF16),
            jax.ShapeDtypeStruct((seqs, 3 * width, total), BF16),
            jax.ShapeDtypeStruct((seqs, heads, STATES, FEAT), BF16),
            jax.ShapeDtypeStruct((seqs, heads, HD, total), F32),
            jax.ShapeDtypeStruct((seqs, heads, 8, total), F32),
            jax.ShapeDtypeStruct((seqs, 16, total), BF16),
            jax.ShapeDtypeStruct((3 * width, model), BF16),
            jax.ShapeDtypeStruct((heads, HD, FEAT), BF16),
            jax.ShapeDtypeStruct((seqs, heads, total, total), BF16),
            jax.ShapeDtypeStruct((seqs, heads, FEAT, total), BF16),
            jax.ShapeDtypeStruct((seqs, heads, FEAT, total), BF16),
        ),
        in_specs=[
            pl.BlockSpec(memory_space=pltpu.SMEM),
            whole(seqs, rows, model), whole(model), whole(model), whole(3 * model), anywhere,
            whole(*draws.shape), whole(seqs, rows, model), anywhere,
        ],
        out_specs=(
            anywhere, anywhere, anywhere, by_seq(3 * width, total), by_head(STATES, FEAT), by_head(HD, total),
            by_head(8, total), by_seq(16, total), whole(3 * width, model), whole(heads, HD, FEAT),
            by_head(total, total), by_head(FEAT, total), by_head(FEAT, total),
        ),
        scratch_shapes=[
            pltpu.VMEM((seqs, GROUP, rows, model), BF16),
            pltpu.VMEM((seqs, GROUP, width, rows), BF16),
            pltpu.VMEM((seqs, 3, width, rows), BF16),
            pltpu.VMEM((3, model, 2 * width), BF16),
            pltpu.VMEM((1, 3 * model), F32),
            pltpu.VMEM((3 * width, 128), F32),
            pltpu.VMEM((3, heads, HD, draws.shape[2]), BF16),
            pltpu.VMEM(down.shape, BF16),
            pltpu.VMEM((tiles, seqs * rows, model), BF16),
            pltpu.VMEM((HD + 16, total), BF16),
            pltpu.VMEM((total, HD + 16), BF16),
            pltpu.VMEM((HD + 16, total), BF16),
            pltpu.VMEM((HD + 8, total), F32),
            pltpu.SemaphoreType.DMA((3,)),
            pltpu.SemaphoreType.DMA((seqs, 3)),
            pltpu.SemaphoreType.DMA((seqs, 3)),
            pltpu.SemaphoreType.DMA((3,)),
            pltpu.SemaphoreType.DMA((3,)),
            pltpu.SemaphoreType.DMA((seqs, heads, 3)),
            pltpu.SemaphoreType.DMA((seqs, heads, 3)),
            pltpu.SemaphoreType.DMA((seqs + 1,)),
            pltpu.SemaphoreType.DMA,
            pltpu.SemaphoreType.DMA,
        ],
        compiler_params=pltpu.CompilerParams(
            vmem_limit_bytes=VMEM, collective_id=1, has_side_effects=True
        ),
        cost_estimate=pl.CostEstimate(
            flops=24_000_000_000, bytes_accessed=20_000_000, transcendentals=0
        ),
        name="attend",
    )(bucket, hidden, gain, shift, bias, weight, draws, grad, down)


def block_kernel(
    direct, parts_ref, hidden, grad, out_w, out_b, gain_ref, shift_ref, down_b, up_b, up, down,
    act_grad_ref,
    layer_out, resid_out, grads_any, first_any, slab_any, down_any, up_any, tail_any,
    mixed_t, resid_scr, in_scr, in_t, acc_out, acc_in, act_scr, pre_scr, vec_scr, bias_row, back_t,
    slab_vm, down_vm, up_vm, tail_vm, grads_vm, first_land, send_sem, recv_sem, out_sem,
):
    step = pl.program_id(0)
    model = hidden.shape[1]
    count = hidden.shape[0] // CHUNK
    tiles = act_scr.shape[0]
    spans = [slice(c * CHUNK, (c + 1) * CHUNK) for c in range(count)]
    owners = slab_vm.shape[0] if direct else tail_vm.shape[0]
    small = model // owners
    share = tiles * small
    own = lax.axis_index("feat")
    barrier = pltpu.get_barrier_semaphore()

    part = model // GROUP

    def group_rows(r):
        return pl.ds(pl.multiple_of(partner(own, r) * part, part), part)

    def grad_copy(r):
        return remote(
            grads_vm.at[0, r], first_land.at[r - 1], send_sem.at[r - 1], recv_sem.at[r - 1],
            {"feat": partner(own, r)},
        )

    def out_copy(i):
        pieces = [(down_vm, down_any), (up_vm, up_any), (tail_vm, tail_any)]
        if direct:
            cuts = (0, share, 2 * share, slab_vm.shape[1])
            pieces = [
                (slab_vm.at[:, pl.ds(low, high - low)], slab_any.at[:, pl.ds(low, high - low)])
                for low, high in zip(cuts, cuts[1:])
            ]
        src, dst = (
            *pieces, (grads_vm, grads_any), (first_land, first_any),
        )[i]
        return pltpu.make_async_copy(src, dst, out_sem.at[i])

    @pl.when(step == 0)
    def _():
        for r in (1, 2, 3):
            pl.semaphore_signal(
                barrier, inc=1, device_id={"feat": partner(own, r)}, device_id_type=MESH
            )
        for c, span in enumerate(spans):
            for r in range(GROUP):
                mixed_t[group_rows(r), span] = parts_ref[c, r]
            resid = hidden[span].astype(F32) + mat_tn(mixed_t[:, span], out_w[...]) + as_row(out_b)
            resid_scr[span] = resid
            normed, _ = row_stats(resid)
            inner = normed * as_row(gain_ref) + as_row(shift_ref)
            in_scr[span] = inner.astype(BF16)
            in_t[:, span] = inner.T.astype(BF16)
        acc_out[...] = jnp.zeros_like(acc_out)
        acc_in[...] = jnp.zeros_like(acc_in)
        bias_row[...] = as_row(up_b)

    slope = math.sqrt(2.0 / math.pi)
    total = jnp.zeros((1, model), F32)
    up_bias = bias_row[:, pl.ds(pl.multiple_of(step * model, model), model)]
    for span in spans:
        pre = mat(in_scr[span], up[...]) + up_bias
        square = pre * pre
        tanh = jnp.tanh(pre * (slope + (slope * 0.044715) * square))
        half = 0.5 * (1.0 + tanh)
        act = (pre * half).astype(BF16)
        bend = half + (0.5 * pre) * (1.0 - tanh * tanh) * (
            slope + (3.0 * slope * 0.044715) * square
        )
        pre_grad = act_grad_ref[span].astype(F32) * bend
        total = total + jnp.sum(pre_grad, axis=0, keepdims=True)
        pre_low = pre_grad.astype(BF16)
        act_scr[step, span] = act
        pre_scr[step, span] = pre_low
        acc_out[span] += mat(act, down[...])
        acc_in[span] += mat_nt(pre_low, up[...])
    vec_scr[pl.ds(4 + step, 1)] = total

    @pl.when(step == pl.num_programs(0) - 1)
    def _():
        pl.semaphore_wait(barrier, 3)
        sums = [jnp.zeros((1, model), F32) for _ in range(4)]
        for c, span in enumerate(spans):
            resid = resid_scr[span]
            normed, scale = row_stats(resid)
            inner_grad = acc_in[span]
            wide = grad[span].astype(F32)
            resid_grad = wide + norm_back(inner_grad * as_row(gain_ref), normed, scale)
            resid_out[span] = resid_grad
            low = resid_grad.astype(BF16)
            in_scr[span] = low
            back_t[...] = mat_nt(out_w[...], low).astype(BF16)
            for r in (2, 3, 1, 0):
                grads_vm[c, r] = back_t[group_rows(r)]
                if c == 0 and r:
                    grad_copy(r).start()
            layer_out[span] = (resid + acc_out[span] + as_row(down_b)).astype(BF16)
            for i, term in enumerate((wide, resid_grad, inner_grad * normed, inner_grad)):
                sums[i] = sums[i] + jnp.sum(term, axis=0, keepdims=True)
        out_copy(3).start()
        for i in range(4):
            vec_scr[i : i + 1] = sums[i]
        for t in range(tiles):
            down_term = mat_tn(act_scr[t], grad[...])
            if direct:
                for i in range(model // share):
                    slab_vm[t * (model // share) + i, 0:share] = down_term[
                        i * share : (i + 1) * share
                    ].astype(BF16)
            else:
                down_vm[t * model : (t + 1) * model] = down_term.astype(BF16)
        out_copy(0).start()
        for t in range(0, tiles, 2):
            terms = [mat(in_t[...], pre_scr[t]), mat(in_t[...], pre_scr[t + 1])]
            if direct:
                for i in range(owners):
                    own_rows = slice(i * small, (i + 1) * small)
                    slab_vm[i, share + t * small : share + (t + 2) * small] = jnp.concatenate(
                        [term[own_rows] for term in terms], axis=0
                    ).astype(BF16)
            else:
                for u, term in enumerate(terms):
                    up_vm[:, (t + u) * model : (t + u + 1) * model] = term.astype(BF16)
        out_copy(1).start()
        out_term = mat(mixed_t[...], in_scr[...])
        fill = aligned(small + 8) - small - 8
        extra = [jnp.zeros((fill, model), F32)] if fill else []
        for i in range(owners):
            rest = jnp.concatenate(
                [out_term[i * small : (i + 1) * small], vec_scr[...]] + extra, axis=0
            ).astype(BF16)
            if direct:
                slab_vm[i, 2 * share :] = rest
            else:
                tail_vm[i] = rest
        out_copy(2).start()
        for r in (1, 2, 3):
            grad_copy(r).wait_recv()
        out_copy(4).start()
        for r in (1, 2, 3):
            grad_copy(r).wait_send()
        for i in range(5):
            out_copy(i).wait()


def block_layer(
    parts, hidden, grad, out_w, out_b, gain, shift, down_b, up_b, up, down, act_grad, devices
):
    tokens, model = hidden.shape
    ff = up.shape[1]
    steps = ff // model
    seqs = parts.shape[0]
    small, share = model // devices, ff // devices
    direct = small % 8 == 0 and share % 16 == 0
    tail_rows = aligned(small + 8)
    single = pl.Buffered(1)
    whole = lambda *shape: pl.BlockSpec(
        shape, lambda t: (0,) * len(shape), pipeline_mode=single
    )
    anywhere = pl.BlockSpec(memory_space=pl.ANY)
    unused = (16, 128)
    slab_shape, down_shape, up_shape, tail_shape = (
        ((devices, 2 * share + tail_rows, model), unused, unused, unused) if direct
        else (unused, (ff, model), (model, ff), (devices, tail_rows, model))
    )
    layer_out, resid_grad, grads, first, slab, down_grad, up_grad, tail = pl.pallas_call(
        lambda *refs: block_kernel(direct, *refs),
        grid=(steps,),
        out_shape=(
            jax.ShapeDtypeStruct((tokens, model), BF16),
            jax.ShapeDtypeStruct((tokens, model), F32),
            jax.ShapeDtypeStruct(parts.shape, BF16),
            jax.ShapeDtypeStruct((3,) + parts.shape[2:], BF16),
            jax.ShapeDtypeStruct(slab_shape, BF16),
            jax.ShapeDtypeStruct(down_shape, BF16),
            jax.ShapeDtypeStruct(up_shape, BF16),
            jax.ShapeDtypeStruct(tail_shape, BF16),
        ),
        in_specs=[
            whole(*parts.shape), whole(tokens, model), whole(tokens, model), whole(model, model),
            whole(model), whole(model), whole(model), whole(model), whole(ff),
            pl.BlockSpec((model, model), lambda t: (0, t)),
            pl.BlockSpec((model, model), lambda t: (t, 0)),
            pl.BlockSpec((None, tokens, model), lambda t: (t, 0, 0)),
        ],
        out_specs=(
            whole(tokens, model), whole(tokens, model), anywhere, anywhere, anywhere, anywhere,
            anywhere, anywhere,
        ),
        scratch_shapes=[
            pltpu.VMEM((model, tokens), BF16),
            pltpu.VMEM((tokens, model), F32),
            pltpu.VMEM((tokens, model), BF16),
            pltpu.VMEM((model, tokens), BF16),
            pltpu.VMEM((tokens, model), F32),
            pltpu.VMEM((tokens, model), F32),
            pltpu.VMEM((steps, tokens, model), BF16),
            pltpu.VMEM((steps, tokens, model), BF16),
            pltpu.VMEM((8, model), F32),
            pltpu.VMEM((1, ff), F32),
            pltpu.VMEM((model, CHUNK), BF16),
            pltpu.VMEM(slab_shape, BF16),
            pltpu.VMEM(down_shape, BF16),
            pltpu.VMEM(up_shape, BF16),
            pltpu.VMEM(tail_shape, BF16),
            pltpu.VMEM(parts.shape, BF16),
            pltpu.VMEM((3,) + parts.shape[2:], BF16),
            pltpu.SemaphoreType.DMA((3,)),
            pltpu.SemaphoreType.DMA((3,)),
            pltpu.SemaphoreType.DMA((5,)),
        ],
        compiler_params=pltpu.CompilerParams(
            vmem_limit_bytes=VMEM, collective_id=3, has_side_effects=True
        ),
        cost_estimate=pl.CostEstimate(
            flops=26_000_000_000, bytes_accessed=30_000_000, transcendentals=0
        ),
        name="block_layer",
    )(parts, hidden, grad, out_w, out_b, gain, shift, down_b, up_b, up, down, act_grad)
    if not direct:
        fit = lambda a: jnp.pad(a, ((0, 0), (0, aligned(a.shape[1]) - a.shape[1]), (0, 0)))
        down_grad = fit(down_grad.reshape(devices, share, model))
        up_grad = up_grad.reshape(devices, small, ff // model, model).transpose(0, 2, 1, 3)
        up_grad = fit(up_grad.reshape(devices, ff // model * small, model))
        slab = jnp.concatenate([down_grad, up_grad, tail], axis=1)
    return layer_out, resid_grad, grads, first, slab


def attend_back_kernel(
    dp_size, x_ref, grads_ref, first_ref, weight, draws_ref, hot_ref, proj, state_ref, mixed_ref, den_ref,
    soft_ref, phi_q_ref, phi_k_ref, slab_any,
    attn_out, ring_out, proj_out,
    grad_scr, num_scr, value_scr, score_scr, exact_scr, proj_scr,
    grad_land, near_send, near_land, far_keep, far_send, far_land,
    mine, met, ring_land, cross_land,
    weight_acc, own_send, pair_land, own_mid, own_land, part_send, part_land,
    grad_sems, near_sems, far_sems, mine_sem, met_send, met_sems, ring_send, ring_sems, cross_sems,
    pair_sems, own_send_sem, own_sems,
    part_sems,
):
    s, h = pl.program_id(0), pl.program_id(1)
    seqs, heads = pl.num_programs(0), pl.num_programs(1)
    rows, model = x_ref.shape[1], x_ref.shape[2]
    head_count = proj_scr.shape[0] // (3 * HD)
    width = head_count * HD
    total = GROUP * rows
    root = 1.0 / math.sqrt(HD)
    own, me = lax.axis_index("feat"), lax.axis_index("dp")
    own_x, own_core = own // 2, own % 2
    near, across = {"feat": partner(own, 1)}, {"feat": partner(own, 2)}
    last = (s == seqs - 1) & (h == heads - 1)

    def grad_copy(q, r):
        return remote(
            grads_ref.at[q, r], grad_land.at[q - 1, r - 1], grad_sems.at[0, q - 1, r - 1],
            grad_sems.at[1, q - 1, r - 1], {"feat": partner(own, r)},
        )

    def near_copy(q, i):
        return remote(
            near_send.at[i], near_land.at[q, i], near_sems.at[0, q, i], near_sems.at[1, q, i], near
        )

    def far_copy(q):
        return remote(far_send, far_land.at[q], far_sems.at[0, q], far_sems.at[1, q], across)

    half = dp_size // 2
    parity, pair = lax.rem(me, 2), lax.div(me, 2)
    spot = pair + parity * (dp_size - 1 - 2 * pair)

    def at_spot(p):
        p = lax.rem(p + dp_size, dp_size)
        upper = lax.div(p, half)
        return 2 * p + upper * (2 * dp_size - 1 - 4 * p)

    places = ({"dp": at_spot(spot + 1)}, {"dp": at_spot(spot - 1)})

    def chunk(k, way):
        return at_spot(spot - 1 - k) if way == 0 else at_spot(spot + 1 + k)

    def mine_copy(k, way, owner):
        return pltpu.make_async_copy(
            slab_any.at[owner + own_core], mine.at[k, way], mine_sem.at[k, way]
        )

    def met_copy(k, way, owner):
        return remote(
            slab_any.at[owner + 1 - own_core], met.at[k, way], met_send, met_sems.at[k, way], near
        )

    cut = aligned(mine.shape[2] // 2)
    halves = (pl.ds(0, cut), pl.ds(cut, mine.shape[2] - cut))

    def ring_copy(k, way, part):
        return remote(
            mine.at[k, way, halves[part]], ring_land.at[k, way, halves[part]], ring_send,
            ring_sems.at[k, way, part], places[way],
        )

    def cross_copy(part):
        return remote(
            mine.at[dp_size - 1, 1 - own_x, halves[part]], cross_land.at[halves[part]],
            cross_sems.at[0, part], cross_sems.at[1, part], across,
        )

    def begin_pieces(k):
        for way in range(2):
            owner = chunk(k, way) * GROUP + 2 * way
            met_copy(k, way, owner).start()
            mine_copy(k, way, owner).start()

    def ring_step(k, part):
        span = halves[part]
        if part == 0:

            @pl.when(k + 2 < dp_size)
            def _():
                begin_pieces(k + 2)

        @pl.when(k < dp_size)
        def _():
            for way in range(2):
                if part == 0:
                    mine_copy(k, way, 0).wait()
                    met_copy(k, way, 0).wait_recv()

                @pl.when(k == 0)
                def _():
                    mine[k, way, span] = mine[k, way, span] + met[k, way, span]

                @pl.when(k > 0)
                def _():
                    ring_copy(k - 1, way, part).wait_recv()
                    chip = mine[k, way, span] + met[k, way, span]
                    mine[k, way, span] = chip + ring_land[k - 1, way, span]

                @pl.when(k < dp_size - 1)
                def _():
                    ring_copy(k, way, part).start()

            @pl.when(k == dp_size - 1)
            def _():
                cross_copy(part).start()

        @pl.when(k == dp_size)
        def _():
            cross_copy(part).wait_recv()
            ring_out[span] = mine[dp_size - 1, own_x, span].astype(F32) + cross_land[span].astype(F32)

    def ring_turn(part):
        turn = s * heads + h
        count = seqs * heads
        steps = dp_size + 1

        def body(k, carry):
            ring_step(k, part)
            return carry

        lax.fori_loop(lax.div(turn * steps, count), lax.div((turn + 1) * steps, count), body, 0)

    mate = me + 1 - 2 * parity

    def pair_copy(q):
        return remote(
            own_send.at[q, 1 - parity], pair_land.at[q], pair_sems.at[0, q], pair_sems.at[1, q],
            {"dp": mate},
        )

    def own_copy(q, k):
        to = lax.rem(pair + k, half)
        return remote(
            own_mid.at[q, to], own_land.at[q, k], own_send_sem, own_sems.at[q, k],
            {"dp": 2 * to + parity},
        )

    base = model // dp_size

    def folded(values):
        middle = values.shape[0] // 2
        return jnp.concatenate([values[0:middle], values[middle:]], axis=1)

    def begin_own(q):
        turned = weight_acc[pl.ds(pl.multiple_of(q * 3 * HD, 3 * HD), 3 * HD)].T
        biases = turned[model : model + 16]
        blank = own_send.shape[3] - base - base // 2 - 16
        extra = [jnp.zeros((blank, 2 * HD), F32)] if blank else []
        for c in range(dp_size):
            block = turned[c * base : (c + 1) * base]
            own_send[q, c % 2, c // 2] = jnp.concatenate(
                [
                    block[:, 0 : 2 * HD], folded(block[:, 2 * HD :]), biases[0:8, 0 : 2 * HD],
                    folded(biases[:, 2 * HD :]),
                ] + extra,
                axis=0,
            ).astype(BF16)
        pair_copy(q).start()

    def relay_own(q):
        pair_copy(q).wait_recv()
        own_mid[q] = (own_send[q, parity].astype(F32) + pair_land[q].astype(F32)).astype(BF16)

        def start(k, carry):
            own_copy(q, k).start()
            return carry

        lax.fori_loop(1, half, start, 0)

    def part_copy(r):
        other = partner(own, r)
        return remote(
            part_send.at[other], part_land.at[r - 1], part_sems.at[0, r - 1],
            part_sems.at[1, r - 1], {"feat": other},
        )

    def seq_span(q):
        return pl.ds(pl.multiple_of(q * rows, rows), rows)

    def add_near(q):
        near_copy(q, 1).wait_recv()

        @pl.when(q > 0)
        def _():
            far_copy(q - 1).wait_send()

        far_send[...] = (far_keep[1] + near_land[q, 1].astype(F32)).astype(BF16)
        far_copy(q).start()
        near_copy(q, 0).wait_recv()
        attn_out[seq_span(q)] = far_keep[0] + near_land[q, 0].astype(F32)

    def finish(q):
        far_copy(q).wait_recv()
        span = seq_span(q)
        attn_out[span] = attn_out[span] + far_land[q].astype(F32)

    @pl.when((s == 0) & (h == 0))
    def _():
        barrier = pltpu.get_barrier_semaphore()
        for r in (1, 2, 3):
            pl.semaphore_signal(
                barrier, inc=1, device_id={"feat": partner(own, r)}, device_id_type=MESH
            )

        def greet(k, carry):
            pl.semaphore_signal(
                barrier, inc=1, device_id={"dp": lax.rem(me + k, dp_size)}, device_id_type=MESH
            )
            return carry

        lax.fori_loop(1, dp_size, greet, 0)
        pl.semaphore_wait(barrier, 3 + dp_size - 1)
        for q in range(1, near_land.shape[0]):
            for r in (2, 3, 1):
                grad_copy(q, r).start()
        for k in range(2):
            begin_pieces(k)
        weight_acc[...] = jnp.zeros_like(weight_acc)

    @pl.when(h == 0)
    def _():
        grad_scr[:, 0:rows] = grads_ref[s, 0].astype(F32)

        @pl.when(s == 0)
        def _():
            for r in (1, 2, 3):
                grad_scr[:, r * rows : (r + 1) * rows] = first_ref[r - 1].astype(F32)

        @pl.when(s > 0)
        def _():
            for r in (1, 2, 3):
                grad_copy(s, r).wait_recv()
                grad_scr[:, r * rows : (r + 1) * rows] = grad_land[s - 1, r - 1].astype(F32)

    query = proj[head_rows(h, 0, head_count)]
    key = proj[head_rows(h, 1, head_count)]
    value = proj[head_rows(h, 2, head_count)]
    draws = draws_ref[...]
    draws_ext = jnp.concatenate([draws, jnp.ones((16, FEAT), BF16)], axis=0)
    hot = hot_ref[...]
    away_wide = away_marks(hot)
    away = away_wide.astype(BF16)
    inverse = 1.0 / den_ref[0:1]
    head_grad = grad_scr[pl.ds(pl.multiple_of(h * HD, HD), HD)]
    grad_num = (head_grad * inverse).astype(BF16)
    grad_den = -jnp.sum(head_grad * mixed_ref[...], axis=0, keepdims=True) * inverse
    den_rows = jnp.broadcast_to(grad_den, (16, total)).astype(BF16)
    spread_grad = jnp.concatenate(spread(grad_num, hot) + [den_rows * hot], axis=0)
    spread_value = jnp.concatenate(spread(value, away) + [away], axis=0)

    phi_q, phi_k = phi_q_ref[...], phi_k_ref[...]
    state_grad = mat_nt(spread_grad, phi_q).astype(BF16)
    phi_q_grad = mat_tn(state_ref[...], spread_grad)
    phi_k_grad = mat_tn(state_grad, spread_value)
    value_low = mat(state_grad[0 : NBUCK * HD], phi_k)
    scaled_q = phi_q_grad.astype(BF16) * phi_q
    back_q = mat(draws_ext, scaled_q)
    scaled_k = phi_k_grad.astype(BF16) * phi_k
    back_k = mat(draws_ext, scaled_k)
    value_grad = pick(value_low, away_wide)
    query_grad = back_q[0:HD] - query.astype(F32) * (back_q[HD : HD + 1] * root)
    key_grad = back_k[0:HD] - key.astype(F32) * (back_k[HD : HD + 1] * root)

    ring_turn(0)
    one = (lax.broadcasted_iota(jnp.int32, hot.shape, 0) < 1).astype(F32).astype(BF16)
    num_scr[...] = jnp.concatenate([grad_num, den_rows], axis=0)
    value_scr[...] = jnp.concatenate([value, one], axis=0).astype(F32).T.astype(BF16)

    later = mat(value_scr[...], num_scr[:, 0:CHUNK])
    for c in range(total // CHUNK):
        cols = slice(c * CHUNK, (c + 1) * CHUNK)
        ahead = slice((c + 1) * CHUNK, (c + 2) * CHUNK)
        score = later
        later = mat(value_scr[...], num_scr[:, ahead]) if ahead.stop <= total else None
        score = score.astype(BF16) * soft_ref[:, cols]
        score_scr[:, cols] = score
        exact_scr[:, cols] = mat(proj[head_rows(h, 1, head_count)], score)
    query_grad = query_grad + exact_scr[...] * root
    key_grad = key_grad + mat_nt(query, score_scr[...]) * root
    value_grad = value_grad + mat_nt(grad_num, soft_ref[...])
    wide_grad = jnp.concatenate([query_grad, key_grad, value_grad], axis=0)
    low_grad = wide_grad.astype(BF16)
    for kind in range(3):
        proj_scr[head_rows(h, kind, head_count)] = low_grad[kind * HD : (kind + 1) * HD]
    weight_grad = mat(low_grad[:, 0:rows], x_ref[0])
    for r in (1, 2, 3):
        weight_grad = weight_grad + mat(low_grad[:, r * rows : (r + 1) * rows], x_ref[r])
    span = pl.ds(pl.multiple_of(h * 3 * HD, 3 * HD), 3 * HD)
    weight_acc[span, 0:model] += weight_grad
    weight_acc[span, model:] += jnp.broadcast_to(
        jnp.sum(wide_grad, axis=1, keepdims=True), (3 * HD, 128)
    )

    @pl.when(s == seqs - 1)
    def _():
        begin_own(h)

        @pl.when(h > 0)
        def _():
            relay_own(h - 1)

    @pl.when((s > 0) & (h == 0))
    def _():
        add_near(s - 1)

    @pl.when(h == heads - 1)
    def _():
        @pl.when(s > 0)
        def _():
            for i in range(2):
                near_copy(s - 1, i).wait_send()

        for r in (3, 1, 2, 0):
            term = mat_tn(proj_scr[:, r * rows : (r + 1) * rows], weight[...])
            if r % 2:
                near_send[r // 2] = term.astype(BF16)
                near_copy(s, r // 2).start()
            else:
                far_keep[r // 2] = term

    ring_turn(1)

    @pl.when(last)
    def _():
        add_near(s)
        relay_own(h)
        for q in range(near_land.shape[0] - 1):
            finish(q)

        sums = []
        for q in range(head_count):

            def arrive(k, carry):
                own_copy(q, k).wait_recv()
                return carry + own_land[q, k].astype(F32)

            sums.append(lax.fori_loop(1, half, arrive, own_mid[q, pair].astype(F32)))
        blocks, biases = [], []
        end = base + base // 2
        for total_sum in sums:
            value_rows = total_sum[base:end]
            value_rows = jnp.concatenate([value_rows[:, 0:HD], value_rows[:, HD:]], axis=0)
            blocks += [total_sum[0:base], value_rows]
            biases += [total_sum[end : end + 1], total_sum[end + 8 : end + 9, 0:HD]]
        joined = jnp.concatenate(blocks, axis=1)
        small = base // GROUP
        fill = jnp.broadcast_to(
            jnp.concatenate(biases, axis=1), (part_send.shape[1] - small, joined.shape[1])
        )
        for a in range(GROUP):
            part_send[a] = jnp.concatenate(
                [joined[a * small : (a + 1) * small], fill], axis=0
            ).astype(BF16)
        for r in (2, 3, 1):
            part_copy(r).start()
        finish(s)
        proj_out[own] = part_send[own].astype(F32)
        for r in (1, 2, 3):
            part_copy(r).wait_recv()
            proj_out[partner(own, r)] = part_land[r - 1].astype(F32)

        for i in range(2):
            near_copy(s, i).wait_send()
        far_copy(s).wait_send()
        for r in (1, 2, 3):
            part_copy(r).wait_send()
        for part in range(2):
            cross_copy(part).wait_send()
        for q in range(1, near_land.shape[0]):
            for r in (1, 2, 3):
                grad_copy(q, r).wait_send()
        for q in range(head_count):
            pair_copy(q).wait_send()
        every = pl.ds(0, half - 1)
        if half > 1:
            remote(
                own_mid.at[:, every], own_land.at[:, every], own_send_sem, own_sems.at[0, 0],
                {"dp": mate},
            ).wait_send()
        remote(
            mine.at[pl.ds(0, dp_size - 1)], ring_land, ring_send, ring_sems.at[0, 0, 0], places[0]
        ).wait_send()
        remote(mine, met, met_send, met_sems.at[0, 0], near).wait_send()


def attend_back(
    dp_size, parts, grads, first, weight, draws, hot, proj, state, mixed, den, soft, phi_q, phi_k,
    slab,
):
    seqs, _, rows, model = parts.shape
    heads = draws.shape[0]
    width = heads * HD
    total = GROUP * rows
    n = dp_size
    ring_rows = slab.shape[1]
    own_rows = aligned(model // n + model // n // 2 + 16)
    part_rows = aligned(model // (n * GROUP) + 1)
    single = pl.Buffered(1)
    whole = lambda *shape: pl.BlockSpec(
        shape, lambda s, h: (0,) * len(shape), pipeline_mode=single
    )
    mode = single if n > 16 else None
    by_seq = lambda *shape: pl.BlockSpec(
        (None,) + shape, lambda s, h: (s,) + (0,) * len(shape), pipeline_mode=mode
    )
    by_head = lambda *shape: pl.BlockSpec(
        (None, None) + shape, lambda s, h: (s, h) + (0,) * len(shape), pipeline_mode=mode
    )
    anywhere = pl.BlockSpec(memory_space=pl.ANY)
    dma = pltpu.SemaphoreType.DMA
    return pl.pallas_call(
        lambda *refs: attend_back_kernel(dp_size, *refs),
        grid=(seqs, heads),
        out_shape=(
            jax.ShapeDtypeStruct((seqs * rows, model), F32),
            jax.ShapeDtypeStruct((ring_rows, model), F32),
            jax.ShapeDtypeStruct((GROUP, part_rows, 3 * width), F32),
        ),
        in_specs=[
            by_seq(GROUP, rows, model), whole(*grads.shape), whole(*first.shape),
            whole(3 * width, model),
            pl.BlockSpec((None, HD, FEAT), lambda s, h: (h, 0, 0)),
            by_seq(16, total), by_seq(3 * width, total), by_head(STATES, FEAT), by_head(HD, total),
            by_head(8, total), by_head(total, total), by_head(FEAT, total), by_head(FEAT, total),
            anywhere,
        ],
        out_specs=(
            whole(seqs * rows, model), whole(ring_rows, model), whole(GROUP, part_rows, 3 * width),
        ),
        scratch_shapes=[
            pltpu.VMEM((width, total), F32),
            pltpu.VMEM((HD + 16, total), BF16),
            pltpu.VMEM((total, HD + 16), BF16),
            pltpu.VMEM((total, total), BF16),
            pltpu.VMEM((HD, total), F32),
            pltpu.VMEM((3 * width, total), BF16),
            pltpu.VMEM((seqs - 1, 3, width, rows), BF16),
            pltpu.VMEM((2, rows, model), BF16),
            pltpu.VMEM((seqs, 2, rows, model), BF16),
            pltpu.VMEM((2, rows, model), F32),
            pltpu.VMEM((rows, model), BF16),
            pltpu.VMEM((seqs, rows, model), BF16),
            pltpu.VMEM((n, 2, ring_rows, model), BF16),
            pltpu.VMEM((n, 2, ring_rows, model), BF16),
            pltpu.VMEM((n - 1, 2, ring_rows, model), BF16),
            pltpu.VMEM((ring_rows, model), BF16),
            pltpu.VMEM((3 * width, model + 128), F32),
            pltpu.VMEM((heads, 2, n // 2, own_rows, 2 * HD), BF16),
            pltpu.VMEM((heads, n // 2, own_rows, 2 * HD), BF16),
            pltpu.VMEM((heads, n // 2, own_rows, 2 * HD), BF16),
            pltpu.VMEM((heads, n // 2, own_rows, 2 * HD), BF16),
            pltpu.VMEM((GROUP, part_rows, 3 * width), BF16),
            pltpu.VMEM((3, part_rows, 3 * width), BF16),
            dma((2, seqs - 1, 3)),
            dma((2, seqs, 2)),
            dma((2, seqs)),
            dma((n, 2)),
            dma,
            dma((n, 2)),
            dma,
            dma((n - 1, 2, 2)),
            dma((2, 2)),
            dma((2, heads)),
            dma,
            dma((heads, n // 2)),
            dma((2, 3)),
        ],
        compiler_params=pltpu.CompilerParams(
            vmem_limit_bytes=VMEM + (3 * 1024 * 1024 if n > 16 else 0), collective_id=2, has_side_effects=True
        ),
        cost_estimate=pl.CostEstimate(
            flops=48_000_000_000, bytes_accessed=40_000_000, transcendentals=0
        ),
        name="attend_back",
    )(
        parts, grads, first, weight, draws, hot, proj, state, mixed, den, soft, phi_q, phi_k, slab,
    )


def finish_kernel(
    starts, heads, attn_grad, resid_grad, hidden, sums, proj_sums, weight_any, gain_ref, shift_ref,
    input_out, norm1_gain_out, norm1_bias_out, qkv_out, qkv_bias_out, out_out, out_bias_out,
    norm2_gain_out, norm2_bias_out, up_out, up_bias_out, down_out, down_bias_out,
    weight_vm, weight_sem,
):
    gain, shift = as_row(gain_ref), as_row(shift_ref)
    index = lax.axis_index("dp") * GROUP + lax.axis_index("feat")
    small, model = out_out.shape
    window = weight_vm.shape[0]
    begin = jnp.minimum(lax.div(index * small, 16) * 16, model - window)
    weight_copy = pltpu.make_async_copy(
        weight_any.at[pl.ds(pl.multiple_of(begin, 16), window)], weight_vm, weight_sem
    )

    @pl.when(pl.program_id(0) == 0)
    def _():
        weight_copy.start()

    normed, scale = row_stats(hidden[...].astype(F32))
    input_out[...] = resid_grad[...] + norm_back(attn_grad[...] * gain, normed, scale)

    @pl.when(pl.program_id(0) == 0)
    def _():
        share = down_out.shape[0]
        ff = up_out.shape[1]

        def own(row, size):
            length = row.shape[1]
            wide = jnp.broadcast_to(row, (8, length))
            back = lax.rem(length - lax.rem(index * size, length), length)
            return pltpu.roll(wide, back, 1)[0:1, 0:size]

        down_out[...] = sums[0:share]
        first = starts[0]
        up_out[...] = jnp.concatenate(
            [sums[first + i * small : first + (i + 1) * small] for i in range(ff // model)], axis=1
        )
        first = starts[1]
        out_out[...] = sums[first : first + small]
        totals = first + small
        for i, out in enumerate((down_bias_out, out_bias_out, norm2_gain_out, norm2_bias_out)):
            out[...] = own(sums[totals + i : totals + i + 1], small).reshape(small)
        per_row = model // share
        level = index // per_row
        row = jnp.zeros((1, model), F32)
        for i in range(ff // model):
            row = jnp.where(level == i, sums[totals + 4 + i : totals + 5 + i], row)
        up_bias_out[...] = own(row, share).reshape(share)

        pieces = []
        for kind in range(3):
            for f in range(GROUP):
                for h in range(heads):
                    lanes = slice((h * 3 + kind) * HD, (h * 3 + kind + 1) * HD)
                    pieces.append(proj_sums[f, 0 : small + 1, lanes])
        grid = jnp.concatenate(pieces, axis=1)
        weight_sum, bias_sum = grid[0:small], grid[small : small + 1]
        qkv_out[...] = weight_sum
        qkv_bias_out[...] = own(bias_sum, 3 * small).reshape(3 * small)
        weight_copy.wait()
        near_rows = weight_vm[...].astype(F32)
        step = math.gcd(small, 16)
        wide = near_rows[0:small]
        for offset in range(step, window - small + 1, step):
            wide = jnp.where(
                index * small - begin == offset, near_rows[offset : offset + small], wide
            )

        def to_row(column):
            column = jnp.concatenate(
                [column, jnp.zeros((-small % 128, 1), F32)], axis=0
            )
            return jnp.broadcast_to(column, (column.shape[0], 128)).T[0:1, 0:small]

        bias_grad = to_row(jnp.sum(wide * bias_sum, axis=1, keepdims=True))
        gain_grad = to_row(jnp.sum(wide * weight_sum, axis=1, keepdims=True))
        norm1_bias_out[...] = bias_grad.reshape(small)
        gain_grad = (gain_grad - own(shift, small) * bias_grad) / own(gain, small)
        norm1_gain_out[...] = gain_grad.reshape(small)


def finish_all(
    attn_grad, resid_grad, hidden, sums, proj_sums, weight, gain, shift, devices, ff, heads,
):
    seqs, rows, model = hidden.shape
    small, share = model // devices, ff // devices
    starts = (aligned(share), 2 * aligned(share))
    whole = lambda *shape: pl.BlockSpec(shape, lambda s: (0,) * len(shape))
    by_seq = pl.BlockSpec((rows, model), lambda s: (s, 0))
    shapes = (
        (small,), (small,), (small, 3 * model), (3 * small,), (small, model), (small,), (small,),
        (small,), (small, ff), (share,), (share, model), (small,),
    )
    return pl.pallas_call(
        lambda *refs: finish_kernel(starts, heads, *refs),
        grid=(seqs,),
        out_shape=(jax.ShapeDtypeStruct((seqs * rows, model), F32),)
        + tuple(jax.ShapeDtypeStruct(shape, F32) for shape in shapes),
        in_specs=[
            by_seq, by_seq, pl.BlockSpec((None, rows, model), lambda s: (s, 0, 0)),
            whole(*sums.shape), whole(*proj_sums.shape), pl.BlockSpec(memory_space=pl.ANY), whole(model),
            whole(model),
        ],
        out_specs=(by_seq,) + tuple(whole(*shape) for shape in shapes),
        scratch_shapes=[
            pltpu.VMEM((aligned(small) + 16, 3 * model), BF16), pltpu.SemaphoreType.DMA,
        ],
        compiler_params=pltpu.CompilerParams(vmem_limit_bytes=VMEM),
        name="finish_all",
    )(attn_grad, resid_grad, hidden, sums, proj_sums, weight, gain, shift)


def per_device(
    hidden_in, norm1_gain, norm1_bias, qkv_weight, qkv_bias, feature_draws, out_weight, out_bias,
    norm2_gain, norm2_bias, up_weight, up_bias, down_weight, down_bias, block_bucket, out_grad,
):
    seqs, rows, model = hidden_in.shape
    ff = up_weight.shape[1]
    dp_size = lax.axis_size("dp")
    devices = dp_size * GROUP
    heads = feature_draws.shape[0] // GROUP
    flat = (seqs * rows, model)

    (
        parts, mixed_parts, act_grad, proj, state, mixed, den, hot, own_weight, own_draws, soft,
        phi_q, phi_k,
    ) = attend(
        block_bucket, hidden_in, norm1_gain, norm1_bias, qkv_bias, qkv_weight, feature_draws,
        out_grad, down_weight,
    )
    layer_out, resid_grad, grads, first, slab = block_layer(
        mixed_parts, hidden_in.reshape(flat), out_grad.reshape(flat), out_weight, out_bias,
        norm2_gain, norm2_bias, down_bias, up_bias, up_weight, down_weight, act_grad, devices,
    )
    attn_grad, sums, proj_sums = attend_back(
        dp_size, parts, grads, first, own_weight, own_draws, hot, proj, state, mixed, den, soft,
        phi_q, phi_k, slab,
    )
    (
        input_grad, norm1_gain_sum, norm1_bias_sum, qkv_weight_sum, qkv_bias_sum, out_weight_sum,
        out_bias_sum, norm2_gain_sum, norm2_bias_sum, up_sum, up_bias_sum, down_sum, down_bias_sum,
    ) = finish_all(
        attn_grad, resid_grad, hidden_in, sums, proj_sums, qkv_weight, norm1_gain, norm1_bias,
        devices, ff, heads,
    )
    return (
        layer_out.reshape(hidden_in.shape), input_grad.reshape(hidden_in.shape), norm1_gain_sum,
        norm1_bias_sum, qkv_weight_sum, qkv_bias_sum, out_weight_sum, out_bias_sum, norm2_gain_sum,
        norm2_bias_sum, up_sum, up_bias_sum, down_sum, down_bias_sum,
    )


def solution(mesh):
    both = ("dp", "feat")
    rows = P("dp", "feat", None)
    in_specs = (
        rows, P(), P(), P(), P(), P(None, None, "feat"), P(), P(), P(), P(), P(), P(), P(), P(),
        P("dp", None, None), rows,
    )
    out_specs = (
        rows, rows, P(both), P(both), P(both, None), P(both), P(both, None), P(both), P(both),
        P(both), P(both, None), P(both), P(both, None), P(both),
    )
    return jax.shard_map(
        per_device, mesh=mesh, in_specs=in_specs, out_specs=out_specs, check_vma=False
    )
```

```python
import math

import jax
import jax.numpy as jnp
from jax import lax
from jax.experimental import pallas as pl
from jax.experimental.pallas import tpu as pltpu
from jax.sharding import PartitionSpec as P

HD = 64
FEAT = 256
BLOCK = 64
NBUCK = 4
GROUP = 4
CHUNK = 256
STATES = NBUCK * HD + 16
FAR = 16384.0
VMEM = 60 * 1024 * 1024

F32 = jnp.float32
BF16 = jnp.bfloat16
MESH = pl.DeviceIdType.MESH


def mat(left, right):
    return jnp.dot(left, right, preferred_element_type=F32)


def mat_nt(left, right):
    return lax.dot_general(left, right, (((1,), (1,)), ((), ())), preferred_element_type=F32)


def mat_tn(left, right):
    return lax.dot_general(left, right, (((0,), (0,)), ((), ())), preferred_element_type=F32)


def row_stats(values):
    row_mean = jnp.mean(values, axis=-1, keepdims=True)
    centered = values - row_mean
    scale = lax.rsqrt(jnp.mean(centered * centered, axis=-1, keepdims=True) + 1e-05)
    return (centered * scale, scale)


def norm_back(cotangent, normed, scale):
    mean_one = jnp.mean(cotangent, axis=-1, keepdims=True)
    mean_two = jnp.mean(cotangent * normed, axis=-1, keepdims=True)
    return scale * (cotangent - mean_one - normed * mean_two)


def features(vectors, draws):
    wide = vectors.astype(F32)
    square = jnp.sum(wide * wide, axis=0, keepdims=True) * (0.5 / math.sqrt(HD))
    return jnp.exp(mat_tn(draws, vectors) - (square + 0.5 * math.log(FEAT)))


def spread(rows, marks):
    return [rows * marks[u : u + 1] for u in range(NBUCK)]


def pick(stacked, marks):
    total = stacked[0:HD] * marks[0:1]
    for u in range(1, NBUCK):
        total = total + stacked[u * HD : (u + 1) * HD] * marks[u : u + 1]
    return total


def away_marks(hot):
    live = (lax.broadcasted_iota(jnp.int32, hot.shape, 0) < NBUCK).astype(F32)
    return live - hot.astype(F32)


def partner(own, r):
    x, core = own // 2, own % 2
    if r & 2:
        x = 1 - x
    if r & 1:
        core = 1 - core
    return 2 * x + core


def as_row(ref):
    return ref[...].reshape(1, ref.shape[0])


def aligned(count):
    return -(-count // 16) * 16


def remote(src, dst, send, recv, place):
    return pltpu.make_async_remote_copy(
        src_ref=src, dst_ref=dst, send_sem=send, recv_sem=recv, device_id=place, device_id_type=MESH
    )


def head_rows(h, kind, heads):
    return pl.ds(pl.multiple_of((kind * heads + h) * HD, HD), HD)


def attend_kernel(
    bucket, hidden, gain_ref, shift_ref, bias_ref, weight_any, draws_in, grad, down_any,
    parts_any, mix_any, act_grad_any, proj_out, state_out, mixed_out, den_out, hot_out, weight_out, draws_out,
    soft_out, phi_q_out, phi_k_out,
    parts, mix_land, mix_send, raw, bias_row, bias_scr, draws_land, down_vm, act_grad,
    query_scr, key_scr, value_scr, low_scr,
    raw_sem, part_send, part_recv, draw_send, draw_recv, mix_send_sem, mix_recv_sem, out_sem,
    down_sem, act_sem,
):
    s, h = pl.program_id(0), pl.program_id(1)
    seqs, rows, model = hidden.shape
    heads = draws_out.shape[0]
    total = GROUP * rows
    width = heads * HD
    own = lax.axis_index("feat")
    near, across = {"feat": partner(own, 1)}, {"feat": partner(own, 2)}

    def part_copy(q, kind):
        src, dst, place = ((0, 1, near), (0, 2, across), (2, 3, near))[kind]
        return remote(
            parts.at[q, src], parts.at[q, dst], part_send.at[q, kind], part_recv.at[q, kind], place
        )

    def draw_copy(r):
        other = partner(own, r)
        return remote(
            draws_in.at[pl.ds(other * heads, heads)], draws_land.at[r - 1],
            draw_send.at[r - 1], draw_recv.at[r - 1], {"feat": other},
        )

    def mix_copy(q, g, r):
        span = pl.ds(pl.multiple_of(g * HD, HD), HD)
        return remote(
            mix_send.at[q, r - 1, span], mix_land.at[q, r, span], mix_send_sem.at[q, g, r - 1],
            mix_recv_sem.at[q, g, r - 1], {"feat": partner(own, r)},
        )

    down_copy = pltpu.make_async_copy(down_any, down_vm, down_sem)
    act_copy = pltpu.make_async_copy(act_grad, act_grad_any, act_sem)

    def raw_copy(j):
        cols = pl.ds(pl.multiple_of(j * model + (own // 2) * 2 * width, 2 * width), 2 * width)
        return pltpu.make_async_copy(weight_any.at[:, cols], raw.at[j], raw_sem.at[j])

    def out_copy(q):
        return pltpu.make_async_copy(parts.at[q], parts_any.at[q], out_sem.at[q])

    @pl.when((s == 0) & (h == 0))
    def _():
        for j in range(3):
            raw_copy(j).start()
        down_copy.start()
        barrier = pltpu.get_barrier_semaphore()
        for r in (1, 2, 3):
            pl.semaphore_signal(
                barrier, inc=1, device_id={"feat": partner(own, r)}, device_id_type=MESH
            )
        gain, shift = as_row(gain_ref), as_row(shift_ref)
        first = row_stats(hidden[0].astype(F32))[0] * gain + shift
        parts[0, 0] = first.astype(BF16)
        pl.semaphore_wait(barrier, 3)
        part_copy(0, 1).start()
        part_copy(0, 0).start()
        for r in (1, 2, 3):
            draw_copy(r).start()
        for q in range(1, seqs):
            normed = row_stats(hidden[q].astype(F32))[0] * gain + shift
            parts[q, 0] = normed.astype(BF16)
            part_copy(q, 1).start()
            part_copy(q, 0).start()
        core = own % 2
        bias_row[...] = as_row(bias_ref)
        for j in range(3):
            raw_copy(j).wait()
            piece = raw[j].astype(F32)
            piece = jnp.where(core == 0, piece[:, 0:width], piece[:, width:])
            weight_out[j * width : (j + 1) * width] = piece.T.astype(BF16)
            cols = pl.ds(pl.multiple_of(j * model + (own // 2) * 2 * width, 2 * width), 2 * width)
            pair = jnp.broadcast_to(bias_row[:, cols], (128, 2 * width))
            pair = jnp.where(core == 0, pair[:, 0:width], pair[:, width:])
            bias_scr[j * width : (j + 1) * width] = pair.T
        down_copy.wait()
        for t in range(act_grad.shape[0]):
            tile = down_vm[t * model : (t + 1) * model]
            for q in range(seqs):
                act_grad[t, q * rows : (q + 1) * rows] = mat_nt(grad[q], tile).astype(BF16)
        act_copy.start()
        part_copy(0, 1).wait_recv()
        part_copy(0, 2).start()
        for r in (1, 2, 3):
            draw_copy(r).wait_recv()
        mine = draws_in[pl.ds(own * heads, heads)]
        draws_out[...] = jnp.concatenate(
            [mine] + [draws_land[r - 1] for r in (1, 2, 3)], axis=2
        )

    @pl.when(h == 0)
    def _():
        per = rows // BLOCK
        lanes = lax.broadcasted_iota(jnp.int32, (16, total), 1) // BLOCK
        level = lax.broadcasted_iota(jnp.int32, (16, total), 0)
        ids = jnp.full((16, total), -1, jnp.int32)
        for r in range(GROUP):
            for i in range(per):
                ids = jnp.where(
                    lanes == r * per + i, bucket[s, partner(own, r) * per + i, 0], ids
                )
        hot_out[...] = (ids == level).astype(F32).astype(BF16)

        def project(r):
            cols = slice(r * rows, (r + 1) * rows)
            piece = mat_nt(weight_out[...], parts[s, r]) + bias_scr[:, 0:1]
            proj_out[:, cols] = piece.astype(BF16)

        project(0)
        part_copy(s, 0).wait_recv()
        project(1)
        project(2)
        part_copy(s, 2).wait_recv()
        project(3)
        out_copy(s).start()

    query = proj_out[head_rows(h, 0, heads)]
    key = proj_out[head_rows(h, 1, heads)]
    value = proj_out[head_rows(h, 2, heads)]
    draws = draws_out[h]
    hot = hot_out[...]
    hot_wide = hot.astype(F32)
    away = away_marks(hot).astype(BF16)
    phi_q = features(query, draws).astype(BF16)
    phi_k = features(key, draws).astype(BF16)
    phi_q_out[...] = phi_q
    phi_k_out[...] = phi_k
    spread_value = jnp.concatenate(spread(value, away) + [away], axis=0)
    state = mat_nt(spread_value, phi_k).astype(BF16)
    state_out[...] = state
    low = mat(state, phi_q)
    low_scr[0:HD] = pick(low, hot_wide)
    low_den = jnp.sum(low[NBUCK * HD :] * hot_wide, axis=0, keepdims=True)
    low_scr[HD : HD + 8] = jnp.broadcast_to(low_den, (8, total))
    query_scr[...] = jnp.concatenate([query * (1.0 / math.sqrt(HD)), hot], axis=0).astype(BF16)
    key_scr[...] = jnp.concatenate([key, away * -FAR], axis=0).astype(F32).T.astype(BF16)
    value_scr[0:HD] = value
    value_scr[HD:] = jnp.ones((16, total), BF16)

    head_span = pl.ds(pl.multiple_of(h * HD, HD), HD)
    score = mat(key_scr[...], query_scr[:, 0:CHUNK])
    for c in range(total // CHUNK):
        cols = slice(c * CHUNK, (c + 1) * CHUNK)
        ahead = slice((c + 1) * CHUNK, (c + 2) * CHUNK)
        later = mat(key_scr[...], query_scr[:, ahead]) if ahead.stop <= total else None
        weights = jnp.exp(score).astype(BF16)
        score = later
        soft_out[:, cols] = weights
        exact = mat(value_scr[...], weights)
        den = low_scr[HD : HD + 8, cols] + exact[HD : HD + 8]
        mixed = (low_scr[0:HD, cols] + exact[0:HD]) / den[0:1]
        mixed_out[:, cols] = mixed
        den_out[:, cols] = den
        mixed_low = mixed.astype(BF16)
        for r in range(GROUP):
            low_col, high_col = max(cols.start, r * rows), min(cols.stop, (r + 1) * rows)
            if low_col < high_col:
                piece = mixed_low[:, low_col - cols.start : high_col - cols.start]
                inner = slice(low_col - r * rows, high_col - r * rows)
                if r:
                    mix_send[s, r - 1, head_span, inner] = piece
                else:
                    mix_land[s, 0, head_span, inner] = piece
    for r in (2, 3, 1):
        mix_copy(s, h, r).start()

    @pl.when((h == heads - 2) & (s < seqs - 1))
    def _():
        part_copy(s + 1, 1).wait_recv()
        part_copy(s + 1, 2).start()

    @pl.when((s == seqs - 1) & (h == heads - 1))
    def _():
        for q in range(seqs):
            for g in range(heads):
                for r in (1, 2, 3):
                    mix_copy(q, g, r).wait_recv()
        done = pltpu.make_async_copy(mix_land, mix_any, out_sem.at[seqs])
        done.start()
        for q in range(seqs):
            for kind in range(3):
                part_copy(q, kind).wait_send()
            for g in range(heads):
                for r in (1, 2, 3):
                    mix_copy(q, g, r).wait_send()
            out_copy(q).wait()
        act_copy.wait()
        for r in (1, 2, 3):
            draw_copy(r).wait_send()
        done.wait()


def attend(bucket, hidden, gain, shift, bias, weight, draws, grad, down):
    seqs, rows, model = hidden.shape
    tiles = down.shape[0] // model
    heads = draws.shape[0] // GROUP
    width = heads * HD
    total = GROUP * rows
    whole = lambda *shape: pl.BlockSpec(shape, lambda s, h: (0,) * len(shape))
    by_seq = lambda *shape: pl.BlockSpec((None,) + shape, lambda s, h: (s,) + (0,) * len(shape))
    by_head = lambda *shape: pl.BlockSpec(
        (None, None) + shape, lambda s, h: (s, h) + (0,) * len(shape)
    )
    anywhere = pl.BlockSpec(memory_space=pl.ANY)
    return pl.pallas_call(
        attend_kernel,
        grid=(seqs, heads),
        out_shape=(
            jax.ShapeDtypeStruct((seqs, GROUP, rows, model), BF16),
            jax.ShapeDtypeStruct((seqs, GROUP, width, rows), BF16),
            jax.ShapeDtypeStruct((tiles, seqs * rows, model), BF16),
            jax.ShapeDtypeStruct((seqs, 3 * width, total), BF16),
            jax.ShapeDtypeStruct((seqs, heads, STATES, FEAT), BF16),
            jax.ShapeDtypeStruct((seqs, heads, HD, total), F32),
            jax.ShapeDtypeStruct((seqs, heads, 8, total), F32),
            jax.ShapeDtypeStruct((seqs, 16, total), BF16),
            jax.ShapeDtypeStruct((3 * width, model), BF16),
            jax.ShapeDtypeStruct((heads, HD, FEAT), BF16),
            jax.ShapeDtypeStruct((seqs, heads, total, total), BF16),
            jax.ShapeDtypeStruct((seqs, heads, FEAT, total), BF16),
            jax.ShapeDtypeStruct((seqs, heads, FEAT, total), BF16),
        ),
        in_specs=[
            pl.BlockSpec(memory_space=pltpu.SMEM),
            whole(seqs, rows, model), whole(model), whole(model), whole(3 * model), anywhere,
            whole(*draws.shape), whole(seqs, rows, model), anywhere,
        ],
        out_specs=(
            anywhere, anywhere, anywhere, by_seq(3 * width, total), by_head(STATES, FEAT), by_head(HD, total),
            by_head(8, total), by_seq(16, total), whole(3 * width, model), whole(heads, HD, FEAT),
            by_head(total, total), by_head(FEAT, total), by_head(FEAT, total),
        ),
        scratch_shapes=[
            pltpu.VMEM((seqs, GROUP, rows, model), BF16),
            pltpu.VMEM((seqs, GROUP, width, rows), BF16),
            pltpu.VMEM((seqs, 3, width, rows), BF16),
            pltpu.VMEM((3, model, 2 * width), BF16),
            pltpu.VMEM((1, 3 * model), F32),
            pltpu.VMEM((3 * width, 128), F32),
            pltpu.VMEM((3, heads, HD, draws.shape[2]), BF16),
            pltpu.VMEM(down.shape, BF16),
            pltpu.VMEM((tiles, seqs * rows, model), BF16),
            pltpu.VMEM((HD + 16, total), BF16),
            pltpu.VMEM((total, HD + 16), BF16),
            pltpu.VMEM((HD + 16, total), BF16),
            pltpu.VMEM((HD + 8, total), F32),
            pltpu.SemaphoreType.DMA((3,)),
            pltpu.SemaphoreType.DMA((seqs, 3)),
            pltpu.SemaphoreType.DMA((seqs, 3)),
            pltpu.SemaphoreType.DMA((3,)),
            pltpu.SemaphoreType.DMA((3,)),
            pltpu.SemaphoreType.DMA((seqs, heads, 3)),
            pltpu.SemaphoreType.DMA((seqs, heads, 3)),
            pltpu.SemaphoreType.DMA((seqs + 1,)),
            pltpu.SemaphoreType.DMA,
            pltpu.SemaphoreType.DMA,
        ],
        compiler_params=pltpu.CompilerParams(
            vmem_limit_bytes=VMEM, collective_id=1, has_side_effects=True
        ),
        cost_estimate=pl.CostEstimate(
            flops=24_000_000_000, bytes_accessed=20_000_000, transcendentals=0
        ),
        name="attend",
    )(bucket, hidden, gain, shift, bias, weight, draws, grad, down)


def block_kernel(
    direct, parts_ref, hidden, grad, out_w, out_b, gain_ref, shift_ref, down_b, up_b, up, down,
    act_grad_ref,
    layer_out, resid_out, grads_any, first_any, slab_any, down_any, up_any, tail_any,
    mixed_t, resid_scr, in_scr, in_t, acc_out, acc_in, act_scr, pre_scr, vec_scr, bias_row, back_t,
    slab_vm, down_vm, up_vm, tail_vm, grads_vm, first_land, send_sem, recv_sem, out_sem,
):
    step = pl.program_id(0)
    model = hidden.shape[1]
    count = hidden.shape[0] // CHUNK
    tiles = act_scr.shape[0]
    spans = [slice(c * CHUNK, (c + 1) * CHUNK) for c in range(count)]
    owners = slab_vm.shape[0] if direct else tail_vm.shape[0]
    small = model // owners
    share = tiles * small
    own = lax.axis_index("feat")
    barrier = pltpu.get_barrier_semaphore()

    part = model // GROUP

    def group_rows(r):
        return pl.ds(pl.multiple_of(partner(own, r) * part, part), part)

    def grad_copy(r):
        return remote(
            grads_vm.at[0, r], first_land.at[r - 1], send_sem.at[r - 1], recv_sem.at[r - 1],
            {"feat": partner(own, r)},
        )

    def out_copy(i):
        pieces = [(down_vm, down_any), (up_vm, up_any), (tail_vm, tail_any)]
        if direct:
            cuts = (0, share, 2 * share, slab_vm.shape[1])
            pieces = [
                (slab_vm.at[:, pl.ds(low, high - low)], slab_any.at[:, pl.ds(low, high - low)])
                for low, high in zip(cuts, cuts[1:])
            ]
        src, dst = (
            *pieces, (grads_vm, grads_any), (first_land, first_any),
        )[i]
        return pltpu.make_async_copy(src, dst, out_sem.at[i])

    @pl.when(step == 0)
    def _():
        for r in (1, 2, 3):
            pl.semaphore_signal(
                barrier, inc=1, device_id={"feat": partner(own, r)}, device_id_type=MESH
            )
        for c, span in enumerate(spans):
            for r in range(GROUP):
                mixed_t[group_rows(r), span] = parts_ref[c, r]
            resid = hidden[span].astype(F32) + mat_tn(mixed_t[:, span], out_w[...]) + as_row(out_b)
            resid_scr[span] = resid
            normed, _ = row_stats(resid)
            inner = normed * as_row(gain_ref) + as_row(shift_ref)
            in_scr[span] = inner.astype(BF16)
            in_t[:, span] = inner.T.astype(BF16)
        acc_out[...] = jnp.zeros_like(acc_out)
        acc_in[...] = jnp.zeros_like(acc_in)
        bias_row[...] = as_row(up_b)

    slope = math.sqrt(2.0 / math.pi)
    total = jnp.zeros((1, model), F32)
    up_bias = bias_row[:, pl.ds(pl.multiple_of(step * model, model), model)]
    for span in spans:
        pre = mat(in_scr[span], up[...]) + up_bias
        square = pre * pre
        tanh = jnp.tanh(pre * (slope + (slope * 0.044715) * square))
        half = 0.5 * (1.0 + tanh)
        act = (pre * half).astype(BF16)
        bend = half + (0.5 * pre) * (1.0 - tanh * tanh) * (
            slope + (3.0 * slope * 0.044715) * square
        )
        pre_grad = act_grad_ref[span].astype(F32) * bend
        total = total + jnp.sum(pre_grad, axis=0, keepdims=True)
        pre_low = pre_grad.astype(BF16)
        act_scr[step, span] = act
        pre_scr[step, span] = pre_low
        acc_out[span] += mat(act, down[...])
        acc_in[span] += mat_nt(pre_low, up[...])
    vec_scr[pl.ds(4 + step, 1)] = total
    down_term = mat_tn(act_scr[step], grad[...])
    if direct:
        for i in range(model // share):
            slab_vm[step * (model // share) + i, 0:share] = down_term[
                i * share : (i + 1) * share
            ].astype(BF16)
    else:
        down_vm[pl.ds(pl.multiple_of(step * model, model), model)] = down_term.astype(BF16)

    @pl.when(step == pl.num_programs(0) - 1)
    def _():
        pl.semaphore_wait(barrier, 3)
        sums = [jnp.zeros((1, model), F32) for _ in range(4)]
        for c, span in enumerate(spans):
            resid = resid_scr[span]
            normed, scale = row_stats(resid)
            inner_grad = acc_in[span]
            wide = grad[span].astype(F32)
            resid_grad = wide + norm_back(inner_grad * as_row(gain_ref), normed, scale)
            resid_out[span] = resid_grad
            low = resid_grad.astype(BF16)
            in_scr[span] = low
            back_t[...] = mat_nt(out_w[...], low).astype(BF16)
            for r in (2, 3, 1, 0):
                grads_vm[c, r] = back_t[group_rows(r)]
                if c == 0 and r:
                    grad_copy(r).start()
            layer_out[span] = (resid + acc_out[span] + as_row(down_b)).astype(BF16)
            for i, term in enumerate((wide, resid_grad, inner_grad * normed, inner_grad)):
                sums[i] = sums[i] + jnp.sum(term, axis=0, keepdims=True)
        out_copy(3).start()
        for i in range(4):
            vec_scr[i : i + 1] = sums[i]
        out_copy(0).start()
        for t in range(0, tiles, 2):
            terms = [mat(in_t[...], pre_scr[t]), mat(in_t[...], pre_scr[t + 1])]
            if direct:
                for i in range(owners):
                    own_rows = slice(i * small, (i + 1) * small)
                    slab_vm[i, share + t * small : share + (t + 2) * small] = jnp.concatenate(
                        [term[own_rows] for term in terms], axis=0
                    ).astype(BF16)
            else:
                for u, term in enumerate(terms):
                    up_vm[:, (t + u) * model : (t + u + 1) * model] = term.astype(BF16)
        out_copy(1).start()
        out_term = mat(mixed_t[...], in_scr[...])
        fill = aligned(small + 8) - small - 8
        extra = [jnp.zeros((fill, model), F32)] if fill else []
        for i in range(owners):
            rest = jnp.concatenate(
                [out_term[i * small : (i + 1) * small], vec_scr[...]] + extra, axis=0
            ).astype(BF16)
            if direct:
                slab_vm[i, 2 * share :] = rest
            else:
                tail_vm[i] = rest
        out_copy(2).start()
        for r in (1, 2, 3):
            grad_copy(r).wait_recv()
        out_copy(4).start()
        for r in (1, 2, 3):
            grad_copy(r).wait_send()
        for i in range(5):
            out_copy(i).wait()


def block_layer(
    parts, hidden, grad, out_w, out_b, gain, shift, down_b, up_b, up, down, act_grad, devices
):
    tokens, model = hidden.shape
    ff = up.shape[1]
    steps = ff // model
    seqs = parts.shape[0]
    small, share = model // devices, ff // devices
    direct = small % 8 == 0 and share % 16 == 0
    tail_rows = aligned(small + 8)
    single = pl.Buffered(1)
    whole = lambda *shape: pl.BlockSpec(
        shape, lambda t: (0,) * len(shape), pipeline_mode=single
    )
    anywhere = pl.BlockSpec(memory_space=pl.ANY)
    unused = (16, 128)
    slab_shape, down_shape, up_shape, tail_shape = (
        ((devices, 2 * share + tail_rows, model), unused, unused, unused) if direct
        else (unused, (ff, model), (model, ff), (devices, tail_rows, model))
    )
    layer_out, resid_grad, grads, first, slab, down_grad, up_grad, tail = pl.pallas_call(
        lambda *refs: block_kernel(direct, *refs),
        grid=(steps,),
        out_shape=(
            jax.ShapeDtypeStruct((tokens, model), BF16),
            jax.ShapeDtypeStruct((tokens, model), F32),
            jax.ShapeDtypeStruct(parts.shape, BF16),
            jax.ShapeDtypeStruct((3,) + parts.shape[2:], BF16),
            jax.ShapeDtypeStruct(slab_shape, BF16),
            jax.ShapeDtypeStruct(down_shape, BF16),
            jax.ShapeDtypeStruct(up_shape, BF16),
            jax.ShapeDtypeStruct(tail_shape, BF16),
        ),
        in_specs=[
            whole(*parts.shape), whole(tokens, model), whole(tokens, model), whole(model, model),
            whole(model), whole(model), whole(model), whole(model), whole(ff),
            pl.BlockSpec((model, model), lambda t: (0, t)),
            pl.BlockSpec((model, model), lambda t: (t, 0)),
            pl.BlockSpec((None, tokens, model), lambda t: (t, 0, 0)),
        ],
        out_specs=(
            whole(tokens, model), whole(tokens, model), anywhere, anywhere, anywhere, anywhere,
            anywhere, anywhere,
        ),
        scratch_shapes=[
            pltpu.VMEM((model, tokens), BF16),
            pltpu.VMEM((tokens, model), F32),
            pltpu.VMEM((tokens, model), BF16),
            pltpu.VMEM((model, tokens), BF16),
            pltpu.VMEM((tokens, model), F32),
            pltpu.VMEM((tokens, model), F32),
            pltpu.VMEM((steps, tokens, model), BF16),
            pltpu.VMEM((steps, tokens, model), BF16),
            pltpu.VMEM((8, model), F32),
            pltpu.VMEM((1, ff), F32),
            pltpu.VMEM((model, CHUNK), BF16),
            pltpu.VMEM(slab_shape, BF16),
            pltpu.VMEM(down_shape, BF16),
            pltpu.VMEM(up_shape, BF16),
            pltpu.VMEM(tail_shape, BF16),
            pltpu.VMEM(parts.shape, BF16),
            pltpu.VMEM((3,) + parts.shape[2:], BF16),
            pltpu.SemaphoreType.DMA((3,)),
            pltpu.SemaphoreType.DMA((3,)),
            pltpu.SemaphoreType.DMA((5,)),
        ],
        compiler_params=pltpu.CompilerParams(
            vmem_limit_bytes=VMEM, collective_id=3, has_side_effects=True
        ),
        cost_estimate=pl.CostEstimate(
            flops=26_000_000_000, bytes_accessed=30_000_000, transcendentals=0
        ),
        name="block_layer",
    )(parts, hidden, grad, out_w, out_b, gain, shift, down_b, up_b, up, down, act_grad)
    if not direct:
        fit = lambda a: jnp.pad(a, ((0, 0), (0, aligned(a.shape[1]) - a.shape[1]), (0, 0)))
        down_grad = fit(down_grad.reshape(devices, share, model))
        up_grad = up_grad.reshape(devices, small, ff // model, model).transpose(0, 2, 1, 3)
        up_grad = fit(up_grad.reshape(devices, ff // model * small, model))
        slab = jnp.concatenate([down_grad, up_grad, tail], axis=1)
    return layer_out, resid_grad, grads, first, slab


def attend_back_kernel(
    dp_size, x_ref, grads_ref, first_ref, weight, draws_ref, hot_ref, proj, state_ref, mixed_ref, den_ref,
    soft_ref, phi_q_ref, phi_k_ref, slab_any,
    attn_out, ring_out, proj_out,
    grad_scr, num_scr, value_scr, score_scr, exact_scr, proj_scr,
    grad_land, near_send, near_land, far_keep, far_send, far_land,
    mine, met, ring_land, cross_land,
    weight_acc, own_send, pair_land, own_mid, own_land, part_send, part_land,
    grad_sems, near_sems, far_sems, mine_sem, met_send, met_sems, ring_send, ring_sems, cross_sems,
    pair_sems, own_send_sem, own_sems,
    part_sems,
):
    s, h = pl.program_id(0), pl.program_id(1)
    seqs, heads = pl.num_programs(0), pl.num_programs(1)
    rows, model = x_ref.shape[1], x_ref.shape[2]
    head_count = proj_scr.shape[0] // (3 * HD)
    width = head_count * HD
    total = GROUP * rows
    root = 1.0 / math.sqrt(HD)
    own, me = lax.axis_index("feat"), lax.axis_index("dp")
    own_x, own_core = own // 2, own % 2
    near, across = {"feat": partner(own, 1)}, {"feat": partner(own, 2)}
    last = (s == seqs - 1) & (h == heads - 1)

    def grad_copy(q, r):
        return remote(
            grads_ref.at[q, r], grad_land.at[q - 1, r - 1], grad_sems.at[0, q - 1, r - 1],
            grad_sems.at[1, q - 1, r - 1], {"feat": partner(own, r)},
        )

    def near_copy(q, i):
        return remote(
            near_send.at[i], near_land.at[q, i], near_sems.at[0, q, i], near_sems.at[1, q, i], near
        )

    def far_copy(q):
        return remote(far_send, far_land.at[q], far_sems.at[0, q], far_sems.at[1, q], across)

    half = dp_size // 2
    parity, pair = lax.rem(me, 2), lax.div(me, 2)
    spot = pair + parity * (dp_size - 1 - 2 * pair)

    def at_spot(p):
        p = lax.rem(p + dp_size, dp_size)
        upper = lax.div(p, half)
        return 2 * p + upper * (2 * dp_size - 1 - 4 * p)

    places = ({"dp": at_spot(spot + 1)}, {"dp": at_spot(spot - 1)})

    def chunk(k, way):
        return at_spot(spot - 1 - k) if way == 0 else at_spot(spot + 1 + k)

    def mine_copy(k, way, owner):
        return pltpu.make_async_copy(
            slab_any.at[owner + own_core], mine.at[k, way], mine_sem.at[k, way]
        )

    def met_copy(k, way, owner):
        return remote(
            slab_any.at[owner + 1 - own_core], met.at[k, way], met_send, met_sems.at[k, way], near
        )

    cut = aligned(mine.shape[2] // 2)
    halves = (pl.ds(0, cut), pl.ds(cut, mine.shape[2] - cut))

    def ring_copy(k, way, part):
        return remote(
            mine.at[k, way, halves[part]], ring_land.at[k, way, halves[part]], ring_send,
            ring_sems.at[k, way, part], places[way],
        )

    def cross_copy(part):
        return remote(
            mine.at[dp_size - 1, 1 - own_x, halves[part]], cross_land.at[halves[part]],
            cross_sems.at[0, part], cross_sems.at[1, part], across,
        )

    def begin_pieces(k):
        for way in range(2):
            owner = chunk(k, way) * GROUP + 2 * way
            met_copy(k, way, owner).start()
            mine_copy(k, way, owner).start()

    def ring_step(k, part):
        span = halves[part]
        if part == 0:

            @pl.when(k + 2 < dp_size)
            def _():
                begin_pieces(k + 2)

        @pl.when(k < dp_size)
        def _():
            for way in range(2):
                if part == 0:
                    mine_copy(k, way, 0).wait()
                    met_copy(k, way, 0).wait_recv()

                @pl.when(k == 0)
                def _():
                    mine[k, way, span] = mine[k, way, span] + met[k, way, span]

                @pl.when(k > 0)
                def _():
                    ring_copy(k - 1, way, part).wait_recv()
                    chip = mine[k, way, span] + met[k, way, span]
                    mine[k, way, span] = chip + ring_land[k - 1, way, span]

                @pl.when(k < dp_size - 1)
                def _():
                    ring_copy(k, way, part).start()

            @pl.when(k == dp_size - 1)
            def _():
                cross_copy(part).start()

        @pl.when(k == dp_size)
        def _():
            cross_copy(part).wait_recv()
            ring_out[span] = mine[dp_size - 1, own_x, span].astype(F32) + cross_land[span].astype(F32)

    def ring_turn(part):
        turn = s * heads + h
        count = seqs * heads
        steps = dp_size + 1

        def body(k, carry):
            ring_step(k, part)
            return carry

        lax.fori_loop(lax.div(turn * steps, count), lax.div((turn + 1) * steps, count), body, 0)

    mate = me + 1 - 2 * parity

    def pair_copy(q):
        return remote(
            own_send.at[q, 1 - parity], pair_land.at[q], pair_sems.at[0, q], pair_sems.at[1, q],
            {"dp": mate},
        )

    def own_copy(q, k):
        to = lax.rem(pair + k, half)
        return remote(
            own_mid.at[q, to], own_land.at[q, k], own_send_sem, own_sems.at[q, k],
            {"dp": 2 * to + parity},
        )

    base = model // dp_size

    def folded(values):
        middle = values.shape[0] // 2
        return jnp.concatenate([values[0:middle], values[middle:]], axis=1)

    def begin_own(q):
        turned = weight_acc[pl.ds(pl.multiple_of(q * 3 * HD, 3 * HD), 3 * HD)].T
        biases = turned[model : model + 16]
        blank = own_send.shape[3] - base - base // 2 - 16
        extra = [jnp.zeros((blank, 2 * HD), F32)] if blank else []
        for c in range(dp_size):
            block = turned[c * base : (c + 1) * base]
            own_send[q, c % 2, c // 2] = jnp.concatenate(
                [
                    block[:, 0 : 2 * HD], folded(block[:, 2 * HD :]), biases[0:8, 0 : 2 * HD],
                    folded(biases[:, 2 * HD :]),
                ] + extra,
                axis=0,
            ).astype(BF16)
        pair_copy(q).start()

    def relay_own(q):
        pair_copy(q).wait_recv()
        own_mid[q] = (own_send[q, parity].astype(F32) + pair_land[q].astype(F32)).astype(BF16)

        def start(k, carry):
            own_copy(q, k).start()
            return carry

        lax.fori_loop(1, half, start, 0)

    def part_copy(r):
        other = partner(own, r)
        return remote(
            part_send.at[other], part_land.at[r - 1], part_sems.at[0, r - 1],
            part_sems.at[1, r - 1], {"feat": other},
        )

    def seq_span(q):
        return pl.ds(pl.multiple_of(q * rows, rows), rows)

    def add_near(q):
        near_copy(q, 1).wait_recv()

        @pl.when(q > 0)
        def _():
            far_copy(q - 1).wait_send()

        far_send[...] = (far_keep[1] + near_land[q, 1].astype(F32)).astype(BF16)
        far_copy(q).start()
        near_copy(q, 0).wait_recv()
        attn_out[seq_span(q)] = far_keep[0] + near_land[q, 0].astype(F32)

    def finish(q):
        far_copy(q).wait_recv()
        span = seq_span(q)
        attn_out[span] = attn_out[span] + far_land[q].astype(F32)

    @pl.when((s == 0) & (h == 0))
    def _():
        barrier = pltpu.get_barrier_semaphore()
        for r in (1, 2, 3):
            pl.semaphore_signal(
                barrier, inc=1, device_id={"feat": partner(own, r)}, device_id_type=MESH
            )

        def greet(k, carry):
            pl.semaphore_signal(
                barrier, inc=1, device_id={"dp": lax.rem(me + k, dp_size)}, device_id_type=MESH
            )
            return carry

        lax.fori_loop(1, dp_size, greet, 0)
        pl.semaphore_wait(barrier, 3 + dp_size - 1)
        for q in range(1, near_land.shape[0]):
            for r in (2, 3, 1):
                grad_copy(q, r).start()
        for k in range(2):
            begin_pieces(k)
        weight_acc[...] = jnp.zeros_like(weight_acc)

    @pl.when(h == 0)
    def _():
        grad_scr[:, 0:rows] = grads_ref[s, 0].astype(F32)

        @pl.when(s == 0)
        def _():
            for r in (1, 2, 3):
                grad_scr[:, r * rows : (r + 1) * rows] = first_ref[r - 1].astype(F32)

        @pl.when(s > 0)
        def _():
            for r in (1, 2, 3):
                grad_copy(s, r).wait_recv()
                grad_scr[:, r * rows : (r + 1) * rows] = grad_land[s - 1, r - 1].astype(F32)

    query = proj[head_rows(h, 0, head_count)]
    key = proj[head_rows(h, 1, head_count)]
    value = proj[head_rows(h, 2, head_count)]
    draws = draws_ref[...]
    draws_ext = jnp.concatenate([draws, jnp.ones((16, FEAT), BF16)], axis=0)
    hot = hot_ref[...]
    away_wide = away_marks(hot)
    away = away_wide.astype(BF16)
    inverse = 1.0 / den_ref[0:1]
    head_grad = grad_scr[pl.ds(pl.multiple_of(h * HD, HD), HD)]
    grad_num = (head_grad * inverse).astype(BF16)
    grad_den = -jnp.sum(head_grad * mixed_ref[...], axis=0, keepdims=True) * inverse
    den_rows = jnp.broadcast_to(grad_den, (16, total)).astype(BF16)
    spread_grad = jnp.concatenate(spread(grad_num, hot) + [den_rows * hot], axis=0)
    spread_value = jnp.concatenate(spread(value, away) + [away], axis=0)

    phi_q, phi_k = phi_q_ref[...], phi_k_ref[...]
    state_grad = mat_nt(spread_grad, phi_q).astype(BF16)
    phi_q_grad = mat_tn(state_ref[...], spread_grad)
    phi_k_grad = mat_tn(state_grad, spread_value)
    value_low = mat(state_grad[0 : NBUCK * HD], phi_k)
    scaled_q = phi_q_grad.astype(BF16) * phi_q
    back_q = mat(draws_ext, scaled_q)
    scaled_k = phi_k_grad.astype(BF16) * phi_k
    back_k = mat(draws_ext, scaled_k)
    value_grad = pick(value_low, away_wide)
    query_grad = back_q[0:HD] - query.astype(F32) * (back_q[HD : HD + 1] * root)
    key_grad = back_k[0:HD] - key.astype(F32) * (back_k[HD : HD + 1] * root)

    ring_turn(0)
    one = (lax.broadcasted_iota(jnp.int32, hot.shape, 0) < 1).astype(F32).astype(BF16)
    num_scr[...] = jnp.concatenate([grad_num, den_rows], axis=0)
    value_scr[...] = jnp.concatenate([value, one], axis=0).astype(F32).T.astype(BF16)

    later = mat(value_scr[...], num_scr[:, 0:CHUNK])
    for c in range(total // CHUNK):
        cols = slice(c * CHUNK, (c + 1) * CHUNK)
        ahead = slice((c + 1) * CHUNK, (c + 2) * CHUNK)
        score = later
        later = mat(value_scr[...], num_scr[:, ahead]) if ahead.stop <= total else None
        score = score.astype(BF16) * soft_ref[:, cols]
        score_scr[:, cols] = score
        exact_scr[:, cols] = mat(proj[head_rows(h, 1, head_count)], score)
    query_grad = query_grad + exact_scr[...] * root
    key_grad = key_grad + mat_nt(query, score_scr[...]) * root
    value_grad = value_grad + mat_nt(grad_num, soft_ref[...])
    wide_grad = jnp.concatenate([query_grad, key_grad, value_grad], axis=0)
    low_grad = wide_grad.astype(BF16)
    for kind in range(3):
        proj_scr[head_rows(h, kind, head_count)] = low_grad[kind * HD : (kind + 1) * HD]
    weight_grad = mat(low_grad[:, 0:rows], x_ref[0])
    for r in (1, 2, 3):
        weight_grad = weight_grad + mat(low_grad[:, r * rows : (r + 1) * rows], x_ref[r])
    span = pl.ds(pl.multiple_of(h * 3 * HD, 3 * HD), 3 * HD)
    weight_acc[span, 0:model] += weight_grad
    weight_acc[span, model:] += jnp.broadcast_to(
        jnp.sum(wide_grad, axis=1, keepdims=True), (3 * HD, 128)
    )

    @pl.when(s == seqs - 1)
    def _():
        begin_own(h)

        @pl.when(h > 0)
        def _():
            relay_own(h - 1)

    @pl.when((s > 0) & (h == 0))
    def _():
        add_near(s - 1)

    @pl.when(h == heads - 1)
    def _():
        @pl.when(s > 0)
        def _():
            for i in range(2):
                near_copy(s - 1, i).wait_send()

        for r in (3, 1, 2, 0):
            term = mat_tn(proj_scr[:, r * rows : (r + 1) * rows], weight[...])
            if r % 2:
                near_send[r // 2] = term.astype(BF16)
                near_copy(s, r // 2).start()
            else:
                far_keep[r // 2] = term

    ring_turn(1)

    @pl.when(last)
    def _():
        add_near(s)
        relay_own(h)
        for q in range(near_land.shape[0] - 1):
            finish(q)

        sums = []
        for q in range(head_count):

            def arrive(k, carry):
                own_copy(q, k).wait_recv()
                return carry + own_land[q, k].astype(F32)

            sums.append(lax.fori_loop(1, half, arrive, own_mid[q, pair].astype(F32)))
        blocks, biases = [], []
        end = base + base // 2
        for total_sum in sums:
            value_rows = total_sum[base:end]
            value_rows = jnp.concatenate([value_rows[:, 0:HD], value_rows[:, HD:]], axis=0)
            blocks += [total_sum[0:base], value_rows]
            biases += [total_sum[end : end + 1], total_sum[end + 8 : end + 9, 0:HD]]
        joined = jnp.concatenate(blocks, axis=1)
        small = base // GROUP
        fill = jnp.broadcast_to(
            jnp.concatenate(biases, axis=1), (part_send.shape[1] - small, joined.shape[1])
        )
        for a in range(GROUP):
            part_send[a] = jnp.concatenate(
                [joined[a * small : (a + 1) * small], fill], axis=0
            ).astype(BF16)
        for r in (2, 3, 1):
            part_copy(r).start()
        finish(s)
        proj_out[own] = part_send[own].astype(F32)
        for r in (1, 2, 3):
            part_copy(r).wait_recv()
            proj_out[partner(own, r)] = part_land[r - 1].astype(F32)

        for i in range(2):
            near_copy(s, i).wait_send()
        far_copy(s).wait_send()
        for r in (1, 2, 3):
            part_copy(r).wait_send()
        for part in range(2):
            cross_copy(part).wait_send()
        for q in range(1, near_land.shape[0]):
            for r in (1, 2, 3):
                grad_copy(q, r).wait_send()
        for q in range(head_count):
            pair_copy(q).wait_send()
        every = pl.ds(0, half - 1)
        if half > 1:
            remote(
                own_mid.at[:, every], own_land.at[:, every], own_send_sem, own_sems.at[0, 0],
                {"dp": mate},
            ).wait_send()
        remote(
            mine.at[pl.ds(0, dp_size - 1)], ring_land, ring_send, ring_sems.at[0, 0, 0], places[0]
        ).wait_send()
        remote(mine, met, met_send, met_sems.at[0, 0], near).wait_send()


def attend_back(
    dp_size, parts, grads, first, weight, draws, hot, proj, state, mixed, den, soft, phi_q, phi_k,
    slab,
):
    seqs, _, rows, model = parts.shape
    heads = draws.shape[0]
    width = heads * HD
    total = GROUP * rows
    n = dp_size
    ring_rows = slab.shape[1]
    own_rows = aligned(model // n + model // n // 2 + 16)
    part_rows = aligned(model // (n * GROUP) + 1)
    single = pl.Buffered(1)
    whole = lambda *shape: pl.BlockSpec(
        shape, lambda s, h: (0,) * len(shape), pipeline_mode=single
    )
    mode = single if n > 16 else None
    by_seq = lambda *shape: pl.BlockSpec(
        (None,) + shape, lambda s, h: (s,) + (0,) * len(shape), pipeline_mode=mode
    )
    by_head = lambda *shape: pl.BlockSpec(
        (None, None) + shape, lambda s, h: (s, h) + (0,) * len(shape), pipeline_mode=mode
    )
    anywhere = pl.BlockSpec(memory_space=pl.ANY)
    dma = pltpu.SemaphoreType.DMA
    return pl.pallas_call(
        lambda *refs: attend_back_kernel(dp_size, *refs),
        grid=(seqs, heads),
        out_shape=(
            jax.ShapeDtypeStruct((seqs * rows, model), F32),
            jax.ShapeDtypeStruct((ring_rows, model), F32),
            jax.ShapeDtypeStruct((GROUP, part_rows, 3 * width), F32),
        ),
        in_specs=[
            by_seq(GROUP, rows, model), whole(*grads.shape), whole(*first.shape),
            whole(3 * width, model),
            pl.BlockSpec((None, HD, FEAT), lambda s, h: (h, 0, 0)),
            by_seq(16, total), by_seq(3 * width, total), by_head(STATES, FEAT), by_head(HD, total),
            by_head(8, total), by_head(total, total), by_head(FEAT, total), by_head(FEAT, total),
            anywhere,
        ],
        out_specs=(
            whole(seqs * rows, model), whole(ring_rows, model), whole(GROUP, part_rows, 3 * width),
        ),
        scratch_shapes=[
            pltpu.VMEM((width, total), F32),
            pltpu.VMEM((HD + 16, total), BF16),
            pltpu.VMEM((total, HD + 16), BF16),
            pltpu.VMEM((total, total), BF16),
            pltpu.VMEM((HD, total), F32),
            pltpu.VMEM((3 * width, total), BF16),
            pltpu.VMEM((seqs - 1, 3, width, rows), BF16),
            pltpu.VMEM((2, rows, model), BF16),
            pltpu.VMEM((seqs, 2, rows, model), BF16),
            pltpu.VMEM((2, rows, model), F32),
            pltpu.VMEM((rows, model), BF16),
            pltpu.VMEM((seqs, rows, model), BF16),
            pltpu.VMEM((n, 2, ring_rows, model), BF16),
            pltpu.VMEM((n, 2, ring_rows, model), BF16),
            pltpu.VMEM((n - 1, 2, ring_rows, model), BF16),
            pltpu.VMEM((ring_rows, model), BF16),
            pltpu.VMEM((3 * width, model + 128), F32),
            pltpu.VMEM((heads, 2, n // 2, own_rows, 2 * HD), BF16),
            pltpu.VMEM((heads, n // 2, own_rows, 2 * HD), BF16),
            pltpu.VMEM((heads, n // 2, own_rows, 2 * HD), BF16),
            pltpu.VMEM((heads, n // 2, own_rows, 2 * HD), BF16),
            pltpu.VMEM((GROUP, part_rows, 3 * width), BF16),
            pltpu.VMEM((3, part_rows, 3 * width), BF16),
            dma((2, seqs - 1, 3)),
            dma((2, seqs, 2)),
            dma((2, seqs)),
            dma((n, 2)),
            dma,
            dma((n, 2)),
            dma,
            dma((n - 1, 2, 2)),
            dma((2, 2)),
            dma((2, heads)),
            dma,
            dma((heads, n // 2)),
            dma((2, 3)),
        ],
        compiler_params=pltpu.CompilerParams(
            vmem_limit_bytes=VMEM + (3 * 1024 * 1024 if n > 16 else 0), collective_id=2, has_side_effects=True
        ),
        cost_estimate=pl.CostEstimate(
            flops=48_000_000_000, bytes_accessed=40_000_000, transcendentals=0
        ),
        name="attend_back",
    )(
        parts, grads, first, weight, draws, hot, proj, state, mixed, den, soft, phi_q, phi_k, slab,
    )


def finish_kernel(
    starts, heads, attn_grad, resid_grad, hidden, sums, proj_sums, weight_any, gain_ref, shift_ref,
    input_out, norm1_gain_out, norm1_bias_out, qkv_out, qkv_bias_out, out_out, out_bias_out,
    norm2_gain_out, norm2_bias_out, up_out, up_bias_out, down_out, down_bias_out,
    weight_vm, weight_sem,
):
    gain, shift = as_row(gain_ref), as_row(shift_ref)
    index = lax.axis_index("dp") * GROUP + lax.axis_index("feat")
    small, model = out_out.shape
    window = weight_vm.shape[0]
    begin = jnp.minimum(lax.div(index * small, 16) * 16, model - window)
    weight_copy = pltpu.make_async_copy(
        weight_any.at[pl.ds(pl.multiple_of(begin, 16), window)], weight_vm, weight_sem
    )

    @pl.when(pl.program_id(0) == 0)
    def _():
        weight_copy.start()

    normed, scale = row_stats(hidden[...].astype(F32))
    input_out[...] = resid_grad[...] + norm_back(attn_grad[...] * gain, normed, scale)

    @pl.when(pl.program_id(0) == 0)
    def _():
        share = down_out.shape[0]
        ff = up_out.shape[1]

        def own(row, size):
            length = row.shape[1]
            wide = jnp.broadcast_to(row, (8, length))
            back = lax.rem(length - lax.rem(index * size, length), length)
            return pltpu.roll(wide, back, 1)[0:1, 0:size]

        down_out[...] = sums[0:share]
        first = starts[0]
        up_out[...] = jnp.concatenate(
            [sums[first + i * small : first + (i + 1) * small] for i in range(ff // model)], axis=1
        )
        first = starts[1]
        out_out[...] = sums[first : first + small]
        totals = first + small
        for i, out in enumerate((down_bias_out, out_bias_out, norm2_gain_out, norm2_bias_out)):
            out[...] = own(sums[totals + i : totals + i + 1], small).reshape(small)
        per_row = model // share
        level = index // per_row
        row = jnp.zeros((1, model), F32)
        for i in range(ff // model):
            row = jnp.where(level == i, sums[totals + 4 + i : totals + 5 + i], row)
        up_bias_out[...] = own(row, share).reshape(share)

        pieces = []
        for kind in range(3):
            for f in range(GROUP):
                for h in range(heads):
                    lanes = slice((h * 3 + kind) * HD, (h * 3 + kind + 1) * HD)
                    pieces.append(proj_sums[f, 0 : small + 1, lanes])
        grid = jnp.concatenate(pieces, axis=1)
        weight_sum, bias_sum = grid[0:small], grid[small : small + 1]
        qkv_out[...] = weight_sum
        qkv_bias_out[...] = own(bias_sum, 3 * small).reshape(3 * small)
        weight_copy.wait()
        near_rows = weight_vm[...].astype(F32)
        step = math.gcd(small, 16)
        wide = near_rows[0:small]
        for offset in range(step, window - small + 1, step):
            wide = jnp.where(
                index * small - begin == offset, near_rows[offset : offset + small], wide
            )

        def to_row(column):
            column = jnp.concatenate(
                [column, jnp.zeros((-small % 128, 1), F32)], axis=0
            )
            return jnp.broadcast_to(column, (column.shape[0], 128)).T[0:1, 0:small]

        bias_grad = to_row(jnp.sum(wide * bias_sum, axis=1, keepdims=True))
        gain_grad = to_row(jnp.sum(wide * weight_sum, axis=1, keepdims=True))
        norm1_bias_out[...] = bias_grad.reshape(small)
        gain_grad = (gain_grad - own(shift, small) * bias_grad) / own(gain, small)
        norm1_gain_out[...] = gain_grad.reshape(small)


def finish_all(
    attn_grad, resid_grad, hidden, sums, proj_sums, weight, gain, shift, devices, ff, heads,
):
    seqs, rows, model = hidden.shape
    small, share = model // devices, ff // devices
    starts = (aligned(share), 2 * aligned(share))
    whole = lambda *shape: pl.BlockSpec(shape, lambda s: (0,) * len(shape))
    by_seq = pl.BlockSpec((rows, model), lambda s: (s, 0))
    shapes = (
        (small,), (small,), (small, 3 * model), (3 * small,), (small, model), (small,), (small,),
        (small,), (small, ff), (share,), (share, model), (small,),
    )
    return pl.pallas_call(
        lambda *refs: finish_kernel(starts, heads, *refs),
        grid=(seqs,),
        out_shape=(jax.ShapeDtypeStruct((seqs * rows, model), F32),)
        + tuple(jax.ShapeDtypeStruct(shape, F32) for shape in shapes),
        in_specs=[
            by_seq, by_seq, pl.BlockSpec((None, rows, model), lambda s: (s, 0, 0)),
            whole(*sums.shape), whole(*proj_sums.shape), pl.BlockSpec(memory_space=pl.ANY), whole(model),
            whole(model),
        ],
        out_specs=(by_seq,) + tuple(whole(*shape) for shape in shapes),
        scratch_shapes=[
            pltpu.VMEM((aligned(small) + 16, 3 * model), BF16), pltpu.SemaphoreType.DMA,
        ],
        compiler_params=pltpu.CompilerParams(vmem_limit_bytes=VMEM),
        name="finish_all",
    )(attn_grad, resid_grad, hidden, sums, proj_sums, weight, gain, shift)


def per_device(
    hidden_in, norm1_gain, norm1_bias, qkv_weight, qkv_bias, feature_draws, out_weight, out_bias,
    norm2_gain, norm2_bias, up_weight, up_bias, down_weight, down_bias, block_bucket, out_grad,
):
    seqs, rows, model = hidden_in.shape
    ff = up_weight.shape[1]
    dp_size = lax.axis_size("dp")
    devices = dp_size * GROUP
    heads = feature_draws.shape[0] // GROUP
    flat = (seqs * rows, model)

    (
        parts, mixed_parts, act_grad, proj, state, mixed, den, hot, own_weight, own_draws, soft,
        phi_q, phi_k,
    ) = attend(
        block_bucket, hidden_in, norm1_gain, norm1_bias, qkv_bias, qkv_weight, feature_draws,
        out_grad, down_weight,
    )
    layer_out, resid_grad, grads, first, slab = block_layer(
        mixed_parts, hidden_in.reshape(flat), out_grad.reshape(flat), out_weight, out_bias,
        norm2_gain, norm2_bias, down_bias, up_bias, up_weight, down_weight, act_grad, devices,
    )
    attn_grad, sums, proj_sums = attend_back(
        dp_size, parts, grads, first, own_weight, own_draws, hot, proj, state, mixed, den, soft,
        phi_q, phi_k, slab,
    )
    (
        input_grad, norm1_gain_sum, norm1_bias_sum, qkv_weight_sum, qkv_bias_sum, out_weight_sum,
        out_bias_sum, norm2_gain_sum, norm2_bias_sum, up_sum, up_bias_sum, down_sum, down_bias_sum,
    ) = finish_all(
        attn_grad, resid_grad, hidden_in, sums, proj_sums, qkv_weight, norm1_gain, norm1_bias,
        devices, ff, heads,
    )
    return (
        layer_out.reshape(hidden_in.shape), input_grad.reshape(hidden_in.shape), norm1_gain_sum,
        norm1_bias_sum, qkv_weight_sum, qkv_bias_sum, out_weight_sum, out_bias_sum, norm2_gain_sum,
        norm2_bias_sum, up_sum, up_bias_sum, down_sum, down_bias_sum,
    )


def solution(mesh):
    both = ("dp", "feat")
    rows = P("dp", "feat", None)
    in_specs = (
        rows, P(), P(), P(), P(), P(None, None, "feat"), P(), P(), P(), P(), P(), P(), P(), P(),
        P("dp", None, None), rows,
    )
    out_specs = (
        rows, rows, P(both), P(both), P(both, None), P(both), P(both, None), P(both), P(both),
        P(both), P(both, None), P(both), P(both, None), P(both),
    )
    return jax.shard_map(
        per_device, mesh=mesh, in_specs=in_specs, out_specs=out_specs, check_vma=False
    )
```
